32 devices in a mesh: dp: 16 (over z, y, x), section: 2 (over core).
Axes of the slice: x: 2, y: 2, z: 4, core: 2. Of those that a mesh axis runs over, the one named last changes fastest.
Arguments:
- tokens: bfloat16 [2, 4096, 768], P(None, 'dp'), may hold values from -6 to 6
- latents: bfloat16 [2, 128, 768], P(None, 'dp'), may hold values from -6 to 6
- slot_group: int32 [2, 16], replicated, may hold values from 0 to 15, each once within a row
- image_groups: int32 [2, 4], replicated, may hold values from 1 to 8, 16 in all within a row
- gain_attn: float32 [2, 768], P('section'), may hold values from 0.5 to 1.5
- w_qkv: bfloat16 [2, 768, 2304], P('section'), may hold values from -0.21875 to 0.21875
- w_out: bfloat16 [2, 768, 768], P('section'), may hold values from -0.875 to 0.875
- gain_mlp: float32 [2, 768], P('section'), may hold values from 0.5 to 1.5
- w_up: bfloat16 [2, 768, 3072], P('section'), may hold values from -0.21875 to 0.21875
- w_down: bfloat16 [2, 3072, 768], P('section'), may hold values from -0.109375 to 0.109375
- d_tokens: float32 [2, 4096, 768], P(None, 'dp'), may hold values from -6 to 6
- d_latents: float32 [2, 128, 768], P(None, 'dp'), may hold values from -6 to 6
Outputs:
- layer_tokens: float32 [2, 2, 4096, 768], P('section', None, 'dp')
- layer_latents: float32 [2, 2, 128, 768], P('section', None, 'dp')
- grad_tokens: float32 [2, 2, 4096, 768], P('section', None, 'dp')
- grad_latents: float32 [2, 2, 128, 768], P('section', None, 'dp')
- grad_gain_attn: float32 [2, 768], P('section', 'dp')
- grad_w_qkv: float32 [2, 768, 2304], P('section', None, 'dp')
- grad_w_out: float32 [2, 768, 768], P('section', None, 'dp')
- grad_gain_mlp: float32 [2, 768], P('section', 'dp')
- grad_w_up: float32 [2, 768, 3072], P('section', None, 'dp')
- grad_w_down: float32 [2, 3072, 768], P('section', None, 'dp')
The draws below stay inside these ranges and needn't reach their ends.
Inputs may be any that keep to these rules, and one draw needn't show every extreme that they name: `slot_group`: each micro-batch's row is a permutation of the 16 groups; slots go 1 to an index of dp in order. `image_groups`: each row sums to 16; its largest entry is exactly 8.
All inputs are finite; a program needn't handle non-finite values.
Results may differ from the reference program's by a relative error of at most 0.024.
Values may be sent and summed in bfloat16 or wider, within the bound.
A program may use at most 256 MiB of HBM per device.

```python
import math
import jax
import jax.numpy as jnp
import numpy as np
from jax import lax

D = 768
HEADS = 12
HEAD_DIM = 64
FF = 3072
GROUP = 256
LAT = 8
MICRO = 2
SLOTS = 16
TOKENS = 4096
LATS = 128
IMAGES = 4
MOSTG = 8


def spiked(entries, stream_key, source, target, shards_of, factor):
    def block_of(dim):
        return (jnp.arange(entries.shape[dim]) // (entries.shape[dim] // shards_of)).reshape((-1,) + (1,) * (entries.ndim - 1 - dim))

    first = jax.random.permutation(stream_key, shards_of)[block_of(target)]
    far = (block_of(target) + shards_of // 2) % shards_of
    return jnp.where((block_of(source) == first) | (block_of(source) == far), factor * entries, entries)


def shard_levels(rng, dims, shards, smallest, high):
    loudness = 1.0
    for axis_at, shards_of in shards:
        steps = jax.random.uniform(jax.random.fold_in(jax.random.fold_in(rng, 6), axis_at), (shards_of,), jnp.float32, smallest / len(shards), high / len(shards))
        loudness = loudness * jnp.repeat(jnp.exp(steps), dims[axis_at] // shards_of).reshape((-1,) + (1,) * (len(dims) - 1 - axis_at))
    return loudness


def split_up(number_of, total, bound, skew):
    loads = [(1 << 20) // math.isqrt(grade ** skew) + 1 for grade in range(2, number_of + 1)]
    spare, holding = total - bound - (number_of - 1), [1] * (number_of - 1)
    while spare > 0:
        free = [i for i in range(number_of - 1) if holding[i] < bound]
        whole, left = sum([loads[i] for i in free]), spare
        for i in free:
            more = min(bound - holding[i], max(1, left * loads[i] // whole), spare)
            holding[i] = holding[i] + more
            spare = spare - more
    return np.array([bound] + holding)


def uneven(rng, number_of, total, reach, skew):
    if number_of == 2:
        one = jax.random.randint(rng, (), max(1, total - reach), min(reach, total - 1) + 1)
        return jnp.stack([one, total - one])
    sizes = jnp.asarray(split_up(number_of, total, reach, skew), jnp.int32)
    twos = (number_of - 1) // 2
    source_of, sink = sizes[1:1 + 2 * twos:2], sizes[2:2 + 2 * twos:2]
    slack = jnp.minimum(source_of - 1, reach - sink)
    shifted = jax.random.randint(jax.random.fold_in(rng, 1), (twos,), 0, 1 << 20) % (slack + 1)
    sizes = sizes.at[1:1 + 2 * twos:2].set(source_of - shifted).at[2:2 + 2 * twos:2].set(sink + shifted)
    return sizes[jax.random.permutation(jax.random.fold_in(rng, 2), number_of)]


def bell_draw(rng, dims, spread, bound, pieces=(), held_as=jnp.bfloat16):
    factor_of = shard_levels(rng, dims, pieces, -0.22, 0.18) if pieces else 1.0
    entries = jax.random.normal(rng, dims, jnp.float32) * spread * factor_of
    return jnp.minimum(jnp.maximum(entries, -bound), bound).astype(held_as)


def gaussian_with(own_key, shape, deviation, most, split, heavy, held_as=jnp.bfloat16):
    drawn = deviation * jax.random.normal(own_key, shape, jnp.float32)
    if split:
        drawn = drawn * shard_levels(own_key, shape, split, -0.22, 0.18)
    return jnp.clip(spiked(drawn, jax.random.fold_in(own_key, 3), *heavy), -most, most).astype(held_as)


def setup_inputs(seed: int = 0) -> dict:
    key_of = jax.random.split(jax.random.key(seed), 13)
    tokens = bell_draw(key_of[0], (MICRO, TOKENS, D), 1.0, 6.0, ((1, 16),))
    latents = bell_draw(key_of[1], (MICRO, LATS, D), 1.0, 6.0, ((1, 16),))
    slot_group = jax.vmap(lambda own: jax.random.permutation(own, SLOTS))(jax.random.split(key_of[2], MICRO)).reshape((MICRO, SLOTS)).astype(jnp.int32)
    image_groups = jax.vmap(lambda own: uneven(own, IMAGES, SLOTS, MOSTG, 2))(jax.random.split(key_of[3], MICRO)).reshape((MICRO, IMAGES)).astype(jnp.int32)
    gain_attn = jnp.clip(1.0 + 0.1 * jax.random.normal(key_of[4], (2, D), jnp.float32), 0.5, 1.5)
    w_qkv = bell_draw(key_of[5], (2, D, 3 * D), D ** -0.5, 0.21875, ((0, 2),))
    w_out = bell_draw(key_of[6], (2, D, D), (D // 16) ** -0.5, 0.875, ((0, 2),))
    gain_mlp = jnp.clip(1.0 + 0.1 * jax.random.normal(key_of[7], (2, D), jnp.float32), 0.5, 1.5)
    w_up = bell_draw(key_of[8], (2, D, FF), D ** -0.5, 0.21875, ((0, 2),))
    w_down = bell_draw(key_of[9], (2, FF, D), FF ** -0.5, 0.109375, ((0, 2),))
    d_tokens = gaussian_with(key_of[10], (MICRO, TOKENS, D), 1.0, 6.0, ((1, 16),), (1, 2, 16, 2.0), jnp.float32)
    d_latents = bell_draw(key_of[11], (MICRO, LATS, D), 1.0, 6.0, ((1, 16),), jnp.float32)
    return {"tokens": tokens, "latents": latents, "slot_group": slot_group, "image_groups": image_groups, "gain_attn": gain_attn, "w_qkv": w_qkv, "w_out": w_out, "gain_mlp": gain_mlp, "w_up": w_up, "w_down": w_down, "d_tokens": d_tokens, "d_latents": d_latents}


epsilon = 1e-05
masked_score = -1e+30
highest = lax.Precision.HIGHEST

@jax.custom_vjp
def low(v):
    return lax.optimization_barrier(v.astype(jnp.bfloat16)).astype(jnp.float32)

@jax.custom_vjp
def low_back(v):
    return v

def low_keep(v):
    return (low(v), None)

def low_pass(kept, grad):
    return (grad,)

def back_keep(v):
    return (v, None)

def back_low(kept, grad):
    return (low(grad),)
low.defvjp(low_keep, low_pass)
low_back.defvjp(back_keep, back_low)

def layer_norm(values, gain):
    row_mean = lax.optimization_barrier(jnp.mean(values, axis=-1, keepdims=True))
    centred = values - row_mean
    row_var = lax.optimization_barrier(jnp.mean(centred * centred, axis=-1, keepdims=True))
    return centred * lax.rsqrt(row_var + epsilon) * gain

def rounded_both(value):
    return low_back(low(value))

def attend(queries, key_rows, value_rows, allowed):
    scores = low_back(jnp.einsum('qhd,khd->hqk', queries, key_rows, precision=highest) * HEAD_DIM ** (-0.5))
    weights = jax.nn.softmax(jnp.where(allowed[None], scores, masked_score), axis=-1)
    return jnp.einsum('hqk,khd->qhd', low(weights), value_rows, precision=highest)

def fit_layer(token_rows, latent_rows, params, global_layer, slot_images):
    gain_attn, w_qkv, w_out, gain_mlp, w_up, w_down = params
    grouped_tokens = token_rows.reshape(SLOTS, GROUP, D)
    grouped_latents = latent_rows.reshape(SLOTS, LAT, D)
    all_rows = jnp.concatenate([grouped_tokens, grouped_latents], axis=1)
    normed = low(layer_norm(all_rows, gain_attn))
    projected = rounded_both(jnp.einsum('sgd,de->sge', normed, w_qkv, precision=highest))
    split_heads = projected.reshape(SLOTS, GROUP + LAT, 3, HEADS, HEAD_DIM)
    queries = split_heads[:, :, 0]
    key_rows = split_heads[:, :, 1]
    value_rows = split_heads[:, :, 2]
    group_attend = jax.vmap(attend, in_axes=(0, 0, 0, None))
    if global_layer:
        token_mixed = group_attend(queries[:, :GROUP], key_rows[:, GROUP:], value_rows[:, GROUP:], jnp.ones((GROUP, LAT), jnp.bool_))
        latent_images = jnp.repeat(slot_images, LAT)
        same_image = latent_images[:, None] == latent_images[None, :]
        latent_mixed = attend(queries[:, GROUP:].reshape(LATS, HEADS, HEAD_DIM), key_rows[:, GROUP:].reshape(LATS, HEADS, HEAD_DIM), value_rows[:, GROUP:].reshape(LATS, HEADS, HEAD_DIM), same_image)
        mixed = jnp.concatenate([token_mixed, latent_mixed.reshape(SLOTS, LAT, HEADS, HEAD_DIM)], axis=1)
    else:
        mixed = group_attend(queries, key_rows, value_rows, jnp.ones((GROUP + LAT, GROUP + LAT), jnp.bool_))
    mixed_low = rounded_both(mixed.reshape(SLOTS, GROUP + LAT, D))
    mid_rows = all_rows + low_back(jnp.einsum('sgd,de->sge', mixed_low, w_out, precision=highest))
    normed_mlp = low(layer_norm(mid_rows, gain_mlp))
    up_proj = low_back(jnp.einsum('sgd,de->sge', normed_mlp, w_up, precision=highest))
    activated = low(jax.nn.gelu(up_proj))
    result = mid_rows + low_back(jnp.einsum('sgf,fd->sgd', activated, w_down, precision=highest))
    return (result[:, :GROUP].reshape(TOKENS, D), result[:, GROUP:].reshape(LATS, D))

def reference(tokens, latents, slot_group, image_groups, gain_attn, w_qkv, w_out, gain_mlp, w_up, w_down, d_tokens, d_latents):
    image_ends = jnp.cumsum(image_groups, axis=1).astype(jnp.int32)
    slot_images = lax.optimization_barrier(jnp.sum((image_ends[:, None, :] <= slot_group[:, :, None]).astype(jnp.int32), axis=2)).astype(jnp.int32)
    params = tuple((weight_array.astype(jnp.float32) for weight_array in (gain_attn, w_qkv, w_out, gain_mlp, w_up, w_down)))
    token_input = tokens.astype(jnp.float32)
    latent_input = latents.astype(jnp.float32)
    probe_tokens = jnp.zeros(tokens.shape, jnp.float32)
    probe_latents = jnp.zeros(latents.shape, jnp.float32)

    def forward(token_input, latent_input, probe_tokens, probe_latents, params):
        first = tuple((weight_array[0] for weight_array in params))
        second = tuple((weight_array[1] for weight_array in params))
        mids_tok, mids_lat, finals_tok, finals_lat = ([], [], [], [])
        for batch in range(MICRO):
            mid_tok, mid_lat = fit_layer(token_input[batch], latent_input[batch], first, False, slot_images[batch])
            mid_tok = rounded_both(mid_tok + probe_tokens[batch])
            mid_lat = rounded_both(mid_lat + probe_latents[batch])
            final_tok, final_lat = fit_layer(mid_tok, mid_lat, second, True, slot_images[batch])
            mids_tok.append(mid_tok)
            mids_lat.append(mid_lat)
            finals_tok.append(final_tok)
            finals_lat.append(final_lat)
        return ((jnp.stack(finals_tok), jnp.stack(finals_lat)), (jnp.stack(mids_tok), jnp.stack(mids_lat)))
    finals, back_fn, middles = jax.vjp(forward, token_input, latent_input, probe_tokens, probe_latents, params, has_aux=True)
    grad_tok, grad_lat, grad_probe_tok, grad_probe_lat, grad_params = back_fn((d_tokens.astype(jnp.float32), d_latents.astype(jnp.float32)))
    layer_tokens = jnp.stack([middles[0], finals[0]])
    layer_latents = jnp.stack([middles[1], finals[1]])
    grad_tokens = jnp.stack([grad_tok, grad_probe_tok])
    grad_latents = jnp.stack([grad_lat, grad_probe_lat])
    return (layer_tokens, layer_latents, grad_tokens, grad_latents, grad_params[0], grad_params[1], grad_params[2], grad_params[3], grad_params[4], grad_params[5])
```

```python
import functools

import jax
import jax.numpy as jnp
from jax import lax
from jax.experimental import pallas as pl
from jax.experimental.pallas import tpu as pltpu
from jax.sharding import PartitionSpec as P

HEADS = 12
GROUP = 256
LAT = 8


epsilon = 1e-05
masked_score = -1e30


MESH = pl.DeviceIdType.MESH


def grid_of(mesh):
    n = mesh.shape["dp"]
    coords = [getattr(d, "coords", None) for d in mesh.devices.reshape(n, -1)[:, 0]]
    if any(c is None for c in coords):
        return (n // 4, 2, 2) if n % 4 == 0 else (n, 1, 1)
    sizes = {a: len({c[a] for c in coords}) for a in range(3)}
    strides = {
        a: min([i for i in range(n) if coords[i][a] != coords[0][a]], default=n) for a in range(3)
    }
    order = sorted(range(3), key=lambda a: -strides[a])
    return tuple(sizes[a] for a in order)


def spread_kernel(grid, pairs, g_ref, gain_ref, out_ref, gout_ref, *scratch):
    acc = scratch[0:3]
    land = [scratch[3 + 3 * i : 6 + 3 * i] for i in range(3)]
    send_sem, recv_sem, own_sem = scratch[12:15]
    me = lax.axis_index("dp")
    section = lax.axis_index("section")
    l0, l1, l2 = grid
    here = (me // (l1 * l2), lax.rem(me // l2, l1), lax.rem(me, l2))

    def device(axis, shift):
        there = list(here)
        there[axis] = lax.rem(here[axis] + shift, grid[axis])
        return there[axis], ((there[0] * l1 + there[1]) * l2 + there[2], section)

    barrier = pltpu.get_barrier_semaphore()
    for axis in range(3):
        for shift in range(1, grid[axis]):
            pl.semaphore_signal(
                barrier, inc=1, device_id=device(axis, shift)[1], device_id_type=MESH
            )
    pl.semaphore_wait(barrier, sum(grid) - 3)

    orders = ((2, 1, 0), (1, 2, 0), (2, 1, 0))

    def source(stream, phase, k, at):
        if phase == 0:
            if stream == 0:
                return g_ref.at[2 * k, :, :, at]
            if stream == 1:
                return g_ref.at[2 * k + 1, :, at]
            return gain_ref.at[:, :, at]
        if phase == 1:
            return acc[stream].at[k, :, at]
        return acc[stream].at[k, at, here[orders[stream][1]]]

    def copies(stream, phase, k):
        axis = orders[stream][phase]
        for shift in range(1, grid[axis]):
            at, target = device(axis, shift)
            yield pltpu.make_async_remote_copy(
                src_ref=source(stream, phase, k, at),
                dst_ref=land[phase][stream].at[k, shift - 1],
                send_sem=send_sem.at[stream, phase, k, shift - 1],
                recv_sem=recv_sem.at[stream, phase, k, shift - 1],
                device_id=target,
                device_id_type=MESH,
            )

    def own(stream, k):
        return pltpu.make_async_copy(
            source(stream, 0, k, here[orders[stream][0]]), acc[stream].at[k], own_sem.at[stream, k]
        )

    def launch(stream, phase, k):
        for copy in copies(stream, phase, k):
            copy.start()

    def absorb(stream, phase, k):
        axis = orders[stream][phase]
        if phase == 0:
            own(stream, k).wait()
        for copy in copies(stream, phase, k):
            copy.wait_recv()
        into = land[phase][stream]
        count = grid[axis] - 1
        if phase == 0:
            for a in range(acc[stream].shape[1]):
                for b in range(acc[stream].shape[2]):
                    total = acc[stream][k, a, b].astype(jnp.float32)
                    for s in range(count):
                        total += into[k, s, a, b].astype(jnp.float32)
                    acc[stream][k, a, b] = total.astype(acc[stream].dtype)
        elif phase == 1:
            mine = here[axis]
            for a in range(acc[stream].shape[1]):
                total = acc[stream][k, a, mine].astype(jnp.float32)
                for s in range(count):
                    total += into[k, s, a].astype(jnp.float32)
                acc[stream][k, a, mine] = total.astype(acc[stream].dtype)
        else:
            total = acc[stream][k, here[0], here[orders[stream][1]]].astype(jnp.float32)
            for s in range(count):
                total += into[k, s].astype(jnp.float32)
            if stream < 2:
                out_ref[2 * k + stream] = total
            else:
                gout_ref[...] = total

    own(2, 0).start()
    launch(2, 0, 0)

    def start_own(k, carry):
        for stream in (0, 1):
            own(stream, k).start()
        return carry

    for stream in (0, 1):
        launch(stream, 0, 0)
    lax.fori_loop(0, pairs, start_own, 0)

    def turn(t, carry):
        @pl.when(t + 1 < pairs)
        def _():
            for stream in (0, 1):
                launch(stream, 0, t + 1)

        @pl.when(t < pairs)
        def _():
            for stream in (0, 1):
                absorb(stream, 0, t)
                launch(stream, 1, t)

        @pl.when((t >= 1) & (t - 1 < pairs))
        def _():
            for stream in (0, 1):
                absorb(stream, 1, t - 1)
                launch(stream, 2, t - 1)

        @pl.when(t >= 2)
        def _():
            for stream in (0, 1):
                absorb(stream, 2, t - 2)

        return carry

    lax.fori_loop(0, pairs + 2, turn, 0)
    absorb(2, 0, 0)
    launch(2, 1, 0)
    absorb(2, 1, 0)
    launch(2, 2, 0)
    absorb(2, 2, 0)

    def finish(k, carry):
        for stream in (0, 1):
            for phase in range(3):
                for copy in copies(stream, phase, k):
                    copy.wait_send()
        return carry

    lax.fori_loop(0, pairs, finish, 0)
    for phase in range(3):
        for copy in copies(2, phase, 0):
            copy.wait_send()


def spread(grid, grads, gains):
    chunks, n, rows, width = grads.shape
    pairs = chunks // 2
    l0, l1, l2 = grid
    most = max(max(grid) - 1, 1)
    low = jnp.bfloat16
    shapes = ((pairs, rows, width, low), (pairs, rows, width, low), (1, 8, 128, jnp.float32))
    inner = ((l1, l2), (l2, l1), (l1, l2))
    acc, first, second, third = [], [], [], []
    for (count, r, w, dt), (kept, sent) in zip(shapes, inner):
        acc.append(pltpu.VMEM((count, l0, kept, r, w), dt))
        first.append(pltpu.VMEM((count, max(sent - 1, 1), l0, kept, r, w), dt))
        second.append(pltpu.VMEM((count, max(kept - 1, 1), l0, r, w), dt))
        third.append(pltpu.VMEM((count, max(l0 - 1, 1), r, w), dt))
    return pl.pallas_call(
        functools.partial(spread_kernel, grid, pairs),
        out_shape=(
            jax.ShapeDtypeStruct((chunks, rows, width), jnp.float32),
            jax.ShapeDtypeStruct((8, 128), jnp.float32),
        ),
        in_specs=[pl.BlockSpec(memory_space=pl.ANY)] * 2,
        out_specs=(pl.BlockSpec(memory_space=pltpu.VMEM),) * 2,
        scratch_shapes=acc
        + first
        + second
        + third
        + [
            pltpu.SemaphoreType.DMA((3, 3, pairs, most)),
            pltpu.SemaphoreType.DMA((3, 3, pairs, most)),
            pltpu.SemaphoreType.DMA((3, pairs)),
        ],
        compiler_params=pltpu.CompilerParams(
            collective_id=0, has_side_effects=True, vmem_limit_bytes=60 * 1024 * 1024
        ),
        cost_estimate=pl.CostEstimate(flops=0, bytes_accessed=grads.size * 4, transcendentals=0),
    )(grads.reshape(chunks, l0, l1, l2, rows, width), gains.reshape(l0, l1, l2, 8, 128))


def from_behind(x, axis, by):
    devices = lax.axis_size(axis)
    pairs = [(i, i + by) for i in range(devices) if 0 <= i + by < devices]
    return lax.ppermute(x, axis, pairs)


def layer_norm(values, gain):
    row_mean = jnp.mean(values, axis=-1, keepdims=True)
    centred = values - row_mean
    row_var = jnp.mean(centred * centred, axis=-1, keepdims=True)
    return centred * lax.rsqrt(row_var + epsilon) * gain


def front_half(all_rows, gain_attn, w_qkv):
    normed = layer_norm(all_rows, gain_attn).astype(jnp.bfloat16)
    projected = jnp.dot(normed, w_qkv, preferred_element_type=jnp.float32).astype(jnp.bfloat16)
    return (normed, projected)


def latent_operand(projected, tok_rows, model_width):
    return projected[tok_rows:, model_width:]


def back_half(all_rows, projected, remote_rows, allowed, weights):
    gain_attn, w_qkv, w_out, gain_mlp, w_up, w_down = weights
    row_count, model_width = all_rows.shape
    head_size = model_width // HEADS
    remote_pairs = remote_rows[:, remote_rows.shape[1] - 2 * model_width :]
    queries = projected[:, :model_width].reshape(row_count, HEADS, head_size)
    key_rows = jnp.concatenate(
        [projected[:, model_width : 2 * model_width], remote_pairs[:, :model_width]], axis=0
    )
    value_rows = jnp.concatenate(
        [projected[:, 2 * model_width :], remote_pairs[:, model_width:]], axis=0
    )
    key_rows = key_rows.reshape(-1, HEADS, head_size)
    value_rows = value_rows.reshape(-1, HEADS, head_size)
    scores = jnp.einsum(
        "qhd,khd->hqk", queries, key_rows, preferred_element_type=jnp.float32
    ) * head_size ** (-0.5)
    attn_weights = jax.nn.softmax(jnp.where(allowed[None], scores, masked_score), axis=-1)
    attn_low = attn_weights.astype(jnp.bfloat16)
    mixed_low = jnp.einsum("hqk,khd->qhd", attn_low, value_rows, preferred_element_type=jnp.float32)
    mixed_low = mixed_low.reshape(row_count, model_width).astype(jnp.bfloat16)
    mid_rows = all_rows + jnp.dot(mixed_low, w_out, preferred_element_type=jnp.float32)
    normed_mlp = layer_norm(mid_rows, gain_mlp).astype(jnp.bfloat16)
    up_proj = jnp.dot(normed_mlp, w_up, preferred_element_type=jnp.float32)
    activated = jax.nn.gelu(up_proj).astype(jnp.bfloat16)
    result = mid_rows + jnp.dot(activated, w_down, preferred_element_type=jnp.float32)
    return dict(
        queries=queries,
        key_rows=key_rows,
        value_rows=value_rows,
        attn_weights=attn_weights,
        attn_low=attn_low,
        mixed_low=mixed_low,
        mid_rows=mid_rows,
        normed_mlp=normed_mlp,
        up_proj=up_proj,
        activated=activated,
        result=result,
    )


def section_backward(saved, d_result, all_rows, normed, allowed, weights, latent_start):
    gain_attn, w_qkv, w_out, gain_mlp, w_up, w_down = weights
    row_count, model_width = all_rows.shape
    head_size = model_width // HEADS
    score_scale = head_size ** (-0.5)
    d_low = d_result.astype(jnp.bfloat16)
    grad_down = jnp.dot(d_low.T, saved["activated"], preferred_element_type=jnp.float32)
    d_activated = jnp.dot(d_low, w_down.T, preferred_element_type=jnp.float32)
    unused_up, gelu_back = jax.vjp(jax.nn.gelu, saved["up_proj"])
    d_up = gelu_back(d_activated)[0].astype(jnp.bfloat16)
    grad_up = jnp.dot(d_up.T, saved["normed_mlp"], preferred_element_type=jnp.float32)
    d_normed_mlp = jnp.dot(d_up, w_up.T, preferred_element_type=jnp.float32)
    unused_mid, second_back = jax.vjp(layer_norm, saved["mid_rows"], gain_mlp)
    d_mid_norm, grad_gain_mlp = second_back(d_normed_mlp)
    d_mid = d_result + d_mid_norm
    d_mid_low = d_mid.astype(jnp.bfloat16)
    grad_out = jnp.dot(d_mid_low.T, saved["mixed_low"], preferred_element_type=jnp.float32)
    d_mixed = jnp.dot(d_mid_low, w_out.T, preferred_element_type=jnp.float32).astype(jnp.bfloat16)
    d_mixed = d_mixed.reshape(row_count, HEADS, head_size)
    d_weights = jnp.einsum(
        "qhd,khd->hqk", d_mixed, saved["value_rows"], preferred_element_type=jnp.float32
    )
    d_values = jnp.einsum(
        "hqk,qhd->khd", saved["attn_low"], d_mixed, preferred_element_type=jnp.float32
    )
    attn_weights = saved["attn_weights"]
    d_scores = attn_weights * (
        d_weights - jnp.sum(attn_weights * d_weights, axis=-1, keepdims=True)
    )
    d_scores_low = jnp.where(allowed[None], d_scores, 0.0).astype(jnp.bfloat16)
    d_queries = (
        jnp.einsum(
            "hqk,khd->qhd", d_scores_low, saved["key_rows"], preferred_element_type=jnp.float32
        )
        * score_scale
    )
    d_keys = (
        jnp.einsum(
            "hqk,qhd->khd", d_scores_low, saved["queries"], preferred_element_type=jnp.float32
        )
        * score_scale
    )
    remote_part = jnp.concatenate(
        [
            d_keys[row_count:].reshape(-1, model_width),
            d_values[row_count:].reshape(-1, model_width),
        ],
        axis=1,
    )
    own_part = lax.psum_scatter(remote_part, "dp", scatter_dimension=0, tiled=True)
    local_pairs = jnp.concatenate(
        [
            d_keys[:row_count].reshape(row_count, model_width),
            d_values[:row_count].reshape(row_count, model_width),
        ],
        axis=1,
    )
    local_pairs = jnp.concatenate(
        [local_pairs[:latent_start], local_pairs[latent_start:] + own_part], axis=0
    )
    d_projected = jnp.concatenate(
        [d_queries.reshape(row_count, model_width), local_pairs], axis=1
    ).astype(jnp.bfloat16)
    grad_qkv = jnp.dot(d_projected.T, normed, preferred_element_type=jnp.float32)
    d_normed = jnp.dot(d_projected, w_qkv.T, preferred_element_type=jnp.float32)
    unused_rows, first_back = jax.vjp(layer_norm, all_rows, gain_attn)
    d_rows_norm, grad_gain_attn = first_back(d_normed)
    return (
        d_mid + d_rows_norm,
        (grad_gain_attn, grad_qkv, grad_out, grad_gain_mlp, grad_up, grad_down),
    )


def packed(grads, n):
    gain_first, qkv_grad, out_grad, gain_second, up_grad, down_grad = grads
    width = out_grad.shape[0]
    rows = width // n

    def by_rows(grad):
        return grad.reshape(n, -1, rows, width).transpose(1, 0, 2, 3).astype(jnp.bfloat16)

    down = down_grad.reshape(n, rows, -1, width).transpose(2, 0, 1, 3).astype(jnp.bfloat16)
    chunks = jnp.concatenate([down, by_rows(up_grad), by_rows(out_grad), by_rows(qkv_grad)], axis=0)
    gains = jnp.stack([gain_first.reshape(n, rows), gain_second.reshape(n, rows)], axis=1)
    return chunks, jnp.pad(gains, ((0, 0), (0, 6), (0, 128 - rows)))


def shards(
    grid,
    tokens,
    latents,
    slot_group,
    image_groups,
    gain_attn,
    w_qkv,
    w_out,
    gain_mlp,
    w_up,
    w_down,
    d_tokens,
    d_latents,
):
    micro = tokens.shape[0]
    tok_rows = tokens.shape[1]
    lat_rows = latents.shape[1]
    model_width = tokens.shape[2]
    local_groups = tok_rows // GROUP
    section_index = lax.axis_index("section")
    is_global = section_index == 1
    dp_index = lax.axis_index("dp")
    weights = (gain_attn[0], w_qkv[0], w_out[0], gain_mlp[0], w_up[0], w_down[0])
    image_ends = jnp.cumsum(image_groups, axis=1)
    slot_images = jnp.sum(
        (image_ends[:, None, :] <= slot_group[:, :, None]).astype(jnp.int32), axis=2
    )
    slot_total = slot_group.shape[1]
    row_group = jnp.concatenate([jnp.arange(tok_rows) // GROUP, jnp.arange(lat_rows) // LAT])
    row_latent = jnp.concatenate(
        [jnp.zeros((tok_rows,), jnp.bool_), jnp.ones((lat_rows,), jnp.bool_)]
    )
    same_group = row_group[:, None] == row_group[None, :]
    local_mask = jnp.where(
        is_global, (~row_latent)[:, None] & row_latent[None, :] & same_group, same_group
    )
    group_match = row_group[:, None] == jnp.arange(local_groups)[None, :]

    def key_images(batch):
        images_row = lax.dynamic_index_in_dim(slot_images, batch, 0, keepdims=False)
        return (images_row, jnp.broadcast_to(images_row[:, None], (slot_total, LAT)).reshape(-1))

    def allowed_for(batch):
        images_row, key_image = key_images(batch)
        own_images = lax.dynamic_slice_in_dim(images_row, dp_index * local_groups, local_groups)
        row_image = jnp.sum(jnp.where(group_match, own_images[None, :], 0), axis=1)
        remote_mask = is_global & row_latent[:, None] & (row_image[:, None] == key_image[None, :])
        return jnp.concatenate([local_mask, remote_mask], axis=1)

    recv_tokens = jnp.zeros((tok_rows, model_width), jnp.bfloat16)
    recv_latents = jnp.zeros((lat_rows, model_width), jnp.bfloat16)
    kept_rows, kept_pairs, tok_outputs, lat_outputs = ([], [], [], [])
    for turn in range(micro + 1):
        batch = jnp.clip(turn - section_index, 0, micro - 1)
        own_tok = lax.dynamic_index_in_dim(tokens, batch, 0, keepdims=False)
        own_lat = lax.dynamic_index_in_dim(latents, batch, 0, keepdims=False)
        input_rows = jnp.concatenate(
            [
                jnp.where(is_global, recv_tokens, own_tok),
                jnp.where(is_global, recv_latents, own_lat),
            ],
            axis=0,
        )
        all_rows = input_rows.astype(jnp.float32)
        normed, projected = front_half(all_rows, weights[0], weights[1])
        remote_rows = lax.all_gather(
            latent_operand(projected, tok_rows, model_width), "dp", axis=0, tiled=True
        )
        saved = back_half(all_rows, projected, remote_rows, allowed_for(batch), weights)
        result = saved["result"]
        result_low = result.astype(jnp.bfloat16)
        stored = jnp.where(is_global, result, result_low.astype(jnp.float32))
        kept_rows.append(input_rows)
        kept_pairs.append(remote_rows)
        tok_outputs.append(stored[:tok_rows])
        lat_outputs.append(stored[tok_rows:])
        if turn < micro:
            recv_tokens, recv_latents = from_behind(
                (result_low[:tok_rows], result_low[tok_rows:]), "section", 1
            )
    kept_rows = jnp.stack(kept_rows)
    kept_pairs = jnp.stack(kept_pairs)
    totals = tuple(
        jnp.zeros(w.shape[::-1] if w.ndim == 2 else w.shape, jnp.float32) for w in weights
    )
    recv_grad_tok = jnp.zeros((tok_rows, model_width), jnp.bfloat16)
    recv_grad_lat = jnp.zeros((lat_rows, model_width), jnp.bfloat16)
    tok_grads, lat_grads = ([], [])
    for turn in range(micro + 1):
        raw_batch = micro - turn - section_index
        valid = ((raw_batch >= 0) & (raw_batch < micro)).astype(jnp.float32)
        batch = jnp.clip(raw_batch, 0, micro - 1)
        all_rows = lax.dynamic_index_in_dim(
            kept_rows, batch + section_index, 0, keepdims=False
        ).astype(jnp.float32)
        normed, projected = front_half(all_rows, weights[0], weights[1])
        remote_rows = lax.all_gather(
            latent_operand(projected, tok_rows, model_width), "dp", axis=0, tiled=True
        )
        allowed = allowed_for(batch)
        saved = back_half(all_rows, projected, remote_rows, allowed, weights)
        given = (
            jnp.concatenate(
                [
                    lax.dynamic_index_in_dim(d_tokens, batch, 0, keepdims=False),
                    lax.dynamic_index_in_dim(d_latents, batch, 0, keepdims=False),
                ],
                axis=0,
            )
            * valid
        )
        passed = jnp.concatenate([recv_grad_tok, recv_grad_lat], axis=0).astype(jnp.float32)
        d_result = jnp.where(is_global, given, passed)
        d_rows, grads = section_backward(
            saved, d_result, all_rows, normed, allowed, weights, tok_rows
        )
        totals = tuple((accum + piece for accum, piece in zip(totals, grads)))
        d_rows_low = d_rows.astype(jnp.bfloat16)
        stored = jnp.where(is_global, d_rows_low.astype(jnp.float32), d_rows)
        tok_grads.append(stored[:tok_rows])
        lat_grads.append(stored[tok_rows:])
        if turn < micro:
            recv_grad_tok, recv_grad_lat = from_behind(
                (d_rows_low[:tok_rows], d_rows_low[tok_rows:]), "section", -1
            )
    chunks, gains = packed(totals, lax.axis_size("dp"))
    summed, gain_sums = spread(grid, chunks, gains)
    rows = summed.shape[1]
    layer_tokens = lax.dynamic_slice_in_dim(jnp.stack(tok_outputs), section_index, micro, 0)[None]
    layer_latents = lax.dynamic_slice_in_dim(jnp.stack(lat_outputs), section_index, micro, 0)[None]
    grad_tokens = lax.dynamic_slice_in_dim(jnp.stack(tok_grads), 1 - section_index, micro, 0)[::-1][
        None
    ]
    grad_latents = lax.dynamic_slice_in_dim(jnp.stack(lat_grads), 1 - section_index, micro, 0)[
        ::-1
    ][None]
    return (
        layer_tokens,
        layer_latents,
        grad_tokens,
        grad_latents,
        gain_sums[0:1, :rows],
        summed[9:].reshape(-1, model_width).T[None],
        summed[8].T[None],
        gain_sums[1:2, :rows],
        summed[4:8].reshape(-1, model_width).T[None],
        summed[0:4].transpose(0, 2, 1).reshape(-1, rows)[None],
    )


def solution(mesh):
    in_specs = (
        P(None, "dp", None),
        P(None, "dp", None),
        P(),
        P(),
        P("section", None),
        P("section", None, None),
        P("section", None, None),
        P("section", None),
        P("section", None, None),
        P("section", None, None),
        P(None, "dp", None),
        P(None, "dp", None),
    )
    out_specs = (
        P("section", None, "dp", None),
        P("section", None, "dp", None),
        P("section", None, "dp", None),
        P("section", None, "dp", None),
        P("section", "dp"),
        P("section", None, "dp"),
        P("section", None, "dp"),
        P("section", "dp"),
        P("section", None, "dp"),
        P("section", None, "dp"),
    )
    return jax.shard_map(
        functools.partial(shards, grid_of(mesh)), mesh=mesh, in_specs=in_specs, out_specs=out_specs, check_vma=False)
```

```python
import functools

import jax
import jax.numpy as jnp
from jax import lax
from jax.experimental import pallas as pl
from jax.experimental.pallas import tpu as pltpu
from jax.sharding import PartitionSpec as P

HEADS = 12
GROUP = 256
LAT = 8


epsilon = 1e-05
masked_score = -1e30


MESH = pl.DeviceIdType.MESH


def grid_of(mesh):
    n = mesh.shape["dp"]
    coords = [getattr(d, "coords", None) for d in mesh.devices.reshape(n, -1)[:, 0]]
    if any(c is None for c in coords):
        return (n // 4, 2, 2) if n % 4 == 0 else (n, 1, 1)
    sizes = {a: len({c[a] for c in coords}) for a in range(3)}
    strides = {
        a: min([i for i in range(n) if coords[i][a] != coords[0][a]], default=n) for a in range(3)
    }
    order = sorted(range(3), key=lambda a: -strides[a])
    return tuple(sizes[a] for a in order)


def spread_kernel(grid, pairs, g_ref, gain_ref, out_ref, gout_ref, *scratch):
    acc = scratch[0:3]
    land = [scratch[3 + 3 * i : 6 + 3 * i] for i in range(3)]
    send_sem, recv_sem, own_sem = scratch[12:15]
    me = lax.axis_index("dp")
    section = lax.axis_index("section")
    l0, l1, l2 = grid
    here = (me // (l1 * l2), lax.rem(me // l2, l1), lax.rem(me, l2))

    def device(axis, shift):
        there = list(here)
        there[axis] = lax.rem(here[axis] + shift, grid[axis])
        return there[axis], ((there[0] * l1 + there[1]) * l2 + there[2], section)

    barrier = pltpu.get_barrier_semaphore()
    for axis in range(3):
        for shift in range(1, grid[axis]):
            pl.semaphore_signal(
                barrier, inc=1, device_id=device(axis, shift)[1], device_id_type=MESH
            )
    pl.semaphore_wait(barrier, sum(grid) - 3)

    orders = ((2, 1, 0), (1, 2, 0), (2, 1, 0))

    def source(stream, phase, k, at):
        if phase == 0:
            if stream == 0:
                return g_ref.at[2 * k, :, :, at]
            if stream == 1:
                return g_ref.at[2 * k + 1, :, at]
            return gain_ref.at[:, :, at]
        if phase == 1:
            return acc[stream].at[k, :, at]
        return acc[stream].at[k, at, here[orders[stream][1]]]

    def copies(stream, phase, k):
        axis = orders[stream][phase]
        for shift in range(1, grid[axis]):
            at, target = device(axis, shift)
            yield pltpu.make_async_remote_copy(
                src_ref=source(stream, phase, k, at),
                dst_ref=land[phase][stream].at[k, shift - 1],
                send_sem=send_sem.at[stream, phase, k, shift - 1],
                recv_sem=recv_sem.at[stream, phase, k, shift - 1],
                device_id=target,
                device_id_type=MESH,
            )

    def own(stream, k):
        return pltpu.make_async_copy(
            source(stream, 0, k, here[orders[stream][0]]), acc[stream].at[k], own_sem.at[stream, k]
        )

    def launch(stream, phase, k):
        for copy in copies(stream, phase, k):
            copy.start()

    def absorb(stream, phase, k):
        axis = orders[stream][phase]
        if phase == 0:
            own(stream, k).wait()
        for copy in copies(stream, phase, k):
            copy.wait_recv()
        into = land[phase][stream]
        count = grid[axis] - 1
        if phase == 0:
            for a in range(acc[stream].shape[1]):
                for b in range(acc[stream].shape[2]):
                    total = acc[stream][k, a, b].astype(jnp.float32)
                    for s in range(count):
                        total += into[k, s, a, b].astype(jnp.float32)
                    acc[stream][k, a, b] = total.astype(acc[stream].dtype)
        elif phase == 1:
            mine = here[axis]
            for a in range(acc[stream].shape[1]):
                total = acc[stream][k, a, mine].astype(jnp.float32)
                for s in range(count):
                    total += into[k, s, a].astype(jnp.float32)
                acc[stream][k, a, mine] = total.astype(acc[stream].dtype)
        else:
            total = acc[stream][k, here[0], here[orders[stream][1]]].astype(jnp.float32)
            for s in range(count):
                total += into[k, s].astype(jnp.float32)
            if stream < 2:
                out_ref[2 * k + stream] = total
            else:
                gout_ref[...] = total

    own(2, 0).start()
    launch(2, 0, 0)

    def start_own(k, carry):
        for stream in (0, 1):
            own(stream, k).start()
        return carry

    for stream in (0, 1):
        launch(stream, 0, 0)
    lax.fori_loop(0, pairs, start_own, 0)

    def turn(t, carry):
        @pl.when(t + 1 < pairs)
        def _():
            for stream in (0, 1):
                launch(stream, 0, t + 1)

        @pl.when(t < pairs)
        def _():
            for stream in (0, 1):
                absorb(stream, 0, t)
                launch(stream, 1, t)

        @pl.when((t >= 1) & (t - 1 < pairs))
        def _():
            for stream in (0, 1):
                absorb(stream, 1, t - 1)
                launch(stream, 2, t - 1)

        @pl.when(t >= 2)
        def _():
            for stream in (0, 1):
                absorb(stream, 2, t - 2)

        return carry

    lax.fori_loop(0, pairs + 2, turn, 0)
    absorb(2, 0, 0)
    launch(2, 1, 0)
    absorb(2, 1, 0)
    launch(2, 2, 0)
    absorb(2, 2, 0)

    def finish(k, carry):
        for stream in (0, 1):
            for phase in range(3):
                for copy in copies(stream, phase, k):
                    copy.wait_send()
        return carry

    lax.fori_loop(0, pairs, finish, 0)
    for phase in range(3):
        for copy in copies(2, phase, 0):
            copy.wait_send()


def spread(grid, grads, gains):
    chunks, n, rows, width = grads.shape
    pairs = chunks // 2
    l0, l1, l2 = grid
    most = max(max(grid) - 1, 1)
    low = jnp.bfloat16
    shapes = ((pairs, rows, width, low), (pairs, rows, width, low), (1, 8, 128, jnp.float32))
    inner = ((l1, l2), (l2, l1), (l1, l2))
    acc, first, second, third = [], [], [], []
    for (count, r, w, dt), (kept, sent) in zip(shapes, inner):
        acc.append(pltpu.VMEM((count, l0, kept, r, w), dt))
        first.append(pltpu.VMEM((count, max(sent - 1, 1), l0, kept, r, w), dt))
        second.append(pltpu.VMEM((count, max(kept - 1, 1), l0, r, w), dt))
        third.append(pltpu.VMEM((count, max(l0 - 1, 1), r, w), dt))
    return pl.pallas_call(
        functools.partial(spread_kernel, grid, pairs),
        out_shape=(
            jax.ShapeDtypeStruct((chunks, rows, width), jnp.float32),
            jax.ShapeDtypeStruct((8, 128), jnp.float32),
        ),
        in_specs=[pl.BlockSpec(memory_space=pl.ANY)] * 2,
        out_specs=(pl.BlockSpec(memory_space=pltpu.VMEM),) * 2,
        scratch_shapes=acc
        + first
        + second
        + third
        + [
            pltpu.SemaphoreType.DMA((3, 3, pairs, most)),
            pltpu.SemaphoreType.DMA((3, 3, pairs, most)),
            pltpu.SemaphoreType.DMA((3, pairs)),
        ],
        compiler_params=pltpu.CompilerParams(
            collective_id=0, has_side_effects=True, vmem_limit_bytes=60 * 1024 * 1024
        ),
        cost_estimate=pl.CostEstimate(flops=0, bytes_accessed=grads.size * 4, transcendentals=0),
    )(grads.reshape(chunks, l0, l1, l2, rows, width), gains.reshape(l0, l1, l2, 8, 128))


def from_behind(x, axis, by):
    devices = lax.axis_size(axis)
    pairs = [(i, i + by) for i in range(devices) if 0 <= i + by < devices]
    return lax.ppermute(x, axis, pairs)


def layer_norm(values, gain):
    row_mean = jnp.mean(values, axis=-1, keepdims=True)
    centred = values - row_mean
    row_var = jnp.mean(centred * centred, axis=-1, keepdims=True)
    return centred * lax.rsqrt(row_var + epsilon) * gain


def front_half(all_rows, gain_attn, w_qkv):
    normed = layer_norm(all_rows, gain_attn).astype(jnp.bfloat16)
    projected = jnp.dot(normed, w_qkv, preferred_element_type=jnp.float32).astype(jnp.bfloat16)
    return (normed, projected)


def latent_operand(projected, tok_rows, model_width):
    return projected[tok_rows:, model_width:]


def back_half(all_rows, projected, remote_rows, allowed, weights):
    gain_attn, w_qkv, w_out, gain_mlp, w_up, w_down = weights
    row_count, model_width = all_rows.shape
    head_size = model_width // HEADS
    remote_pairs = remote_rows[:, remote_rows.shape[1] - 2 * model_width :]
    queries = projected[:, :model_width].reshape(row_count, HEADS, head_size)
    key_rows = jnp.concatenate(
        [projected[:, model_width : 2 * model_width], remote_pairs[:, :model_width]], axis=0
    )
    value_rows = jnp.concatenate(
        [projected[:, 2 * model_width :], remote_pairs[:, model_width:]], axis=0
    )
    key_rows = key_rows.reshape(-1, HEADS, head_size)
    value_rows = value_rows.reshape(-1, HEADS, head_size)
    scores = jnp.einsum(
        "qhd,khd->hqk", queries, key_rows, preferred_element_type=jnp.float32
    ) * head_size ** (-0.5)
    attn_weights = jax.nn.softmax(jnp.where(allowed[None], scores, masked_score), axis=-1)
    attn_low = attn_weights.astype(jnp.bfloat16)
    mixed_low = jnp.einsum("hqk,khd->qhd", attn_low, value_rows, preferred_element_type=jnp.float32)
    mixed_low = mixed_low.reshape(row_count, model_width).astype(jnp.bfloat16)
    mid_rows = all_rows + jnp.dot(mixed_low, w_out, preferred_element_type=jnp.float32)
    normed_mlp = layer_norm(mid_rows, gain_mlp).astype(jnp.bfloat16)
    up_proj = jnp.dot(normed_mlp, w_up, preferred_element_type=jnp.float32)
    activated = jax.nn.gelu(up_proj).astype(jnp.bfloat16)
    result = mid_rows + jnp.dot(activated, w_down, preferred_element_type=jnp.float32)
    return dict(
        queries=queries,
        key_rows=key_rows,
        value_rows=value_rows,
        attn_weights=attn_weights,
        attn_low=attn_low,
        mixed_low=mixed_low,
        mid_rows=mid_rows,
        normed_mlp=normed_mlp,
        up_proj=up_proj,
        activated=activated,
        result=result,
    )


def section_backward(saved, d_result, all_rows, normed, allowed, weights, latent_start):
    gain_attn, w_qkv, w_out, gain_mlp, w_up, w_down = weights
    row_count, model_width = all_rows.shape
    head_size = model_width // HEADS
    score_scale = head_size ** (-0.5)
    d_low = d_result.astype(jnp.bfloat16)
    grad_down = jnp.dot(d_low.T, saved["activated"], preferred_element_type=jnp.float32)
    d_activated = jnp.dot(d_low, w_down.T, preferred_element_type=jnp.float32)
    unused_up, gelu_back = jax.vjp(jax.nn.gelu, saved["up_proj"])
    d_up = gelu_back(d_activated)[0].astype(jnp.bfloat16)
    grad_up = jnp.dot(d_up.T, saved["normed_mlp"], preferred_element_type=jnp.float32)
    d_normed_mlp = jnp.dot(d_up, w_up.T, preferred_element_type=jnp.float32)
    unused_mid, second_back = jax.vjp(layer_norm, saved["mid_rows"], gain_mlp)
    d_mid_norm, grad_gain_mlp = second_back(d_normed_mlp)
    d_mid = d_result + d_mid_norm
    d_mid_low = d_mid.astype(jnp.bfloat16)
    grad_out = jnp.dot(d_mid_low.T, saved["mixed_low"], preferred_element_type=jnp.float32)
    d_mixed = jnp.dot(d_mid_low, w_out.T, preferred_element_type=jnp.float32).astype(jnp.bfloat16)
    d_mixed = d_mixed.reshape(row_count, HEADS, head_size)
    d_weights = jnp.einsum(
        "qhd,khd->hqk", d_mixed, saved["value_rows"], preferred_element_type=jnp.float32
    )
    d_values = jnp.einsum(
        "hqk,qhd->khd", saved["attn_low"], d_mixed, preferred_element_type=jnp.float32
    )
    attn_weights = saved["attn_weights"]
    d_scores = attn_weights * (
        d_weights - jnp.sum(attn_weights * d_weights, axis=-1, keepdims=True)
    )
    d_scores_low = jnp.where(allowed[None], d_scores, 0.0).astype(jnp.bfloat16)
    d_queries = (
        jnp.einsum(
            "hqk,khd->qhd", d_scores_low, saved["key_rows"], preferred_element_type=jnp.float32
        )
        * score_scale
    )
    d_keys = (
        jnp.einsum(
            "hqk,qhd->khd", d_scores_low, saved["queries"], preferred_element_type=jnp.float32
        )
        * score_scale
    )
    remote_part = jnp.concatenate(
        [
            d_keys[row_count:].reshape(-1, model_width),
            d_values[row_count:].reshape(-1, model_width),
        ],
        axis=1,
    )
    own_part = lax.psum_scatter(remote_part, "dp", scatter_dimension=0, tiled=True)
    local_pairs = jnp.concatenate(
        [
            d_keys[:row_count].reshape(row_count, model_width),
            d_values[:row_count].reshape(row_count, model_width),
        ],
        axis=1,
    )
    local_pairs = jnp.concatenate(
        [local_pairs[:latent_start], local_pairs[latent_start:] + own_part], axis=0
    )
    d_projected = jnp.concatenate(
        [d_queries.reshape(row_count, model_width), local_pairs], axis=1
    ).astype(jnp.bfloat16)
    grad_qkv = jnp.dot(d_projected.T, normed, preferred_element_type=jnp.float32)
    d_normed = jnp.dot(d_projected, w_qkv.T, preferred_element_type=jnp.float32)
    unused_rows, first_back = jax.vjp(layer_norm, all_rows, gain_attn)
    d_rows_norm, grad_gain_attn = first_back(d_normed)
    return (
        d_mid + d_rows_norm,
        (grad_gain_attn, grad_qkv, grad_out, grad_gain_mlp, grad_up, grad_down),
    )


def packed(grads, n):
    gain_first, qkv_grad, out_grad, gain_second, up_grad, down_grad = grads
    width = out_grad.shape[0]
    rows = width // n

    def by_rows(grad):
        return grad.reshape(n, -1, rows, width).transpose(1, 0, 2, 3).astype(jnp.bfloat16)

    down = down_grad.reshape(n, rows, -1, width).transpose(2, 0, 1, 3).astype(jnp.bfloat16)
    chunks = jnp.concatenate([down, by_rows(up_grad), by_rows(out_grad), by_rows(qkv_grad)], axis=0)
    gains = jnp.stack([gain_first.reshape(n, rows), gain_second.reshape(n, rows)], axis=1)
    return chunks, jnp.pad(gains, ((0, 0), (0, 6), (0, 128 - rows)))


def shards(
    grid,
    tokens,
    latents,
    slot_group,
    image_groups,
    gain_attn,
    w_qkv,
    w_out,
    gain_mlp,
    w_up,
    w_down,
    d_tokens,
    d_latents,
):
    micro = tokens.shape[0]
    tok_rows = tokens.shape[1]
    lat_rows = latents.shape[1]
    model_width = tokens.shape[2]
    local_groups = tok_rows // GROUP
    section_index = lax.axis_index("section")
    is_global = section_index == 1
    dp_index = lax.axis_index("dp")
    weights = (gain_attn[0], w_qkv[0], w_out[0], gain_mlp[0], w_up[0], w_down[0])
    image_ends = jnp.cumsum(image_groups, axis=1)
    slot_images = jnp.sum(
        (image_ends[:, None, :] <= slot_group[:, :, None]).astype(jnp.int32), axis=2
    )
    slot_total = slot_group.shape[1]
    row_group = jnp.concatenate([jnp.arange(tok_rows) // GROUP, jnp.arange(lat_rows) // LAT])
    row_latent = jnp.concatenate(
        [jnp.zeros((tok_rows,), jnp.bool_), jnp.ones((lat_rows,), jnp.bool_)]
    )
    same_group = row_group[:, None] == row_group[None, :]
    local_mask = jnp.where(
        is_global, (~row_latent)[:, None] & row_latent[None, :] & same_group, same_group
    )
    group_match = row_group[:, None] == jnp.arange(local_groups)[None, :]

    def key_images(batch):
        images_row = lax.dynamic_index_in_dim(slot_images, batch, 0, keepdims=False)
        return (images_row, jnp.broadcast_to(images_row[:, None], (slot_total, LAT)).reshape(-1))

    def allowed_for(batch):
        images_row, key_image = key_images(batch)
        own_images = lax.dynamic_slice_in_dim(images_row, dp_index * local_groups, local_groups)
        row_image = jnp.sum(jnp.where(group_match, own_images[None, :], 0), axis=1)
        remote_mask = is_global & row_latent[:, None] & (row_image[:, None] == key_image[None, :])
        return jnp.concatenate([local_mask, remote_mask], axis=1)

    recv_tokens = jnp.zeros((tok_rows, model_width), jnp.bfloat16)
    recv_latents = jnp.zeros((lat_rows, model_width), jnp.bfloat16)
    kept_rows, kept_pairs, tok_outputs, lat_outputs = ([], [], [], [])
    for turn in range(micro + 1):
        batch = jnp.clip(turn - section_index, 0, micro - 1)
        own_tok = lax.dynamic_index_in_dim(tokens, batch, 0, keepdims=False)
        own_lat = lax.dynamic_index_in_dim(latents, batch, 0, keepdims=False)
        input_rows = jnp.concatenate(
            [
                jnp.where(is_global, recv_tokens, own_tok),
                jnp.where(is_global, recv_latents, own_lat),
            ],
            axis=0,
        )
        all_rows = input_rows.astype(jnp.float32)
        normed, projected = front_half(all_rows, weights[0], weights[1])
        remote_rows = lax.all_gather(
            latent_operand(projected, tok_rows, model_width), "dp", axis=0, tiled=True
        )
        saved = back_half(all_rows, projected, remote_rows, allowed_for(batch), weights)
        result = saved["result"]
        result_low = result.astype(jnp.bfloat16)
        stored = jnp.where(is_global, result, result_low.astype(jnp.float32))
        kept_rows.append(input_rows)
        kept_pairs.append(remote_rows)
        tok_outputs.append(stored[:tok_rows])
        lat_outputs.append(stored[tok_rows:])
        if turn < micro:
            recv_tokens, recv_latents = from_behind(
                (result_low[:tok_rows], result_low[tok_rows:]), "section", 1
            )
    kept_rows = jnp.stack(kept_rows)
    kept_pairs = jnp.stack(kept_pairs)
    totals = tuple(
        jnp.zeros(w.shape[::-1] if w.ndim == 2 else w.shape, jnp.float32) for w in weights
    )
    recv_grad_tok = jnp.zeros((tok_rows, model_width), jnp.bfloat16)
    recv_grad_lat = jnp.zeros((lat_rows, model_width), jnp.bfloat16)
    tok_grads, lat_grads = ([], [])
    for turn in range(micro + 1):
        raw_batch = micro - turn - section_index
        valid = ((raw_batch >= 0) & (raw_batch < micro)).astype(jnp.float32)
        batch = jnp.clip(raw_batch, 0, micro - 1)
        all_rows = lax.dynamic_index_in_dim(
            kept_rows, batch + section_index, 0, keepdims=False
        ).astype(jnp.float32)
        normed, projected = front_half(all_rows, weights[0], weights[1])
        remote_rows = lax.all_gather(
            latent_operand(projected, tok_rows, model_width), "dp", axis=0, tiled=True
        )
        allowed = allowed_for(batch)
        saved = back_half(all_rows, projected, remote_rows, allowed, weights)
        given = (
            jnp.concatenate(
                [
                    lax.dynamic_index_in_dim(d_tokens, batch, 0, keepdims=False),
                    lax.dynamic_index_in_dim(d_latents, batch, 0, keepdims=False),
                ],
                axis=0,
            )
            * valid
        )
        passed = jnp.concatenate([recv_grad_tok, recv_grad_lat], axis=0).astype(jnp.float32)
        d_result = jnp.where(is_global, given, passed)
        d_rows, grads = section_backward(
            saved, d_result, all_rows, normed, allowed, weights, tok_rows
        )
        totals = tuple((accum + piece for accum, piece in zip(totals, grads)))
        d_rows_low = d_rows.astype(jnp.bfloat16)
        stored = jnp.where(is_global, d_rows_low.astype(jnp.float32), d_rows)
        tok_grads.append(stored[:tok_rows])
        lat_grads.append(stored[tok_rows:])
        if turn < micro:
            recv_grad_tok, recv_grad_lat = from_behind(
                (d_rows_low[:tok_rows], d_rows_low[tok_rows:]), "section", -1
            )
    chunks, gains = packed(totals, lax.axis_size("dp"))
    summed, gain_sums = spread(grid, chunks, gains)
    rows = summed.shape[1]
    layer_tokens = lax.dynamic_slice_in_dim(jnp.stack(tok_outputs), section_index, micro, 0)[None]
    layer_latents = lax.dynamic_slice_in_dim(jnp.stack(lat_outputs), section_index, micro, 0)[None]
    grad_tokens = lax.dynamic_slice_in_dim(jnp.stack(tok_grads), 1 - section_index, micro, 0)[::-1][
        None
    ]
    grad_latents = lax.dynamic_slice_in_dim(jnp.stack(lat_grads), 1 - section_index, micro, 0)[
        ::-1
    ][None]
    return (
        layer_tokens,
        layer_latents,
        grad_tokens,
        grad_latents,
        gain_sums[0:1, :rows],
        summed[9:].reshape(-1, model_width).T[None],
        summed[8].T[None],
        gain_sums[1:2, :rows],
        summed[4:8].reshape(-1, model_width).T[None],
        summed[0:4].transpose(0, 2, 1).reshape(-1, rows)[None],
    )


F32 = jnp.float32
LOW = jnp.bfloat16
HEAD_PAD = 16
BAND = 48
TILE = 256


def nn(a, b):
    return jnp.dot(a, b, preferred_element_type=F32)


def nt(a, b):
    return lax.dot_general(a, b, (((1,), (1,)), ((), ())), preferred_element_type=F32)


def tn(a, b):
    return lax.dot_general(a, b, (((0,), (0,)), ((), ())), preferred_element_type=F32)


def normed_rows(values):
    centred = values - jnp.mean(values, axis=-1, keepdims=True)
    scale = lax.rsqrt(jnp.mean(centred * centred, axis=-1, keepdims=True) + epsilon)
    return centred * scale, scale


def norm_back(grad, hat, scale, gain):
    scaled = grad * gain
    mean = jnp.mean(scaled, axis=-1, keepdims=True)
    along = jnp.mean(scaled * hat, axis=-1, keepdims=True)
    return scale * (scaled - mean - hat * along)


def at(start, size):
    return pl.ds(pl.multiple_of(start, size), size)


def class_max(s):
    for by in (16, 32, 64):
        s = jnp.maximum(s, pltpu.roll(s, by, 1))
    return s


def class_sum(s):
    for by in (16, 32, 64):
        s = s + pltpu.roll(s, by, 1)
    return s


def layer_kernel(
    n,
    tokens,
    latents,
    key_mask,
    gain_attn,
    gain_mlp,
    w_qkv,
    w_out,
    w_up,
    w_down,
    d_tokens,
    d_latents,
    out_rows,
    out_grads,
    grads,
    g_gains,
    wq,
    wo,
    wu,
    wd,
    xb,
    n1,
    proj,
    mixed,
    mid,
    n2,
    act,
    dup,
    yb,
    dy,
    ef,
    tmp,
    dm,
    dmix,
    dproj,
    dkv,
    probs,
    probs_lat,
    latf,
    mixf,
    qbd,
    kbd,
    vbd,
    kv_all,
    kvg_send,
    kvg_recv,
    stage,
    load_sem,
    stage_sem,
    relay_send,
    relay_recv,
    kv_sem_s,
    kv_sem_r,
    kvg_sem_s,
    kvg_sem_r,
):
    rows, width = xb.shape
    ff = act.shape[1]
    tok = tokens.shape[0]
    lat = latents.shape[0]
    half = lat // LAT
    pairs = width // 128
    me = lax.axis_index("dp")
    section = lax.axis_index("section")
    first = section == 0
    second = section == 1
    partner = (me, 1 - section)

    loads = [
        pltpu.make_async_copy(src, dst, load_sem.at[i])
        for i, (src, dst) in enumerate(((w_qkv, wq), (w_out, wo), (w_up, wu), (w_down, wd)))
    ]
    x_loads = [
        pltpu.make_async_copy(tokens, xb.at[0:tok], load_sem.at[4]),
        pltpu.make_async_copy(latents, xb.at[tok:rows], load_sem.at[5]),
    ]
    e_loads = [
        pltpu.make_async_copy(d_tokens, ef.at[0:tok], load_sem.at[6]),
        pltpu.make_async_copy(d_latents, ef.at[tok:rows], load_sem.at[7]),
    ]

    @pl.when(first)
    def _():
        for copy in x_loads:
            copy.start()

    for copy in loads:
        copy.start()

    @pl.when(second)
    def _():
        for copy in e_loads:
            copy.start()

    barrier = pltpu.get_barrier_semaphore()
    pl.semaphore_signal(barrier, inc=1, device_id=partner, device_id_type=MESH)

    @pl.when(second)
    def _():
        for shift in range(1, n):
            pl.semaphore_signal(
                barrier, inc=1, device_id=(lax.rem(me + shift, n), section), device_id_type=MESH
            )
        pl.semaphore_wait(barrier, n)

    @pl.when(first)
    def _():
        pl.semaphore_wait(barrier, 1)

    forward_relay = pltpu.make_async_remote_copy(
        src_ref=yb, dst_ref=xb, send_sem=relay_send.at[0], recv_sem=relay_recv.at[0],
        device_id=partner, device_id_type=MESH,
    )
    backward_relay = pltpu.make_async_remote_copy(
        src_ref=yb, dst_ref=dy, send_sem=relay_send.at[1], recv_sem=relay_recv.at[1],
        device_id=partner, device_id_type=MESH,
    )

    def kv_copy(shift, incoming):
        slot = lax.rem(me + n - shift, n) if incoming else me
        return pltpu.make_async_remote_copy(
            src_ref=kv_all.at[me], dst_ref=kv_all.at[slot],
            send_sem=kv_sem_s.at[shift - 1], recv_sem=kv_sem_r.at[shift - 1],
            device_id=(lax.rem(me + shift, n), section), device_id_type=MESH,
        )

    def kvg_copy(shift):
        there = lax.rem(me + shift, n)
        return pltpu.make_async_remote_copy(
            src_ref=kvg_send.at[there], dst_ref=kvg_recv.at[shift - 1],
            send_sem=kvg_sem_s.at[shift - 1], recv_sem=kvg_sem_r.at[shift - 1],
            device_id=(there, section), device_id_type=MESH,
        )

    lane = lax.broadcasted_iota(jnp.int32, (1, 128), 1)
    halves = [(lane < 64).astype(F32).astype(LOW), (lane >= 64).astype(F32).astype(LOW)]
    eighths = [(h.astype(F32) * 0.125).astype(LOW) for h in halves]
    heads = (
        lax.broadcasted_iota(jnp.int32, (HEAD_PAD, width), 1) // 64
        == lax.broadcasted_iota(jnp.int32, (HEAD_PAD, width), 0)
    ).astype(F32)

    def block_diagonal(dst, base, src, row, column, scale):
        for i in range(LAT):
            line = src[row + i : row + i + 1, column : column + width] * scale
            dst[base + i * HEAD_PAD : base + (i + 1) * HEAD_PAD, :] = (line * heads).astype(LOW)

    def head_sum(dst, row, column, value, scale, add):
        for i in range(LAT):
            line = jnp.sum(
                value[i * HEAD_PAD : (i + 1) * HEAD_PAD] * heads, axis=0, keepdims=True
            )
            line = line * scale
            if add:
                line = line + dst[row + i : row + i + 1, column : column + width]
            dst[row + i : row + i + 1, column : column + width] = line

    def bands(body):
        def one(i, carry):
            body(at(i * BAND, BAND))
            return carry

        lax.fori_loop(0, rows // BAND, one, 0)

    def tiles(count, body, size=TILE):
        def one(i, carry):
            body(at(i * size, size))
            return carry

        lax.fori_loop(0, count, one, 0)

    @pl.when(first)
    def _():
        for copy in x_loads:
            copy.wait()

    @pl.when(second)
    def _():
        forward_relay.wait_recv()

    def norm_in(r):
        hat, unused = normed_rows(xb[r, :].astype(F32))
        n1[r, :] = (hat * gain_attn[...]).astype(LOW)

    bands(norm_in)
    loads[0].wait()

    @pl.when(second)
    def _():
        own = nn(n1[tok:rows, :], wq[:, width:]).astype(LOW)
        kv_all[me] = own
        latf[:, width:] = own.astype(F32)
        for shift in range(1, n):
            kv_copy(shift, False).start()

    def project(c):
        proj[:, c] = nn(n1[...], wq[:, c]).astype(LOW)

    per = width // TILE
    tiles(jnp.where(first, 3 * per, per), project)

    def lat_bias(m, shape, axis):
        return jnp.where(
            lax.broadcasted_iota(jnp.int32, shape, axis) // LAT == m, 0.0, masked_score
        ).astype(F32)

    @pl.when(first)
    def _():
        latf[...] = proj[tok:rows, :].astype(F32)

        def pair(it, carry):
            m, p = it // pairs, lax.rem(it, pairs)
            r = at(m * GROUP, GROUP)
            q = proj[r, at(p * 128, 128)]
            k = proj[r, at(width + p * 128, 128)]
            v = proj[r, at(2 * width + p * 128, 128)]
            kl = proj[tok:rows, at(width + p * 128, 128)]
            vl = proj[tok:rows, at(2 * width + p * 128, 128)]
            bias = lat_bias(m, (lat, GROUP), 0)
            total = jnp.zeros((GROUP, 128), F32)
            for e in (0, 1):
                qe = q * eighths[e]
                st = nt(k, qe)
                sl = nt(kl, qe) + bias
                top = jnp.maximum(
                    jnp.max(st, axis=0, keepdims=True), jnp.max(sl, axis=0, keepdims=True)
                )
                et = jnp.exp(st - top)
                el = jnp.exp(sl - top)
                scale = 1.0 / (
                    jnp.sum(et, axis=0, keepdims=True) + jnp.sum(el, axis=0, keepdims=True)
                )
                pt = (et * scale).astype(LOW)
                pe = (el * scale).astype(LOW)
                probs[2 * it + e, 0:GROUP, :] = pt
                probs[2 * it + e, GROUP : GROUP + lat, :] = pe
                total += tn(pt, v * halves[e]) + tn(pe, vl * halves[e])
            mixed[r, at(p * 128, 128)] = total.astype(LOW)
            return carry

        lax.fori_loop(0, half * pairs, pair, 0)
        for m in range(half):
            r = slice(m * GROUP, (m + 1) * GROUP)
            b = slice(m * 128, (m + 1) * 128)
            block_diagonal(qbd, m * 128, latf, m * LAT, 0, 0.125)
            s = nt(qbd[b, :], proj[r, width : 2 * width])
            sl = nt(qbd[b, :], proj[tok:rows, width : 2 * width]) + lat_bias(m, (128, lat), 1)
            top = jnp.maximum(
                jnp.max(s, axis=1, keepdims=True), jnp.max(sl, axis=1, keepdims=True)
            )
            et = jnp.exp(s - top)
            el = jnp.exp(sl - top)
            scale = 1.0 / (
                jnp.sum(et, axis=1, keepdims=True) + jnp.sum(el, axis=1, keepdims=True)
            )
            pt = (et * scale).astype(LOW)
            pe = (el * scale).astype(LOW)
            probs_lat[b, 0:GROUP] = pt
            probs_lat[b, GROUP : GROUP + lat] = pe
            o = nn(pt, proj[r, 2 * width :]) + nn(pe, proj[tok:rows, 2 * width :])
            head_sum(mixf, m * LAT, 0, o, 1.0, False)
        mixed[tok:rows, :] = mixf[...].astype(LOW)

    keys = n * lat

    @pl.when(second)
    def _():
        latf[:, :width] = proj[tok:rows, :width].astype(F32)
        for m in range(half):
            r = slice(m * GROUP, (m + 1) * GROUP)
            b = slice(m * 128, (m + 1) * 128)
            block_diagonal(qbd, m * 128, latf, m * LAT, 0, 0.125)
            block_diagonal(kbd, m * 128, latf, m * LAT, width, 1.0)
            block_diagonal(vbd, m * 128, latf, m * LAT, 2 * width, 1.0)
            s = nt(proj[r, :width] * jnp.asarray(0.125, LOW), kbd[b, :])
            et = jnp.exp(s - class_max(s))
            pt = (et / class_sum(et)).astype(LOW)
            probs[m, 0:GROUP, 0:128] = pt
            mixed[r, :] = nn(pt, vbd[b, :]).astype(LOW)
        for shift in range(1, n):
            kv_copy(shift, True).wait_recv()
        k = kv_all[:, :, :width].reshape(keys, width)
        v = kv_all[:, :, width:].reshape(keys, width)
        for m in range(half):
            b = slice(m * 128, (m + 1) * 128)
            s = nt(qbd[b, :], k) + key_mask[m : m + 1, :]
            et = jnp.exp(s - jnp.max(s, axis=1, keepdims=True))
            pt = (et / jnp.sum(et, axis=1, keepdims=True)).astype(LOW)
            probs_lat[b, 0:keys] = pt
            head_sum(mixf, m * LAT, 0, nn(pt, v), 1.0, False)
        mixed[tok:rows, :] = mixf[...].astype(LOW)

    loads[1].wait()

    def attend_out(c):
        mid[:, c] = xb[:, c].astype(F32) + nn(mixed[...], wo[:, c])

    tiles(width // TILE, attend_out)

    def norm_mid(r):
        hat, unused = normed_rows(mid[r, :])
        n2[r, :] = (hat * gain_mlp[...]).astype(LOW)

    bands(norm_mid)
    loads[2].wait()
    root = 0.7978845608028654

    def widen(c):
        up = nn(n2[...], wu[:, c])
        square = up * up
        t = jnp.tanh(up * (root + (root * 0.044715) * square))
        gate = 0.5 + 0.5 * t
        value = up * gate
        slope = gate + 2.0 * value * (1.0 - gate) * (root + (3.0 * root * 0.044715) * square)
        act[:, c] = value.astype(LOW)
        dup[:, c] = slope.astype(LOW)

    tiles(ff // TILE, widen)
    loads[3].wait()

    def narrow(c):
        y = mid[:, c] + nn(act[...], wd[:, c])
        low = y.astype(LOW)
        yb[:, c] = low
        out_rows[:, c] = jnp.where(first, low.astype(F32), y)

    tiles(width // TILE, narrow)

    @pl.when(first)
    def _():
        forward_relay.start()
        backward_relay.wait_recv()

        def widen_e(r):
            ef[r, :] = dy[r, :].astype(F32)

        bands(widen_e)

    @pl.when(second)
    def _():
        for copy in e_loads:
            copy.wait()

        def narrow_e(r):
            dy[r, :] = ef[r, :].astype(LOW)

        bands(narrow_e)

    part = 384
    unit = width // n
    many = part // unit

    def staged(slot, piece, chunk, share):
        return pltpu.make_async_copy(
            stage.at[slot, piece], grads.at[chunk, share], stage_sem.at[slot, piece]
        )

    def drain(slot):
        def one(piece, carry):
            staged(slot, piece, 0, 0).wait()
            return carry

        lax.fori_loop(0, many, one, 0)

    def weight_grad(place, count, left, right, fresh=False):
        def one(i, carry):
            slot = lax.rem(i, 2)
            value = tn(left(i), right(i)).astype(LOW)
            if fresh:

                @pl.when(i >= 2)
                def _():
                    drain(slot)

            else:
                drain(slot)
            for piece in range(many):
                stage[slot, piece] = value[piece * unit : (piece + 1) * unit]
                staged(slot, piece, *place(i * many + piece)).start()
            return carry

        lax.fori_loop(0, count, one, 0)

    wide = ff // width
    per_part = width // part
    weight_grad(
        lambda p: (p // n, lax.rem(p, n)),
        ff // part,
        lambda i: dy[:, at(lax.rem(i, per_part) * part, part)],
        lambda i: act[:, at((i // per_part) * width, width)],
        fresh=True,
    )

    def unwiden(c):
        dup[:, c] = (nt(dy[...], wd[c, :]) * dup[:, c].astype(F32)).astype(LOW)

    tiles(ff // TILE, unwiden)
    weight_grad(
        lambda p: (wide + lax.rem(p, wide), p // wide),
        ff // part,
        lambda i: dup[:, at(i * part, part)],
        lambda i: n2[...],
    )

    def to_mid(c):
        tmp[:, c] = nt(dup[...], wu[c, :])

    tiles(width // TILE, to_mid)
    g_gains[...] = jnp.zeros_like(g_gains)

    def fold(value):
        total = value[0:8]
        for i in range(1, BAND // 8):
            total = total + value[8 * i : 8 * i + 8]
        return total

    def mid_back(r):
        hat, scale = normed_rows(mid[r, :])
        grad = tmp[r, :]
        g_gains[8:16, :] += fold(grad * hat)
        total = ef[r, :] + norm_back(grad, hat, scale, gain_mlp[...])
        ef[r, :] = total
        dm[r, :] = total.astype(LOW)

    bands(mid_back)

    def to_mix(c):
        dmix[:, c] = nt(dm[...], wo[c, :]).astype(LOW)

    tiles(width // TILE, to_mix)
    weight_grad(
        lambda p: (2 * wide, p),
        width // part,
        lambda i: dm[:, at(i * part, part)],
        lambda i: mixed[...],
    )
    mixf[...] = dmix[tok:rows, :].astype(F32)

    @pl.when(first)
    def _():
        for m in range(half):
            r = slice(m * GROUP, (m + 1) * GROUP)
            b = slice(m * 128, (m + 1) * 128)
            block_diagonal(vbd, m * 128, mixf, m * LAT, 0, 1.0)
            do = vbd[b, :]
            dp = nt(do, proj[r, 2 * width :])
            dl = nt(do, proj[tok:rows, 2 * width :])
            pt = probs_lat[b, 0:GROUP]
            pe = probs_lat[b, GROUP : GROUP + lat]
            pf = pt.astype(F32)
            pg = pe.astype(F32)
            along = jnp.sum(pf * dp, axis=1, keepdims=True) + jnp.sum(
                pg * dl, axis=1, keepdims=True
            )
            ds = (pf * (dp - along)).astype(LOW)
            dsl = (pg * (dl - along)).astype(LOW)
            dq = nn(ds, proj[r, width : 2 * width]) + nn(dsl, proj[tok:rows, width : 2 * width])
            head_sum(latf, m * LAT, 0, dq, 0.125, False)
            dkv[r, :width] = tn(ds, qbd[b, :])
            dkv[r, width:] = tn(pt, do)
            if m == 0:
                dkv[tok:rows, :width] = tn(dsl, qbd[b, :])
                dkv[tok:rows, width:] = tn(pe, do)
            else:
                dkv[tok:rows, :width] += tn(dsl, qbd[b, :])
                dkv[tok:rows, width:] += tn(pe, do)
        dproj[tok:rows, :width] = latf[:, :width].astype(LOW)

        def pair(it, carry):
            m, p = it // pairs, lax.rem(it, pairs)
            r = at(m * GROUP, GROUP)
            qc, vc = at(p * 128, 128), at(width + p * 128, 128)
            q = proj[r, qc]
            k = proj[r, at(width + p * 128, 128)]
            v = proj[r, at(2 * width + p * 128, 128)]
            kl = proj[tok:rows, at(width + p * 128, 128)]
            vl = proj[tok:rows, at(2 * width + p * 128, 128)]
            dx = dmix[r, qc]
            dq = jnp.zeros((GROUP, 128), F32)
            dk = dkv[r, qc]
            dv = dkv[r, vc]
            dkl = dkv[tok:rows, qc]
            dvl = dkv[tok:rows, vc]
            for e in (0, 1):
                qe = q * eighths[e]
                de = dx * halves[e]
                pt = probs[2 * it + e, 0:GROUP, :]
                pe = probs[2 * it + e, GROUP : GROUP + lat, :]
                pf = pt.astype(F32)
                pg = pe.astype(F32)
                dp = nt(v, de)
                dl = nt(vl, de)
                along = jnp.sum(pf * dp, axis=0, keepdims=True) + jnp.sum(
                    pg * dl, axis=0, keepdims=True
                )
                ds = (pf * (dp - along)).astype(LOW)
                dsl = (pg * (dl - along)).astype(LOW)
                dq += tn(ds, k * halves[e]) + tn(dsl, kl * halves[e])
                dk += nn(ds, qe)
                dkl += nn(dsl, qe)
                dv += nn(pt, de)
                dvl += nn(pe, de)
            dproj[r, qc] = (dq * 0.125).astype(LOW)
            dproj[r, at(width + p * 128, 128)] = dk.astype(LOW)
            dproj[r, at(2 * width + p * 128, 128)] = dv.astype(LOW)
            dkv[tok:rows, qc] = dkl
            dkv[tok:rows, vc] = dvl
            return carry

        lax.fori_loop(0, half * pairs, pair, 0)
        dproj[tok:rows, width:] = dkv[tok:rows, :].astype(LOW)

    @pl.when(second)
    def _():
        k = kv_all[:, :, :width].reshape(keys, width)
        v = kv_all[:, :, width:].reshape(keys, width)
        for m in range(half):
            b = slice(m * 128, (m + 1) * 128)
            block_diagonal(vbd.at[pl.ds(256, 256)], m * 128, mixf, m * LAT, 0, 1.0)
        both = slice(0, half * 128)
        do = vbd[256 : 256 + half * 128, :]
        pt = probs_lat[both, 0:keys]
        pf = pt.astype(F32)
        dp = nt(do, v)
        along = jnp.sum(pf * dp, axis=1, keepdims=True)
        ds = (pf * (dp - along)).astype(LOW)
        kvg_send[:, :, :width] = tn(ds, qbd[both, :]).astype(LOW).reshape(n, lat, width)
        kvg_send[:, :, width:] = tn(pt, do).astype(LOW).reshape(n, lat, width)
        for shift in range(1, n):
            kvg_copy(shift).start()
        dq = nn(ds, k)
        for m in range(half):
            head_sum(latf, m * LAT, 0, dq[m * 128 : (m + 1) * 128], 0.125, False)
        dproj[tok:rows, :width] = latf[:, :width].astype(LOW)
        for m in range(half):
            r = slice(m * GROUP, (m + 1) * GROUP)
            b = slice(m * 128, (m + 1) * 128)
            pt = probs[m, 0:GROUP, 0:128]
            pf = pt.astype(F32)
            dx = dmix[r, :]
            dp = nt(dx, vbd[b, :])
            ds = (pf * (dp - class_sum(pf * dp))).astype(LOW)
            dproj[r, :width] = (nn(ds, kbd[b, :]) * 0.125).astype(LOW)
            dk = tn(ds, proj[r, :width])
            dv = tn(pt, dx)
            head_sum(latf, m * LAT, width, dk, 0.125, False)
            head_sum(latf, m * LAT, 2 * width, dv, 1.0, False)
        dproj[0:tok, width:] = jnp.zeros((tok, 2 * width), LOW)
        total = latf[:, width:] + kvg_send[me].astype(F32)
        for shift in range(1, n):
            kvg_copy(shift).wait_recv()
            total += kvg_recv[shift - 1].astype(F32)
        dproj[tok:rows, width:] = total.astype(LOW)

    def to_in(c):
        tmp[:, c] = nt(dproj[...], wq[c, :])

    tiles(width // TILE, to_in)

    @pl.when(first)
    def _():
        forward_relay.wait_send()

    def in_back(r):
        hat, scale = normed_rows(xb[r, :].astype(F32))
        grad = tmp[r, :]
        g_gains[0:8, :] += fold(grad * hat)
        total = ef[r, :] + norm_back(grad, hat, scale, gain_attn[...])
        low = total.astype(LOW)
        yb[r, :] = low
        out_grads[r, :] = jnp.where(first, total, low.astype(F32))

    bands(in_back)

    @pl.when(second)
    def _():
        backward_relay.start()

    weight_grad(
        lambda p: (2 * wide + 1 + lax.rem(p, 3), p // 3),
        3 * width // part,
        lambda i: dproj[:, at(i * part, part)],
        lambda i: n1[...],
    )
    for slot in (0, 1):
        drain(slot)

    @pl.when(second)
    def _():
        backward_relay.wait_send()
        for shift in range(1, n):
            kv_copy(shift, False).wait_send()
            kvg_copy(shift).wait_send()


def both_layers(n, tokens, latents, key_mask, gains, weights, d_tokens, d_latents):
    tok, width = tokens.shape
    lat = latents.shape[0]
    rows = tok + lat
    w_qkv, w_out, w_up, w_down = weights
    ff = w_up.shape[1]
    keys = n * lat
    half = lat // LAT
    vm, hbm = pl.BlockSpec(memory_space=pltpu.VMEM), pl.BlockSpec(memory_space=pl.ANY)
    scratch = [
        pltpu.VMEM(w.shape, LOW) for w in (w_qkv, w_out, w_up, w_down)
    ] + [
        pltpu.VMEM(shape, dtype)
        for shape, dtype in (
            ((rows, width), LOW),
            ((rows, width), LOW),
            ((rows, 3 * width), LOW),
            ((rows, width), LOW),
            ((rows, width), F32),
            ((rows, width), LOW),
            ((rows, ff), LOW),
            ((rows, ff), LOW),
            ((rows, width), LOW),
            ((rows, width), LOW),
            ((rows, width), F32),
            ((rows, width), F32),
            ((rows, width), LOW),
            ((rows, width), LOW),
            ((rows, 3 * width), LOW),
            ((rows, 2 * width), F32),
            ((half * width // 64, GROUP + lat, GROUP), LOW),
            ((half * 128, max(keys, GROUP + 128)), LOW),
            ((lat, 3 * width), F32),
            ((lat, width), F32),
            ((half * 128, width), LOW),
            ((half * 128, width), LOW),
            ((half * 256, width), LOW),
            ((n, lat, 2 * width), LOW),
            ((n, lat, 2 * width), LOW),
            ((n - 1, lat, 2 * width), LOW),
            ((2, 384 * n // width, width // n, width), LOW),
        )
    ] + [
        pltpu.SemaphoreType.DMA((8,)),
        pltpu.SemaphoreType.DMA((2, 384 * n // width)),
        pltpu.SemaphoreType.DMA((2,)),
        pltpu.SemaphoreType.DMA((2,)),
        pltpu.SemaphoreType.DMA((n - 1,)),
        pltpu.SemaphoreType.DMA((n - 1,)),
        pltpu.SemaphoreType.DMA((n - 1,)),
        pltpu.SemaphoreType.DMA((n - 1,)),
    ]
    size = sum(w.size for w in weights)
    return pl.pallas_call(
        functools.partial(layer_kernel, n),
        out_shape=(
            jax.ShapeDtypeStruct((rows, width), F32),
            jax.ShapeDtypeStruct((rows, width), F32),
            jax.ShapeDtypeStruct((size // (width * width), n, width // n, width), LOW),
            jax.ShapeDtypeStruct((16, width), F32),
        ),
        in_specs=[hbm, hbm, vm, vm, vm] + [hbm] * 6,
        out_specs=(vm, vm, hbm, vm),
        scratch_shapes=scratch,
        compiler_params=pltpu.CompilerParams(
            collective_id=1, has_side_effects=True, vmem_limit_bytes=62 * 1024 * 1024
        ),
        cost_estimate=pl.CostEstimate(
            flops=6 * rows * size, bytes_accessed=4 * size, transcendentals=0
        ),
    )(tokens, latents, key_mask, *gains, *weights, d_tokens, d_latents)


def fused_shards(
    grid,
    tokens,
    latents,
    slot_group,
    image_groups,
    gain_attn,
    w_qkv,
    w_out,
    gain_mlp,
    w_up,
    w_down,
    d_tokens,
    d_latents,
):
    micro, tok, width = tokens.shape
    lat = latents.shape[1]
    n = slot_group.shape[1]
    dp_index = lax.axis_index("dp")
    image_ends = jnp.cumsum(image_groups, axis=1)
    images = jnp.sum((image_ends[:, None, :] <= slot_group[:, :, None]).astype(jnp.int32), axis=2)
    own = lax.dynamic_slice_in_dim(images, dp_index, 1, 1)
    same = (images == own)[:, :, None, None] & jnp.eye(micro, dtype=jnp.bool_)[:, None, :, None]
    bias = jnp.where(same, 0.0, masked_score).astype(F32)
    bias = jnp.broadcast_to(bias, (micro, n, micro, lat)).reshape(micro, -1)
    rows_out, rows_grad, grads, gains = both_layers(
        n,
        tokens.reshape(micro * tok, width),
        latents.reshape(micro * lat, width),
        bias,
        (gain_attn, gain_mlp),
        (w_qkv[0], w_out[0], w_up[0], w_down[0]),
        d_tokens.reshape(micro * tok, width),
        d_latents.reshape(micro * lat, width),
    )
    unit = width // n
    gains = jnp.sum(gains.reshape(2, 8, n, unit), axis=1).transpose(1, 0, 2)
    gains = jnp.pad(gains, ((0, 0), (0, 6), (0, 128 - unit)))
    summed, gain_sums = spread(grid, grads, gains)
    wide = w_up.shape[2] // width
    tokens_end = micro * tok
    return (
        rows_out[:tokens_end].reshape(1, micro, tok, width),
        rows_out[tokens_end:].reshape(1, micro, lat, width),
        rows_grad[:tokens_end].reshape(1, micro, tok, width),
        rows_grad[tokens_end:].reshape(1, micro, lat, width),
        gain_sums[0:1, :unit],
        summed[2 * wide + 1 :].reshape(-1, width).T[None],
        summed[2 * wide].T[None],
        gain_sums[1:2, :unit],
        summed[wide : 2 * wide].reshape(-1, width).T[None],
        summed[0:wide].transpose(0, 2, 1).reshape(-1, unit)[None],
    )


def solution(mesh):
    in_specs = (
        P(None, "dp", None),
        P(None, "dp", None),
        P(),
        P(),
        P("section", None),
        P("section", None, None),
        P("section", None, None),
        P("section", None),
        P("section", None, None),
        P("section", None, None),
        P(None, "dp", None),
        P(None, "dp", None),
    )
    out_specs = (
        P("section", None, "dp", None),
        P("section", None, "dp", None),
        P("section", None, "dp", None),
        P("section", None, "dp", None),
        P("section", "dp"),
        P("section", None, "dp"),
        P("section", None, "dp"),
        P("section", "dp"),
        P("section", None, "dp"),
        P("section", None, "dp"),
    )
    grid = grid_of(mesh)

    def program(*args):
        n, width = mesh.shape["dp"], args[0].shape[2]
        one_group = args[0].shape[1] == n * GROUP
        body = fused_shards if one_group and width % (16 * n) == 0 else shards
        return jax.shard_map(
            functools.partial(body, grid), mesh=mesh, in_specs=in_specs, out_specs=out_specs, check_vma=False
        )(*args)

    return program
```

```python
import functools

import jax
import jax.numpy as jnp
from jax import lax
from jax.experimental import pallas as pl
from jax.experimental.pallas import tpu as pltpu
from jax.sharding import PartitionSpec as P

HEADS = 12
GROUP = 256
LAT = 8


epsilon = 1e-05
masked_score = -1e30


MESH = pl.DeviceIdType.MESH


def grid_of(mesh):
    n = mesh.shape["dp"]
    coords = [getattr(d, "coords", None) for d in mesh.devices.reshape(n, -1)[:, 0]]
    if any(c is None for c in coords):
        return (n // 4, 2, 2) if n % 4 == 0 else (n, 1, 1)
    sizes = {a: len({c[a] for c in coords}) for a in range(3)}
    strides = {
        a: min([i for i in range(n) if coords[i][a] != coords[0][a]], default=n) for a in range(3)
    }
    order = sorted(range(3), key=lambda a: -strides[a])
    return tuple(sizes[a] for a in order)


def spread_kernel(grid, pairs, g_ref, gain_ref, out_ref, gout_ref, *scratch):
    acc = scratch[0:3]
    land = [scratch[3 + 3 * i : 6 + 3 * i] for i in range(3)]
    send_sem, recv_sem, own_sem = scratch[12:15]
    me = lax.axis_index("dp")
    section = lax.axis_index("section")
    l0, l1, l2 = grid
    here = (me // (l1 * l2), lax.rem(me // l2, l1), lax.rem(me, l2))

    def device(axis, shift):
        there = list(here)
        there[axis] = lax.rem(here[axis] + shift, grid[axis])
        return there[axis], ((there[0] * l1 + there[1]) * l2 + there[2], section)

    barrier = pltpu.get_barrier_semaphore()
    for axis in range(3):
        for shift in range(1, grid[axis]):
            pl.semaphore_signal(
                barrier, inc=1, device_id=device(axis, shift)[1], device_id_type=MESH
            )
    pl.semaphore_wait(barrier, sum(grid) - 3)

    orders = ((2, 1, 0), (1, 2, 0), (2, 1, 0))

    def source(stream, phase, k, at):
        if phase == 0:
            if stream == 0:
                return g_ref.at[2 * k, :, :, at]
            if stream == 1:
                return g_ref.at[2 * k + 1, :, at]
            return gain_ref.at[:, :, at]
        if phase == 1:
            return acc[stream].at[k, :, at]
        return acc[stream].at[k, at, here[orders[stream][1]]]

    def copies(stream, phase, k):
        axis = orders[stream][phase]
        for shift in range(1, grid[axis]):
            at, target = device(axis, shift)
            yield pltpu.make_async_remote_copy(
                src_ref=source(stream, phase, k, at),
                dst_ref=land[phase][stream].at[k, shift - 1],
                send_sem=send_sem.at[stream, phase, k, shift - 1],
                recv_sem=recv_sem.at[stream, phase, k, shift - 1],
                device_id=target,
                device_id_type=MESH,
            )

    def own(stream, k):
        return pltpu.make_async_copy(
            source(stream, 0, k, here[orders[stream][0]]), acc[stream].at[k], own_sem.at[stream, k]
        )

    def launch(stream, phase, k):
        for copy in copies(stream, phase, k):
            copy.start()

    def absorb(stream, phase, k):
        axis = orders[stream][phase]
        if phase == 0:
            own(stream, k).wait()
        for copy in copies(stream, phase, k):
            copy.wait_recv()
        into = land[phase][stream]
        count = grid[axis] - 1
        if phase == 0:
            for a in range(acc[stream].shape[1]):
                for b in range(acc[stream].shape[2]):
                    total = acc[stream][k, a, b].astype(jnp.float32)
                    for s in range(count):
                        total += into[k, s, a, b].astype(jnp.float32)
                    acc[stream][k, a, b] = total.astype(acc[stream].dtype)
        elif phase == 1:
            mine = here[axis]
            for a in range(acc[stream].shape[1]):
                total = acc[stream][k, a, mine].astype(jnp.float32)
                for s in range(count):
                    total += into[k, s, a].astype(jnp.float32)
                acc[stream][k, a, mine] = total.astype(acc[stream].dtype)
        else:
            total = acc[stream][k, here[0], here[orders[stream][1]]].astype(jnp.float32)
            for s in range(count):
                total += into[k, s].astype(jnp.float32)
            if stream < 2:
                out_ref[2 * k + stream] = total
            else:
                gout_ref[...] = total

    own(2, 0).start()
    launch(2, 0, 0)

    def start_own(k, carry):
        for stream in (0, 1):
            own(stream, k).start()
        return carry

    for stream in (0, 1):
        launch(stream, 0, 0)
    lax.fori_loop(0, pairs, start_own, 0)

    def turn(t, carry):
        @pl.when(t + 1 < pairs)
        def _():
            for stream in (0, 1):
                launch(stream, 0, t + 1)

        @pl.when(t < pairs)
        def _():
            for stream in (0, 1):
                absorb(stream, 0, t)
                launch(stream, 1, t)

        @pl.when((t >= 1) & (t - 1 < pairs))
        def _():
            for stream in (0, 1):
                absorb(stream, 1, t - 1)
                launch(stream, 2, t - 1)

        @pl.when(t >= 2)
        def _():
            for stream in (0, 1):
                absorb(stream, 2, t - 2)

        return carry

    lax.fori_loop(0, pairs + 2, turn, 0)
    absorb(2, 0, 0)
    launch(2, 1, 0)
    absorb(2, 1, 0)
    launch(2, 2, 0)
    absorb(2, 2, 0)

    def finish(k, carry):
        for stream in (0, 1):
            for phase in range(3):
                for copy in copies(stream, phase, k):
                    copy.wait_send()
        return carry

    lax.fori_loop(0, pairs, finish, 0)
    for phase in range(3):
        for copy in copies(2, phase, 0):
            copy.wait_send()


def spread(grid, grads, gains):
    chunks, n, rows, width = grads.shape
    pairs = chunks // 2
    l0, l1, l2 = grid
    most = max(max(grid) - 1, 1)
    low = jnp.bfloat16
    shapes = ((pairs, rows, width, low), (pairs, rows, width, low), (1, 8, 128, jnp.float32))
    inner = ((l1, l2), (l2, l1), (l1, l2))
    acc, first, second, third = [], [], [], []
    for (count, r, w, dt), (kept, sent) in zip(shapes, inner):
        acc.append(pltpu.VMEM((count, l0, kept, r, w), dt))
        first.append(pltpu.VMEM((count, max(sent - 1, 1), l0, kept, r, w), dt))
        second.append(pltpu.VMEM((count, max(kept - 1, 1), l0, r, w), dt))
        third.append(pltpu.VMEM((count, max(l0 - 1, 1), r, w), dt))
    return pl.pallas_call(
        functools.partial(spread_kernel, grid, pairs),
        out_shape=(
            jax.ShapeDtypeStruct((chunks, rows, width), jnp.float32),
            jax.ShapeDtypeStruct((8, 128), jnp.float32),
        ),
        in_specs=[pl.BlockSpec(memory_space=pl.ANY)] * 2,
        out_specs=(pl.BlockSpec(memory_space=pltpu.VMEM),) * 2,
        scratch_shapes=acc
        + first
        + second
        + third
        + [
            pltpu.SemaphoreType.DMA((3, 3, pairs, most)),
            pltpu.SemaphoreType.DMA((3, 3, pairs, most)),
            pltpu.SemaphoreType.DMA((3, pairs)),
        ],
        compiler_params=pltpu.CompilerParams(
            collective_id=0, has_side_effects=True, vmem_limit_bytes=60 * 1024 * 1024
        ),
        cost_estimate=pl.CostEstimate(flops=0, bytes_accessed=grads.size * 4, transcendentals=0),
    )(grads.reshape(chunks, l0, l1, l2, rows, width), gains.reshape(l0, l1, l2, 8, 128))


def from_behind(x, axis, by):
    devices = lax.axis_size(axis)
    pairs = [(i, i + by) for i in range(devices) if 0 <= i + by < devices]
    return lax.ppermute(x, axis, pairs)


def layer_norm(values, gain):
    row_mean = jnp.mean(values, axis=-1, keepdims=True)
    centred = values - row_mean
    row_var = jnp.mean(centred * centred, axis=-1, keepdims=True)
    return centred * lax.rsqrt(row_var + epsilon) * gain


def front_half(all_rows, gain_attn, w_qkv):
    normed = layer_norm(all_rows, gain_attn).astype(jnp.bfloat16)
    projected = jnp.dot(normed, w_qkv, preferred_element_type=jnp.float32).astype(jnp.bfloat16)
    return (normed, projected)


def latent_operand(projected, tok_rows, model_width):
    return projected[tok_rows:, model_width:]


def back_half(all_rows, projected, remote_rows, allowed, weights):
    gain_attn, w_qkv, w_out, gain_mlp, w_up, w_down = weights
    row_count, model_width = all_rows.shape
    head_size = model_width // HEADS
    remote_pairs = remote_rows[:, remote_rows.shape[1] - 2 * model_width :]
    queries = projected[:, :model_width].reshape(row_count, HEADS, head_size)
    key_rows = jnp.concatenate(
        [projected[:, model_width : 2 * model_width], remote_pairs[:, :model_width]], axis=0
    )
    value_rows = jnp.concatenate(
        [projected[:, 2 * model_width :], remote_pairs[:, model_width:]], axis=0
    )
    key_rows = key_rows.reshape(-1, HEADS, head_size)
    value_rows = value_rows.reshape(-1, HEADS, head_size)
    scores = jnp.einsum(
        "qhd,khd->hqk", queries, key_rows, preferred_element_type=jnp.float32
    ) * head_size ** (-0.5)
    attn_weights = jax.nn.softmax(jnp.where(allowed[None], scores, masked_score), axis=-1)
    attn_low = attn_weights.astype(jnp.bfloat16)
    mixed_low = jnp.einsum("hqk,khd->qhd", attn_low, value_rows, preferred_element_type=jnp.float32)
    mixed_low = mixed_low.reshape(row_count, model_width).astype(jnp.bfloat16)
    mid_rows = all_rows + jnp.dot(mixed_low, w_out, preferred_element_type=jnp.float32)
    normed_mlp = layer_norm(mid_rows, gain_mlp).astype(jnp.bfloat16)
    up_proj = jnp.dot(normed_mlp, w_up, preferred_element_type=jnp.float32)
    activated = jax.nn.gelu(up_proj).astype(jnp.bfloat16)
    result = mid_rows + jnp.dot(activated, w_down, preferred_element_type=jnp.float32)
    return dict(
        queries=queries,
        key_rows=key_rows,
        value_rows=value_rows,
        attn_weights=attn_weights,
        attn_low=attn_low,
        mixed_low=mixed_low,
        mid_rows=mid_rows,
        normed_mlp=normed_mlp,
        up_proj=up_proj,
        activated=activated,
        result=result,
    )


def section_backward(saved, d_result, all_rows, normed, allowed, weights, latent_start):
    gain_attn, w_qkv, w_out, gain_mlp, w_up, w_down = weights
    row_count, model_width = all_rows.shape
    head_size = model_width // HEADS
    score_scale = head_size ** (-0.5)
    d_low = d_result.astype(jnp.bfloat16)
    grad_down = jnp.dot(d_low.T, saved["activated"], preferred_element_type=jnp.float32)
    d_activated = jnp.dot(d_low, w_down.T, preferred_element_type=jnp.float32)
    unused_up, gelu_back = jax.vjp(jax.nn.gelu, saved["up_proj"])
    d_up = gelu_back(d_activated)[0].astype(jnp.bfloat16)
    grad_up = jnp.dot(d_up.T, saved["normed_mlp"], preferred_element_type=jnp.float32)
    d_normed_mlp = jnp.dot(d_up, w_up.T, preferred_element_type=jnp.float32)
    unused_mid, second_back = jax.vjp(layer_norm, saved["mid_rows"], gain_mlp)
    d_mid_norm, grad_gain_mlp = second_back(d_normed_mlp)
    d_mid = d_result + d_mid_norm
    d_mid_low = d_mid.astype(jnp.bfloat16)
    grad_out = jnp.dot(d_mid_low.T, saved["mixed_low"], preferred_element_type=jnp.float32)
    d_mixed = jnp.dot(d_mid_low, w_out.T, preferred_element_type=jnp.float32).astype(jnp.bfloat16)
    d_mixed = d_mixed.reshape(row_count, HEADS, head_size)
    d_weights = jnp.einsum(
        "qhd,khd->hqk", d_mixed, saved["value_rows"], preferred_element_type=jnp.float32
    )
    d_values = jnp.einsum(
        "hqk,qhd->khd", saved["attn_low"], d_mixed, preferred_element_type=jnp.float32
    )
    attn_weights = saved["attn_weights"]
    d_scores = attn_weights * (
        d_weights - jnp.sum(attn_weights * d_weights, axis=-1, keepdims=True)
    )
    d_scores_low = jnp.where(allowed[None], d_scores, 0.0).astype(jnp.bfloat16)
    d_queries = (
        jnp.einsum(
            "hqk,khd->qhd", d_scores_low, saved["key_rows"], preferred_element_type=jnp.float32
        )
        * score_scale
    )
    d_keys = (
        jnp.einsum(
            "hqk,qhd->khd", d_scores_low, saved["queries"], preferred_element_type=jnp.float32
        )
        * score_scale
    )
    remote_part = jnp.concatenate(
        [
            d_keys[row_count:].reshape(-1, model_width),
            d_values[row_count:].reshape(-1, model_width),
        ],
        axis=1,
    )
    own_part = lax.psum_scatter(remote_part, "dp", scatter_dimension=0, tiled=True)
    local_pairs = jnp.concatenate(
        [
            d_keys[:row_count].reshape(row_count, model_width),
            d_values[:row_count].reshape(row_count, model_width),
        ],
        axis=1,
    )
    local_pairs = jnp.concatenate(
        [local_pairs[:latent_start], local_pairs[latent_start:] + own_part], axis=0
    )
    d_projected = jnp.concatenate(
        [d_queries.reshape(row_count, model_width), local_pairs], axis=1
    ).astype(jnp.bfloat16)
    grad_qkv = jnp.dot(d_projected.T, normed, preferred_element_type=jnp.float32)
    d_normed = jnp.dot(d_projected, w_qkv.T, preferred_element_type=jnp.float32)
    unused_rows, first_back = jax.vjp(layer_norm, all_rows, gain_attn)
    d_rows_norm, grad_gain_attn = first_back(d_normed)
    return (
        d_mid + d_rows_norm,
        (grad_gain_attn, grad_qkv, grad_out, grad_gain_mlp, grad_up, grad_down),
    )


def packed(grads, n):
    gain_first, qkv_grad, out_grad, gain_second, up_grad, down_grad = grads
    width = out_grad.shape[0]
    rows = width // n

    def by_rows(grad):
        return grad.reshape(n, -1, rows, width).transpose(1, 0, 2, 3).astype(jnp.bfloat16)

    down = down_grad.reshape(n, rows, -1, width).transpose(2, 0, 1, 3).astype(jnp.bfloat16)
    chunks = jnp.concatenate([down, by_rows(up_grad), by_rows(out_grad), by_rows(qkv_grad)], axis=0)
    gains = jnp.stack([gain_first.reshape(n, rows), gain_second.reshape(n, rows)], axis=1)
    return chunks, jnp.pad(gains, ((0, 0), (0, 6), (0, 128 - rows)))


def shards(
    grid,
    tokens,
    latents,
    slot_group,
    image_groups,
    gain_attn,
    w_qkv,
    w_out,
    gain_mlp,
    w_up,
    w_down,
    d_tokens,
    d_latents,
):
    micro = tokens.shape[0]
    tok_rows = tokens.shape[1]
    lat_rows = latents.shape[1]
    model_width = tokens.shape[2]
    local_groups = tok_rows // GROUP
    section_index = lax.axis_index("section")
    is_global = section_index == 1
    dp_index = lax.axis_index("dp")
    weights = (gain_attn[0], w_qkv[0], w_out[0], gain_mlp[0], w_up[0], w_down[0])
    image_ends = jnp.cumsum(image_groups, axis=1)
    slot_images = jnp.sum(
        (image_ends[:, None, :] <= slot_group[:, :, None]).astype(jnp.int32), axis=2
    )
    slot_total = slot_group.shape[1]
    row_group = jnp.concatenate([jnp.arange(tok_rows) // GROUP, jnp.arange(lat_rows) // LAT])
    row_latent = jnp.concatenate(
        [jnp.zeros((tok_rows,), jnp.bool_), jnp.ones((lat_rows,), jnp.bool_)]
    )
    same_group = row_group[:, None] == row_group[None, :]
    local_mask = jnp.where(
        is_global, (~row_latent)[:, None] & row_latent[None, :] & same_group, same_group
    )
    group_match = row_group[:, None] == jnp.arange(local_groups)[None, :]

    def key_images(batch):
        images_row = lax.dynamic_index_in_dim(slot_images, batch, 0, keepdims=False)
        return (images_row, jnp.broadcast_to(images_row[:, None], (slot_total, LAT)).reshape(-1))

    def allowed_for(batch):
        images_row, key_image = key_images(batch)
        own_images = lax.dynamic_slice_in_dim(images_row, dp_index * local_groups, local_groups)
        row_image = jnp.sum(jnp.where(group_match, own_images[None, :], 0), axis=1)
        remote_mask = is_global & row_latent[:, None] & (row_image[:, None] == key_image[None, :])
        return jnp.concatenate([local_mask, remote_mask], axis=1)

    def forward_turn(received, turn):
        recv_tokens, recv_latents = received
        batch = jnp.clip(turn - section_index, 0, micro - 1)
        own_tok = lax.dynamic_index_in_dim(tokens, batch, 0, keepdims=False)
        own_lat = lax.dynamic_index_in_dim(latents, batch, 0, keepdims=False)
        input_rows = jnp.concatenate(
            [
                jnp.where(is_global, recv_tokens, own_tok),
                jnp.where(is_global, recv_latents, own_lat),
            ],
            axis=0,
        )
        all_rows = input_rows.astype(jnp.float32)
        normed, projected = front_half(all_rows, weights[0], weights[1])
        remote_rows = lax.all_gather(
            latent_operand(projected, tok_rows, model_width), "dp", axis=0, tiled=True
        )
        saved = back_half(all_rows, projected, remote_rows, allowed_for(batch), weights)
        result = saved["result"]
        result_low = result.astype(jnp.bfloat16)
        stored = jnp.where(is_global, result, result_low.astype(jnp.float32))
        passed_on = from_behind((result_low[:tok_rows], result_low[tok_rows:]), "section", 1)
        return passed_on, (input_rows, stored[:tok_rows], stored[tok_rows:])

    nothing = (
        jnp.zeros((tok_rows, model_width), jnp.bfloat16),
        jnp.zeros((lat_rows, model_width), jnp.bfloat16),
    )
    turns = jnp.arange(micro + 1)
    unused_end, (kept_rows, tok_outputs, lat_outputs) = lax.scan(forward_turn, nothing, turns)

    def backward_turn(carry, turn):
        (recv_grad_tok, recv_grad_lat), totals = carry
        raw_batch = micro - turn - section_index
        valid = ((raw_batch >= 0) & (raw_batch < micro)).astype(jnp.float32)
        batch = jnp.clip(raw_batch, 0, micro - 1)
        all_rows = lax.dynamic_index_in_dim(
            kept_rows, batch + section_index, 0, keepdims=False
        ).astype(jnp.float32)
        normed, projected = front_half(all_rows, weights[0], weights[1])
        remote_rows = lax.all_gather(
            latent_operand(projected, tok_rows, model_width), "dp", axis=0, tiled=True
        )
        allowed = allowed_for(batch)
        saved = back_half(all_rows, projected, remote_rows, allowed, weights)
        given = (
            jnp.concatenate(
                [
                    lax.dynamic_index_in_dim(d_tokens, batch, 0, keepdims=False),
                    lax.dynamic_index_in_dim(d_latents, batch, 0, keepdims=False),
                ],
                axis=0,
            )
            * valid
        )
        passed = jnp.concatenate([recv_grad_tok, recv_grad_lat], axis=0).astype(jnp.float32)
        d_result = jnp.where(is_global, given, passed)
        d_rows, grads = section_backward(
            saved, d_result, all_rows, normed, allowed, weights, tok_rows
        )
        totals = tuple((accum + piece for accum, piece in zip(totals, grads)))
        d_rows_low = d_rows.astype(jnp.bfloat16)
        stored = jnp.where(is_global, d_rows_low.astype(jnp.float32), d_rows)
        sent = from_behind((d_rows_low[:tok_rows], d_rows_low[tok_rows:]), "section", -1)
        return (sent, totals), (stored[:tok_rows], stored[tok_rows:])

    totals = tuple(
        jnp.zeros(w.shape[::-1] if w.ndim == 2 else w.shape, jnp.float32) for w in weights
    )
    (unused_sent, totals), (tok_grads, lat_grads) = lax.scan(
        backward_turn, (nothing, totals), turns
    )
    chunks, gains = packed(totals, lax.axis_size("dp"))
    summed, gain_sums = spread(grid, chunks, gains)
    rows = summed.shape[1]
    layer_tokens = lax.dynamic_slice_in_dim(tok_outputs, section_index, micro, 0)[None]
    layer_latents = lax.dynamic_slice_in_dim(lat_outputs, section_index, micro, 0)[None]
    grad_tokens = lax.dynamic_slice_in_dim(tok_grads, 1 - section_index, micro, 0)[::-1][
        None
    ]
    grad_latents = lax.dynamic_slice_in_dim(lat_grads, 1 - section_index, micro, 0)[
        ::-1
    ][None]
    return (
        layer_tokens,
        layer_latents,
        grad_tokens,
        grad_latents,
        gain_sums[0:1, :rows],
        summed[9:].reshape(-1, model_width).T[None],
        summed[8].T[None],
        gain_sums[1:2, :rows],
        summed[4:8].reshape(-1, model_width).T[None],
        summed[0:4].transpose(0, 2, 1).reshape(-1, rows)[None],
    )


F32 = jnp.float32
LOW = jnp.bfloat16
HEAD_PAD = 16
BAND = 48
TILE = 768


def nn(a, b):
    return jnp.dot(a, b, preferred_element_type=F32)


def nt(a, b):
    return lax.dot_general(a, b, (((1,), (1,)), ((), ())), preferred_element_type=F32)


def tn(a, b):
    return lax.dot_general(a, b, (((0,), (0,)), ((), ())), preferred_element_type=F32)


def normed_rows(values):
    centred = values - jnp.mean(values, axis=-1, keepdims=True)
    scale = lax.rsqrt(jnp.mean(centred * centred, axis=-1, keepdims=True) + epsilon)
    return centred * scale, scale


def norm_back(grad, hat, scale, gain):
    scaled = grad * gain
    mean = jnp.mean(scaled, axis=-1, keepdims=True)
    along = jnp.mean(scaled * hat, axis=-1, keepdims=True)
    return scale * (scaled - mean - hat * along)


def at(start, size):
    return pl.ds(pl.multiple_of(start, size), size)


def class_max(s):
    for by in (16, 32, 64):
        s = jnp.maximum(s, pltpu.roll(s, by, 1))
    return s


def class_sum(s):
    for by in (16, 32, 64):
        s = s + pltpu.roll(s, by, 1)
    return s


def layer_kernel(
    grid,
    tokens,
    latents,
    key_mask,
    gain_attn,
    gain_mlp,
    w_qkv,
    w_out,
    w_up,
    w_down,
    d_tokens,
    d_latents,
    out_tok,
    out_lat,
    grad_tok,
    grad_lat,
    grads,
    summed,
    gain_sums,
    wq,
    wo,
    wu,
    wd,
    xb,
    n1,
    proj,
    mixed,
    mid,
    n2,
    act,
    dup,
    yb,
    dy,
    ef,
    tmp,
    out,
    probs,
    probs_lat,
    latf,
    mixf,
    qbd,
    kbd,
    vbd,
    kv_all,
    kvg_send,
    kvg_recv,
    stage,
    gains,
    own_a,
    own_b,
    land1_a,
    land1_b,
    land2_a,
    land2_b,
    land3_a,
    land3_b,
    land_g,
    load_sem,
    stage_sem,
    own_sem,
    send_sem,
    recv_sem,
    gain_s,
    gain_r,
    relay_send,
    relay_recv,
    kv_sem_s,
    kv_sem_r,
    kvg_sem_s,
    kvg_sem_r,
):
    l0, l1, l2 = grid
    n = l0 * l1 * l2
    rows, width = xb.shape
    ff = act.shape[1]
    tok = tokens.shape[0]
    lat = latents.shape[0]
    half = lat // LAT
    pairs = width // 128
    me = lax.axis_index("dp")
    section = lax.axis_index("section")
    first = section == 0
    second = section == 1
    partner = (me, 1 - section)

    loads = [
        pltpu.make_async_copy(src, dst, load_sem.at[i])
        for i, (src, dst) in enumerate(((w_qkv, wq), (w_out, wo), (w_up, wu), (w_down, wd)))
    ]
    x_loads = [
        pltpu.make_async_copy(tokens, xb.at[0:tok], load_sem.at[4]),
        pltpu.make_async_copy(latents, xb.at[tok:rows], load_sem.at[5]),
    ]
    e_loads = [
        pltpu.make_async_copy(d_tokens, ef.at[0:tok], load_sem.at[6]),
        pltpu.make_async_copy(d_latents, ef.at[tok:rows], load_sem.at[7]),
    ]

    @pl.when(first)
    def _():
        for copy in x_loads:
            copy.start()

    for copy in loads:
        copy.start()

    @pl.when(second)
    def _():
        for copy in e_loads:
            copy.start()

    barrier = pltpu.get_barrier_semaphore()
    pl.semaphore_signal(barrier, inc=1, device_id=partner, device_id_type=MESH)

    here = (me // (l1 * l2), lax.rem(me // l2, l1), lax.rem(me, l2))

    def along(axis, shift):
        there = list(here)
        there[axis] = lax.rem(here[axis] + shift, grid[axis])
        return there[axis], ((there[0] * l1 + there[1]) * l2 + there[2], section)

    @pl.when(second)
    def _():
        for shift in range(1, n):
            pl.semaphore_signal(
                barrier, inc=1, device_id=(lax.rem(me + shift, n), section), device_id_type=MESH
            )
        pl.semaphore_wait(barrier, n)

    @pl.when(first)
    def _():
        for axis in range(3):
            for shift in range(1, grid[axis]):
                pl.semaphore_signal(
                    barrier, inc=1, device_id=along(axis, shift)[1], device_id_type=MESH
                )
        pl.semaphore_wait(barrier, sum(grid) - 2)

    forward_relay = pltpu.make_async_remote_copy(
        src_ref=yb, dst_ref=xb, send_sem=relay_send.at[0], recv_sem=relay_recv.at[0],
        device_id=partner, device_id_type=MESH,
    )
    backward_relay = pltpu.make_async_remote_copy(
        src_ref=yb, dst_ref=dy, send_sem=relay_send.at[1], recv_sem=relay_recv.at[1],
        device_id=partner, device_id_type=MESH,
    )

    def kv_copy(shift, incoming):
        slot = lax.rem(me + n - shift, n) if incoming else me
        return pltpu.make_async_remote_copy(
            src_ref=kv_all.at[me], dst_ref=kv_all.at[slot],
            send_sem=kv_sem_s.at[shift - 1], recv_sem=kv_sem_r.at[shift - 1],
            device_id=(lax.rem(me + shift, n), section), device_id_type=MESH,
        )

    def kvg_copy(shift):
        there = lax.rem(me + shift, n)
        return pltpu.make_async_remote_copy(
            src_ref=kvg_send.at[there], dst_ref=kvg_recv.at[shift - 1],
            send_sem=kvg_sem_s.at[shift - 1], recv_sem=kvg_sem_r.at[shift - 1],
            device_id=(there, section), device_id_type=MESH,
        )

    lane = lax.broadcasted_iota(jnp.int32, (1, 128), 1)
    halves = [(lane < 64).astype(F32).astype(LOW), (lane >= 64).astype(F32).astype(LOW)]
    eighths = [(h.astype(F32) * 0.125).astype(LOW) for h in halves]
    heads = (
        lax.broadcasted_iota(jnp.int32, (HEAD_PAD, width), 1) // 64
        == lax.broadcasted_iota(jnp.int32, (HEAD_PAD, width), 0)
    ).astype(F32)

    def block_diagonal(dst, base, src, row, column, scale):
        for i in range(LAT):
            line = src[row + i : row + i + 1, column : column + width] * scale
            dst[base + i * HEAD_PAD : base + (i + 1) * HEAD_PAD, :] = (line * heads).astype(LOW)

    def head_sum(dst, row, column, value, scale, add):
        for i in range(LAT):
            line = jnp.sum(
                value[i * HEAD_PAD : (i + 1) * HEAD_PAD] * heads, axis=0, keepdims=True
            )
            line = line * scale
            if add:
                line = line + dst[row + i : row + i + 1, column : column + width]
            dst[row + i : row + i + 1, column : column + width] = line

    def bands(body):
        def one(i, carry):
            body(at(i * BAND, BAND))
            return carry

        lax.fori_loop(0, rows // BAND, one, 0)

    def tiles(count, body, size=TILE):
        def one(i, carry):
            body(at(i * size, size))
            return carry

        lax.fori_loop(0, count, one, 0)

    @pl.when(first)
    def _():
        for copy in x_loads:
            copy.wait()

    @pl.when(second)
    def _():
        forward_relay.wait_recv()

    def norm_in(r):
        hat, unused = normed_rows(xb[r, :].astype(F32))
        n1[r, :] = (hat * gain_attn[...]).astype(LOW)

    bands(norm_in)
    loads[0].wait()

    @pl.when(second)
    def _():
        own = nn(n1[tok:rows, :], wq[:, width:]).astype(LOW)
        kv_all[me] = own
        latf[:, width:] = own.astype(F32)
        for shift in range(1, n):
            kv_copy(shift, False).start()

    def project(c):
        proj[:, c] = nn(n1[...], wq[:, c]).astype(LOW)

    per = width // TILE
    tiles(jnp.where(first, 3 * per, per), project)

    def lat_bias(m, shape, axis):
        return jnp.where(
            lax.broadcasted_iota(jnp.int32, shape, axis) // LAT == m, 0.0, masked_score
        ).astype(F32)

    @pl.when(first)
    def _():
        latf[...] = proj[tok:rows, :].astype(F32)

        def pair(it, carry):
            m, p = it // pairs, lax.rem(it, pairs)
            r = at(m * GROUP, GROUP)
            q = proj[r, at(p * 128, 128)]
            k = proj[r, at(width + p * 128, 128)]
            v = proj[r, at(2 * width + p * 128, 128)]
            kl = proj[tok:rows, at(width + p * 128, 128)]
            vl = proj[tok:rows, at(2 * width + p * 128, 128)]
            bias = lat_bias(m, (lat, GROUP), 0)
            total = jnp.zeros((GROUP, 128), F32)
            for e in (0, 1):
                qe = q * eighths[e]
                st = nt(k, qe)
                sl = nt(kl, qe) + bias
                top = jnp.maximum(
                    jnp.max(st, axis=0, keepdims=True), jnp.max(sl, axis=0, keepdims=True)
                )
                et = jnp.exp(st - top)
                el = jnp.exp(sl - top)
                scale = 1.0 / (
                    jnp.sum(et, axis=0, keepdims=True) + jnp.sum(el, axis=0, keepdims=True)
                )
                pt = (et * scale).astype(LOW)
                pe = (el * scale).astype(LOW)
                probs[2 * it + e, 0:GROUP, :] = pt
                probs[2 * it + e, GROUP : GROUP + lat, :] = pe
                total += tn(pt, v * halves[e]) + tn(pe, vl * halves[e])
            mixed[r, at(p * 128, 128)] = total.astype(LOW)
            return carry

        lax.fori_loop(0, half * pairs, pair, 0)
        for m in range(half):
            r = slice(m * GROUP, (m + 1) * GROUP)
            b = slice(m * 128, (m + 1) * 128)
            block_diagonal(qbd, m * 128, latf, m * LAT, 0, 0.125)
            s = nt(qbd[b, :], proj[r, width : 2 * width])
            sl = nt(qbd[b, :], proj[tok:rows, width : 2 * width]) + lat_bias(m, (128, lat), 1)
            top = jnp.maximum(
                jnp.max(s, axis=1, keepdims=True), jnp.max(sl, axis=1, keepdims=True)
            )
            et = jnp.exp(s - top)
            el = jnp.exp(sl - top)
            scale = 1.0 / (
                jnp.sum(et, axis=1, keepdims=True) + jnp.sum(el, axis=1, keepdims=True)
            )
            pt = (et * scale).astype(LOW)
            pe = (el * scale).astype(LOW)
            probs_lat[b, 0:GROUP] = pt
            probs_lat[b, GROUP : GROUP + lat] = pe
            o = nn(pt, proj[r, 2 * width :]) + nn(pe, proj[tok:rows, 2 * width :])
            head_sum(mixf, m * LAT, 0, o, 1.0, False)
        mixed[tok:rows, :] = mixf[...].astype(LOW)

    keys = n * lat

    @pl.when(second)
    def _():
        latf[:, :width] = proj[tok:rows, :width].astype(F32)
        for m in range(half):
            r = slice(m * GROUP, (m + 1) * GROUP)
            b = slice(m * 128, (m + 1) * 128)
            block_diagonal(qbd, m * 128, latf, m * LAT, 0, 0.125)
            block_diagonal(kbd, m * 128, latf, m * LAT, width, 1.0)
            block_diagonal(vbd, m * 128, latf, m * LAT, 2 * width, 1.0)
            s = nt(proj[r, :width] * jnp.asarray(0.125, LOW), kbd[b, :])
            et = jnp.exp(s - class_max(s))
            pt = (et / class_sum(et)).astype(LOW)
            probs[m, 0:GROUP, 0:128] = pt
            mixed[r, :] = nn(pt, vbd[b, :]).astype(LOW)
        for shift in range(1, n):
            kv_copy(shift, True).wait_recv()
        k = kv_all[:, :, :width].reshape(keys, width)
        v = kv_all[:, :, width:].reshape(keys, width)
        for m in range(half):
            b = slice(m * 128, (m + 1) * 128)
            s = nt(qbd[b, :], k) + key_mask[m : m + 1, :]
            et = jnp.exp(s - jnp.max(s, axis=1, keepdims=True))
            pt = (et / jnp.sum(et, axis=1, keepdims=True)).astype(LOW)
            probs_lat[b, 0:keys] = pt
            head_sum(mixf, m * LAT, 0, nn(pt, v), 1.0, False)
        mixed[tok:rows, :] = mixf[...].astype(LOW)

    loads[1].wait()

    def attend_out(c):
        mid[:, c] = xb[:, c].astype(F32) + nn(mixed[...], wo[:, c])

    tiles(width // TILE, attend_out)

    def norm_mid(r):
        hat, unused = normed_rows(mid[r, :])
        n2[r, :] = (hat * gain_mlp[...]).astype(LOW)

    bands(norm_mid)
    loads[2].wait()
    root = 0.7978845608028654

    def widen(c):
        up = nn(n2[...], wu[:, c])
        square = up * up
        t = jnp.tanh(up * (root + (root * 0.044715) * square))
        gate = 0.5 + 0.5 * t
        value = up * gate
        slope = gate + 2.0 * value * (1.0 - gate) * (root + (3.0 * root * 0.044715) * square)
        act[:, c] = value.astype(LOW)
        dup[:, c] = slope.astype(LOW)

    tiles(ff // TILE, widen)
    loads[3].wait()

    def narrow(c):
        y = mid[:, c] + nn(act[...], wd[:, c])
        low = y.astype(LOW)
        yb[:, c] = low
        out[:, c] = jnp.where(first, low.astype(F32), y)

    tiles(width // TILE, narrow)
    out_copies = [
        pltpu.make_async_copy(out.at[0:tok], out_tok, load_sem.at[8]),
        pltpu.make_async_copy(out.at[tok:rows], out_lat, load_sem.at[9]),
    ]
    grad_copies = [
        pltpu.make_async_copy(out.at[0:tok], grad_tok, load_sem.at[8]),
        pltpu.make_async_copy(out.at[tok:rows], grad_lat, load_sem.at[9]),
    ]
    for copy in out_copies:
        copy.start()

    @pl.when(first)
    def _():
        forward_relay.start()
        backward_relay.wait_recv()

        def widen_e(r):
            ef[r, :] = dy[r, :].astype(F32)

        bands(widen_e)

    @pl.when(second)
    def _():
        for copy in e_loads:
            copy.wait()

        def narrow_e(r):
            dy[r, :] = ef[r, :].astype(LOW)

        bands(narrow_e)

    part = 384
    unit = width // n
    many = part // unit

    def staged(slot, piece, chunk, share):
        return pltpu.make_async_copy(
            stage.at[slot, piece],
            grads.at[chunk, share // (l1 * l2), lax.rem(share // l2, l1), lax.rem(share, l2)],
            stage_sem.at[slot, piece],
        )

    def drain(slot):
        def one(piece, carry):
            staged(slot, piece, 0, 0).wait()
            return carry

        lax.fori_loop(0, many, one, 0)

    def weight_grad(place, start, count, left, right):
        def one(i, carry):
            slot = lax.rem(i, 2)
            value = tn(left(i), right(i)).astype(LOW)

            @pl.when(i >= start + 2)
            def _():
                drain(slot)

            for piece in range(many):
                stage[slot, piece] = value[piece * unit : (piece + 1) * unit]
                staged(slot, piece, *place(i * many + piece)).start()
            return carry

        lax.fori_loop(start, start + count, one, 0)
        for slot in (0, 1):
            drain(slot)

    orders = ((2, 1, 0), (1, 2, 0))
    own_buf = (own_a, own_b)
    land = ((land1_a, land1_b), (land2_a, land2_b), (land3_a, land3_b))
    spread_pairs = land1_a.shape[0]

    def whole(stream, k, index):
        if stream == 0:
            return grads.at[2 * k, :, :, index]
        return grads.at[2 * k + 1, :, index]

    def source(stream, phase, k, index):
        if phase == 0:
            return whole(stream, k, index)
        if phase == 1:
            return land[0][stream].at[k, 0, :, index]
        return land[0][stream].at[k, 0, index, here[orders[stream][1]]]

    def copies(stream, phase, k):
        axis = orders[stream][phase]
        for shift in range(1, grid[axis]):
            index, target = along(axis, shift)
            yield pltpu.make_async_remote_copy(
                src_ref=source(stream, phase, k, index),
                dst_ref=land[phase][stream].at[k, shift - 1],
                send_sem=send_sem.at[stream, phase, k, shift - 1],
                recv_sem=recv_sem.at[stream, phase, k, shift - 1],
                device_id=target,
                device_id_type=MESH,
            )

    def own(stream, k):
        return pltpu.make_async_copy(
            whole(stream, k, here[orders[stream][0]]), own_buf[stream], own_sem.at[stream]
        )

    def launch(phase, k):
        for stream in (0, 1):
            for copy in copies(stream, phase, k):
                copy.start()

    def absorb(phase, k):
        for stream in (0, 1):
            axis = orders[stream][phase]
            if phase == 0:
                own(stream, k).wait()
            for copy in copies(stream, phase, k):
                copy.wait_recv()
            base = land[0][stream]
            into = land[phase][stream]
            if phase == 0:
                for i in range(base.shape[2]):
                    for j in range(base.shape[3]):
                        total = own_buf[stream][i, j].astype(F32)
                        for s in range(grid[axis] - 1):
                            total += into[k, s, i, j].astype(F32)
                        base[k, 0, i, j] = total.astype(LOW)
            elif phase == 1:
                for i in range(base.shape[2]):
                    total = base[k, 0, i, here[axis]].astype(F32)
                    for s in range(grid[axis] - 1):
                        total += into[k, s, i].astype(F32)
                    base[k, 0, i, here[axis]] = total.astype(LOW)
            else:
                total = base[k, 0, here[0], here[orders[stream][1]]].astype(F32)
                for s in range(grid[axis] - 1):
                    total += into[k, s].astype(F32)
                summed[2 * k + stream] = total

    def turn(t):
        def stage_of(ok, body):
            if isinstance(ok, bool):
                if ok:
                    body()
            else:
                pl.when(ok)(body)

        def first_stage():
            absorb(0, t)
            launch(1, t)

        def second_stage():
            absorb(1, t - 1)
            launch(2, t - 1)

        def next_own():
            for stream in (0, 1):
                own(stream, t + 1).start()

        stage_of(t < spread_pairs, first_stage)
        stage_of(t + 1 < spread_pairs, next_own)
        late = (t >= 1) & (t - 1 < spread_pairs)
        stage_of(late, second_stage)
        stage_of(t >= 2, lambda: absorb(2, t - 2))

    wide = ff // width
    per_part = width // part

    def down_grad(start, count):
        weight_grad(
            lambda p: (p // n, lax.rem(p, n)),
            start,
            count,
            lambda i: dy[:, at(lax.rem(i, per_part) * part, part)],
            lambda i: act[:, at((i // per_part) * width, width)],
        )

    down_grad(0, ff // part // 2)
    launch(0, 0)
    for stream in (0, 1):
        own(stream, 0).start()
    down_grad(ff // part // 2, ff // part // 2)
    launch(0, 1)

    def unwiden(c):
        dup[:, c] = (nt(dy[...], wd[c, :]) * dup[:, c].astype(F32)).astype(LOW)

    tiles(ff // TILE, unwiden)
    weight_grad(
        lambda p: (wide + lax.rem(p, wide), p // wide),
        0,
        ff // part,
        lambda i: dup[:, at(i * part, part)],
        lambda i: n2[...],
    )
    launch(0, 2)
    launch(0, 3)

    def to_mid(c):
        tmp[:, c] = nt(dup[...], wu[c, :])

    tiles(width // TILE, to_mid)
    gains[0] = jnp.zeros_like(gains[0])

    def fold(value):
        total = value[0:8]
        for i in range(1, BAND // 8):
            total = total + value[8 * i : 8 * i + 8]
        return total

    def mid_back(r):
        hat, scale = normed_rows(mid[r, :])
        grad = tmp[r, :]
        gains[0, 8:16, :] += fold(grad * hat)
        total = ef[r, :] + norm_back(grad, hat, scale, gain_mlp[...])
        ef[r, :] = total
        dy[r, :] = total.astype(LOW)

    bands(mid_back)

    def to_mix(c):
        n2[:, c] = nt(dy[...], wo[c, :]).astype(LOW)

    tiles(width // TILE, to_mix)
    weight_grad(
        lambda p: (2 * wide, p),
        0,
        width // part,
        lambda i: dy[:, at(i * part, part)],
        lambda i: mixed[...],
    )
    mixf[...] = n2[tok:rows, :].astype(F32)
    turn(0)
    for copy in out_copies:
        copy.wait()

    @pl.when(first)
    def _():
        for m in range(half):
            r = slice(m * GROUP, (m + 1) * GROUP)
            b = slice(m * 128, (m + 1) * 128)
            block_diagonal(vbd, m * 128, mixf, m * LAT, 0, 1.0)
            do = vbd[b, :]
            dp = nt(do, proj[r, 2 * width :])
            dl = nt(do, proj[tok:rows, 2 * width :])
            pt = probs_lat[b, 0:GROUP]
            pe = probs_lat[b, GROUP : GROUP + lat]
            pf = pt.astype(F32)
            pg = pe.astype(F32)
            along = jnp.sum(pf * dp, axis=1, keepdims=True) + jnp.sum(
                pg * dl, axis=1, keepdims=True
            )
            ds = (pf * (dp - along)).astype(LOW)
            dsl = (pg * (dl - along)).astype(LOW)
            dq = nn(ds, proj[r, width : 2 * width]) + nn(dsl, proj[tok:rows, width : 2 * width])
            head_sum(latf, m * LAT, 0, dq, 0.125, False)
            tmp[r, :] = tn(ds, qbd[b, :])
            out[r, :] = tn(pt, do)
            if m == 0:
                tmp[tok:rows, :] = tn(dsl, qbd[b, :])
                out[tok:rows, :] = tn(pe, do)
            else:
                tmp[tok:rows, :] += tn(dsl, qbd[b, :])
                out[tok:rows, :] += tn(pe, do)
        proj[tok:rows, :width] = latf[:, :width].astype(LOW)

        def pair(it, carry):
            m, p = it // pairs, lax.rem(it, pairs)
            r = at(m * GROUP, GROUP)
            qc = at(p * 128, 128)
            q = proj[r, qc]
            k = proj[r, at(width + p * 128, 128)]
            v = proj[r, at(2 * width + p * 128, 128)]
            kl = proj[tok:rows, at(width + p * 128, 128)]
            vl = proj[tok:rows, at(2 * width + p * 128, 128)]
            dx = n2[r, qc]
            dq = jnp.zeros((GROUP, 128), F32)
            dk = tmp[r, qc]
            dv = out[r, qc]
            dkl = tmp[tok:rows, qc]
            dvl = out[tok:rows, qc]
            for e in (0, 1):
                qe = q * eighths[e]
                de = dx * halves[e]
                pt = probs[2 * it + e, 0:GROUP, :]
                pe = probs[2 * it + e, GROUP : GROUP + lat, :]
                pf = pt.astype(F32)
                pg = pe.astype(F32)
                dp = nt(v, de)
                dl = nt(vl, de)
                along = jnp.sum(pf * dp, axis=0, keepdims=True) + jnp.sum(
                    pg * dl, axis=0, keepdims=True
                )
                ds = (pf * (dp - along)).astype(LOW)
                dsl = (pg * (dl - along)).astype(LOW)
                dq += tn(ds, k * halves[e]) + tn(dsl, kl * halves[e])
                dk += nn(ds, qe)
                dkl += nn(dsl, qe)
                dv += nn(pt, de)
                dvl += nn(pe, de)
            proj[r, qc] = (dq * 0.125).astype(LOW)
            proj[r, at(width + p * 128, 128)] = dk.astype(LOW)
            proj[r, at(2 * width + p * 128, 128)] = dv.astype(LOW)
            tmp[tok:rows, qc] = dkl
            out[tok:rows, qc] = dvl
            return carry

        lax.fori_loop(0, half * pairs, pair, 0)
        proj[tok:rows, width : 2 * width] = tmp[tok:rows, :].astype(LOW)
        proj[tok:rows, 2 * width :] = out[tok:rows, :].astype(LOW)

    @pl.when(second)
    def _():
        k = kv_all[:, :, :width].reshape(keys, width)
        v = kv_all[:, :, width:].reshape(keys, width)
        for m in range(half):
            b = slice(m * 128, (m + 1) * 128)
            block_diagonal(vbd.at[pl.ds(256, 256)], m * 128, mixf, m * LAT, 0, 1.0)
        both = slice(0, half * 128)
        do = vbd[256 : 256 + half * 128, :]
        pt = probs_lat[both, 0:keys]
        pf = pt.astype(F32)
        dp = nt(do, v)
        along = jnp.sum(pf * dp, axis=1, keepdims=True)
        ds = (pf * (dp - along)).astype(LOW)
        kvg_send[:, :, :width] = tn(ds, qbd[both, :]).astype(LOW).reshape(n, lat, width)
        kvg_send[:, :, width:] = tn(pt, do).astype(LOW).reshape(n, lat, width)
        for shift in range(1, n):
            kvg_copy(shift).start()
        dq = nn(ds, k)
        for m in range(half):
            head_sum(latf, m * LAT, 0, dq[m * 128 : (m + 1) * 128], 0.125, False)
        proj[tok:rows, :width] = latf[:, :width].astype(LOW)
        for m in range(half):
            r = slice(m * GROUP, (m + 1) * GROUP)
            b = slice(m * 128, (m + 1) * 128)
            pt = probs[m, 0:GROUP, 0:128]
            pf = pt.astype(F32)
            dx = n2[r, :]
            dp = nt(dx, vbd[b, :])
            ds = (pf * (dp - class_sum(pf * dp))).astype(LOW)
            dk = tn(ds, proj[r, :width])
            dv = tn(pt, dx)
            proj[r, :width] = (nn(ds, kbd[b, :]) * 0.125).astype(LOW)
            head_sum(latf, m * LAT, width, dk, 0.125, False)
            head_sum(latf, m * LAT, 2 * width, dv, 1.0, False)
        total = latf[:, width:] + kvg_send[me].astype(F32)
        for shift in range(1, n):
            kvg_copy(shift).wait_recv()
            total += kvg_recv[shift - 1].astype(F32)
        proj[tok:rows, width:] = total.astype(LOW)

    turn(1)

    @pl.when(first)
    def _():
        tmp[...] = nt(proj[...], wq[...])

    @pl.when(second)
    def _():
        tmp[0:tok, :] = nt(proj[0:tok, :width], wq[:, :width])
        tmp[tok:rows, :] = nt(proj[tok:rows, :], wq[...])

    @pl.when(first)
    def _():
        forward_relay.wait_send()

    def in_back(r):
        hat, scale = normed_rows(xb[r, :].astype(F32))
        grad = tmp[r, :]
        gains[0, 0:8, :] += fold(grad * hat)
        total = ef[r, :] + norm_back(grad, hat, scale, gain_attn[...])
        low = total.astype(LOW)
        yb[r, :] = low
        out[r, :] = jnp.where(first, total, low.astype(F32))

    bands(in_back)
    for copy in grad_copies:
        copy.start()

    @pl.when(second)
    def _():
        backward_relay.start()

    def qkv_grad(start, count, r):
        weight_grad(
            lambda p: (2 * wide + 1 + lax.rem(p, 3), p // 3),
            start,
            count,
            lambda i: proj[r, at(i * part, part)],
            lambda i: n1[r, :],
        )

    @pl.when(first)
    def _():
        qkv_grad(0, 3 * per_part, slice(0, rows))

    @pl.when(second)
    def _():
        qkv_grad(0, per_part, slice(0, rows))
        qkv_grad(per_part, 2 * per_part, slice(tok, rows))

    for pair in range(4, spread_pairs):
        launch(0, pair)

    def gain_copy(axis, shift):
        return pltpu.make_async_remote_copy(
            src_ref=gains.at[2 - axis],
            dst_ref=land_g.at[2 - axis, shift - 1],
            send_sem=gain_s.at[axis, shift - 1],
            recv_sem=gain_r.at[axis, shift - 1],
            device_id=along(axis, shift)[1],
            device_id_type=MESH,
        )

    def gain_step(axis):
        total = gains[2 - axis]
        for shift in range(1, grid[axis]):
            gain_copy(axis, shift).wait_recv()
            total = total + land_g[2 - axis, shift - 1]
        gains[3 - axis] = total

    def gain_start(axis):
        for shift in range(1, grid[axis]):
            gain_copy(axis, shift).start()

    gain_start(2)
    turn(2)
    gain_step(2)
    gain_start(1)
    turn(3)
    gain_step(1)
    gain_start(0)

    def later(t, carry):
        turn(t)
        return carry

    lax.fori_loop(4, spread_pairs + 2, later, 0)
    gain_step(0)
    final = gains[3]
    gain_sums[0:8, :] = jnp.broadcast_to(jnp.sum(final[0:8], axis=0, keepdims=True), (8, width))
    gain_sums[8:16, :] = jnp.broadcast_to(jnp.sum(final[8:16], axis=0, keepdims=True), (8, width))

    def finish(k, carry):
        for stream in (0, 1):
            for phase in range(3):
                for copy in copies(stream, phase, k):
                    copy.wait_send()
        return carry

    lax.fori_loop(0, spread_pairs, finish, 0)
    for axis in range(3):
        for shift in range(1, grid[axis]):
            gain_copy(axis, shift).wait_send()
    for copy in grad_copies:
        copy.wait()

    @pl.when(second)
    def _():
        backward_relay.wait_send()
        for shift in range(1, n):
            kv_copy(shift, False).wait_send()
            kvg_copy(shift).wait_send()


def both_layers(grid, tokens, latents, key_mask, gains, weights, d_tokens, d_latents):
    l0, l1, l2 = grid
    n = l0 * l1 * l2
    tok, width = tokens.shape
    lat = latents.shape[0]
    rows = tok + lat
    w_qkv, w_out, w_up, w_down = weights
    ff = w_up.shape[1]
    keys = n * lat
    half = lat // LAT
    size = sum(w.size for w in weights)
    chunks = size // (width * width)
    pairs = chunks // 2
    unit = width // n
    most = max(grid) - 1
    vm, hbm = pl.BlockSpec(memory_space=pltpu.VMEM), pl.BlockSpec(memory_space=pl.ANY)
    scratch = [
        pltpu.VMEM(w.shape, LOW) for w in (w_qkv, w_out, w_up, w_down)
    ] + [
        pltpu.VMEM(shape, dtype)
        for shape, dtype in (
            ((rows, width), LOW),
            ((rows, width), LOW),
            ((rows, 3 * width), LOW),
            ((rows, width), LOW),
            ((rows, width), F32),
            ((rows, width), LOW),
            ((rows, ff), LOW),
            ((rows, ff), LOW),
            ((rows, width), LOW),
            ((rows, width), LOW),
            ((rows, width), F32),
            ((rows, width), F32),
            ((rows, width), F32),
            ((half * width // 64, GROUP + lat, GROUP), LOW),
            ((half * 128, max(keys, GROUP + 128)), LOW),
            ((lat, 3 * width), F32),
            ((lat, width), F32),
            ((half * 128, width), LOW),
            ((half * 128, width), LOW),
            ((half * 256, width), LOW),
            ((n, lat, 2 * width), LOW),
            ((n, lat, 2 * width), LOW),
            ((n - 1, lat, 2 * width), LOW),
            ((2, 384 // unit, unit, width), LOW),
            ((4, 16, width), F32),
            ((l0, l1, unit, width), LOW),
            ((l0, l2, unit, width), LOW),
            ((pairs, l2 - 1, l0, l1, unit, width), LOW),
            ((pairs, l1 - 1, l0, l2, unit, width), LOW),
            ((pairs, l1 - 1, l0, unit, width), LOW),
            ((pairs, l2 - 1, l0, unit, width), LOW),
            ((pairs, l0 - 1, unit, width), LOW),
            ((pairs, l0 - 1, unit, width), LOW),
            ((3, max(grid) - 1, 16, width), F32),
        )
    ] + [
        pltpu.SemaphoreType.DMA((10,)),
        pltpu.SemaphoreType.DMA((2, 384 // unit)),
        pltpu.SemaphoreType.DMA((2,)),
        pltpu.SemaphoreType.DMA((2, 3, pairs, most)),
        pltpu.SemaphoreType.DMA((2, 3, pairs, most)),
        pltpu.SemaphoreType.DMA((3, most)),
        pltpu.SemaphoreType.DMA((3, most)),
        pltpu.SemaphoreType.DMA((2,)),
        pltpu.SemaphoreType.DMA((2,)),
        pltpu.SemaphoreType.DMA((n - 1,)),
        pltpu.SemaphoreType.DMA((n - 1,)),
        pltpu.SemaphoreType.DMA((n - 1,)),
        pltpu.SemaphoreType.DMA((n - 1,)),
    ]
    return pl.pallas_call(
        functools.partial(layer_kernel, grid),
        out_shape=(
            jax.ShapeDtypeStruct((tok, width), F32),
            jax.ShapeDtypeStruct((lat, width), F32),
            jax.ShapeDtypeStruct((tok, width), F32),
            jax.ShapeDtypeStruct((lat, width), F32),
            jax.ShapeDtypeStruct((chunks, l0, l1, l2, unit, width), LOW),
            jax.ShapeDtypeStruct((chunks, unit, width), F32),
            jax.ShapeDtypeStruct((16, width), F32),
        ),
        in_specs=[hbm, hbm, vm, vm, vm] + [hbm] * 6,
        out_specs=(hbm,) * 5 + (vm, vm),
        scratch_shapes=scratch,
        compiler_params=pltpu.CompilerParams(
            collective_id=1, has_side_effects=True, vmem_limit_bytes=63 * 1024 * 1024
        ),
        cost_estimate=pl.CostEstimate(
            flops=6 * rows * size, bytes_accessed=4 * size, transcendentals=0
        ),
    )(tokens, latents, key_mask, *gains, *weights, d_tokens, d_latents)


def fused_shards(
    grid,
    tokens,
    latents,
    slot_group,
    image_groups,
    gain_attn,
    w_qkv,
    w_out,
    gain_mlp,
    w_up,
    w_down,
    d_tokens,
    d_latents,
):
    micro, tok, width = tokens.shape
    lat = latents.shape[1]
    n = slot_group.shape[1]
    dp_index = lax.axis_index("dp")
    image_ends = jnp.cumsum(image_groups, axis=1)
    images = jnp.sum((image_ends[:, None, :] <= slot_group[:, :, None]).astype(jnp.int32), axis=2)
    own = lax.dynamic_slice_in_dim(images, dp_index, 1, 1)
    same = (images == own)[:, :, None, None] & jnp.eye(micro, dtype=jnp.bool_)[:, None, :, None]
    bias = jnp.where(same, 0.0, masked_score).astype(F32)
    bias = jnp.broadcast_to(bias, (micro, n, micro, lat)).reshape(micro, -1)
    out_tok, out_lat, grad_tok, grad_lat, unused_grads, summed, gains = both_layers(
        grid,
        tokens.reshape(micro * tok, width),
        latents.reshape(micro * lat, width),
        bias,
        (gain_attn, gain_mlp),
        (w_qkv[0], w_out[0], w_up[0], w_down[0]),
        d_tokens.reshape(micro * tok, width),
        d_latents.reshape(micro * lat, width),
    )
    unit = width // n
    gains = lax.dynamic_slice_in_dim(gains, dp_index * unit, unit, 1)
    wide = w_up.shape[2] // width
    return (
        out_tok.reshape(1, micro, tok, width),
        out_lat.reshape(1, micro, lat, width),
        grad_tok.reshape(1, micro, tok, width),
        grad_lat.reshape(1, micro, lat, width),
        gains[0:1],
        summed[2 * wide + 1 :].reshape(-1, width).T[None],
        summed[2 * wide].T[None],
        gains[8:9],
        summed[wide : 2 * wide].reshape(-1, width).T[None],
        summed[0:wide].transpose(0, 2, 1).reshape(-1, unit)[None],
    )


def solution(mesh):
    in_specs = (
        P(None, "dp", None),
        P(None, "dp", None),
        P(),
        P(),
        P("section", None),
        P("section", None, None),
        P("section", None, None),
        P("section", None),
        P("section", None, None),
        P("section", None, None),
        P(None, "dp", None),
        P(None, "dp", None),
    )
    out_specs = (
        P("section", None, "dp", None),
        P("section", None, "dp", None),
        P("section", None, "dp", None),
        P("section", None, "dp", None),
        P("section", "dp"),
        P("section", None, "dp"),
        P("section", None, "dp"),
        P("section", "dp"),
        P("section", None, "dp"),
        P("section", None, "dp"),
    )
    grid = grid_of(mesh)

    def program(*args):
        n, width = mesh.shape["dp"], args[0].shape[2]
        one_group = args[0].shape[1] == n * GROUP
        body = fused_shards if one_group and width % (16 * n) == 0 and min(grid) > 1 else shards
        return jax.shard_map(
            functools.partial(body, grid), mesh=mesh, in_specs=in_specs, out_specs=out_specs, check_vma=False
        )(*args)

    return program
```

```python
import functools

import jax
import jax.numpy as jnp
from jax import lax
from jax.experimental import pallas as pl
from jax.experimental.pallas import tpu as pltpu
from jax.sharding import PartitionSpec as P

HEADS = 12
GROUP = 256
LAT = 8


epsilon = 1e-05
masked_score = -1e30


MESH = pl.DeviceIdType.MESH


def grid_of(mesh):
    n = mesh.shape["dp"]
    coords = [getattr(d, "coords", None) for d in mesh.devices.reshape(n, -1)[:, 0]]
    if any(c is None for c in coords):
        return (n // 4, 2, 2) if n % 4 == 0 else (n, 1, 1)
    sizes = {a: len({c[a] for c in coords}) for a in range(3)}
    strides = {
        a: min([i for i in range(n) if coords[i][a] != coords[0][a]], default=n) for a in range(3)
    }
    order = sorted(range(3), key=lambda a: -strides[a])
    return tuple(sizes[a] for a in order)


def spread_kernel(grid, pairs, g_ref, gain_ref, out_ref, gout_ref, *scratch):
    acc = scratch[0:3]
    land = [scratch[3 + 3 * i : 6 + 3 * i] for i in range(3)]
    send_sem, recv_sem, own_sem = scratch[12:15]
    me = lax.axis_index("dp")
    section = lax.axis_index("section")
    l0, l1, l2 = grid
    here = (me // (l1 * l2), lax.rem(me // l2, l1), lax.rem(me, l2))

    def device(axis, shift):
        there = list(here)
        there[axis] = lax.rem(here[axis] + shift, grid[axis])
        return there[axis], ((there[0] * l1 + there[1]) * l2 + there[2], section)

    barrier = pltpu.get_barrier_semaphore()
    for axis in range(3):
        for shift in range(1, grid[axis]):
            pl.semaphore_signal(
                barrier, inc=1, device_id=device(axis, shift)[1], device_id_type=MESH
            )
    pl.semaphore_wait(barrier, sum(grid) - 3)

    orders = ((2, 1, 0), (1, 2, 0), (2, 1, 0))

    def source(stream, phase, k, at):
        if phase == 0:
            if stream == 0:
                return g_ref.at[2 * k, :, :, at]
            if stream == 1:
                return g_ref.at[2 * k + 1, :, at]
            return gain_ref.at[:, :, at]
        if phase == 1:
            return acc[stream].at[k, :, at]
        return acc[stream].at[k, at, here[orders[stream][1]]]

    def copies(stream, phase, k):
        axis = orders[stream][phase]
        for shift in range(1, grid[axis]):
            at, target = device(axis, shift)
            yield pltpu.make_async_remote_copy(
                src_ref=source(stream, phase, k, at),
                dst_ref=land[phase][stream].at[k, shift - 1],
                send_sem=send_sem.at[stream, phase, k, shift - 1],
                recv_sem=recv_sem.at[stream, phase, k, shift - 1],
                device_id=target,
                device_id_type=MESH,
            )

    def own(stream, k):
        return pltpu.make_async_copy(
            source(stream, 0, k, here[orders[stream][0]]), acc[stream].at[k], own_sem.at[stream, k]
        )

    def launch(stream, phase, k):
        for copy in copies(stream, phase, k):
            copy.start()

    def absorb(stream, phase, k):
        axis = orders[stream][phase]
        if phase == 0:
            own(stream, k).wait()
        for copy in copies(stream, phase, k):
            copy.wait_recv()
        into = land[phase][stream]
        count = grid[axis] - 1
        if phase == 0:
            for a in range(acc[stream].shape[1]):
                for b in range(acc[stream].shape[2]):
                    total = acc[stream][k, a, b].astype(jnp.float32)
                    for s in range(count):
                        total += into[k, s, a, b].astype(jnp.float32)
                    acc[stream][k, a, b] = total.astype(acc[stream].dtype)
        elif phase == 1:
            mine = here[axis]
            for a in range(acc[stream].shape[1]):
                total = acc[stream][k, a, mine].astype(jnp.float32)
                for s in range(count):
                    total += into[k, s, a].astype(jnp.float32)
                acc[stream][k, a, mine] = total.astype(acc[stream].dtype)
        else:
            total = acc[stream][k, here[0], here[orders[stream][1]]].astype(jnp.float32)
            for s in range(count):
                total += into[k, s].astype(jnp.float32)
            if stream < 2:
                out_ref[2 * k + stream] = total
            else:
                gout_ref[...] = total

    own(2, 0).start()
    launch(2, 0, 0)

    def start_own(k, carry):
        for stream in (0, 1):
            own(stream, k).start()
        return carry

    for stream in (0, 1):
        launch(stream, 0, 0)
    lax.fori_loop(0, pairs, start_own, 0)

    def turn(t, carry):
        @pl.when(t + 1 < pairs)
        def _():
            for stream in (0, 1):
                launch(stream, 0, t + 1)

        @pl.when(t < pairs)
        def _():
            for stream in (0, 1):
                absorb(stream, 0, t)
                launch(stream, 1, t)

        @pl.when((t >= 1) & (t - 1 < pairs))
        def _():
            for stream in (0, 1):
                absorb(stream, 1, t - 1)
                launch(stream, 2, t - 1)

        @pl.when(t >= 2)
        def _():
            for stream in (0, 1):
                absorb(stream, 2, t - 2)

        return carry

    lax.fori_loop(0, pairs + 2, turn, 0)
    absorb(2, 0, 0)
    launch(2, 1, 0)
    absorb(2, 1, 0)
    launch(2, 2, 0)
    absorb(2, 2, 0)

    def finish(k, carry):
        for stream in (0, 1):
            for phase in range(3):
                for copy in copies(stream, phase, k):
                    copy.wait_send()
        return carry

    lax.fori_loop(0, pairs, finish, 0)
    for phase in range(3):
        for copy in copies(2, phase, 0):
            copy.wait_send()


def spread(grid, grads, gains):
    chunks, n, rows, width = grads.shape
    pairs = chunks // 2
    l0, l1, l2 = grid
    most = max(max(grid) - 1, 1)
    low = jnp.bfloat16
    shapes = ((pairs, rows, width, low), (pairs, rows, width, low), (1, 8, 128, jnp.float32))
    inner = ((l1, l2), (l2, l1), (l1, l2))
    acc, first, second, third = [], [], [], []
    for (count, r, w, dt), (kept, sent) in zip(shapes, inner):
        acc.append(pltpu.VMEM((count, l0, kept, r, w), dt))
        first.append(pltpu.VMEM((count, max(sent - 1, 1), l0, kept, r, w), dt))
        second.append(pltpu.VMEM((count, max(kept - 1, 1), l0, r, w), dt))
        third.append(pltpu.VMEM((count, max(l0 - 1, 1), r, w), dt))
    return pl.pallas_call(
        functools.partial(spread_kernel, grid, pairs),
        out_shape=(
            jax.ShapeDtypeStruct((chunks, rows, width), jnp.float32),
            jax.ShapeDtypeStruct((8, 128), jnp.float32),
        ),
        in_specs=[pl.BlockSpec(memory_space=pl.ANY)] * 2,
        out_specs=(pl.BlockSpec(memory_space=pltpu.VMEM),) * 2,
        scratch_shapes=acc
        + first
        + second
        + third
        + [
            pltpu.SemaphoreType.DMA((3, 3, pairs, most)),
            pltpu.SemaphoreType.DMA((3, 3, pairs, most)),
            pltpu.SemaphoreType.DMA((3, pairs)),
        ],
        compiler_params=pltpu.CompilerParams(
            collective_id=0, has_side_effects=True, vmem_limit_bytes=60 * 1024 * 1024
        ),
        cost_estimate=pl.CostEstimate(flops=0, bytes_accessed=grads.size * 4, transcendentals=0),
    )(grads.reshape(chunks, l0, l1, l2, rows, width), gains.reshape(l0, l1, l2, 8, 128))


def from_behind(x, axis, by):
    devices = lax.axis_size(axis)
    pairs = [(i, i + by) for i in range(devices) if 0 <= i + by < devices]
    return lax.ppermute(x, axis, pairs)


def layer_norm(values, gain):
    row_mean = jnp.mean(values, axis=-1, keepdims=True)
    centred = values - row_mean
    row_var = jnp.mean(centred * centred, axis=-1, keepdims=True)
    return centred * lax.rsqrt(row_var + epsilon) * gain


def front_half(all_rows, gain_attn, w_qkv):
    normed = layer_norm(all_rows, gain_attn).astype(jnp.bfloat16)
    projected = jnp.dot(normed, w_qkv, preferred_element_type=jnp.float32).astype(jnp.bfloat16)
    return (normed, projected)


def latent_operand(projected, tok_rows, model_width):
    return projected[tok_rows:, model_width:]


def back_half(all_rows, projected, remote_rows, allowed, weights):
    gain_attn, w_qkv, w_out, gain_mlp, w_up, w_down = weights
    row_count, model_width = all_rows.shape
    head_size = model_width // HEADS
    remote_pairs = remote_rows[:, remote_rows.shape[1] - 2 * model_width :]
    queries = projected[:, :model_width].reshape(row_count, HEADS, head_size)
    key_rows = jnp.concatenate(
        [projected[:, model_width : 2 * model_width], remote_pairs[:, :model_width]], axis=0
    )
    value_rows = jnp.concatenate(
        [projected[:, 2 * model_width :], remote_pairs[:, model_width:]], axis=0
    )
    key_rows = key_rows.reshape(-1, HEADS, head_size)
    value_rows = value_rows.reshape(-1, HEADS, head_size)
    scores = jnp.einsum(
        "qhd,khd->hqk", queries, key_rows, preferred_element_type=jnp.float32
    ) * head_size ** (-0.5)
    attn_weights = jax.nn.softmax(jnp.where(allowed[None], scores, masked_score), axis=-1)
    attn_low = attn_weights.astype(jnp.bfloat16)
    mixed_low = jnp.einsum("hqk,khd->qhd", attn_low, value_rows, preferred_element_type=jnp.float32)
    mixed_low = mixed_low.reshape(row_count, model_width).astype(jnp.bfloat16)
    mid_rows = all_rows + jnp.dot(mixed_low, w_out, preferred_element_type=jnp.float32)
    normed_mlp = layer_norm(mid_rows, gain_mlp).astype(jnp.bfloat16)
    up_proj = jnp.dot(normed_mlp, w_up, preferred_element_type=jnp.float32)
    activated = jax.nn.gelu(up_proj).astype(jnp.bfloat16)
    result = mid_rows + jnp.dot(activated, w_down, preferred_element_type=jnp.float32)
    return dict(
        queries=queries,
        key_rows=key_rows,
        value_rows=value_rows,
        attn_weights=attn_weights,
        attn_low=attn_low,
        mixed_low=mixed_low,
        mid_rows=mid_rows,
        normed_mlp=normed_mlp,
        up_proj=up_proj,
        activated=activated,
        result=result,
    )


def section_backward(saved, d_result, all_rows, normed, allowed, weights, latent_start):
    gain_attn, w_qkv, w_out, gain_mlp, w_up, w_down = weights
    row_count, model_width = all_rows.shape
    head_size = model_width // HEADS
    score_scale = head_size ** (-0.5)
    d_low = d_result.astype(jnp.bfloat16)
    grad_down = jnp.dot(d_low.T, saved["activated"], preferred_element_type=jnp.float32)
    d_activated = jnp.dot(d_low, w_down.T, preferred_element_type=jnp.float32)
    unused_up, gelu_back = jax.vjp(jax.nn.gelu, saved["up_proj"])
    d_up = gelu_back(d_activated)[0].astype(jnp.bfloat16)
    grad_up = jnp.dot(d_up.T, saved["normed_mlp"], preferred_element_type=jnp.float32)
    d_normed_mlp = jnp.dot(d_up, w_up.T, preferred_element_type=jnp.float32)
    unused_mid, second_back = jax.vjp(layer_norm, saved["mid_rows"], gain_mlp)
    d_mid_norm, grad_gain_mlp = second_back(d_normed_mlp)
    d_mid = d_result + d_mid_norm
    d_mid_low = d_mid.astype(jnp.bfloat16)
    grad_out = jnp.dot(d_mid_low.T, saved["mixed_low"], preferred_element_type=jnp.float32)
    d_mixed = jnp.dot(d_mid_low, w_out.T, preferred_element_type=jnp.float32).astype(jnp.bfloat16)
    d_mixed = d_mixed.reshape(row_count, HEADS, head_size)
    d_weights = jnp.einsum(
        "qhd,khd->hqk", d_mixed, saved["value_rows"], preferred_element_type=jnp.float32
    )
    d_values = jnp.einsum(
        "hqk,qhd->khd", saved["attn_low"], d_mixed, preferred_element_type=jnp.float32
    )
    attn_weights = saved["attn_weights"]
    d_scores = attn_weights * (
        d_weights - jnp.sum(attn_weights * d_weights, axis=-1, keepdims=True)
    )
    d_scores_low = jnp.where(allowed[None], d_scores, 0.0).astype(jnp.bfloat16)
    d_queries = (
        jnp.einsum(
            "hqk,khd->qhd", d_scores_low, saved["key_rows"], preferred_element_type=jnp.float32
        )
        * score_scale
    )
    d_keys = (
        jnp.einsum(
            "hqk,qhd->khd", d_scores_low, saved["queries"], preferred_element_type=jnp.float32
        )
        * score_scale
    )
    remote_part = jnp.concatenate(
        [
            d_keys[row_count:].reshape(-1, model_width),
            d_values[row_count:].reshape(-1, model_width),
        ],
        axis=1,
    )
    own_part = lax.psum_scatter(remote_part, "dp", scatter_dimension=0, tiled=True)
    local_pairs = jnp.concatenate(
        [
            d_keys[:row_count].reshape(row_count, model_width),
            d_values[:row_count].reshape(row_count, model_width),
        ],
        axis=1,
    )
    local_pairs = jnp.concatenate(
        [local_pairs[:latent_start], local_pairs[latent_start:] + own_part], axis=0
    )
    d_projected = jnp.concatenate(
        [d_queries.reshape(row_count, model_width), local_pairs], axis=1
    ).astype(jnp.bfloat16)
    grad_qkv = jnp.dot(d_projected.T, normed, preferred_element_type=jnp.float32)
    d_normed = jnp.dot(d_projected, w_qkv.T, preferred_element_type=jnp.float32)
    unused_rows, first_back = jax.vjp(layer_norm, all_rows, gain_attn)
    d_rows_norm, grad_gain_attn = first_back(d_normed)
    return (
        d_mid + d_rows_norm,
        (grad_gain_attn, grad_qkv, grad_out, grad_gain_mlp, grad_up, grad_down),
    )


def packed(grads, n):
    gain_first, qkv_grad, out_grad, gain_second, up_grad, down_grad = grads
    width = out_grad.shape[0]
    rows = width // n

    def by_rows(grad):
        return grad.reshape(n, -1, rows, width).transpose(1, 0, 2, 3).astype(jnp.bfloat16)

    down = down_grad.reshape(n, rows, -1, width).transpose(2, 0, 1, 3).astype(jnp.bfloat16)
    chunks = jnp.concatenate([down, by_rows(up_grad), by_rows(out_grad), by_rows(qkv_grad)], axis=0)
    gains = jnp.stack([gain_first.reshape(n, rows), gain_second.reshape(n, rows)], axis=1)
    return chunks, jnp.pad(gains, ((0, 0), (0, 6), (0, 128 - rows)))


def shards(
    grid,
    tokens,
    latents,
    slot_group,
    image_groups,
    gain_attn,
    w_qkv,
    w_out,
    gain_mlp,
    w_up,
    w_down,
    d_tokens,
    d_latents,
):
    micro = tokens.shape[0]
    tok_rows = tokens.shape[1]
    lat_rows = latents.shape[1]
    model_width = tokens.shape[2]
    local_groups = tok_rows // GROUP
    section_index = lax.axis_index("section")
    is_global = section_index == 1
    dp_index = lax.axis_index("dp")
    weights = (gain_attn[0], w_qkv[0], w_out[0], gain_mlp[0], w_up[0], w_down[0])
    image_ends = jnp.cumsum(image_groups, axis=1)
    slot_images = jnp.sum(
        (image_ends[:, None, :] <= slot_group[:, :, None]).astype(jnp.int32), axis=2
    )
    slot_total = slot_group.shape[1]
    row_group = jnp.concatenate([jnp.arange(tok_rows) // GROUP, jnp.arange(lat_rows) // LAT])
    row_latent = jnp.concatenate(
        [jnp.zeros((tok_rows,), jnp.bool_), jnp.ones((lat_rows,), jnp.bool_)]
    )
    same_group = row_group[:, None] == row_group[None, :]
    local_mask = jnp.where(
        is_global, (~row_latent)[:, None] & row_latent[None, :] & same_group, same_group
    )
    group_match = row_group[:, None] == jnp.arange(local_groups)[None, :]

    def key_images(batch):
        images_row = lax.dynamic_index_in_dim(slot_images, batch, 0, keepdims=False)
        return (images_row, jnp.broadcast_to(images_row[:, None], (slot_total, LAT)).reshape(-1))

    def allowed_for(batch):
        images_row, key_image = key_images(batch)
        own_images = lax.dynamic_slice_in_dim(images_row, dp_index * local_groups, local_groups)
        row_image = jnp.sum(jnp.where(group_match, own_images[None, :], 0), axis=1)
        remote_mask = is_global & row_latent[:, None] & (row_image[:, None] == key_image[None, :])
        return jnp.concatenate([local_mask, remote_mask], axis=1)

    def forward_turn(received, turn):
        recv_tokens, recv_latents = received
        batch = jnp.clip(turn - section_index, 0, micro - 1)
        own_tok = lax.dynamic_index_in_dim(tokens, batch, 0, keepdims=False)
        own_lat = lax.dynamic_index_in_dim(latents, batch, 0, keepdims=False)
        input_rows = jnp.concatenate(
            [
                jnp.where(is_global, recv_tokens, own_tok),
                jnp.where(is_global, recv_latents, own_lat),
            ],
            axis=0,
        )
        all_rows = input_rows.astype(jnp.float32)
        normed, projected = front_half(all_rows, weights[0], weights[1])
        remote_rows = lax.all_gather(
            latent_operand(projected, tok_rows, model_width), "dp", axis=0, tiled=True
        )
        saved = back_half(all_rows, projected, remote_rows, allowed_for(batch), weights)
        result = saved["result"]
        result_low = result.astype(jnp.bfloat16)
        stored = jnp.where(is_global, result, result_low.astype(jnp.float32))
        passed_on = from_behind((result_low[:tok_rows], result_low[tok_rows:]), "section", 1)
        return passed_on, (input_rows, stored[:tok_rows], stored[tok_rows:])

    nothing = (
        jnp.zeros((tok_rows, model_width), jnp.bfloat16),
        jnp.zeros((lat_rows, model_width), jnp.bfloat16),
    )
    turns = jnp.arange(micro + 1)
    unused_end, (kept_rows, tok_outputs, lat_outputs) = lax.scan(forward_turn, nothing, turns)

    def backward_turn(carry, turn):
        (recv_grad_tok, recv_grad_lat), totals = carry
        raw_batch = micro - turn - section_index
        valid = ((raw_batch >= 0) & (raw_batch < micro)).astype(jnp.float32)
        batch = jnp.clip(raw_batch, 0, micro - 1)
        all_rows = lax.dynamic_index_in_dim(
            kept_rows, batch + section_index, 0, keepdims=False
        ).astype(jnp.float32)
        normed, projected = front_half(all_rows, weights[0], weights[1])
        remote_rows = lax.all_gather(
            latent_operand(projected, tok_rows, model_width), "dp", axis=0, tiled=True
        )
        allowed = allowed_for(batch)
        saved = back_half(all_rows, projected, remote_rows, allowed, weights)
        given = (
            jnp.concatenate(
                [
                    lax.dynamic_index_in_dim(d_tokens, batch, 0, keepdims=False),
                    lax.dynamic_index_in_dim(d_latents, batch, 0, keepdims=False),
                ],
                axis=0,
            )
            * valid
        )
        passed = jnp.concatenate([recv_grad_tok, recv_grad_lat], axis=0).astype(jnp.float32)
        d_result = jnp.where(is_global, given, passed)
        d_rows, grads = section_backward(
            saved, d_result, all_rows, normed, allowed, weights, tok_rows
        )
        totals = tuple((accum + piece for accum, piece in zip(totals, grads)))
        d_rows_low = d_rows.astype(jnp.bfloat16)
        stored = jnp.where(is_global, d_rows_low.astype(jnp.float32), d_rows)
        sent = from_behind((d_rows_low[:tok_rows], d_rows_low[tok_rows:]), "section", -1)
        return (sent, totals), (stored[:tok_rows], stored[tok_rows:])

    totals = tuple(
        jnp.zeros(w.shape[::-1] if w.ndim == 2 else w.shape, jnp.float32) for w in weights
    )
    (unused_sent, totals), (tok_grads, lat_grads) = lax.scan(
        backward_turn, (nothing, totals), turns
    )
    chunks, gains = packed(totals, lax.axis_size("dp"))
    summed, gain_sums = spread(grid, chunks, gains)
    rows = summed.shape[1]
    layer_tokens = lax.dynamic_slice_in_dim(tok_outputs, section_index, micro, 0)[None]
    layer_latents = lax.dynamic_slice_in_dim(lat_outputs, section_index, micro, 0)[None]
    grad_tokens = lax.dynamic_slice_in_dim(tok_grads, 1 - section_index, micro, 0)[::-1][
        None
    ]
    grad_latents = lax.dynamic_slice_in_dim(lat_grads, 1 - section_index, micro, 0)[
        ::-1
    ][None]
    return (
        layer_tokens,
        layer_latents,
        grad_tokens,
        grad_latents,
        gain_sums[0:1, :rows],
        summed[9:].reshape(-1, model_width).T[None],
        summed[8].T[None],
        gain_sums[1:2, :rows],
        summed[4:8].reshape(-1, model_width).T[None],
        summed[0:4].transpose(0, 2, 1).reshape(-1, rows)[None],
    )


F32 = jnp.float32
LOW = jnp.bfloat16
HEAD_PAD = 16
TILE = 768


def nn(a, b):
    return jnp.dot(a, b, preferred_element_type=F32)


def nt(a, b):
    return lax.dot_general(a, b, (((1,), (1,)), ((), ())), preferred_element_type=F32)


def tn(a, b):
    return lax.dot_general(a, b, (((0,), (0,)), ((), ())), preferred_element_type=F32)


def normed_rows(values):
    centred = values - jnp.mean(values, axis=-1, keepdims=True)
    scale = lax.rsqrt(jnp.mean(centred * centred, axis=-1, keepdims=True) + epsilon)
    return centred * scale, scale


def norm_back(grad, hat, scale, gain):
    scaled = grad * gain
    mean = jnp.mean(scaled, axis=-1, keepdims=True)
    along = jnp.mean(scaled * hat, axis=-1, keepdims=True)
    return scale * (scaled - mean - hat * along)


def at(start, size):
    return pl.ds(pl.multiple_of(start, size), size)


def class_max(s):
    for by in (16, 32, 64):
        s = jnp.maximum(s, pltpu.roll(s, by, 1))
    return s


def class_sum(s):
    for by in (16, 32, 64):
        s = s + pltpu.roll(s, by, 1)
    return s


def layer_kernel(
    grid,
    tokens,
    latents,
    slots,
    slot_at,
    image_at,
    gain_attn,
    gain_mlp,
    w_qkv,
    w_out,
    w_up,
    w_down,
    d_tokens,
    d_latents,
    out_tok,
    out_lat,
    grad_tok,
    grad_lat,
    grads,
    summed,
    gain_sums,
    wq,
    wo,
    wu,
    wd,
    xb,
    n1,
    proj,
    mixed,
    mid,
    n2,
    act,
    dup,
    yb,
    dy,
    ef,
    tmp,
    out,
    probs,
    probs_lat,
    latf,
    mixf,
    key_mask,
    qbd,
    kbd,
    vbd,
    kv_all,
    kvg_send,
    kvg_recv,
    stage,
    gains,
    leaving,
    own_a,
    own_b,
    land1_a,
    land1_b,
    land2_a,
    land2_b,
    land3_a,
    land3_b,
    land_g,
    load_sem,
    stage_sem,
    own_sem,
    leave_sem,
    send_sem,
    recv_sem,
    gain_s,
    gain_r,
    relay_send,
    relay_recv,
    kv_sem_s,
    kv_sem_r,
    kvg_sem_s,
    kvg_sem_r,
):
    l0, l1, l2 = grid
    n = l0 * l1 * l2
    rows, width = xb.shape
    ff = act.shape[1]
    tok = tokens.shape[0]
    lat = latents.shape[0]
    half = lat // LAT
    pairs = width // 128
    me = lax.axis_index("dp")
    section = lax.axis_index("section")
    first = section == 0
    second = section == 1
    partner = (me, 1 - section)

    loads = [
        pltpu.make_async_copy(src, dst, load_sem.at[i])
        for i, (src, dst) in enumerate(((w_qkv, wq), (w_out, wo), (w_up, wu), (w_down, wd)))
    ]
    x_loads = [
        pltpu.make_async_copy(tokens, xb.at[0:tok], load_sem.at[4]),
        pltpu.make_async_copy(latents, xb.at[tok:rows], load_sem.at[5]),
    ]
    e_loads = [
        pltpu.make_async_copy(d_tokens, ef.at[0:tok], load_sem.at[6]),
        pltpu.make_async_copy(d_latents, ef.at[tok:rows], load_sem.at[7]),
    ]

    @pl.when(first)
    def _():
        for copy in x_loads:
            copy.start()

    for copy in loads:
        copy.start()

    @pl.when(second)
    def _():
        for copy in e_loads:
            copy.start()

    barrier = pltpu.get_barrier_semaphore()
    pl.semaphore_signal(barrier, inc=1, device_id=partner, device_id_type=MESH)

    here = (me // (l1 * l2), lax.rem(me // l2, l1), lax.rem(me, l2))

    def along(axis, shift):
        there = list(here)
        there[axis] = lax.rem(here[axis] + shift, grid[axis])
        return there[axis], ((there[0] * l1 + there[1]) * l2 + there[2], section)

    @pl.when(second)
    def _():
        for shift in range(1, n):
            pl.semaphore_signal(
                barrier, inc=1, device_id=(lax.rem(me + shift, n), section), device_id_type=MESH
            )
        pl.semaphore_wait(barrier, n)

    @pl.when(first)
    def _():
        for axis in range(3):
            for shift in range(1, grid[axis]):
                pl.semaphore_signal(
                    barrier, inc=1, device_id=along(axis, shift)[1], device_id_type=MESH
                )
        pl.semaphore_wait(barrier, sum(grid) - 2)

    forward_relay = pltpu.make_async_remote_copy(
        src_ref=yb, dst_ref=xb, send_sem=relay_send.at[0], recv_sem=relay_recv.at[0],
        device_id=partner, device_id_type=MESH,
    )
    backward_relay = pltpu.make_async_remote_copy(
        src_ref=yb, dst_ref=dy, send_sem=relay_send.at[1], recv_sem=relay_recv.at[1],
        device_id=partner, device_id_type=MESH,
    )

    def kv_copy(shift, incoming):
        slot = lax.rem(me + n - shift, n) if incoming else me
        return pltpu.make_async_remote_copy(
            src_ref=kv_all.at[me], dst_ref=kv_all.at[slot],
            send_sem=kv_sem_s.at[shift - 1], recv_sem=kv_sem_r.at[shift - 1],
            device_id=(lax.rem(me + shift, n), section), device_id_type=MESH,
        )

    def kvg_copy(shift):
        there = lax.rem(me + shift, n)
        return pltpu.make_async_remote_copy(
            src_ref=kvg_send.at[there], dst_ref=kvg_recv.at[shift - 1],
            send_sem=kvg_sem_s.at[shift - 1], recv_sem=kvg_sem_r.at[shift - 1],
            device_id=(there, section), device_id_type=MESH,
        )

    lane = lax.broadcasted_iota(jnp.int32, (1, 128), 1)
    halves = [(lane < 64).astype(F32).astype(LOW), (lane >= 64).astype(F32).astype(LOW)]
    eighths = [(h.astype(F32) * 0.125).astype(LOW) for h in halves]
    heads = (
        lax.broadcasted_iota(jnp.int32, (HEAD_PAD, width), 1) // 64
        == lax.broadcasted_iota(jnp.int32, (HEAD_PAD, width), 0)
    ).astype(F32)

    def block_diagonal(dst, base, src, row, column, scale):
        for i in range(LAT):
            line = src[row + i : row + i + 1, column : column + width] * scale
            dst[base + i * HEAD_PAD : base + (i + 1) * HEAD_PAD, :] = (line * heads).astype(LOW)

    def head_sum(dst, row, column, value, scale, add):
        for i in range(LAT):
            line = jnp.sum(
                value[i * HEAD_PAD : (i + 1) * HEAD_PAD] * heads, axis=0, keepdims=True
            )
            line = line * scale
            if add:
                line = line + dst[row + i : row + i + 1, column : column + width]
            dst[row + i : row + i + 1, column : column + width] = line

    def bands(body, lo, hi, size):
        def one(i, carry):
            body(pl.ds(pl.multiple_of(lo + i * size, 16), size))
            return carry

        lax.fori_loop(0, (hi - lo) // size, one, 0)

    third = rows // 3

    def tiles(count, body, size=TILE):
        def one(i, carry):
            body(at(i * size, size))
            return carry

        lax.fori_loop(0, count, one, 0)

    @pl.when(first)
    def _():
        for copy in x_loads:
            copy.wait()

    @pl.when(second)
    def _():
        spots = lax.broadcasted_iota(jnp.int32, (n, n * lat), 1) // lat
        spread_out = (spots == lax.broadcasted_iota(jnp.int32, (n, n * lat), 0)).astype(F32)
        groups = nn(slots[...].astype(F32).astype(LOW), spread_out.astype(LOW))
        of_micro = lax.rem(lax.broadcasted_iota(jnp.int32, (1, n * lat), 1), lat) // LAT
        for m in range(half):
            images = jnp.zeros((1, n * lat), F32)
            own_image = jnp.float32(0)
            end = jnp.int32(0)
            for i in range(image_at.shape[1]):
                end = end + image_at[m, i]
                images += jnp.where(end.astype(F32) <= groups[m : m + 1], 1.0, 0.0)
                own_image += jnp.where(end <= slot_at[m, me], 1.0, 0.0)
            seen = (images == own_image) & (of_micro == m)
            key_mask[m : m + 1, :] = jnp.where(seen, 0.0, masked_score)
        forward_relay.wait_recv()

    def norm_in(r):
        hat, unused = normed_rows(xb[r, :].astype(F32))
        n1[r, :] = (hat * gain_attn[...]).astype(LOW)

    bands(norm_in, 0, rows, third)
    loads[0].wait()

    @pl.when(second)
    def _():
        own = nn(n1[tok:rows, :], wq[:, width:]).astype(LOW)
        kv_all[me] = own
        latf[:, width:] = own.astype(F32)
        for shift in range(1, n):
            kv_copy(shift, False).start()

    def project(c):
        proj[:, c] = nn(n1[...], wq[:, c]).astype(LOW)

    per = width // TILE
    tiles(jnp.where(first, 3 * per, per), project)

    def lat_bias(m, shape, axis):
        return jnp.where(
            lax.broadcasted_iota(jnp.int32, shape, axis) // LAT == m, 0.0, masked_score
        ).astype(F32)

    @pl.when(first)
    def _():
        latf[...] = proj[tok:rows, :].astype(F32)

        def one_pair(it):
            m, p = it // pairs, lax.rem(it, pairs)
            r = at(m * GROUP, GROUP)
            q = proj[r, at(p * 128, 128)]
            k = proj[r, at(width + p * 128, 128)]
            v = proj[r, at(2 * width + p * 128, 128)]
            kl = proj[tok:rows, at(width + p * 128, 128)]
            vl = proj[tok:rows, at(2 * width + p * 128, 128)]
            bias = lat_bias(m, (lat, GROUP), 0)
            total = jnp.zeros((GROUP, 128), F32)
            for e in (0, 1):
                qe = q * eighths[e]
                st = nt(k, qe)
                sl = nt(kl, qe) + bias
                top = jnp.maximum(
                    jnp.max(st, axis=0, keepdims=True), jnp.max(sl, axis=0, keepdims=True)
                )
                et = jnp.exp(st - top)
                el = jnp.exp(sl - top)
                scale = 1.0 / (
                    jnp.sum(et, axis=0, keepdims=True) + jnp.sum(el, axis=0, keepdims=True)
                )
                pt = (et * scale).astype(LOW)
                pe = (el * scale).astype(LOW)
                probs[2 * it + e, 0:GROUP, :] = pt
                probs[2 * it + e, GROUP : GROUP + lat, :] = pe
                total += tn(pt, v * halves[e]) + tn(pe, vl * halves[e])
            mixed[r, at(p * 128, 128)] = total.astype(LOW)

        def pair(i, carry):
            one_pair(2 * i)
            one_pair(2 * i + 1)
            return carry

        lax.fori_loop(0, half * pairs // 2, pair, 0)
        for m in range(half):
            r = slice(m * GROUP, (m + 1) * GROUP)
            b = slice(m * 128, (m + 1) * 128)
            block_diagonal(qbd, m * 128, latf, m * LAT, 0, 0.125)
            s = nt(qbd[b, :], proj[r, width : 2 * width])
            sl = nt(qbd[b, :], proj[tok:rows, width : 2 * width]) + lat_bias(m, (128, lat), 1)
            top = jnp.maximum(
                jnp.max(s, axis=1, keepdims=True), jnp.max(sl, axis=1, keepdims=True)
            )
            et = jnp.exp(s - top)
            el = jnp.exp(sl - top)
            scale = 1.0 / (
                jnp.sum(et, axis=1, keepdims=True) + jnp.sum(el, axis=1, keepdims=True)
            )
            pt = (et * scale).astype(LOW)
            pe = (el * scale).astype(LOW)
            probs_lat[b, 0:GROUP] = pt
            probs_lat[b, GROUP : GROUP + lat] = pe
            o = nn(pt, proj[r, 2 * width :]) + nn(pe, proj[tok:rows, 2 * width :])
            head_sum(mixf, m * LAT, 0, o, 1.0, False)
        mixed[tok:rows, :] = mixf[...].astype(LOW)

    keys = n * lat

    @pl.when(second)
    def _():
        latf[:, :width] = proj[tok:rows, :width].astype(F32)
        for m in range(half):
            r = slice(m * GROUP, (m + 1) * GROUP)
            b = slice(m * 128, (m + 1) * 128)
            block_diagonal(qbd, m * 128, latf, m * LAT, 0, 0.125)
            block_diagonal(kbd, m * 128, latf, m * LAT, width, 1.0)
            block_diagonal(vbd, m * 128, latf, m * LAT, 2 * width, 1.0)
            s = nt(proj[r, :width] * jnp.asarray(0.125, LOW), kbd[b, :])
            et = jnp.exp(s - class_max(s))
            pt = (et / class_sum(et)).astype(LOW)
            probs[m, 0:GROUP, 0:128] = pt
            mixed[r, :] = nn(pt, vbd[b, :]).astype(LOW)

    root = 0.7978845608028654

    def mlp_in(lo, hi, size):
        r0 = slice(lo, hi)
        mid[r0, :] = xb[r0, :].astype(F32) + nn(mixed[r0, :], wo[...])

        def norm_mid(r):
            hat, unused = normed_rows(mid[r, :])
            n2[r, :] = (hat * gain_mlp[...]).astype(LOW)

        bands(norm_mid, lo, hi, size)

        def widen(c):
            up = nn(n2[r0, :], wu[:, c])
            square = up * up
            t = jnp.tanh(up * (root + (root * 0.044715) * square))
            gate = 0.5 + 0.5 * t
            value = up * gate
            slope = gate + 2.0 * value * (1.0 - gate) * (root + (3.0 * root * 0.044715) * square)
            act[r0, c] = value.astype(LOW)
            dup[r0, c] = slope.astype(LOW)

        tiles(ff // 384, widen, 384)

    for copy in loads[1:]:
        copy.wait()

    @pl.when(first)
    def _():
        mlp_in(0, rows, third)

    @pl.when(second)
    def _():
        mlp_in(0, tok, tok // 4)
        for shift in range(1, n):
            kv_copy(shift, True).wait_recv()
        k = kv_all[:, :, :width].reshape(keys, width)
        v = kv_all[:, :, width:].reshape(keys, width)
        for m in range(half):
            b = slice(m * 128, (m + 1) * 128)
            s = nt(qbd[b, :], k) + key_mask[m : m + 1, :]
            et = jnp.exp(s - jnp.max(s, axis=1, keepdims=True))
            pt = (et / jnp.sum(et, axis=1, keepdims=True)).astype(LOW)
            probs_lat[b, 0:keys] = pt
            head_sum(mixf, m * LAT, 0, nn(pt, v), 1.0, False)
        mixed[tok:rows, :] = mixf[...].astype(LOW)

        mlp_in(tok, rows, lat)

    out_copies = [
        pltpu.make_async_copy(out.at[0:tok], out_tok, load_sem.at[8]),
        pltpu.make_async_copy(out.at[tok:rows], out_lat, load_sem.at[9]),
    ]
    grad_copies = [
        pltpu.make_async_copy(out.at[0:tok], grad_tok, load_sem.at[8]),
        pltpu.make_async_copy(out.at[tok:rows], grad_lat, load_sem.at[9]),
    ]

    def layer_output(passed_on):
        def narrow(c):
            y = mid[:, c] + nn(act[...], wd[:, c])
            if passed_on:
                low = y.astype(LOW)
                yb[:, c] = low
                y = low.astype(F32)
            out[:, c] = y

        tiles(width // 384, narrow, 384)
        for copy in out_copies:
            copy.start()

    @pl.when(first)
    def _():
        layer_output(True)
        forward_relay.start()
        backward_relay.wait_recv()

        def widen_e(r):
            ef[r, :] = dy[r, :].astype(F32)

        bands(widen_e, 0, rows, third)

    @pl.when(second)
    def _():
        for copy in e_loads:
            copy.wait()

        def narrow_e(r):
            dy[r, :] = ef[r, :].astype(LOW)

        bands(narrow_e, 0, rows, third)

    part = 384
    unit = width // n
    many = part // unit

    def staged(slot, piece, chunk, share):
        return pltpu.make_async_copy(
            stage.at[slot, piece],
            grads.at[chunk, share // (l1 * l2), lax.rem(share // l2, l1), lax.rem(share, l2)],
            stage_sem.at[slot, piece],
        )

    def drain(slot):
        def one(piece, carry):
            staged(slot, piece, 0, 0).wait()
            return carry

        lax.fori_loop(0, many, one, 0)

    def weight_grad(place, start, count, left, right):
        def one(i, carry):
            slot = lax.rem(i, 2)
            value = tn(left(i), right(i)).astype(LOW)

            @pl.when(i >= start + 2)
            def _():
                drain(slot)

            for piece in range(many):
                stage[slot, piece] = value[piece * unit : (piece + 1) * unit]
                staged(slot, piece, *place(i * many + piece)).start()
            return carry

        lax.fori_loop(start, start + count, one, 0)
        for slot in (0, 1):
            drain(slot)

    orders = ((2, 1, 0), (1, 2, 0))
    own_buf = (own_a, own_b)
    land = ((land1_a, land1_b), (land2_a, land2_b), (land3_a, land3_b))
    spread_pairs = land1_a.shape[0]

    def whole(stream, k, index):
        if stream == 0:
            return grads.at[2 * k, :, :, index]
        return grads.at[2 * k + 1, :, index]

    def source(stream, phase, k, index):
        if phase == 0:
            return whole(stream, k, index)
        if phase == 1:
            return land[0][stream].at[k, 0, :, index]
        return land[0][stream].at[k, 0, index, here[orders[stream][1]]]

    def copies(stream, phase, k):
        axis = orders[stream][phase]
        for shift in range(1, grid[axis]):
            index, target = along(axis, shift)
            yield pltpu.make_async_remote_copy(
                src_ref=source(stream, phase, k, index),
                dst_ref=land[phase][stream].at[k, shift - 1],
                send_sem=send_sem.at[stream, phase, k, shift - 1],
                recv_sem=recv_sem.at[stream, phase, k, shift - 1],
                device_id=target,
                device_id_type=MESH,
            )

    def own(stream, k):
        return pltpu.make_async_copy(
            whole(stream, k, here[orders[stream][0]]), own_buf[stream], own_sem.at[stream]
        )

    def leave(stream, k):
        slot = lax.rem(k, 2)
        return pltpu.make_async_copy(
            leaving.at[slot, stream], summed.at[2 * k + stream], leave_sem.at[slot, stream]
        )

    def launch(phase, k):
        for stream in (0, 1):
            for copy in copies(stream, phase, k):
                copy.start()

    def absorb(phase, k):
        for stream in (0, 1):
            axis = orders[stream][phase]
            if phase == 0:
                own(stream, k).wait()
            for copy in copies(stream, phase, k):
                copy.wait_recv()
            base = land[0][stream]
            into = land[phase][stream]
            if phase == 0:

                def add(i, carry):
                    for j in range(base.shape[3]):
                        total = own_buf[stream][i, j].astype(F32)
                        for s in range(grid[axis] - 1):
                            total += into[k, s, i, j].astype(F32)
                        base[k, 0, i, j] = total.astype(LOW)
                    return carry

                lax.fori_loop(0, base.shape[2], add, 0)
            elif phase == 1:

                def add(i, carry):
                    total = base[k, 0, i, here[axis]].astype(F32)
                    for s in range(grid[axis] - 1):
                        total += into[k, s, i].astype(F32)
                    base[k, 0, i, here[axis]] = total.astype(LOW)
                    return carry

                lax.fori_loop(0, base.shape[2], add, 0)
            else:
                total = base[k, 0, here[0], here[orders[stream][1]]].astype(F32)
                for s in range(grid[axis] - 1):
                    total += into[k, s].astype(F32)
                slot = lax.rem(k, 2)

                @pl.when(k >= 2)
                def _():
                    leave(stream, k - 2).wait()

                leaving[slot, stream] = total
                leave(stream, k).start()

    def start_own(k):
        for stream in (0, 1):
            own(stream, k).start()

    def relaunch(k, following=True):
        absorb(0, k)
        launch(1, k)
        if following:
            start_own(k + 1)

    def onward(k):
        absorb(1, k)
        launch(2, k)

    wide = ff // width
    per_part = width // part

    def down_grad(start, count):
        weight_grad(
            lambda p: (p // n, lax.rem(p, n)),
            start,
            count,
            lambda i: dy[:, at(lax.rem(i, per_part) * part, part)],
            lambda i: act[:, at((i // per_part) * width, width)],
        )

    down_grad(0, ff // part // 2)
    launch(0, 0)
    start_own(0)
    down_grad(ff // part // 2, ff // part // 2)
    launch(0, 1)

    def unwiden(c):
        dup[:, c] = (nt(dy[...], wd[c, :]) * dup[:, c].astype(F32)).astype(LOW)

    tiles(ff // TILE, unwiden)
    def to_mid(c):
        tmp[:, c] = nt(dup[...], wu[c, :])

    tiles(width // 384, to_mid, 384)
    gains[0] = jnp.zeros_like(gains[0])

    def fold(value):
        total = value[0:8]
        for i in range(1, value.shape[0] // 8):
            total = total + value[8 * i : 8 * i + 8]
        return total

    def mid_back(r):
        hat, scale = normed_rows(mid[r, :])
        grad = tmp[r, :]
        gains[0, 8:16, :] += fold(grad * hat)
        total = ef[r, :] + norm_back(grad, hat, scale, gain_mlp[...])
        ef[r, :] = total
        dy[r, :] = total.astype(LOW)

    bands(mid_back, 0, rows, third)

    @pl.when(first)
    def _():
        forward_relay.wait_send()

    def to_mix(c):
        yb[:, c] = nt(dy[...], wo[c, :]).astype(LOW)

    tiles(width // TILE, to_mix)
    mixf[...] = yb[tok:rows, :].astype(F32)

    @pl.when(second)
    def _():
        k = kv_all[:, :, :width].reshape(keys, width)
        v = kv_all[:, :, width:].reshape(keys, width)
        for m in range(half):
            b = slice(m * 128, (m + 1) * 128)
            block_diagonal(vbd.at[pl.ds(256, 256)], m * 128, mixf, m * LAT, 0, 1.0)
        both = slice(0, half * 128)
        do = vbd[256 : 256 + half * 128, :]
        pt = probs_lat[both, 0:keys]
        pf = pt.astype(F32)
        dp = nt(do, v)
        along = jnp.sum(pf * dp, axis=1, keepdims=True)
        ds = (pf * (dp - along)).astype(LOW)
        kvg_send[:, :, :width] = tn(ds, qbd[both, :]).astype(LOW).reshape(n, lat, width)
        kvg_send[:, :, width:] = tn(pt, do).astype(LOW).reshape(n, lat, width)
        for shift in range(1, n):
            kvg_copy(shift).start()
        dq = nn(ds, k)
        for m in range(half):
            head_sum(latf, m * LAT, 0, dq[m * 128 : (m + 1) * 128], 0.125, False)
        proj[tok:rows, :width] = latf[:, :width].astype(LOW)
        layer_output(False)

    weight_grad(
        lambda p: (wide + lax.rem(p, wide), p // wide),
        0,
        ff // part,
        lambda i: dup[:, at(i * part, part)],
        lambda i: n2[...],
    )
    launch(0, 2)
    launch(0, 3)

    relaunch(0)
    weight_grad(
        lambda p: (2 * wide, p),
        0,
        width // part,
        lambda i: dy[:, at(i * part, part)],
        lambda i: mixed[...],
    )
    relaunch(1)
    for copy in out_copies:
        copy.wait()

    @pl.when(first)
    def _():
        for m in range(half):
            r = slice(m * GROUP, (m + 1) * GROUP)
            b = slice(m * 128, (m + 1) * 128)
            block_diagonal(vbd, m * 128, mixf, m * LAT, 0, 1.0)
            do = vbd[b, :]
            dp = nt(do, proj[r, 2 * width :])
            dl = nt(do, proj[tok:rows, 2 * width :])
            pt = probs_lat[b, 0:GROUP]
            pe = probs_lat[b, GROUP : GROUP + lat]
            pf = pt.astype(F32)
            pg = pe.astype(F32)
            along = jnp.sum(pf * dp, axis=1, keepdims=True) + jnp.sum(
                pg * dl, axis=1, keepdims=True
            )
            ds = (pf * (dp - along)).astype(LOW)
            dsl = (pg * (dl - along)).astype(LOW)
            dq = nn(ds, proj[r, width : 2 * width]) + nn(dsl, proj[tok:rows, width : 2 * width])
            head_sum(latf, m * LAT, 0, dq, 0.125, False)
            tmp[r, :] = tn(ds, qbd[b, :])
            out[r, :] = tn(pt, do)
            if m == 0:
                tmp[tok:rows, :] = tn(dsl, qbd[b, :])
                out[tok:rows, :] = tn(pe, do)
            else:
                tmp[tok:rows, :] += tn(dsl, qbd[b, :])
                out[tok:rows, :] += tn(pe, do)
        proj[tok:rows, :width] = latf[:, :width].astype(LOW)

        def one_pair(it):
            m, p = it // pairs, lax.rem(it, pairs)
            r = at(m * GROUP, GROUP)
            qc = at(p * 128, 128)
            q = proj[r, qc]
            k = proj[r, at(width + p * 128, 128)]
            v = proj[r, at(2 * width + p * 128, 128)]
            kl = proj[tok:rows, at(width + p * 128, 128)]
            vl = proj[tok:rows, at(2 * width + p * 128, 128)]
            dx = yb[r, qc]
            dq = jnp.zeros((GROUP, 128), F32)
            dk = tmp[r, qc]
            dv = out[r, qc]
            dkl = tmp[tok:rows, qc]
            dvl = out[tok:rows, qc]
            for e in (0, 1):
                qe = q * eighths[e]
                de = dx * halves[e]
                pt = probs[2 * it + e, 0:GROUP, :]
                pe = probs[2 * it + e, GROUP : GROUP + lat, :]
                pf = pt.astype(F32)
                pg = pe.astype(F32)
                dp = nt(v, de)
                dl = nt(vl, de)
                along = jnp.sum(pf * dp, axis=0, keepdims=True) + jnp.sum(
                    pg * dl, axis=0, keepdims=True
                )
                ds = (pf * (dp - along)).astype(LOW)
                dsl = (pg * (dl - along)).astype(LOW)
                dq += tn(ds, k * halves[e]) + tn(dsl, kl * halves[e])
                dk += nn(ds, qe)
                dkl += nn(dsl, qe)
                dv += nn(pt, de)
                dvl += nn(pe, de)
            proj[r, qc] = (dq * 0.125).astype(LOW)
            proj[r, at(width + p * 128, 128)] = dk.astype(LOW)
            proj[r, at(2 * width + p * 128, 128)] = dv.astype(LOW)
            tmp[tok:rows, qc] = dkl
            out[tok:rows, qc] = dvl

        def pair(i, carry):
            one_pair(2 * i)
            one_pair(2 * i + 1)
            return carry

        lax.fori_loop(0, half * pairs // 2, pair, 0)
        proj[tok:rows, width : 2 * width] = tmp[tok:rows, :].astype(LOW)
        proj[tok:rows, 2 * width :] = out[tok:rows, :].astype(LOW)

    @pl.when(second)
    def _():
        for m in range(half):
            r = slice(m * GROUP, (m + 1) * GROUP)
            b = slice(m * 128, (m + 1) * 128)
            pt = probs[m, 0:GROUP, 0:128]
            pf = pt.astype(F32)
            dx = yb[r, :]
            dp = nt(dx, vbd[b, :])
            ds = (pf * (dp - class_sum(pf * dp))).astype(LOW)
            dk = tn(ds, proj[r, :width])
            dv = tn(pt, dx)
            proj[r, :width] = (nn(ds, kbd[b, :]) * 0.125).astype(LOW)
            head_sum(latf, m * LAT, width, dk, 0.125, False)
            head_sum(latf, m * LAT, 2 * width, dv, 1.0, False)
        total = latf[:, width:] + kvg_send[me].astype(F32)
        for shift in range(1, n):
            kvg_copy(shift).wait_recv()
            total += kvg_recv[shift - 1].astype(F32)
        proj[tok:rows, width:] = total.astype(LOW)

    relaunch(2)

    @pl.when(first)
    def _():
        def to_in(c):
            tmp[:, c] = nt(proj[...], wq[c, :])

        tiles(width // 384, to_in, 384)

    @pl.when(second)
    def _():
        tmp[0:tok, :] = nt(proj[0:tok, :width], wq[:, :width])
        tmp[tok:rows, :] = nt(proj[tok:rows, :], wq[...])

    def in_back(r):
        hat, scale = normed_rows(xb[r, :].astype(F32))
        grad = tmp[r, :]
        gains[0, 0:8, :] += fold(grad * hat)
        total = ef[r, :] + norm_back(grad, hat, scale, gain_attn[...])
        low = total.astype(LOW)
        yb[r, :] = low
        out[r, :] = jnp.where(first, total, low.astype(F32))

    bands(in_back, 0, rows, third)
    for copy in grad_copies:
        copy.start()
    relaunch(3, False)

    @pl.when(second)
    def _():
        backward_relay.start()

    def qkv_grad(start, count, r):
        weight_grad(
            lambda p: (2 * wide + 1 + lax.rem(p, 3), p // 3),
            start,
            count,
            lambda i: proj[r, at(i * part, part)],
            lambda i: n1[r, :],
        )

    @pl.when(first)
    def _():
        qkv_grad(0, 3 * per_part, slice(0, rows))

    @pl.when(second)
    def _():
        qkv_grad(0, per_part, slice(0, rows))
        qkv_grad(per_part, 2 * per_part, slice(tok, rows))

    for pair in range(4, spread_pairs):
        launch(0, pair)
    start_own(4)

    def gain_copy(axis, shift):
        return pltpu.make_async_remote_copy(
            src_ref=gains.at[2 - axis],
            dst_ref=land_g.at[2 - axis, shift - 1],
            send_sem=gain_s.at[axis, shift - 1],
            recv_sem=gain_r.at[axis, shift - 1],
            device_id=along(axis, shift)[1],
            device_id_type=MESH,
        )

    def gain_step(axis):
        total = gains[2 - axis]
        for shift in range(1, grid[axis]):
            gain_copy(axis, shift).wait_recv()
            total = total + land_g[2 - axis, shift - 1]
        gains[3 - axis] = total

    def gain_start(axis):
        for shift in range(1, grid[axis]):
            gain_copy(axis, shift).start()

    def each(lo, hi, body):
        def one(i, carry):
            body(i)
            return carry

        lax.fori_loop(lo, hi, one, 0)

    gain_start(2)
    each(0, 2, onward)
    relaunch(4)
    gain_step(2)
    gain_start(1)
    each(2, 4, onward)
    relaunch(5, False)
    gain_step(1)
    gain_start(0)
    each(0, 2, lambda i: absorb(2, i))
    each(4, 6, onward)
    each(2, 6, lambda i: absorb(2, i))
    gain_step(0)
    final = gains[3]
    for i in (0, 1):
        whole_gain = jnp.sum(final[8 * i : 8 * i + 8], axis=0, keepdims=True)
        whole_gain = jnp.broadcast_to(whole_gain, (8, width))
        rolled = pltpu.roll(whole_gain, lax.rem(width - me * unit, width), 1)
        gain_sums[8 * i : 8 * i + 8, :] = rolled[:, 0:128]

    def finish(k, carry):
        for stream in (0, 1):
            for phase in range(3):
                for copy in copies(stream, phase, k):
                    copy.wait_send()
        return carry

    lax.fori_loop(0, spread_pairs, finish, 0)
    for axis in range(3):
        for shift in range(1, grid[axis]):
            gain_copy(axis, shift).wait_send()
    for copy in grad_copies:
        copy.wait()
    for stream in (0, 1):
        for pair in (spread_pairs - 2, spread_pairs - 1):
            leave(stream, pair).wait()

    @pl.when(second)
    def _():
        backward_relay.wait_send()
        for shift in range(1, n):
            kv_copy(shift, False).wait_send()
            kvg_copy(shift).wait_send()


def both_layers(grid, tokens, latents, slots, images, gains, weights, d_tokens, d_latents):
    l0, l1, l2 = grid
    n = l0 * l1 * l2
    tok, width = tokens.shape
    lat = latents.shape[0]
    rows = tok + lat
    w_qkv, w_out, w_up, w_down = weights
    ff = w_up.shape[1]
    keys = n * lat
    half = lat // LAT
    size = sum(w.size for w in weights)
    chunks = size // (width * width)
    pairs = chunks // 2
    unit = width // n
    most = max(grid) - 1
    vm, hbm = pl.BlockSpec(memory_space=pltpu.VMEM), pl.BlockSpec(memory_space=pl.ANY)
    sm = pl.BlockSpec(memory_space=pltpu.SMEM)
    scratch = [
        pltpu.VMEM(w.shape, LOW) for w in (w_qkv, w_out, w_up, w_down)
    ] + [
        pltpu.VMEM(shape, dtype)
        for shape, dtype in (
            ((rows, width), LOW),
            ((rows, width), LOW),
            ((rows, 3 * width), LOW),
            ((rows, width), LOW),
            ((rows, width), F32),
            ((rows, width), LOW),
            ((rows, ff), LOW),
            ((rows, ff), LOW),
            ((rows, width), LOW),
            ((rows, width), LOW),
            ((rows, width), F32),
            ((rows, width), F32),
            ((rows, width), F32),
            ((half * width // 64, GROUP + lat, GROUP), LOW),
            ((half * 128, max(keys, GROUP + 128)), LOW),
            ((lat, 3 * width), F32),
            ((lat, width), F32),
            ((8, keys), F32),
            ((half * 128, width), LOW),
            ((half * 128, width), LOW),
            ((half * 256, width), LOW),
            ((n, lat, 2 * width), LOW),
            ((n, lat, 2 * width), LOW),
            ((n - 1, lat, 2 * width), LOW),
            ((2, 384 // unit, unit, width), LOW),
            ((4, 16, width), F32),
            ((2, 2, unit, width), F32),
            ((l0, l1, unit, width), LOW),
            ((l0, l2, unit, width), LOW),
            ((pairs, l2 - 1, l0, l1, unit, width), LOW),
            ((pairs, l1 - 1, l0, l2, unit, width), LOW),
            ((pairs, l1 - 1, l0, unit, width), LOW),
            ((pairs, l2 - 1, l0, unit, width), LOW),
            ((pairs, l0 - 1, unit, width), LOW),
            ((pairs, l0 - 1, unit, width), LOW),
            ((3, max(grid) - 1, 16, width), F32),
        )
    ] + [
        pltpu.SemaphoreType.DMA((10,)),
        pltpu.SemaphoreType.DMA((2, 384 // unit)),
        pltpu.SemaphoreType.DMA((2,)),
        pltpu.SemaphoreType.DMA((2, 2)),
        pltpu.SemaphoreType.DMA((2, 3, pairs, most)),
        pltpu.SemaphoreType.DMA((2, 3, pairs, most)),
        pltpu.SemaphoreType.DMA((3, most)),
        pltpu.SemaphoreType.DMA((3, most)),
        pltpu.SemaphoreType.DMA((2,)),
        pltpu.SemaphoreType.DMA((2,)),
        pltpu.SemaphoreType.DMA((n - 1,)),
        pltpu.SemaphoreType.DMA((n - 1,)),
        pltpu.SemaphoreType.DMA((n - 1,)),
        pltpu.SemaphoreType.DMA((n - 1,)),
    ]
    return pl.pallas_call(
        functools.partial(layer_kernel, grid),
        out_shape=(
            jax.ShapeDtypeStruct((tok, width), F32),
            jax.ShapeDtypeStruct((lat, width), F32),
            jax.ShapeDtypeStruct((tok, width), F32),
            jax.ShapeDtypeStruct((lat, width), F32),
            jax.ShapeDtypeStruct((chunks, l0, l1, l2, unit, width), LOW),
            jax.ShapeDtypeStruct((chunks, unit, width), F32),
            jax.ShapeDtypeStruct((16, 128), F32),
        ),
        in_specs=[hbm, hbm, vm, sm, sm, vm, vm] + [hbm] * 6,
        out_specs=(hbm,) * 6 + (vm,),
        scratch_shapes=scratch,
        compiler_params=pltpu.CompilerParams(
            collective_id=1, has_side_effects=True, vmem_limit_bytes=63 * 1024 * 1024
        ),
        cost_estimate=pl.CostEstimate(
            flops=6 * rows * size, bytes_accessed=4 * size, transcendentals=0
        ),
    )(tokens, latents, slots, slots, images, *gains, *weights, d_tokens, d_latents)


def finish_kernel(width, *refs):
    rows_in, (summed, gains), rows_out = refs[0:4], refs[4:6], refs[6:10]
    gain_attn, g_qkv, g_out, gain_mlp, g_up, g_down = refs[10:16]
    sem = refs[16]
    wide = g_down.shape[1] // width
    unit = g_out.shape[1]
    moves = list(zip(rows_in, rows_out))
    for c in range(wide):
        moves.append((summed.at[c], g_down.at[:, c * width : (c + 1) * width]))
    moves.append((summed.at[wide : 2 * wide], g_up))
    moves.append((summed.at[2 * wide : 2 * wide + 1], g_out))
    moves.append((summed.at[2 * wide + 1 :], g_qkv))
    moves = [
        pltpu.make_async_copy(src, dst, sem.at[i]) for i, (src, dst) in enumerate(moves)
    ]
    for move in moves:
        move.start()
    gain_attn[...] = gains[0:1, 0:unit]
    gain_mlp[...] = gains[8:9, 0:unit]
    for move in moves:
        move.wait()


def finished(rows, summed, gains, wide):
    chunks, unit, width = summed.shape
    hbm, vm = pl.BlockSpec(memory_space=pl.ANY), pl.BlockSpec(memory_space=pltpu.VMEM)
    shapes = [r.shape for r in rows] + [
        (1, unit),
        (3, unit, width),
        (1, unit, width),
        (1, unit),
        (wide, unit, width),
        (unit, wide * width),
    ]
    return pl.pallas_call(
        functools.partial(finish_kernel, width),
        out_shape=tuple(jax.ShapeDtypeStruct(s, F32) for s in shapes),
        in_specs=[hbm] * 5 + [vm],
        out_specs=(hbm,) * 4 + (vm, hbm, hbm, vm, hbm, hbm),
        scratch_shapes=[pltpu.SemaphoreType.DMA((7 + wide,))],
    )(*rows, summed, gains)
def fused_shards(
    grid,
    tokens,
    latents,
    slot_group,
    image_groups,
    gain_attn,
    w_qkv,
    w_out,
    gain_mlp,
    w_up,
    w_down,
    d_tokens,
    d_latents,
):
    micro, tok, width = tokens.shape
    lat = latents.shape[1]
    out_tok, out_lat, grad_tok, grad_lat, unused_grads, summed, gains = both_layers(
        grid,
        tokens.reshape(micro * tok, width),
        latents.reshape(micro * lat, width),
        slot_group,
        image_groups,
        (gain_attn, gain_mlp),
        (w_qkv[0], w_out[0], w_up[0], w_down[0]),
        d_tokens.reshape(micro * tok, width),
        d_latents.reshape(micro * lat, width),
    )
    wide = w_up.shape[2] // width
    rows = (out_tok, out_lat, grad_tok, grad_lat)
    *rows, first_gain, qkv, out, second_gain, up, down = finished(rows, summed, gains, wide)
    return (
        rows[0].reshape(1, micro, tok, width),
        rows[1].reshape(1, micro, lat, width),
        rows[2].reshape(1, micro, tok, width),
        rows[3].reshape(1, micro, lat, width),
        first_gain,
        qkv.reshape(-1, width).T[None],
        out.reshape(-1, width).T[None],
        second_gain,
        up.reshape(-1, width).T[None],
        down.T[None],
    )

def solution(mesh):
    in_specs = (
        P(None, "dp", None),
        P(None, "dp", None),
        P(),
        P(),
        P("section", None),
        P("section", None, None),
        P("section", None, None),
        P("section", None),
        P("section", None, None),
        P("section", None, None),
        P(None, "dp", None),
        P(None, "dp", None),
    )
    out_specs = (
        P("section", None, "dp", None),
        P("section", None, "dp", None),
        P("section", None, "dp", None),
        P("section", None, "dp", None),
        P("section", "dp"),
        P("section", None, "dp"),
        P("section", None, "dp"),
        P("section", "dp"),
        P("section", None, "dp"),
        P("section", None, "dp"),
    )
    grid = grid_of(mesh)

    def program(*args):
        n, width = mesh.shape["dp"], args[0].shape[2]
        one_group = args[0].shape[1] == n * GROUP
        body = fused_shards if one_group and width % (16 * n) == 0 and min(grid) > 1 else shards
        return jax.shard_map(
            functools.partial(body, grid), mesh=mesh, in_specs=in_specs, out_specs=out_specs, check_vma=False
        )(*args)

    return program
```

```python
import functools

import jax
import jax.numpy as jnp
from jax import lax
from jax.experimental import pallas as pl
from jax.experimental.pallas import tpu as pltpu
from jax.sharding import PartitionSpec as P

HEADS = 12
GROUP = 256
LAT = 8


epsilon = 1e-05
masked_score = -1e30


MESH = pl.DeviceIdType.MESH


def grid_of(mesh):
    n = mesh.shape["dp"]
    coords = [getattr(d, "coords", None) for d in mesh.devices.reshape(n, -1)[:, 0]]
    if any(c is None for c in coords):
        return (n // 4, 2, 2) if n % 4 == 0 else (n, 1, 1)
    sizes = {a: len({c[a] for c in coords}) for a in range(3)}
    strides = {
        a: min([i for i in range(n) if coords[i][a] != coords[0][a]], default=n) for a in range(3)
    }
    order = sorted(range(3), key=lambda a: -strides[a])
    return tuple(sizes[a] for a in order)


def spread_kernel(grid, pairs, g_ref, gain_ref, out_ref, gout_ref, *scratch):
    acc = scratch[0:3]
    land = [scratch[3 + 3 * i : 6 + 3 * i] for i in range(3)]
    send_sem, recv_sem, own_sem = scratch[12:15]
    me = lax.axis_index("dp")
    section = lax.axis_index("section")
    l0, l1, l2 = grid
    here = (me // (l1 * l2), lax.rem(me // l2, l1), lax.rem(me, l2))

    def device(axis, shift):
        there = list(here)
        there[axis] = lax.rem(here[axis] + shift, grid[axis])
        return there[axis], ((there[0] * l1 + there[1]) * l2 + there[2], section)

    barrier = pltpu.get_barrier_semaphore()
    for axis in range(3):
        for shift in range(1, grid[axis]):
            pl.semaphore_signal(
                barrier, inc=1, device_id=device(axis, shift)[1], device_id_type=MESH
            )
    pl.semaphore_wait(barrier, sum(grid) - 3)

    orders = ((2, 1, 0), (1, 2, 0), (2, 1, 0))

    def source(stream, phase, k, at):
        if phase == 0:
            if stream == 0:
                return g_ref.at[2 * k, :, :, at]
            if stream == 1:
                return g_ref.at[2 * k + 1, :, at]
            return gain_ref.at[:, :, at]
        if phase == 1:
            return acc[stream].at[k, :, at]
        return acc[stream].at[k, at, here[orders[stream][1]]]

    def copies(stream, phase, k):
        axis = orders[stream][phase]
        for shift in range(1, grid[axis]):
            at, target = device(axis, shift)
            yield pltpu.make_async_remote_copy(
                src_ref=source(stream, phase, k, at),
                dst_ref=land[phase][stream].at[k, shift - 1],
                send_sem=send_sem.at[stream, phase, k, shift - 1],
                recv_sem=recv_sem.at[stream, phase, k, shift - 1],
                device_id=target,
                device_id_type=MESH,
            )

    def own(stream, k):
        return pltpu.make_async_copy(
            source(stream, 0, k, here[orders[stream][0]]), acc[stream].at[k], own_sem.at[stream, k]
        )

    def launch(stream, phase, k):
        for copy in copies(stream, phase, k):
            copy.start()

    def absorb(stream, phase, k):
        axis = orders[stream][phase]
        if phase == 0:
            own(stream, k).wait()
        for copy in copies(stream, phase, k):
            copy.wait_recv()
        into = land[phase][stream]
        count = grid[axis] - 1
        if phase == 0:
            for a in range(acc[stream].shape[1]):
                for b in range(acc[stream].shape[2]):
                    total = acc[stream][k, a, b].astype(jnp.float32)
                    for s in range(count):
                        total += into[k, s, a, b].astype(jnp.float32)
                    acc[stream][k, a, b] = total.astype(acc[stream].dtype)
        elif phase == 1:
            mine = here[axis]
            for a in range(acc[stream].shape[1]):
                total = acc[stream][k, a, mine].astype(jnp.float32)
                for s in range(count):
                    total += into[k, s, a].astype(jnp.float32)
                acc[stream][k, a, mine] = total.astype(acc[stream].dtype)
        else:
            total = acc[stream][k, here[0], here[orders[stream][1]]].astype(jnp.float32)
            for s in range(count):
                total += into[k, s].astype(jnp.float32)
            if stream < 2:
                out_ref[2 * k + stream] = total
            else:
                gout_ref[...] = total

    own(2, 0).start()
    launch(2, 0, 0)

    def start_own(k, carry):
        for stream in (0, 1):
            own(stream, k).start()
        return carry

    for stream in (0, 1):
        launch(stream, 0, 0)
    lax.fori_loop(0, pairs, start_own, 0)

    def turn(t, carry):
        @pl.when(t + 1 < pairs)
        def _():
            for stream in (0, 1):
                launch(stream, 0, t + 1)

        @pl.when(t < pairs)
        def _():
            for stream in (0, 1):
                absorb(stream, 0, t)
                launch(stream, 1, t)

        @pl.when((t >= 1) & (t - 1 < pairs))
        def _():
            for stream in (0, 1):
                absorb(stream, 1, t - 1)
                launch(stream, 2, t - 1)

        @pl.when(t >= 2)
        def _():
            for stream in (0, 1):
                absorb(stream, 2, t - 2)

        return carry

    lax.fori_loop(0, pairs + 2, turn, 0)
    absorb(2, 0, 0)
    launch(2, 1, 0)
    absorb(2, 1, 0)
    launch(2, 2, 0)
    absorb(2, 2, 0)

    def finish(k, carry):
        for stream in (0, 1):
            for phase in range(3):
                for copy in copies(stream, phase, k):
                    copy.wait_send()
        return carry

    lax.fori_loop(0, pairs, finish, 0)
    for phase in range(3):
        for copy in copies(2, phase, 0):
            copy.wait_send()


def spread(grid, grads, gains):
    chunks, n, rows, width = grads.shape
    pairs = chunks // 2
    l0, l1, l2 = grid
    most = max(max(grid) - 1, 1)
    low = jnp.bfloat16
    shapes = ((pairs, rows, width, low), (pairs, rows, width, low), (1, 8, 128, jnp.float32))
    inner = ((l1, l2), (l2, l1), (l1, l2))
    acc, first, second, third = [], [], [], []
    for (count, r, w, dt), (kept, sent) in zip(shapes, inner):
        acc.append(pltpu.VMEM((count, l0, kept, r, w), dt))
        first.append(pltpu.VMEM((count, max(sent - 1, 1), l0, kept, r, w), dt))
        second.append(pltpu.VMEM((count, max(kept - 1, 1), l0, r, w), dt))
        third.append(pltpu.VMEM((count, max(l0 - 1, 1), r, w), dt))
    return pl.pallas_call(
        functools.partial(spread_kernel, grid, pairs),
        out_shape=(
            jax.ShapeDtypeStruct((chunks, rows, width), jnp.float32),
            jax.ShapeDtypeStruct((8, 128), jnp.float32),
        ),
        in_specs=[pl.BlockSpec(memory_space=pl.ANY)] * 2,
        out_specs=(pl.BlockSpec(memory_space=pltpu.VMEM),) * 2,
        scratch_shapes=acc
        + first
        + second
        + third
        + [
            pltpu.SemaphoreType.DMA((3, 3, pairs, most)),
            pltpu.SemaphoreType.DMA((3, 3, pairs, most)),
            pltpu.SemaphoreType.DMA((3, pairs)),
        ],
        compiler_params=pltpu.CompilerParams(
            collective_id=0, has_side_effects=True, vmem_limit_bytes=60 * 1024 * 1024
        ),
        cost_estimate=pl.CostEstimate(flops=0, bytes_accessed=grads.size * 4, transcendentals=0),
    )(grads.reshape(chunks, l0, l1, l2, rows, width), gains.reshape(l0, l1, l2, 8, 128))


def from_behind(x, axis, by):
    devices = lax.axis_size(axis)
    pairs = [(i, i + by) for i in range(devices) if 0 <= i + by < devices]
    return lax.ppermute(x, axis, pairs)


def layer_norm(values, gain):
    row_mean = jnp.mean(values, axis=-1, keepdims=True)
    centred = values - row_mean
    row_var = jnp.mean(centred * centred, axis=-1, keepdims=True)
    return centred * lax.rsqrt(row_var + epsilon) * gain


def front_half(all_rows, gain_attn, w_qkv):
    normed = layer_norm(all_rows, gain_attn).astype(jnp.bfloat16)
    projected = jnp.dot(normed, w_qkv, preferred_element_type=jnp.float32).astype(jnp.bfloat16)
    return (normed, projected)


def latent_operand(projected, tok_rows, model_width):
    return projected[tok_rows:, model_width:]


def back_half(all_rows, projected, remote_rows, allowed, weights):
    gain_attn, w_qkv, w_out, gain_mlp, w_up, w_down = weights
    row_count, model_width = all_rows.shape
    head_size = model_width // HEADS
    remote_pairs = remote_rows[:, remote_rows.shape[1] - 2 * model_width :]
    queries = projected[:, :model_width].reshape(row_count, HEADS, head_size)
    key_rows = jnp.concatenate(
        [projected[:, model_width : 2 * model_width], remote_pairs[:, :model_width]], axis=0
    )
    value_rows = jnp.concatenate(
        [projected[:, 2 * model_width :], remote_pairs[:, model_width:]], axis=0
    )
    key_rows = key_rows.reshape(-1, HEADS, head_size)
    value_rows = value_rows.reshape(-1, HEADS, head_size)
    scores = jnp.einsum(
        "qhd,khd->hqk", queries, key_rows, preferred_element_type=jnp.float32
    ) * head_size ** (-0.5)
    attn_weights = jax.nn.softmax(jnp.where(allowed[None], scores, masked_score), axis=-1)
    attn_low = attn_weights.astype(jnp.bfloat16)
    mixed_low = jnp.einsum("hqk,khd->qhd", attn_low, value_rows, preferred_element_type=jnp.float32)
    mixed_low = mixed_low.reshape(row_count, model_width).astype(jnp.bfloat16)
    mid_rows = all_rows + jnp.dot(mixed_low, w_out, preferred_element_type=jnp.float32)
    normed_mlp = layer_norm(mid_rows, gain_mlp).astype(jnp.bfloat16)
    up_proj = jnp.dot(normed_mlp, w_up, preferred_element_type=jnp.float32)
    activated = jax.nn.gelu(up_proj).astype(jnp.bfloat16)
    result = mid_rows + jnp.dot(activated, w_down, preferred_element_type=jnp.float32)
    return dict(
        queries=queries,
        key_rows=key_rows,
        value_rows=value_rows,
        attn_weights=attn_weights,
        attn_low=attn_low,
        mixed_low=mixed_low,
        mid_rows=mid_rows,
        normed_mlp=normed_mlp,
        up_proj=up_proj,
        activated=activated,
        result=result,
    )


def section_backward(saved, d_result, all_rows, normed, allowed, weights, latent_start):
    gain_attn, w_qkv, w_out, gain_mlp, w_up, w_down = weights
    row_count, model_width = all_rows.shape
    head_size = model_width // HEADS
    score_scale = head_size ** (-0.5)
    d_low = d_result.astype(jnp.bfloat16)
    grad_down = jnp.dot(d_low.T, saved["activated"], preferred_element_type=jnp.float32)
    d_activated = jnp.dot(d_low, w_down.T, preferred_element_type=jnp.float32)
    unused_up, gelu_back = jax.vjp(jax.nn.gelu, saved["up_proj"])
    d_up = gelu_back(d_activated)[0].astype(jnp.bfloat16)
    grad_up = jnp.dot(d_up.T, saved["normed_mlp"], preferred_element_type=jnp.float32)
    d_normed_mlp = jnp.dot(d_up, w_up.T, preferred_element_type=jnp.float32)
    unused_mid, second_back = jax.vjp(layer_norm, saved["mid_rows"], gain_mlp)
    d_mid_norm, grad_gain_mlp = second_back(d_normed_mlp)
    d_mid = d_result + d_mid_norm
    d_mid_low = d_mid.astype(jnp.bfloat16)
    grad_out = jnp.dot(d_mid_low.T, saved["mixed_low"], preferred_element_type=jnp.float32)
    d_mixed = jnp.dot(d_mid_low, w_out.T, preferred_element_type=jnp.float32).astype(jnp.bfloat16)
    d_mixed = d_mixed.reshape(row_count, HEADS, head_size)
    d_weights = jnp.einsum(
        "qhd,khd->hqk", d_mixed, saved["value_rows"], preferred_element_type=jnp.float32
    )
    d_values = jnp.einsum(
        "hqk,qhd->khd", saved["attn_low"], d_mixed, preferred_element_type=jnp.float32
    )
    attn_weights = saved["attn_weights"]
    d_scores = attn_weights * (
        d_weights - jnp.sum(attn_weights * d_weights, axis=-1, keepdims=True)
    )
    d_scores_low = jnp.where(allowed[None], d_scores, 0.0).astype(jnp.bfloat16)
    d_queries = (
        jnp.einsum(
            "hqk,khd->qhd", d_scores_low, saved["key_rows"], preferred_element_type=jnp.float32
        )
        * score_scale
    )
    d_keys = (
        jnp.einsum(
            "hqk,qhd->khd", d_scores_low, saved["queries"], preferred_element_type=jnp.float32
        )
        * score_scale
    )
    remote_part = jnp.concatenate(
        [
            d_keys[row_count:].reshape(-1, model_width),
            d_values[row_count:].reshape(-1, model_width),
        ],
        axis=1,
    )
    own_part = lax.psum_scatter(remote_part, "dp", scatter_dimension=0, tiled=True)
    local_pairs = jnp.concatenate(
        [
            d_keys[:row_count].reshape(row_count, model_width),
            d_values[:row_count].reshape(row_count, model_width),
        ],
        axis=1,
    )
    local_pairs = jnp.concatenate(
        [local_pairs[:latent_start], local_pairs[latent_start:] + own_part], axis=0
    )
    d_projected = jnp.concatenate(
        [d_queries.reshape(row_count, model_width), local_pairs], axis=1
    ).astype(jnp.bfloat16)
    grad_qkv = jnp.dot(d_projected.T, normed, preferred_element_type=jnp.float32)
    d_normed = jnp.dot(d_projected, w_qkv.T, preferred_element_type=jnp.float32)
    unused_rows, first_back = jax.vjp(layer_norm, all_rows, gain_attn)
    d_rows_norm, grad_gain_attn = first_back(d_normed)
    return (
        d_mid + d_rows_norm,
        (grad_gain_attn, grad_qkv, grad_out, grad_gain_mlp, grad_up, grad_down),
    )


def packed(grads, n):
    gain_first, qkv_grad, out_grad, gain_second, up_grad, down_grad = grads
    width = out_grad.shape[0]
    rows = width // n

    def by_rows(grad):
        return grad.reshape(n, -1, rows, width).transpose(1, 0, 2, 3).astype(jnp.bfloat16)

    down = down_grad.reshape(n, rows, -1, width).transpose(2, 0, 1, 3).astype(jnp.bfloat16)
    chunks = jnp.concatenate([down, by_rows(up_grad), by_rows(out_grad), by_rows(qkv_grad)], axis=0)
    gains = jnp.stack([gain_first.reshape(n, rows), gain_second.reshape(n, rows)], axis=1)
    return chunks, jnp.pad(gains, ((0, 0), (0, 6), (0, 128 - rows)))


def shards(
    grid,
    tokens,
    latents,
    slot_group,
    image_groups,
    gain_attn,
    w_qkv,
    w_out,
    gain_mlp,
    w_up,
    w_down,
    d_tokens,
    d_latents,
):
    micro = tokens.shape[0]
    tok_rows = tokens.shape[1]
    lat_rows = latents.shape[1]
    model_width = tokens.shape[2]
    local_groups = tok_rows // GROUP
    section_index = lax.axis_index("section")
    is_global = section_index == 1
    dp_index = lax.axis_index("dp")
    weights = (gain_attn[0], w_qkv[0], w_out[0], gain_mlp[0], w_up[0], w_down[0])
    image_ends = jnp.cumsum(image_groups, axis=1)
    slot_images = jnp.sum(
        (image_ends[:, None, :] <= slot_group[:, :, None]).astype(jnp.int32), axis=2
    )
    slot_total = slot_group.shape[1]
    row_group = jnp.concatenate([jnp.arange(tok_rows) // GROUP, jnp.arange(lat_rows) // LAT])
    row_latent = jnp.concatenate(
        [jnp.zeros((tok_rows,), jnp.bool_), jnp.ones((lat_rows,), jnp.bool_)]
    )
    same_group = row_group[:, None] == row_group[None, :]
    local_mask = jnp.where(
        is_global, (~row_latent)[:, None] & row_latent[None, :] & same_group, same_group
    )
    group_match = row_group[:, None] == jnp.arange(local_groups)[None, :]

    def key_images(batch):
        images_row = lax.dynamic_index_in_dim(slot_images, batch, 0, keepdims=False)
        return (images_row, jnp.broadcast_to(images_row[:, None], (slot_total, LAT)).reshape(-1))

    def allowed_for(batch):
        images_row, key_image = key_images(batch)
        own_images = lax.dynamic_slice_in_dim(images_row, dp_index * local_groups, local_groups)
        row_image = jnp.sum(jnp.where(group_match, own_images[None, :], 0), axis=1)
        remote_mask = is_global & row_latent[:, None] & (row_image[:, None] == key_image[None, :])
        return jnp.concatenate([local_mask, remote_mask], axis=1)

    def forward_turn(received, turn):
        recv_tokens, recv_latents = received
        batch = jnp.clip(turn - section_index, 0, micro - 1)
        own_tok = lax.dynamic_index_in_dim(tokens, batch, 0, keepdims=False)
        own_lat = lax.dynamic_index_in_dim(latents, batch, 0, keepdims=False)
        input_rows = jnp.concatenate(
            [
                jnp.where(is_global, recv_tokens, own_tok),
                jnp.where(is_global, recv_latents, own_lat),
            ],
            axis=0,
        )
        all_rows = input_rows.astype(jnp.float32)
        normed, projected = front_half(all_rows, weights[0], weights[1])
        remote_rows = lax.all_gather(
            latent_operand(projected, tok_rows, model_width), "dp", axis=0, tiled=True
        )
        saved = back_half(all_rows, projected, remote_rows, allowed_for(batch), weights)
        result = saved["result"]
        result_low = result.astype(jnp.bfloat16)
        stored = jnp.where(is_global, result, result_low.astype(jnp.float32))
        passed_on = from_behind((result_low[:tok_rows], result_low[tok_rows:]), "section", 1)
        return passed_on, (input_rows, stored[:tok_rows], stored[tok_rows:])

    nothing = (
        jnp.zeros((tok_rows, model_width), jnp.bfloat16),
        jnp.zeros((lat_rows, model_width), jnp.bfloat16),
    )
    turns = jnp.arange(micro + 1)
    unused_end, (kept_rows, tok_outputs, lat_outputs) = lax.scan(forward_turn, nothing, turns)

    def backward_turn(carry, turn):
        (recv_grad_tok, recv_grad_lat), totals = carry
        raw_batch = micro - turn - section_index
        valid = ((raw_batch >= 0) & (raw_batch < micro)).astype(jnp.float32)
        batch = jnp.clip(raw_batch, 0, micro - 1)
        all_rows = lax.dynamic_index_in_dim(
            kept_rows, batch + section_index, 0, keepdims=False
        ).astype(jnp.float32)
        normed, projected = front_half(all_rows, weights[0], weights[1])
        remote_rows = lax.all_gather(
            latent_operand(projected, tok_rows, model_width), "dp", axis=0, tiled=True
        )
        allowed = allowed_for(batch)
        saved = back_half(all_rows, projected, remote_rows, allowed, weights)
        given = (
            jnp.concatenate(
                [
                    lax.dynamic_index_in_dim(d_tokens, batch, 0, keepdims=False),
                    lax.dynamic_index_in_dim(d_latents, batch, 0, keepdims=False),
                ],
                axis=0,
            )
            * valid
        )
        passed = jnp.concatenate([recv_grad_tok, recv_grad_lat], axis=0).astype(jnp.float32)
        d_result = jnp.where(is_global, given, passed)
        d_rows, grads = section_backward(
            saved, d_result, all_rows, normed, allowed, weights, tok_rows
        )
        totals = tuple((accum + piece for accum, piece in zip(totals, grads)))
        d_rows_low = d_rows.astype(jnp.bfloat16)
        stored = jnp.where(is_global, d_rows_low.astype(jnp.float32), d_rows)
        sent = from_behind((d_rows_low[:tok_rows], d_rows_low[tok_rows:]), "section", -1)
        return (sent, totals), (stored[:tok_rows], stored[tok_rows:])

    totals = tuple(
        jnp.zeros(w.shape[::-1] if w.ndim == 2 else w.shape, jnp.float32) for w in weights
    )
    (unused_sent, totals), (tok_grads, lat_grads) = lax.scan(
        backward_turn, (nothing, totals), turns
    )
    chunks, gains = packed(totals, lax.axis_size("dp"))
    summed, gain_sums = spread(grid, chunks, gains)
    rows = summed.shape[1]
    layer_tokens = lax.dynamic_slice_in_dim(tok_outputs, section_index, micro, 0)[None]
    layer_latents = lax.dynamic_slice_in_dim(lat_outputs, section_index, micro, 0)[None]
    grad_tokens = lax.dynamic_slice_in_dim(tok_grads, 1 - section_index, micro, 0)[::-1][
        None
    ]
    grad_latents = lax.dynamic_slice_in_dim(lat_grads, 1 - section_index, micro, 0)[
        ::-1
    ][None]
    return (
        layer_tokens,
        layer_latents,
        grad_tokens,
        grad_latents,
        gain_sums[0:1, :rows],
        summed[9:].reshape(-1, model_width).T[None],
        summed[8].T[None],
        gain_sums[1:2, :rows],
        summed[4:8].reshape(-1, model_width).T[None],
        summed[0:4].transpose(0, 2, 1).reshape(-1, rows)[None],
    )


F32 = jnp.float32
LOW = jnp.bfloat16
HEAD_PAD = 16
TILE = 768


def nn(a, b):
    return jnp.dot(a, b, preferred_element_type=F32)


def nt(a, b):
    return lax.dot_general(a, b, (((1,), (1,)), ((), ())), preferred_element_type=F32)


def tn(a, b):
    return lax.dot_general(a, b, (((0,), (0,)), ((), ())), preferred_element_type=F32)


def normed_rows(values):
    centred = values - jnp.mean(values, axis=-1, keepdims=True)
    scale = lax.rsqrt(jnp.mean(centred * centred, axis=-1, keepdims=True) + epsilon)
    return centred * scale, scale


def norm_back(grad, hat, scale, gain):
    scaled = grad * gain
    mean = jnp.mean(scaled, axis=-1, keepdims=True)
    along = jnp.mean(scaled * hat, axis=-1, keepdims=True)
    return scale * (scaled - mean - hat * along)


def at(start, size):
    return pl.ds(pl.multiple_of(start, size), size)


def class_max(s):
    for by in (16, 32, 64):
        s = jnp.maximum(s, pltpu.roll(s, by, 1))
    return s


def class_sum(s):
    for by in (16, 32, 64):
        s = s + pltpu.roll(s, by, 1)
    return s


def layer_kernel(
    n,
    tokens,
    latents,
    slots,
    slot_at,
    image_at,
    gain_attn,
    gain_mlp,
    w_qkv,
    w_out,
    w_up,
    w_down,
    d_tokens,
    d_latents,
    out_tok,
    out_lat,
    grad_tok,
    grad_lat,
    grads,
    summed,
    gain_sums,
    wq,
    wo,
    wu,
    wd,
    xb,
    n1,
    proj,
    mixed,
    mid,
    n2,
    act,
    dup,
    yb,
    dy,
    ef,
    tmp,
    out,
    probs,
    probs_lat,
    latf,
    mixf,
    key_mask,
    qbd,
    kbd,
    vbd,
    kv_all,
    kvg_send,
    kvg_recv,
    stage,
    gains,
    leaving,
    own_a,
    own_b,
    land1_a,
    land1_b,
    land2_a,
    land2_b,
    land3_a,
    land3_b,
    land4_a,
    land4_b,
    land_g,
    load_sem,
    stage_sem,
    own_sem,
    leave_sem,
    send_sem,
    recv_sem,
    gain_s,
    gain_r,
    relay_send,
    relay_recv,
    kv_sem_s,
    kv_sem_r,
    kvg_sem_s,
    kvg_sem_r,
):
    rows, width = xb.shape
    ff = act.shape[1]
    tok = tokens.shape[0]
    lat = latents.shape[0]
    half = lat // LAT
    pairs = width // 128
    me = lax.axis_index("dp")
    section = lax.axis_index("section")
    first = section == 0
    second = section == 1
    partner = (me, 1 - section)

    loads = [
        pltpu.make_async_copy(src, dst, load_sem.at[i])
        for i, (src, dst) in enumerate(((w_qkv, wq), (w_out, wo), (w_up, wu), (w_down, wd)))
    ]
    x_loads = [
        pltpu.make_async_copy(tokens, xb.at[0:tok], load_sem.at[4]),
        pltpu.make_async_copy(latents, xb.at[tok:rows], load_sem.at[5]),
    ]
    e_loads = [
        pltpu.make_async_copy(d_tokens, ef.at[0:tok], load_sem.at[6]),
        pltpu.make_async_copy(d_latents, ef.at[tok:rows], load_sem.at[7]),
    ]

    @pl.when(first)
    def _():
        for copy in x_loads:
            copy.start()

    for copy in loads:
        copy.start()

    @pl.when(second)
    def _():
        for copy in e_loads:
            copy.start()

    barrier = pltpu.get_barrier_semaphore()
    pl.semaphore_signal(barrier, inc=1, device_id=partner, device_id_type=MESH)

    here = [lax.rem(me // (1 << bit), 2) for bit in range(4)]

    def across(bit):
        return (me + (1 - 2 * here[bit]) * (1 << bit), section)

    @pl.when(second)
    def _():
        for shift in range(1, n):
            pl.semaphore_signal(
                barrier, inc=1, device_id=(lax.rem(me + shift, n), section), device_id_type=MESH
            )
        pl.semaphore_wait(barrier, n)

    @pl.when(first)
    def _():
        for bit in range(4):
            pl.semaphore_signal(barrier, inc=1, device_id=across(bit), device_id_type=MESH)
        pl.semaphore_wait(barrier, 5)

    forward_relay = pltpu.make_async_remote_copy(
        src_ref=yb, dst_ref=xb, send_sem=relay_send.at[0], recv_sem=relay_recv.at[0],
        device_id=partner, device_id_type=MESH,
    )
    backward_relay = pltpu.make_async_remote_copy(
        src_ref=yb, dst_ref=dy, send_sem=relay_send.at[1], recv_sem=relay_recv.at[1],
        device_id=partner, device_id_type=MESH,
    )

    def kv_copy(shift, incoming):
        slot = lax.rem(me + n - shift, n) if incoming else me
        return pltpu.make_async_remote_copy(
            src_ref=kv_all.at[me], dst_ref=kv_all.at[slot],
            send_sem=kv_sem_s.at[shift - 1], recv_sem=kv_sem_r.at[shift - 1],
            device_id=(lax.rem(me + shift, n), section), device_id_type=MESH,
        )

    def kvg_copy(shift):
        there = lax.rem(me + shift, n)
        return pltpu.make_async_remote_copy(
            src_ref=kvg_send.at[there], dst_ref=kvg_recv.at[shift - 1],
            send_sem=kvg_sem_s.at[shift - 1], recv_sem=kvg_sem_r.at[shift - 1],
            device_id=(there, section), device_id_type=MESH,
        )

    lane = lax.broadcasted_iota(jnp.int32, (1, 128), 1)
    halves = [(lane < 64).astype(F32).astype(LOW), (lane >= 64).astype(F32).astype(LOW)]
    eighths = [(h.astype(F32) * 0.125).astype(LOW) for h in halves]
    heads = (
        lax.broadcasted_iota(jnp.int32, (HEAD_PAD, width), 1) // 64
        == lax.broadcasted_iota(jnp.int32, (HEAD_PAD, width), 0)
    ).astype(F32)

    def block_diagonal(dst, base, src, row, column, scale):
        for i in range(LAT):
            line = src[row + i : row + i + 1, column : column + width] * scale
            dst[base + i * HEAD_PAD : base + (i + 1) * HEAD_PAD, :] = (line * heads).astype(LOW)

    def head_sum(dst, row, column, value, scale, add):
        for i in range(LAT):
            line = jnp.sum(
                value[i * HEAD_PAD : (i + 1) * HEAD_PAD] * heads, axis=0, keepdims=True
            )
            line = line * scale
            if add:
                line = line + dst[row + i : row + i + 1, column : column + width]
            dst[row + i : row + i + 1, column : column + width] = line

    def bands(body, lo, hi, size):
        def one(i, carry):
            body(pl.ds(pl.multiple_of(lo + i * size, 16), size))
            return carry

        lax.fori_loop(0, (hi - lo) // size, one, 0)

    third = rows // 3

    def tiles(count, body, size=TILE):
        def one(i, carry):
            body(at(i * size, size))
            return carry

        lax.fori_loop(0, count, one, 0)

    @pl.when(first)
    def _():
        for copy in x_loads:
            copy.wait()

    @pl.when(second)
    def _():
        spots = lax.broadcasted_iota(jnp.int32, (n, n * lat), 1) // lat
        spread_out = (spots == lax.broadcasted_iota(jnp.int32, (n, n * lat), 0)).astype(F32)
        groups = nn(slots[...].astype(F32).astype(LOW), spread_out.astype(LOW))
        of_micro = lax.rem(lax.broadcasted_iota(jnp.int32, (1, n * lat), 1), lat) // LAT
        for m in range(half):
            images = jnp.zeros((1, n * lat), F32)
            own_image = jnp.float32(0)
            end = jnp.int32(0)
            for i in range(image_at.shape[1]):
                end = end + image_at[m, i]
                images += jnp.where(end.astype(F32) <= groups[m : m + 1], 1.0, 0.0)
                own_image += jnp.where(end <= slot_at[m, me], 1.0, 0.0)
            seen = (images == own_image) & (of_micro == m)
            key_mask[m : m + 1, :] = jnp.where(seen, 0.0, masked_score)
        forward_relay.wait_recv()

    def norm_in(r):
        hat, unused = normed_rows(xb[r, :].astype(F32))
        n1[r, :] = (hat * gain_attn[...]).astype(LOW)

    bands(norm_in, 0, rows, third)
    loads[0].wait()

    @pl.when(second)
    def _():
        own = nn(n1[tok:rows, :], wq[:, width:]).astype(LOW)
        kv_all[me] = own
        latf[:, width:] = own.astype(F32)
        for shift in range(1, n):
            kv_copy(shift, False).start()

    def project(c):
        proj[:, c] = nn(n1[...], wq[:, c]).astype(LOW)

    per = width // TILE
    tiles(jnp.where(first, 3 * per, per), project)

    def lat_bias(m, shape, axis):
        return jnp.where(
            lax.broadcasted_iota(jnp.int32, shape, axis) // LAT == m, 0.0, masked_score
        ).astype(F32)

    @pl.when(first)
    def _():
        latf[...] = proj[tok:rows, :].astype(F32)

        def one_pair(it):
            m, p = it // pairs, lax.rem(it, pairs)
            r = at(m * GROUP, GROUP)
            q = proj[r, at(p * 128, 128)]
            k = proj[r, at(width + p * 128, 128)]
            v = proj[r, at(2 * width + p * 128, 128)]
            kl = proj[tok:rows, at(width + p * 128, 128)]
            vl = proj[tok:rows, at(2 * width + p * 128, 128)]
            bias = lat_bias(m, (lat, GROUP), 0)
            total = jnp.zeros((GROUP, 128), F32)
            for e in (0, 1):
                qe = q * eighths[e]
                st = nt(k, qe)
                sl = nt(kl, qe) + bias
                top = jnp.maximum(
                    jnp.max(st, axis=0, keepdims=True), jnp.max(sl, axis=0, keepdims=True)
                )
                et = jnp.exp(st - top)
                el = jnp.exp(sl - top)
                scale = 1.0 / (
                    jnp.sum(et, axis=0, keepdims=True) + jnp.sum(el, axis=0, keepdims=True)
                )
                pt = (et * scale).astype(LOW)
                pe = (el * scale).astype(LOW)
                probs[2 * it + e, 0:GROUP, :] = pt
                probs[2 * it + e, GROUP : GROUP + lat, :] = pe
                total += tn(pt, v * halves[e]) + tn(pe, vl * halves[e])
            mixed[r, at(p * 128, 128)] = total.astype(LOW)

        def pair(i, carry):
            one_pair(2 * i)
            one_pair(2 * i + 1)
            return carry

        lax.fori_loop(0, half * pairs // 2, pair, 0)
        for m in range(half):
            r = slice(m * GROUP, (m + 1) * GROUP)
            b = slice(m * 128, (m + 1) * 128)
            block_diagonal(qbd, m * 128, latf, m * LAT, 0, 0.125)
            s = nt(qbd[b, :], proj[r, width : 2 * width])
            sl = nt(qbd[b, :], proj[tok:rows, width : 2 * width]) + lat_bias(m, (128, lat), 1)
            top = jnp.maximum(
                jnp.max(s, axis=1, keepdims=True), jnp.max(sl, axis=1, keepdims=True)
            )
            et = jnp.exp(s - top)
            el = jnp.exp(sl - top)
            scale = 1.0 / (
                jnp.sum(et, axis=1, keepdims=True) + jnp.sum(el, axis=1, keepdims=True)
            )
            pt = (et * scale).astype(LOW)
            pe = (el * scale).astype(LOW)
            probs_lat[b, 0:GROUP] = pt
            probs_lat[b, GROUP : GROUP + lat] = pe
            o = nn(pt, proj[r, 2 * width :]) + nn(pe, proj[tok:rows, 2 * width :])
            head_sum(mixf, m * LAT, 0, o, 1.0, False)
        mixed[tok:rows, :] = mixf[...].astype(LOW)

    keys = n * lat

    @pl.when(second)
    def _():
        latf[:, :width] = proj[tok:rows, :width].astype(F32)
        for m in range(half):
            r = slice(m * GROUP, (m + 1) * GROUP)
            b = slice(m * 128, (m + 1) * 128)
            block_diagonal(qbd, m * 128, latf, m * LAT, 0, 0.125)
            block_diagonal(kbd, m * 128, latf, m * LAT, width, 1.0)
            block_diagonal(vbd, m * 128, latf, m * LAT, 2 * width, 1.0)
            s = nt(proj[r, :width] * jnp.asarray(0.125, LOW), kbd[b, :])
            et = jnp.exp(s - class_max(s))
            pt = (et / class_sum(et)).astype(LOW)
            probs[m, 0:GROUP, 0:128] = pt
            mixed[r, :] = nn(pt, vbd[b, :]).astype(LOW)

    root = 0.7978845608028654

    def mlp_in(lo, hi, size):
        r0 = slice(lo, hi)
        mid[r0, :] = xb[r0, :].astype(F32) + nn(mixed[r0, :], wo[...])

        def norm_mid(r):
            hat, unused = normed_rows(mid[r, :])
            n2[r, :] = (hat * gain_mlp[...]).astype(LOW)

        bands(norm_mid, lo, hi, size)

        def widen(c):
            up = nn(n2[r0, :], wu[:, c])
            square = up * up
            t = jnp.tanh(up * (root + (root * 0.044715) * square))
            gate = 0.5 + 0.5 * t
            value = up * gate
            slope = gate + 2.0 * value * (1.0 - gate) * (root + (3.0 * root * 0.044715) * square)
            act[r0, c] = value.astype(LOW)
            dup[r0, c] = slope.astype(LOW)

        tiles(ff // 384, widen, 384)

    for copy in loads[1:]:
        copy.wait()

    @pl.when(first)
    def _():
        mlp_in(0, rows, third)

    @pl.when(second)
    def _():
        mlp_in(0, tok, tok // 4)
        for shift in range(1, n):
            kv_copy(shift, True).wait_recv()
        k = kv_all[:, :, :width].reshape(keys, width)
        v = kv_all[:, :, width:].reshape(keys, width)
        for m in range(half):
            b = slice(m * 128, (m + 1) * 128)
            s = nt(qbd[b, :], k) + key_mask[m : m + 1, :]
            et = jnp.exp(s - jnp.max(s, axis=1, keepdims=True))
            pt = (et / jnp.sum(et, axis=1, keepdims=True)).astype(LOW)
            probs_lat[b, 0:keys] = pt
            head_sum(mixf, m * LAT, 0, nn(pt, v), 1.0, False)
        mixed[tok:rows, :] = mixf[...].astype(LOW)

        mlp_in(tok, rows, lat)

    out_copies = [
        pltpu.make_async_copy(out.at[0:tok], out_tok, load_sem.at[8]),
        pltpu.make_async_copy(out.at[tok:rows], out_lat, load_sem.at[9]),
    ]
    grad_copies = [
        pltpu.make_async_copy(out.at[0:tok], grad_tok, load_sem.at[8]),
        pltpu.make_async_copy(out.at[tok:rows], grad_lat, load_sem.at[9]),
    ]

    def layer_output(passed_on):
        def narrow(c):
            y = mid[:, c] + nn(act[...], wd[:, c])
            if passed_on:
                low = y.astype(LOW)
                yb[:, c] = low
                y = low.astype(F32)
            out[:, c] = y

        tiles(width // 384, narrow, 384)
        for copy in out_copies:
            copy.start()

    @pl.when(first)
    def _():
        layer_output(True)
        forward_relay.start()
        backward_relay.wait_recv()

        def widen_e(r):
            ef[r, :] = dy[r, :].astype(F32)

        bands(widen_e, 0, rows, third)

    @pl.when(second)
    def _():
        for copy in e_loads:
            copy.wait()

        def narrow_e(r):
            dy[r, :] = ef[r, :].astype(LOW)

        bands(narrow_e, 0, rows, third)

    part = 384
    unit = width // n
    many = part // unit

    def staged(slot, piece, chunk, share):
        return pltpu.make_async_copy(
            stage.at[slot, piece],
            grads.at[
                chunk,
                share // 8,
                lax.rem(share // 4, 2),
                lax.rem(share // 2, 2),
                lax.rem(share, 2),
            ],
            stage_sem.at[slot, piece],
        )

    def drain(slot):
        def one(piece, carry):
            staged(slot, piece, 0, 0).wait()
            return carry

        lax.fori_loop(0, many, one, 0)

    def weight_grad(place, start, count, left, *rights):
        def one(i, carry):
            turned = left(i).T
            for at_right, right in enumerate(rights):
                tile = i * len(rights) + at_right
                slot = lax.rem(tile, 2)
                value = nn(turned, right(i)).astype(LOW)

                @pl.when(tile >= start * len(rights) + 2)
                def _():
                    drain(slot)

                for piece in range(many):
                    stage[slot, piece] = value[piece * unit : (piece + 1) * unit]
                    staged(slot, piece, *place(i, at_right, piece)).start()
            return carry

        lax.fori_loop(start, start + count, one, 0)
        for slot in (0, 1):
            drain(slot)

    orders = ((0, 2, 1, 3), (1, 2, 0, 3))
    own_buf = (own_a, own_b)
    land = (
        (land1_a, land1_b),
        (land2_a, land2_b),
        (land3_a, land3_b),
        (land4_a, land4_b),
    )
    spread_pairs = land1_a.shape[0]

    def source(stream, phase, k, theirs):
        pick = [(1 - here[bit]) if theirs else here[bit] for bit in orders[stream]]
        own_bit = [here[bit] for bit in orders[stream]]
        base = land[0][stream]
        if phase == 0:
            if stream == 0:
                return grads.at[2 * k, :, :, :, pick[0]]
            return grads.at[2 * k + 1, :, :, pick[0]]
        if phase == 1:
            return base.at[k, :, pick[1]]
        if phase == 2:
            return base.at[k, :, own_bit[1], pick[2]]
        return base.at[k, pick[3], own_bit[1], own_bit[2]]

    def copy_of(stream, phase, k):
        return pltpu.make_async_remote_copy(
            src_ref=source(stream, phase, k, True),
            dst_ref=land[phase][stream].at[k],
            send_sem=send_sem.at[stream, phase, k],
            recv_sem=recv_sem.at[stream, phase, k],
            device_id=across(orders[stream][phase]),
            device_id_type=MESH,
        )

    def own(stream, k):
        return pltpu.make_async_copy(
            source(stream, 0, k, False), own_buf[stream], own_sem.at[stream]
        )

    def leave(stream, k):
        slot = lax.rem(k, 2)
        return pltpu.make_async_copy(
            leaving.at[slot, stream], summed.at[2 * k + stream], leave_sem.at[slot, stream]
        )

    def launch(phase, k):
        for stream in (0, 1):
            copy_of(stream, phase, k).start()

    def absorb(phase, k):
        for stream in (0, 1):
            if phase == 0:
                own(stream, k).wait()
            copy_of(stream, phase, k).wait_recv()
            base, into = land[0][stream], land[phase][stream]
            mine = [here[bit] for bit in orders[stream]]
            if phase == 0:

                def add(i, carry):
                    for j in (0, 1):
                        for h in (0, 1):
                            total = own_buf[stream][i, j, h].astype(F32)
                            total += base[k, i, j, h].astype(F32)
                            base[k, i, j, h] = total.astype(LOW)
                    return carry

                lax.fori_loop(0, 2, add, 0)
            elif phase == 1:
                for i in (0, 1):
                    for h in (0, 1):
                        total = base[k, i, mine[1], h].astype(F32)
                        total += into[k, i, h].astype(F32)
                        base[k, i, mine[1], h] = total.astype(LOW)
            elif phase == 2:
                for i in (0, 1):
                    total = base[k, i, mine[1], mine[2]].astype(F32)
                    total += into[k, i].astype(F32)
                    base[k, i, mine[1], mine[2]] = total.astype(LOW)
            else:
                total = base[k, mine[3], mine[1], mine[2]].astype(F32)
                total += into[k].astype(F32)
                slot = lax.rem(k, 2)

                @pl.when(k >= 2)
                def _():
                    leave(stream, k - 2).wait()

                leaving[slot, stream] = total
                leave(stream, k).start()

    def start_own(k):
        for stream in (0, 1):
            own(stream, k).start()

    def relaunch(k, following=True):
        absorb(0, k)
        launch(1, k)
        if following:
            start_own(k + 1)

    def onward(phase, k):
        absorb(phase, k)
        if phase < 3:
            launch(phase + 1, k)

    wide = ff // width
    per_part = width // part

    def down_grad(pair):
        weight_grad(
            lambda i, right, piece: (2 * pair + right, i * many + piece),
            0,
            per_part,
            lambda i: dy[:, at(i * part, part)],
            lambda i: act[:, 2 * pair * width : (2 * pair + 1) * width],
            lambda i: act[:, (2 * pair + 1) * width : (2 * pair + 2) * width],
        )

    down_grad(0)
    launch(0, 0)
    start_own(0)
    down_grad(1)
    launch(0, 1)

    def unwiden(c):
        dup[:, c] = (nt(dy[...], wd[c, :]) * dup[:, c].astype(F32)).astype(LOW)

    tiles(ff // TILE, unwiden)
    weight_grad(
        lambda i, right, piece: (
            wide + lax.rem(i * many + piece, wide),
            (i * many + piece) // wide,
        ),
        0,
        ff // part,
        lambda i: dup[:, at(i * part, part)],
        lambda i: n2[...],
    )
    launch(0, 2)
    launch(0, 3)

    relaunch(0)

    def to_mid(c):
        tmp[:, c] = nt(dup[...], wu[c, :])

    tiles(width // 384, to_mid, 384)
    gains[0] = jnp.zeros_like(gains[0])

    def fold(value):
        total = value[0:8]
        for i in range(1, value.shape[0] // 8):
            total = total + value[8 * i : 8 * i + 8]
        return total

    def mid_back(r):
        hat, scale = normed_rows(mid[r, :])
        grad = tmp[r, :]
        gains[0, 8:16, :] += fold(grad * hat)
        total = ef[r, :] + norm_back(grad, hat, scale, gain_mlp[...])
        ef[r, :] = total
        dy[r, :] = total.astype(LOW)

    bands(mid_back, 0, rows, third)
    relaunch(1)

    @pl.when(first)
    def _():
        forward_relay.wait_send()

    def to_mix(c):
        yb[:, c] = nt(dy[...], wo[c, :]).astype(LOW)

    tiles(width // TILE, to_mix)
    mixf[...] = yb[tok:rows, :].astype(F32)

    @pl.when(second)
    def _():
        k = kv_all[:, :, :width].reshape(keys, width)
        v = kv_all[:, :, width:].reshape(keys, width)
        for m in range(half):
            b = slice(m * 128, (m + 1) * 128)
            block_diagonal(vbd.at[pl.ds(256, 256)], m * 128, mixf, m * LAT, 0, 1.0)
        both = slice(0, half * 128)
        do = vbd[256 : 256 + half * 128, :]
        pt = probs_lat[both, 0:keys]
        pf = pt.astype(F32)
        dp = nt(do, v)
        along = jnp.sum(pf * dp, axis=1, keepdims=True)
        ds = (pf * (dp - along)).astype(LOW)
        kvg_send[:, :, :width] = tn(ds, qbd[both, :]).astype(LOW).reshape(n, lat, width)
        kvg_send[:, :, width:] = tn(pt, do).astype(LOW).reshape(n, lat, width)
        for shift in range(1, n):
            kvg_copy(shift).start()
        dq = nn(ds, k)
        for m in range(half):
            head_sum(latf, m * LAT, 0, dq[m * 128 : (m + 1) * 128], 0.125, False)
        proj[tok:rows, :width] = latf[:, :width].astype(LOW)
        layer_output(False)

    onward(1, 0)
    relaunch(2)
    weight_grad(
        lambda i, right, piece: (2 * wide, i * many + piece),
        0,
        width // part,
        lambda i: dy[:, at(i * part, part)],
        lambda i: mixed[...],
    )
    for copy in out_copies:
        copy.wait()

    @pl.when(first)
    def _():
        for m in range(half):
            r = slice(m * GROUP, (m + 1) * GROUP)
            b = slice(m * 128, (m + 1) * 128)
            block_diagonal(vbd, m * 128, mixf, m * LAT, 0, 1.0)
            do = vbd[b, :]
            dp = nt(do, proj[r, 2 * width :])
            dl = nt(do, proj[tok:rows, 2 * width :])
            pt = probs_lat[b, 0:GROUP]
            pe = probs_lat[b, GROUP : GROUP + lat]
            pf = pt.astype(F32)
            pg = pe.astype(F32)
            along = jnp.sum(pf * dp, axis=1, keepdims=True) + jnp.sum(
                pg * dl, axis=1, keepdims=True
            )
            ds = (pf * (dp - along)).astype(LOW)
            dsl = (pg * (dl - along)).astype(LOW)
            dq = nn(ds, proj[r, width : 2 * width]) + nn(dsl, proj[tok:rows, width : 2 * width])
            head_sum(latf, m * LAT, 0, dq, 0.125, False)
            tmp[r, :] = tn(ds, qbd[b, :])
            out[r, :] = tn(pt, do)
            if m == 0:
                tmp[tok:rows, :] = tn(dsl, qbd[b, :])
                out[tok:rows, :] = tn(pe, do)
            else:
                tmp[tok:rows, :] += tn(dsl, qbd[b, :])
                out[tok:rows, :] += tn(pe, do)
        proj[tok:rows, :width] = latf[:, :width].astype(LOW)

        def one_pair(it):
            m, p = it // pairs, lax.rem(it, pairs)
            r = at(m * GROUP, GROUP)
            qc = at(p * 128, 128)
            q = proj[r, qc]
            k = proj[r, at(width + p * 128, 128)]
            v = proj[r, at(2 * width + p * 128, 128)]
            kl = proj[tok:rows, at(width + p * 128, 128)]
            vl = proj[tok:rows, at(2 * width + p * 128, 128)]
            dx = yb[r, qc]
            dq = jnp.zeros((GROUP, 128), F32)
            dk = tmp[r, qc]
            dv = out[r, qc]
            dkl = tmp[tok:rows, qc]
            dvl = out[tok:rows, qc]
            for e in (0, 1):
                qe = q * eighths[e]
                de = dx * halves[e]
                pt = probs[2 * it + e, 0:GROUP, :]
                pe = probs[2 * it + e, GROUP : GROUP + lat, :]
                pf = pt.astype(F32)
                pg = pe.astype(F32)
                dp = nt(v, de)
                dl = nt(vl, de)
                along = jnp.sum(pf * dp, axis=0, keepdims=True) + jnp.sum(
                    pg * dl, axis=0, keepdims=True
                )
                ds = (pf * (dp - along)).astype(LOW)
                dsl = (pg * (dl - along)).astype(LOW)
                dq += tn(ds, k * halves[e]) + tn(dsl, kl * halves[e])
                dk += nn(ds, qe)
                dkl += nn(dsl, qe)
                dv += nn(pt, de)
                dvl += nn(pe, de)
            proj[r, qc] = (dq * 0.125).astype(LOW)
            proj[r, at(width + p * 128, 128)] = dk.astype(LOW)
            proj[r, at(2 * width + p * 128, 128)] = dv.astype(LOW)
            tmp[tok:rows, qc] = dkl
            out[tok:rows, qc] = dvl

        def pair(i, carry):
            one_pair(2 * i)
            one_pair(2 * i + 1)
            return carry

        lax.fori_loop(0, half * pairs // 2, pair, 0)
        proj[tok:rows, width : 2 * width] = tmp[tok:rows, :].astype(LOW)
        proj[tok:rows, 2 * width :] = out[tok:rows, :].astype(LOW)

    @pl.when(second)
    def _():
        for m in range(half):
            r = slice(m * GROUP, (m + 1) * GROUP)
            b = slice(m * 128, (m + 1) * 128)
            pt = probs[m, 0:GROUP, 0:128]
            pf = pt.astype(F32)
            dx = yb[r, :]
            dp = nt(dx, vbd[b, :])
            ds = (pf * (dp - class_sum(pf * dp))).astype(LOW)
            dk = tn(ds, proj[r, :width])
            dv = tn(pt, dx)
            proj[r, :width] = (nn(ds, kbd[b, :]) * 0.125).astype(LOW)
            head_sum(latf, m * LAT, width, dk, 0.125, False)
            head_sum(latf, m * LAT, 2 * width, dv, 1.0, False)
        total = latf[:, width:] + kvg_send[me].astype(F32)
        for shift in range(1, n):
            kvg_copy(shift).wait_recv()
            total += kvg_recv[shift - 1].astype(F32)
        proj[tok:rows, width:] = total.astype(LOW)

    onward(1, 1)
    relaunch(3, False)

    @pl.when(first)
    def _():
        def to_in(c):
            tmp[:, c] = nt(proj[...], wq[c, :])

        tiles(width // 384, to_in, 384)

    @pl.when(second)
    def _():
        tmp[0:tok, :] = nt(proj[0:tok, :width], wq[:, :width])
        tmp[tok:rows, :] = nt(proj[tok:rows, :], wq[...])

    def in_back(r):
        hat, scale = normed_rows(xb[r, :].astype(F32))
        grad = tmp[r, :]
        gains[0, 0:8, :] += fold(grad * hat)
        total = ef[r, :] + norm_back(grad, hat, scale, gain_attn[...])
        low = total.astype(LOW)
        yb[r, :] = low
        out[r, :] = jnp.where(first, total, low.astype(F32))

    bands(in_back, 0, rows, third)
    for copy in grad_copies:
        copy.start()
    onward(2, 0)
    onward(1, 2)

    @pl.when(second)
    def _():
        backward_relay.start()

    def qkv_grad(start, count, r):
        weight_grad(
            lambda i, right, piece: (
                2 * wide + 1 + lax.rem(i * many + piece, 3),
                (i * many + piece) // 3,
            ),
            start,
            count,
            lambda i: proj[r, at(i * part, part)],
            lambda i: n1[r, :],
        )

    @pl.when(first)
    def _():
        qkv_grad(0, 3 * per_part, slice(0, rows))

    @pl.when(second)
    def _():
        qkv_grad(0, per_part, slice(0, rows))
        qkv_grad(per_part, 2 * per_part, slice(tok, rows))

    for pair in range(4, spread_pairs):
        launch(0, pair)
    start_own(4)

    def gain_copy(bit):
        return pltpu.make_async_remote_copy(
            src_ref=gains.at[bit],
            dst_ref=land_g.at[bit],
            send_sem=gain_s.at[bit],
            recv_sem=gain_r.at[bit],
            device_id=across(bit),
            device_id_type=MESH,
        )

    def gain_step(bit):
        gain_copy(bit).wait_recv()
        gains[bit + 1] = gains[bit] + land_g[bit]

    def each(lo, hi, phase):
        def one(i, carry):
            onward(phase, i)
            return carry

        lax.fori_loop(lo, hi, one, 0)

    gain_copy(0).start()
    onward(2, 1)
    onward(1, 3)
    relaunch(4)
    gain_step(0)
    gain_copy(1).start()
    each(0, 2, 3)
    each(2, 4, 2)
    relaunch(5, False)
    gain_step(1)
    gain_copy(2).start()
    each(4, 6, 1)
    each(2, 4, 3)
    gain_step(2)
    gain_copy(3).start()
    each(4, 6, 2)
    gain_step(3)
    each(4, 6, 3)
    final = gains[4]
    for i in (0, 1):
        whole_gain = jnp.sum(final[8 * i : 8 * i + 8], axis=0, keepdims=True)
        whole_gain = jnp.broadcast_to(whole_gain, (8, width))
        rolled = pltpu.roll(whole_gain, lax.rem(width - me * unit, width), 1)
        gain_sums[8 * i : 8 * i + 8, :] = rolled[:, 0:128]

    def finish(k, carry):
        for stream in (0, 1):
            for phase in range(4):
                copy_of(stream, phase, k).wait_send()
        return carry

    lax.fori_loop(0, spread_pairs, finish, 0)
    for bit in range(4):
        gain_copy(bit).wait_send()
    for copy in grad_copies:
        copy.wait()
    for stream in (0, 1):
        for pair in (spread_pairs - 2, spread_pairs - 1):
            leave(stream, pair).wait()

    @pl.when(second)
    def _():
        backward_relay.wait_send()
        for shift in range(1, n):
            kv_copy(shift, False).wait_send()
            kvg_copy(shift).wait_send()


def both_layers(n, tokens, latents, slots, images, gains, weights, d_tokens, d_latents):
    tok, width = tokens.shape
    lat = latents.shape[0]
    rows = tok + lat
    w_qkv, w_out, w_up, w_down = weights
    ff = w_up.shape[1]
    keys = n * lat
    half = lat // LAT
    size = sum(w.size for w in weights)
    chunks = size // (width * width)
    pairs = chunks // 2
    unit = width // n
    vm, hbm = pl.BlockSpec(memory_space=pltpu.VMEM), pl.BlockSpec(memory_space=pl.ANY)
    sm = pl.BlockSpec(memory_space=pltpu.SMEM)
    scratch = [
        pltpu.VMEM(w.shape, LOW) for w in (w_qkv, w_out, w_up, w_down)
    ] + [
        pltpu.VMEM(shape, dtype)
        for shape, dtype in (
            ((rows, width), LOW),
            ((rows, width), LOW),
            ((rows, 3 * width), LOW),
            ((rows, width), LOW),
            ((rows, width), F32),
            ((rows, width), LOW),
            ((rows, ff), LOW),
            ((rows, ff), LOW),
            ((rows, width), LOW),
            ((rows, width), LOW),
            ((rows, width), F32),
            ((rows, width), F32),
            ((rows, width), F32),
            ((half * width // 64, GROUP + lat, GROUP), LOW),
            ((half * 128, max(keys, GROUP + 128)), LOW),
            ((lat, 3 * width), F32),
            ((lat, width), F32),
            ((8, keys), F32),
            ((half * 128, width), LOW),
            ((half * 128, width), LOW),
            ((half * 256, width), LOW),
            ((n, lat, 2 * width), LOW),
            ((n, lat, 2 * width), LOW),
            ((n - 1, lat, 2 * width), LOW),
            ((2, 384 // unit, unit, width), LOW),
            ((5, 16, width), F32),
            ((2, 2, unit, width), F32),
            ((2, 2, 2, unit, width), LOW),
            ((2, 2, 2, unit, width), LOW),
            ((pairs, 2, 2, 2, unit, width), LOW),
            ((pairs, 2, 2, 2, unit, width), LOW),
            ((pairs, 2, 2, unit, width), LOW),
            ((pairs, 2, 2, unit, width), LOW),
            ((pairs, 2, unit, width), LOW),
            ((pairs, 2, unit, width), LOW),
            ((pairs, unit, width), LOW),
            ((pairs, unit, width), LOW),
            ((4, 16, width), F32),
        )
    ] + [
        pltpu.SemaphoreType.DMA((10,)),
        pltpu.SemaphoreType.DMA((2, 384 // unit)),
        pltpu.SemaphoreType.DMA((2,)),
        pltpu.SemaphoreType.DMA((2, 2)),
        pltpu.SemaphoreType.DMA((2, 4, pairs)),
        pltpu.SemaphoreType.DMA((2, 4, pairs)),
        pltpu.SemaphoreType.DMA((4,)),
        pltpu.SemaphoreType.DMA((4,)),
        pltpu.SemaphoreType.DMA((2,)),
        pltpu.SemaphoreType.DMA((2,)),
        pltpu.SemaphoreType.DMA((n - 1,)),
        pltpu.SemaphoreType.DMA((n - 1,)),
        pltpu.SemaphoreType.DMA((n - 1,)),
        pltpu.SemaphoreType.DMA((n - 1,)),
    ]
    return pl.pallas_call(
        functools.partial(layer_kernel, n),
        out_shape=(
            jax.ShapeDtypeStruct((tok, width), F32),
            jax.ShapeDtypeStruct((lat, width), F32),
            jax.ShapeDtypeStruct((tok, width), F32),
            jax.ShapeDtypeStruct((lat, width), F32),
            jax.ShapeDtypeStruct((chunks, 2, 2, 2, 2, unit, width), LOW),
            jax.ShapeDtypeStruct((chunks, unit, width), F32),
            jax.ShapeDtypeStruct((16, 128), F32),
        ),
        in_specs=[hbm, hbm, vm, sm, sm, vm, vm] + [hbm] * 6,
        out_specs=(hbm,) * 6 + (vm,),
        scratch_shapes=scratch,
        compiler_params=pltpu.CompilerParams(
            collective_id=1, has_side_effects=True, vmem_limit_bytes=63 * 1024 * 1024
        ),
        cost_estimate=pl.CostEstimate(
            flops=6 * rows * size, bytes_accessed=4 * size, transcendentals=0
        ),
    )(tokens, latents, slots, slots, images, *gains, *weights, d_tokens, d_latents)


def finish_kernel(width, *refs):
    rows_in, (summed, gains), rows_out = refs[0:4], refs[4:6], refs[6:10]
    gain_attn, g_qkv, g_out, gain_mlp, g_up, g_down = refs[10:16]
    held, (sem_in, sem_out) = refs[16:21], refs[21:23]
    wide = g_down.shape[1] // width
    unit = g_out.shape[1]
    loads = [
        pltpu.make_async_copy(src, dst, sem_in.at[i])
        for i, (src, dst) in enumerate(zip((*rows_in, summed), held))
    ]
    for load in loads:
        load.start()
    all_rows, sums = held[0:4], held[4]
    moves = [[pair] for pair in zip(all_rows, rows_out)] + [
        [(sums.at[c], g_down.at[:, c * width : (c + 1) * width]) for c in range(wide)]
        + [
            (sums.at[wide : 2 * wide], g_up),
            (sums.at[2 * wide : 2 * wide + 1], g_out),
            (sums.at[2 * wide + 1 :], g_qkv),
        ]
    ]
    gain_attn[...] = gains[0:1, 0:unit]
    gain_mlp[...] = gains[8:9, 0:unit]
    started = []
    for load, group in zip(loads, moves):
        load.wait()
        for src, dst in group:
            started.append(pltpu.make_async_copy(src, dst, sem_out.at[len(started)]))
            started[-1].start()
    for move in started:
        move.wait()


def finished(rows, summed, gains, wide):
    chunks, unit, width = summed.shape
    hbm, vm = pl.BlockSpec(memory_space=pl.ANY), pl.BlockSpec(memory_space=pltpu.VMEM)
    shapes = [r.shape for r in rows] + [
        (1, unit),
        (3, unit, width),
        (1, unit, width),
        (1, unit),
        (wide, unit, width),
        (unit, wide * width),
    ]
    return pl.pallas_call(
        functools.partial(finish_kernel, width),
        out_shape=tuple(jax.ShapeDtypeStruct(s, F32) for s in shapes),
        in_specs=[hbm] * 5 + [vm],
        out_specs=(hbm,) * 4 + (vm, hbm, hbm, vm, hbm, hbm),
        scratch_shapes=[pltpu.VMEM(x.shape, F32) for x in (*rows, summed)]
        + [pltpu.SemaphoreType.DMA((5,)), pltpu.SemaphoreType.DMA((7 + wide,))],
        compiler_params=pltpu.CompilerParams(vmem_limit_bytes=32 * 1024 * 1024),
    )(*rows, summed, gains)
def fused_shards(
    unused_grid,
    tokens,
    latents,
    slot_group,
    image_groups,
    gain_attn,
    w_qkv,
    w_out,
    gain_mlp,
    w_up,
    w_down,
    d_tokens,
    d_latents,
):
    micro, tok, width = tokens.shape
    lat = latents.shape[1]
    out_tok, out_lat, grad_tok, grad_lat, unused_grads, summed, gains = both_layers(
        slot_group.shape[1],
        tokens.reshape(micro * tok, width),
        latents.reshape(micro * lat, width),
        slot_group,
        image_groups,
        (gain_attn, gain_mlp),
        (w_qkv[0], w_out[0], w_up[0], w_down[0]),
        d_tokens.reshape(micro * tok, width),
        d_latents.reshape(micro * lat, width),
    )
    wide = w_up.shape[2] // width
    rows = (out_tok, out_lat, grad_tok, grad_lat)
    *rows, first_gain, qkv, out, second_gain, up, down = finished(rows, summed, gains, wide)
    return (
        rows[0].reshape(1, micro, tok, width),
        rows[1].reshape(1, micro, lat, width),
        rows[2].reshape(1, micro, tok, width),
        rows[3].reshape(1, micro, lat, width),
        first_gain,
        qkv.reshape(-1, width).T[None],
        out.reshape(-1, width).T[None],
        second_gain,
        up.reshape(-1, width).T[None],
        down.T[None],
    )

def solution(mesh):
    in_specs = (
        P(None, "dp", None),
        P(None, "dp", None),
        P(),
        P(),
        P("section", None),
        P("section", None, None),
        P("section", None, None),
        P("section", None),
        P("section", None, None),
        P("section", None, None),
        P(None, "dp", None),
        P(None, "dp", None),
    )
    out_specs = (
        P("section", None, "dp", None),
        P("section", None, "dp", None),
        P("section", None, "dp", None),
        P("section", None, "dp", None),
        P("section", "dp"),
        P("section", None, "dp"),
        P("section", None, "dp"),
        P("section", "dp"),
        P("section", None, "dp"),
        P("section", None, "dp"),
    )
    grid = grid_of(mesh)

    def program(*args):
        n, width = mesh.shape["dp"], args[0].shape[2]
        one_group = args[0].shape[1] == n * GROUP
        body = fused_shards if one_group and n == 16 and width % (16 * n) == 0 else shards
        return jax.shard_map(
            functools.partial(body, grid), mesh=mesh, in_specs=in_specs, out_specs=out_specs, check_vma=False
        )(*args)

    return program
```

```python
import functools

import jax
import jax.numpy as jnp
from jax import lax
from jax.experimental import pallas as pl
from jax.experimental.pallas import tpu as pltpu
from jax.sharding import PartitionSpec as P

HEADS = 12
GROUP = 256
LAT = 8


epsilon = 1e-05
masked_score = -1e30


MESH = pl.DeviceIdType.MESH


def grid_of(mesh):
    n = mesh.shape["dp"]
    coords = [getattr(d, "coords", None) for d in mesh.devices.reshape(n, -1)[:, 0]]
    if any(c is None for c in coords):
        return (n // 4, 2, 2) if n % 4 == 0 else (n, 1, 1)
    sizes = {a: len({c[a] for c in coords}) for a in range(3)}
    strides = {
        a: min([i for i in range(n) if coords[i][a] != coords[0][a]], default=n) for a in range(3)
    }
    order = sorted(range(3), key=lambda a: -strides[a])
    return tuple(sizes[a] for a in order)


def spread_kernel(grid, pairs, g_ref, gain_ref, out_ref, gout_ref, *scratch):
    acc = scratch[0:3]
    land = [scratch[3 + 3 * i : 6 + 3 * i] for i in range(3)]
    send_sem, recv_sem, own_sem = scratch[12:15]
    me = lax.axis_index("dp")
    section = lax.axis_index("section")
    l0, l1, l2 = grid
    here = (me // (l1 * l2), lax.rem(me // l2, l1), lax.rem(me, l2))

    def device(axis, shift):
        there = list(here)
        there[axis] = lax.rem(here[axis] + shift, grid[axis])
        return there[axis], ((there[0] * l1 + there[1]) * l2 + there[2], section)

    barrier = pltpu.get_barrier_semaphore()
    for axis in range(3):
        for shift in range(1, grid[axis]):
            pl.semaphore_signal(
                barrier, inc=1, device_id=device(axis, shift)[1], device_id_type=MESH
            )
    pl.semaphore_wait(barrier, sum(grid) - 3)

    orders = ((2, 1, 0), (1, 2, 0), (2, 1, 0))

    def source(stream, phase, k, at):
        if phase == 0:
            if stream == 0:
                return g_ref.at[2 * k, :, :, at]
            if stream == 1:
                return g_ref.at[2 * k + 1, :, at]
            return gain_ref.at[:, :, at]
        if phase == 1:
            return acc[stream].at[k, :, at]
        return acc[stream].at[k, at, here[orders[stream][1]]]

    def copies(stream, phase, k):
        axis = orders[stream][phase]
        for shift in range(1, grid[axis]):
            at, target = device(axis, shift)
            yield pltpu.make_async_remote_copy(
                src_ref=source(stream, phase, k, at),
                dst_ref=land[phase][stream].at[k, shift - 1],
                send_sem=send_sem.at[stream, phase, k, shift - 1],
                recv_sem=recv_sem.at[stream, phase, k, shift - 1],
                device_id=target,
                device_id_type=MESH,
            )

    def own(stream, k):
        return pltpu.make_async_copy(
            source(stream, 0, k, here[orders[stream][0]]), acc[stream].at[k], own_sem.at[stream, k]
        )

    def launch(stream, phase, k):
        for copy in copies(stream, phase, k):
            copy.start()

    def absorb(stream, phase, k):
        axis = orders[stream][phase]
        if phase == 0:
            own(stream, k).wait()
        for copy in copies(stream, phase, k):
            copy.wait_recv()
        into = land[phase][stream]
        count = grid[axis] - 1
        if phase == 0:
            for a in range(acc[stream].shape[1]):
                for b in range(acc[stream].shape[2]):
                    total = acc[stream][k, a, b].astype(jnp.float32)
                    for s in range(count):
                        total += into[k, s, a, b].astype(jnp.float32)
                    acc[stream][k, a, b] = total.astype(acc[stream].dtype)
        elif phase == 1:
            mine = here[axis]
            for a in range(acc[stream].shape[1]):
                total = acc[stream][k, a, mine].astype(jnp.float32)
                for s in range(count):
                    total += into[k, s, a].astype(jnp.float32)
                acc[stream][k, a, mine] = total.astype(acc[stream].dtype)
        else:
            total = acc[stream][k, here[0], here[orders[stream][1]]].astype(jnp.float32)
            for s in range(count):
                total += into[k, s].astype(jnp.float32)
            if stream < 2:
                out_ref[2 * k + stream] = total
            else:
                gout_ref[...] = total

    own(2, 0).start()
    launch(2, 0, 0)

    def start_own(k, carry):
        for stream in (0, 1):
            own(stream, k).start()
        return carry

    for stream in (0, 1):
        launch(stream, 0, 0)
    lax.fori_loop(0, pairs, start_own, 0)

    def turn(t, carry):
        @pl.when(t + 1 < pairs)
        def _():
            for stream in (0, 1):
                launch(stream, 0, t + 1)

        @pl.when(t < pairs)
        def _():
            for stream in (0, 1):
                absorb(stream, 0, t)
                launch(stream, 1, t)

        @pl.when((t >= 1) & (t - 1 < pairs))
        def _():
            for stream in (0, 1):
                absorb(stream, 1, t - 1)
                launch(stream, 2, t - 1)

        @pl.when(t >= 2)
        def _():
            for stream in (0, 1):
                absorb(stream, 2, t - 2)

        return carry

    lax.fori_loop(0, pairs + 2, turn, 0)
    absorb(2, 0, 0)
    launch(2, 1, 0)
    absorb(2, 1, 0)
    launch(2, 2, 0)
    absorb(2, 2, 0)

    def finish(k, carry):
        for stream in (0, 1):
            for phase in range(3):
                for copy in copies(stream, phase, k):
                    copy.wait_send()
        return carry

    lax.fori_loop(0, pairs, finish, 0)
    for phase in range(3):
        for copy in copies(2, phase, 0):
            copy.wait_send()


def spread(grid, grads, gains):
    chunks, n, rows, width = grads.shape
    pairs = chunks // 2
    l0, l1, l2 = grid
    most = max(max(grid) - 1, 1)
    low = jnp.bfloat16
    shapes = ((pairs, rows, width, low), (pairs, rows, width, low), (1, 8, 128, jnp.float32))
    inner = ((l1, l2), (l2, l1), (l1, l2))
    acc, first, second, third = [], [], [], []
    for (count, r, w, dt), (kept, sent) in zip(shapes, inner):
        acc.append(pltpu.VMEM((count, l0, kept, r, w), dt))
        first.append(pltpu.VMEM((count, max(sent - 1, 1), l0, kept, r, w), dt))
        second.append(pltpu.VMEM((count, max(kept - 1, 1), l0, r, w), dt))
        third.append(pltpu.VMEM((count, max(l0 - 1, 1), r, w), dt))
    return pl.pallas_call(
        functools.partial(spread_kernel, grid, pairs),
        out_shape=(
            jax.ShapeDtypeStruct((chunks, rows, width), jnp.float32),
            jax.ShapeDtypeStruct((8, 128), jnp.float32),
        ),
        in_specs=[pl.BlockSpec(memory_space=pl.ANY)] * 2,
        out_specs=(pl.BlockSpec(memory_space=pltpu.VMEM),) * 2,
        scratch_shapes=acc
        + first
        + second
        + third
        + [
            pltpu.SemaphoreType.DMA((3, 3, pairs, most)),
            pltpu.SemaphoreType.DMA((3, 3, pairs, most)),
            pltpu.SemaphoreType.DMA((3, pairs)),
        ],
        compiler_params=pltpu.CompilerParams(
            collective_id=0, has_side_effects=True, vmem_limit_bytes=60 * 1024 * 1024
        ),
        cost_estimate=pl.CostEstimate(flops=0, bytes_accessed=grads.size * 4, transcendentals=0),
    )(grads.reshape(chunks, l0, l1, l2, rows, width), gains.reshape(l0, l1, l2, 8, 128))


def from_behind(x, axis, by):
    devices = lax.axis_size(axis)
    pairs = [(i, i + by) for i in range(devices) if 0 <= i + by < devices]
    return lax.ppermute(x, axis, pairs)


def layer_norm(values, gain):
    row_mean = jnp.mean(values, axis=-1, keepdims=True)
    centred = values - row_mean
    row_var = jnp.mean(centred * centred, axis=-1, keepdims=True)
    return centred * lax.rsqrt(row_var + epsilon) * gain


def front_half(all_rows, gain_attn, w_qkv):
    normed = layer_norm(all_rows, gain_attn).astype(jnp.bfloat16)
    projected = jnp.dot(normed, w_qkv, preferred_element_type=jnp.float32).astype(jnp.bfloat16)
    return (normed, projected)


def latent_operand(projected, tok_rows, model_width):
    return projected[tok_rows:, model_width:]


def back_half(all_rows, projected, remote_rows, allowed, weights):
    gain_attn, w_qkv, w_out, gain_mlp, w_up, w_down = weights
    row_count, model_width = all_rows.shape
    head_size = model_width // HEADS
    remote_pairs = remote_rows[:, remote_rows.shape[1] - 2 * model_width :]
    queries = projected[:, :model_width].reshape(row_count, HEADS, head_size)
    key_rows = jnp.concatenate(
        [projected[:, model_width : 2 * model_width], remote_pairs[:, :model_width]], axis=0
    )
    value_rows = jnp.concatenate(
        [projected[:, 2 * model_width :], remote_pairs[:, model_width:]], axis=0
    )
    key_rows = key_rows.reshape(-1, HEADS, head_size)
    value_rows = value_rows.reshape(-1, HEADS, head_size)
    scores = jnp.einsum(
        "qhd,khd->hqk", queries, key_rows, preferred_element_type=jnp.float32
    ) * head_size ** (-0.5)
    attn_weights = jax.nn.softmax(jnp.where(allowed[None], scores, masked_score), axis=-1)
    attn_low = attn_weights.astype(jnp.bfloat16)
    mixed_low = jnp.einsum("hqk,khd->qhd", attn_low, value_rows, preferred_element_type=jnp.float32)
    mixed_low = mixed_low.reshape(row_count, model_width).astype(jnp.bfloat16)
    mid_rows = all_rows + jnp.dot(mixed_low, w_out, preferred_element_type=jnp.float32)
    normed_mlp = layer_norm(mid_rows, gain_mlp).astype(jnp.bfloat16)
    up_proj = jnp.dot(normed_mlp, w_up, preferred_element_type=jnp.float32)
    activated = jax.nn.gelu(up_proj).astype(jnp.bfloat16)
    result = mid_rows + jnp.dot(activated, w_down, preferred_element_type=jnp.float32)
    return dict(
        queries=queries,
        key_rows=key_rows,
        value_rows=value_rows,
        attn_weights=attn_weights,
        attn_low=attn_low,
        mixed_low=mixed_low,
        mid_rows=mid_rows,
        normed_mlp=normed_mlp,
        up_proj=up_proj,
        activated=activated,
        result=result,
    )


def section_backward(saved, d_result, all_rows, normed, allowed, weights, latent_start):
    gain_attn, w_qkv, w_out, gain_mlp, w_up, w_down = weights
    row_count, model_width = all_rows.shape
    head_size = model_width // HEADS
    score_scale = head_size ** (-0.5)
    d_low = d_result.astype(jnp.bfloat16)
    grad_down = jnp.dot(d_low.T, saved["activated"], preferred_element_type=jnp.float32)
    d_activated = jnp.dot(d_low, w_down.T, preferred_element_type=jnp.float32)
    unused_up, gelu_back = jax.vjp(jax.nn.gelu, saved["up_proj"])
    d_up = gelu_back(d_activated)[0].astype(jnp.bfloat16)
    grad_up = jnp.dot(d_up.T, saved["normed_mlp"], preferred_element_type=jnp.float32)
    d_normed_mlp = jnp.dot(d_up, w_up.T, preferred_element_type=jnp.float32)
    unused_mid, second_back = jax.vjp(layer_norm, saved["mid_rows"], gain_mlp)
    d_mid_norm, grad_gain_mlp = second_back(d_normed_mlp)
    d_mid = d_result + d_mid_norm
    d_mid_low = d_mid.astype(jnp.bfloat16)
    grad_out = jnp.dot(d_mid_low.T, saved["mixed_low"], preferred_element_type=jnp.float32)
    d_mixed = jnp.dot(d_mid_low, w_out.T, preferred_element_type=jnp.float32).astype(jnp.bfloat16)
    d_mixed = d_mixed.reshape(row_count, HEADS, head_size)
    d_weights = jnp.einsum(
        "qhd,khd->hqk", d_mixed, saved["value_rows"], preferred_element_type=jnp.float32
    )
    d_values = jnp.einsum(
        "hqk,qhd->khd", saved["attn_low"], d_mixed, preferred_element_type=jnp.float32
    )
    attn_weights = saved["attn_weights"]
    d_scores = attn_weights * (
        d_weights - jnp.sum(attn_weights * d_weights, axis=-1, keepdims=True)
    )
    d_scores_low = jnp.where(allowed[None], d_scores, 0.0).astype(jnp.bfloat16)
    d_queries = (
        jnp.einsum(
            "hqk,khd->qhd", d_scores_low, saved["key_rows"], preferred_element_type=jnp.float32
        )
        * score_scale
    )
    d_keys = (
        jnp.einsum(
            "hqk,qhd->khd", d_scores_low, saved["queries"], preferred_element_type=jnp.float32
        )
        * score_scale
    )
    remote_part = jnp.concatenate(
        [
            d_keys[row_count:].reshape(-1, model_width),
            d_values[row_count:].reshape(-1, model_width),
        ],
        axis=1,
    )
    own_part = lax.psum_scatter(remote_part, "dp", scatter_dimension=0, tiled=True)
    local_pairs = jnp.concatenate(
        [
            d_keys[:row_count].reshape(row_count, model_width),
            d_values[:row_count].reshape(row_count, model_width),
        ],
        axis=1,
    )
    local_pairs = jnp.concatenate(
        [local_pairs[:latent_start], local_pairs[latent_start:] + own_part], axis=0
    )
    d_projected = jnp.concatenate(
        [d_queries.reshape(row_count, model_width), local_pairs], axis=1
    ).astype(jnp.bfloat16)
    grad_qkv = jnp.dot(d_projected.T, normed, preferred_element_type=jnp.float32)
    d_normed = jnp.dot(d_projected, w_qkv.T, preferred_element_type=jnp.float32)
    unused_rows, first_back = jax.vjp(layer_norm, all_rows, gain_attn)
    d_rows_norm, grad_gain_attn = first_back(d_normed)
    return (
        d_mid + d_rows_norm,
        (grad_gain_attn, grad_qkv, grad_out, grad_gain_mlp, grad_up, grad_down),
    )


def packed(grads, n):
    gain_first, qkv_grad, out_grad, gain_second, up_grad, down_grad = grads
    width = out_grad.shape[0]
    rows = width // n

    def by_rows(grad):
        return grad.reshape(n, -1, rows, width).transpose(1, 0, 2, 3).astype(jnp.bfloat16)

    down = down_grad.reshape(n, rows, -1, width).transpose(2, 0, 1, 3).astype(jnp.bfloat16)
    chunks = jnp.concatenate([down, by_rows(up_grad), by_rows(out_grad), by_rows(qkv_grad)], axis=0)
    gains = jnp.stack([gain_first.reshape(n, rows), gain_second.reshape(n, rows)], axis=1)
    return chunks, jnp.pad(gains, ((0, 0), (0, 6), (0, 128 - rows)))


def shards(
    grid,
    tokens,
    latents,
    slot_group,
    image_groups,
    gain_attn,
    w_qkv,
    w_out,
    gain_mlp,
    w_up,
    w_down,
    d_tokens,
    d_latents,
):
    micro = tokens.shape[0]
    tok_rows = tokens.shape[1]
    lat_rows = latents.shape[1]
    model_width = tokens.shape[2]
    local_groups = tok_rows // GROUP
    section_index = lax.axis_index("section")
    is_global = section_index == 1
    dp_index = lax.axis_index("dp")
    weights = (gain_attn[0], w_qkv[0], w_out[0], gain_mlp[0], w_up[0], w_down[0])
    image_ends = jnp.cumsum(image_groups, axis=1)
    slot_images = jnp.sum(
        (image_ends[:, None, :] <= slot_group[:, :, None]).astype(jnp.int32), axis=2
    )
    slot_total = slot_group.shape[1]
    row_group = jnp.concatenate([jnp.arange(tok_rows) // GROUP, jnp.arange(lat_rows) // LAT])
    row_latent = jnp.concatenate(
        [jnp.zeros((tok_rows,), jnp.bool_), jnp.ones((lat_rows,), jnp.bool_)]
    )
    same_group = row_group[:, None] == row_group[None, :]
    local_mask = jnp.where(
        is_global, (~row_latent)[:, None] & row_latent[None, :] & same_group, same_group
    )
    group_match = row_group[:, None] == jnp.arange(local_groups)[None, :]

    def key_images(batch):
        images_row = lax.dynamic_index_in_dim(slot_images, batch, 0, keepdims=False)
        return (images_row, jnp.broadcast_to(images_row[:, None], (slot_total, LAT)).reshape(-1))

    def allowed_for(batch):
        images_row, key_image = key_images(batch)
        own_images = lax.dynamic_slice_in_dim(images_row, dp_index * local_groups, local_groups)
        row_image = jnp.sum(jnp.where(group_match, own_images[None, :], 0), axis=1)
        remote_mask = is_global & row_latent[:, None] & (row_image[:, None] == key_image[None, :])
        return jnp.concatenate([local_mask, remote_mask], axis=1)

    def forward_turn(received, turn):
        recv_tokens, recv_latents = received
        batch = jnp.clip(turn - section_index, 0, micro - 1)
        own_tok = lax.dynamic_index_in_dim(tokens, batch, 0, keepdims=False)
        own_lat = lax.dynamic_index_in_dim(latents, batch, 0, keepdims=False)
        input_rows = jnp.concatenate(
            [
                jnp.where(is_global, recv_tokens, own_tok),
                jnp.where(is_global, recv_latents, own_lat),
            ],
            axis=0,
        )
        all_rows = input_rows.astype(jnp.float32)
        normed, projected = front_half(all_rows, weights[0], weights[1])
        remote_rows = lax.all_gather(
            latent_operand(projected, tok_rows, model_width), "dp", axis=0, tiled=True
        )
        saved = back_half(all_rows, projected, remote_rows, allowed_for(batch), weights)
        result = saved["result"]
        result_low = result.astype(jnp.bfloat16)
        stored = jnp.where(is_global, result, result_low.astype(jnp.float32))
        passed_on = from_behind((result_low[:tok_rows], result_low[tok_rows:]), "section", 1)
        return passed_on, (input_rows, stored[:tok_rows], stored[tok_rows:])

    nothing = (
        jnp.zeros((tok_rows, model_width), jnp.bfloat16),
        jnp.zeros((lat_rows, model_width), jnp.bfloat16),
    )
    turns = jnp.arange(micro + 1)
    unused_end, (kept_rows, tok_outputs, lat_outputs) = lax.scan(forward_turn, nothing, turns)

    def backward_turn(carry, turn):
        (recv_grad_tok, recv_grad_lat), totals = carry
        raw_batch = micro - turn - section_index
        valid = ((raw_batch >= 0) & (raw_batch < micro)).astype(jnp.float32)
        batch = jnp.clip(raw_batch, 0, micro - 1)
        all_rows = lax.dynamic_index_in_dim(
            kept_rows, batch + section_index, 0, keepdims=False
        ).astype(jnp.float32)
        normed, projected = front_half(all_rows, weights[0], weights[1])
        remote_rows = lax.all_gather(
            latent_operand(projected, tok_rows, model_width), "dp", axis=0, tiled=True
        )
        allowed = allowed_for(batch)
        saved = back_half(all_rows, projected, remote_rows, allowed, weights)
        given = (
            jnp.concatenate(
                [
                    lax.dynamic_index_in_dim(d_tokens, batch, 0, keepdims=False),
                    lax.dynamic_index_in_dim(d_latents, batch, 0, keepdims=False),
                ],
                axis=0,
            )
            * valid
        )
        passed = jnp.concatenate([recv_grad_tok, recv_grad_lat], axis=0).astype(jnp.float32)
        d_result = jnp.where(is_global, given, passed)
        d_rows, grads = section_backward(
            saved, d_result, all_rows, normed, allowed, weights, tok_rows
        )
        totals = tuple((accum + piece for accum, piece in zip(totals, grads)))
        d_rows_low = d_rows.astype(jnp.bfloat16)
        stored = jnp.where(is_global, d_rows_low.astype(jnp.float32), d_rows)
        sent = from_behind((d_rows_low[:tok_rows], d_rows_low[tok_rows:]), "section", -1)
        return (sent, totals), (stored[:tok_rows], stored[tok_rows:])

    totals = tuple(
        jnp.zeros(w.shape[::-1] if w.ndim == 2 else w.shape, jnp.float32) for w in weights
    )
    (unused_sent, totals), (tok_grads, lat_grads) = lax.scan(
        backward_turn, (nothing, totals), turns
    )
    chunks, gains = packed(totals, lax.axis_size("dp"))
    summed, gain_sums = spread(grid, chunks, gains)
    rows = summed.shape[1]
    layer_tokens = lax.dynamic_slice_in_dim(tok_outputs, section_index, micro, 0)[None]
    layer_latents = lax.dynamic_slice_in_dim(lat_outputs, section_index, micro, 0)[None]
    grad_tokens = lax.dynamic_slice_in_dim(tok_grads, 1 - section_index, micro, 0)[::-1][
        None
    ]
    grad_latents = lax.dynamic_slice_in_dim(lat_grads, 1 - section_index, micro, 0)[
        ::-1
    ][None]
    return (
        layer_tokens,
        layer_latents,
        grad_tokens,
        grad_latents,
        gain_sums[0:1, :rows],
        summed[9:].reshape(-1, model_width).T[None],
        summed[8].T[None],
        gain_sums[1:2, :rows],
        summed[4:8].reshape(-1, model_width).T[None],
        summed[0:4].transpose(0, 2, 1).reshape(-1, rows)[None],
    )


F32 = jnp.float32
LOW = jnp.bfloat16
HEAD_PAD = 16
TILE = 768


def nn(a, b):
    return jnp.dot(a, b, preferred_element_type=F32)


def nt(a, b):
    return lax.dot_general(a, b, (((1,), (1,)), ((), ())), preferred_element_type=F32)


def tn(a, b):
    return lax.dot_general(a, b, (((0,), (0,)), ((), ())), preferred_element_type=F32)


def row_mean(values):
    return jnp.mean(values, axis=-1, keepdims=True)


def row_stats(load, spans):
    means = [row_mean(load(r)) for r in spans]
    scales = []
    for r, mean in zip(spans, means):
        centred = load(r) - mean
        scales.append(lax.rsqrt(row_mean(centred * centred) + epsilon))
    return means, scales


def at(start, size):
    return pl.ds(pl.multiple_of(start, size), size)


def class_max(s):
    for by in (16, 32, 64):
        s = jnp.maximum(s, pltpu.roll(s, by, 1))
    return s


def class_sum(s):
    for by in (16, 32, 64):
        s = s + pltpu.roll(s, by, 1)
    return s


def layer_kernel(
    n,
    tokens,
    latents,
    slots,
    slot_at,
    image_at,
    gain_attn,
    gain_mlp,
    w_qkv,
    w_out,
    w_up,
    w_down,
    d_tokens,
    d_latents,
    out_tok,
    out_lat,
    grad_tok,
    grad_lat,
    grads,
    summed,
    gain_sums,
    wq,
    wo,
    wu,
    wd,
    xb,
    n1,
    proj,
    mixed,
    mid,
    n2,
    act,
    dup,
    yb,
    dy,
    ef,
    tmp,
    out,
    probs,
    probs_lat,
    scores,
    slopes,
    latf,
    mixf,
    key_mask,
    qbd,
    kbd,
    vbd,
    kv_all,
    kvg_send,
    kvg_recv,
    stage,
    gains,
    leaving,
    own_a,
    own_b,
    land1_a,
    land1_b,
    land2_a,
    land2_b,
    land3_a,
    land3_b,
    land4_a,
    land4_b,
    land_g,
    load_sem,
    stage_sem,
    own_sem,
    leave_sem,
    send_sem,
    recv_sem,
    gain_s,
    gain_r,
    relay_send,
    relay_recv,
    kv_sem_s,
    kv_sem_r,
    kvg_sem_s,
    kvg_sem_r,
):
    rows, width = xb.shape
    ff = act.shape[1]
    tok = tokens.shape[0]
    lat = latents.shape[0]
    half = lat // LAT
    pairs = width // 128
    me = lax.axis_index("dp")
    section = lax.axis_index("section")
    first = section == 0
    second = section == 1
    partner = (me, 1 - section)

    loads = [
        pltpu.make_async_copy(src, dst, load_sem.at[i])
        for i, (src, dst) in enumerate(((w_qkv, wq), (w_out, wo), (w_up, wu), (w_down, wd)))
    ]
    x_loads = [
        pltpu.make_async_copy(tokens, xb.at[0:tok], load_sem.at[4]),
        pltpu.make_async_copy(latents, xb.at[tok:rows], load_sem.at[5]),
    ]
    e_loads = [
        pltpu.make_async_copy(d_tokens, ef.at[0:tok], load_sem.at[6]),
        pltpu.make_async_copy(d_latents, ef.at[tok:rows], load_sem.at[7]),
    ]

    @pl.when(first)
    def _():
        for copy in x_loads:
            copy.start()

    for copy in loads:
        copy.start()

    @pl.when(second)
    def _():
        for copy in e_loads:
            copy.start()

    barrier = pltpu.get_barrier_semaphore()
    pl.semaphore_signal(barrier, inc=1, device_id=partner, device_id_type=MESH)

    here = [lax.rem(me // (1 << bit), 2) for bit in range(4)]

    def across(bit):
        return (me + (1 - 2 * here[bit]) * (1 << bit), section)

    @pl.when(second)
    def _():
        for shift in range(1, n):
            pl.semaphore_signal(
                barrier, inc=1, device_id=(lax.rem(me + shift, n), section), device_id_type=MESH
            )
        pl.semaphore_wait(barrier, n)

    @pl.when(first)
    def _():
        for bit in range(4):
            pl.semaphore_signal(barrier, inc=1, device_id=across(bit), device_id_type=MESH)
        pl.semaphore_wait(barrier, 5)

    forward_relay = pltpu.make_async_remote_copy(
        src_ref=yb, dst_ref=xb, send_sem=relay_send.at[0], recv_sem=relay_recv.at[0],
        device_id=partner, device_id_type=MESH,
    )
    backward_relay = pltpu.make_async_remote_copy(
        src_ref=yb, dst_ref=dy, send_sem=relay_send.at[1], recv_sem=relay_recv.at[1],
        device_id=partner, device_id_type=MESH,
    )

    def kv_copy(shift, incoming):
        slot = lax.rem(me + n - shift, n) if incoming else me
        return pltpu.make_async_remote_copy(
            src_ref=kv_all.at[me], dst_ref=kv_all.at[slot],
            send_sem=kv_sem_s.at[shift - 1], recv_sem=kv_sem_r.at[shift - 1],
            device_id=(lax.rem(me + shift, n), section), device_id_type=MESH,
        )

    def kvg_copy(shift):
        there = lax.rem(me + shift, n)
        return pltpu.make_async_remote_copy(
            src_ref=kvg_send.at[there], dst_ref=kvg_recv.at[shift - 1],
            send_sem=kvg_sem_s.at[shift - 1], recv_sem=kvg_sem_r.at[shift - 1],
            device_id=(there, section), device_id_type=MESH,
        )

    chunks = [slice(c, c + 64) for c in range(0, GROUP, 64)]
    lane = lax.broadcasted_iota(jnp.int32, (1, 128), 1)
    halves = [(lane < 64).astype(F32).astype(LOW), (lane >= 64).astype(F32).astype(LOW)]
    eighths = [(h.astype(F32) * 0.125).astype(LOW) for h in halves]
    heads = (
        lax.broadcasted_iota(jnp.int32, (HEAD_PAD, width), 1) // 64
        == lax.broadcasted_iota(jnp.int32, (HEAD_PAD, width), 0)
    ).astype(F32)

    def block_diagonal(dst, base, src, row, column, scale):
        for i in range(LAT):
            line = src[row + i : row + i + 1, column : column + width] * scale
            dst[base + i * HEAD_PAD : base + (i + 1) * HEAD_PAD, :] = (line * heads).astype(LOW)

    def head_sum(dst, row, column, value, scale, add):
        for i in range(LAT):
            line = jnp.sum(
                value[i * HEAD_PAD : (i + 1) * HEAD_PAD] * heads, axis=0, keepdims=True
            )
            line = line * scale
            if add:
                line = line + dst[row + i : row + i + 1, column : column + width]
            dst[row + i : row + i + 1, column : column + width] = line

    def bands(body, lo, hi, size):
        def one(i, carry):
            body(pl.ds(pl.multiple_of(lo + i * size, 16), size))
            return carry

        lax.fori_loop(0, (hi - lo) // size, one, 0)

    third = rows // 3

    def grouped(body, lo, hi, count):
        def one(i, carry):
            base = lo + i * 16 * count
            body([pl.ds(pl.multiple_of(base + 16 * g, 16), 16) for g in range(count)])
            return carry

        lax.fori_loop(0, (hi - lo) // (16 * count), one, 0)

    def norm(load, gain, dst, lo, hi, count):
        def body(spans):
            means, scales = row_stats(load, spans)
            for r, mean, scale in zip(spans, means, scales):
                dst[r, :] = ((load(r) - mean) * scale * gain[...]).astype(LOW)

        grouped(body, lo, hi, count)

    def norm_back(load, grad, gain, gain_rows, store, lo, hi, count):
        def body(spans):
            means, scales = row_stats(load, spans)
            firsts, seconds = [], []
            kept = gains[0, gain_rows, :]
            for r, mean, scale in zip(spans, means, scales):
                along = grad[r, :] * ((load(r) - mean) * scale)
                kept = kept + along[0:8] + along[8:16]
                firsts.append(row_mean(grad[r, :] * gain[...]))
                seconds.append(row_mean(along * gain[...]))
            gains[0, gain_rows, :] = kept
            for r, mean, scale, one, two in zip(spans, means, scales, firsts, seconds):
                hat = (load(r) - mean) * scale
                store(r, ef[r, :] + scale * (grad[r, :] * gain[...] - one - hat * two))

        grouped(body, lo, hi, count)

    def tiles(count, body, size=TILE):
        def one(i, carry):
            body(at(i * size, size))
            return carry

        lax.fori_loop(0, count, one, 0)

    @pl.when(first)
    def _():
        for copy in x_loads:
            copy.wait()

    @pl.when(second)
    def _():
        spots = lax.broadcasted_iota(jnp.int32, (n, n * lat), 1) // lat
        spread_out = (spots == lax.broadcasted_iota(jnp.int32, (n, n * lat), 0)).astype(F32)
        groups = nn(slots[...].astype(F32).astype(LOW), spread_out.astype(LOW))
        of_micro = lax.rem(lax.broadcasted_iota(jnp.int32, (1, n * lat), 1), lat) // LAT
        for m in range(half):
            images = jnp.zeros((1, n * lat), F32)
            own_image = jnp.float32(0)
            end = jnp.int32(0)
            for i in range(image_at.shape[1]):
                end = end + image_at[m, i]
                images += jnp.where(end.astype(F32) <= groups[m : m + 1], 1.0, 0.0)
                own_image += jnp.where(end <= slot_at[m, me], 1.0, 0.0)
            seen = (images == own_image) & (of_micro == m)
            key_mask[m : m + 1, :] = jnp.where(seen, 0.0, masked_score)
        forward_relay.wait_recv()

    def load_in(r):
        return xb[r, :].astype(F32)

    def load_mid(r):
        return mid[r, :]

    norm(load_in, gain_attn, n1, 0, rows, 11)
    loads[0].wait()

    @pl.when(second)
    def _():
        own = nn(n1[tok:rows, :], wq[:, width:]).astype(LOW)
        kv_all[me] = own
        latf[:, width:] = own.astype(F32)
        for shift in range(1, n):
            kv_copy(shift, False).start()

    def project(c):
        proj[:, c] = nn(n1[...], wq[:, c]).astype(LOW)

    per = width // TILE
    tiles(jnp.where(first, 3 * per, per), project)

    def lat_bias(m, shape, axis):
        return jnp.where(
            lax.broadcasted_iota(jnp.int32, shape, axis) // LAT == m, 0.0, masked_score
        ).astype(F32)

    @pl.when(first)
    def _():
        latf[...] = proj[tok:rows, :].astype(F32)

        def one_pair(it, side):
            m, p = it // pairs, lax.rem(it, pairs)
            r = at(m * GROUP, GROUP)
            q = proj[r, at(p * 128, 128)]
            k = proj[r, at(width + p * 128, 128)]
            v = proj[r, at(2 * width + p * 128, 128)]
            kl = proj[tok:rows, at(width + p * 128, 128)]
            vl = proj[tok:rows, at(2 * width + p * 128, 128)]
            bias = lat_bias(m, (lat, GROUP), 0)
            total = jnp.zeros((GROUP, 128), F32)
            for e in (0, 1):
                qe = q * eighths[e]
                s = scores.at[2 * side + e]
                s[...] = nt(k, qe)
                sl = nt(kl, qe) + bias
                top = jnp.max(sl, axis=0, keepdims=True)
                for c in chunks:
                    top = jnp.maximum(top, jnp.max(s[c, :], axis=0, keepdims=True))
                el = jnp.exp(sl - top)
                whole_sum = jnp.sum(el, axis=0, keepdims=True)
                for c in chunks:
                    et = jnp.exp(s[c, :] - top)
                    s[c, :] = et
                    whole_sum += jnp.sum(et, axis=0, keepdims=True)
                scale = 1.0 / whole_sum
                for c in chunks:
                    probs[2 * it + e, c, :] = (s[c, :] * scale).astype(LOW)
                pe = (el * scale).astype(LOW)
                probs[2 * it + e, GROUP : GROUP + lat, :] = pe
                total += tn(probs[2 * it + e, 0:GROUP, :], v * halves[e])
                total += tn(pe, vl * halves[e])
            mixed[r, at(p * 128, 128)] = total.astype(LOW)

        def pair(i, carry):
            one_pair(2 * i, 0)
            one_pair(2 * i + 1, 1)
            return carry

        lax.fori_loop(0, half * pairs // 2, pair, 0)
        for m in range(half):
            r = slice(m * GROUP, (m + 1) * GROUP)
            b = slice(m * 128, (m + 1) * 128)
            block_diagonal(qbd, m * 128, latf, m * LAT, 0, 0.125)
            s = nt(qbd[b, :], proj[r, width : 2 * width])
            sl = nt(qbd[b, :], proj[tok:rows, width : 2 * width]) + lat_bias(m, (128, lat), 1)
            top = jnp.maximum(
                jnp.max(s, axis=1, keepdims=True), jnp.max(sl, axis=1, keepdims=True)
            )
            et = jnp.exp(s - top)
            el = jnp.exp(sl - top)
            scale = 1.0 / (
                jnp.sum(et, axis=1, keepdims=True) + jnp.sum(el, axis=1, keepdims=True)
            )
            pt = (et * scale).astype(LOW)
            pe = (el * scale).astype(LOW)
            probs_lat[b, 0:GROUP] = pt
            probs_lat[b, GROUP : GROUP + lat] = pe
            o = nn(pt, proj[r, 2 * width :]) + nn(pe, proj[tok:rows, 2 * width :])
            head_sum(mixf, m * LAT, 0, o, 1.0, False)
        mixed[tok:rows, :] = mixf[...].astype(LOW)

    keys = n * lat

    @pl.when(second)
    def _():
        latf[:, :width] = proj[tok:rows, :width].astype(F32)
        for m in range(half):
            r = slice(m * GROUP, (m + 1) * GROUP)
            b = slice(m * 128, (m + 1) * 128)
            block_diagonal(qbd, m * 128, latf, m * LAT, 0, 0.125)
            block_diagonal(kbd, m * 128, latf, m * LAT, width, 1.0)
            block_diagonal(vbd, m * 128, latf, m * LAT, 2 * width, 1.0)
            s = nt(proj[r, :width] * jnp.asarray(0.125, LOW), kbd[b, :])
            et = jnp.exp(s - class_max(s))
            pt = (et / class_sum(et)).astype(LOW)
            probs[m, 0:GROUP, 0:128] = pt
            mixed[r, :] = nn(pt, vbd[b, :]).astype(LOW)

    root = 0.7978845608028654

    def mlp_in(lo, hi, count):
        r0 = slice(lo, hi)
        mid[r0, :] = xb[r0, :].astype(F32) + nn(mixed[r0, :], wo[...])

        norm(load_mid, gain_mlp, n2, lo, hi, count)

        def widen(i, carry):
            c = at(i * 512, 512)
            tmp[r0, 0:512] = nn(n2[r0, :], wu[:, c])

            def gelu(spans):
                for r in spans:
                    up = tmp[r, 0:512]
                    square = up * up
                    t = jnp.tanh(up * (root + (root * 0.044715) * square))
                    gate = 0.5 + 0.5 * t
                    value = up * gate
                    slope = gate + (value + value) * (1.0 - gate) * (
                        root + (3.0 * root * 0.044715) * square
                    )
                    act[r, c] = value.astype(LOW)
                    dup[r, c] = slope.astype(LOW)

            grouped(gelu, lo, hi, count)
            return carry

        lax.fori_loop(0, ff // 512, widen, 0)

    for copy in loads[1:]:
        copy.wait()

    @pl.when(first)
    def _():
        mlp_in(0, rows, 11)

    @pl.when(second)
    def _():
        mlp_in(0, tok, 8)
        for shift in range(1, n):
            kv_copy(shift, True).wait_recv()
        k = kv_all[:, :, :width].reshape(keys, width)
        v = kv_all[:, :, width:].reshape(keys, width)
        for m in range(half):
            b = slice(m * 128, (m + 1) * 128)
            s = nt(qbd[b, :], k) + key_mask[m : m + 1, :]
            et = jnp.exp(s - jnp.max(s, axis=1, keepdims=True))
            pt = (et / jnp.sum(et, axis=1, keepdims=True)).astype(LOW)
            probs_lat[b, 0:keys] = pt
            head_sum(mixf, m * LAT, 0, nn(pt, v), 1.0, False)
        mixed[tok:rows, :] = mixf[...].astype(LOW)

        mlp_in(tok, rows, 1)

    out_copies = [
        pltpu.make_async_copy(out.at[0:tok], out_tok, load_sem.at[8]),
        pltpu.make_async_copy(out.at[tok:rows], out_lat, load_sem.at[9]),
    ]
    grad_copies = [
        pltpu.make_async_copy(out.at[0:tok], grad_tok, load_sem.at[8]),
        pltpu.make_async_copy(out.at[tok:rows], grad_lat, load_sem.at[9]),
    ]

    def layer_output(passed_on):
        def narrow(c):
            y = mid[:, c] + nn(act[...], wd[:, c])
            if passed_on:
                low = y.astype(LOW)
                yb[:, c] = low
                y = low.astype(F32)
            out[:, c] = y

        tiles(width // 256, narrow, 256)
        for copy in out_copies:
            copy.start()

    @pl.when(first)
    def _():
        layer_output(True)
        forward_relay.start()
        backward_relay.wait_recv()

        def widen_e(r):
            ef[r, :] = dy[r, :].astype(F32)

        bands(widen_e, 0, rows, third)

    @pl.when(second)
    def _():
        for copy in e_loads:
            copy.wait()

        def narrow_e(r):
            dy[r, :] = ef[r, :].astype(LOW)

        bands(narrow_e, 0, rows, third)

    part = 384
    unit = width // n
    many = part // unit

    def staged(slot, piece, chunk, share):
        return pltpu.make_async_copy(
            stage.at[slot, piece],
            grads.at[
                chunk,
                share // 8,
                lax.rem(share // 4, 2),
                lax.rem(share // 2, 2),
                lax.rem(share, 2),
            ],
            stage_sem.at[slot, piece],
        )

    def drain(slot):
        def one(piece, carry):
            staged(slot, piece, 0, 0).wait()
            return carry

        lax.fori_loop(0, many, one, 0)

    def weight_grad(place, start, count, left, *rights):
        def one(i, carry):
            turned = left(i).T
            for at_right, right in enumerate(rights):
                tile = i * len(rights) + at_right
                slot = lax.rem(tile, 2)
                value = nn(turned, right(i)).astype(LOW)

                @pl.when(tile >= start * len(rights) + 2)
                def _():
                    drain(slot)

                for piece in range(many):
                    stage[slot, piece] = value[piece * unit : (piece + 1) * unit]
                    staged(slot, piece, *place(i, at_right, piece)).start()
            return carry

        lax.fori_loop(start, start + count, one, 0)
        for slot in (0, 1):
            drain(slot)

    orders = ((0, 2, 1, 3), (1, 2, 0, 3))
    own_buf = (own_a, own_b)
    land = (
        (land1_a, land1_b),
        (land2_a, land2_b),
        (land3_a, land3_b),
        (land4_a, land4_b),
    )
    spread_pairs = land1_a.shape[0]

    def source(stream, phase, k, theirs):
        pick = [(1 - here[bit]) if theirs else here[bit] for bit in orders[stream]]
        own_bit = [here[bit] for bit in orders[stream]]
        base = land[0][stream]
        if phase == 0:
            if stream == 0:
                return grads.at[2 * k, :, :, :, pick[0]]
            return grads.at[2 * k + 1, :, :, pick[0]]
        if phase == 1:
            return base.at[k, :, pick[1]]
        if phase == 2:
            return base.at[k, :, own_bit[1], pick[2]]
        return base.at[k, pick[3], own_bit[1], own_bit[2]]

    def copy_of(stream, phase, k):
        return pltpu.make_async_remote_copy(
            src_ref=source(stream, phase, k, True),
            dst_ref=land[phase][stream].at[k],
            send_sem=send_sem.at[stream, phase, k],
            recv_sem=recv_sem.at[stream, phase, k],
            device_id=across(orders[stream][phase]),
            device_id_type=MESH,
        )

    def own(stream, k):
        return pltpu.make_async_copy(
            source(stream, 0, k, False), own_buf[stream], own_sem.at[stream]
        )

    def leave(stream, k):
        slot = lax.rem(k, 2)
        return pltpu.make_async_copy(
            leaving.at[slot, stream], summed.at[2 * k + stream], leave_sem.at[slot, stream]
        )

    def launch(phase, k):
        for stream in (0, 1):
            copy_of(stream, phase, k).start()

    def absorb(phase, k):
        for stream in (0, 1):
            if phase == 0:
                own(stream, k).wait()
            copy_of(stream, phase, k).wait_recv()
            base, into = land[0][stream], land[phase][stream]
            mine = [here[bit] for bit in orders[stream]]
            if phase == 0:

                def add(i, carry):
                    for j in (0, 1):
                        for h in (0, 1):
                            total = own_buf[stream][i, j, h].astype(F32)
                            total += base[k, i, j, h].astype(F32)
                            base[k, i, j, h] = total.astype(LOW)
                    return carry

                lax.fori_loop(0, 2, add, 0)
            elif phase == 1:
                for i in (0, 1):
                    for h in (0, 1):
                        total = base[k, i, mine[1], h].astype(F32)
                        total += into[k, i, h].astype(F32)
                        base[k, i, mine[1], h] = total.astype(LOW)
            elif phase == 2:
                for i in (0, 1):
                    total = base[k, i, mine[1], mine[2]].astype(F32)
                    total += into[k, i].astype(F32)
                    base[k, i, mine[1], mine[2]] = total.astype(LOW)
            else:
                total = base[k, mine[3], mine[1], mine[2]].astype(F32)
                total += into[k].astype(F32)
                slot = lax.rem(k, 2)

                @pl.when(k >= 2)
                def _():
                    leave(stream, k - 2).wait()

                leaving[slot, stream] = total
                leave(stream, k).start()

    def start_own(k):
        for stream in (0, 1):
            own(stream, k).start()

    def relaunch(k, following=True):
        absorb(0, k)
        launch(1, k)
        if following:
            start_own(k + 1)

    def onward(phase, k):
        absorb(phase, k)
        if phase < 3:
            launch(phase + 1, k)

    wide = ff // width
    per_part = width // part

    def down_grad(pair):
        weight_grad(
            lambda i, right, piece: (2 * pair + right, i * many + piece),
            0,
            per_part,
            lambda i: dy[:, at(i * part, part)],
            lambda i: act[:, 2 * pair * width : (2 * pair + 1) * width],
            lambda i: act[:, (2 * pair + 1) * width : (2 * pair + 2) * width],
        )

    down_grad(0)
    launch(0, 0)
    start_own(0)
    down_grad(1)
    launch(0, 1)

    def unwiden(c):
        dup[:, c] = (nt(dy[...], wd[c, :]) * dup[:, c].astype(F32)).astype(LOW)

    tiles(ff // TILE, unwiden)
    weight_grad(
        lambda i, right, piece: (
            wide + lax.rem(i * many + piece, wide),
            (i * many + piece) // wide,
        ),
        0,
        ff // part,
        lambda i: dup[:, at(i * part, part)],
        lambda i: n2[...],
    )
    launch(0, 2)
    launch(0, 3)

    relaunch(0)

    def to_mid(c):
        tmp[:, c] = nt(dup[...], wu[c, :])

    tiles(width // 256, to_mid, 256)
    gains[0] = jnp.zeros_like(gains[0])

    def store_mid(r, total):
        ef[r, :] = total
        dy[r, :] = total.astype(LOW)

    norm_back(load_mid, tmp, gain_mlp, slice(8, 16), store_mid, 0, rows, 11)
    relaunch(1)

    @pl.when(first)
    def _():
        forward_relay.wait_send()

    def to_mix(c):
        yb[:, c] = nt(dy[...], wo[c, :]).astype(LOW)

    tiles(width // TILE, to_mix)
    mixf[...] = yb[tok:rows, :].astype(F32)

    @pl.when(second)
    def _():
        k = kv_all[:, :, :width].reshape(keys, width)
        v = kv_all[:, :, width:].reshape(keys, width)
        for m in range(half):
            b = slice(m * 128, (m + 1) * 128)
            block_diagonal(vbd.at[pl.ds(256, 256)], m * 128, mixf, m * LAT, 0, 1.0)
        both = slice(0, half * 128)
        do = vbd[256 : 256 + half * 128, :]
        pt = probs_lat[both, 0:keys]
        pf = pt.astype(F32)
        dp = nt(do, v)
        along = jnp.sum(pf * dp, axis=1, keepdims=True)
        ds = (pf * (dp - along)).astype(LOW)
        kvg_send[:, :, :width] = tn(ds, qbd[both, :]).astype(LOW).reshape(n, lat, width)
        kvg_send[:, :, width:] = tn(pt, do).astype(LOW).reshape(n, lat, width)
        for shift in range(1, n):
            kvg_copy(shift).start()
        dq = nn(ds, k)
        for m in range(half):
            head_sum(latf, m * LAT, 0, dq[m * 128 : (m + 1) * 128], 0.125, False)
        proj[tok:rows, :width] = latf[:, :width].astype(LOW)
        layer_output(False)

    onward(1, 0)
    relaunch(2)
    weight_grad(
        lambda i, right, piece: (2 * wide, i * many + piece),
        0,
        width // part,
        lambda i: dy[:, at(i * part, part)],
        lambda i: mixed[...],
    )
    for copy in out_copies:
        copy.wait()

    @pl.when(first)
    def _():
        for m in range(half):
            r = slice(m * GROUP, (m + 1) * GROUP)
            b = slice(m * 128, (m + 1) * 128)
            block_diagonal(vbd, m * 128, mixf, m * LAT, 0, 1.0)
            do = vbd[b, :]
            dp = nt(do, proj[r, 2 * width :])
            dl = nt(do, proj[tok:rows, 2 * width :])
            pt = probs_lat[b, 0:GROUP]
            pe = probs_lat[b, GROUP : GROUP + lat]
            pf = pt.astype(F32)
            pg = pe.astype(F32)
            along = jnp.sum(pf * dp, axis=1, keepdims=True) + jnp.sum(
                pg * dl, axis=1, keepdims=True
            )
            ds = (pf * (dp - along)).astype(LOW)
            dsl = (pg * (dl - along)).astype(LOW)
            dq = nn(ds, proj[r, width : 2 * width]) + nn(dsl, proj[tok:rows, width : 2 * width])
            head_sum(latf, m * LAT, 0, dq, 0.125, False)
            tmp[r, :] = tn(ds, qbd[b, :])
            out[r, :] = tn(pt, do)
            if m == 0:
                tmp[tok:rows, :] = tn(dsl, qbd[b, :])
                out[tok:rows, :] = tn(pe, do)
            else:
                tmp[tok:rows, :] += tn(dsl, qbd[b, :])
                out[tok:rows, :] += tn(pe, do)
        proj[tok:rows, :width] = latf[:, :width].astype(LOW)

        def one_pair(it, side):
            m, p = it // pairs, lax.rem(it, pairs)
            r = at(m * GROUP, GROUP)
            qc = at(p * 128, 128)
            q = proj[r, qc]
            k = proj[r, at(width + p * 128, 128)]
            v = proj[r, at(2 * width + p * 128, 128)]
            kl = proj[tok:rows, at(width + p * 128, 128)]
            vl = proj[tok:rows, at(2 * width + p * 128, 128)]
            dx = yb[r, qc]
            dq = jnp.zeros((GROUP, 128), F32)
            dk = tmp[r, qc]
            dv = out[r, qc]
            dkl = tmp[tok:rows, qc]
            dvl = out[tok:rows, qc]
            for e in (0, 1):
                qe = q * eighths[e]
                de = dx * halves[e]
                s = scores.at[2 * side + e]
                s[...] = nt(v, de)
                dl = nt(vl, de)
                pt = probs[2 * it + e, 0:GROUP, :]
                pe = probs[2 * it + e, GROUP : GROUP + lat, :]
                pg = pe.astype(F32)
                along = jnp.sum(pg * dl, axis=0, keepdims=True)
                for c in chunks:
                    pf = probs[2 * it + e, c, :].astype(F32)
                    along += jnp.sum(pf * s[c, :], axis=0, keepdims=True)
                for c in chunks:
                    pf = probs[2 * it + e, c, :].astype(F32)
                    slopes[2 * side + e, c, :] = (pf * (s[c, :] - along)).astype(LOW)
                ds = slopes[2 * side + e]
                dsl = (pg * (dl - along)).astype(LOW)
                dq += tn(ds, k * halves[e]) + tn(dsl, kl * halves[e])
                dk += nn(ds, qe)
                dkl += nn(dsl, qe)
                dv += nn(pt, de)
                dvl += nn(pe, de)
            proj[r, qc] = (dq * 0.125).astype(LOW)
            proj[r, at(width + p * 128, 128)] = dk.astype(LOW)
            proj[r, at(2 * width + p * 128, 128)] = dv.astype(LOW)
            tmp[tok:rows, qc] = dkl
            out[tok:rows, qc] = dvl

        def pair(i, carry):
            one_pair(2 * i, 0)
            one_pair(2 * i + 1, 1)
            return carry

        lax.fori_loop(0, half * pairs // 2, pair, 0)
        proj[tok:rows, width : 2 * width] = tmp[tok:rows, :].astype(LOW)
        proj[tok:rows, 2 * width :] = out[tok:rows, :].astype(LOW)

    @pl.when(second)
    def _():
        for m in range(half):
            r = slice(m * GROUP, (m + 1) * GROUP)
            b = slice(m * 128, (m + 1) * 128)
            pt = probs[m, 0:GROUP, 0:128]
            pf = pt.astype(F32)
            dx = yb[r, :]
            dp = nt(dx, vbd[b, :])
            ds = (pf * (dp - class_sum(pf * dp))).astype(LOW)
            dk = tn(ds, proj[r, :width])
            dv = tn(pt, dx)
            proj[r, :width] = (nn(ds, kbd[b, :]) * 0.125).astype(LOW)
            head_sum(latf, m * LAT, width, dk, 0.125, False)
            head_sum(latf, m * LAT, 2 * width, dv, 1.0, False)
        total = latf[:, width:] + kvg_send[me].astype(F32)
        for shift in range(1, n):
            kvg_copy(shift).wait_recv()
            total += kvg_recv[shift - 1].astype(F32)
        proj[tok:rows, width:] = total.astype(LOW)

    onward(1, 1)
    relaunch(3, False)

    @pl.when(first)
    def _():
        def to_in(c):
            tmp[:, c] = nt(proj[...], wq[c, :])

        tiles(width // 256, to_in, 256)

    @pl.when(second)
    def _():
        tmp[0:tok, :] = nt(proj[0:tok, :width], wq[:, :width])
        tmp[tok:rows, :] = nt(proj[tok:rows, :], wq[...])

    def store_in(r, total):
        low = total.astype(LOW)
        yb[r, :] = low
        out[r, :] = jnp.where(first, total, low.astype(F32))

    norm_back(load_in, tmp, gain_attn, slice(0, 8), store_in, 0, rows, 11)
    for copy in grad_copies:
        copy.start()
    onward(2, 0)
    onward(1, 2)

    @pl.when(second)
    def _():
        backward_relay.start()

    def qkv_grad(start, count, r):
        weight_grad(
            lambda i, right, piece: (
                2 * wide + 1 + lax.rem(i * many + piece, 3),
                (i * many + piece) // 3,
            ),
            start,
            count,
            lambda i: proj[r, at(i * part, part)],
            lambda i: n1[r, :],
        )

    @pl.when(first)
    def _():
        qkv_grad(0, 3 * per_part, slice(0, rows))

    @pl.when(second)
    def _():
        qkv_grad(0, per_part, slice(0, rows))
        qkv_grad(per_part, 2 * per_part, slice(tok, rows))

    for pair in range(4, spread_pairs):
        launch(0, pair)
    start_own(4)

    def gain_copy(bit):
        return pltpu.make_async_remote_copy(
            src_ref=gains.at[bit],
            dst_ref=land_g.at[bit],
            send_sem=gain_s.at[bit],
            recv_sem=gain_r.at[bit],
            device_id=across(bit),
            device_id_type=MESH,
        )

    def gain_step(bit):
        gain_copy(bit).wait_recv()
        gains[bit + 1] = gains[bit] + land_g[bit]

    def each(lo, hi, phase):
        def one(i, carry):
            onward(phase, i)
            return carry

        lax.fori_loop(lo, hi, one, 0)

    gain_copy(0).start()
    onward(2, 1)
    onward(1, 3)
    relaunch(4)
    gain_step(0)
    gain_copy(1).start()
    each(0, 2, 3)
    each(2, 4, 2)
    relaunch(5, False)
    gain_step(1)
    gain_copy(2).start()
    each(4, 6, 1)
    each(2, 4, 3)
    gain_step(2)
    gain_copy(3).start()
    each(4, 6, 2)
    gain_step(3)
    each(4, 6, 3)
    final = gains[4]
    for i in (0, 1):
        whole_gain = jnp.sum(final[8 * i : 8 * i + 8], axis=0, keepdims=True)
        whole_gain = jnp.broadcast_to(whole_gain, (8, width))
        rolled = pltpu.roll(whole_gain, lax.rem(width - me * unit, width), 1)
        gain_sums[8 * i : 8 * i + 8, :] = rolled[:, 0:128]

    def finish(k, carry):
        for stream in (0, 1):
            for phase in range(4):
                copy_of(stream, phase, k).wait_send()
        return carry

    lax.fori_loop(0, spread_pairs, finish, 0)
    for bit in range(4):
        gain_copy(bit).wait_send()
    for copy in grad_copies:
        copy.wait()
    for stream in (0, 1):
        for pair in (spread_pairs - 2, spread_pairs - 1):
            leave(stream, pair).wait()

    @pl.when(second)
    def _():
        backward_relay.wait_send()
        for shift in range(1, n):
            kv_copy(shift, False).wait_send()
            kvg_copy(shift).wait_send()


def both_layers(n, tokens, latents, slots, images, gains, weights, d_tokens, d_latents):
    tok, width = tokens.shape
    lat = latents.shape[0]
    rows = tok + lat
    w_qkv, w_out, w_up, w_down = weights
    ff = w_up.shape[1]
    keys = n * lat
    half = lat // LAT
    size = sum(w.size for w in weights)
    chunks = size // (width * width)
    pairs = chunks // 2
    unit = width // n
    vm, hbm = pl.BlockSpec(memory_space=pltpu.VMEM), pl.BlockSpec(memory_space=pl.ANY)
    sm = pl.BlockSpec(memory_space=pltpu.SMEM)
    scratch = [
        pltpu.VMEM(w.shape, LOW) for w in (w_qkv, w_out, w_up, w_down)
    ] + [
        pltpu.VMEM(shape, dtype)
        for shape, dtype in (
            ((rows, width), LOW),
            ((rows, width), LOW),
            ((rows, 3 * width), LOW),
            ((rows, width), LOW),
            ((rows, width), F32),
            ((rows, width), LOW),
            ((rows, ff), LOW),
            ((rows, ff), LOW),
            ((rows, width), LOW),
            ((rows, width), LOW),
            ((rows, width), F32),
            ((rows, width), F32),
            ((rows, width), F32),
            ((half * width // 64, GROUP + lat, GROUP), LOW),
            ((half * 128, max(keys, GROUP + 128)), LOW),
            ((4, GROUP, GROUP), F32),
            ((4, GROUP, GROUP), LOW),
            ((lat, 3 * width), F32),
            ((lat, width), F32),
            ((8, keys), F32),
            ((half * 128, width), LOW),
            ((half * 128, width), LOW),
            ((half * 256, width), LOW),
            ((n, lat, 2 * width), LOW),
            ((n, lat, 2 * width), LOW),
            ((n - 1, lat, 2 * width), LOW),
            ((2, 384 // unit, unit, width), LOW),
            ((5, 16, width), F32),
            ((2, 2, unit, width), F32),
            ((2, 2, 2, unit, width), LOW),
            ((2, 2, 2, unit, width), LOW),
            ((pairs, 2, 2, 2, unit, width), LOW),
            ((pairs, 2, 2, 2, unit, width), LOW),
            ((pairs, 2, 2, unit, width), LOW),
            ((pairs, 2, 2, unit, width), LOW),
            ((pairs, 2, unit, width), LOW),
            ((pairs, 2, unit, width), LOW),
            ((pairs, unit, width), LOW),
            ((pairs, unit, width), LOW),
            ((4, 16, width), F32),
        )
    ] + [
        pltpu.SemaphoreType.DMA((10,)),
        pltpu.SemaphoreType.DMA((2, 384 // unit)),
        pltpu.SemaphoreType.DMA((2,)),
        pltpu.SemaphoreType.DMA((2, 2)),
        pltpu.SemaphoreType.DMA((2, 4, pairs)),
        pltpu.SemaphoreType.DMA((2, 4, pairs)),
        pltpu.SemaphoreType.DMA((4,)),
        pltpu.SemaphoreType.DMA((4,)),
        pltpu.SemaphoreType.DMA((2,)),
        pltpu.SemaphoreType.DMA((2,)),
        pltpu.SemaphoreType.DMA((n - 1,)),
        pltpu.SemaphoreType.DMA((n - 1,)),
        pltpu.SemaphoreType.DMA((n - 1,)),
        pltpu.SemaphoreType.DMA((n - 1,)),
    ]
    return pl.pallas_call(
        functools.partial(layer_kernel, n),
        out_shape=(
            jax.ShapeDtypeStruct((tok, width), F32),
            jax.ShapeDtypeStruct((lat, width), F32),
            jax.ShapeDtypeStruct((tok, width), F32),
            jax.ShapeDtypeStruct((lat, width), F32),
            jax.ShapeDtypeStruct((chunks, 2, 2, 2, 2, unit, width), LOW),
            jax.ShapeDtypeStruct((chunks, unit, width), F32),
            jax.ShapeDtypeStruct((16, 128), F32),
        ),
        in_specs=[hbm, hbm, vm, sm, sm, vm, vm] + [hbm] * 6,
        out_specs=(hbm,) * 6 + (vm,),
        scratch_shapes=scratch,
        compiler_params=pltpu.CompilerParams(
            collective_id=1, has_side_effects=True, vmem_limit_bytes=63 * 1024 * 1024
        ),
        cost_estimate=pl.CostEstimate(
            flops=6 * rows * size, bytes_accessed=4 * size, transcendentals=0
        ),
    )(tokens, latents, slots, slots, images, *gains, *weights, d_tokens, d_latents)


def finish_kernel(width, *refs):
    rows_in, (summed, gains), rows_out = refs[0:4], refs[4:6], refs[6:10]
    gain_attn, g_qkv, g_out, gain_mlp, g_up, g_down = refs[10:16]
    held, (sem_in, sem_out) = refs[16:21], refs[21:23]
    wide = g_down.shape[1] // width
    unit = g_out.shape[1]
    loads = [
        pltpu.make_async_copy(src, dst, sem_in.at[i])
        for i, (src, dst) in enumerate(zip((*rows_in, summed), held))
    ]
    for load in loads:
        load.start()
    all_rows, sums = held[0:4], held[4]
    moves = [[pair] for pair in zip(all_rows, rows_out)] + [
        [(sums.at[c], g_down.at[:, c * width : (c + 1) * width]) for c in range(wide)]
        + [
            (sums.at[wide : 2 * wide], g_up),
            (sums.at[2 * wide : 2 * wide + 1], g_out),
            (sums.at[2 * wide + 1 :], g_qkv),
        ]
    ]
    gain_attn[...] = gains[0:1, 0:unit]
    gain_mlp[...] = gains[8:9, 0:unit]
    started = []
    for load, group in zip(loads, moves):
        load.wait()
        for src, dst in group:
            started.append(pltpu.make_async_copy(src, dst, sem_out.at[len(started)]))
            started[-1].start()
    for move in started:
        move.wait()


def finished(rows, summed, gains, wide):
    chunks, unit, width = summed.shape
    hbm, vm = pl.BlockSpec(memory_space=pl.ANY), pl.BlockSpec(memory_space=pltpu.VMEM)
    shapes = [r.shape for r in rows] + [
        (1, unit),
        (3, unit, width),
        (1, unit, width),
        (1, unit),
        (wide, unit, width),
        (unit, wide * width),
    ]
    return pl.pallas_call(
        functools.partial(finish_kernel, width),
        out_shape=tuple(jax.ShapeDtypeStruct(s, F32) for s in shapes),
        in_specs=[hbm] * 5 + [vm],
        out_specs=(hbm,) * 4 + (vm, hbm, hbm, vm, hbm, hbm),
        scratch_shapes=[pltpu.VMEM(x.shape, F32) for x in (*rows, summed)]
        + [pltpu.SemaphoreType.DMA((5,)), pltpu.SemaphoreType.DMA((7 + wide,))],
        compiler_params=pltpu.CompilerParams(vmem_limit_bytes=62 * 1024 * 1024),
    )(*rows, summed, gains)
def fused_shards(
    unused_grid,
    tokens,
    latents,
    slot_group,
    image_groups,
    gain_attn,
    w_qkv,
    w_out,
    gain_mlp,
    w_up,
    w_down,
    d_tokens,
    d_latents,
):
    micro, tok, width = tokens.shape
    lat = latents.shape[1]
    out_tok, out_lat, grad_tok, grad_lat, unused_grads, summed, gains = both_layers(
        slot_group.shape[1],
        tokens.reshape(micro * tok, width),
        latents.reshape(micro * lat, width),
        slot_group,
        image_groups,
        (gain_attn, gain_mlp),
        (w_qkv[0], w_out[0], w_up[0], w_down[0]),
        d_tokens.reshape(micro * tok, width),
        d_latents.reshape(micro * lat, width),
    )
    wide = w_up.shape[2] // width
    rows = (out_tok, out_lat, grad_tok, grad_lat)
    *rows, first_gain, qkv, out, second_gain, up, down = finished(rows, summed, gains, wide)
    return (
        rows[0].reshape(1, micro, tok, width),
        rows[1].reshape(1, micro, lat, width),
        rows[2].reshape(1, micro, tok, width),
        rows[3].reshape(1, micro, lat, width),
        first_gain,
        qkv.reshape(-1, width).T[None],
        out.reshape(-1, width).T[None],
        second_gain,
        up.reshape(-1, width).T[None],
        down.T[None],
    )

def solution(mesh):
    in_specs = (
        P(None, "dp", None),
        P(None, "dp", None),
        P(),
        P(),
        P("section", None),
        P("section", None, None),
        P("section", None, None),
        P("section", None),
        P("section", None, None),
        P("section", None, None),
        P(None, "dp", None),
        P(None, "dp", None),
    )
    out_specs = (
        P("section", None, "dp", None),
        P("section", None, "dp", None),
        P("section", None, "dp", None),
        P("section", None, "dp", None),
        P("section", "dp"),
        P("section", None, "dp"),
        P("section", None, "dp"),
        P("section", "dp"),
        P("section", None, "dp"),
        P("section", None, "dp"),
    )
    grid = grid_of(mesh)

    def program(*args):
        n, width = mesh.shape["dp"], args[0].shape[2]
        one_group = args[0].shape[1] == n * GROUP
        body = fused_shards if one_group and n == 16 and width % (16 * n) == 0 else shards
        return jax.shard_map(
            functools.partial(body, grid), mesh=mesh, in_specs=in_specs, out_specs=out_specs, check_vma=False
        )(*args)

    return program
```

```python
import functools

import jax
import jax.numpy as jnp
from jax import lax
from jax.experimental import pallas as pl
from jax.experimental.pallas import tpu as pltpu
from jax.sharding import PartitionSpec as P

HEADS = 12
GROUP = 256
LAT = 8


epsilon = 1e-05
masked_score = -1e30


MESH = pl.DeviceIdType.MESH


def grid_of(mesh):
    n = mesh.shape["dp"]
    coords = [getattr(d, "coords", None) for d in mesh.devices.reshape(n, -1)[:, 0]]
    if any(c is None for c in coords):
        return (n // 4, 2, 2) if n % 4 == 0 else (n, 1, 1)
    sizes = {a: len({c[a] for c in coords}) for a in range(3)}
    strides = {
        a: min([i for i in range(n) if coords[i][a] != coords[0][a]], default=n) for a in range(3)
    }
    order = sorted(range(3), key=lambda a: -strides[a])
    return tuple(sizes[a] for a in order)


def spread_kernel(grid, pairs, g_ref, gain_ref, out_ref, gout_ref, *scratch):
    acc = scratch[0:3]
    land = [scratch[3 + 3 * i : 6 + 3 * i] for i in range(3)]
    send_sem, recv_sem, own_sem = scratch[12:15]
    me = lax.axis_index("dp")
    section = lax.axis_index("section")
    l0, l1, l2 = grid
    here = (me // (l1 * l2), lax.rem(me // l2, l1), lax.rem(me, l2))

    def device(axis, shift):
        there = list(here)
        there[axis] = lax.rem(here[axis] + shift, grid[axis])
        return there[axis], ((there[0] * l1 + there[1]) * l2 + there[2], section)

    barrier = pltpu.get_barrier_semaphore()
    for axis in range(3):
        for shift in range(1, grid[axis]):
            pl.semaphore_signal(
                barrier, inc=1, device_id=device(axis, shift)[1], device_id_type=MESH
            )
    pl.semaphore_wait(barrier, sum(grid) - 3)

    orders = ((2, 1, 0), (1, 2, 0), (2, 1, 0))

    def source(stream, phase, k, at):
        if phase == 0:
            if stream == 0:
                return g_ref.at[2 * k, :, :, at]
            if stream == 1:
                return g_ref.at[2 * k + 1, :, at]
            return gain_ref.at[:, :, at]
        if phase == 1:
            return acc[stream].at[k, :, at]
        return acc[stream].at[k, at, here[orders[stream][1]]]

    def copies(stream, phase, k):
        axis = orders[stream][phase]
        for shift in range(1, grid[axis]):
            at, target = device(axis, shift)
            yield pltpu.make_async_remote_copy(
                src_ref=source(stream, phase, k, at),
                dst_ref=land[phase][stream].at[k, shift - 1],
                send_sem=send_sem.at[stream, phase, k, shift - 1],
                recv_sem=recv_sem.at[stream, phase, k, shift - 1],
                device_id=target,
                device_id_type=MESH,
            )

    def own(stream, k):
        return pltpu.make_async_copy(
            source(stream, 0, k, here[orders[stream][0]]), acc[stream].at[k], own_sem.at[stream, k]
        )

    def launch(stream, phase, k):
        for copy in copies(stream, phase, k):
            copy.start()

    def absorb(stream, phase, k):
        axis = orders[stream][phase]
        if phase == 0:
            own(stream, k).wait()
        for copy in copies(stream, phase, k):
            copy.wait_recv()
        into = land[phase][stream]
        count = grid[axis] - 1
        if phase == 0:
            for a in range(acc[stream].shape[1]):
                for b in range(acc[stream].shape[2]):
                    total = acc[stream][k, a, b].astype(jnp.float32)
                    for s in range(count):
                        total += into[k, s, a, b].astype(jnp.float32)
                    acc[stream][k, a, b] = total.astype(acc[stream].dtype)
        elif phase == 1:
            mine = here[axis]
            for a in range(acc[stream].shape[1]):
                total = acc[stream][k, a, mine].astype(jnp.float32)
                for s in range(count):
                    total += into[k, s, a].astype(jnp.float32)
                acc[stream][k, a, mine] = total.astype(acc[stream].dtype)
        else:
            total = acc[stream][k, here[0], here[orders[stream][1]]].astype(jnp.float32)
            for s in range(count):
                total += into[k, s].astype(jnp.float32)
            if stream < 2:
                out_ref[2 * k + stream] = total
            else:
                gout_ref[...] = total

    own(2, 0).start()
    launch(2, 0, 0)

    def start_own(k, carry):
        for stream in (0, 1):
            own(stream, k).start()
        return carry

    for stream in (0, 1):
        launch(stream, 0, 0)
    lax.fori_loop(0, pairs, start_own, 0)

    def turn(t, carry):
        @pl.when(t + 1 < pairs)
        def _():
            for stream in (0, 1):
                launch(stream, 0, t + 1)

        @pl.when(t < pairs)
        def _():
            for stream in (0, 1):
                absorb(stream, 0, t)
                launch(stream, 1, t)

        @pl.when((t >= 1) & (t - 1 < pairs))
        def _():
            for stream in (0, 1):
                absorb(stream, 1, t - 1)
                launch(stream, 2, t - 1)

        @pl.when(t >= 2)
        def _():
            for stream in (0, 1):
                absorb(stream, 2, t - 2)

        return carry

    lax.fori_loop(0, pairs + 2, turn, 0)
    absorb(2, 0, 0)
    launch(2, 1, 0)
    absorb(2, 1, 0)
    launch(2, 2, 0)
    absorb(2, 2, 0)

    def finish(k, carry):
        for stream in (0, 1):
            for phase in range(3):
                for copy in copies(stream, phase, k):
                    copy.wait_send()
        return carry

    lax.fori_loop(0, pairs, finish, 0)
    for phase in range(3):
        for copy in copies(2, phase, 0):
            copy.wait_send()


def spread(grid, grads, gains):
    chunks, n, rows, width = grads.shape
    pairs = chunks // 2
    l0, l1, l2 = grid
    most = max(max(grid) - 1, 1)
    low = jnp.bfloat16
    shapes = ((pairs, rows, width, low), (pairs, rows, width, low), (1, 8, 128, jnp.float32))
    inner = ((l1, l2), (l2, l1), (l1, l2))
    acc, first, second, third = [], [], [], []
    for (count, r, w, dt), (kept, sent) in zip(shapes, inner):
        acc.append(pltpu.VMEM((count, l0, kept, r, w), dt))
        first.append(pltpu.VMEM((count, max(sent - 1, 1), l0, kept, r, w), dt))
        second.append(pltpu.VMEM((count, max(kept - 1, 1), l0, r, w), dt))
        third.append(pltpu.VMEM((count, max(l0 - 1, 1), r, w), dt))
    return pl.pallas_call(
        functools.partial(spread_kernel, grid, pairs),
        out_shape=(
            jax.ShapeDtypeStruct((chunks, rows, width), jnp.float32),
            jax.ShapeDtypeStruct((8, 128), jnp.float32),
        ),
        in_specs=[pl.BlockSpec(memory_space=pl.ANY)] * 2,
        out_specs=(pl.BlockSpec(memory_space=pltpu.VMEM),) * 2,
        scratch_shapes=acc
        + first
        + second
        + third
        + [
            pltpu.SemaphoreType.DMA((3, 3, pairs, most)),
            pltpu.SemaphoreType.DMA((3, 3, pairs, most)),
            pltpu.SemaphoreType.DMA((3, pairs)),
        ],
        compiler_params=pltpu.CompilerParams(
            collective_id=0, has_side_effects=True, vmem_limit_bytes=60 * 1024 * 1024
        ),
        cost_estimate=pl.CostEstimate(flops=0, bytes_accessed=grads.size * 4, transcendentals=0),
    )(grads.reshape(chunks, l0, l1, l2, rows, width), gains.reshape(l0, l1, l2, 8, 128))


def from_behind(x, axis, by):
    devices = lax.axis_size(axis)
    pairs = [(i, i + by) for i in range(devices) if 0 <= i + by < devices]
    return lax.ppermute(x, axis, pairs)


def layer_norm(values, gain):
    row_mean = jnp.mean(values, axis=-1, keepdims=True)
    centred = values - row_mean
    row_var = jnp.mean(centred * centred, axis=-1, keepdims=True)
    return centred * lax.rsqrt(row_var + epsilon) * gain


def front_half(all_rows, gain_attn, w_qkv):
    normed = layer_norm(all_rows, gain_attn).astype(jnp.bfloat16)
    projected = jnp.dot(normed, w_qkv, preferred_element_type=jnp.float32).astype(jnp.bfloat16)
    return (normed, projected)


def latent_operand(projected, tok_rows, model_width):
    return projected[tok_rows:, model_width:]


def back_half(all_rows, projected, remote_rows, allowed, weights):
    gain_attn, w_qkv, w_out, gain_mlp, w_up, w_down = weights
    row_count, model_width = all_rows.shape
    head_size = model_width // HEADS
    remote_pairs = remote_rows[:, remote_rows.shape[1] - 2 * model_width :]
    queries = projected[:, :model_width].reshape(row_count, HEADS, head_size)
    key_rows = jnp.concatenate(
        [projected[:, model_width : 2 * model_width], remote_pairs[:, :model_width]], axis=0
    )
    value_rows = jnp.concatenate(
        [projected[:, 2 * model_width :], remote_pairs[:, model_width:]], axis=0
    )
    key_rows = key_rows.reshape(-1, HEADS, head_size)
    value_rows = value_rows.reshape(-1, HEADS, head_size)
    scores = jnp.einsum(
        "qhd,khd->hqk", queries, key_rows, preferred_element_type=jnp.float32
    ) * head_size ** (-0.5)
    attn_weights = jax.nn.softmax(jnp.where(allowed[None], scores, masked_score), axis=-1)
    attn_low = attn_weights.astype(jnp.bfloat16)
    mixed_low = jnp.einsum("hqk,khd->qhd", attn_low, value_rows, preferred_element_type=jnp.float32)
    mixed_low = mixed_low.reshape(row_count, model_width).astype(jnp.bfloat16)
    mid_rows = all_rows + jnp.dot(mixed_low, w_out, preferred_element_type=jnp.float32)
    normed_mlp = layer_norm(mid_rows, gain_mlp).astype(jnp.bfloat16)
    up_proj = jnp.dot(normed_mlp, w_up, preferred_element_type=jnp.float32)
    activated = jax.nn.gelu(up_proj).astype(jnp.bfloat16)
    result = mid_rows + jnp.dot(activated, w_down, preferred_element_type=jnp.float32)
    return dict(
        queries=queries,
        key_rows=key_rows,
        value_rows=value_rows,
        attn_weights=attn_weights,
        attn_low=attn_low,
        mixed_low=mixed_low,
        mid_rows=mid_rows,
        normed_mlp=normed_mlp,
        up_proj=up_proj,
        activated=activated,
        result=result,
    )


def section_backward(saved, d_result, all_rows, normed, allowed, weights, latent_start):
    gain_attn, w_qkv, w_out, gain_mlp, w_up, w_down = weights
    row_count, model_width = all_rows.shape
    head_size = model_width // HEADS
    score_scale = head_size ** (-0.5)
    d_low = d_result.astype(jnp.bfloat16)
    grad_down = jnp.dot(d_low.T, saved["activated"], preferred_element_type=jnp.float32)
    d_activated = jnp.dot(d_low, w_down.T, preferred_element_type=jnp.float32)
    unused_up, gelu_back = jax.vjp(jax.nn.gelu, saved["up_proj"])
    d_up = gelu_back(d_activated)[0].astype(jnp.bfloat16)
    grad_up = jnp.dot(d_up.T, saved["normed_mlp"], preferred_element_type=jnp.float32)
    d_normed_mlp = jnp.dot(d_up, w_up.T, preferred_element_type=jnp.float32)
    unused_mid, second_back = jax.vjp(layer_norm, saved["mid_rows"], gain_mlp)
    d_mid_norm, grad_gain_mlp = second_back(d_normed_mlp)
    d_mid = d_result + d_mid_norm
    d_mid_low = d_mid.astype(jnp.bfloat16)
    grad_out = jnp.dot(d_mid_low.T, saved["mixed_low"], preferred_element_type=jnp.float32)
    d_mixed = jnp.dot(d_mid_low, w_out.T, preferred_element_type=jnp.float32).astype(jnp.bfloat16)
    d_mixed = d_mixed.reshape(row_count, HEADS, head_size)
    d_weights = jnp.einsum(
        "qhd,khd->hqk", d_mixed, saved["value_rows"], preferred_element_type=jnp.float32
    )
    d_values = jnp.einsum(
        "hqk,qhd->khd", saved["attn_low"], d_mixed, preferred_element_type=jnp.float32
    )
    attn_weights = saved["attn_weights"]
    d_scores = attn_weights * (
        d_weights - jnp.sum(attn_weights * d_weights, axis=-1, keepdims=True)
    )
    d_scores_low = jnp.where(allowed[None], d_scores, 0.0).astype(jnp.bfloat16)
    d_queries = (
        jnp.einsum(
            "hqk,khd->qhd", d_scores_low, saved["key_rows"], preferred_element_type=jnp.float32
        )
        * score_scale
    )
    d_keys = (
        jnp.einsum(
            "hqk,qhd->khd", d_scores_low, saved["queries"], preferred_element_type=jnp.float32
        )
        * score_scale
    )
    remote_part = jnp.concatenate(
        [
            d_keys[row_count:].reshape(-1, model_width),
            d_values[row_count:].reshape(-1, model_width),
        ],
        axis=1,
    )
    own_part = lax.psum_scatter(remote_part, "dp", scatter_dimension=0, tiled=True)
    local_pairs = jnp.concatenate(
        [
            d_keys[:row_count].reshape(row_count, model_width),
            d_values[:row_count].reshape(row_count, model_width),
        ],
        axis=1,
    )
    local_pairs = jnp.concatenate(
        [local_pairs[:latent_start], local_pairs[latent_start:] + own_part], axis=0
    )
    d_projected = jnp.concatenate(
        [d_queries.reshape(row_count, model_width), local_pairs], axis=1
    ).astype(jnp.bfloat16)
    grad_qkv = jnp.dot(d_projected.T, normed, preferred_element_type=jnp.float32)
    d_normed = jnp.dot(d_projected, w_qkv.T, preferred_element_type=jnp.float32)
    unused_rows, first_back = jax.vjp(layer_norm, all_rows, gain_attn)
    d_rows_norm, grad_gain_attn = first_back(d_normed)
    return (
        d_mid + d_rows_norm,
        (grad_gain_attn, grad_qkv, grad_out, grad_gain_mlp, grad_up, grad_down),
    )


def packed(grads, n):
    gain_first, qkv_grad, out_grad, gain_second, up_grad, down_grad = grads
    width = out_grad.shape[0]
    rows = width // n

    def by_rows(grad):
        return grad.reshape(n, -1, rows, width).transpose(1, 0, 2, 3).astype(jnp.bfloat16)

    down = down_grad.reshape(n, rows, -1, width).transpose(2, 0, 1, 3).astype(jnp.bfloat16)
    chunks = jnp.concatenate([down, by_rows(up_grad), by_rows(out_grad), by_rows(qkv_grad)], axis=0)
    gains = jnp.stack([gain_first.reshape(n, rows), gain_second.reshape(n, rows)], axis=1)
    return chunks, jnp.pad(gains, ((0, 0), (0, 6), (0, 128 - rows)))


def shards(
    grid,
    tokens,
    latents,
    slot_group,
    image_groups,
    gain_attn,
    w_qkv,
    w_out,
    gain_mlp,
    w_up,
    w_down,
    d_tokens,
    d_latents,
):
    micro = tokens.shape[0]
    tok_rows = tokens.shape[1]
    lat_rows = latents.shape[1]
    model_width = tokens.shape[2]
    local_groups = tok_rows // GROUP
    section_index = lax.axis_index("section")
    is_global = section_index == 1
    dp_index = lax.axis_index("dp")
    weights = (gain_attn[0], w_qkv[0], w_out[0], gain_mlp[0], w_up[0], w_down[0])
    image_ends = jnp.cumsum(image_groups, axis=1)
    slot_images = jnp.sum(
        (image_ends[:, None, :] <= slot_group[:, :, None]).astype(jnp.int32), axis=2
    )
    slot_total = slot_group.shape[1]
    row_group = jnp.concatenate([jnp.arange(tok_rows) // GROUP, jnp.arange(lat_rows) // LAT])
    row_latent = jnp.concatenate(
        [jnp.zeros((tok_rows,), jnp.bool_), jnp.ones((lat_rows,), jnp.bool_)]
    )
    same_group = row_group[:, None] == row_group[None, :]
    local_mask = jnp.where(
        is_global, (~row_latent)[:, None] & row_latent[None, :] & same_group, same_group
    )
    group_match = row_group[:, None] == jnp.arange(local_groups)[None, :]

    def key_images(batch):
        images_row = lax.dynamic_index_in_dim(slot_images, batch, 0, keepdims=False)
        return (images_row, jnp.broadcast_to(images_row[:, None], (slot_total, LAT)).reshape(-1))

    def allowed_for(batch):
        images_row, key_image = key_images(batch)
        own_images = lax.dynamic_slice_in_dim(images_row, dp_index * local_groups, local_groups)
        row_image = jnp.sum(jnp.where(group_match, own_images[None, :], 0), axis=1)
        remote_mask = is_global & row_latent[:, None] & (row_image[:, None] == key_image[None, :])
        return jnp.concatenate([local_mask, remote_mask], axis=1)

    def forward_turn(received, turn):
        recv_tokens, recv_latents = received
        batch = jnp.clip(turn - section_index, 0, micro - 1)
        own_tok = lax.dynamic_index_in_dim(tokens, batch, 0, keepdims=False)
        own_lat = lax.dynamic_index_in_dim(latents, batch, 0, keepdims=False)
        input_rows = jnp.concatenate(
            [
                jnp.where(is_global, recv_tokens, own_tok),
                jnp.where(is_global, recv_latents, own_lat),
            ],
            axis=0,
        )
        all_rows = input_rows.astype(jnp.float32)
        normed, projected = front_half(all_rows, weights[0], weights[1])
        remote_rows = lax.all_gather(
            latent_operand(projected, tok_rows, model_width), "dp", axis=0, tiled=True
        )
        saved = back_half(all_rows, projected, remote_rows, allowed_for(batch), weights)
        result = saved["result"]
        result_low = result.astype(jnp.bfloat16)
        stored = jnp.where(is_global, result, result_low.astype(jnp.float32))
        passed_on = from_behind((result_low[:tok_rows], result_low[tok_rows:]), "section", 1)
        return passed_on, (input_rows, stored[:tok_rows], stored[tok_rows:])

    nothing = (
        jnp.zeros((tok_rows, model_width), jnp.bfloat16),
        jnp.zeros((lat_rows, model_width), jnp.bfloat16),
    )
    turns = jnp.arange(micro + 1)
    unused_end, (kept_rows, tok_outputs, lat_outputs) = lax.scan(forward_turn, nothing, turns)

    def backward_turn(carry, turn):
        (recv_grad_tok, recv_grad_lat), totals = carry
        raw_batch = micro - turn - section_index
        valid = ((raw_batch >= 0) & (raw_batch < micro)).astype(jnp.float32)
        batch = jnp.clip(raw_batch, 0, micro - 1)
        all_rows = lax.dynamic_index_in_dim(
            kept_rows, batch + section_index, 0, keepdims=False
        ).astype(jnp.float32)
        normed, projected = front_half(all_rows, weights[0], weights[1])
        remote_rows = lax.all_gather(
            latent_operand(projected, tok_rows, model_width), "dp", axis=0, tiled=True
        )
        allowed = allowed_for(batch)
        saved = back_half(all_rows, projected, remote_rows, allowed, weights)
        given = (
            jnp.concatenate(
                [
                    lax.dynamic_index_in_dim(d_tokens, batch, 0, keepdims=False),
                    lax.dynamic_index_in_dim(d_latents, batch, 0, keepdims=False),
                ],
                axis=0,
            )
            * valid
        )
        passed = jnp.concatenate([recv_grad_tok, recv_grad_lat], axis=0).astype(jnp.float32)
        d_result = jnp.where(is_global, given, passed)
        d_rows, grads = section_backward(
            saved, d_result, all_rows, normed, allowed, weights, tok_rows
        )
        totals = tuple((accum + piece for accum, piece in zip(totals, grads)))
        d_rows_low = d_rows.astype(jnp.bfloat16)
        stored = jnp.where(is_global, d_rows_low.astype(jnp.float32), d_rows)
        sent = from_behind((d_rows_low[:tok_rows], d_rows_low[tok_rows:]), "section", -1)
        return (sent, totals), (stored[:tok_rows], stored[tok_rows:])

    totals = tuple(
        jnp.zeros(w.shape[::-1] if w.ndim == 2 else w.shape, jnp.float32) for w in weights
    )
    (unused_sent, totals), (tok_grads, lat_grads) = lax.scan(
        backward_turn, (nothing, totals), turns
    )
    chunks, gains = packed(totals, lax.axis_size("dp"))
    summed, gain_sums = spread(grid, chunks, gains)
    rows = summed.shape[1]
    layer_tokens = lax.dynamic_slice_in_dim(tok_outputs, section_index, micro, 0)[None]
    layer_latents = lax.dynamic_slice_in_dim(lat_outputs, section_index, micro, 0)[None]
    grad_tokens = lax.dynamic_slice_in_dim(tok_grads, 1 - section_index, micro, 0)[::-1][
        None
    ]
    grad_latents = lax.dynamic_slice_in_dim(lat_grads, 1 - section_index, micro, 0)[
        ::-1
    ][None]
    return (
        layer_tokens,
        layer_latents,
        grad_tokens,
        grad_latents,
        gain_sums[0:1, :rows],
        summed[9:].reshape(-1, model_width).T[None],
        summed[8].T[None],
        gain_sums[1:2, :rows],
        summed[4:8].reshape(-1, model_width).T[None],
        summed[0:4].transpose(0, 2, 1).reshape(-1, rows)[None],
    )


F32 = jnp.float32
LOW = jnp.bfloat16
HEAD_PAD = 16
TILE = 768


def nn(a, b):
    return jnp.dot(a, b, preferred_element_type=F32)


def nt(a, b):
    return lax.dot_general(a, b, (((1,), (1,)), ((), ())), preferred_element_type=F32)


def row_mean(values):
    return jnp.mean(values, axis=-1, keepdims=True)


def row_stats(load, spans):
    means = [row_mean(load(r)) for r in spans]
    scales = []
    for r, mean in zip(spans, means):
        centred = load(r) - mean
        scales.append(lax.rsqrt(row_mean(centred * centred) + epsilon))
    return means, scales


def at(start, size):
    return pl.ds(pl.multiple_of(start, size), size)


def class_max(s):
    for by in (16, 32, 64):
        s = jnp.maximum(s, pltpu.roll(s, by, 1))
    return s


def class_sum(s):
    for by in (16, 32, 64):
        s = s + pltpu.roll(s, by, 1)
    return s


def layer_kernel(
    n,
    tokens,
    latents,
    slots,
    slot_at,
    image_at,
    gain_attn,
    gain_mlp,
    w_qkv,
    w_out,
    w_up,
    w_down,
    d_tokens,
    d_latents,
    out_tok,
    out_lat,
    grad_tok,
    grad_lat,
    grads,
    summed,
    gain_sums,
    wq,
    wo,
    wu,
    wd,
    xb,
    n1,
    proj,
    mixed,
    mid,
    n2,
    act,
    dup,
    yb,
    dy,
    ef,
    tmp,
    out,
    probs,
    probs_lat,
    scores,
    slopes,
    eye,
    turned,
    latf,
    mixf,
    key_mask,
    qbd,
    kbd,
    vbd,
    kv_all,
    kvg_send,
    kvg_recv,
    stage,
    gains,
    leaving,
    own_a,
    own_b,
    land1_a,
    land1_b,
    land2_a,
    land2_b,
    land3_a,
    land3_b,
    land4_a,
    land4_b,
    land_g,
    load_sem,
    stage_sem,
    own_sem,
    leave_sem,
    send_sem,
    recv_sem,
    gain_s,
    gain_r,
    relay_send,
    relay_recv,
    kv_sem_s,
    kv_sem_r,
    kvg_sem_s,
    kvg_sem_r,
):
    rows, width = xb.shape
    ff = act.shape[1]
    tok = tokens.shape[0]
    lat = latents.shape[0]
    half = lat // LAT
    pairs = width // 128
    me = lax.axis_index("dp")
    section = lax.axis_index("section")
    first = section == 0
    second = section == 1
    partner = (me, 1 - section)

    loads = [
        pltpu.make_async_copy(src, dst, load_sem.at[i])
        for i, (src, dst) in enumerate(((w_qkv, wq), (w_out, wo), (w_up, wu), (w_down, wd)))
    ]
    x_loads = [
        pltpu.make_async_copy(tokens, xb.at[0:tok], load_sem.at[4]),
        pltpu.make_async_copy(latents, xb.at[tok:rows], load_sem.at[5]),
    ]
    e_loads = [
        pltpu.make_async_copy(d_tokens, ef.at[0:tok], load_sem.at[6]),
        pltpu.make_async_copy(d_latents, ef.at[tok:rows], load_sem.at[7]),
    ]

    @pl.when(first)
    def _():
        for copy in x_loads:
            copy.start()

    for copy in loads:
        copy.start()

    @pl.when(second)
    def _():
        for copy in e_loads:
            copy.start()

    barrier = pltpu.get_barrier_semaphore()
    pl.semaphore_signal(barrier, inc=1, device_id=partner, device_id_type=MESH)

    here = [lax.rem(me // (1 << bit), 2) for bit in range(4)]

    def across(bit):
        return (me + (1 - 2 * here[bit]) * (1 << bit), section)

    @pl.when(second)
    def _():
        for shift in range(1, n):
            pl.semaphore_signal(
                barrier, inc=1, device_id=(lax.rem(me + shift, n), section), device_id_type=MESH
            )
        pl.semaphore_wait(barrier, n)

    @pl.when(first)
    def _():
        for bit in range(4):
            pl.semaphore_signal(barrier, inc=1, device_id=across(bit), device_id_type=MESH)
        pl.semaphore_wait(barrier, 5)

    forward_relay = pltpu.make_async_remote_copy(
        src_ref=yb, dst_ref=xb, send_sem=relay_send.at[0], recv_sem=relay_recv.at[0],
        device_id=partner, device_id_type=MESH,
    )
    backward_relay = pltpu.make_async_remote_copy(
        src_ref=yb, dst_ref=dy, send_sem=relay_send.at[1], recv_sem=relay_recv.at[1],
        device_id=partner, device_id_type=MESH,
    )

    def kv_copy(shift, incoming):
        slot = lax.rem(me + n - shift, n) if incoming else me
        return pltpu.make_async_remote_copy(
            src_ref=kv_all.at[me], dst_ref=kv_all.at[slot],
            send_sem=kv_sem_s.at[shift - 1], recv_sem=kv_sem_r.at[shift - 1],
            device_id=(lax.rem(me + shift, n), section), device_id_type=MESH,
        )

    def kvg_copy(shift):
        there = lax.rem(me + shift, n)
        return pltpu.make_async_remote_copy(
            src_ref=kvg_send.at[there], dst_ref=kvg_recv.at[shift - 1],
            send_sem=kvg_sem_s.at[shift - 1], recv_sem=kvg_sem_r.at[shift - 1],
            device_id=(there, section), device_id_type=MESH,
        )

    chunks = [slice(c, c + 64) for c in range(0, GROUP, 64)]
    lane = lax.broadcasted_iota(jnp.int32, (1, 128), 1)
    halves = [(lane < 64).astype(F32).astype(LOW), (lane >= 64).astype(F32).astype(LOW)]
    down = lax.broadcasted_iota(jnp.int32, (128, 1), 0)
    downs = [(down < 64).astype(F32).astype(LOW), (down >= 64).astype(F32).astype(LOW)]
    eighths = [(h.astype(F32) * 0.125).astype(LOW) for h in halves]
    heads = (
        lax.broadcasted_iota(jnp.int32, (HEAD_PAD, width), 1) // 64
        == lax.broadcasted_iota(jnp.int32, (HEAD_PAD, width), 0)
    ).astype(F32)

    def block_diagonal(dst, base, src, row, column, scale):
        for i in range(LAT):
            line = src[row + i : row + i + 1, column : column + width] * scale
            dst[base + i * HEAD_PAD : base + (i + 1) * HEAD_PAD, :] = (line * heads).astype(LOW)

    def head_sum(dst, row, column, value, scale, add):
        for i in range(LAT):
            line = jnp.sum(
                value[i * HEAD_PAD : (i + 1) * HEAD_PAD] * heads, axis=0, keepdims=True
            )
            line = line * scale
            if add:
                line = line + dst[row + i : row + i + 1, column : column + width]
            dst[row + i : row + i + 1, column : column + width] = line

    def bands(body, lo, hi, size):
        def one(i, carry):
            body(pl.ds(pl.multiple_of(lo + i * size, 16), size))
            return carry

        lax.fori_loop(0, (hi - lo) // size, one, 0)

    third = rows // 3
    corner = lax.broadcasted_iota(jnp.int32, (TILE // 3, TILE // 3), 0)
    eye[...] = (
        (corner == lax.broadcasted_iota(jnp.int32, (TILE // 3, TILE // 3), 1))
        .astype(F32)
        .astype(LOW)
    )

    def flip(a):
        side = a.shape[1]
        return nt(eye[0:side, 0:side], a).astype(LOW)

    def tn(a, b):
        return nn(flip(a), b)


    def grouped(body, lo, hi, count):
        def one(i, carry):
            base = lo + i * 16 * count
            body([pl.ds(pl.multiple_of(base + 16 * g, 16), 16) for g in range(count)])
            return carry

        lax.fori_loop(0, (hi - lo) // (16 * count), one, 0)

    def norm(load, gain, dst, lo, hi, count):
        def body(spans):
            means, scales = row_stats(load, spans)
            for r, mean, scale in zip(spans, means, scales):
                dst[r, :] = ((load(r) - mean) * scale * gain[...]).astype(LOW)

        grouped(body, lo, hi, count)

    def norm_back(load, grad, gain, gain_rows, store, lo, hi, count):
        def body(spans):
            means, scales = row_stats(load, spans)
            firsts, seconds = [], []
            kept = gains[0, gain_rows, :]
            for r, mean, scale in zip(spans, means, scales):
                along = grad[r, :] * ((load(r) - mean) * scale)
                kept = kept + along[0:8] + along[8:16]
                firsts.append(row_mean(grad[r, :] * gain[...]))
                seconds.append(row_mean(along * gain[...]))
            gains[0, gain_rows, :] = kept
            for r, mean, scale, one, two in zip(spans, means, scales, firsts, seconds):
                hat = (load(r) - mean) * scale
                store(r, ef[r, :] + scale * (grad[r, :] * gain[...] - one - hat * two))

        grouped(body, lo, hi, count)

    def tiles(count, body, size=TILE):
        def one(i, carry):
            body(at(i * size, size))
            return carry

        lax.fori_loop(0, count, one, 0)

    @pl.when(first)
    def _():
        for copy in x_loads:
            copy.wait()

    @pl.when(second)
    def _():
        spots = lax.broadcasted_iota(jnp.int32, (n, n * lat), 1) // lat
        spread_out = (spots == lax.broadcasted_iota(jnp.int32, (n, n * lat), 0)).astype(F32)
        groups = nn(slots[...].astype(F32).astype(LOW), spread_out.astype(LOW))
        of_micro = lax.rem(lax.broadcasted_iota(jnp.int32, (1, n * lat), 1), lat) // LAT
        for m in range(half):
            images = jnp.zeros((1, n * lat), F32)
            own_image = jnp.float32(0)
            end = jnp.int32(0)
            for i in range(image_at.shape[1]):
                end = end + image_at[m, i]
                images += jnp.where(end.astype(F32) <= groups[m : m + 1], 1.0, 0.0)
                own_image += jnp.where(end <= slot_at[m, me], 1.0, 0.0)
            seen = (images == own_image) & (of_micro == m)
            key_mask[m : m + 1, :] = jnp.where(seen, 0.0, masked_score)
        forward_relay.wait_recv()

    def load_in(r):
        return xb[r, :].astype(F32)

    def load_mid(r):
        return mid[r, :]

    norm(load_in, gain_attn, n1, 0, rows, 11)
    loads[0].wait()

    @pl.when(second)
    def _():
        own = nn(n1[tok:rows, :], wq[:, width:]).astype(LOW)
        kv_all[me] = own
        latf[:, width:] = own.astype(F32)
        for shift in range(1, n):
            kv_copy(shift, False).start()

    def project(c):
        proj[:, c] = nn(n1[...], wq[:, c]).astype(LOW)

    per = width // TILE
    tiles(jnp.where(first, 3 * per, per), project)

    def lat_bias(m, shape, axis):
        return jnp.where(
            lax.broadcasted_iota(jnp.int32, shape, axis) // LAT == m, 0.0, masked_score
        ).astype(F32)

    @pl.when(first)
    def _():
        latf[...] = proj[tok:rows, :].astype(F32)

        def one_pair(it, side):
            m, p = it // pairs, lax.rem(it, pairs)
            r = at(m * GROUP, GROUP)
            q = proj[r, at(p * 128, 128)]
            k = proj[r, at(width + p * 128, 128)]
            v = proj[r, at(2 * width + p * 128, 128)]
            kl = proj[tok:rows, at(width + p * 128, 128)]
            vl = proj[tok:rows, at(2 * width + p * 128, 128)]
            bias = lat_bias(m, (lat, GROUP), 0)
            vt, vlt = flip(v), flip(vl)
            total = jnp.zeros((128, GROUP), F32)
            for e in (0, 1):
                qe = q * eighths[e]
                s = scores.at[2 * side + e]
                s[...] = nt(k, qe)
                sl = nt(kl, qe) + bias
                top = jnp.max(sl, axis=0, keepdims=True)
                for c in chunks:
                    top = jnp.maximum(top, jnp.max(s[c, :], axis=0, keepdims=True))
                el = jnp.exp(sl - top)
                whole_sum = jnp.sum(el, axis=0, keepdims=True)
                for c in chunks:
                    et = jnp.exp(s[c, :] - top)
                    s[c, :] = et
                    whole_sum += jnp.sum(et, axis=0, keepdims=True)
                scale = 1.0 / whole_sum
                for c in chunks:
                    probs[2 * it + e, c, :] = (s[c, :] * scale).astype(LOW)
                pe = (el * scale).astype(LOW)
                probs[2 * it + e, GROUP : GROUP + lat, :] = pe
                total += nn(vt * downs[e], probs[2 * it + e, 0:GROUP, :])
                total += nn(vlt * downs[e], pe)
            mixed[r, at(p * 128, 128)] = nt(eye[...], total.astype(LOW)).astype(LOW)

        def pair(i, carry):
            one_pair(2 * i, 0)
            one_pair(2 * i + 1, 1)
            return carry

        lax.fori_loop(0, half * pairs // 2, pair, 0)
        for m in range(half):
            r = slice(m * GROUP, (m + 1) * GROUP)
            b = slice(m * 128, (m + 1) * 128)
            block_diagonal(qbd, m * 128, latf, m * LAT, 0, 0.125)
            s = nt(qbd[b, :], proj[r, width : 2 * width])
            sl = nt(qbd[b, :], proj[tok:rows, width : 2 * width]) + lat_bias(m, (128, lat), 1)
            top = jnp.maximum(
                jnp.max(s, axis=1, keepdims=True), jnp.max(sl, axis=1, keepdims=True)
            )
            et = jnp.exp(s - top)
            el = jnp.exp(sl - top)
            scale = 1.0 / (
                jnp.sum(et, axis=1, keepdims=True) + jnp.sum(el, axis=1, keepdims=True)
            )
            pt = (et * scale).astype(LOW)
            pe = (el * scale).astype(LOW)
            probs_lat[b, 0:GROUP] = pt
            probs_lat[b, GROUP : GROUP + lat] = pe
            o = nn(pt, proj[r, 2 * width :]) + nn(pe, proj[tok:rows, 2 * width :])
            head_sum(mixf, m * LAT, 0, o, 1.0, False)
        mixed[tok:rows, :] = mixf[...].astype(LOW)

    keys = n * lat

    @pl.when(second)
    def _():
        latf[:, :width] = proj[tok:rows, :width].astype(F32)
        for m in range(half):
            r = slice(m * GROUP, (m + 1) * GROUP)
            b = slice(m * 128, (m + 1) * 128)
            block_diagonal(qbd, m * 128, latf, m * LAT, 0, 0.125)
            block_diagonal(kbd, m * 128, latf, m * LAT, width, 1.0)
            block_diagonal(vbd, m * 128, latf, m * LAT, 2 * width, 1.0)
            s = nt(proj[r, :width] * jnp.asarray(0.125, LOW), kbd[b, :])
            et = jnp.exp(s - class_max(s))
            pt = (et / class_sum(et)).astype(LOW)
            probs[m, 0:GROUP, 0:128] = pt
            mixed[r, :] = nn(pt, vbd[b, :]).astype(LOW)

    root = 0.7978845608028654

    def mlp_in(lo, hi, count):
        r0 = slice(lo, hi)
        mid[r0, :] = xb[r0, :].astype(F32) + nn(mixed[r0, :], wo[...])

        norm(load_mid, gain_mlp, n2, lo, hi, count)

        def widen(i, carry):
            c = at(i * 512, 512)
            tmp[r0, 0:512] = nn(n2[r0, :], wu[:, c])

            def gelu(spans):
                for r in spans:
                    up = tmp[r, 0:512]
                    square = up * up
                    t = jnp.tanh(up * (root + (root * 0.044715) * square))
                    gate = 0.5 + 0.5 * t
                    value = up * gate
                    slope = gate + (value + value) * (1.0 - gate) * (
                        root + (3.0 * root * 0.044715) * square
                    )
                    act[r, c] = value.astype(LOW)
                    dup[r, c] = slope.astype(LOW)

            grouped(gelu, lo, hi, count)
            return carry

        lax.fori_loop(0, ff // 512, widen, 0)

    for copy in loads[1:]:
        copy.wait()

    @pl.when(first)
    def _():
        mlp_in(0, rows, 11)

    @pl.when(second)
    def _():
        mlp_in(0, tok, 8)
        for shift in range(1, n):
            kv_copy(shift, True).wait_recv()
        k = kv_all[:, :, :width].reshape(keys, width)
        v = kv_all[:, :, width:].reshape(keys, width)
        for m in range(half):
            b = slice(m * 128, (m + 1) * 128)
            s = nt(qbd[b, :], k) + key_mask[m : m + 1, :]
            et = jnp.exp(s - jnp.max(s, axis=1, keepdims=True))
            pt = (et / jnp.sum(et, axis=1, keepdims=True)).astype(LOW)
            probs_lat[b, 0:keys] = pt
            head_sum(mixf, m * LAT, 0, nn(pt, v), 1.0, False)
        mixed[tok:rows, :] = mixf[...].astype(LOW)

        mlp_in(tok, rows, 1)

    out_copies = [
        pltpu.make_async_copy(out.at[0:tok], out_tok, load_sem.at[8]),
        pltpu.make_async_copy(out.at[tok:rows], out_lat, load_sem.at[9]),
    ]
    grad_copies = [
        pltpu.make_async_copy(out.at[0:tok], grad_tok, load_sem.at[8]),
        pltpu.make_async_copy(out.at[tok:rows], grad_lat, load_sem.at[9]),
    ]

    def layer_output(passed_on):
        def narrow(c):
            y = mid[:, c] + nn(act[...], wd[:, c])
            if passed_on:
                low = y.astype(LOW)
                yb[:, c] = low
                y = low.astype(F32)
            out[:, c] = y

        tiles(width // 256, narrow, 256)
        for copy in out_copies:
            copy.start()

    @pl.when(first)
    def _():
        layer_output(True)
        forward_relay.start()
        backward_relay.wait_recv()

        def widen_e(r):
            ef[r, :] = dy[r, :].astype(F32)

        bands(widen_e, 0, rows, third)

    @pl.when(second)
    def _():
        for copy in e_loads:
            copy.wait()

        def narrow_e(r):
            dy[r, :] = ef[r, :].astype(LOW)

        bands(narrow_e, 0, rows, third)

    part = 384
    unit = width // n
    many = part // unit

    def staged(slot, piece, chunk, share):
        return pltpu.make_async_copy(
            stage.at[slot, piece],
            grads.at[
                chunk,
                share // 8,
                lax.rem(share // 4, 2),
                lax.rem(share // 2, 2),
                lax.rem(share, 2),
            ],
            stage_sem.at[slot, piece],
        )

    def drain(slot):
        def one(piece, carry):
            staged(slot, piece, 0, 0).wait()
            return carry

        lax.fori_loop(0, many, one, 0)

    def weight_grad(place, start, count, depth, left, *rights):
        def one(i, carry):
            for lo in range(0, part, 128):
                turned[lo : lo + 128, 0:depth] = flip(left(i, lo))
            for at_right, right in enumerate(rights):
                tile = i * len(rights) + at_right
                slot = lax.rem(tile, 2)
                value = nn(turned[:, 0:depth], right(i)).astype(LOW)

                @pl.when(tile >= start * len(rights) + 2)
                def _():
                    drain(slot)

                for piece in range(many):
                    stage[slot, piece] = value[piece * unit : (piece + 1) * unit]
                    staged(slot, piece, *place(i, at_right, piece)).start()
            return carry

        lax.fori_loop(start, start + count, one, 0)
        for slot in (0, 1):
            drain(slot)

    orders = ((0, 2, 1, 3), (1, 2, 0, 3))
    own_buf = (own_a, own_b)
    land = (
        (land1_a, land1_b),
        (land2_a, land2_b),
        (land3_a, land3_b),
        (land4_a, land4_b),
    )
    spread_pairs = land1_a.shape[0]

    def source(stream, phase, k, theirs):
        pick = [(1 - here[bit]) if theirs else here[bit] for bit in orders[stream]]
        own_bit = [here[bit] for bit in orders[stream]]
        base = land[0][stream]
        if phase == 0:
            if stream == 0:
                return grads.at[2 * k, :, :, :, pick[0]]
            return grads.at[2 * k + 1, :, :, pick[0]]
        if phase == 1:
            return base.at[k, :, pick[1]]
        if phase == 2:
            return base.at[k, :, own_bit[1], pick[2]]
        return base.at[k, pick[3], own_bit[1], own_bit[2]]

    def copy_of(stream, phase, k):
        return pltpu.make_async_remote_copy(
            src_ref=source(stream, phase, k, True),
            dst_ref=land[phase][stream].at[k],
            send_sem=send_sem.at[stream, phase, k],
            recv_sem=recv_sem.at[stream, phase, k],
            device_id=across(orders[stream][phase]),
            device_id_type=MESH,
        )

    def own(stream, k):
        return pltpu.make_async_copy(
            source(stream, 0, k, False), own_buf[stream], own_sem.at[stream]
        )

    def leave(stream, k):
        slot = lax.rem(k, 2)
        return pltpu.make_async_copy(
            leaving.at[slot, stream], summed.at[2 * k + stream], leave_sem.at[slot, stream]
        )

    def launch(phase, k):
        for stream in (0, 1):
            copy_of(stream, phase, k).start()

    def absorb(phase, k):
        for stream in (0, 1):
            if phase == 0:
                own(stream, k).wait()
            copy_of(stream, phase, k).wait_recv()
            base, into = land[0][stream], land[phase][stream]
            mine = [here[bit] for bit in orders[stream]]
            if phase == 0:

                def add(i, carry):
                    for j in (0, 1):
                        for h in (0, 1):
                            total = own_buf[stream][i, j, h].astype(F32)
                            total += base[k, i, j, h].astype(F32)
                            base[k, i, j, h] = total.astype(LOW)
                    return carry

                lax.fori_loop(0, 2, add, 0)
            elif phase == 1:
                for i in (0, 1):
                    for h in (0, 1):
                        total = base[k, i, mine[1], h].astype(F32)
                        total += into[k, i, h].astype(F32)
                        base[k, i, mine[1], h] = total.astype(LOW)
            elif phase == 2:
                for i in (0, 1):
                    total = base[k, i, mine[1], mine[2]].astype(F32)
                    total += into[k, i].astype(F32)
                    base[k, i, mine[1], mine[2]] = total.astype(LOW)
            else:
                total = base[k, mine[3], mine[1], mine[2]].astype(F32)
                total += into[k].astype(F32)
                slot = lax.rem(k, 2)

                @pl.when(k >= 2)
                def _():
                    leave(stream, k - 2).wait()

                leaving[slot, stream] = total
                leave(stream, k).start()

    def start_own(k):
        for stream in (0, 1):
            own(stream, k).start()

    def relaunch(k, following=True):
        absorb(0, k)
        launch(1, k)
        if following:
            start_own(k + 1)

    def onward(phase, k):
        absorb(phase, k)
        if phase < 3:
            launch(phase + 1, k)

    wide = ff // width
    per_part = width // part

    def down_grad(pair):
        weight_grad(
            lambda i, right, piece: (2 * pair + right, i * many + piece),
            0,
            per_part,
            rows,
            lambda i, lo: dy[:, at(i * part + lo, 128)],
            lambda i: act[:, 2 * pair * width : (2 * pair + 1) * width],
            lambda i: act[:, (2 * pair + 1) * width : (2 * pair + 2) * width],
        )

    down_grad(0)
    launch(0, 0)
    start_own(0)
    down_grad(1)
    launch(0, 1)

    def unwiden(c):
        dup[:, c] = (nt(dy[...], wd[c, :]) * dup[:, c].astype(F32)).astype(LOW)

    tiles(ff // TILE, unwiden)
    weight_grad(
        lambda i, right, piece: (
            wide + lax.rem(i * many + piece, wide),
            (i * many + piece) // wide,
        ),
        0,
        ff // part,
        rows,
        lambda i, lo: dup[:, at(i * part + lo, 128)],
        lambda i: n2[...],
    )
    launch(0, 2)
    launch(0, 3)

    relaunch(0)

    def to_mid(c):
        tmp[:, c] = nt(dup[...], wu[c, :])

    tiles(width // 256, to_mid, 256)
    gains[0] = jnp.zeros_like(gains[0])

    def store_mid(r, total):
        ef[r, :] = total
        dy[r, :] = total.astype(LOW)

    norm_back(load_mid, tmp, gain_mlp, slice(8, 16), store_mid, 0, rows, 11)
    relaunch(1)

    @pl.when(first)
    def _():
        forward_relay.wait_send()

    def to_mix(c):
        yb[:, c] = nt(dy[...], wo[c, :]).astype(LOW)

    tiles(width // TILE, to_mix)
    mixf[...] = yb[tok:rows, :].astype(F32)

    @pl.when(second)
    def _():
        k = kv_all[:, :, :width].reshape(keys, width)
        v = kv_all[:, :, width:].reshape(keys, width)
        for m in range(half):
            b = slice(m * 128, (m + 1) * 128)
            block_diagonal(vbd.at[pl.ds(256, 256)], m * 128, mixf, m * LAT, 0, 1.0)
        both = slice(0, half * 128)
        do = vbd[256 : 256 + half * 128, :]
        pt = probs_lat[both, 0:keys]
        pf = pt.astype(F32)
        dp = nt(do, v)
        along = jnp.sum(pf * dp, axis=1, keepdims=True)
        ds = (pf * (dp - along)).astype(LOW)
        kvg_send[:, :, :width] = tn(ds, qbd[both, :]).astype(LOW).reshape(n, lat, width)
        kvg_send[:, :, width:] = tn(pt, do).astype(LOW).reshape(n, lat, width)
        for shift in range(1, n):
            kvg_copy(shift).start()
        dq = nn(ds, k)
        for m in range(half):
            head_sum(latf, m * LAT, 0, dq[m * 128 : (m + 1) * 128], 0.125, False)
        proj[tok:rows, :width] = latf[:, :width].astype(LOW)
        layer_output(False)

    onward(1, 0)
    relaunch(2)
    weight_grad(
        lambda i, right, piece: (2 * wide, i * many + piece),
        0,
        width // part,
        rows,
        lambda i, lo: dy[:, at(i * part + lo, 128)],
        lambda i: mixed[...],
    )
    for copy in out_copies:
        copy.wait()

    @pl.when(first)
    def _():
        for m in range(half):
            r = slice(m * GROUP, (m + 1) * GROUP)
            b = slice(m * 128, (m + 1) * 128)
            block_diagonal(vbd, m * 128, mixf, m * LAT, 0, 1.0)
            do = vbd[b, :]
            dp = nt(do, proj[r, 2 * width :])
            dl = nt(do, proj[tok:rows, 2 * width :])
            pt = probs_lat[b, 0:GROUP]
            pe = probs_lat[b, GROUP : GROUP + lat]
            pf = pt.astype(F32)
            pg = pe.astype(F32)
            along = jnp.sum(pf * dp, axis=1, keepdims=True) + jnp.sum(
                pg * dl, axis=1, keepdims=True
            )
            ds = (pf * (dp - along)).astype(LOW)
            dsl = (pg * (dl - along)).astype(LOW)
            dq = nn(ds, proj[r, width : 2 * width]) + nn(dsl, proj[tok:rows, width : 2 * width])
            head_sum(latf, m * LAT, 0, dq, 0.125, False)
            tmp[r, :] = tn(ds, qbd[b, :])
            out[r, :] = tn(pt, do)
            if m == 0:
                tmp[tok:rows, :] = tn(dsl, qbd[b, :])
                out[tok:rows, :] = tn(pe, do)
            else:
                tmp[tok:rows, :] += tn(dsl, qbd[b, :])
                out[tok:rows, :] += tn(pe, do)
        proj[tok:rows, :width] = latf[:, :width].astype(LOW)

        def one_pair(it, side):
            m, p = it // pairs, lax.rem(it, pairs)
            r = at(m * GROUP, GROUP)
            qc = at(p * 128, 128)
            q = proj[r, qc]
            k = proj[r, at(width + p * 128, 128)]
            v = proj[r, at(2 * width + p * 128, 128)]
            kl = proj[tok:rows, at(width + p * 128, 128)]
            vl = proj[tok:rows, at(2 * width + p * 128, 128)]
            dx = yb[r, qc]
            kt, klt = flip(k), flip(kl)
            dq = jnp.zeros((128, GROUP), F32)
            dk = tmp[r, qc]
            dv = out[r, qc]
            dkl = tmp[tok:rows, qc]
            dvl = out[tok:rows, qc]
            for e in (0, 1):
                qe = q * eighths[e]
                de = dx * halves[e]
                s = scores.at[2 * side + e]
                s[...] = nt(v, de)
                dl = nt(vl, de)
                pt = probs[2 * it + e, 0:GROUP, :]
                pe = probs[2 * it + e, GROUP : GROUP + lat, :]
                pg = pe.astype(F32)
                along = jnp.sum(pg * dl, axis=0, keepdims=True)
                for c in chunks:
                    pf = probs[2 * it + e, c, :].astype(F32)
                    along += jnp.sum(pf * s[c, :], axis=0, keepdims=True)
                for c in chunks:
                    pf = probs[2 * it + e, c, :].astype(F32)
                    slopes[2 * side + e, c, :] = (pf * (s[c, :] - along)).astype(LOW)
                ds = slopes[2 * side + e]
                dsl = (pg * (dl - along)).astype(LOW)
                dq += nn(kt * downs[e], ds) + nn(klt * downs[e], dsl)
                dk += nn(ds, qe)
                dkl += nn(dsl, qe)
                dv += nn(pt, de)
                dvl += nn(pe, de)
            proj[r, qc] = nt(eye[...], (dq * 0.125).astype(LOW)).astype(LOW)
            proj[r, at(width + p * 128, 128)] = dk.astype(LOW)
            proj[r, at(2 * width + p * 128, 128)] = dv.astype(LOW)
            tmp[tok:rows, qc] = dkl
            out[tok:rows, qc] = dvl

        def pair(i, carry):
            one_pair(2 * i, 0)
            one_pair(2 * i + 1, 1)
            return carry

        lax.fori_loop(0, half * pairs // 2, pair, 0)
        proj[tok:rows, width : 2 * width] = tmp[tok:rows, :].astype(LOW)
        proj[tok:rows, 2 * width :] = out[tok:rows, :].astype(LOW)

    @pl.when(second)
    def _():
        for m in range(half):
            r = slice(m * GROUP, (m + 1) * GROUP)
            b = slice(m * 128, (m + 1) * 128)
            pt = probs[m, 0:GROUP, 0:128]
            pf = pt.astype(F32)
            dx = yb[r, :]
            dp = nt(dx, vbd[b, :])
            ds = (pf * (dp - class_sum(pf * dp))).astype(LOW)
            dk = tn(ds, proj[r, :width])
            dv = tn(pt, dx)
            proj[r, :width] = (nn(ds, kbd[b, :]) * 0.125).astype(LOW)
            head_sum(latf, m * LAT, width, dk, 0.125, False)
            head_sum(latf, m * LAT, 2 * width, dv, 1.0, False)
        total = latf[:, width:] + kvg_send[me].astype(F32)
        for shift in range(1, n):
            kvg_copy(shift).wait_recv()
            total += kvg_recv[shift - 1].astype(F32)
        proj[tok:rows, width:] = total.astype(LOW)

    onward(1, 1)
    relaunch(3, False)

    @pl.when(first)
    def _():
        def to_in(c):
            tmp[:, c] = nt(proj[...], wq[c, :])

        tiles(width // 256, to_in, 256)

    @pl.when(second)
    def _():
        tmp[0:tok, :] = nt(proj[0:tok, :width], wq[:, :width])
        tmp[tok:rows, :] = nt(proj[tok:rows, :], wq[...])

    def store_in(r, total):
        low = total.astype(LOW)
        yb[r, :] = low
        out[r, :] = jnp.where(first, total, low.astype(F32))

    norm_back(load_in, tmp, gain_attn, slice(0, 8), store_in, 0, rows, 11)
    for copy in grad_copies:
        copy.start()
    onward(2, 0)
    onward(1, 2)

    @pl.when(second)
    def _():
        backward_relay.start()

    def qkv_grad(start, count, r):
        weight_grad(
            lambda i, right, piece: (
                2 * wide + 1 + lax.rem(i * many + piece, 3),
                (i * many + piece) // 3,
            ),
            start,
            count,
            r.stop - r.start,
            lambda i, lo: proj[r, at(i * part + lo, 128)],
            lambda i: n1[r, :],
        )

    @pl.when(first)
    def _():
        qkv_grad(0, 3 * per_part, slice(0, rows))

    @pl.when(second)
    def _():
        qkv_grad(0, per_part, slice(0, rows))
        qkv_grad(per_part, 2 * per_part, slice(tok, rows))

    for pair in range(4, spread_pairs):
        launch(0, pair)
    start_own(4)

    def gain_copy(bit):
        return pltpu.make_async_remote_copy(
            src_ref=gains.at[bit],
            dst_ref=land_g.at[bit],
            send_sem=gain_s.at[bit],
            recv_sem=gain_r.at[bit],
            device_id=across(bit),
            device_id_type=MESH,
        )

    def gain_step(bit):
        gain_copy(bit).wait_recv()
        gains[bit + 1] = gains[bit] + land_g[bit]

    def each(lo, hi, phase):
        def one(i, carry):
            onward(phase, i)
            return carry

        lax.fori_loop(lo, hi, one, 0)

    gain_copy(0).start()
    onward(2, 1)
    onward(1, 3)
    relaunch(4)
    gain_step(0)
    gain_copy(1).start()
    each(0, 2, 3)
    each(2, 4, 2)
    relaunch(5, False)
    gain_step(1)
    gain_copy(2).start()
    each(4, 6, 1)
    each(2, 4, 3)
    gain_step(2)
    gain_copy(3).start()
    each(4, 6, 2)
    gain_step(3)
    each(4, 6, 3)
    final = gains[4]
    for i in (0, 1):
        whole_gain = jnp.sum(final[8 * i : 8 * i + 8], axis=0, keepdims=True)
        whole_gain = jnp.broadcast_to(whole_gain, (8, width))
        rolled = pltpu.roll(whole_gain, lax.rem(width - me * unit, width), 1)
        gain_sums[8 * i : 8 * i + 8, :] = rolled[:, 0:128]

    def finish(k, carry):
        for stream in (0, 1):
            for phase in range(4):
                copy_of(stream, phase, k).wait_send()
        return carry

    lax.fori_loop(0, spread_pairs, finish, 0)
    for bit in range(4):
        gain_copy(bit).wait_send()
    for copy in grad_copies:
        copy.wait()
    for stream in (0, 1):
        for pair in (spread_pairs - 2, spread_pairs - 1):
            leave(stream, pair).wait()

    @pl.when(second)
    def _():
        backward_relay.wait_send()
        for shift in range(1, n):
            kv_copy(shift, False).wait_send()
            kvg_copy(shift).wait_send()


def both_layers(n, tokens, latents, slots, images, gains, weights, d_tokens, d_latents):
    tok, width = tokens.shape
    lat = latents.shape[0]
    rows = tok + lat
    w_qkv, w_out, w_up, w_down = weights
    ff = w_up.shape[1]
    keys = n * lat
    half = lat // LAT
    size = sum(w.size for w in weights)
    chunks = size // (width * width)
    pairs = chunks // 2
    unit = width // n
    vm, hbm = pl.BlockSpec(memory_space=pltpu.VMEM), pl.BlockSpec(memory_space=pl.ANY)
    sm = pl.BlockSpec(memory_space=pltpu.SMEM)
    scratch = [
        pltpu.VMEM(w.shape, LOW) for w in (w_qkv, w_out, w_up, w_down)
    ] + [
        pltpu.VMEM(shape, dtype)
        for shape, dtype in (
            ((rows, width), LOW),
            ((rows, width), LOW),
            ((rows, 3 * width), LOW),
            ((rows, width), LOW),
            ((rows, width), F32),
            ((rows, width), LOW),
            ((rows, ff), LOW),
            ((rows, ff), LOW),
            ((rows, width), LOW),
            ((rows, width), LOW),
            ((rows, width), F32),
            ((rows, width), F32),
            ((rows, width), F32),
            ((half * width // 64, GROUP + lat, GROUP), LOW),
            ((half * 128, max(keys, GROUP + 128)), LOW),
            ((4, GROUP, GROUP), F32),
            ((4, GROUP, GROUP), LOW),
            ((256, 256), LOW),
            ((384, rows), LOW),
            ((lat, 3 * width), F32),
            ((lat, width), F32),
            ((8, keys), F32),
            ((half * 128, width), LOW),
            ((half * 128, width), LOW),
            ((half * 256, width), LOW),
            ((n, lat, 2 * width), LOW),
            ((n, lat, 2 * width), LOW),
            ((n - 1, lat, 2 * width), LOW),
            ((2, 384 // unit, unit, width), LOW),
            ((5, 16, width), F32),
            ((2, 2, unit, width), F32),
            ((2, 2, 2, unit, width), LOW),
            ((2, 2, 2, unit, width), LOW),
            ((pairs, 2, 2, 2, unit, width), LOW),
            ((pairs, 2, 2, 2, unit, width), LOW),
            ((pairs, 2, 2, unit, width), LOW),
            ((pairs, 2, 2, unit, width), LOW),
            ((pairs, 2, unit, width), LOW),
            ((pairs, 2, unit, width), LOW),
            ((pairs, unit, width), LOW),
            ((pairs, unit, width), LOW),
            ((4, 16, width), F32),
        )
    ] + [
        pltpu.SemaphoreType.DMA((10,)),
        pltpu.SemaphoreType.DMA((2, 384 // unit)),
        pltpu.SemaphoreType.DMA((2,)),
        pltpu.SemaphoreType.DMA((2, 2)),
        pltpu.SemaphoreType.DMA((2, 4, pairs)),
        pltpu.SemaphoreType.DMA((2, 4, pairs)),
        pltpu.SemaphoreType.DMA((4,)),
        pltpu.SemaphoreType.DMA((4,)),
        pltpu.SemaphoreType.DMA((2,)),
        pltpu.SemaphoreType.DMA((2,)),
        pltpu.SemaphoreType.DMA((n - 1,)),
        pltpu.SemaphoreType.DMA((n - 1,)),
        pltpu.SemaphoreType.DMA((n - 1,)),
        pltpu.SemaphoreType.DMA((n - 1,)),
    ]
    return pl.pallas_call(
        functools.partial(layer_kernel, n),
        out_shape=(
            jax.ShapeDtypeStruct((tok, width), F32),
            jax.ShapeDtypeStruct((lat, width), F32),
            jax.ShapeDtypeStruct((tok, width), F32),
            jax.ShapeDtypeStruct((lat, width), F32),
            jax.ShapeDtypeStruct((chunks, 2, 2, 2, 2, unit, width), LOW),
            jax.ShapeDtypeStruct((chunks, unit, width), F32),
            jax.ShapeDtypeStruct((16, 128), F32),
        ),
        in_specs=[hbm, hbm, vm, sm, sm, vm, vm] + [hbm] * 6,
        out_specs=(hbm,) * 6 + (vm,),
        scratch_shapes=scratch,
        compiler_params=pltpu.CompilerParams(
            collective_id=1, has_side_effects=True, vmem_limit_bytes=63 * 1024 * 1024
        ),
        cost_estimate=pl.CostEstimate(
            flops=6 * rows * size, bytes_accessed=4 * size, transcendentals=0
        ),
    )(tokens, latents, slots, slots, images, *gains, *weights, d_tokens, d_latents)


def finish_kernel(width, *refs):
    rows_in, (summed, gains), rows_out = refs[0:4], refs[4:6], refs[6:10]
    gain_attn, g_qkv, g_out, gain_mlp, g_up, g_down = refs[10:16]
    held, (sem_in, sem_out) = refs[16:21], refs[21:23]
    wide = g_down.shape[1] // width
    unit = g_out.shape[1]
    loads = [
        pltpu.make_async_copy(src, dst, sem_in.at[i])
        for i, (src, dst) in enumerate(zip((*rows_in, summed), held))
    ]
    for load in loads:
        load.start()
    all_rows, sums = held[0:4], held[4]
    moves = [[pair] for pair in zip(all_rows, rows_out)] + [
        [(sums.at[c], g_down.at[:, c * width : (c + 1) * width]) for c in range(wide)]
        + [
            (sums.at[wide : 2 * wide], g_up),
            (sums.at[2 * wide : 2 * wide + 1], g_out),
            (sums.at[2 * wide + 1 :], g_qkv),
        ]
    ]
    gain_attn[...] = gains[0:1, 0:unit]
    gain_mlp[...] = gains[8:9, 0:unit]
    started = []
    for load, group in zip(loads, moves):
        load.wait()
        for src, dst in group:
            started.append(pltpu.make_async_copy(src, dst, sem_out.at[len(started)]))
            started[-1].start()
    for move in started:
        move.wait()


def finished(rows, summed, gains, wide):
    chunks, unit, width = summed.shape
    hbm, vm = pl.BlockSpec(memory_space=pl.ANY), pl.BlockSpec(memory_space=pltpu.VMEM)
    shapes = [r.shape for r in rows] + [
        (1, unit),
        (3, unit, width),
        (1, unit, width),
        (1, unit),
        (wide, unit, width),
        (unit, wide * width),
    ]
    return pl.pallas_call(
        functools.partial(finish_kernel, width),
        out_shape=tuple(jax.ShapeDtypeStruct(s, F32) for s in shapes),
        in_specs=[hbm] * 5 + [vm],
        out_specs=(hbm,) * 4 + (vm, hbm, hbm, vm, hbm, hbm),
        scratch_shapes=[pltpu.VMEM(x.shape, F32) for x in (*rows, summed)]
        + [pltpu.SemaphoreType.DMA((5,)), pltpu.SemaphoreType.DMA((7 + wide,))],
        compiler_params=pltpu.CompilerParams(vmem_limit_bytes=62 * 1024 * 1024),
    )(*rows, summed, gains)
def fused_shards(
    unused_grid,
    tokens,
    latents,
    slot_group,
    image_groups,
    gain_attn,
    w_qkv,
    w_out,
    gain_mlp,
    w_up,
    w_down,
    d_tokens,
    d_latents,
):
    micro, tok, width = tokens.shape
    lat = latents.shape[1]
    out_tok, out_lat, grad_tok, grad_lat, unused_grads, summed, gains = both_layers(
        slot_group.shape[1],
        tokens.reshape(micro * tok, width),
        latents.reshape(micro * lat, width),
        slot_group,
        image_groups,
        (gain_attn, gain_mlp),
        (w_qkv[0], w_out[0], w_up[0], w_down[0]),
        d_tokens.reshape(micro * tok, width),
        d_latents.reshape(micro * lat, width),
    )
    wide = w_up.shape[2] // width
    rows = (out_tok, out_lat, grad_tok, grad_lat)
    *rows, first_gain, qkv, out, second_gain, up, down = finished(rows, summed, gains, wide)
    return (
        rows[0].reshape(1, micro, tok, width),
        rows[1].reshape(1, micro, lat, width),
        rows[2].reshape(1, micro, tok, width),
        rows[3].reshape(1, micro, lat, width),
        first_gain,
        qkv.reshape(-1, width).T[None],
        out.reshape(-1, width).T[None],
        second_gain,
        up.reshape(-1, width).T[None],
        down.T[None],
    )

def solution(mesh):
    in_specs = (
        P(None, "dp", None),
        P(None, "dp", None),
        P(),
        P(),
        P("section", None),
        P("section", None, None),
        P("section", None, None),
        P("section", None),
        P("section", None, None),
        P("section", None, None),
        P(None, "dp", None),
        P(None, "dp", None),
    )
    out_specs = (
        P("section", None, "dp", None),
        P("section", None, "dp", None),
        P("section", None, "dp", None),
        P("section", None, "dp", None),
        P("section", "dp"),
        P("section", None, "dp"),
        P("section", None, "dp"),
        P("section", "dp"),
        P("section", None, "dp"),
        P("section", None, "dp"),
    )
    grid = grid_of(mesh)

    def program(*args):
        n, width = mesh.shape["dp"], args[0].shape[2]
        one_group = args[0].shape[1] == n * GROUP
        body = fused_shards if one_group and n == 16 and width % (16 * n) == 0 else shards
        return jax.shard_map(
            functools.partial(body, grid), mesh=mesh, in_specs=in_specs, out_specs=out_specs, check_vma=False
        )(*args)

    return program
```

```python
import functools

import jax
import jax.numpy as jnp
from jax import lax
from jax.experimental import pallas as pl
from jax.experimental.pallas import tpu as pltpu
from jax.sharding import PartitionSpec as P

HEADS = 12
GROUP = 256
LAT = 8


epsilon = 1e-05
masked_score = -1e30


MESH = pl.DeviceIdType.MESH


def grid_of(mesh):
    n = mesh.shape["dp"]
    coords = [getattr(d, "coords", None) for d in mesh.devices.reshape(n, -1)[:, 0]]
    if any(c is None for c in coords):
        return (n // 4, 2, 2) if n % 4 == 0 else (n, 1, 1)
    sizes = {a: len({c[a] for c in coords}) for a in range(3)}
    strides = {
        a: min([i for i in range(n) if coords[i][a] != coords[0][a]], default=n) for a in range(3)
    }
    order = sorted(range(3), key=lambda a: -strides[a])
    return tuple(sizes[a] for a in order)


def spread_kernel(grid, pairs, g_ref, gain_ref, out_ref, gout_ref, *scratch):
    acc = scratch[0:3]
    land = [scratch[3 + 3 * i : 6 + 3 * i] for i in range(3)]
    send_sem, recv_sem, own_sem = scratch[12:15]
    me = lax.axis_index("dp")
    section = lax.axis_index("section")
    l0, l1, l2 = grid
    here = (me // (l1 * l2), lax.rem(me // l2, l1), lax.rem(me, l2))

    def device(axis, shift):
        there = list(here)
        there[axis] = lax.rem(here[axis] + shift, grid[axis])
        return there[axis], ((there[0] * l1 + there[1]) * l2 + there[2], section)

    barrier = pltpu.get_barrier_semaphore()
    for axis in range(3):
        for shift in range(1, grid[axis]):
            pl.semaphore_signal(
                barrier, inc=1, device_id=device(axis, shift)[1], device_id_type=MESH
            )
    pl.semaphore_wait(barrier, sum(grid) - 3)

    orders = ((2, 1, 0), (1, 2, 0), (2, 1, 0))

    def source(stream, phase, k, at):
        if phase == 0:
            if stream == 0:
                return g_ref.at[2 * k, :, :, at]
            if stream == 1:
                return g_ref.at[2 * k + 1, :, at]
            return gain_ref.at[:, :, at]
        if phase == 1:
            return acc[stream].at[k, :, at]
        return acc[stream].at[k, at, here[orders[stream][1]]]

    def copies(stream, phase, k):
        axis = orders[stream][phase]
        for shift in range(1, grid[axis]):
            at, target = device(axis, shift)
            yield pltpu.make_async_remote_copy(
                src_ref=source(stream, phase, k, at),
                dst_ref=land[phase][stream].at[k, shift - 1],
                send_sem=send_sem.at[stream, phase, k, shift - 1],
                recv_sem=recv_sem.at[stream, phase, k, shift - 1],
                device_id=target,
                device_id_type=MESH,
            )

    def own(stream, k):
        return pltpu.make_async_copy(
            source(stream, 0, k, here[orders[stream][0]]), acc[stream].at[k], own_sem.at[stream, k]
        )

    def launch(stream, phase, k):
        for copy in copies(stream, phase, k):
            copy.start()

    def absorb(stream, phase, k):
        axis = orders[stream][phase]
        if phase == 0:
            own(stream, k).wait()
        for copy in copies(stream, phase, k):
            copy.wait_recv()
        into = land[phase][stream]
        count = grid[axis] - 1
        if phase == 0:
            for a in range(acc[stream].shape[1]):
                for b in range(acc[stream].shape[2]):
                    total = acc[stream][k, a, b].astype(jnp.float32)
                    for s in range(count):
                        total += into[k, s, a, b].astype(jnp.float32)
                    acc[stream][k, a, b] = total.astype(acc[stream].dtype)
        elif phase == 1:
            mine = here[axis]
            for a in range(acc[stream].shape[1]):
                total = acc[stream][k, a, mine].astype(jnp.float32)
                for s in range(count):
                    total += into[k, s, a].astype(jnp.float32)
                acc[stream][k, a, mine] = total.astype(acc[stream].dtype)
        else:
            total = acc[stream][k, here[0], here[orders[stream][1]]].astype(jnp.float32)
            for s in range(count):
                total += into[k, s].astype(jnp.float32)
            if stream < 2:
                out_ref[2 * k + stream] = total
            else:
                gout_ref[...] = total

    own(2, 0).start()
    launch(2, 0, 0)

    def start_own(k, carry):
        for stream in (0, 1):
            own(stream, k).start()
        return carry

    for stream in (0, 1):
        launch(stream, 0, 0)
    lax.fori_loop(0, pairs, start_own, 0)

    def turn(t, carry):
        @pl.when(t + 1 < pairs)
        def _():
            for stream in (0, 1):
                launch(stream, 0, t + 1)

        @pl.when(t < pairs)
        def _():
            for stream in (0, 1):
                absorb(stream, 0, t)
                launch(stream, 1, t)

        @pl.when((t >= 1) & (t - 1 < pairs))
        def _():
            for stream in (0, 1):
                absorb(stream, 1, t - 1)
                launch(stream, 2, t - 1)

        @pl.when(t >= 2)
        def _():
            for stream in (0, 1):
                absorb(stream, 2, t - 2)

        return carry

    lax.fori_loop(0, pairs + 2, turn, 0)
    absorb(2, 0, 0)
    launch(2, 1, 0)
    absorb(2, 1, 0)
    launch(2, 2, 0)
    absorb(2, 2, 0)

    def finish(k, carry):
        for stream in (0, 1):
            for phase in range(3):
                for copy in copies(stream, phase, k):
                    copy.wait_send()
        return carry

    lax.fori_loop(0, pairs, finish, 0)
    for phase in range(3):
        for copy in copies(2, phase, 0):
            copy.wait_send()


def spread(grid, grads, gains):
    chunks, n, rows, width = grads.shape
    pairs = chunks // 2
    l0, l1, l2 = grid
    most = max(max(grid) - 1, 1)
    low = jnp.bfloat16
    shapes = ((pairs, rows, width, low), (pairs, rows, width, low), (1, 8, 128, jnp.float32))
    inner = ((l1, l2), (l2, l1), (l1, l2))
    acc, first, second, third = [], [], [], []
    for (count, r, w, dt), (kept, sent) in zip(shapes, inner):
        acc.append(pltpu.VMEM((count, l0, kept, r, w), dt))
        first.append(pltpu.VMEM((count, max(sent - 1, 1), l0, kept, r, w), dt))
        second.append(pltpu.VMEM((count, max(kept - 1, 1), l0, r, w), dt))
        third.append(pltpu.VMEM((count, max(l0 - 1, 1), r, w), dt))
    return pl.pallas_call(
        functools.partial(spread_kernel, grid, pairs),
        out_shape=(
            jax.ShapeDtypeStruct((chunks, rows, width), jnp.float32),
            jax.ShapeDtypeStruct((8, 128), jnp.float32),
        ),
        in_specs=[pl.BlockSpec(memory_space=pl.ANY)] * 2,
        out_specs=(pl.BlockSpec(memory_space=pltpu.VMEM),) * 2,
        scratch_shapes=acc
        + first
        + second
        + third
        + [
            pltpu.SemaphoreType.DMA((3, 3, pairs, most)),
            pltpu.SemaphoreType.DMA((3, 3, pairs, most)),
            pltpu.SemaphoreType.DMA((3, pairs)),
        ],
        compiler_params=pltpu.CompilerParams(
            collective_id=0, has_side_effects=True, vmem_limit_bytes=60 * 1024 * 1024
        ),
        cost_estimate=pl.CostEstimate(flops=0, bytes_accessed=grads.size * 4, transcendentals=0),
    )(grads.reshape(chunks, l0, l1, l2, rows, width), gains.reshape(l0, l1, l2, 8, 128))


def from_behind(x, axis, by):
    devices = lax.axis_size(axis)
    pairs = [(i, i + by) for i in range(devices) if 0 <= i + by < devices]
    return lax.ppermute(x, axis, pairs)


def layer_norm(values, gain):
    row_mean = jnp.mean(values, axis=-1, keepdims=True)
    centred = values - row_mean
    row_var = jnp.mean(centred * centred, axis=-1, keepdims=True)
    return centred * lax.rsqrt(row_var + epsilon) * gain


def front_half(all_rows, gain_attn, w_qkv):
    normed = layer_norm(all_rows, gain_attn).astype(jnp.bfloat16)
    projected = jnp.dot(normed, w_qkv, preferred_element_type=jnp.float32).astype(jnp.bfloat16)
    return (normed, projected)


def latent_operand(projected, tok_rows, model_width):
    return projected[tok_rows:, model_width:]


def back_half(all_rows, projected, remote_rows, allowed, weights):
    gain_attn, w_qkv, w_out, gain_mlp, w_up, w_down = weights
    row_count, model_width = all_rows.shape
    head_size = model_width // HEADS
    remote_pairs = remote_rows[:, remote_rows.shape[1] - 2 * model_width :]
    queries = projected[:, :model_width].reshape(row_count, HEADS, head_size)
    key_rows = jnp.concatenate(
        [projected[:, model_width : 2 * model_width], remote_pairs[:, :model_width]], axis=0
    )
    value_rows = jnp.concatenate(
        [projected[:, 2 * model_width :], remote_pairs[:, model_width:]], axis=0
    )
    key_rows = key_rows.reshape(-1, HEADS, head_size)
    value_rows = value_rows.reshape(-1, HEADS, head_size)
    scores = jnp.einsum(
        "qhd,khd->hqk", queries, key_rows, preferred_element_type=jnp.float32
    ) * head_size ** (-0.5)
    attn_weights = jax.nn.softmax(jnp.where(allowed[None], scores, masked_score), axis=-1)
    attn_low = attn_weights.astype(jnp.bfloat16)
    mixed_low = jnp.einsum("hqk,khd->qhd", attn_low, value_rows, preferred_element_type=jnp.float32)
    mixed_low = mixed_low.reshape(row_count, model_width).astype(jnp.bfloat16)
    mid_rows = all_rows + jnp.dot(mixed_low, w_out, preferred_element_type=jnp.float32)
    normed_mlp = layer_norm(mid_rows, gain_mlp).astype(jnp.bfloat16)
    up_proj = jnp.dot(normed_mlp, w_up, preferred_element_type=jnp.float32)
    activated = jax.nn.gelu(up_proj).astype(jnp.bfloat16)
    result = mid_rows + jnp.dot(activated, w_down, preferred_element_type=jnp.float32)
    return dict(
        queries=queries,
        key_rows=key_rows,
        value_rows=value_rows,
        attn_weights=attn_weights,
        attn_low=attn_low,
        mixed_low=mixed_low,
        mid_rows=mid_rows,
        normed_mlp=normed_mlp,
        up_proj=up_proj,
        activated=activated,
        result=result,
    )


def section_backward(saved, d_result, all_rows, normed, allowed, weights, latent_start):
    gain_attn, w_qkv, w_out, gain_mlp, w_up, w_down = weights
    row_count, model_width = all_rows.shape
    head_size = model_width // HEADS
    score_scale = head_size ** (-0.5)
    d_low = d_result.astype(jnp.bfloat16)
    grad_down = jnp.dot(d_low.T, saved["activated"], preferred_element_type=jnp.float32)
    d_activated = jnp.dot(d_low, w_down.T, preferred_element_type=jnp.float32)
    unused_up, gelu_back = jax.vjp(jax.nn.gelu, saved["up_proj"])
    d_up = gelu_back(d_activated)[0].astype(jnp.bfloat16)
    grad_up = jnp.dot(d_up.T, saved["normed_mlp"], preferred_element_type=jnp.float32)
    d_normed_mlp = jnp.dot(d_up, w_up.T, preferred_element_type=jnp.float32)
    unused_mid, second_back = jax.vjp(layer_norm, saved["mid_rows"], gain_mlp)
    d_mid_norm, grad_gain_mlp = second_back(d_normed_mlp)
    d_mid = d_result + d_mid_norm
    d_mid_low = d_mid.astype(jnp.bfloat16)
    grad_out = jnp.dot(d_mid_low.T, saved["mixed_low"], preferred_element_type=jnp.float32)
    d_mixed = jnp.dot(d_mid_low, w_out.T, preferred_element_type=jnp.float32).astype(jnp.bfloat16)
    d_mixed = d_mixed.reshape(row_count, HEADS, head_size)
    d_weights = jnp.einsum(
        "qhd,khd->hqk", d_mixed, saved["value_rows"], preferred_element_type=jnp.float32
    )
    d_values = jnp.einsum(
        "hqk,qhd->khd", saved["attn_low"], d_mixed, preferred_element_type=jnp.float32
    )
    attn_weights = saved["attn_weights"]
    d_scores = attn_weights * (
        d_weights - jnp.sum(attn_weights * d_weights, axis=-1, keepdims=True)
    )
    d_scores_low = jnp.where(allowed[None], d_scores, 0.0).astype(jnp.bfloat16)
    d_queries = (
        jnp.einsum(
            "hqk,khd->qhd", d_scores_low, saved["key_rows"], preferred_element_type=jnp.float32
        )
        * score_scale
    )
    d_keys = (
        jnp.einsum(
            "hqk,qhd->khd", d_scores_low, saved["queries"], preferred_element_type=jnp.float32
        )
        * score_scale
    )
    remote_part = jnp.concatenate(
        [
            d_keys[row_count:].reshape(-1, model_width),
            d_values[row_count:].reshape(-1, model_width),
        ],
        axis=1,
    )
    own_part = lax.psum_scatter(remote_part, "dp", scatter_dimension=0, tiled=True)
    local_pairs = jnp.concatenate(
        [
            d_keys[:row_count].reshape(row_count, model_width),
            d_values[:row_count].reshape(row_count, model_width),
        ],
        axis=1,
    )
    local_pairs = jnp.concatenate(
        [local_pairs[:latent_start], local_pairs[latent_start:] + own_part], axis=0
    )
    d_projected = jnp.concatenate(
        [d_queries.reshape(row_count, model_width), local_pairs], axis=1
    ).astype(jnp.bfloat16)
    grad_qkv = jnp.dot(d_projected.T, normed, preferred_element_type=jnp.float32)
    d_normed = jnp.dot(d_projected, w_qkv.T, preferred_element_type=jnp.float32)
    unused_rows, first_back = jax.vjp(layer_norm, all_rows, gain_attn)
    d_rows_norm, grad_gain_attn = first_back(d_normed)
    return (
        d_mid + d_rows_norm,
        (grad_gain_attn, grad_qkv, grad_out, grad_gain_mlp, grad_up, grad_down),
    )


def packed(grads, n):
    gain_first, qkv_grad, out_grad, gain_second, up_grad, down_grad = grads
    width = out_grad.shape[0]
    rows = width // n

    def by_rows(grad):
        return grad.reshape(n, -1, rows, width).transpose(1, 0, 2, 3).astype(jnp.bfloat16)

    down = down_grad.reshape(n, rows, -1, width).transpose(2, 0, 1, 3).astype(jnp.bfloat16)
    chunks = jnp.concatenate([down, by_rows(up_grad), by_rows(out_grad), by_rows(qkv_grad)], axis=0)
    gains = jnp.stack([gain_first.reshape(n, rows), gain_second.reshape(n, rows)], axis=1)
    return chunks, jnp.pad(gains, ((0, 0), (0, 6), (0, 128 - rows)))


def shards(
    grid,
    tokens,
    latents,
    slot_group,
    image_groups,
    gain_attn,
    w_qkv,
    w_out,
    gain_mlp,
    w_up,
    w_down,
    d_tokens,
    d_latents,
):
    micro = tokens.shape[0]
    tok_rows = tokens.shape[1]
    lat_rows = latents.shape[1]
    model_width = tokens.shape[2]
    local_groups = tok_rows // GROUP
    section_index = lax.axis_index("section")
    is_global = section_index == 1
    dp_index = lax.axis_index("dp")
    weights = (gain_attn[0], w_qkv[0], w_out[0], gain_mlp[0], w_up[0], w_down[0])
    image_ends = jnp.cumsum(image_groups, axis=1)
    slot_images = jnp.sum(
        (image_ends[:, None, :] <= slot_group[:, :, None]).astype(jnp.int32), axis=2
    )
    slot_total = slot_group.shape[1]
    row_group = jnp.concatenate([jnp.arange(tok_rows) // GROUP, jnp.arange(lat_rows) // LAT])
    row_latent = jnp.concatenate(
        [jnp.zeros((tok_rows,), jnp.bool_), jnp.ones((lat_rows,), jnp.bool_)]
    )
    same_group = row_group[:, None] == row_group[None, :]
    local_mask = jnp.where(
        is_global, (~row_latent)[:, None] & row_latent[None, :] & same_group, same_group
    )
    group_match = row_group[:, None] == jnp.arange(local_groups)[None, :]

    def key_images(batch):
        images_row = lax.dynamic_index_in_dim(slot_images, batch, 0, keepdims=False)
        return (images_row, jnp.broadcast_to(images_row[:, None], (slot_total, LAT)).reshape(-1))

    def allowed_for(batch):
        images_row, key_image = key_images(batch)
        own_images = lax.dynamic_slice_in_dim(images_row, dp_index * local_groups, local_groups)
        row_image = jnp.sum(jnp.where(group_match, own_images[None, :], 0), axis=1)
        remote_mask = is_global & row_latent[:, None] & (row_image[:, None] == key_image[None, :])
        return jnp.concatenate([local_mask, remote_mask], axis=1)

    def forward_turn(received, turn):
        recv_tokens, recv_latents = received
        batch = jnp.clip(turn - section_index, 0, micro - 1)
        own_tok = lax.dynamic_index_in_dim(tokens, batch, 0, keepdims=False)
        own_lat = lax.dynamic_index_in_dim(latents, batch, 0, keepdims=False)
        input_rows = jnp.concatenate(
            [
                jnp.where(is_global, recv_tokens, own_tok),
                jnp.where(is_global, recv_latents, own_lat),
            ],
            axis=0,
        )
        all_rows = input_rows.astype(jnp.float32)
        normed, projected = front_half(all_rows, weights[0], weights[1])
        remote_rows = lax.all_gather(
            latent_operand(projected, tok_rows, model_width), "dp", axis=0, tiled=True
        )
        saved = back_half(all_rows, projected, remote_rows, allowed_for(batch), weights)
        result = saved["result"]
        result_low = result.astype(jnp.bfloat16)
        stored = jnp.where(is_global, result, result_low.astype(jnp.float32))
        passed_on = from_behind((result_low[:tok_rows], result_low[tok_rows:]), "section", 1)
        return passed_on, (input_rows, stored[:tok_rows], stored[tok_rows:])

    nothing = (
        jnp.zeros((tok_rows, model_width), jnp.bfloat16),
        jnp.zeros((lat_rows, model_width), jnp.bfloat16),
    )
    turns = jnp.arange(micro + 1)
    unused_end, (kept_rows, tok_outputs, lat_outputs) = lax.scan(forward_turn, nothing, turns)

    def backward_turn(carry, turn):
        (recv_grad_tok, recv_grad_lat), totals = carry
        raw_batch = micro - turn - section_index
        valid = ((raw_batch >= 0) & (raw_batch < micro)).astype(jnp.float32)
        batch = jnp.clip(raw_batch, 0, micro - 1)
        all_rows = lax.dynamic_index_in_dim(
            kept_rows, batch + section_index, 0, keepdims=False
        ).astype(jnp.float32)
        normed, projected = front_half(all_rows, weights[0], weights[1])
        remote_rows = lax.all_gather(
            latent_operand(projected, tok_rows, model_width), "dp", axis=0, tiled=True
        )
        allowed = allowed_for(batch)
        saved = back_half(all_rows, projected, remote_rows, allowed, weights)
        given = (
            jnp.concatenate(
                [
                    lax.dynamic_index_in_dim(d_tokens, batch, 0, keepdims=False),
                    lax.dynamic_index_in_dim(d_latents, batch, 0, keepdims=False),
                ],
                axis=0,
            )
            * valid
        )
        passed = jnp.concatenate([recv_grad_tok, recv_grad_lat], axis=0).astype(jnp.float32)
        d_result = jnp.where(is_global, given, passed)
        d_rows, grads = section_backward(
            saved, d_result, all_rows, normed, allowed, weights, tok_rows
        )
        totals = tuple((accum + piece for accum, piece in zip(totals, grads)))
        d_rows_low = d_rows.astype(jnp.bfloat16)
        stored = jnp.where(is_global, d_rows_low.astype(jnp.float32), d_rows)
        sent = from_behind((d_rows_low[:tok_rows], d_rows_low[tok_rows:]), "section", -1)
        return (sent, totals), (stored[:tok_rows], stored[tok_rows:])

    totals = tuple(
        jnp.zeros(w.shape[::-1] if w.ndim == 2 else w.shape, jnp.float32) for w in weights
    )
    (unused_sent, totals), (tok_grads, lat_grads) = lax.scan(
        backward_turn, (nothing, totals), turns
    )
    chunks, gains = packed(totals, lax.axis_size("dp"))
    summed, gain_sums = spread(grid, chunks, gains)
    rows = summed.shape[1]
    layer_tokens = lax.dynamic_slice_in_dim(tok_outputs, section_index, micro, 0)[None]
    layer_latents = lax.dynamic_slice_in_dim(lat_outputs, section_index, micro, 0)[None]
    grad_tokens = lax.dynamic_slice_in_dim(tok_grads, 1 - section_index, micro, 0)[::-1][
        None
    ]
    grad_latents = lax.dynamic_slice_in_dim(lat_grads, 1 - section_index, micro, 0)[
        ::-1
    ][None]
    return (
        layer_tokens,
        layer_latents,
        grad_tokens,
        grad_latents,
        gain_sums[0:1, :rows],
        summed[9:].reshape(-1, model_width).T[None],
        summed[8].T[None],
        gain_sums[1:2, :rows],
        summed[4:8].reshape(-1, model_width).T[None],
        summed[0:4].transpose(0, 2, 1).reshape(-1, rows)[None],
    )


F32 = jnp.float32
LOW = jnp.bfloat16
HEAD_PAD = 16
TILE = 768


def nn(a, b):
    return jnp.dot(a, b, preferred_element_type=F32)


def nt(a, b):
    return lax.dot_general(a, b, (((1,), (1,)), ((), ())), preferred_element_type=F32)


def tn(a, b):
    return lax.dot_general(a, b, (((0,), (0,)), ((), ())), preferred_element_type=F32)


def row_mean(values):
    return jnp.mean(values, axis=-1, keepdims=True)


def row_stats(load, spans):
    means = [row_mean(load(r)) for r in spans]
    scales = []
    for r, mean in zip(spans, means):
        centred = load(r) - mean
        scales.append(lax.rsqrt(row_mean(centred * centred) + epsilon))
    return means, scales


def at(start, size):
    return pl.ds(pl.multiple_of(start, size), size)


def class_max(s):
    for by in (16, 32, 64):
        s = jnp.maximum(s, pltpu.roll(s, by, 1))
    return s


def class_sum(s):
    for by in (16, 32, 64):
        s = s + pltpu.roll(s, by, 1)
    return s


def layer_kernel(
    n,
    tokens,
    latents,
    slots,
    slot_at,
    image_at,
    gain_attn,
    gain_mlp,
    w_qkv,
    w_out,
    w_up,
    w_down,
    d_tokens,
    d_latents,
    out_tok,
    out_lat,
    grad_tok,
    grad_lat,
    grads,
    summed,
    gain_sums,
    wq,
    wo,
    wu,
    wd,
    xb,
    n1,
    proj,
    mixed,
    mid,
    n2,
    act,
    dup,
    yb,
    dy,
    ef,
    tmp,
    out,
    probs,
    probs_lat,
    scores,
    slopes,
    latf,
    mixf,
    key_mask,
    qbd,
    kbd,
    vbd,
    kv_all,
    kvg_send,
    kvg_recv,
    stage,
    gains,
    leaving,
    own_a,
    own_b,
    land1_a,
    land1_b,
    land2_a,
    land2_b,
    land3_a,
    land3_b,
    land4_a,
    land4_b,
    land_g,
    load_sem,
    stage_sem,
    own_sem,
    leave_sem,
    send_sem,
    recv_sem,
    gain_s,
    gain_r,
    relay_send,
    relay_recv,
    kv_sem_s,
    kv_sem_r,
    kvg_sem_s,
    kvg_sem_r,
):
    rows, width = xb.shape
    ff = act.shape[1]
    tok = tokens.shape[0]
    lat = latents.shape[0]
    half = lat // LAT
    pairs = width // 128
    me = lax.axis_index("dp")
    section = lax.axis_index("section")
    first = section == 0
    second = section == 1
    partner = (me, 1 - section)

    loads = [
        pltpu.make_async_copy(src, dst, load_sem.at[i])
        for i, (src, dst) in enumerate(((w_qkv, wq), (w_out, wo), (w_up, wu), (w_down, wd)))
    ]
    x_loads = [
        pltpu.make_async_copy(tokens, xb.at[0:tok], load_sem.at[4]),
        pltpu.make_async_copy(latents, xb.at[tok:rows], load_sem.at[5]),
    ]
    e_loads = [
        pltpu.make_async_copy(d_tokens, ef.at[0:tok], load_sem.at[6]),
        pltpu.make_async_copy(d_latents, ef.at[tok:rows], load_sem.at[7]),
    ]

    @pl.when(first)
    def _():
        for copy in x_loads:
            copy.start()

    for copy in loads:
        copy.start()

    @pl.when(second)
    def _():
        for copy in e_loads:
            copy.start()

    barrier = pltpu.get_barrier_semaphore()
    pl.semaphore_signal(barrier, inc=1, device_id=partner, device_id_type=MESH)

    here = [lax.rem(me // (1 << bit), 2) for bit in range(4)]

    def across(bit):
        return (me + (1 - 2 * here[bit]) * (1 << bit), section)

    @pl.when(second)
    def _():
        for shift in range(1, n):
            pl.semaphore_signal(
                barrier, inc=1, device_id=(lax.rem(me + shift, n), section), device_id_type=MESH
            )
        pl.semaphore_wait(barrier, n)

    @pl.when(first)
    def _():
        for bit in range(4):
            pl.semaphore_signal(barrier, inc=1, device_id=across(bit), device_id_type=MESH)
        pl.semaphore_wait(barrier, 5)

    def relay(back, band):
        low, high = ((0, rows // 3), (rows // 3, 2 * rows // 3), (2 * rows // 3, rows))[band]
        if not back:
            low, high = ((0, GROUP + lat), (GROUP + lat, rows))[band]
        return pltpu.make_async_remote_copy(
            src_ref=yb.at[low:high],
            dst_ref=(dy if back else xb).at[low:high],
            send_sem=relay_send.at[3 * back + band],
            recv_sem=relay_recv.at[3 * back + band],
            device_id=partner,
            device_id_type=MESH,
        )

    def kv_copy(shift, incoming):
        slot = lax.rem(me + n - shift, n) if incoming else me
        return pltpu.make_async_remote_copy(
            src_ref=kv_all.at[me], dst_ref=kv_all.at[slot],
            send_sem=kv_sem_s.at[shift - 1], recv_sem=kv_sem_r.at[shift - 1],
            device_id=(lax.rem(me + shift, n), section), device_id_type=MESH,
        )

    def kvg_copy(shift):
        there = lax.rem(me + shift, n)
        return pltpu.make_async_remote_copy(
            src_ref=kvg_send.at[there], dst_ref=kvg_recv.at[shift - 1],
            send_sem=kvg_sem_s.at[shift - 1], recv_sem=kvg_sem_r.at[shift - 1],
            device_id=(there, section), device_id_type=MESH,
        )

    chunks = [slice(c, c + 64) for c in range(0, GROUP, 64)]
    lane = lax.broadcasted_iota(jnp.int32, (1, 128), 1)
    halves = [(lane < 64).astype(F32).astype(LOW), (lane >= 64).astype(F32).astype(LOW)]
    eighths = [(h.astype(F32) * 0.125).astype(LOW) for h in halves]
    heads = (
        lax.broadcasted_iota(jnp.int32, (HEAD_PAD, width), 1) // 64
        == lax.broadcasted_iota(jnp.int32, (HEAD_PAD, width), 0)
    ).astype(F32)

    def block_diagonal(dst, base, src, row, column, scale):
        for i in range(LAT):
            line = src[row + i : row + i + 1, column : column + width] * scale
            dst[base + i * HEAD_PAD : base + (i + 1) * HEAD_PAD, :] = (line * heads).astype(LOW)

    def head_sum(dst, row, column, value, scale, add):
        for i in range(LAT):
            line = jnp.sum(
                value[i * HEAD_PAD : (i + 1) * HEAD_PAD] * heads, axis=0, keepdims=True
            )
            line = line * scale
            if add:
                line = line + dst[row + i : row + i + 1, column : column + width]
            dst[row + i : row + i + 1, column : column + width] = line

    def bands(body, lo, hi, size):
        def one(i, carry):
            body(pl.ds(pl.multiple_of(lo + i * size, 16), size))
            return carry

        lax.fori_loop(0, (hi - lo) // size, one, 0)

    third = rows // 3

    def grouped(body, lo, hi, count):
        def one(i, carry):
            base = lo + i * 16 * count
            body([pl.ds(pl.multiple_of(base + 16 * g, 16), 16) for g in range(count)])
            return carry

        lax.fori_loop(0, (hi - lo) // (16 * count), one, 0)

    def norm(load, gain, dst, lo, hi, count):
        def body(spans):
            means, scales = row_stats(load, spans)
            for r, mean, scale in zip(spans, means, scales):
                dst[r, :] = ((load(r) - mean) * scale * gain[...]).astype(LOW)

        grouped(body, lo, hi, count)

    def norm_back(load, grad, gain, gain_rows, store, lo, hi, count):
        def body(spans):
            means, scales = row_stats(load, spans)
            firsts, seconds = [], []
            kept = gains[0, gain_rows, :]
            for r, mean, scale in zip(spans, means, scales):
                along = grad[r, :] * ((load(r) - mean) * scale)
                kept = kept + along[0:8] + along[8:16]
                firsts.append(row_mean(grad[r, :] * gain[...]))
                seconds.append(row_mean(along * gain[...]))
            gains[0, gain_rows, :] = kept
            for r, mean, scale, one, two in zip(spans, means, scales, firsts, seconds):
                hat = (load(r) - mean) * scale
                store(r, ef[r, :] + scale * (grad[r, :] * gain[...] - one - hat * two))

        grouped(body, lo, hi, count)

    def tiles(count, body, size=TILE):
        def one(i, carry):
            body(at(i * size, size))
            return carry

        lax.fori_loop(0, count, one, 0)

    @pl.when(first)
    def _():
        for copy in x_loads:
            copy.wait()

    @pl.when(second)
    def _():
        spots = lax.broadcasted_iota(jnp.int32, (n, n * lat), 1) // lat
        spread_out = (spots == lax.broadcasted_iota(jnp.int32, (n, n * lat), 0)).astype(F32)
        groups = nn(slots[...].astype(F32).astype(LOW), spread_out.astype(LOW))
        of_micro = lax.rem(lax.broadcasted_iota(jnp.int32, (1, n * lat), 1), lat) // LAT
        for m in range(half):
            images = jnp.zeros((1, n * lat), F32)
            own_image = jnp.float32(0)
            end = jnp.int32(0)
            for i in range(image_at.shape[1]):
                end = end + image_at[m, i]
                images += jnp.where(end.astype(F32) <= groups[m : m + 1], 1.0, 0.0)
                own_image += jnp.where(end <= slot_at[m, me], 1.0, 0.0)
            seen = (images == own_image) & (of_micro == m)
            key_mask[m : m + 1, :] = jnp.where(seen, 0.0, masked_score)
        for band in (0, 1):
            relay(0, band).wait_recv()

    def load_in(r):
        return xb[r, :].astype(F32)

    def load_mid(r):
        return mid[r, :]

    norm(load_in, gain_attn, n1, 0, rows, 11)
    loads[0].wait()

    @pl.when(second)
    def _():
        own = nn(n1[tok:rows, :], wq[:, width:]).astype(LOW)
        kv_all[me] = own
        latf[:, width:] = own.astype(F32)
        for shift in range(1, n):
            kv_copy(shift, False).start()

    def project(c):
        proj[:, c] = nn(n1[...], wq[:, c]).astype(LOW)

    per = width // TILE
    tiles(jnp.where(first, 3 * per, per), project)

    def lat_bias(m, shape, axis):
        return jnp.where(
            lax.broadcasted_iota(jnp.int32, shape, axis) // LAT == m, 0.0, masked_score
        ).astype(F32)

    @pl.when(first)
    def _():
        latf[...] = proj[tok:rows, :].astype(F32)

        def one_pair(it, side):
            m, p = it // pairs, lax.rem(it, pairs)
            r = at(m * GROUP, GROUP)
            q = proj[r, at(p * 128, 128)]
            k = proj[r, at(width + p * 128, 128)]
            v = proj[r, at(2 * width + p * 128, 128)]
            kl = proj[tok:rows, at(width + p * 128, 128)]
            vl = proj[tok:rows, at(2 * width + p * 128, 128)]
            bias = lat_bias(m, (lat, GROUP), 0)
            total = jnp.zeros((GROUP, 128), F32)
            for e in (0, 1):
                qe = q * eighths[e]
                s = scores.at[2 * side + e]
                s[...] = nt(k, qe)
                sl = nt(kl, qe) + bias
                top = jnp.max(sl, axis=0, keepdims=True)
                for c in chunks:
                    top = jnp.maximum(top, jnp.max(s[c, :], axis=0, keepdims=True))
                el = jnp.exp(sl - top)
                whole_sum = jnp.sum(el, axis=0, keepdims=True)
                for c in chunks:
                    et = jnp.exp(s[c, :] - top)
                    s[c, :] = et
                    whole_sum += jnp.sum(et, axis=0, keepdims=True)
                scale = 1.0 / whole_sum
                for c in chunks:
                    probs[2 * it + e, c, :] = (s[c, :] * scale).astype(LOW)
                pe = (el * scale).astype(LOW)
                probs[2 * it + e, GROUP : GROUP + lat, :] = pe
                total += tn(probs[2 * it + e, 0:GROUP, :], v * halves[e])
                total += tn(pe, vl * halves[e])
            mixed[r, at(p * 128, 128)] = total.astype(LOW)

        def pair(i, carry):
            one_pair(2 * i, 0)
            one_pair(2 * i + 1, 1)
            return carry

        lax.fori_loop(0, half * pairs // 2, pair, 0)
        for m in range(half):
            r = slice(m * GROUP, (m + 1) * GROUP)
            b = slice(m * 128, (m + 1) * 128)
            block_diagonal(qbd, m * 128, latf, m * LAT, 0, 0.125)
            s = nt(qbd[b, :], proj[r, width : 2 * width])
            sl = nt(qbd[b, :], proj[tok:rows, width : 2 * width]) + lat_bias(m, (128, lat), 1)
            top = jnp.maximum(
                jnp.max(s, axis=1, keepdims=True), jnp.max(sl, axis=1, keepdims=True)
            )
            et = jnp.exp(s - top)
            el = jnp.exp(sl - top)
            scale = 1.0 / (
                jnp.sum(et, axis=1, keepdims=True) + jnp.sum(el, axis=1, keepdims=True)
            )
            pt = (et * scale).astype(LOW)
            pe = (el * scale).astype(LOW)
            probs_lat[b, 0:GROUP] = pt
            probs_lat[b, GROUP : GROUP + lat] = pe
            o = nn(pt, proj[r, 2 * width :]) + nn(pe, proj[tok:rows, 2 * width :])
            head_sum(mixf, m * LAT, 0, o, 1.0, False)
        mixed[tok:rows, :] = mixf[...].astype(LOW)

    keys = n * lat

    @pl.when(second)
    def _():
        latf[:, :width] = proj[tok:rows, :width].astype(F32)
        for m in range(half):
            r = slice(m * GROUP, (m + 1) * GROUP)
            b = slice(m * 128, (m + 1) * 128)
            block_diagonal(qbd, m * 128, latf, m * LAT, 0, 0.125)
            block_diagonal(kbd, m * 128, latf, m * LAT, width, 1.0)
            block_diagonal(vbd, m * 128, latf, m * LAT, 2 * width, 1.0)
            s = nt(proj[r, :width] * jnp.asarray(0.125, LOW), kbd[b, :])
            et = jnp.exp(s - class_max(s))
            pt = (et / class_sum(et)).astype(LOW)
            probs[m, 0:GROUP, 0:128] = pt
            mixed[r, :] = nn(pt, vbd[b, :]).astype(LOW)

    root = 0.7978845608028654

    def mlp_in(lo, hi, count):
        r0 = slice(lo, hi)
        mid[r0, :] = xb[r0, :].astype(F32) + nn(mixed[r0, :], wo[...])

        norm(load_mid, gain_mlp, n2, lo, hi, count)

        def widen(i, carry):
            c = at(i * 512, 512)
            tmp[r0, 0:512] = nn(n2[r0, :], wu[:, c])

            def gelu(spans):
                for r in spans:
                    up = tmp[r, 0:512]
                    square = up * up
                    t = jnp.tanh(up * (root + (root * 0.044715) * square))
                    gate = 0.5 + 0.5 * t
                    value = up * gate
                    slope = gate + (value + value) * (1.0 - gate) * (
                        root + (3.0 * root * 0.044715) * square
                    )
                    act[r, c] = value.astype(LOW)
                    dup[r, c] = slope.astype(LOW)

            grouped(gelu, lo, hi, count)
            return carry

        lax.fori_loop(0, ff // 512, widen, 0)

    for copy in loads[1:]:
        copy.wait()

    @pl.when(first)
    def _():
        mlp_in(0, rows, 11)

    @pl.when(second)
    def _():
        mlp_in(0, tok, 8)
        for shift in range(1, n):
            kv_copy(shift, True).wait_recv()
        k = kv_all[:, :, :width].reshape(keys, width)
        v = kv_all[:, :, width:].reshape(keys, width)
        for m in range(half):
            b = slice(m * 128, (m + 1) * 128)
            s = nt(qbd[b, :], k) + key_mask[m : m + 1, :]
            et = jnp.exp(s - jnp.max(s, axis=1, keepdims=True))
            pt = (et / jnp.sum(et, axis=1, keepdims=True)).astype(LOW)
            probs_lat[b, 0:keys] = pt
            head_sum(mixf, m * LAT, 0, nn(pt, v), 1.0, False)
        mixed[tok:rows, :] = mixf[...].astype(LOW)

        mlp_in(tok, rows, 1)

    out_copies = [
        pltpu.make_async_copy(out.at[0:tok], out_tok, load_sem.at[8]),
        pltpu.make_async_copy(out.at[tok:rows], out_lat, load_sem.at[9]),
    ]
    grad_copies = [
        pltpu.make_async_copy(out.at[0:tok], grad_tok, load_sem.at[8]),
        pltpu.make_async_copy(out.at[tok:rows], grad_lat, load_sem.at[9]),
    ]

    def layer_output(passed_on):
        for band, r in enumerate((slice(0, GROUP + lat), slice(GROUP + lat, rows))):
            y = mid[r, :] + nn(act[r, :], wd[...])
            if passed_on:
                low = y.astype(LOW)
                yb[r, :] = low
                y = low.astype(F32)
            out[r, :] = y
            if passed_on:
                relay(0, band).start()

        for copy in out_copies:
            copy.start()

    @pl.when(first)
    def _():
        layer_output(True)
        for band in range(3):
            relay(1, band).wait_recv()

        def widen_e(r):
            ef[r, :] = dy[r, :].astype(F32)

        bands(widen_e, 0, rows, third)

    @pl.when(second)
    def _():
        for copy in e_loads:
            copy.wait()

        def narrow_e(r):
            dy[r, :] = ef[r, :].astype(LOW)

        bands(narrow_e, 0, rows, third)

    part = 384
    unit = width // n
    many = part // unit

    def staged(slot, piece, chunk, share):
        return pltpu.make_async_copy(
            stage.at[slot, piece],
            grads.at[
                chunk,
                share // 8,
                lax.rem(share // 4, 2),
                lax.rem(share // 2, 2),
                lax.rem(share, 2),
            ],
            stage_sem.at[slot, piece],
        )

    def drain(slot):
        def one(piece, carry):
            staged(slot, piece, 0, 0).wait()
            return carry

        lax.fori_loop(0, many, one, 0)

    def weight_grad(place, start, count, left, *rights):
        def one(i, carry):
            turned = left(i).T
            for at_right, right in enumerate(rights):
                tile = i * len(rights) + at_right
                slot = lax.rem(tile, 2)
                value = nn(turned, right(i)).astype(LOW)

                @pl.when(tile >= start * len(rights) + 2)
                def _():
                    drain(slot)

                for piece in range(many):
                    stage[slot, piece] = value[piece * unit : (piece + 1) * unit]
                    staged(slot, piece, *place(i, at_right, piece)).start()
            return carry

        lax.fori_loop(start, start + count, one, 0)
        for slot in (0, 1):
            drain(slot)

    orders = ((0, 2, 1, 3), (1, 2, 0, 3))
    own_buf = (own_a, own_b)
    land = (
        (land1_a, land1_b),
        (land2_a, land2_b),
        (land3_a, land3_b),
        (land4_a, land4_b),
    )
    spread_pairs = land1_a.shape[0]

    def source(stream, phase, k, theirs):
        pick = [(1 - here[bit]) if theirs else here[bit] for bit in orders[stream]]
        own_bit = [here[bit] for bit in orders[stream]]
        base = land[0][stream]
        if phase == 0:
            if stream == 0:
                return grads.at[2 * k, :, :, :, pick[0]]
            return grads.at[2 * k + 1, :, :, pick[0]]
        if phase == 1:
            return base.at[k, :, pick[1]]
        if phase == 2:
            return base.at[k, :, own_bit[1], pick[2]]
        return base.at[k, pick[3], own_bit[1], own_bit[2]]

    def copy_of(stream, phase, k):
        return pltpu.make_async_remote_copy(
            src_ref=source(stream, phase, k, True),
            dst_ref=land[phase][stream].at[k],
            send_sem=send_sem.at[stream, phase, k],
            recv_sem=recv_sem.at[stream, phase, k],
            device_id=across(orders[stream][phase]),
            device_id_type=MESH,
        )

    def own(stream, k):
        return pltpu.make_async_copy(
            source(stream, 0, k, False), own_buf[stream], own_sem.at[stream]
        )

    def leave(stream, k):
        slot = lax.rem(k, 2)
        return pltpu.make_async_copy(
            leaving.at[slot, stream], summed.at[2 * k + stream], leave_sem.at[slot, stream]
        )

    def launch(phase, k):
        for stream in (0, 1):
            copy_of(stream, phase, k).start()

    def absorb(phase, k):
        for stream in (0, 1):
            if phase == 0:
                own(stream, k).wait()
            copy_of(stream, phase, k).wait_recv()
            base, into = land[0][stream], land[phase][stream]
            mine = [here[bit] for bit in orders[stream]]
            if phase == 0:

                def add(i, carry):
                    for j in (0, 1):
                        for h in (0, 1):
                            total = own_buf[stream][i, j, h].astype(F32)
                            total += base[k, i, j, h].astype(F32)
                            base[k, i, j, h] = total.astype(LOW)
                    return carry

                lax.fori_loop(0, 2, add, 0)
            elif phase == 1:
                for i in (0, 1):
                    for h in (0, 1):
                        total = base[k, i, mine[1], h].astype(F32)
                        total += into[k, i, h].astype(F32)
                        base[k, i, mine[1], h] = total.astype(LOW)
            elif phase == 2:
                for i in (0, 1):
                    total = base[k, i, mine[1], mine[2]].astype(F32)
                    total += into[k, i].astype(F32)
                    base[k, i, mine[1], mine[2]] = total.astype(LOW)
            else:
                total = base[k, mine[3], mine[1], mine[2]].astype(F32)
                total += into[k].astype(F32)
                slot = lax.rem(k, 2)

                @pl.when(k >= 2)
                def _():
                    leave(stream, k - 2).wait()

                leaving[slot, stream] = total
                leave(stream, k).start()

    def start_own(k):
        for stream in (0, 1):
            own(stream, k).start()

    def relaunch(k, following=True):
        absorb(0, k)
        launch(1, k)
        if following:
            start_own(k + 1)

    def onward(phase, k):
        absorb(phase, k)
        if phase < 3:
            launch(phase + 1, k)

    wide = ff // width
    per_part = width // part

    def up_grad():
        weight_grad(
            lambda i, right, piece: (
                wide + lax.rem(i * many + piece, wide),
                (i * many + piece) // wide,
            ),
            0,
            ff // part,
            lambda i: dup[:, at(i * part, part)],
            lambda i: n2[...],
        )
        launch(0, 2)
        launch(0, 3)

    def down_grad(pair):
        weight_grad(
            lambda i, right, piece: (2 * pair + right, i * many + piece),
            0,
            per_part,
            lambda i: dy[:, at(i * part, part)],
            lambda i: act[:, 2 * pair * width : (2 * pair + 1) * width],
            lambda i: act[:, (2 * pair + 1) * width : (2 * pair + 2) * width],
        )

    down_grad(0)
    launch(0, 0)
    start_own(0)
    down_grad(1)
    launch(0, 1)

    def unwiden(c):
        dup[:, c] = (nt(dy[...], wd[c, :]) * dup[:, c].astype(F32)).astype(LOW)

    tiles(ff // TILE, unwiden)
    @pl.when(first)
    def _():
        up_grad()

    def to_mid(c):
        tmp[:, c] = nt(dup[...], wu[c, :])

    tiles(width // 256, to_mid, 256)
    gains[0] = jnp.zeros_like(gains[0])

    def store_mid(r, total):
        ef[r, :] = total
        dy[r, :] = total.astype(LOW)

    norm_back(load_mid, tmp, gain_mlp, slice(8, 16), store_mid, 0, rows, 11)

    @pl.when(first)
    def _():
        for band in (0, 1):
            relay(0, band).wait_send()

    def to_mix(c):
        yb[:, c] = nt(dy[...], wo[c, :]).astype(LOW)

    tiles(width // TILE, to_mix)
    mixf[...] = yb[tok:rows, :].astype(F32)

    @pl.when(second)
    def _():
        k = kv_all[:, :, :width].reshape(keys, width)
        v = kv_all[:, :, width:].reshape(keys, width)
        for m in range(half):
            b = slice(m * 128, (m + 1) * 128)
            block_diagonal(vbd.at[pl.ds(256, 256)], m * 128, mixf, m * LAT, 0, 1.0)
        both = slice(0, half * 128)
        do = vbd[256 : 256 + half * 128, :]
        pt = probs_lat[both, 0:keys]
        pf = pt.astype(F32)
        dp = nt(do, v)
        along = jnp.sum(pf * dp, axis=1, keepdims=True)
        ds = (pf * (dp - along)).astype(LOW)
        kvg_send[:, :, :width] = tn(ds, qbd[both, :]).astype(LOW).reshape(n, lat, width)
        kvg_send[:, :, width:] = tn(pt, do).astype(LOW).reshape(n, lat, width)
        for shift in range(1, n):
            kvg_copy(shift).start()
        dq = nn(ds, k)
        for m in range(half):
            head_sum(latf, m * LAT, 0, dq[m * 128 : (m + 1) * 128], 0.125, False)
        proj[tok:rows, :width] = latf[:, :width].astype(LOW)
        layer_output(False)

    weight_grad(
        lambda i, right, piece: (2 * wide, i * many + piece),
        0,
        width // part,
        lambda i: dy[:, at(i * part, part)],
        lambda i: mixed[...],
    )
    for copy in out_copies:
        copy.wait()

    @pl.when(first)
    def _():
        for m in range(half):
            r = slice(m * GROUP, (m + 1) * GROUP)
            b = slice(m * 128, (m + 1) * 128)
            block_diagonal(vbd, m * 128, mixf, m * LAT, 0, 1.0)
            do = vbd[b, :]
            dp = nt(do, proj[r, 2 * width :])
            dl = nt(do, proj[tok:rows, 2 * width :])
            pt = probs_lat[b, 0:GROUP]
            pe = probs_lat[b, GROUP : GROUP + lat]
            pf = pt.astype(F32)
            pg = pe.astype(F32)
            along = jnp.sum(pf * dp, axis=1, keepdims=True) + jnp.sum(
                pg * dl, axis=1, keepdims=True
            )
            ds = (pf * (dp - along)).astype(LOW)
            dsl = (pg * (dl - along)).astype(LOW)
            dq = nn(ds, proj[r, width : 2 * width]) + nn(dsl, proj[tok:rows, width : 2 * width])
            head_sum(latf, m * LAT, 0, dq, 0.125, False)
            tmp[r, :] = tn(ds, qbd[b, :])
            out[r, :] = tn(pt, do)
            if m == 0:
                tmp[tok:rows, :] = tn(dsl, qbd[b, :])
                out[tok:rows, :] = tn(pe, do)
            else:
                tmp[tok:rows, :] += tn(dsl, qbd[b, :])
                out[tok:rows, :] += tn(pe, do)
        proj[tok:rows, :width] = latf[:, :width].astype(LOW)

        def one_pair(it, side):
            m, p = it // pairs, lax.rem(it, pairs)
            r = at(m * GROUP, GROUP)
            qc = at(p * 128, 128)
            q = proj[r, qc]
            k = proj[r, at(width + p * 128, 128)]
            v = proj[r, at(2 * width + p * 128, 128)]
            kl = proj[tok:rows, at(width + p * 128, 128)]
            vl = proj[tok:rows, at(2 * width + p * 128, 128)]
            dx = yb[r, qc]
            dq = jnp.zeros((GROUP, 128), F32)
            dk = tmp[r, qc]
            dv = out[r, qc]
            dkl = tmp[tok:rows, qc]
            dvl = out[tok:rows, qc]
            for e in (0, 1):
                qe = q * eighths[e]
                de = dx * halves[e]
                s = scores.at[2 * side + e]
                s[...] = nt(v, de)
                dl = nt(vl, de)
                pt = probs[2 * it + e, 0:GROUP, :]
                pe = probs[2 * it + e, GROUP : GROUP + lat, :]
                pg = pe.astype(F32)
                along = jnp.sum(pg * dl, axis=0, keepdims=True)
                for c in chunks:
                    pf = probs[2 * it + e, c, :].astype(F32)
                    along += jnp.sum(pf * s[c, :], axis=0, keepdims=True)
                for c in chunks:
                    pf = probs[2 * it + e, c, :].astype(F32)
                    slopes[2 * side + e, c, :] = (pf * (s[c, :] - along)).astype(LOW)
                ds = slopes[2 * side + e]
                dsl = (pg * (dl - along)).astype(LOW)
                dq += tn(ds, k * halves[e]) + tn(dsl, kl * halves[e])
                dk += nn(ds, qe)
                dkl += nn(dsl, qe)
                dv += nn(pt, de)
                dvl += nn(pe, de)
            proj[r, qc] = (dq * 0.125).astype(LOW)
            proj[r, at(width + p * 128, 128)] = dk.astype(LOW)
            proj[r, at(2 * width + p * 128, 128)] = dv.astype(LOW)
            tmp[tok:rows, qc] = dkl
            out[tok:rows, qc] = dvl

        def pair(i, carry):
            one_pair(2 * i, 0)
            one_pair(2 * i + 1, 1)
            return carry

        lax.fori_loop(0, half * pairs // 2, pair, 0)
        proj[tok:rows, width : 2 * width] = tmp[tok:rows, :].astype(LOW)
        proj[tok:rows, 2 * width :] = out[tok:rows, :].astype(LOW)

    @pl.when(second)
    def _():
        for m in range(half):
            r = slice(m * GROUP, (m + 1) * GROUP)
            b = slice(m * 128, (m + 1) * 128)
            pt = probs[m, 0:GROUP, 0:128]
            pf = pt.astype(F32)
            dx = yb[r, :]
            dp = nt(dx, vbd[b, :])
            ds = (pf * (dp - class_sum(pf * dp))).astype(LOW)
            dk = tn(ds, proj[r, :width])
            dv = tn(pt, dx)
            proj[r, :width] = (nn(ds, kbd[b, :]) * 0.125).astype(LOW)
            head_sum(latf, m * LAT, width, dk, 0.125, False)
            head_sum(latf, m * LAT, 2 * width, dv, 1.0, False)
        total = latf[:, width:] + kvg_send[me].astype(F32)
        for shift in range(1, n):
            kvg_copy(shift).wait_recv()
            total += kvg_recv[shift - 1].astype(F32)
        proj[tok:rows, width:] = total.astype(LOW)

    @pl.when(first)
    def _():
        relaunch(0)
        relaunch(1)

    @pl.when(first)
    def _():
        def to_in(c):
            tmp[:, c] = nt(proj[...], wq[c, :])

        tiles(width // 256, to_in, 256)

    @pl.when(second)
    def _():
        tmp[0:tok, :] = nt(proj[0:tok, :width], wq[:, :width])
        tmp[tok:rows, :] = nt(proj[tok:rows, :], wq[...])

    def store_in(r, total):
        low = total.astype(LOW)
        yb[r, :] = low
        out[r, :] = jnp.where(first, total, low.astype(F32))

    for band in range(3):
        norm_back(
            load_in, tmp, gain_attn, slice(0, 8), store_in, band * third, (band + 1) * third, 11
        )

        @pl.when(second)
        def _():
            relay(1, band).start()

    for copy in grad_copies:
        copy.start()

    @pl.when(second)
    def _():
        up_grad()
        relaunch(0)
        relaunch(1)

    relaunch(2)
    relaunch(3, False)

    def qkv_grad(start, count, r):
        weight_grad(
            lambda i, right, piece: (
                2 * wide + 1 + lax.rem(i * many + piece, 3),
                (i * many + piece) // 3,
            ),
            start,
            count,
            lambda i: proj[r, at(i * part, part)],
            lambda i: n1[r, :],
        )

    @pl.when(first)
    def _():
        qkv_grad(0, 3 * per_part, slice(0, rows))

    @pl.when(second)
    def _():
        qkv_grad(0, per_part, slice(0, rows))
        qkv_grad(per_part, 2 * per_part, slice(tok, rows))

    for pair in range(4, spread_pairs):
        launch(0, pair)
    start_own(4)

    def gain_copy(bit):
        return pltpu.make_async_remote_copy(
            src_ref=gains.at[bit],
            dst_ref=land_g.at[bit],
            send_sem=gain_s.at[bit],
            recv_sem=gain_r.at[bit],
            device_id=across(bit),
            device_id_type=MESH,
        )

    def gain_step(bit):
        gain_copy(bit).wait_recv()
        gains[bit + 1] = gains[bit] + land_g[bit]

    def each(lo, hi, phase):
        def one(i, carry):
            onward(phase, i)
            return carry

        lax.fori_loop(lo, hi, one, 0)

    gain_copy(0).start()
    each(0, 4, 1)
    gain_step(0)
    gain_copy(1).start()
    relaunch(4)
    each(0, 2, 2)
    relaunch(5, False)
    each(2, 4, 2)
    gain_step(1)
    gain_copy(2).start()
    each(4, 6, 1)
    each(0, 4, 3)
    gain_step(2)
    gain_copy(3).start()
    each(4, 6, 2)
    gain_step(3)
    each(4, 6, 3)
    final = gains[4]
    for i in (0, 1):
        whole_gain = jnp.sum(final[8 * i : 8 * i + 8], axis=0, keepdims=True)
        whole_gain = jnp.broadcast_to(whole_gain, (8, width))
        rolled = pltpu.roll(whole_gain, lax.rem(width - me * unit, width), 1)
        gain_sums[8 * i : 8 * i + 8, :] = rolled[:, 0:128]

    def finish(k, carry):
        for stream in (0, 1):
            for phase in range(4):
                copy_of(stream, phase, k).wait_send()
        return carry

    lax.fori_loop(0, spread_pairs, finish, 0)
    for bit in range(4):
        gain_copy(bit).wait_send()
    for copy in grad_copies:
        copy.wait()
    for stream in (0, 1):
        for pair in (spread_pairs - 2, spread_pairs - 1):
            leave(stream, pair).wait()

    @pl.when(second)
    def _():
        for band in range(3):
            relay(1, band).wait_send()
        for shift in range(1, n):
            kv_copy(shift, False).wait_send()
            kvg_copy(shift).wait_send()


def both_layers(n, tokens, latents, slots, images, gains, weights, d_tokens, d_latents):
    tok, width = tokens.shape
    lat = latents.shape[0]
    rows = tok + lat
    w_qkv, w_out, w_up, w_down = weights
    ff = w_up.shape[1]
    keys = n * lat
    half = lat // LAT
    size = sum(w.size for w in weights)
    chunks = size // (width * width)
    pairs = chunks // 2
    unit = width // n
    vm, hbm = pl.BlockSpec(memory_space=pltpu.VMEM), pl.BlockSpec(memory_space=pl.ANY)
    sm = pl.BlockSpec(memory_space=pltpu.SMEM)
    scratch = [
        pltpu.VMEM(w.shape, LOW) for w in (w_qkv, w_out, w_up, w_down)
    ] + [
        pltpu.VMEM(shape, dtype)
        for shape, dtype in (
            ((rows, width), LOW),
            ((rows, width), LOW),
            ((rows, 3 * width), LOW),
            ((rows, width), LOW),
            ((rows, width), F32),
            ((rows, width), LOW),
            ((rows, ff), LOW),
            ((rows, ff), LOW),
            ((rows, width), LOW),
            ((rows, width), LOW),
            ((rows, width), F32),
            ((rows, width), F32),
            ((rows, width), F32),
            ((half * width // 64, GROUP + lat, GROUP), LOW),
            ((half * 128, max(keys, GROUP + 128)), LOW),
            ((4, GROUP, GROUP), F32),
            ((4, GROUP, GROUP), LOW),
            ((lat, 3 * width), F32),
            ((lat, width), F32),
            ((8, keys), F32),
            ((half * 128, width), LOW),
            ((half * 128, width), LOW),
            ((half * 256, width), LOW),
            ((n, lat, 2 * width), LOW),
            ((n, lat, 2 * width), LOW),
            ((n - 1, lat, 2 * width), LOW),
            ((2, 384 // unit, unit, width), LOW),
            ((5, 16, width), F32),
            ((2, 2, unit, width), F32),
            ((2, 2, 2, unit, width), LOW),
            ((2, 2, 2, unit, width), LOW),
            ((pairs, 2, 2, 2, unit, width), LOW),
            ((pairs, 2, 2, 2, unit, width), LOW),
            ((pairs, 2, 2, unit, width), LOW),
            ((pairs, 2, 2, unit, width), LOW),
            ((pairs, 2, unit, width), LOW),
            ((pairs, 2, unit, width), LOW),
            ((pairs, unit, width), LOW),
            ((pairs, unit, width), LOW),
            ((4, 16, width), F32),
        )
    ] + [
        pltpu.SemaphoreType.DMA((10,)),
        pltpu.SemaphoreType.DMA((2, 384 // unit)),
        pltpu.SemaphoreType.DMA((2,)),
        pltpu.SemaphoreType.DMA((2, 2)),
        pltpu.SemaphoreType.DMA((2, 4, pairs)),
        pltpu.SemaphoreType.DMA((2, 4, pairs)),
        pltpu.SemaphoreType.DMA((4,)),
        pltpu.SemaphoreType.DMA((4,)),
        pltpu.SemaphoreType.DMA((6,)),
        pltpu.SemaphoreType.DMA((6,)),
        pltpu.SemaphoreType.DMA((n - 1,)),
        pltpu.SemaphoreType.DMA((n - 1,)),
        pltpu.SemaphoreType.DMA((n - 1,)),
        pltpu.SemaphoreType.DMA((n - 1,)),
    ]
    return pl.pallas_call(
        functools.partial(layer_kernel, n),
        out_shape=(
            jax.ShapeDtypeStruct((tok, width), F32),
            jax.ShapeDtypeStruct((lat, width), F32),
            jax.ShapeDtypeStruct((tok, width), F32),
            jax.ShapeDtypeStruct((lat, width), F32),
            jax.ShapeDtypeStruct((chunks, 2, 2, 2, 2, unit, width), LOW),
            jax.ShapeDtypeStruct((chunks, unit, width), F32),
            jax.ShapeDtypeStruct((16, 128), F32),
        ),
        in_specs=[hbm, hbm, vm, sm, sm, vm, vm] + [hbm] * 6,
        out_specs=(hbm,) * 6 + (vm,),
        scratch_shapes=scratch,
        compiler_params=pltpu.CompilerParams(
            collective_id=1, has_side_effects=True, vmem_limit_bytes=63 * 1024 * 1024
        ),
        cost_estimate=pl.CostEstimate(
            flops=6 * rows * size, bytes_accessed=4 * size, transcendentals=0
        ),
    )(tokens, latents, slots, slots, images, *gains, *weights, d_tokens, d_latents)


def finish_kernel(width, *refs):
    rows_in, (summed, gains), rows_out = refs[0:4], refs[4:6], refs[6:10]
    gain_attn, g_qkv, g_out, gain_mlp, g_up, g_down = refs[10:16]
    held, (sem_in, sem_out) = refs[16:21], refs[21:23]
    wide = g_down.shape[1] // width
    unit = g_out.shape[1]
    loads = [
        pltpu.make_async_copy(src, dst, sem_in.at[i])
        for i, (src, dst) in enumerate(zip((*rows_in, summed), held))
    ]
    for load in loads:
        load.start()
    all_rows, sums = held[0:4], held[4]
    moves = [[pair] for pair in zip(all_rows, rows_out)] + [
        [(sums.at[c], g_down.at[:, c * width : (c + 1) * width]) for c in range(wide)]
        + [
            (sums.at[wide : 2 * wide], g_up),
            (sums.at[2 * wide : 2 * wide + 1], g_out),
            (sums.at[2 * wide + 1 :], g_qkv),
        ]
    ]
    gain_attn[...] = gains[0:1, 0:unit]
    gain_mlp[...] = gains[8:9, 0:unit]
    started = []
    for load, group in zip(loads, moves):
        load.wait()
        for src, dst in group:
            started.append(pltpu.make_async_copy(src, dst, sem_out.at[len(started)]))
            started[-1].start()
    for move in started:
        move.wait()


def finished(rows, summed, gains, wide):
    chunks, unit, width = summed.shape
    hbm, vm = pl.BlockSpec(memory_space=pl.ANY), pl.BlockSpec(memory_space=pltpu.VMEM)
    shapes = [r.shape for r in rows] + [
        (1, unit),
        (3, unit, width),
        (1, unit, width),
        (1, unit),
        (wide, unit, width),
        (unit, wide * width),
    ]
    return pl.pallas_call(
        functools.partial(finish_kernel, width),
        out_shape=tuple(jax.ShapeDtypeStruct(s, F32) for s in shapes),
        in_specs=[hbm] * 5 + [vm],
        out_specs=(hbm,) * 4 + (vm, hbm, hbm, vm, hbm, hbm),
        scratch_shapes=[pltpu.VMEM(x.shape, F32) for x in (*rows, summed)]
        + [pltpu.SemaphoreType.DMA((5,)), pltpu.SemaphoreType.DMA((7 + wide,))],
        compiler_params=pltpu.CompilerParams(vmem_limit_bytes=62 * 1024 * 1024),
    )(*rows, summed, gains)
def fused_shards(
    unused_grid,
    tokens,
    latents,
    slot_group,
    image_groups,
    gain_attn,
    w_qkv,
    w_out,
    gain_mlp,
    w_up,
    w_down,
    d_tokens,
    d_latents,
):
    micro, tok, width = tokens.shape
    lat = latents.shape[1]
    out_tok, out_lat, grad_tok, grad_lat, unused_grads, summed, gains = both_layers(
        slot_group.shape[1],
        tokens.reshape(micro * tok, width),
        latents.reshape(micro * lat, width),
        slot_group,
        image_groups,
        (gain_attn, gain_mlp),
        (w_qkv[0], w_out[0], w_up[0], w_down[0]),
        d_tokens.reshape(micro * tok, width),
        d_latents.reshape(micro * lat, width),
    )
    wide = w_up.shape[2] // width
    rows = (out_tok, out_lat, grad_tok, grad_lat)
    *rows, first_gain, qkv, out, second_gain, up, down = finished(rows, summed, gains, wide)
    return (
        rows[0].reshape(1, micro, tok, width),
        rows[1].reshape(1, micro, lat, width),
        rows[2].reshape(1, micro, tok, width),
        rows[3].reshape(1, micro, lat, width),
        first_gain,
        qkv.reshape(-1, width).T[None],
        out.reshape(-1, width).T[None],
        second_gain,
        up.reshape(-1, width).T[None],
        down.T[None],
    )

def solution(mesh):
    in_specs = (
        P(None, "dp", None),
        P(None, "dp", None),
        P(),
        P(),
        P("section", None),
        P("section", None, None),
        P("section", None, None),
        P("section", None),
        P("section", None, None),
        P("section", None, None),
        P(None, "dp", None),
        P(None, "dp", None),
    )
    out_specs = (
        P("section", None, "dp", None),
        P("section", None, "dp", None),
        P("section", None, "dp", None),
        P("section", None, "dp", None),
        P("section", "dp"),
        P("section", None, "dp"),
        P("section", None, "dp"),
        P("section", "dp"),
        P("section", None, "dp"),
        P("section", None, "dp"),
    )
    grid = grid_of(mesh)

    def program(*args):
        n, width = mesh.shape["dp"], args[0].shape[2]
        one_group = args[0].shape[1] == n * GROUP
        body = fused_shards if one_group and n == 16 and width % (16 * n) == 0 else shards
        return jax.shard_map(
            functools.partial(body, grid), mesh=mesh, in_specs=in_specs, out_specs=out_specs, check_vma=False
        )(*args)

    return program
```

```python
import functools

import jax
import jax.numpy as jnp
from jax import lax
from jax.experimental import pallas as pl
from jax.experimental.pallas import tpu as pltpu
from jax.sharding import PartitionSpec as P

HEADS = 12
GROUP = 256
LAT = 8


epsilon = 1e-05
masked_score = -1e30


MESH = pl.DeviceIdType.MESH


def grid_of(mesh):
    n = mesh.shape["dp"]
    coords = [getattr(d, "coords", None) for d in mesh.devices.reshape(n, -1)[:, 0]]
    if any(c is None for c in coords):
        return (n // 4, 2, 2) if n % 4 == 0 else (n, 1, 1)
    sizes = {a: len({c[a] for c in coords}) for a in range(3)}
    strides = {
        a: min([i for i in range(n) if coords[i][a] != coords[0][a]], default=n) for a in range(3)
    }
    order = sorted(range(3), key=lambda a: -strides[a])
    return tuple(sizes[a] for a in order)


def spread_kernel(grid, pairs, g_ref, gain_ref, out_ref, gout_ref, *scratch):
    acc = scratch[0:3]
    land = [scratch[3 + 3 * i : 6 + 3 * i] for i in range(3)]
    send_sem, recv_sem, own_sem = scratch[12:15]
    me = lax.axis_index("dp")
    section = lax.axis_index("section")
    l0, l1, l2 = grid
    here = (me // (l1 * l2), lax.rem(me // l2, l1), lax.rem(me, l2))

    def device(axis, shift):
        there = list(here)
        there[axis] = lax.rem(here[axis] + shift, grid[axis])
        return there[axis], ((there[0] * l1 + there[1]) * l2 + there[2], section)

    barrier = pltpu.get_barrier_semaphore()
    for axis in range(3):
        for shift in range(1, grid[axis]):
            pl.semaphore_signal(
                barrier, inc=1, device_id=device(axis, shift)[1], device_id_type=MESH
            )
    pl.semaphore_wait(barrier, sum(grid) - 3)

    orders = ((2, 1, 0), (1, 2, 0), (2, 1, 0))

    def source(stream, phase, k, at):
        if phase == 0:
            if stream == 0:
                return g_ref.at[2 * k, :, :, at]
            if stream == 1:
                return g_ref.at[2 * k + 1, :, at]
            return gain_ref.at[:, :, at]
        if phase == 1:
            return acc[stream].at[k, :, at]
        return acc[stream].at[k, at, here[orders[stream][1]]]

    def copies(stream, phase, k):
        axis = orders[stream][phase]
        for shift in range(1, grid[axis]):
            at, target = device(axis, shift)
            yield pltpu.make_async_remote_copy(
                src_ref=source(stream, phase, k, at),
                dst_ref=land[phase][stream].at[k, shift - 1],
                send_sem=send_sem.at[stream, phase, k, shift - 1],
                recv_sem=recv_sem.at[stream, phase, k, shift - 1],
                device_id=target,
                device_id_type=MESH,
            )

    def own(stream, k):
        return pltpu.make_async_copy(
            source(stream, 0, k, here[orders[stream][0]]), acc[stream].at[k], own_sem.at[stream, k]
        )

    def launch(stream, phase, k):
        for copy in copies(stream, phase, k):
            copy.start()

    def absorb(stream, phase, k):
        axis = orders[stream][phase]
        if phase == 0:
            own(stream, k).wait()
        for copy in copies(stream, phase, k):
            copy.wait_recv()
        into = land[phase][stream]
        count = grid[axis] - 1
        if phase == 0:
            for a in range(acc[stream].shape[1]):
                for b in range(acc[stream].shape[2]):
                    total = acc[stream][k, a, b].astype(jnp.float32)
                    for s in range(count):
                        total += into[k, s, a, b].astype(jnp.float32)
                    acc[stream][k, a, b] = total.astype(acc[stream].dtype)
        elif phase == 1:
            mine = here[axis]
            for a in range(acc[stream].shape[1]):
                total = acc[stream][k, a, mine].astype(jnp.float32)
                for s in range(count):
                    total += into[k, s, a].astype(jnp.float32)
                acc[stream][k, a, mine] = total.astype(acc[stream].dtype)
        else:
            total = acc[stream][k, here[0], here[orders[stream][1]]].astype(jnp.float32)
            for s in range(count):
                total += into[k, s].astype(jnp.float32)
            if stream < 2:
                out_ref[2 * k + stream] = total
            else:
                gout_ref[...] = total

    own(2, 0).start()
    launch(2, 0, 0)

    def start_own(k, carry):
        for stream in (0, 1):
            own(stream, k).start()
        return carry

    for stream in (0, 1):
        launch(stream, 0, 0)
    lax.fori_loop(0, pairs, start_own, 0)

    def turn(t, carry):
        @pl.when(t + 1 < pairs)
        def _():
            for stream in (0, 1):
                launch(stream, 0, t + 1)

        @pl.when(t < pairs)
        def _():
            for stream in (0, 1):
                absorb(stream, 0, t)
                launch(stream, 1, t)

        @pl.when((t >= 1) & (t - 1 < pairs))
        def _():
            for stream in (0, 1):
                absorb(stream, 1, t - 1)
                launch(stream, 2, t - 1)

        @pl.when(t >= 2)
        def _():
            for stream in (0, 1):
                absorb(stream, 2, t - 2)

        return carry

    lax.fori_loop(0, pairs + 2, turn, 0)
    absorb(2, 0, 0)
    launch(2, 1, 0)
    absorb(2, 1, 0)
    launch(2, 2, 0)
    absorb(2, 2, 0)

    def finish(k, carry):
        for stream in (0, 1):
            for phase in range(3):
                for copy in copies(stream, phase, k):
                    copy.wait_send()
        return carry

    lax.fori_loop(0, pairs, finish, 0)
    for phase in range(3):
        for copy in copies(2, phase, 0):
            copy.wait_send()


def spread(grid, grads, gains):
    chunks, n, rows, width = grads.shape
    pairs = chunks // 2
    l0, l1, l2 = grid
    most = max(max(grid) - 1, 1)
    low = jnp.bfloat16
    shapes = ((pairs, rows, width, low), (pairs, rows, width, low), (1, 8, 128, jnp.float32))
    inner = ((l1, l2), (l2, l1), (l1, l2))
    acc, first, second, third = [], [], [], []
    for (count, r, w, dt), (kept, sent) in zip(shapes, inner):
        acc.append(pltpu.VMEM((count, l0, kept, r, w), dt))
        first.append(pltpu.VMEM((count, max(sent - 1, 1), l0, kept, r, w), dt))
        second.append(pltpu.VMEM((count, max(kept - 1, 1), l0, r, w), dt))
        third.append(pltpu.VMEM((count, max(l0 - 1, 1), r, w), dt))
    return pl.pallas_call(
        functools.partial(spread_kernel, grid, pairs),
        out_shape=(
            jax.ShapeDtypeStruct((chunks, rows, width), jnp.float32),
            jax.ShapeDtypeStruct((8, 128), jnp.float32),
        ),
        in_specs=[pl.BlockSpec(memory_space=pl.ANY)] * 2,
        out_specs=(pl.BlockSpec(memory_space=pltpu.VMEM),) * 2,
        scratch_shapes=acc
        + first
        + second
        + third
        + [
            pltpu.SemaphoreType.DMA((3, 3, pairs, most)),
            pltpu.SemaphoreType.DMA((3, 3, pairs, most)),
            pltpu.SemaphoreType.DMA((3, pairs)),
        ],
        compiler_params=pltpu.CompilerParams(
            collective_id=0, has_side_effects=True, vmem_limit_bytes=60 * 1024 * 1024
        ),
        cost_estimate=pl.CostEstimate(flops=0, bytes_accessed=grads.size * 4, transcendentals=0),
    )(grads.reshape(chunks, l0, l1, l2, rows, width), gains.reshape(l0, l1, l2, 8, 128))


def from_behind(x, axis, by):
    devices = lax.axis_size(axis)
    pairs = [(i, i + by) for i in range(devices) if 0 <= i + by < devices]
    return lax.ppermute(x, axis, pairs)


def layer_norm(values, gain):
    row_mean = jnp.mean(values, axis=-1, keepdims=True)
    centred = values - row_mean
    row_var = jnp.mean(centred * centred, axis=-1, keepdims=True)
    return centred * lax.rsqrt(row_var + epsilon) * gain


def front_half(all_rows, gain_attn, w_qkv):
    normed = layer_norm(all_rows, gain_attn).astype(jnp.bfloat16)
    projected = jnp.dot(normed, w_qkv, preferred_element_type=jnp.float32).astype(jnp.bfloat16)
    return (normed, projected)


def latent_operand(projected, tok_rows, model_width):
    return projected[tok_rows:, model_width:]


def back_half(all_rows, projected, remote_rows, allowed, weights):
    gain_attn, w_qkv, w_out, gain_mlp, w_up, w_down = weights
    row_count, model_width = all_rows.shape
    head_size = model_width // HEADS
    remote_pairs = remote_rows[:, remote_rows.shape[1] - 2 * model_width :]
    queries = projected[:, :model_width].reshape(row_count, HEADS, head_size)
    key_rows = jnp.concatenate(
        [projected[:, model_width : 2 * model_width], remote_pairs[:, :model_width]], axis=0
    )
    value_rows = jnp.concatenate(
        [projected[:, 2 * model_width :], remote_pairs[:, model_width:]], axis=0
    )
    key_rows = key_rows.reshape(-1, HEADS, head_size)
    value_rows = value_rows.reshape(-1, HEADS, head_size)
    scores = jnp.einsum(
        "qhd,khd->hqk", queries, key_rows, preferred_element_type=jnp.float32
    ) * head_size ** (-0.5)
    attn_weights = jax.nn.softmax(jnp.where(allowed[None], scores, masked_score), axis=-1)
    attn_low = attn_weights.astype(jnp.bfloat16)
    mixed_low = jnp.einsum("hqk,khd->qhd", attn_low, value_rows, preferred_element_type=jnp.float32)
    mixed_low = mixed_low.reshape(row_count, model_width).astype(jnp.bfloat16)
    mid_rows = all_rows + jnp.dot(mixed_low, w_out, preferred_element_type=jnp.float32)
    normed_mlp = layer_norm(mid_rows, gain_mlp).astype(jnp.bfloat16)
    up_proj = jnp.dot(normed_mlp, w_up, preferred_element_type=jnp.float32)
    activated = jax.nn.gelu(up_proj).astype(jnp.bfloat16)
    result = mid_rows + jnp.dot(activated, w_down, preferred_element_type=jnp.float32)
    return dict(
        queries=queries,
        key_rows=key_rows,
        value_rows=value_rows,
        attn_weights=attn_weights,
        attn_low=attn_low,
        mixed_low=mixed_low,
        mid_rows=mid_rows,
        normed_mlp=normed_mlp,
        up_proj=up_proj,
        activated=activated,
        result=result,
    )


def section_backward(saved, d_result, all_rows, normed, allowed, weights, latent_start):
    gain_attn, w_qkv, w_out, gain_mlp, w_up, w_down = weights
    row_count, model_width = all_rows.shape
    head_size = model_width // HEADS
    score_scale = head_size ** (-0.5)
    d_low = d_result.astype(jnp.bfloat16)
    grad_down = jnp.dot(d_low.T, saved["activated"], preferred_element_type=jnp.float32)
    d_activated = jnp.dot(d_low, w_down.T, preferred_element_type=jnp.float32)
    unused_up, gelu_back = jax.vjp(jax.nn.gelu, saved["up_proj"])
    d_up = gelu_back(d_activated)[0].astype(jnp.bfloat16)
    grad_up = jnp.dot(d_up.T, saved["normed_mlp"], preferred_element_type=jnp.float32)
    d_normed_mlp = jnp.dot(d_up, w_up.T, preferred_element_type=jnp.float32)
    unused_mid, second_back = jax.vjp(layer_norm, saved["mid_rows"], gain_mlp)
    d_mid_norm, grad_gain_mlp = second_back(d_normed_mlp)
    d_mid = d_result + d_mid_norm
    d_mid_low = d_mid.astype(jnp.bfloat16)
    grad_out = jnp.dot(d_mid_low.T, saved["mixed_low"], preferred_element_type=jnp.float32)
    d_mixed = jnp.dot(d_mid_low, w_out.T, preferred_element_type=jnp.float32).astype(jnp.bfloat16)
    d_mixed = d_mixed.reshape(row_count, HEADS, head_size)
    d_weights = jnp.einsum(
        "qhd,khd->hqk", d_mixed, saved["value_rows"], preferred_element_type=jnp.float32
    )
    d_values = jnp.einsum(
        "hqk,qhd->khd", saved["attn_low"], d_mixed, preferred_element_type=jnp.float32
    )
    attn_weights = saved["attn_weights"]
    d_scores = attn_weights * (
        d_weights - jnp.sum(attn_weights * d_weights, axis=-1, keepdims=True)
    )
    d_scores_low = jnp.where(allowed[None], d_scores, 0.0).astype(jnp.bfloat16)
    d_queries = (
        jnp.einsum(
            "hqk,khd->qhd", d_scores_low, saved["key_rows"], preferred_element_type=jnp.float32
        )
        * score_scale
    )
    d_keys = (
        jnp.einsum(
            "hqk,qhd->khd", d_scores_low, saved["queries"], preferred_element_type=jnp.float32
        )
        * score_scale
    )
    remote_part = jnp.concatenate(
        [
            d_keys[row_count:].reshape(-1, model_width),
            d_values[row_count:].reshape(-1, model_width),
        ],
        axis=1,
    )
    own_part = lax.psum_scatter(remote_part, "dp", scatter_dimension=0, tiled=True)
    local_pairs = jnp.concatenate(
        [
            d_keys[:row_count].reshape(row_count, model_width),
            d_values[:row_count].reshape(row_count, model_width),
        ],
        axis=1,
    )
    local_pairs = jnp.concatenate(
        [local_pairs[:latent_start], local_pairs[latent_start:] + own_part], axis=0
    )
    d_projected = jnp.concatenate(
        [d_queries.reshape(row_count, model_width), local_pairs], axis=1
    ).astype(jnp.bfloat16)
    grad_qkv = jnp.dot(d_projected.T, normed, preferred_element_type=jnp.float32)
    d_normed = jnp.dot(d_projected, w_qkv.T, preferred_element_type=jnp.float32)
    unused_rows, first_back = jax.vjp(layer_norm, all_rows, gain_attn)
    d_rows_norm, grad_gain_attn = first_back(d_normed)
    return (
        d_mid + d_rows_norm,
        (grad_gain_attn, grad_qkv, grad_out, grad_gain_mlp, grad_up, grad_down),
    )


def packed(grads, n):
    gain_first, qkv_grad, out_grad, gain_second, up_grad, down_grad = grads
    width = out_grad.shape[0]
    rows = width // n

    def by_rows(grad):
        return grad.reshape(n, -1, rows, width).transpose(1, 0, 2, 3).astype(jnp.bfloat16)

    down = down_grad.reshape(n, rows, -1, width).transpose(2, 0, 1, 3).astype(jnp.bfloat16)
    chunks = jnp.concatenate([down, by_rows(up_grad), by_rows(out_grad), by_rows(qkv_grad)], axis=0)
    gains = jnp.stack([gain_first.reshape(n, rows), gain_second.reshape(n, rows)], axis=1)
    return chunks, jnp.pad(gains, ((0, 0), (0, 6), (0, 128 - rows)))


def shards(
    grid,
    tokens,
    latents,
    slot_group,
    image_groups,
    gain_attn,
    w_qkv,
    w_out,
    gain_mlp,
    w_up,
    w_down,
    d_tokens,
    d_latents,
):
    micro = tokens.shape[0]
    tok_rows = tokens.shape[1]
    lat_rows = latents.shape[1]
    model_width = tokens.shape[2]
    local_groups = tok_rows // GROUP
    section_index = lax.axis_index("section")
    is_global = section_index == 1
    dp_index = lax.axis_index("dp")
    weights = (gain_attn[0], w_qkv[0], w_out[0], gain_mlp[0], w_up[0], w_down[0])
    image_ends = jnp.cumsum(image_groups, axis=1)
    slot_images = jnp.sum(
        (image_ends[:, None, :] <= slot_group[:, :, None]).astype(jnp.int32), axis=2
    )
    slot_total = slot_group.shape[1]
    row_group = jnp.concatenate([jnp.arange(tok_rows) // GROUP, jnp.arange(lat_rows) // LAT])
    row_latent = jnp.concatenate(
        [jnp.zeros((tok_rows,), jnp.bool_), jnp.ones((lat_rows,), jnp.bool_)]
    )
    same_group = row_group[:, None] == row_group[None, :]
    local_mask = jnp.where(
        is_global, (~row_latent)[:, None] & row_latent[None, :] & same_group, same_group
    )
    group_match = row_group[:, None] == jnp.arange(local_groups)[None, :]

    def key_images(batch):
        images_row = lax.dynamic_index_in_dim(slot_images, batch, 0, keepdims=False)
        return (images_row, jnp.broadcast_to(images_row[:, None], (slot_total, LAT)).reshape(-1))

    def allowed_for(batch):
        images_row, key_image = key_images(batch)
        own_images = lax.dynamic_slice_in_dim(images_row, dp_index * local_groups, local_groups)
        row_image = jnp.sum(jnp.where(group_match, own_images[None, :], 0), axis=1)
        remote_mask = is_global & row_latent[:, None] & (row_image[:, None] == key_image[None, :])
        return jnp.concatenate([local_mask, remote_mask], axis=1)

    def forward_turn(received, turn):
        recv_tokens, recv_latents = received
        batch = jnp.clip(turn - section_index, 0, micro - 1)
        own_tok = lax.dynamic_index_in_dim(tokens, batch, 0, keepdims=False)
        own_lat = lax.dynamic_index_in_dim(latents, batch, 0, keepdims=False)
        input_rows = jnp.concatenate(
            [
                jnp.where(is_global, recv_tokens, own_tok),
                jnp.where(is_global, recv_latents, own_lat),
            ],
            axis=0,
        )
        all_rows = input_rows.astype(jnp.float32)
        normed, projected = front_half(all_rows, weights[0], weights[1])
        remote_rows = lax.all_gather(
            latent_operand(projected, tok_rows, model_width), "dp", axis=0, tiled=True
        )
        saved = back_half(all_rows, projected, remote_rows, allowed_for(batch), weights)
        result = saved["result"]
        result_low = result.astype(jnp.bfloat16)
        stored = jnp.where(is_global, result, result_low.astype(jnp.float32))
        passed_on = from_behind((result_low[:tok_rows], result_low[tok_rows:]), "section", 1)
        return passed_on, (input_rows, stored[:tok_rows], stored[tok_rows:])

    nothing = (
        jnp.zeros((tok_rows, model_width), jnp.bfloat16),
        jnp.zeros((lat_rows, model_width), jnp.bfloat16),
    )
    turns = jnp.arange(micro + 1)
    unused_end, (kept_rows, tok_outputs, lat_outputs) = lax.scan(forward_turn, nothing, turns)

    def backward_turn(carry, turn):
        (recv_grad_tok, recv_grad_lat), totals = carry
        raw_batch = micro - turn - section_index
        valid = ((raw_batch >= 0) & (raw_batch < micro)).astype(jnp.float32)
        batch = jnp.clip(raw_batch, 0, micro - 1)
        all_rows = lax.dynamic_index_in_dim(
            kept_rows, batch + section_index, 0, keepdims=False
        ).astype(jnp.float32)
        normed, projected = front_half(all_rows, weights[0], weights[1])
        remote_rows = lax.all_gather(
            latent_operand(projected, tok_rows, model_width), "dp", axis=0, tiled=True
        )
        allowed = allowed_for(batch)
        saved = back_half(all_rows, projected, remote_rows, allowed, weights)
        given = (
            jnp.concatenate(
                [
                    lax.dynamic_index_in_dim(d_tokens, batch, 0, keepdims=False),
                    lax.dynamic_index_in_dim(d_latents, batch, 0, keepdims=False),
                ],
                axis=0,
            )
            * valid
        )
        passed = jnp.concatenate([recv_grad_tok, recv_grad_lat], axis=0).astype(jnp.float32)
        d_result = jnp.where(is_global, given, passed)
        d_rows, grads = section_backward(
            saved, d_result, all_rows, normed, allowed, weights, tok_rows
        )
        totals = tuple((accum + piece for accum, piece in zip(totals, grads)))
        d_rows_low = d_rows.astype(jnp.bfloat16)
        stored = jnp.where(is_global, d_rows_low.astype(jnp.float32), d_rows)
        sent = from_behind((d_rows_low[:tok_rows], d_rows_low[tok_rows:]), "section", -1)
        return (sent, totals), (stored[:tok_rows], stored[tok_rows:])

    totals = tuple(
        jnp.zeros(w.shape[::-1] if w.ndim == 2 else w.shape, jnp.float32) for w in weights
    )
    (unused_sent, totals), (tok_grads, lat_grads) = lax.scan(
        backward_turn, (nothing, totals), turns
    )
    chunks, gains = packed(totals, lax.axis_size("dp"))
    summed, gain_sums = spread(grid, chunks, gains)
    rows = summed.shape[1]
    layer_tokens = lax.dynamic_slice_in_dim(tok_outputs, section_index, micro, 0)[None]
    layer_latents = lax.dynamic_slice_in_dim(lat_outputs, section_index, micro, 0)[None]
    grad_tokens = lax.dynamic_slice_in_dim(tok_grads, 1 - section_index, micro, 0)[::-1][
        None
    ]
    grad_latents = lax.dynamic_slice_in_dim(lat_grads, 1 - section_index, micro, 0)[
        ::-1
    ][None]
    return (
        layer_tokens,
        layer_latents,
        grad_tokens,
        grad_latents,
        gain_sums[0:1, :rows],
        summed[9:].reshape(-1, model_width).T[None],
        summed[8].T[None],
        gain_sums[1:2, :rows],
        summed[4:8].reshape(-1, model_width).T[None],
        summed[0:4].transpose(0, 2, 1).reshape(-1, rows)[None],
    )


F32 = jnp.float32
LOW = jnp.bfloat16
HEAD_PAD = 16
TILE = 256


def nn(a, b):
    return jnp.dot(a, b, preferred_element_type=F32)


def nt(a, b):
    return lax.dot_general(a, b, (((1,), (1,)), ((), ())), preferred_element_type=F32)


def tn(a, b):
    return lax.dot_general(a, b, (((0,), (0,)), ((), ())), preferred_element_type=F32)


def row_mean(values):
    return jnp.mean(values, axis=-1, keepdims=True)


def row_stats(load, spans):
    means = [row_mean(load(r)) for r in spans]
    scales = []
    for r, mean in zip(spans, means):
        centred = load(r) - mean
        scales.append(lax.rsqrt(row_mean(centred * centred) + epsilon))
    return means, scales


def at(start, size):
    return pl.ds(pl.multiple_of(start, size), size)


def class_max(s):
    for by in (16, 32, 64):
        s = jnp.maximum(s, pltpu.roll(s, by, 1))
    return s


def class_sum(s):
    for by in (16, 32, 64):
        s = s + pltpu.roll(s, by, 1)
    return s


def layer_kernel(
    n,
    tokens,
    latents,
    slots,
    slot_at,
    image_at,
    gain_attn,
    gain_mlp,
    w_qkv,
    w_out,
    w_up,
    w_down,
    d_tokens,
    d_latents,
    out_tok,
    out_lat,
    grad_tok,
    grad_lat,
    grads,
    summed,
    gain_sums,
    wq,
    wo,
    wu,
    wd,
    xb,
    n1,
    proj,
    mixed,
    mid,
    n2,
    act,
    dup,
    yb,
    dy,
    ef,
    tmp,
    out,
    probs,
    probs_lat,
    scores,
    slopes,
    turned,
    latf,
    mixf,
    key_mask,
    qbd,
    kbd,
    vbd,
    kv_all,
    kvg_send,
    kvg_recv,
    stage,
    gains,
    leaving,
    own_a,
    own_b,
    land1_a,
    land1_b,
    land2_a,
    land2_b,
    land3_a,
    land3_b,
    land4_a,
    land4_b,
    land_g,
    load_sem,
    stage_sem,
    own_sem,
    leave_sem,
    send_sem,
    recv_sem,
    gain_s,
    gain_r,
    relay_send,
    relay_recv,
    kv_sem_s,
    kv_sem_r,
    kvg_sem_s,
    kvg_sem_r,
):
    rows, width = xb.shape
    ff = act.shape[1]
    tok = tokens.shape[0]
    lat = latents.shape[0]
    half = lat // LAT
    pairs = width // 128
    wide = ff // width
    me = lax.axis_index("dp")
    section = lax.axis_index("section")
    first = section == 0
    second = section == 1
    partner = (me, 1 - section)

    loads = [
        pltpu.make_async_copy(src, dst, load_sem.at[i])
        for i, (src, dst) in enumerate(((w_qkv, wq), (w_out, wo), (w_up, wu), (w_down, wd)))
    ]
    x_loads = [
        pltpu.make_async_copy(tokens, xb.at[0:tok], load_sem.at[4]),
        pltpu.make_async_copy(latents, xb.at[tok:rows], load_sem.at[5]),
    ]
    e_loads = [
        pltpu.make_async_copy(d_tokens, ef.at[0:tok], load_sem.at[6]),
        pltpu.make_async_copy(d_latents, ef.at[tok:rows], load_sem.at[7]),
    ]

    @pl.when(first)
    def _():
        for copy in x_loads:
            copy.start()

    for copy in loads:
        copy.start()

    @pl.when(second)
    def _():
        for copy in e_loads:
            copy.start()

    barrier = pltpu.get_barrier_semaphore()
    pl.semaphore_signal(barrier, inc=1, device_id=partner, device_id_type=MESH)

    here = [lax.rem(me // (1 << bit), 2) for bit in range(4)]

    def across(bit):
        return (me + (1 - 2 * here[bit]) * (1 << bit), section)

    @pl.when(second)
    def _():
        for shift in range(1, n):
            pl.semaphore_signal(
                barrier, inc=1, device_id=(lax.rem(me + shift, n), section), device_id_type=MESH
            )
        pl.semaphore_wait(barrier, n)

    @pl.when(first)
    def _():
        for bit in range(4):
            pl.semaphore_signal(barrier, inc=1, device_id=across(bit), device_id_type=MESH)
        pl.semaphore_wait(barrier, 5)

    def relay(back, band):
        r = at(band * (rows // 3), rows // 3)
        return pltpu.make_async_remote_copy(
            src_ref=yb.at[r],
            dst_ref=(dy if back else xb).at[r],
            send_sem=relay_send.at[3 * back + band],
            recv_sem=relay_recv.at[3 * back + band],
            device_id=partner,
            device_id_type=MESH,
        )

    def kv_copy(shift, incoming):
        slot = lax.rem(me + n - shift, n) if incoming else me
        return pltpu.make_async_remote_copy(
            src_ref=kv_all.at[me], dst_ref=kv_all.at[slot],
            send_sem=kv_sem_s.at[shift - 1], recv_sem=kv_sem_r.at[shift - 1],
            device_id=(lax.rem(me + shift, n), section), device_id_type=MESH,
        )

    def kvg_copy(shift):
        there = lax.rem(me + shift, n)
        return pltpu.make_async_remote_copy(
            src_ref=kvg_send.at[there], dst_ref=kvg_recv.at[shift - 1],
            send_sem=kvg_sem_s.at[shift - 1], recv_sem=kvg_sem_r.at[shift - 1],
            device_id=(there, section), device_id_type=MESH,
        )

    chunks = [slice(c, c + 64) for c in range(0, GROUP, 64)]
    lane = lax.broadcasted_iota(jnp.int32, (1, 128), 1)
    halves = [(lane < 64).astype(F32).astype(LOW), (lane >= 64).astype(F32).astype(LOW)]
    eighths = [(h.astype(F32) * 0.125).astype(LOW) for h in halves]
    heads = (
        lax.broadcasted_iota(jnp.int32, (HEAD_PAD, width), 1) // 64
        == lax.broadcasted_iota(jnp.int32, (HEAD_PAD, width), 0)
    ).astype(F32)

    def block_diagonal(dst, base, src, row, column, scale):
        def one(i, carry):
            line = src[pl.ds(row + i, 1), column : column + width] * scale
            dst[at(base + i * HEAD_PAD, HEAD_PAD), :] = (line * heads).astype(LOW)
            return carry

        lax.fori_loop(0, LAT, one, 0)

    def head_sum(dst, row, column, value, scale, add, pad):
        pad[0 : LAT * HEAD_PAD, :] = value

        def one(i, carry):
            line = jnp.sum(pad[at(i * HEAD_PAD, HEAD_PAD), :] * heads, axis=0, keepdims=True)
            line = line * scale
            spot = pl.ds(row + i, 1)
            if add:
                line = line + dst[spot, column : column + width]
            dst[spot, column : column + width] = line
            return carry

        lax.fori_loop(0, LAT, one, 0)

    def bands(body, lo, hi, size):
        def one(i, carry):
            body(pl.ds(pl.multiple_of(lo + i * size, 16), size))
            return carry

        lax.fori_loop(0, (hi - lo) // size, one, 0)

    third = rows // 3

    def deep(dst, base, count, product):
        def one(i, carry):
            c = at((i // count) * TILE, TILE)
            piece = lax.rem(i, count)
            part = product(c, at(piece * width, width))
            if base is None:
                dst[:, c] = jnp.where(piece == 0, 0.0, dst[:, c]) + part
            else:
                dst[:, c] = jnp.where(piece == 0, base[:, c], dst[:, c]) + part
            return carry

        lax.fori_loop(0, width // TILE * count, one, 0)


    def grouped(body, lo, hi, count):
        def one(i, carry):
            base = lo + i * 16 * count
            body([pl.ds(pl.multiple_of(base + 16 * g, 16), 16) for g in range(count)])
            return carry

        trips = (hi - lo) // (16 * count) if isinstance(lo, int) else 1
        lax.fori_loop(0, trips, one, 0)

    def norm(load, gain, dst, lo, hi, count):
        def body(spans):
            means, scales = row_stats(load, spans)
            for r, mean, scale in zip(spans, means, scales):
                dst[r, :] = ((load(r) - mean) * scale * gain[...]).astype(LOW)

        grouped(body, lo, hi, count)

    def norm_back(load, grad, gain, gain_rows, store, lo, hi, count):
        def body(spans):
            means, scales = row_stats(load, spans)
            firsts, seconds = [], []
            kept = gains[0, gain_rows, :]
            for r, mean, scale in zip(spans, means, scales):
                along = grad[r, :] * ((load(r) - mean) * scale)
                kept = kept + along[0:8] + along[8:16]
                firsts.append(row_mean(grad[r, :] * gain[...]))
                seconds.append(row_mean(along * gain[...]))
            gains[0, gain_rows, :] = kept
            for r, mean, scale, one, two in zip(spans, means, scales, firsts, seconds):
                hat = (load(r) - mean) * scale
                store(r, ef[r, :] + scale * (grad[r, :] * gain[...] - one - hat * two))

        grouped(body, lo, hi, count)

    def tiles(count, body, size=TILE):
        def one(i, carry):
            body(at(i * size, size))
            return carry

        lax.fori_loop(0, count, one, 0)

    @pl.when(first)
    def _():
        for copy in x_loads:
            copy.wait()

    @pl.when(second)
    def _():
        spots = lax.broadcasted_iota(jnp.int32, (n, n * lat), 1) // lat
        spread_out = (spots == lax.broadcasted_iota(jnp.int32, (n, n * lat), 0)).astype(F32)
        groups = nn(slots[...].astype(F32).astype(LOW), spread_out.astype(LOW))
        of_micro = lax.rem(lax.broadcasted_iota(jnp.int32, (1, n * lat), 1), lat) // LAT
        for m in range(half):
            images = jnp.zeros((1, n * lat), F32)
            own_image = jnp.float32(0)
            end = jnp.int32(0)
            for i in range(image_at.shape[1]):
                end = end + image_at[m, i]
                images += jnp.where(end.astype(F32) <= groups[m : m + 1], 1.0, 0.0)
                own_image += jnp.where(end <= slot_at[m, me], 1.0, 0.0)
            seen = (images == own_image) & (of_micro == m)
            key_mask[m : m + 1, :] = jnp.where(seen, 0.0, masked_score)
        for band in range(3):
            relay(0, band).wait_recv()

    def load_in(r):
        return xb[r, :].astype(F32)

    def load_mid(r):
        return mid[r, :]

    norm(load_in, gain_attn, n1, 0, rows, 11)
    loads[0].wait()

    @pl.when(second)
    def _():
        own = nn(n1[tok:rows, :], wq[:, width:]).astype(LOW)
        kv_all[me] = own
        latf[:, width:] = own.astype(F32)
        for shift in range(1, n):
            kv_copy(shift, False).start()

    def project(c):
        proj[:, c] = nn(n1[...], wq[:, c]).astype(LOW)

    per = width // TILE
    tiles(jnp.where(first, 3 * per, per), project)

    def lat_bias(m, shape, axis):
        return jnp.where(
            lax.broadcasted_iota(jnp.int32, shape, axis) // LAT == m, 0.0, masked_score
        ).astype(F32)

    @pl.when(first)
    def _():
        latf[...] = proj[tok:rows, :].astype(F32)

        def one_pair(it, side):
            m, p = it // pairs, lax.rem(it, pairs)
            r = at(m * GROUP, GROUP)
            q = proj[r, at(p * 128, 128)]
            k = proj[r, at(width + p * 128, 128)]
            v = proj[r, at(2 * width + p * 128, 128)]
            kl = proj[tok:rows, at(width + p * 128, 128)]
            vl = proj[tok:rows, at(2 * width + p * 128, 128)]
            bias = lat_bias(m, (lat, GROUP), 0)
            total = jnp.zeros((GROUP, 128), F32)
            for e in (0, 1):
                qe = q * eighths[e]
                s = scores.at[2 * side + e]
                s[...] = nt(k, qe)
                sl = nt(kl, qe) + bias
                top = jnp.max(sl, axis=0, keepdims=True)
                for c in chunks:
                    top = jnp.maximum(top, jnp.max(s[c, :], axis=0, keepdims=True))
                el = jnp.exp(sl - top)
                whole_sum = jnp.sum(el, axis=0, keepdims=True)
                for c in chunks:
                    et = jnp.exp(s[c, :] - top)
                    s[c, :] = et
                    whole_sum += jnp.sum(et, axis=0, keepdims=True)
                scale = 1.0 / whole_sum
                for c in chunks:
                    probs[2 * it + e, c, :] = (s[c, :] * scale).astype(LOW)
                pe = (el * scale).astype(LOW)
                probs[2 * it + e, GROUP : GROUP + lat, :] = pe
                total += tn(probs[2 * it + e, 0:GROUP, :], v * halves[e])
                total += tn(pe, vl * halves[e])
            mixed[r, at(p * 128, 128)] = total.astype(LOW)

        def pair(i, carry):
            one_pair(i, 0)
            return carry

        lax.fori_loop(0, half * pairs, pair, 0)
        for m in range(half):
            r = slice(m * GROUP, (m + 1) * GROUP)
            b = slice(m * 128, (m + 1) * 128)
            block_diagonal(qbd, m * 128, latf, m * LAT, 0, 0.125)
            s = nt(qbd[b, :], proj[r, width : 2 * width])
            sl = nt(qbd[b, :], proj[tok:rows, width : 2 * width]) + lat_bias(m, (128, lat), 1)
            top = jnp.maximum(
                jnp.max(s, axis=1, keepdims=True), jnp.max(sl, axis=1, keepdims=True)
            )
            et = jnp.exp(s - top)
            el = jnp.exp(sl - top)
            scale = 1.0 / (
                jnp.sum(et, axis=1, keepdims=True) + jnp.sum(el, axis=1, keepdims=True)
            )
            pt = (et * scale).astype(LOW)
            pe = (el * scale).astype(LOW)
            probs_lat[b, 0:GROUP] = pt
            probs_lat[b, GROUP : GROUP + lat] = pe
            o = nn(pt, proj[r, 2 * width :]) + nn(pe, proj[tok:rows, 2 * width :])
            head_sum(mixf, m * LAT, 0, o, 1.0, False, mid)
        mixed[tok:rows, :] = mixf[...].astype(LOW)

    keys = n * lat

    @pl.when(second)
    def _():
        latf[:, :width] = proj[tok:rows, :width].astype(F32)
        for m in range(half):
            r = slice(m * GROUP, (m + 1) * GROUP)
            b = slice(m * 128, (m + 1) * 128)
            block_diagonal(qbd, m * 128, latf, m * LAT, 0, 0.125)
            block_diagonal(kbd, m * 128, latf, m * LAT, width, 1.0)
            block_diagonal(vbd, m * 128, latf, m * LAT, 2 * width, 1.0)
            s = nt(proj[r, :width] * jnp.asarray(0.125, LOW), kbd[b, :])
            et = jnp.exp(s - class_max(s))
            pt = (et / class_sum(et)).astype(LOW)
            probs[m, 0:GROUP, 0:128] = pt
            mixed[r, :] = nn(pt, vbd[b, :]).astype(LOW)

    root = 0.7978845608028654

    def mlp_in(lo, hi, count):
        r0 = slice(lo, hi)

        def attend_out(c):
            mid[r0, c] = xb[r0, c].astype(F32) + nn(mixed[r0, :], wo[:, c])

        tiles(width // TILE, attend_out)
        norm(load_mid, gain_mlp, n2, lo, hi, count)

        def widen(i, carry):
            c = at(i * TILE, TILE)
            tmp[r0, 0:TILE] = nn(n2[r0, :], wu[:, c])

            def gelu(spans):
                for r in spans:
                    up = tmp[r, 0:TILE]
                    square = up * up
                    t = jnp.tanh(up * (root + (root * 0.044715) * square))
                    gate = 0.5 + 0.5 * t
                    value = up * gate
                    slope = gate + (value + value) * (1.0 - gate) * (
                        root + (3.0 * root * 0.044715) * square
                    )
                    act[r, c] = value.astype(LOW)
                    dup[r, c] = slope.astype(LOW)

            grouped(gelu, lo, hi, count)
            return carry

        lax.fori_loop(0, ff // TILE, widen, 0)

    for copy in loads[1:]:
        copy.wait()

    @pl.when(second)
    def _():
        for shift in range(1, n):
            kv_copy(shift, True).wait_recv()
        k = kv_all[:, :, :width].reshape(keys, width)
        v = kv_all[:, :, width:].reshape(keys, width)
        for m in range(half):
            b = slice(m * 128, (m + 1) * 128)
            s = nt(qbd[b, :], k) + key_mask[m : m + 1, :]
            et = jnp.exp(s - jnp.max(s, axis=1, keepdims=True))
            pt = (et / jnp.sum(et, axis=1, keepdims=True)).astype(LOW)
            probs_lat[b, 0:keys] = pt
            head_sum(mixf, m * LAT, 0, nn(pt, v), 1.0, False, mid)
        mixed[tok:rows, :] = mixf[...].astype(LOW)


    mlp_in(0, rows, 11)

    out_copies = [
        pltpu.make_async_copy(out.at[0:tok], out_tok, load_sem.at[8]),
        pltpu.make_async_copy(out.at[tok:rows], out_lat, load_sem.at[9]),
    ]
    grad_copies = [
        pltpu.make_async_copy(out.at[0:tok], grad_tok, load_sem.at[8]),
        pltpu.make_async_copy(out.at[tok:rows], grad_lat, load_sem.at[9]),
    ]

    def layer_output(passed_on):
        deep(out, mid, wide, lambda c, d: nn(act[:, d], wd[d, c]))
        if passed_on:

            def pass_on(band, carry):
                r = at(band * third, third)
                low = out[r, :].astype(LOW)
                yb[r, :] = low
                out[r, :] = low.astype(F32)
                relay(0, band).start()
                return carry

            lax.fori_loop(0, 3, pass_on, 0)
        for copy in out_copies:
            copy.start()

    @pl.when(first)
    def _():
        layer_output(True)
        for band in range(3):
            relay(1, band).wait_recv()

        def widen_e(r):
            ef[r, :] = dy[r, :].astype(F32)

        bands(widen_e, 0, rows, third)

    @pl.when(second)
    def _():
        for copy in e_loads:
            copy.wait()

        def narrow_e(r):
            dy[r, :] = ef[r, :].astype(LOW)

        bands(narrow_e, 0, rows, third)

    part = 384
    unit = width // n
    many = part // unit

    def staged(slot, piece, chunk, share):
        return pltpu.make_async_copy(
            stage.at[slot, piece],
            grads.at[
                chunk,
                share // 8,
                lax.rem(share // 4, 2),
                lax.rem(share // 2, 2),
                lax.rem(share, 2),
            ],
            stage_sem.at[slot, piece],
        )

    def drain(slot):
        def one(piece, carry):
            staged(slot, piece, 0, 0).wait()
            return carry

        lax.fori_loop(0, many, one, 0)

    def weight_grad(place, start, count, depth, left, right, many_rights=1):
        def one(i, carry):
            turned[:, 0:depth] = left(i).T
            for at_right in range(many_rights):
                tile = i * many_rights + at_right
                slot = lax.rem(tile, 2)

                @pl.when(tile >= start * many_rights + 2)
                def _():
                    drain(slot)

                def columns(c):
                    value = nn(turned[:, 0:depth], right(at_right, c)).astype(LOW)
                    for piece in range(many):
                        stage[slot, piece, :, c] = value[piece * unit : (piece + 1) * unit]

                tiles(width // TILE, columns)

                def leave_piece(piece, carry):
                    staged(slot, piece, *place(i, at_right, piece)).start()
                    return carry

                lax.fori_loop(0, many, leave_piece, 0)
            return carry

        lax.fori_loop(start, start + count, one, 0)
        for slot in (0, 1):
            drain(slot)

    orders = ((0, 2, 1, 3), (1, 2, 0, 3))
    own_buf = (own_a, own_b)
    land = (
        (land1_a, land1_b),
        (land2_a, land2_b),
        (land3_a, land3_b),
        (land4_a, land4_b),
    )
    spread_pairs = land1_a.shape[0]

    def source(stream, phase, k, theirs):
        pick = [(1 - here[bit]) if theirs else here[bit] for bit in orders[stream]]
        own_bit = [here[bit] for bit in orders[stream]]
        base = land[0][stream]
        if phase == 0:
            if stream == 0:
                return grads.at[2 * k, :, :, :, pick[0]]
            return grads.at[2 * k + 1, :, :, pick[0]]
        if phase == 1:
            return base.at[k, :, pick[1]]
        if phase == 2:
            return base.at[k, :, own_bit[1], pick[2]]
        return base.at[k, pick[3], own_bit[1], own_bit[2]]

    def copy_of(stream, phase, k):
        return pltpu.make_async_remote_copy(
            src_ref=source(stream, phase, k, True),
            dst_ref=land[phase][stream].at[k],
            send_sem=send_sem.at[stream, phase, k],
            recv_sem=recv_sem.at[stream, phase, k],
            device_id=across(orders[stream][phase]),
            device_id_type=MESH,
        )

    def own(stream, k):
        return pltpu.make_async_copy(
            source(stream, 0, k, False), own_buf[stream], own_sem.at[stream]
        )

    def leave(stream, k):
        slot = lax.rem(k, 2)
        return pltpu.make_async_copy(
            leaving.at[slot, stream], summed.at[2 * k + stream], leave_sem.at[slot, stream]
        )

    def launch(phase, k):
        for stream in (0, 1):
            copy_of(stream, phase, k).start()

    def absorb(phase, k):
        for stream in (0, 1):
            if phase == 0:
                own(stream, k).wait()
            copy_of(stream, phase, k).wait_recv()
            base, into = land[0][stream], land[phase][stream]
            mine = [here[bit] for bit in orders[stream]]
            if phase == 0:

                def add(at_share, carry):
                    spot = (at_share // 4, lax.rem(at_share // 2, 2), lax.rem(at_share, 2))
                    total = own_buf[stream][spot].astype(F32) + base[(k, *spot)].astype(F32)
                    base[(k, *spot)] = total.astype(LOW)
                    return carry

                lax.fori_loop(0, 8, add, 0)
            elif phase == 1:

                def add(at_share, carry):
                    i, h = at_share // 2, lax.rem(at_share, 2)
                    total = base[k, i, mine[1], h].astype(F32) + into[k, i, h].astype(F32)
                    base[k, i, mine[1], h] = total.astype(LOW)
                    return carry

                lax.fori_loop(0, 4, add, 0)
            elif phase == 2:
                for i in (0, 1):
                    total = base[k, i, mine[1], mine[2]].astype(F32)
                    total += into[k, i].astype(F32)
                    base[k, i, mine[1], mine[2]] = total.astype(LOW)
            else:
                total = base[k, mine[3], mine[1], mine[2]].astype(F32)
                total += into[k].astype(F32)
                slot = lax.rem(k, 2)

                @pl.when(k >= 2)
                def _():
                    leave(stream, k - 2).wait()

                leaving[slot, stream] = total
                leave(stream, k).start()

    def start_own(k):
        for stream in (0, 1):
            own(stream, k).start()

    def run(phase, lo, hi):
        def one(k, carry):
            if phase == 0:
                start_own(k)
            absorb(phase, k)
            if phase < 3:
                launch(phase + 1, k)
            return carry

        lax.fori_loop(lo, hi, one, 0)

    per_part = width // part

    def up_grad():
        weight_grad(
            lambda i, right, piece: (
                wide + lax.rem(i * many + piece, wide),
                (i * many + piece) // wide,
            ),
            0,
            ff // part,
            rows,
            lambda i: dup[:, at(i * part, part)],
            lambda right, c: n2[:, c],
        )
        launch(0, 2)
        launch(0, 3)

    def down_grad(pair, carry):
        def both(side, carry):
            chunk = 2 * pair + side
            weight_grad(
                lambda i, right, piece: (chunk, i * many + piece),
                0,
                per_part,
                rows,
                lambda i: dy[:, at(i * part, part)],
                lambda right, c: act[:, pl.ds(pl.multiple_of(chunk * width + c.start, TILE), TILE)],
            )
            return carry

        lax.fori_loop(0, 2, both, 0)
        launch(0, pair)
        return carry

    lax.fori_loop(0, 2, down_grad, 0)

    def unwiden(c):
        dup[:, c] = (nt(dy[...], wd[c, :]) * dup[:, c].astype(F32)).astype(LOW)

    tiles(ff // TILE, unwiden)
    @pl.when(first)
    def _():
        up_grad()

    deep(tmp, None, wide, lambda c, d: nt(dup[:, d], wu[c, d]))
    gains[0] = jnp.zeros_like(gains[0])

    def store_mid(r, total):
        ef[r, :] = total
        dy[r, :] = total.astype(LOW)

    norm_back(load_mid, tmp, gain_mlp, slice(8, 16), store_mid, 0, rows, 11)

    @pl.when(first)
    def _():
        for band in range(3):
            relay(0, band).wait_send()

    def to_mix(c):
        yb[:, c] = nt(dy[...], wo[c, :]).astype(LOW)

    tiles(width // TILE, to_mix)
    mixf[...] = yb[tok:rows, :].astype(F32)

    @pl.when(second)
    def _():
        k = kv_all[:, :, :width].reshape(keys, width)
        v = kv_all[:, :, width:].reshape(keys, width)
        for m in range(half):
            b = slice(m * 128, (m + 1) * 128)
            block_diagonal(vbd.at[pl.ds(256, 256)], m * 128, mixf, m * LAT, 0, 1.0)
        both = slice(0, half * 128)
        do = vbd[256 : 256 + half * 128, :]
        pt = probs_lat[both, 0:keys]
        pf = pt.astype(F32)
        dp = nt(do, v)
        along = jnp.sum(pf * dp, axis=1, keepdims=True)
        ds = (pf * (dp - along)).astype(LOW)
        kvg_send[:, :, :width] = tn(ds, qbd[both, :]).astype(LOW).reshape(n, lat, width)
        kvg_send[:, :, width:] = tn(pt, do).astype(LOW).reshape(n, lat, width)
        for shift in range(1, n):
            kvg_copy(shift).start()
        dq = nn(ds, k)
        for m in range(half):
            head_sum(latf, m * LAT, 0, dq[m * 128 : (m + 1) * 128], 0.125, False, tmp)
        proj[tok:rows, :width] = latf[:, :width].astype(LOW)
        layer_output(False)

    weight_grad(
        lambda i, right, piece: (2 * wide, i * many + piece),
        0,
        width // part,
        rows,
        lambda i: dy[:, at(i * part, part)],
        lambda right, c: mixed[:, c],
    )
    for copy in out_copies:
        copy.wait()

    @pl.when(first)
    def _():
        for m in range(half):
            r = slice(m * GROUP, (m + 1) * GROUP)
            b = slice(m * 128, (m + 1) * 128)
            block_diagonal(vbd, m * 128, mixf, m * LAT, 0, 1.0)
            do = vbd[b, :]
            dp = nt(do, proj[r, 2 * width :])
            dl = nt(do, proj[tok:rows, 2 * width :])
            pt = probs_lat[b, 0:GROUP]
            pe = probs_lat[b, GROUP : GROUP + lat]
            pf = pt.astype(F32)
            pg = pe.astype(F32)
            along = jnp.sum(pf * dp, axis=1, keepdims=True) + jnp.sum(
                pg * dl, axis=1, keepdims=True
            )
            ds = (pf * (dp - along)).astype(LOW)
            dsl = (pg * (dl - along)).astype(LOW)
            dq = nn(ds, proj[r, width : 2 * width]) + nn(dsl, proj[tok:rows, width : 2 * width])
            head_sum(latf, m * LAT, 0, dq, 0.125, False, mid)
            tmp[r, :] = tn(ds, qbd[b, :])
            out[r, :] = tn(pt, do)
            if m == 0:
                tmp[tok:rows, :] = tn(dsl, qbd[b, :])
                out[tok:rows, :] = tn(pe, do)
            else:
                tmp[tok:rows, :] += tn(dsl, qbd[b, :])
                out[tok:rows, :] += tn(pe, do)
        proj[tok:rows, :width] = latf[:, :width].astype(LOW)

        def one_pair(it, side):
            m, p = it // pairs, lax.rem(it, pairs)
            r = at(m * GROUP, GROUP)
            qc = at(p * 128, 128)
            q = proj[r, qc]
            k = proj[r, at(width + p * 128, 128)]
            v = proj[r, at(2 * width + p * 128, 128)]
            kl = proj[tok:rows, at(width + p * 128, 128)]
            vl = proj[tok:rows, at(2 * width + p * 128, 128)]
            dx = yb[r, qc]
            dq = jnp.zeros((GROUP, 128), F32)
            dk = tmp[r, qc]
            dv = out[r, qc]
            dkl = tmp[tok:rows, qc]
            dvl = out[tok:rows, qc]
            for e in (0, 1):
                qe = q * eighths[e]
                de = dx * halves[e]
                s = scores.at[2 * side + e]
                s[...] = nt(v, de)
                dl = nt(vl, de)
                pt = probs[2 * it + e, 0:GROUP, :]
                pe = probs[2 * it + e, GROUP : GROUP + lat, :]
                pg = pe.astype(F32)
                along = jnp.sum(pg * dl, axis=0, keepdims=True)
                for c in chunks:
                    pf = probs[2 * it + e, c, :].astype(F32)
                    along += jnp.sum(pf * s[c, :], axis=0, keepdims=True)
                for c in chunks:
                    pf = probs[2 * it + e, c, :].astype(F32)
                    slopes[2 * side + e, c, :] = (pf * (s[c, :] - along)).astype(LOW)
                ds = slopes[2 * side + e]
                dsl = (pg * (dl - along)).astype(LOW)
                dq += tn(ds, k * halves[e]) + tn(dsl, kl * halves[e])
                dk += nn(ds, qe)
                dkl += nn(dsl, qe)
                dv += nn(pt, de)
                dvl += nn(pe, de)
            proj[r, qc] = (dq * 0.125).astype(LOW)
            proj[r, at(width + p * 128, 128)] = dk.astype(LOW)
            proj[r, at(2 * width + p * 128, 128)] = dv.astype(LOW)
            tmp[tok:rows, qc] = dkl
            out[tok:rows, qc] = dvl

        def pair(i, carry):
            one_pair(i, 0)
            return carry

        lax.fori_loop(0, half * pairs, pair, 0)
        proj[tok:rows, width : 2 * width] = tmp[tok:rows, :].astype(LOW)
        proj[tok:rows, 2 * width :] = out[tok:rows, :].astype(LOW)

    @pl.when(second)
    def _():
        for m in range(half):
            r = slice(m * GROUP, (m + 1) * GROUP)
            b = slice(m * 128, (m + 1) * 128)
            pt = probs[m, 0:GROUP, 0:128]
            pf = pt.astype(F32)
            dx = yb[r, :]
            dp = nt(dx, vbd[b, :])
            ds = (pf * (dp - class_sum(pf * dp))).astype(LOW)
            dk = tn(ds, proj[r, :width])
            dv = tn(pt, dx)
            proj[r, :width] = (nn(ds, kbd[b, :]) * 0.125).astype(LOW)
            head_sum(latf, m * LAT, width, dk, 0.125, False, tmp)
            head_sum(latf, m * LAT, 2 * width, dv, 1.0, False, tmp)
        total = latf[:, width:] + kvg_send[me].astype(F32)
        for shift in range(1, n):
            kvg_copy(shift).wait_recv()
            total += kvg_recv[shift - 1].astype(F32)
        proj[tok:rows, width:] = total.astype(LOW)

    @pl.when(first)
    def _():
        run(0, 0, 2)

    deep(tmp, None, jnp.where(first, 3, 1), lambda c, d: nt(proj[:, d], wq[c, d]))

    @pl.when(second)
    def _():
        tmp[tok:rows, :] += nt(proj[tok:rows, width:], wq[:, width:])

    def store_in(r, total):
        low = total.astype(LOW)
        yb[r, :] = low
        out[r, :] = jnp.where(first, total, low.astype(F32))

    def band_back(band, carry):
        low = band * third
        norm_back(load_in, tmp, gain_attn, slice(0, 8), store_in, low, low + third, 11)

        @pl.when(second)
        def _():
            relay(1, band).start()

        return carry

    lax.fori_loop(0, 3, band_back, 0)
    for copy in grad_copies:
        copy.start()

    @pl.when(second)
    def _():
        up_grad()
        run(0, 0, 2)

    run(0, 2, 4)

    def qkv_grad(start, count, r):
        weight_grad(
            lambda i, right, piece: (
                2 * wide + 1 + lax.rem(i * many + piece, 3),
                (i * many + piece) // 3,
            ),
            start,
            count,
            r.stop - r.start,
            lambda i: proj[r, at(i * part, part)],
            lambda right, c: n1[r, c],
        )

    qkv_grad(0, jnp.where(first, 3 * per_part, per_part), slice(0, rows))

    @pl.when(second)
    def _():
        qkv_grad(per_part, 2 * per_part, slice(tok, rows))

    for pair in range(4, spread_pairs):
        launch(0, pair)

    def gain_copy(bit):
        return pltpu.make_async_remote_copy(
            src_ref=gains.at[bit],
            dst_ref=land_g.at[bit],
            send_sem=gain_s.at[bit],
            recv_sem=gain_r.at[bit],
            device_id=across(bit),
            device_id_type=MESH,
        )

    def gain_step(bit):
        gain_copy(bit).wait_recv()
        gains[bit + 1] = gains[bit] + land_g[bit]

    gain_copy(0).start()
    run(1, 0, 4)
    gain_step(0)
    gain_copy(1).start()
    run(0, 4, 6)
    run(2, 0, 4)
    gain_step(1)
    gain_copy(2).start()
    run(1, 4, 6)
    run(3, 0, 4)
    gain_step(2)
    gain_copy(3).start()
    run(2, 4, 6)
    gain_step(3)
    run(3, 4, 6)
    final = gains[4]
    for i in (0, 1):
        whole_gain = jnp.sum(final[8 * i : 8 * i + 8], axis=0, keepdims=True)
        whole_gain = jnp.broadcast_to(whole_gain, (8, width))
        rolled = pltpu.roll(whole_gain, lax.rem(width - me * unit, width), 1)
        gain_sums[8 * i : 8 * i + 8, :] = rolled[:, 0:128]

    def finish(k, carry):
        for stream in (0, 1):
            for phase in range(4):
                copy_of(stream, phase, k).wait_send()
        return carry

    lax.fori_loop(0, spread_pairs, finish, 0)
    for bit in range(4):
        gain_copy(bit).wait_send()
    for copy in grad_copies:
        copy.wait()
    for stream in (0, 1):
        for pair in (spread_pairs - 2, spread_pairs - 1):
            leave(stream, pair).wait()

    @pl.when(second)
    def _():
        for band in range(3):
            relay(1, band).wait_send()
        for shift in range(1, n):
            kv_copy(shift, False).wait_send()
            kvg_copy(shift).wait_send()


def both_layers(n, tokens, latents, slots, images, gains, weights, d_tokens, d_latents):
    tok, width = tokens.shape
    lat = latents.shape[0]
    rows = tok + lat
    w_qkv, w_out, w_up, w_down = weights
    ff = w_up.shape[1]
    keys = n * lat
    half = lat // LAT
    size = sum(w.size for w in weights)
    chunks = size // (width * width)
    pairs = chunks // 2
    unit = width // n
    vm, hbm = pl.BlockSpec(memory_space=pltpu.VMEM), pl.BlockSpec(memory_space=pl.ANY)
    sm = pl.BlockSpec(memory_space=pltpu.SMEM)
    scratch = [
        pltpu.VMEM(w.shape, LOW) for w in (w_qkv, w_out, w_up, w_down)
    ] + [
        pltpu.VMEM(shape, dtype)
        for shape, dtype in (
            ((rows, width), LOW),
            ((rows, width), LOW),
            ((rows, 3 * width), LOW),
            ((rows, width), LOW),
            ((rows, width), F32),
            ((rows, width), LOW),
            ((rows, ff), LOW),
            ((rows, ff), LOW),
            ((rows, width), LOW),
            ((rows, width), LOW),
            ((rows, width), F32),
            ((rows, width), F32),
            ((rows, width), F32),
            ((half * width // 64, GROUP + lat, GROUP), LOW),
            ((half * 128, max(keys, GROUP + 128)), LOW),
            ((2, GROUP, GROUP), F32),
            ((2, GROUP, GROUP), LOW),
            ((384, rows), LOW),
            ((lat, 3 * width), F32),
            ((lat, width), F32),
            ((8, keys), F32),
            ((half * 128, width), LOW),
            ((half * 128, width), LOW),
            ((half * 256, width), LOW),
            ((n, lat, 2 * width), LOW),
            ((n, lat, 2 * width), LOW),
            ((n - 1, lat, 2 * width), LOW),
            ((2, 384 // unit, unit, width), LOW),
            ((5, 16, width), F32),
            ((2, 2, unit, width), F32),
            ((2, 2, 2, unit, width), LOW),
            ((2, 2, 2, unit, width), LOW),
            ((pairs, 2, 2, 2, unit, width), LOW),
            ((pairs, 2, 2, 2, unit, width), LOW),
            ((pairs, 2, 2, unit, width), LOW),
            ((pairs, 2, 2, unit, width), LOW),
            ((pairs, 2, unit, width), LOW),
            ((pairs, 2, unit, width), LOW),
            ((pairs, unit, width), LOW),
            ((pairs, unit, width), LOW),
            ((4, 16, width), F32),
        )
    ] + [
        pltpu.SemaphoreType.DMA((10,)),
        pltpu.SemaphoreType.DMA((2, 384 // unit)),
        pltpu.SemaphoreType.DMA((2,)),
        pltpu.SemaphoreType.DMA((2, 2)),
        pltpu.SemaphoreType.DMA((2, 4, pairs)),
        pltpu.SemaphoreType.DMA((2, 4, pairs)),
        pltpu.SemaphoreType.DMA((4,)),
        pltpu.SemaphoreType.DMA((4,)),
        pltpu.SemaphoreType.DMA((6,)),
        pltpu.SemaphoreType.DMA((6,)),
        pltpu.SemaphoreType.DMA((n - 1,)),
        pltpu.SemaphoreType.DMA((n - 1,)),
        pltpu.SemaphoreType.DMA((n - 1,)),
        pltpu.SemaphoreType.DMA((n - 1,)),
    ]
    return pl.pallas_call(
        functools.partial(layer_kernel, n),
        out_shape=(
            jax.ShapeDtypeStruct((tok, width), F32),
            jax.ShapeDtypeStruct((lat, width), F32),
            jax.ShapeDtypeStruct((tok, width), F32),
            jax.ShapeDtypeStruct((lat, width), F32),
            jax.ShapeDtypeStruct((chunks, 2, 2, 2, 2, unit, width), LOW),
            jax.ShapeDtypeStruct((chunks, unit, width), F32),
            jax.ShapeDtypeStruct((16, 128), F32),
        ),
        in_specs=[hbm, hbm, vm, sm, sm, vm, vm] + [hbm] * 6,
        out_specs=(hbm,) * 6 + (vm,),
        scratch_shapes=scratch,
        compiler_params=pltpu.CompilerParams(
            collective_id=1, has_side_effects=True, vmem_limit_bytes=63 * 1024 * 1024
        ),
        cost_estimate=pl.CostEstimate(
            flops=6 * rows * size, bytes_accessed=4 * size, transcendentals=0
        ),
    )(tokens, latents, slots, slots, images, *gains, *weights, d_tokens, d_latents)


def finish_kernel(width, *refs):
    rows_in, (summed, gains), rows_out = refs[0:4], refs[4:6], refs[6:10]
    gain_attn, g_qkv, g_out, gain_mlp, g_up, g_down = refs[10:16]
    held, (sem_in, sem_out) = refs[16:21], refs[21:23]
    wide = g_down.shape[1] // width
    unit = g_out.shape[1]
    loads = [
        pltpu.make_async_copy(src, dst, sem_in.at[i])
        for i, (src, dst) in enumerate(zip((*rows_in, summed), held))
    ]
    for load in loads:
        load.start()
    all_rows, sums = held[0:4], held[4]
    moves = [[pair] for pair in zip(all_rows, rows_out)] + [
        [(sums.at[c], g_down.at[:, c * width : (c + 1) * width]) for c in range(wide)]
        + [
            (sums.at[wide : 2 * wide], g_up),
            (sums.at[2 * wide : 2 * wide + 1], g_out),
            (sums.at[2 * wide + 1 :], g_qkv),
        ]
    ]
    gain_attn[...] = gains[0:1, 0:unit]
    gain_mlp[...] = gains[8:9, 0:unit]
    started = []
    for load, group in zip(loads, moves):
        load.wait()
        for src, dst in group:
            started.append(pltpu.make_async_copy(src, dst, sem_out.at[len(started)]))
            started[-1].start()
    for move in started:
        move.wait()


def finished(rows, summed, gains, wide):
    chunks, unit, width = summed.shape
    hbm, vm = pl.BlockSpec(memory_space=pl.ANY), pl.BlockSpec(memory_space=pltpu.VMEM)
    shapes = [r.shape for r in rows] + [
        (1, unit),
        (3, unit, width),
        (1, unit, width),
        (1, unit),
        (wide, unit, width),
        (unit, wide * width),
    ]
    return pl.pallas_call(
        functools.partial(finish_kernel, width),
        out_shape=tuple(jax.ShapeDtypeStruct(s, F32) for s in shapes),
        in_specs=[hbm] * 5 + [vm],
        out_specs=(hbm,) * 4 + (vm, hbm, hbm, vm, hbm, hbm),
        scratch_shapes=[pltpu.VMEM(x.shape, F32) for x in (*rows, summed)]
        + [pltpu.SemaphoreType.DMA((5,)), pltpu.SemaphoreType.DMA((7 + wide,))],
        compiler_params=pltpu.CompilerParams(vmem_limit_bytes=62 * 1024 * 1024),
    )(*rows, summed, gains)
def fused_shards(
    unused_grid,
    tokens,
    latents,
    slot_group,
    image_groups,
    gain_attn,
    w_qkv,
    w_out,
    gain_mlp,
    w_up,
    w_down,
    d_tokens,
    d_latents,
):
    micro, tok, width = tokens.shape
    lat = latents.shape[1]
    out_tok, out_lat, grad_tok, grad_lat, unused_grads, summed, gains = both_layers(
        slot_group.shape[1],
        tokens.reshape(micro * tok, width),
        latents.reshape(micro * lat, width),
        slot_group,
        image_groups,
        (gain_attn, gain_mlp),
        (w_qkv[0], w_out[0], w_up[0], w_down[0]),
        d_tokens.reshape(micro * tok, width),
        d_latents.reshape(micro * lat, width),
    )
    wide = w_up.shape[2] // width
    rows = (out_tok, out_lat, grad_tok, grad_lat)
    *rows, first_gain, qkv, out, second_gain, up, down = finished(rows, summed, gains, wide)
    return (
        rows[0].reshape(1, micro, tok, width),
        rows[1].reshape(1, micro, lat, width),
        rows[2].reshape(1, micro, tok, width),
        rows[3].reshape(1, micro, lat, width),
        first_gain,
        qkv.reshape(-1, width).T[None],
        out.reshape(-1, width).T[None],
        second_gain,
        up.reshape(-1, width).T[None],
        down.T[None],
    )

def solution(mesh):
    in_specs = (
        P(None, "dp", None),
        P(None, "dp", None),
        P(),
        P(),
        P("section", None),
        P("section", None, None),
        P("section", None, None),
        P("section", None),
        P("section", None, None),
        P("section", None, None),
        P(None, "dp", None),
        P(None, "dp", None),
    )
    out_specs = (
        P("section", None, "dp", None),
        P("section", None, "dp", None),
        P("section", None, "dp", None),
        P("section", None, "dp", None),
        P("section", "dp"),
        P("section", None, "dp"),
        P("section", None, "dp"),
        P("section", "dp"),
        P("section", None, "dp"),
        P("section", None, "dp"),
    )
    grid = grid_of(mesh)

    def program(*args):
        n, width = mesh.shape["dp"], args[0].shape[2]
        one_group = args[0].shape[1] == n * GROUP
        body = fused_shards if one_group and n == 16 and width % (16 * n) == 0 else shards
        return jax.shard_map(
            functools.partial(body, grid), mesh=mesh, in_specs=in_specs, out_specs=out_specs, check_vma=False
        )(*args)

    return program
```

```python
import functools

import jax
import jax.numpy as jnp
from jax import lax
from jax.experimental import pallas as pl
from jax.experimental.pallas import tpu as pltpu
from jax.sharding import PartitionSpec as P

HEADS = 12
GROUP = 256
LAT = 8


epsilon = 1e-05
masked_score = -1e30


MESH = pl.DeviceIdType.MESH


def grid_of(mesh):
    n = mesh.shape["dp"]
    coords = [getattr(d, "coords", None) for d in mesh.devices.reshape(n, -1)[:, 0]]
    if any(c is None for c in coords):
        return (n // 4, 2, 2) if n % 4 == 0 else (n, 1, 1)
    sizes = {a: len({c[a] for c in coords}) for a in range(3)}
    strides = {
        a: min([i for i in range(n) if coords[i][a] != coords[0][a]], default=n) for a in range(3)
    }
    order = sorted(range(3), key=lambda a: -strides[a])
    return tuple(sizes[a] for a in order)


def spread_kernel(grid, pairs, g_ref, gain_ref, out_ref, gout_ref, *scratch):
    acc = scratch[0:3]
    land = [scratch[3 + 3 * i : 6 + 3 * i] for i in range(3)]
    send_sem, recv_sem, own_sem = scratch[12:15]
    me = lax.axis_index("dp")
    section = lax.axis_index("section")
    l0, l1, l2 = grid
    here = (me // (l1 * l2), lax.rem(me // l2, l1), lax.rem(me, l2))

    def device(axis, shift):
        there = list(here)
        there[axis] = lax.rem(here[axis] + shift, grid[axis])
        return there[axis], ((there[0] * l1 + there[1]) * l2 + there[2], section)

    barrier = pltpu.get_barrier_semaphore()
    for axis in range(3):
        for shift in range(1, grid[axis]):
            pl.semaphore_signal(
                barrier, inc=1, device_id=device(axis, shift)[1], device_id_type=MESH
            )
    pl.semaphore_wait(barrier, sum(grid) - 3)

    orders = ((2, 1, 0), (1, 2, 0), (2, 1, 0))

    def source(stream, phase, k, at):
        if phase == 0:
            if stream == 0:
                return g_ref.at[2 * k, :, :, at]
            if stream == 1:
                return g_ref.at[2 * k + 1, :, at]
            return gain_ref.at[:, :, at]
        if phase == 1:
            return acc[stream].at[k, :, at]
        return acc[stream].at[k, at, here[orders[stream][1]]]

    def copies(stream, phase, k):
        axis = orders[stream][phase]
        for shift in range(1, grid[axis]):
            at, target = device(axis, shift)
            yield pltpu.make_async_remote_copy(
                src_ref=source(stream, phase, k, at),
                dst_ref=land[phase][stream].at[k, shift - 1],
                send_sem=send_sem.at[stream, phase, k, shift - 1],
                recv_sem=recv_sem.at[stream, phase, k, shift - 1],
                device_id=target,
                device_id_type=MESH,
            )

    def own(stream, k):
        return pltpu.make_async_copy(
            source(stream, 0, k, here[orders[stream][0]]), acc[stream].at[k], own_sem.at[stream, k]
        )

    def launch(stream, phase, k):
        for copy in copies(stream, phase, k):
            copy.start()

    def absorb(stream, phase, k):
        axis = orders[stream][phase]
        if phase == 0:
            own(stream, k).wait()
        for copy in copies(stream, phase, k):
            copy.wait_recv()
        into = land[phase][stream]
        count = grid[axis] - 1
        if phase == 0:
            for a in range(acc[stream].shape[1]):
                for b in range(acc[stream].shape[2]):
                    total = acc[stream][k, a, b].astype(jnp.float32)
                    for s in range(count):
                        total += into[k, s, a, b].astype(jnp.float32)
                    acc[stream][k, a, b] = total.astype(acc[stream].dtype)
        elif phase == 1:
            mine = here[axis]
            for a in range(acc[stream].shape[1]):
                total = acc[stream][k, a, mine].astype(jnp.float32)
                for s in range(count):
                    total += into[k, s, a].astype(jnp.float32)
                acc[stream][k, a, mine] = total.astype(acc[stream].dtype)
        else:
            total = acc[stream][k, here[0], here[orders[stream][1]]].astype(jnp.float32)
            for s in range(count):
                total += into[k, s].astype(jnp.float32)
            if stream < 2:
                out_ref[2 * k + stream] = total
            else:
                gout_ref[...] = total

    own(2, 0).start()
    launch(2, 0, 0)

    def start_own(k, carry):
        for stream in (0, 1):
            own(stream, k).start()
        return carry

    for stream in (0, 1):
        launch(stream, 0, 0)
    lax.fori_loop(0, pairs, start_own, 0)

    def turn(t, carry):
        @pl.when(t + 1 < pairs)
        def _():
            for stream in (0, 1):
                launch(stream, 0, t + 1)

        @pl.when(t < pairs)
        def _():
            for stream in (0, 1):
                absorb(stream, 0, t)
                launch(stream, 1, t)

        @pl.when((t >= 1) & (t - 1 < pairs))
        def _():
            for stream in (0, 1):
                absorb(stream, 1, t - 1)
                launch(stream, 2, t - 1)

        @pl.when(t >= 2)
        def _():
            for stream in (0, 1):
                absorb(stream, 2, t - 2)

        return carry

    lax.fori_loop(0, pairs + 2, turn, 0)
    absorb(2, 0, 0)
    launch(2, 1, 0)
    absorb(2, 1, 0)
    launch(2, 2, 0)
    absorb(2, 2, 0)

    def finish(k, carry):
        for stream in (0, 1):
            for phase in range(3):
                for copy in copies(stream, phase, k):
                    copy.wait_send()
        return carry

    lax.fori_loop(0, pairs, finish, 0)
    for phase in range(3):
        for copy in copies(2, phase, 0):
            copy.wait_send()


def spread(grid, grads, gains):
    chunks, n, rows, width = grads.shape
    pairs = chunks // 2
    l0, l1, l2 = grid
    most = max(max(grid) - 1, 1)
    low = jnp.bfloat16
    shapes = ((pairs, rows, width, low), (pairs, rows, width, low), (1, 8, 128, jnp.float32))
    inner = ((l1, l2), (l2, l1), (l1, l2))
    acc, first, second, third = [], [], [], []
    for (count, r, w, dt), (kept, sent) in zip(shapes, inner):
        acc.append(pltpu.VMEM((count, l0, kept, r, w), dt))
        first.append(pltpu.VMEM((count, max(sent - 1, 1), l0, kept, r, w), dt))
        second.append(pltpu.VMEM((count, max(kept - 1, 1), l0, r, w), dt))
        third.append(pltpu.VMEM((count, max(l0 - 1, 1), r, w), dt))
    return pl.pallas_call(
        functools.partial(spread_kernel, grid, pairs),
        out_shape=(
            jax.ShapeDtypeStruct((chunks, rows, width), jnp.float32),
            jax.ShapeDtypeStruct((8, 128), jnp.float32),
        ),
        in_specs=[pl.BlockSpec(memory_space=pl.ANY)] * 2,
        out_specs=(pl.BlockSpec(memory_space=pltpu.VMEM),) * 2,
        scratch_shapes=acc
        + first
        + second
        + third
        + [
            pltpu.SemaphoreType.DMA((3, 3, pairs, most)),
            pltpu.SemaphoreType.DMA((3, 3, pairs, most)),
            pltpu.SemaphoreType.DMA((3, pairs)),
        ],
        compiler_params=pltpu.CompilerParams(
            collective_id=0, has_side_effects=True, vmem_limit_bytes=60 * 1024 * 1024
        ),
        cost_estimate=pl.CostEstimate(flops=0, bytes_accessed=grads.size * 4, transcendentals=0),
    )(grads.reshape(chunks, l0, l1, l2, rows, width), gains.reshape(l0, l1, l2, 8, 128))


def from_behind(x, axis, by):
    devices = lax.axis_size(axis)
    pairs = [(i, i + by) for i in range(devices) if 0 <= i + by < devices]
    return lax.ppermute(x, axis, pairs)


def layer_norm(values, gain):
    row_mean = jnp.mean(values, axis=-1, keepdims=True)
    centred = values - row_mean
    row_var = jnp.mean(centred * centred, axis=-1, keepdims=True)
    return centred * lax.rsqrt(row_var + epsilon) * gain


def front_half(all_rows, gain_attn, w_qkv):
    normed = layer_norm(all_rows, gain_attn).astype(jnp.bfloat16)
    projected = jnp.dot(normed, w_qkv, preferred_element_type=jnp.float32).astype(jnp.bfloat16)
    return (normed, projected)


def latent_operand(projected, tok_rows, model_width):
    return projected[tok_rows:, model_width:]


def back_half(all_rows, projected, remote_rows, allowed, weights):
    gain_attn, w_qkv, w_out, gain_mlp, w_up, w_down = weights
    row_count, model_width = all_rows.shape
    head_size = model_width // HEADS
    remote_pairs = remote_rows[:, remote_rows.shape[1] - 2 * model_width :]
    queries = projected[:, :model_width].reshape(row_count, HEADS, head_size)
    key_rows = jnp.concatenate(
        [projected[:, model_width : 2 * model_width], remote_pairs[:, :model_width]], axis=0
    )
    value_rows = jnp.concatenate(
        [projected[:, 2 * model_width :], remote_pairs[:, model_width:]], axis=0
    )
    key_rows = key_rows.reshape(-1, HEADS, head_size)
    value_rows = value_rows.reshape(-1, HEADS, head_size)
    scores = jnp.einsum(
        "qhd,khd->hqk", queries, key_rows, preferred_element_type=jnp.float32
    ) * head_size ** (-0.5)
    attn_weights = jax.nn.softmax(jnp.where(allowed[None], scores, masked_score), axis=-1)
    attn_low = attn_weights.astype(jnp.bfloat16)
    mixed_low = jnp.einsum("hqk,khd->qhd", attn_low, value_rows, preferred_element_type=jnp.float32)
    mixed_low = mixed_low.reshape(row_count, model_width).astype(jnp.bfloat16)
    mid_rows = all_rows + jnp.dot(mixed_low, w_out, preferred_element_type=jnp.float32)
    normed_mlp = layer_norm(mid_rows, gain_mlp).astype(jnp.bfloat16)
    up_proj = jnp.dot(normed_mlp, w_up, preferred_element_type=jnp.float32)
    activated = jax.nn.gelu(up_proj).astype(jnp.bfloat16)
    result = mid_rows + jnp.dot(activated, w_down, preferred_element_type=jnp.float32)
    return dict(
        queries=queries,
        key_rows=key_rows,
        value_rows=value_rows,
        attn_weights=attn_weights,
        attn_low=attn_low,
        mixed_low=mixed_low,
        mid_rows=mid_rows,
        normed_mlp=normed_mlp,
        up_proj=up_proj,
        activated=activated,
        result=result,
    )


def section_backward(saved, d_result, all_rows, normed, allowed, weights, latent_start):
    gain_attn, w_qkv, w_out, gain_mlp, w_up, w_down = weights
    row_count, model_width = all_rows.shape
    head_size = model_width // HEADS
    score_scale = head_size ** (-0.5)
    d_low = d_result.astype(jnp.bfloat16)
    grad_down = jnp.dot(d_low.T, saved["activated"], preferred_element_type=jnp.float32)
    d_activated = jnp.dot(d_low, w_down.T, preferred_element_type=jnp.float32)
    unused_up, gelu_back = jax.vjp(jax.nn.gelu, saved["up_proj"])
    d_up = gelu_back(d_activated)[0].astype(jnp.bfloat16)
    grad_up = jnp.dot(d_up.T, saved["normed_mlp"], preferred_element_type=jnp.float32)
    d_normed_mlp = jnp.dot(d_up, w_up.T, preferred_element_type=jnp.float32)
    unused_mid, second_back = jax.vjp(layer_norm, saved["mid_rows"], gain_mlp)
    d_mid_norm, grad_gain_mlp = second_back(d_normed_mlp)
    d_mid = d_result + d_mid_norm
    d_mid_low = d_mid.astype(jnp.bfloat16)
    grad_out = jnp.dot(d_mid_low.T, saved["mixed_low"], preferred_element_type=jnp.float32)
    d_mixed = jnp.dot(d_mid_low, w_out.T, preferred_element_type=jnp.float32).astype(jnp.bfloat16)
    d_mixed = d_mixed.reshape(row_count, HEADS, head_size)
    d_weights = jnp.einsum(
        "qhd,khd->hqk", d_mixed, saved["value_rows"], preferred_element_type=jnp.float32
    )
    d_values = jnp.einsum(
        "hqk,qhd->khd", saved["attn_low"], d_mixed, preferred_element_type=jnp.float32
    )
    attn_weights = saved["attn_weights"]
    d_scores = attn_weights * (
        d_weights - jnp.sum(attn_weights * d_weights, axis=-1, keepdims=True)
    )
    d_scores_low = jnp.where(allowed[None], d_scores, 0.0).astype(jnp.bfloat16)
    d_queries = (
        jnp.einsum(
            "hqk,khd->qhd", d_scores_low, saved["key_rows"], preferred_element_type=jnp.float32
        )
        * score_scale
    )
    d_keys = (
        jnp.einsum(
            "hqk,qhd->khd", d_scores_low, saved["queries"], preferred_element_type=jnp.float32
        )
        * score_scale
    )
    remote_part = jnp.concatenate(
        [
            d_keys[row_count:].reshape(-1, model_width),
            d_values[row_count:].reshape(-1, model_width),
        ],
        axis=1,
    )
    own_part = lax.psum_scatter(remote_part, "dp", scatter_dimension=0, tiled=True)
    local_pairs = jnp.concatenate(
        [
            d_keys[:row_count].reshape(row_count, model_width),
            d_values[:row_count].reshape(row_count, model_width),
        ],
        axis=1,
    )
    local_pairs = jnp.concatenate(
        [local_pairs[:latent_start], local_pairs[latent_start:] + own_part], axis=0
    )
    d_projected = jnp.concatenate(
        [d_queries.reshape(row_count, model_width), local_pairs], axis=1
    ).astype(jnp.bfloat16)
    grad_qkv = jnp.dot(d_projected.T, normed, preferred_element_type=jnp.float32)
    d_normed = jnp.dot(d_projected, w_qkv.T, preferred_element_type=jnp.float32)
    unused_rows, first_back = jax.vjp(layer_norm, all_rows, gain_attn)
    d_rows_norm, grad_gain_attn = first_back(d_normed)
    return (
        d_mid + d_rows_norm,
        (grad_gain_attn, grad_qkv, grad_out, grad_gain_mlp, grad_up, grad_down),
    )


def packed(grads, n):
    gain_first, qkv_grad, out_grad, gain_second, up_grad, down_grad = grads
    width = out_grad.shape[0]
    rows = width // n

    def by_rows(grad):
        return grad.reshape(n, -1, rows, width).transpose(1, 0, 2, 3).astype(jnp.bfloat16)

    down = down_grad.reshape(n, rows, -1, width).transpose(2, 0, 1, 3).astype(jnp.bfloat16)
    chunks = jnp.concatenate([down, by_rows(up_grad), by_rows(out_grad), by_rows(qkv_grad)], axis=0)
    gains = jnp.stack([gain_first.reshape(n, rows), gain_second.reshape(n, rows)], axis=1)
    return chunks, jnp.pad(gains, ((0, 0), (0, 6), (0, 128 - rows)))


def shards(
    grid,
    tokens,
    latents,
    slot_group,
    image_groups,
    gain_attn,
    w_qkv,
    w_out,
    gain_mlp,
    w_up,
    w_down,
    d_tokens,
    d_latents,
):
    micro = tokens.shape[0]
    tok_rows = tokens.shape[1]
    lat_rows = latents.shape[1]
    model_width = tokens.shape[2]
    local_groups = tok_rows // GROUP
    section_index = lax.axis_index("section")
    is_global = section_index == 1
    dp_index = lax.axis_index("dp")
    weights = (gain_attn[0], w_qkv[0], w_out[0], gain_mlp[0], w_up[0], w_down[0])
    image_ends = jnp.cumsum(image_groups, axis=1)
    slot_images = jnp.sum(
        (image_ends[:, None, :] <= slot_group[:, :, None]).astype(jnp.int32), axis=2
    )
    slot_total = slot_group.shape[1]
    row_group = jnp.concatenate([jnp.arange(tok_rows) // GROUP, jnp.arange(lat_rows) // LAT])
    row_latent = jnp.concatenate(
        [jnp.zeros((tok_rows,), jnp.bool_), jnp.ones((lat_rows,), jnp.bool_)]
    )
    same_group = row_group[:, None] == row_group[None, :]
    local_mask = jnp.where(
        is_global, (~row_latent)[:, None] & row_latent[None, :] & same_group, same_group
    )
    group_match = row_group[:, None] == jnp.arange(local_groups)[None, :]

    def key_images(batch):
        images_row = lax.dynamic_index_in_dim(slot_images, batch, 0, keepdims=False)
        return (images_row, jnp.broadcast_to(images_row[:, None], (slot_total, LAT)).reshape(-1))

    def allowed_for(batch):
        images_row, key_image = key_images(batch)
        own_images = lax.dynamic_slice_in_dim(images_row, dp_index * local_groups, local_groups)
        row_image = jnp.sum(jnp.where(group_match, own_images[None, :], 0), axis=1)
        remote_mask = is_global & row_latent[:, None] & (row_image[:, None] == key_image[None, :])
        return jnp.concatenate([local_mask, remote_mask], axis=1)

    def forward_turn(received, turn):
        recv_tokens, recv_latents = received
        batch = jnp.clip(turn - section_index, 0, micro - 1)
        own_tok = lax.dynamic_index_in_dim(tokens, batch, 0, keepdims=False)
        own_lat = lax.dynamic_index_in_dim(latents, batch, 0, keepdims=False)
        input_rows = jnp.concatenate(
            [
                jnp.where(is_global, recv_tokens, own_tok),
                jnp.where(is_global, recv_latents, own_lat),
            ],
            axis=0,
        )
        all_rows = input_rows.astype(jnp.float32)
        normed, projected = front_half(all_rows, weights[0], weights[1])
        remote_rows = lax.all_gather(
            latent_operand(projected, tok_rows, model_width), "dp", axis=0, tiled=True
        )
        saved = back_half(all_rows, projected, remote_rows, allowed_for(batch), weights)
        result = saved["result"]
        result_low = result.astype(jnp.bfloat16)
        stored = jnp.where(is_global, result, result_low.astype(jnp.float32))
        passed_on = from_behind((result_low[:tok_rows], result_low[tok_rows:]), "section", 1)
        return passed_on, (input_rows, stored[:tok_rows], stored[tok_rows:])

    nothing = (
        jnp.zeros((tok_rows, model_width), jnp.bfloat16),
        jnp.zeros((lat_rows, model_width), jnp.bfloat16),
    )
    turns = jnp.arange(micro + 1)
    unused_end, (kept_rows, tok_outputs, lat_outputs) = lax.scan(forward_turn, nothing, turns)

    def backward_turn(carry, turn):
        (recv_grad_tok, recv_grad_lat), totals = carry
        raw_batch = micro - turn - section_index
        valid = ((raw_batch >= 0) & (raw_batch < micro)).astype(jnp.float32)
        batch = jnp.clip(raw_batch, 0, micro - 1)
        all_rows = lax.dynamic_index_in_dim(
            kept_rows, batch + section_index, 0, keepdims=False
        ).astype(jnp.float32)
        normed, projected = front_half(all_rows, weights[0], weights[1])
        remote_rows = lax.all_gather(
            latent_operand(projected, tok_rows, model_width), "dp", axis=0, tiled=True
        )
        allowed = allowed_for(batch)
        saved = back_half(all_rows, projected, remote_rows, allowed, weights)
        given = (
            jnp.concatenate(
                [
                    lax.dynamic_index_in_dim(d_tokens, batch, 0, keepdims=False),
                    lax.dynamic_index_in_dim(d_latents, batch, 0, keepdims=False),
                ],
                axis=0,
            )
            * valid
        )
        passed = jnp.concatenate([recv_grad_tok, recv_grad_lat], axis=0).astype(jnp.float32)
        d_result = jnp.where(is_global, given, passed)
        d_rows, grads = section_backward(
            saved, d_result, all_rows, normed, allowed, weights, tok_rows
        )
        totals = tuple((accum + piece for accum, piece in zip(totals, grads)))
        d_rows_low = d_rows.astype(jnp.bfloat16)
        stored = jnp.where(is_global, d_rows_low.astype(jnp.float32), d_rows)
        sent = from_behind((d_rows_low[:tok_rows], d_rows_low[tok_rows:]), "section", -1)
        return (sent, totals), (stored[:tok_rows], stored[tok_rows:])

    totals = tuple(
        jnp.zeros(w.shape[::-1] if w.ndim == 2 else w.shape, jnp.float32) for w in weights
    )
    (unused_sent, totals), (tok_grads, lat_grads) = lax.scan(
        backward_turn, (nothing, totals), turns
    )
    chunks, gains = packed(totals, lax.axis_size("dp"))
    summed, gain_sums = spread(grid, chunks, gains)
    rows = summed.shape[1]
    layer_tokens = lax.dynamic_slice_in_dim(tok_outputs, section_index, micro, 0)[None]
    layer_latents = lax.dynamic_slice_in_dim(lat_outputs, section_index, micro, 0)[None]
    grad_tokens = lax.dynamic_slice_in_dim(tok_grads, 1 - section_index, micro, 0)[::-1][
        None
    ]
    grad_latents = lax.dynamic_slice_in_dim(lat_grads, 1 - section_index, micro, 0)[
        ::-1
    ][None]
    return (
        layer_tokens,
        layer_latents,
        grad_tokens,
        grad_latents,
        gain_sums[0:1, :rows],
        summed[9:].reshape(-1, model_width).T[None],
        summed[8].T[None],
        gain_sums[1:2, :rows],
        summed[4:8].reshape(-1, model_width).T[None],
        summed[0:4].transpose(0, 2, 1).reshape(-1, rows)[None],
    )


F32 = jnp.float32
LOW = jnp.bfloat16
HEAD_PAD = 16
TILE = 768


def nn(a, b):
    return jnp.dot(a, b, preferred_element_type=F32)


def nt(a, b):
    return lax.dot_general(a, b, (((1,), (1,)), ((), ())), preferred_element_type=F32)


def tn(a, b):
    return lax.dot_general(a, b, (((0,), (0,)), ((), ())), preferred_element_type=F32)


def row_mean(values):
    return jnp.mean(values, axis=-1, keepdims=True)


def row_stats(load, spans):
    means = [row_mean(load(r)) for r in spans]
    scales = []
    for r, mean in zip(spans, means):
        centred = load(r) - mean
        scales.append(lax.rsqrt(row_mean(centred * centred) + epsilon))
    return means, scales


def at(start, size):
    return pl.ds(pl.multiple_of(start, size), size)


def class_max(s):
    for by in (16, 32, 64):
        s = jnp.maximum(s, pltpu.roll(s, by, 1))
    return s


def class_sum(s):
    for by in (16, 32, 64):
        s = s + pltpu.roll(s, by, 1)
    return s


def layer_kernel(
    n,
    tokens,
    latents,
    slots,
    slot_at,
    image_at,
    gain_attn,
    gain_mlp,
    w_qkv,
    w_out,
    w_up,
    w_down,
    d_tokens,
    d_latents,
    out_tok,
    out_lat,
    grad_tok,
    grad_lat,
    grads,
    summed,
    gain_sums,
    wq,
    wo,
    wu,
    wd,
    xb,
    n1,
    proj,
    mixed,
    mid,
    n2,
    act,
    dup,
    yb,
    dy,
    ef,
    tmp,
    out,
    probs,
    probs_lat,
    scores,
    slopes,
    latf,
    mixf,
    key_mask,
    qbd,
    kbd,
    vbd,
    kv_all,
    kvg_send,
    kvg_recv,
    stage,
    gains,
    leaving,
    own_a,
    own_b,
    land1_a,
    land1_b,
    land2_a,
    land2_b,
    land3_a,
    land3_b,
    land4_a,
    land4_b,
    land_g,
    load_sem,
    stage_sem,
    own_sem,
    leave_sem,
    send_sem,
    recv_sem,
    gain_s,
    gain_r,
    relay_send,
    relay_recv,
    kv_sem_s,
    kv_sem_r,
    kvg_sem_s,
    kvg_sem_r,
):
    rows, width = xb.shape
    ff = act.shape[1]
    tok = tokens.shape[0]
    lat = latents.shape[0]
    half = lat // LAT
    pairs = width // 128
    me = lax.axis_index("dp")
    section = lax.axis_index("section")
    first = section == 0
    second = section == 1
    partner = (me, 1 - section)

    loads = [
        pltpu.make_async_copy(src, dst, load_sem.at[i])
        for i, (src, dst) in enumerate(((w_qkv, wq), (w_out, wo), (w_up, wu), (w_down, wd)))
    ]
    x_loads = [
        pltpu.make_async_copy(tokens, xb.at[lat:rows], load_sem.at[4]),
        pltpu.make_async_copy(latents, xb.at[0:lat], load_sem.at[5]),
    ]
    e_loads = [
        pltpu.make_async_copy(d_tokens, ef.at[lat:rows], load_sem.at[6]),
        pltpu.make_async_copy(d_latents, ef.at[0:lat], load_sem.at[7]),
    ]

    @pl.when(first)
    def _():
        for copy in x_loads:
            copy.start()

    for copy in loads:
        copy.start()

    @pl.when(second)
    def _():
        for copy in e_loads:
            copy.start()

    barrier = pltpu.get_barrier_semaphore()
    pl.semaphore_signal(barrier, inc=1, device_id=partner, device_id_type=MESH)

    here = [lax.rem(me // (1 << bit), 2) for bit in range(4)]

    def across(bit):
        return (me + (1 - 2 * here[bit]) * (1 << bit), section)

    @pl.when(second)
    def _():
        for shift in range(1, n):
            pl.semaphore_signal(
                barrier, inc=1, device_id=(lax.rem(me + shift, n), section), device_id_type=MESH
            )
        pl.semaphore_wait(barrier, n)

    @pl.when(first)
    def _():
        for bit in range(4):
            pl.semaphore_signal(barrier, inc=1, device_id=across(bit), device_id_type=MESH)
        pl.semaphore_wait(barrier, 5)

    def relay(back, band):
        low, high = ((0, rows // 3), (rows // 3, 2 * rows // 3), (2 * rows // 3, rows))[band]
        if not back:
            low, high = ((0, lat), (lat, lat + GROUP), (lat + GROUP, rows))[band]
        return pltpu.make_async_remote_copy(
            src_ref=yb.at[low:high],
            dst_ref=(dy if back else xb).at[low:high],
            send_sem=relay_send.at[3 * back + band],
            recv_sem=relay_recv.at[3 * back + band],
            device_id=partner,
            device_id_type=MESH,
        )

    def kv_copy(shift, incoming):
        slot = lax.rem(me + n - shift, n) if incoming else me
        return pltpu.make_async_remote_copy(
            src_ref=kv_all.at[me], dst_ref=kv_all.at[slot],
            send_sem=kv_sem_s.at[shift - 1], recv_sem=kv_sem_r.at[shift - 1],
            device_id=(lax.rem(me + shift, n), section), device_id_type=MESH,
        )

    def kvg_copy(shift):
        there = lax.rem(me + shift, n)
        return pltpu.make_async_remote_copy(
            src_ref=kvg_send.at[there], dst_ref=kvg_recv.at[shift - 1],
            send_sem=kvg_sem_s.at[shift - 1], recv_sem=kvg_sem_r.at[shift - 1],
            device_id=(there, section), device_id_type=MESH,
        )

    chunks = [slice(c, c + 64) for c in range(0, GROUP, 64)]
    lane = lax.broadcasted_iota(jnp.int32, (1, 128), 1)
    halves = [(lane < 64).astype(F32).astype(LOW), (lane >= 64).astype(F32).astype(LOW)]
    eighths = [(h.astype(F32) * 0.125).astype(LOW) for h in halves]
    heads = (
        lax.broadcasted_iota(jnp.int32, (HEAD_PAD, width), 1) // 64
        == lax.broadcasted_iota(jnp.int32, (HEAD_PAD, width), 0)
    ).astype(F32)

    def block_diagonal(dst, base, src, row, column, scale):
        for i in range(LAT):
            line = src[row + i : row + i + 1, column : column + width] * scale
            dst[base + i * HEAD_PAD : base + (i + 1) * HEAD_PAD, :] = (line * heads).astype(LOW)

    def head_sum(dst, row, column, value, scale, add):
        for i in range(LAT):
            line = jnp.sum(
                value[i * HEAD_PAD : (i + 1) * HEAD_PAD] * heads, axis=0, keepdims=True
            )
            line = line * scale
            if add:
                line = line + dst[row + i : row + i + 1, column : column + width]
            dst[row + i : row + i + 1, column : column + width] = line

    def bands(body, lo, hi, size):
        def one(i, carry):
            body(pl.ds(pl.multiple_of(lo + i * size, 16), size))
            return carry

        lax.fori_loop(0, (hi - lo) // size, one, 0)

    third = rows // 3

    def grouped(body, lo, hi, count):
        def one(i, carry):
            base = lo + i * 16 * count
            body([pl.ds(pl.multiple_of(base + 16 * g, 16), 16) for g in range(count)])
            return carry

        lax.fori_loop(0, (hi - lo) // (16 * count), one, 0)

    def norm(load, gain, dst, lo, hi, count):
        def body(spans):
            means, scales = row_stats(load, spans)
            for r, mean, scale in zip(spans, means, scales):
                dst[r, :] = ((load(r) - mean) * scale * gain[...]).astype(LOW)

        grouped(body, lo, hi, count)

    def norm_back(load, grad, gain, gain_rows, store, lo, hi, count):
        def body(spans):
            means, scales = row_stats(load, spans)
            firsts, seconds = [], []
            kept = gains[0, gain_rows, :]
            for r, mean, scale in zip(spans, means, scales):
                along = grad[r, :] * ((load(r) - mean) * scale)
                kept = kept + along[0:8] + along[8:16]
                firsts.append(row_mean(grad[r, :] * gain[...]))
                seconds.append(row_mean(along * gain[...]))
            gains[0, gain_rows, :] = kept
            for r, mean, scale, one, two in zip(spans, means, scales, firsts, seconds):
                hat = (load(r) - mean) * scale
                store(r, ef[r, :] + scale * (grad[r, :] * gain[...] - one - hat * two))

        grouped(body, lo, hi, count)

    def tiles(count, body, size=TILE):
        def one(i, carry):
            body(at(i * size, size))
            return carry

        lax.fori_loop(0, count, one, 0)

    @pl.when(first)
    def _():
        for copy in x_loads:
            copy.wait()

    @pl.when(second)
    def _():
        spots = lax.broadcasted_iota(jnp.int32, (n, n * lat), 1) // lat
        spread_out = (spots == lax.broadcasted_iota(jnp.int32, (n, n * lat), 0)).astype(F32)
        groups = nn(slots[...].astype(F32).astype(LOW), spread_out.astype(LOW))
        of_micro = lax.rem(lax.broadcasted_iota(jnp.int32, (1, n * lat), 1), lat) // LAT
        for m in range(half):
            images = jnp.zeros((1, n * lat), F32)
            own_image = jnp.float32(0)
            end = jnp.int32(0)
            for i in range(image_at.shape[1]):
                end = end + image_at[m, i]
                images += jnp.where(end.astype(F32) <= groups[m : m + 1], 1.0, 0.0)
                own_image += jnp.where(end <= slot_at[m, me], 1.0, 0.0)
            seen = (images == own_image) & (of_micro == m)
            key_mask[m : m + 1, :] = jnp.where(seen, 0.0, masked_score)

    def load_in(r):
        return xb[r, :].astype(F32)

    def load_mid(r):
        return mid[r, :]

    def lat_bias(m, shape, axis):
        return jnp.where(
            lax.broadcasted_iota(jnp.int32, shape, axis) // LAT == m, 0.0, masked_score
        ).astype(F32)

    @pl.when(first)
    def _():
        norm(load_in, gain_attn, n1, 0, rows, 11)
        loads[0].wait()

        def project(c):
            proj[:, c] = nn(n1[...], wq[:, c]).astype(LOW)

        tiles(3 * width // TILE, project)
        latf[...] = proj[0:lat, :].astype(F32)

        def one_pair(it, side):
            m, p = it // pairs, lax.rem(it, pairs)
            r = pl.ds(pl.multiple_of(lat + m * GROUP, 16), GROUP)
            q = proj[r, at(p * 128, 128)]
            k = proj[r, at(width + p * 128, 128)]
            v = proj[r, at(2 * width + p * 128, 128)]
            kl = proj[0:lat, at(width + p * 128, 128)]
            vl = proj[0:lat, at(2 * width + p * 128, 128)]
            bias = lat_bias(m, (lat, GROUP), 0)
            total = jnp.zeros((GROUP, 128), F32)
            for e in (0, 1):
                qe = q * eighths[e]
                s = scores.at[2 * side + e]
                s[...] = nt(k, qe)
                sl = nt(kl, qe) + bias
                top = jnp.max(sl, axis=0, keepdims=True)
                for c in chunks:
                    top = jnp.maximum(top, jnp.max(s[c, :], axis=0, keepdims=True))
                el = jnp.exp(sl - top)
                whole_sum = jnp.sum(el, axis=0, keepdims=True)
                for c in chunks:
                    et = jnp.exp(s[c, :] - top)
                    s[c, :] = et
                    whole_sum += jnp.sum(et, axis=0, keepdims=True)
                scale = 1.0 / whole_sum
                for c in chunks:
                    probs[2 * it + e, c, :] = (s[c, :] * scale).astype(LOW)
                pe = (el * scale).astype(LOW)
                probs[2 * it + e, GROUP : GROUP + lat, :] = pe
                total += tn(probs[2 * it + e, 0:GROUP, :], v * halves[e])
                total += tn(pe, vl * halves[e])
            mixed[r, at(p * 128, 128)] = total.astype(LOW)

        def pair(i, carry):
            one_pair(2 * i, 0)
            one_pair(2 * i + 1, 1)
            return carry

        lax.fori_loop(0, half * pairs // 2, pair, 0)
        for m in range(half):
            r = slice(lat + m * GROUP, lat + (m + 1) * GROUP)
            b = slice(m * 128, (m + 1) * 128)
            block_diagonal(qbd, m * 128, latf, m * LAT, 0, 0.125)
            s = nt(qbd[b, :], proj[r, width : 2 * width])
            sl = nt(qbd[b, :], proj[0:lat, width : 2 * width]) + lat_bias(m, (128, lat), 1)
            top = jnp.maximum(
                jnp.max(s, axis=1, keepdims=True), jnp.max(sl, axis=1, keepdims=True)
            )
            et = jnp.exp(s - top)
            el = jnp.exp(sl - top)
            scale = 1.0 / (
                jnp.sum(et, axis=1, keepdims=True) + jnp.sum(el, axis=1, keepdims=True)
            )
            pt = (et * scale).astype(LOW)
            pe = (el * scale).astype(LOW)
            probs_lat[b, 0:GROUP] = pt
            probs_lat[b, GROUP : GROUP + lat] = pe
            o = nn(pt, proj[r, 2 * width :]) + nn(pe, proj[0:lat, 2 * width :])
            head_sum(mixf, m * LAT, 0, o, 1.0, False)
        mixed[0:lat, :] = mixf[...].astype(LOW)

    keys = n * lat

    root = 0.7978845608028654

    def mlp_in(lo, hi, count):
        r0 = slice(lo, hi)
        mid[r0, :] = xb[r0, :].astype(F32) + nn(mixed[r0, :], wo[...])

        norm(load_mid, gain_mlp, n2, lo, hi, count)

        def up_tile(dst, i):
            dst[r0, 0:512] = nn(n2[r0, :], wu[:, at(i * 512, 512)])

        def gelu(src, i):
            c = at(i * 512, 512)
            for g in range(lo, hi, 16):
                r = slice(g, g + 16)
                up = src[r, 0:512]
                square = up * up
                t = jnp.tanh(up * (root + (root * 0.044715) * square))
                gate = 0.5 + 0.5 * t
                value = up * gate
                slope = gate + (value + value) * (1.0 - gate) * (
                    root + (3.0 * root * 0.044715) * square
                )
                act[r, c] = value.astype(LOW)
                dup[r, c] = slope.astype(LOW)

        last = ff // 512 - 1

        def widen(i, carry):
            up_tile(out, 2 * i + 1)
            gelu(tmp, 2 * i)
            up_tile(tmp, jnp.minimum(2 * i + 2, last))
            gelu(out, 2 * i + 1)
            return carry

        up_tile(tmp, 0)
        lax.fori_loop(0, ff // 1024, widen, 0)

    out_copies = [
        pltpu.make_async_copy(out.at[lat:rows], out_tok, load_sem.at[8]),
        pltpu.make_async_copy(out.at[0:lat], out_lat, load_sem.at[9]),
    ]
    grad_copies = [
        pltpu.make_async_copy(out.at[lat:rows], grad_tok, load_sem.at[8]),
        pltpu.make_async_copy(out.at[0:lat], grad_lat, load_sem.at[9]),
    ]

    def layer_output(low, high, passed_on):
        r = slice(low, high)
        y = mid[r, :] + nn(act[r, :], wd[...])
        if passed_on:
            narrow_y = y.astype(LOW)
            yb[r, :] = narrow_y
            y = narrow_y.astype(F32)
        out[r, :] = y

    @pl.when(first)
    def _():
        for copy in loads[1:]:
            copy.wait()
        mlp_in(0, lat + GROUP, 17)
        layer_output(0, lat + GROUP, True)
        relay(0, 0).start()
        relay(0, 1).start()
        mlp_in(lat + GROUP, rows, 16)
        layer_output(lat + GROUP, rows, True)
        relay(0, 2).start()
        for copy in out_copies:
            copy.start()

    @pl.when(second)
    def _():
        for copy in loads:
            copy.wait()
        relay(0, 0).wait_recv()
        norm(load_in, gain_attn, n1, 0, lat, 1)
        lat_proj = nn(n1[0:lat, :], wq[...]).astype(LOW)
        kv_all[me] = lat_proj[:, width:]
        latf[...] = lat_proj.astype(F32)
        for shift in range(1, n):
            kv_copy(shift, False).start()
        for m in range(half):
            relay(0, 1 + m).wait_recv()
            low, high = lat + m * GROUP, lat + (m + 1) * GROUP
            r = slice(low, high)
            b = slice(m * 128, (m + 1) * 128)
            norm(load_in, gain_attn, n1, low, high, 16)
            proj[r, :width] = nn(n1[r, :], wq[:, :width]).astype(LOW)
            block_diagonal(qbd, m * 128, latf, m * LAT, 0, 0.125)
            block_diagonal(kbd, m * 128, latf, m * LAT, width, 1.0)
            block_diagonal(vbd, m * 128, latf, m * LAT, 2 * width, 1.0)
            s = nt(proj[r, :width] * jnp.asarray(0.125, LOW), kbd[b, :])
            et = jnp.exp(s - class_max(s))
            pt = (et / class_sum(et)).astype(LOW)
            probs[m, 0:GROUP, 0:128] = pt
            mixed[r, :] = nn(pt, vbd[b, :]).astype(LOW)
            mlp_in(low, high, 16)
        for shift in range(1, n):
            kv_copy(shift, True).wait_recv()
        k = kv_all[:, :, :width].reshape(keys, width)
        v = kv_all[:, :, width:].reshape(keys, width)
        for m in range(half):
            b = slice(m * 128, (m + 1) * 128)
            s = nt(qbd[b, :], k) + key_mask[m : m + 1, :]
            et = jnp.exp(s - jnp.max(s, axis=1, keepdims=True))
            pt = (et / jnp.sum(et, axis=1, keepdims=True)).astype(LOW)
            probs_lat[b, 0:keys] = pt
            head_sum(mixf, m * LAT, 0, nn(pt, v), 1.0, False)
        mixed[0:lat, :] = mixf[...].astype(LOW)
        mlp_in(0, lat, 1)

    @pl.when(first)
    def _():
        for band in range(3):
            relay(1, band).wait_recv()

        def widen_e(r):
            ef[r, :] = dy[r, :].astype(F32)

        bands(widen_e, 0, rows, third)

    @pl.when(second)
    def _():
        for copy in e_loads:
            copy.wait()

        def narrow_e(r):
            dy[r, :] = ef[r, :].astype(LOW)

        bands(narrow_e, 0, rows, third)

    part = 384
    unit = width // n
    many = part // unit

    def staged(slot, piece, chunk, share):
        return pltpu.make_async_copy(
            stage.at[slot, piece],
            grads.at[
                chunk,
                share // 8,
                lax.rem(share // 4, 2),
                lax.rem(share // 2, 2),
                lax.rem(share, 2),
            ],
            stage_sem.at[slot, piece],
        )

    def drain(slot):
        def one(piece, carry):
            staged(slot, piece, 0, 0).wait()
            return carry

        lax.fori_loop(0, many, one, 0)

    def weight_grad(place, start, count, left, *rights):
        def one(i, carry):
            turned = left(i).T
            for at_right, right in enumerate(rights):
                tile = i * len(rights) + at_right
                slot = lax.rem(tile, 2)
                value = nn(turned, right(i)).astype(LOW)

                @pl.when(tile >= start * len(rights) + 2)
                def _():
                    drain(slot)

                for piece in range(many):
                    stage[slot, piece] = value[piece * unit : (piece + 1) * unit]
                    staged(slot, piece, *place(i, at_right, piece)).start()
            return carry

        lax.fori_loop(start, start + count, one, 0)
        for slot in (0, 1):
            drain(slot)

    orders = ((0, 2, 1, 3), (1, 2, 0, 3))
    own_buf = (own_a, own_b)
    land = (
        (land1_a, land1_b),
        (land2_a, land2_b),
        (land3_a, land3_b),
        (land4_a, land4_b),
    )
    spread_pairs = land1_a.shape[0]

    def source(stream, phase, k, theirs):
        pick = [(1 - here[bit]) if theirs else here[bit] for bit in orders[stream]]
        own_bit = [here[bit] for bit in orders[stream]]
        base = land[0][stream]
        if phase == 0:
            if stream == 0:
                return grads.at[2 * k, :, :, :, pick[0]]
            return grads.at[2 * k + 1, :, :, pick[0]]
        if phase == 1:
            return base.at[k, :, pick[1]]
        if phase == 2:
            return base.at[k, :, own_bit[1], pick[2]]
        return base.at[k, pick[3], own_bit[1], own_bit[2]]

    def copy_of(stream, phase, k):
        return pltpu.make_async_remote_copy(
            src_ref=source(stream, phase, k, True),
            dst_ref=land[phase][stream].at[k],
            send_sem=send_sem.at[stream, phase, k],
            recv_sem=recv_sem.at[stream, phase, k],
            device_id=across(orders[stream][phase]),
            device_id_type=MESH,
        )

    def own(stream, k):
        return pltpu.make_async_copy(
            source(stream, 0, k, False), own_buf[stream], own_sem.at[stream]
        )

    def leave(stream, k):
        slot = lax.rem(k, 2)
        return pltpu.make_async_copy(
            leaving.at[slot, stream], summed.at[2 * k + stream], leave_sem.at[slot, stream]
        )

    def launch(phase, k):
        for stream in (0, 1):
            copy_of(stream, phase, k).start()

    def absorb(phase, k):
        for stream in (0, 1):
            if phase == 0:
                own(stream, k).wait()
            copy_of(stream, phase, k).wait_recv()
            base, into = land[0][stream], land[phase][stream]
            mine = [here[bit] for bit in orders[stream]]
            if phase == 0:

                def add(i, carry):
                    for j in (0, 1):
                        for h in (0, 1):
                            total = own_buf[stream][i, j, h].astype(F32)
                            total += base[k, i, j, h].astype(F32)
                            base[k, i, j, h] = total.astype(LOW)
                    return carry

                lax.fori_loop(0, 2, add, 0)
            elif phase == 1:
                for i in (0, 1):
                    for h in (0, 1):
                        total = base[k, i, mine[1], h].astype(F32)
                        total += into[k, i, h].astype(F32)
                        base[k, i, mine[1], h] = total.astype(LOW)
            elif phase == 2:
                for i in (0, 1):
                    total = base[k, i, mine[1], mine[2]].astype(F32)
                    total += into[k, i].astype(F32)
                    base[k, i, mine[1], mine[2]] = total.astype(LOW)
            else:
                total = base[k, mine[3], mine[1], mine[2]].astype(F32)
                total += into[k].astype(F32)
                slot = lax.rem(k, 2)

                @pl.when(k >= 2)
                def _():
                    leave(stream, k - 2).wait()

                leaving[slot, stream] = total
                leave(stream, k).start()

    def start_own(k):
        for stream in (0, 1):
            own(stream, k).start()

    def relaunch(k, following=True):
        absorb(0, k)
        launch(1, k)
        if following:
            start_own(k + 1)

    def onward(phase, k):
        absorb(phase, k)
        if phase < 3:
            launch(phase + 1, k)

    wide = ff // width
    per_part = width // part

    def up_grad():
        weight_grad(
            lambda i, right, piece: (
                wide + lax.rem(i * many + piece, wide),
                (i * many + piece) // wide,
            ),
            0,
            ff // part,
            lambda i: dup[:, at(i * part, part)],
            lambda i: n2[...],
        )
        launch(0, 2)
        launch(0, 3)

    def down_grad(pair):
        weight_grad(
            lambda i, right, piece: (2 * pair + right, i * many + piece),
            0,
            per_part,
            lambda i: dy[:, at(i * part, part)],
            lambda i: act[:, 2 * pair * width : (2 * pair + 1) * width],
            lambda i: act[:, (2 * pair + 1) * width : (2 * pair + 2) * width],
        )

    down_grad(0)
    launch(0, 0)
    start_own(0)
    down_grad(1)
    launch(0, 1)

    def unwiden(c):
        dup[:, c] = (nt(dy[...], wd[c, :]) * dup[:, c].astype(F32)).astype(LOW)

    tiles(ff // TILE, unwiden)
    up_grad()

    def to_mid(c):
        tmp[:, c] = nt(dup[...], wu[c, :])

    tiles(width // 256, to_mid, 256)
    gains[0] = jnp.zeros_like(gains[0])

    def store_mid(r, total):
        ef[r, :] = total
        dy[r, :] = total.astype(LOW)

    norm_back(load_mid, tmp, gain_mlp, slice(8, 16), store_mid, 0, rows, 11)

    @pl.when(first)
    def _():
        for band in range(3):
            relay(0, band).wait_send()

    def to_mix(c):
        yb[:, c] = nt(dy[...], wo[c, :]).astype(LOW)

    tiles(width // TILE, to_mix)
    mixf[...] = yb[0:lat, :].astype(F32)

    @pl.when(second)
    def _():
        k = kv_all[:, :, :width].reshape(keys, width)
        v = kv_all[:, :, width:].reshape(keys, width)
        for m in range(half):
            b = slice(m * 128, (m + 1) * 128)
            block_diagonal(vbd.at[pl.ds(256, 256)], m * 128, mixf, m * LAT, 0, 1.0)
        both = slice(0, half * 128)
        do = vbd[256 : 256 + half * 128, :]
        pt = probs_lat[both, 0:keys]
        pf = pt.astype(F32)
        dp = nt(do, v)
        along = jnp.sum(pf * dp, axis=1, keepdims=True)
        ds = (pf * (dp - along)).astype(LOW)
        kvg_send[:, :, :width] = tn(ds, qbd[both, :]).astype(LOW).reshape(n, lat, width)
        kvg_send[:, :, width:] = tn(pt, do).astype(LOW).reshape(n, lat, width)
        for shift in range(1, n):
            kvg_copy(shift).start()
        dq = nn(ds, k)
        for m in range(half):
            head_sum(latf, m * LAT, 0, dq[m * 128 : (m + 1) * 128], 0.125, False)
        proj[0:lat, :width] = latf[:, :width].astype(LOW)
        layer_output(0, lat + GROUP, False)
        layer_output(lat + GROUP, rows, False)
        for copy in out_copies:
            copy.start()

    weight_grad(
        lambda i, right, piece: (2 * wide, i * many + piece),
        0,
        width // part,
        lambda i: dy[:, at(i * part, part)],
        lambda i: mixed[...],
    )
    for copy in out_copies:
        copy.wait()

    @pl.when(first)
    def _():
        for m in range(half):
            r = slice(lat + m * GROUP, lat + (m + 1) * GROUP)
            b = slice(m * 128, (m + 1) * 128)
            block_diagonal(vbd, m * 128, mixf, m * LAT, 0, 1.0)
            do = vbd[b, :]
            dp = nt(do, proj[r, 2 * width :])
            dl = nt(do, proj[0:lat, 2 * width :])
            pt = probs_lat[b, 0:GROUP]
            pe = probs_lat[b, GROUP : GROUP + lat]
            pf = pt.astype(F32)
            pg = pe.astype(F32)
            along = jnp.sum(pf * dp, axis=1, keepdims=True) + jnp.sum(
                pg * dl, axis=1, keepdims=True
            )
            ds = (pf * (dp - along)).astype(LOW)
            dsl = (pg * (dl - along)).astype(LOW)
            dq = nn(ds, proj[r, width : 2 * width]) + nn(dsl, proj[0:lat, width : 2 * width])
            head_sum(latf, m * LAT, 0, dq, 0.125, False)
            tmp[r, :] = tn(ds, qbd[b, :])
            out[r, :] = tn(pt, do)
            if m == 0:
                tmp[0:lat, :] = tn(dsl, qbd[b, :])
                out[0:lat, :] = tn(pe, do)
            else:
                tmp[0:lat, :] += tn(dsl, qbd[b, :])
                out[0:lat, :] += tn(pe, do)
        proj[0:lat, :width] = latf[:, :width].astype(LOW)

        def one_pair(it, side):
            m, p = it // pairs, lax.rem(it, pairs)
            r = pl.ds(pl.multiple_of(lat + m * GROUP, 16), GROUP)
            qc = at(p * 128, 128)
            q = proj[r, qc]
            k = proj[r, at(width + p * 128, 128)]
            v = proj[r, at(2 * width + p * 128, 128)]
            kl = proj[0:lat, at(width + p * 128, 128)]
            vl = proj[0:lat, at(2 * width + p * 128, 128)]
            dx = yb[r, qc]
            dq = jnp.zeros((GROUP, 128), F32)
            dk = tmp[r, qc]
            dv = out[r, qc]
            dkl = tmp[0:lat, qc]
            dvl = out[0:lat, qc]
            for e in (0, 1):
                qe = q * eighths[e]
                de = dx * halves[e]
                s = scores.at[2 * side + e]
                s[...] = nt(v, de)
                dl = nt(vl, de)
                pt = probs[2 * it + e, 0:GROUP, :]
                pe = probs[2 * it + e, GROUP : GROUP + lat, :]
                pg = pe.astype(F32)
                along = jnp.sum(pg * dl, axis=0, keepdims=True)
                for c in chunks:
                    pf = probs[2 * it + e, c, :].astype(F32)
                    along += jnp.sum(pf * s[c, :], axis=0, keepdims=True)
                for c in chunks:
                    pf = probs[2 * it + e, c, :].astype(F32)
                    slopes[2 * side + e, c, :] = (pf * (s[c, :] - along)).astype(LOW)
                ds = slopes[2 * side + e]
                dsl = (pg * (dl - along)).astype(LOW)
                dq += tn(ds, k * halves[e]) + tn(dsl, kl * halves[e])
                dk += nn(ds, qe)
                dkl += nn(dsl, qe)
                dv += nn(pt, de)
                dvl += nn(pe, de)
            proj[r, qc] = (dq * 0.125).astype(LOW)
            proj[r, at(width + p * 128, 128)] = dk.astype(LOW)
            proj[r, at(2 * width + p * 128, 128)] = dv.astype(LOW)
            tmp[0:lat, qc] = dkl
            out[0:lat, qc] = dvl

        def pair(i, carry):
            one_pair(2 * i, 0)
            one_pair(2 * i + 1, 1)
            return carry

        lax.fori_loop(0, half * pairs // 2, pair, 0)
        proj[0:lat, width : 2 * width] = tmp[0:lat, :].astype(LOW)
        proj[0:lat, 2 * width :] = out[0:lat, :].astype(LOW)

    @pl.when(second)
    def _():
        for m in range(half):
            r = slice(lat + m * GROUP, lat + (m + 1) * GROUP)
            b = slice(m * 128, (m + 1) * 128)
            pt = probs[m, 0:GROUP, 0:128]
            pf = pt.astype(F32)
            dx = yb[r, :]
            dp = nt(dx, vbd[b, :])
            ds = (pf * (dp - class_sum(pf * dp))).astype(LOW)
            dk = tn(ds, proj[r, :width])
            dv = tn(pt, dx)
            proj[r, :width] = (nn(ds, kbd[b, :]) * 0.125).astype(LOW)
            head_sum(latf, m * LAT, width, dk, 0.125, False)
            head_sum(latf, m * LAT, 2 * width, dv, 1.0, False)
        total = latf[:, width:] + kvg_send[me].astype(F32)
        for shift in range(1, n):
            kvg_copy(shift).wait_recv()
            total += kvg_recv[shift - 1].astype(F32)
        proj[0:lat, width:] = total.astype(LOW)

    def qkv_grad(start, count, r):
        weight_grad(
            lambda i, right, piece: (
                2 * wide + 1 + lax.rem(i * many + piece, 3),
                (i * many + piece) // 3,
            ),
            start,
            count,
            lambda i: proj[r, at(i * part, part)],
            lambda i: n1[r, :],
        )

    @pl.when(first)
    def _():
        qkv_grad(0, 3 * per_part, slice(0, rows))
        for pair in range(4, spread_pairs):
            launch(0, pair)
        relaunch(0)
        relaunch(1)
        relaunch(2)
        relaunch(3)

    @pl.when(first)
    def _():
        def to_in(c):
            tmp[:, c] = nt(proj[...], wq[c, :])

        tiles(width // 256, to_in, 256)

    @pl.when(second)
    def _():
        tmp[...] = nt(proj[:, :width], wq[:, :width])
        tmp[0:lat, :] += nt(proj[0:lat, width:], wq[:, width:])

    def store_in(r, total):
        low = total.astype(LOW)
        yb[r, :] = low
        out[r, :] = jnp.where(first, total, low.astype(F32))

    for band in range(3):
        norm_back(
            load_in, tmp, gain_attn, slice(0, 8), store_in, band * third, (band + 1) * third, 11
        )

        @pl.when(second)
        def _():
            relay(1, band).start()

    for copy in grad_copies:
        copy.start()

    @pl.when(second)
    def _():
        relaunch(0)
        relaunch(1)
        relaunch(2)
        relaunch(3, False)


    @pl.when(second)
    def _():
        qkv_grad(0, per_part, slice(0, rows))
        qkv_grad(per_part, 2 * per_part, slice(0, lat))
        for pair in range(4, spread_pairs):
            launch(0, pair)
        start_own(4)


    def gain_copy(bit):
        return pltpu.make_async_remote_copy(
            src_ref=gains.at[bit],
            dst_ref=land_g.at[bit],
            send_sem=gain_s.at[bit],
            recv_sem=gain_r.at[bit],
            device_id=across(bit),
            device_id_type=MESH,
        )

    def gain_step(bit):
        gain_copy(bit).wait_recv()
        gains[bit + 1] = gains[bit] + land_g[bit]

    def each(lo, hi, phase):
        def one(i, carry):
            onward(phase, i)
            return carry

        lax.fori_loop(lo, hi, one, 0)

    gain_copy(0).start()
    each(0, 4, 1)
    gain_step(0)
    gain_copy(1).start()
    relaunch(4)
    each(0, 2, 2)
    relaunch(5, False)
    each(2, 4, 2)
    gain_step(1)
    gain_copy(2).start()
    each(4, 6, 1)
    each(0, 4, 3)
    gain_step(2)
    gain_copy(3).start()
    each(4, 6, 2)
    gain_step(3)
    each(4, 6, 3)
    final = gains[4]
    for i in (0, 1):
        whole_gain = jnp.sum(final[8 * i : 8 * i + 8], axis=0, keepdims=True)
        whole_gain = jnp.broadcast_to(whole_gain, (8, width))
        rolled = pltpu.roll(whole_gain, lax.rem(width - me * unit, width), 1)
        gain_sums[8 * i : 8 * i + 8, :] = rolled[:, 0:128]

    def finish(k, carry):
        for stream in (0, 1):
            for phase in range(4):
                copy_of(stream, phase, k).wait_send()
        return carry

    lax.fori_loop(0, spread_pairs, finish, 0)
    for bit in range(4):
        gain_copy(bit).wait_send()
    for copy in grad_copies:
        copy.wait()
    for stream in (0, 1):
        for pair in (spread_pairs - 2, spread_pairs - 1):
            leave(stream, pair).wait()

    @pl.when(second)
    def _():
        for band in range(3):
            relay(1, band).wait_send()
        for shift in range(1, n):
            kv_copy(shift, False).wait_send()
            kvg_copy(shift).wait_send()


def both_layers(n, tokens, latents, slots, images, gains, weights, d_tokens, d_latents):
    tok, width = tokens.shape
    lat = latents.shape[0]
    rows = tok + lat
    w_qkv, w_out, w_up, w_down = weights
    ff = w_up.shape[1]
    keys = n * lat
    half = lat // LAT
    size = sum(w.size for w in weights)
    chunks = size // (width * width)
    pairs = chunks // 2
    unit = width // n
    vm, hbm = pl.BlockSpec(memory_space=pltpu.VMEM), pl.BlockSpec(memory_space=pl.ANY)
    sm = pl.BlockSpec(memory_space=pltpu.SMEM)
    scratch = [
        pltpu.VMEM(w.shape, LOW) for w in (w_qkv, w_out, w_up, w_down)
    ] + [
        pltpu.VMEM(shape, dtype)
        for shape, dtype in (
            ((rows, width), LOW),
            ((rows, width), LOW),
            ((rows, 3 * width), LOW),
            ((rows, width), LOW),
            ((rows, width), F32),
            ((rows, width), LOW),
            ((rows, ff), LOW),
            ((rows, ff), LOW),
            ((rows, width), LOW),
            ((rows, width), LOW),
            ((rows, width), F32),
            ((rows, width), F32),
            ((rows, width), F32),
            ((half * width // 64, GROUP + lat, GROUP), LOW),
            ((half * 128, max(keys, GROUP + 128)), LOW),
            ((4, GROUP, GROUP), F32),
            ((4, GROUP, GROUP), LOW),
            ((lat, 3 * width), F32),
            ((lat, width), F32),
            ((8, keys), F32),
            ((half * 128, width), LOW),
            ((half * 128, width), LOW),
            ((half * 256, width), LOW),
            ((n, lat, 2 * width), LOW),
            ((n, lat, 2 * width), LOW),
            ((n - 1, lat, 2 * width), LOW),
            ((2, 384 // unit, unit, width), LOW),
            ((5, 16, width), F32),
            ((2, 2, unit, width), F32),
            ((2, 2, 2, unit, width), LOW),
            ((2, 2, 2, unit, width), LOW),
            ((pairs, 2, 2, 2, unit, width), LOW),
            ((pairs, 2, 2, 2, unit, width), LOW),
            ((pairs, 2, 2, unit, width), LOW),
            ((pairs, 2, 2, unit, width), LOW),
            ((pairs, 2, unit, width), LOW),
            ((pairs, 2, unit, width), LOW),
            ((pairs, unit, width), LOW),
            ((pairs, unit, width), LOW),
            ((4, 16, width), F32),
        )
    ] + [
        pltpu.SemaphoreType.DMA((10,)),
        pltpu.SemaphoreType.DMA((2, 384 // unit)),
        pltpu.SemaphoreType.DMA((2,)),
        pltpu.SemaphoreType.DMA((2, 2)),
        pltpu.SemaphoreType.DMA((2, 4, pairs)),
        pltpu.SemaphoreType.DMA((2, 4, pairs)),
        pltpu.SemaphoreType.DMA((4,)),
        pltpu.SemaphoreType.DMA((4,)),
        pltpu.SemaphoreType.DMA((6,)),
        pltpu.SemaphoreType.DMA((6,)),
        pltpu.SemaphoreType.DMA((n - 1,)),
        pltpu.SemaphoreType.DMA((n - 1,)),
        pltpu.SemaphoreType.DMA((n - 1,)),
        pltpu.SemaphoreType.DMA((n - 1,)),
    ]
    return pl.pallas_call(
        functools.partial(layer_kernel, n),
        out_shape=(
            jax.ShapeDtypeStruct((tok, width), F32),
            jax.ShapeDtypeStruct((lat, width), F32),
            jax.ShapeDtypeStruct((tok, width), F32),
            jax.ShapeDtypeStruct((lat, width), F32),
            jax.ShapeDtypeStruct((chunks, 2, 2, 2, 2, unit, width), LOW),
            jax.ShapeDtypeStruct((chunks, unit, width), F32),
            jax.ShapeDtypeStruct((16, 128), F32),
        ),
        in_specs=[hbm, hbm, vm, sm, sm, vm, vm] + [hbm] * 6,
        out_specs=(hbm,) * 6 + (vm,),
        scratch_shapes=scratch,
        compiler_params=pltpu.CompilerParams(
            collective_id=1, has_side_effects=True, vmem_limit_bytes=63 * 1024 * 1024
        ),
        cost_estimate=pl.CostEstimate(
            flops=6 * rows * size, bytes_accessed=4 * size, transcendentals=0
        ),
    )(tokens, latents, slots, slots, images, *gains, *weights, d_tokens, d_latents)


def finish_kernel(width, *refs):
    rows_in, (summed, gains), rows_out = refs[0:4], refs[4:6], refs[6:10]
    gain_attn, g_qkv, g_out, gain_mlp, g_up, g_down = refs[10:16]
    held, (sem_in, sem_out) = refs[16:21], refs[21:23]
    wide = g_down.shape[1] // width
    unit = g_out.shape[1]
    loads = [
        pltpu.make_async_copy(src, dst, sem_in.at[i])
        for i, (src, dst) in enumerate(zip((*rows_in, summed), held))
    ]
    for load in loads:
        load.start()
    all_rows, sums = held[0:4], held[4]
    moves = [[pair] for pair in zip(all_rows, rows_out)] + [
        [(sums.at[c], g_down.at[:, c * width : (c + 1) * width]) for c in range(wide)]
        + [
            (sums.at[wide : 2 * wide], g_up),
            (sums.at[2 * wide : 2 * wide + 1], g_out),
            (sums.at[2 * wide + 1 :], g_qkv),
        ]
    ]
    gain_attn[...] = gains[0:1, 0:unit]
    gain_mlp[...] = gains[8:9, 0:unit]
    started = []
    for load, group in zip(loads, moves):
        load.wait()
        for src, dst in group:
            started.append(pltpu.make_async_copy(src, dst, sem_out.at[len(started)]))
            started[-1].start()
    for move in started:
        move.wait()


def finished(rows, summed, gains, wide):
    chunks, unit, width = summed.shape
    hbm, vm = pl.BlockSpec(memory_space=pl.ANY), pl.BlockSpec(memory_space=pltpu.VMEM)
    shapes = [r.shape for r in rows] + [
        (1, unit),
        (3, unit, width),
        (1, unit, width),
        (1, unit),
        (wide, unit, width),
        (unit, wide * width),
    ]
    return pl.pallas_call(
        functools.partial(finish_kernel, width),
        out_shape=tuple(jax.ShapeDtypeStruct(s, F32) for s in shapes),
        in_specs=[hbm] * 5 + [vm],
        out_specs=(hbm,) * 4 + (vm, hbm, hbm, vm, hbm, hbm),
        scratch_shapes=[pltpu.VMEM(x.shape, F32) for x in (*rows, summed)]
        + [pltpu.SemaphoreType.DMA((5,)), pltpu.SemaphoreType.DMA((7 + wide,))],
        compiler_params=pltpu.CompilerParams(vmem_limit_bytes=62 * 1024 * 1024),
    )(*rows, summed, gains)
def fused_shards(
    unused_grid,
    tokens,
    latents,
    slot_group,
    image_groups,
    gain_attn,
    w_qkv,
    w_out,
    gain_mlp,
    w_up,
    w_down,
    d_tokens,
    d_latents,
):
    micro, tok, width = tokens.shape
    lat = latents.shape[1]
    out_tok, out_lat, grad_tok, grad_lat, unused_grads, summed, gains = both_layers(
        slot_group.shape[1],
        tokens.reshape(micro * tok, width),
        latents.reshape(micro * lat, width),
        slot_group,
        image_groups,
        (gain_attn, gain_mlp),
        (w_qkv[0], w_out[0], w_up[0], w_down[0]),
        d_tokens.reshape(micro * tok, width),
        d_latents.reshape(micro * lat, width),
    )
    wide = w_up.shape[2] // width
    rows = (out_tok, out_lat, grad_tok, grad_lat)
    *rows, first_gain, qkv, out, second_gain, up, down = finished(rows, summed, gains, wide)
    return (
        rows[0].reshape(1, micro, tok, width),
        rows[1].reshape(1, micro, lat, width),
        rows[2].reshape(1, micro, tok, width),
        rows[3].reshape(1, micro, lat, width),
        first_gain,
        qkv.reshape(-1, width).T[None],
        out.reshape(-1, width).T[None],
        second_gain,
        up.reshape(-1, width).T[None],
        down.T[None],
    )

def solution(mesh):
    in_specs = (
        P(None, "dp", None),
        P(None, "dp", None),
        P(),
        P(),
        P("section", None),
        P("section", None, None),
        P("section", None, None),
        P("section", None),
        P("section", None, None),
        P("section", None, None),
        P(None, "dp", None),
        P(None, "dp", None),
    )
    out_specs = (
        P("section", None, "dp", None),
        P("section", None, "dp", None),
        P("section", None, "dp", None),
        P("section", None, "dp", None),
        P("section", "dp"),
        P("section", None, "dp"),
        P("section", None, "dp"),
        P("section", "dp"),
        P("section", None, "dp"),
        P("section", None, "dp"),
    )
    grid = grid_of(mesh)

    def program(*args):
        n, width = mesh.shape["dp"], args[0].shape[2]
        one_group = args[0].shape[1] == n * GROUP
        body = fused_shards if one_group and n == 16 and width % (16 * n) == 0 else shards
        return jax.shard_map(
            functools.partial(body, grid), mesh=mesh, in_specs=in_specs, out_specs=out_specs, check_vma=False
        )(*args)

    return program
```

```python
import functools

import jax
import jax.numpy as jnp
from jax import lax
from jax.experimental import pallas as pl
from jax.experimental.pallas import tpu as pltpu
from jax.sharding import PartitionSpec as P

HEADS = 12
GROUP = 256
LAT = 8


epsilon = 1e-05
masked_score = -1e30


MESH = pl.DeviceIdType.MESH


def grid_of(mesh):
    n = mesh.shape["dp"]
    coords = [getattr(d, "coords", None) for d in mesh.devices.reshape(n, -1)[:, 0]]
    if any(c is None for c in coords):
        return (n // 4, 2, 2) if n % 4 == 0 else (n, 1, 1)
    sizes = {a: len({c[a] for c in coords}) for a in range(3)}
    strides = {
        a: min([i for i in range(n) if coords[i][a] != coords[0][a]], default=n) for a in range(3)
    }
    order = sorted(range(3), key=lambda a: -strides[a])
    return tuple(sizes[a] for a in order)


def spread_kernel(grid, pairs, g_ref, gain_ref, out_ref, gout_ref, *scratch):
    acc = scratch[0:3]
    land = [scratch[3 + 3 * i : 6 + 3 * i] for i in range(3)]
    send_sem, recv_sem, own_sem = scratch[12:15]
    me = lax.axis_index("dp")
    section = lax.axis_index("section")
    l0, l1, l2 = grid
    here = (me // (l1 * l2), lax.rem(me // l2, l1), lax.rem(me, l2))

    def device(axis, shift):
        there = list(here)
        there[axis] = lax.rem(here[axis] + shift, grid[axis])
        return there[axis], ((there[0] * l1 + there[1]) * l2 + there[2], section)

    barrier = pltpu.get_barrier_semaphore()
    for axis in range(3):
        for shift in range(1, grid[axis]):
            pl.semaphore_signal(
                barrier, inc=1, device_id=device(axis, shift)[1], device_id_type=MESH
            )
    pl.semaphore_wait(barrier, sum(grid) - 3)

    orders = ((2, 1, 0), (1, 2, 0), (2, 1, 0))

    def source(stream, phase, k, at):
        if phase == 0:
            if stream == 0:
                return g_ref.at[2 * k, :, :, at]
            if stream == 1:
                return g_ref.at[2 * k + 1, :, at]
            return gain_ref.at[:, :, at]
        if phase == 1:
            return acc[stream].at[k, :, at]
        return acc[stream].at[k, at, here[orders[stream][1]]]

    def copies(stream, phase, k):
        axis = orders[stream][phase]
        for shift in range(1, grid[axis]):
            at, target = device(axis, shift)
            yield pltpu.make_async_remote_copy(
                src_ref=source(stream, phase, k, at),
                dst_ref=land[phase][stream].at[k, shift - 1],
                send_sem=send_sem.at[stream, phase, k, shift - 1],
                recv_sem=recv_sem.at[stream, phase, k, shift - 1],
                device_id=target,
                device_id_type=MESH,
            )

    def own(stream, k):
        return pltpu.make_async_copy(
            source(stream, 0, k, here[orders[stream][0]]), acc[stream].at[k], own_sem.at[stream, k]
        )

    def launch(stream, phase, k):
        for copy in copies(stream, phase, k):
            copy.start()

    def absorb(stream, phase, k):
        axis = orders[stream][phase]
        if phase == 0:
            own(stream, k).wait()
        for copy in copies(stream, phase, k):
            copy.wait_recv()
        into = land[phase][stream]
        count = grid[axis] - 1
        if phase == 0:
            for a in range(acc[stream].shape[1]):
                for b in range(acc[stream].shape[2]):
                    total = acc[stream][k, a, b].astype(jnp.float32)
                    for s in range(count):
                        total += into[k, s, a, b].astype(jnp.float32)
                    acc[stream][k, a, b] = total.astype(acc[stream].dtype)
        elif phase == 1:
            mine = here[axis]
            for a in range(acc[stream].shape[1]):
                total = acc[stream][k, a, mine].astype(jnp.float32)
                for s in range(count):
                    total += into[k, s, a].astype(jnp.float32)
                acc[stream][k, a, mine] = total.astype(acc[stream].dtype)
        else:
            total = acc[stream][k, here[0], here[orders[stream][1]]].astype(jnp.float32)
            for s in range(count):
                total += into[k, s].astype(jnp.float32)
            if stream < 2:
                out_ref[2 * k + stream] = total
            else:
                gout_ref[...] = total

    own(2, 0).start()
    launch(2, 0, 0)

    def start_own(k, carry):
        for stream in (0, 1):
            own(stream, k).start()
        return carry

    for stream in (0, 1):
        launch(stream, 0, 0)
    lax.fori_loop(0, pairs, start_own, 0)

    def turn(t, carry):
        @pl.when(t + 1 < pairs)
        def _():
            for stream in (0, 1):
                launch(stream, 0, t + 1)

        @pl.when(t < pairs)
        def _():
            for stream in (0, 1):
                absorb(stream, 0, t)
                launch(stream, 1, t)

        @pl.when((t >= 1) & (t - 1 < pairs))
        def _():
            for stream in (0, 1):
                absorb(stream, 1, t - 1)
                launch(stream, 2, t - 1)

        @pl.when(t >= 2)
        def _():
            for stream in (0, 1):
                absorb(stream, 2, t - 2)

        return carry

    lax.fori_loop(0, pairs + 2, turn, 0)
    absorb(2, 0, 0)
    launch(2, 1, 0)
    absorb(2, 1, 0)
    launch(2, 2, 0)
    absorb(2, 2, 0)

    def finish(k, carry):
        for stream in (0, 1):
            for phase in range(3):
                for copy in copies(stream, phase, k):
                    copy.wait_send()
        return carry

    lax.fori_loop(0, pairs, finish, 0)
    for phase in range(3):
        for copy in copies(2, phase, 0):
            copy.wait_send()


def spread(grid, grads, gains):
    chunks, n, rows, width = grads.shape
    pairs = chunks // 2
    l0, l1, l2 = grid
    most = max(max(grid) - 1, 1)
    low = jnp.bfloat16
    shapes = ((pairs, rows, width, low), (pairs, rows, width, low), (1, 8, 128, jnp.float32))
    inner = ((l1, l2), (l2, l1), (l1, l2))
    acc, first, second, third = [], [], [], []
    for (count, r, w, dt), (kept, sent) in zip(shapes, inner):
        acc.append(pltpu.VMEM((count, l0, kept, r, w), dt))
        first.append(pltpu.VMEM((count, max(sent - 1, 1), l0, kept, r, w), dt))
        second.append(pltpu.VMEM((count, max(kept - 1, 1), l0, r, w), dt))
        third.append(pltpu.VMEM((count, max(l0 - 1, 1), r, w), dt))
    return pl.pallas_call(
        functools.partial(spread_kernel, grid, pairs),
        out_shape=(
            jax.ShapeDtypeStruct((chunks, rows, width), jnp.float32),
            jax.ShapeDtypeStruct((8, 128), jnp.float32),
        ),
        in_specs=[pl.BlockSpec(memory_space=pl.ANY)] * 2,
        out_specs=(pl.BlockSpec(memory_space=pltpu.VMEM),) * 2,
        scratch_shapes=acc
        + first
        + second
        + third
        + [
            pltpu.SemaphoreType.DMA((3, 3, pairs, most)),
            pltpu.SemaphoreType.DMA((3, 3, pairs, most)),
            pltpu.SemaphoreType.DMA((3, pairs)),
        ],
        compiler_params=pltpu.CompilerParams(
            collective_id=0, has_side_effects=True, vmem_limit_bytes=60 * 1024 * 1024
        ),
        cost_estimate=pl.CostEstimate(flops=0, bytes_accessed=grads.size * 4, transcendentals=0),
    )(grads.reshape(chunks, l0, l1, l2, rows, width), gains.reshape(l0, l1, l2, 8, 128))


def from_behind(x, axis, by):
    devices = lax.axis_size(axis)
    pairs = [(i, i + by) for i in range(devices) if 0 <= i + by < devices]
    return lax.ppermute(x, axis, pairs)


def layer_norm(values, gain):
    row_mean = jnp.mean(values, axis=-1, keepdims=True)
    centred = values - row_mean
    row_var = jnp.mean(centred * centred, axis=-1, keepdims=True)
    return centred * lax.rsqrt(row_var + epsilon) * gain


def front_half(all_rows, gain_attn, w_qkv):
    normed = layer_norm(all_rows, gain_attn).astype(jnp.bfloat16)
    projected = jnp.dot(normed, w_qkv, preferred_element_type=jnp.float32).astype(jnp.bfloat16)
    return (normed, projected)


def latent_operand(projected, tok_rows, model_width):
    return projected[tok_rows:, model_width:]


def back_half(all_rows, projected, remote_rows, allowed, weights):
    gain_attn, w_qkv, w_out, gain_mlp, w_up, w_down = weights
    row_count, model_width = all_rows.shape
    head_size = model_width // HEADS
    remote_pairs = remote_rows[:, remote_rows.shape[1] - 2 * model_width :]
    queries = projected[:, :model_width].reshape(row_count, HEADS, head_size)
    key_rows = jnp.concatenate(
        [projected[:, model_width : 2 * model_width], remote_pairs[:, :model_width]], axis=0
    )
    value_rows = jnp.concatenate(
        [projected[:, 2 * model_width :], remote_pairs[:, model_width:]], axis=0
    )
    key_rows = key_rows.reshape(-1, HEADS, head_size)
    value_rows = value_rows.reshape(-1, HEADS, head_size)
    scores = jnp.einsum(
        "qhd,khd->hqk", queries, key_rows, preferred_element_type=jnp.float32
    ) * head_size ** (-0.5)
    attn_weights = jax.nn.softmax(jnp.where(allowed[None], scores, masked_score), axis=-1)
    attn_low = attn_weights.astype(jnp.bfloat16)
    mixed_low = jnp.einsum("hqk,khd->qhd", attn_low, value_rows, preferred_element_type=jnp.float32)
    mixed_low = mixed_low.reshape(row_count, model_width).astype(jnp.bfloat16)
    mid_rows = all_rows + jnp.dot(mixed_low, w_out, preferred_element_type=jnp.float32)
    normed_mlp = layer_norm(mid_rows, gain_mlp).astype(jnp.bfloat16)
    up_proj = jnp.dot(normed_mlp, w_up, preferred_element_type=jnp.float32)
    activated = jax.nn.gelu(up_proj).astype(jnp.bfloat16)
    result = mid_rows + jnp.dot(activated, w_down, preferred_element_type=jnp.float32)
    return dict(
        queries=queries,
        key_rows=key_rows,
        value_rows=value_rows,
        attn_weights=attn_weights,
        attn_low=attn_low,
        mixed_low=mixed_low,
        mid_rows=mid_rows,
        normed_mlp=normed_mlp,
        up_proj=up_proj,
        activated=activated,
        result=result,
    )


def section_backward(saved, d_result, all_rows, normed, allowed, weights, latent_start):
    gain_attn, w_qkv, w_out, gain_mlp, w_up, w_down = weights
    row_count, model_width = all_rows.shape
    head_size = model_width // HEADS
    score_scale = head_size ** (-0.5)
    d_low = d_result.astype(jnp.bfloat16)
    grad_down = jnp.dot(d_low.T, saved["activated"], preferred_element_type=jnp.float32)
    d_activated = jnp.dot(d_low, w_down.T, preferred_element_type=jnp.float32)
    unused_up, gelu_back = jax.vjp(jax.nn.gelu, saved["up_proj"])
    d_up = gelu_back(d_activated)[0].astype(jnp.bfloat16)
    grad_up = jnp.dot(d_up.T, saved["normed_mlp"], preferred_element_type=jnp.float32)
    d_normed_mlp = jnp.dot(d_up, w_up.T, preferred_element_type=jnp.float32)
    unused_mid, second_back = jax.vjp(layer_norm, saved["mid_rows"], gain_mlp)
    d_mid_norm, grad_gain_mlp = second_back(d_normed_mlp)
    d_mid = d_result + d_mid_norm
    d_mid_low = d_mid.astype(jnp.bfloat16)
    grad_out = jnp.dot(d_mid_low.T, saved["mixed_low"], preferred_element_type=jnp.float32)
    d_mixed = jnp.dot(d_mid_low, w_out.T, preferred_element_type=jnp.float32).astype(jnp.bfloat16)
    d_mixed = d_mixed.reshape(row_count, HEADS, head_size)
    d_weights = jnp.einsum(
        "qhd,khd->hqk", d_mixed, saved["value_rows"], preferred_element_type=jnp.float32
    )
    d_values = jnp.einsum(
        "hqk,qhd->khd", saved["attn_low"], d_mixed, preferred_element_type=jnp.float32
    )
    attn_weights = saved["attn_weights"]
    d_scores = attn_weights * (
        d_weights - jnp.sum(attn_weights * d_weights, axis=-1, keepdims=True)
    )
    d_scores_low = jnp.where(allowed[None], d_scores, 0.0).astype(jnp.bfloat16)
    d_queries = (
        jnp.einsum(
            "hqk,khd->qhd", d_scores_low, saved["key_rows"], preferred_element_type=jnp.float32
        )
        * score_scale
    )
    d_keys = (
        jnp.einsum(
            "hqk,qhd->khd", d_scores_low, saved["queries"], preferred_element_type=jnp.float32
        )
        * score_scale
    )
    remote_part = jnp.concatenate(
        [
            d_keys[row_count:].reshape(-1, model_width),
            d_values[row_count:].reshape(-1, model_width),
        ],
        axis=1,
    )
    own_part = lax.psum_scatter(remote_part, "dp", scatter_dimension=0, tiled=True)
    local_pairs = jnp.concatenate(
        [
            d_keys[:row_count].reshape(row_count, model_width),
            d_values[:row_count].reshape(row_count, model_width),
        ],
        axis=1,
    )
    local_pairs = jnp.concatenate(
        [local_pairs[:latent_start], local_pairs[latent_start:] + own_part], axis=0
    )
    d_projected = jnp.concatenate(
        [d_queries.reshape(row_count, model_width), local_pairs], axis=1
    ).astype(jnp.bfloat16)
    grad_qkv = jnp.dot(d_projected.T, normed, preferred_element_type=jnp.float32)
    d_normed = jnp.dot(d_projected, w_qkv.T, preferred_element_type=jnp.float32)
    unused_rows, first_back = jax.vjp(layer_norm, all_rows, gain_attn)
    d_rows_norm, grad_gain_attn = first_back(d_normed)
    return (
        d_mid + d_rows_norm,
        (grad_gain_attn, grad_qkv, grad_out, grad_gain_mlp, grad_up, grad_down),
    )


def packed(grads, n):
    gain_first, qkv_grad, out_grad, gain_second, up_grad, down_grad = grads
    width = out_grad.shape[0]
    rows = width // n

    def by_rows(grad):
        return grad.reshape(n, -1, rows, width).transpose(1, 0, 2, 3).astype(jnp.bfloat16)

    down = down_grad.reshape(n, rows, -1, width).transpose(2, 0, 1, 3).astype(jnp.bfloat16)
    chunks = jnp.concatenate([down, by_rows(up_grad), by_rows(out_grad), by_rows(qkv_grad)], axis=0)
    gains = jnp.stack([gain_first.reshape(n, rows), gain_second.reshape(n, rows)], axis=1)
    return chunks, jnp.pad(gains, ((0, 0), (0, 6), (0, 128 - rows)))


def shards(
    grid,
    tokens,
    latents,
    slot_group,
    image_groups,
    gain_attn,
    w_qkv,
    w_out,
    gain_mlp,
    w_up,
    w_down,
    d_tokens,
    d_latents,
):
    micro = tokens.shape[0]
    tok_rows = tokens.shape[1]
    lat_rows = latents.shape[1]
    model_width = tokens.shape[2]
    local_groups = tok_rows // GROUP
    section_index = lax.axis_index("section")
    is_global = section_index == 1
    dp_index = lax.axis_index("dp")
    weights = (gain_attn[0], w_qkv[0], w_out[0], gain_mlp[0], w_up[0], w_down[0])
    image_ends = jnp.cumsum(image_groups, axis=1)
    slot_images = jnp.sum(
        (image_ends[:, None, :] <= slot_group[:, :, None]).astype(jnp.int32), axis=2
    )
    slot_total = slot_group.shape[1]
    row_group = jnp.concatenate([jnp.arange(tok_rows) // GROUP, jnp.arange(lat_rows) // LAT])
    row_latent = jnp.concatenate(
        [jnp.zeros((tok_rows,), jnp.bool_), jnp.ones((lat_rows,), jnp.bool_)]
    )
    same_group = row_group[:, None] == row_group[None, :]
    local_mask = jnp.where(
        is_global, (~row_latent)[:, None] & row_latent[None, :] & same_group, same_group
    )
    group_match = row_group[:, None] == jnp.arange(local_groups)[None, :]

    def key_images(batch):
        images_row = lax.dynamic_index_in_dim(slot_images, batch, 0, keepdims=False)
        return (images_row, jnp.broadcast_to(images_row[:, None], (slot_total, LAT)).reshape(-1))

    def allowed_for(batch):
        images_row, key_image = key_images(batch)
        own_images = lax.dynamic_slice_in_dim(images_row, dp_index * local_groups, local_groups)
        row_image = jnp.sum(jnp.where(group_match, own_images[None, :], 0), axis=1)
        remote_mask = is_global & row_latent[:, None] & (row_image[:, None] == key_image[None, :])
        return jnp.concatenate([local_mask, remote_mask], axis=1)

    def forward_turn(received, turn):
        recv_tokens, recv_latents = received
        batch = jnp.clip(turn - section_index, 0, micro - 1)
        own_tok = lax.dynamic_index_in_dim(tokens, batch, 0, keepdims=False)
        own_lat = lax.dynamic_index_in_dim(latents, batch, 0, keepdims=False)
        input_rows = jnp.concatenate(
            [
                jnp.where(is_global, recv_tokens, own_tok),
                jnp.where(is_global, recv_latents, own_lat),
            ],
            axis=0,
        )
        all_rows = input_rows.astype(jnp.float32)
        normed, projected = front_half(all_rows, weights[0], weights[1])
        remote_rows = lax.all_gather(
            latent_operand(projected, tok_rows, model_width), "dp", axis=0, tiled=True
        )
        saved = back_half(all_rows, projected, remote_rows, allowed_for(batch), weights)
        result = saved["result"]
        result_low = result.astype(jnp.bfloat16)
        stored = jnp.where(is_global, result, result_low.astype(jnp.float32))
        passed_on = from_behind((result_low[:tok_rows], result_low[tok_rows:]), "section", 1)
        return passed_on, (input_rows, stored[:tok_rows], stored[tok_rows:])

    nothing = (
        jnp.zeros((tok_rows, model_width), jnp.bfloat16),
        jnp.zeros((lat_rows, model_width), jnp.bfloat16),
    )
    turns = jnp.arange(micro + 1)
    unused_end, (kept_rows, tok_outputs, lat_outputs) = lax.scan(forward_turn, nothing, turns)

    def backward_turn(carry, turn):
        (recv_grad_tok, recv_grad_lat), totals = carry
        raw_batch = micro - turn - section_index
        valid = ((raw_batch >= 0) & (raw_batch < micro)).astype(jnp.float32)
        batch = jnp.clip(raw_batch, 0, micro - 1)
        all_rows = lax.dynamic_index_in_dim(
            kept_rows, batch + section_index, 0, keepdims=False
        ).astype(jnp.float32)
        normed, projected = front_half(all_rows, weights[0], weights[1])
        remote_rows = lax.all_gather(
            latent_operand(projected, tok_rows, model_width), "dp", axis=0, tiled=True
        )
        allowed = allowed_for(batch)
        saved = back_half(all_rows, projected, remote_rows, allowed, weights)
        given = (
            jnp.concatenate(
                [
                    lax.dynamic_index_in_dim(d_tokens, batch, 0, keepdims=False),
                    lax.dynamic_index_in_dim(d_latents, batch, 0, keepdims=False),
                ],
                axis=0,
            )
            * valid
        )
        passed = jnp.concatenate([recv_grad_tok, recv_grad_lat], axis=0).astype(jnp.float32)
        d_result = jnp.where(is_global, given, passed)
        d_rows, grads = section_backward(
            saved, d_result, all_rows, normed, allowed, weights, tok_rows
        )
        totals = tuple((accum + piece for accum, piece in zip(totals, grads)))
        d_rows_low = d_rows.astype(jnp.bfloat16)
        stored = jnp.where(is_global, d_rows_low.astype(jnp.float32), d_rows)
        sent = from_behind((d_rows_low[:tok_rows], d_rows_low[tok_rows:]), "section", -1)
        return (sent, totals), (stored[:tok_rows], stored[tok_rows:])

    totals = tuple(
        jnp.zeros(w.shape[::-1] if w.ndim == 2 else w.shape, jnp.float32) for w in weights
    )
    (unused_sent, totals), (tok_grads, lat_grads) = lax.scan(
        backward_turn, (nothing, totals), turns
    )
    chunks, gains = packed(totals, lax.axis_size("dp"))
    summed, gain_sums = spread(grid, chunks, gains)
    rows = summed.shape[1]
    layer_tokens = lax.dynamic_slice_in_dim(tok_outputs, section_index, micro, 0)[None]
    layer_latents = lax.dynamic_slice_in_dim(lat_outputs, section_index, micro, 0)[None]
    grad_tokens = lax.dynamic_slice_in_dim(tok_grads, 1 - section_index, micro, 0)[::-1][
        None
    ]
    grad_latents = lax.dynamic_slice_in_dim(lat_grads, 1 - section_index, micro, 0)[
        ::-1
    ][None]
    return (
        layer_tokens,
        layer_latents,
        grad_tokens,
        grad_latents,
        gain_sums[0:1, :rows],
        summed[9:].reshape(-1, model_width).T[None],
        summed[8].T[None],
        gain_sums[1:2, :rows],
        summed[4:8].reshape(-1, model_width).T[None],
        summed[0:4].transpose(0, 2, 1).reshape(-1, rows)[None],
    )


F32 = jnp.float32
LOW = jnp.bfloat16
HEAD_PAD = 16
TILE = 768


def nn(a, b):
    return jnp.dot(a, b, preferred_element_type=F32)


def nt(a, b):
    return lax.dot_general(a, b, (((1,), (1,)), ((), ())), preferred_element_type=F32)


def tn(a, b):
    return lax.dot_general(a, b, (((0,), (0,)), ((), ())), preferred_element_type=F32)


def row_mean(values):
    return jnp.mean(values, axis=-1, keepdims=True)


def row_stats(load, spans):
    means = [row_mean(load(r)) for r in spans]
    scales = []
    for r, mean in zip(spans, means):
        centred = load(r) - mean
        scales.append(lax.rsqrt(row_mean(centred * centred) + epsilon))
    return means, scales


def at(start, size):
    return pl.ds(pl.multiple_of(start, size), size)


def class_max(s):
    for by in (16, 32, 64):
        s = jnp.maximum(s, pltpu.roll(s, by, 1))
    return s


def class_sum(s):
    for by in (16, 32, 64):
        s = s + pltpu.roll(s, by, 1)
    return s


def layer_kernel(
    n,
    tokens,
    latents,
    slots,
    slot_at,
    image_at,
    gain_attn,
    gain_mlp,
    w_qkv,
    w_out,
    w_up,
    w_down,
    d_tokens,
    d_latents,
    out_tok,
    out_lat,
    grad_tok,
    grad_lat,
    grads,
    summed,
    gain_sums,
    wq,
    wo,
    wu,
    wd,
    xb,
    n1,
    proj,
    mixed,
    mid,
    n2,
    act,
    dup,
    yb,
    dy,
    ef,
    tmp,
    out,
    probs,
    probs_lat,
    scores,
    slopes,
    latf,
    mixf,
    key_mask,
    qbd,
    kbd,
    vbd,
    kv_all,
    kvg_send,
    kvg_recv,
    stage,
    gains,
    leaving,
    own_a,
    own_b,
    land1_a,
    land1_b,
    land1_c,
    land2_a,
    land2_b,
    land2_c,
    land3_a,
    land3_b,
    land3_c,
    land4_a,
    land4_b,
    land4_c,
    land_g,
    load_sem,
    stage_sem,
    own_sem,
    leave_sem,
    send_sem,
    recv_sem,
    gain_s,
    gain_r,
    relay_send,
    relay_recv,
    kv_sem_s,
    kv_sem_r,
    kvg_sem_s,
    kvg_sem_r,
):
    rows, width = xb.shape
    ff = act.shape[1]
    tok = tokens.shape[0]
    lat = latents.shape[0]
    half = lat // LAT
    pairs = width // 128
    me = lax.axis_index("dp")
    section = lax.axis_index("section")
    first = section == 0
    second = section == 1
    partner = (me, 1 - section)

    loads = [
        pltpu.make_async_copy(src, dst, load_sem.at[i])
        for i, (src, dst) in enumerate(((w_qkv, wq), (w_out, wo), (w_up, wu), (w_down, wd)))
    ]
    x_loads = [
        pltpu.make_async_copy(tokens, xb.at[lat:rows], load_sem.at[4]),
        pltpu.make_async_copy(latents, xb.at[0:lat], load_sem.at[5]),
    ]
    e_loads = [
        pltpu.make_async_copy(d_tokens, ef.at[lat:rows], load_sem.at[6]),
        pltpu.make_async_copy(d_latents, ef.at[0:lat], load_sem.at[7]),
    ]

    @pl.when(first)
    def _():
        for copy in x_loads:
            copy.start()

    for copy in loads:
        copy.start()

    @pl.when(second)
    def _():
        for copy in e_loads:
            copy.start()

    barrier = pltpu.get_barrier_semaphore()
    pl.semaphore_signal(barrier, inc=1, device_id=partner, device_id_type=MESH)

    here = [lax.rem(me // (1 << bit), 2) for bit in range(4)]

    def across(bit):
        return (me + (1 - 2 * here[bit]) * (1 << bit), section)

    @pl.when(second)
    def _():
        for shift in range(1, n):
            pl.semaphore_signal(
                barrier, inc=1, device_id=(lax.rem(me + shift, n), section), device_id_type=MESH
            )
        pl.semaphore_wait(barrier, n)

    @pl.when(first)
    def _():
        for bit in range(4):
            pl.semaphore_signal(barrier, inc=1, device_id=across(bit), device_id_type=MESH)
        pl.semaphore_wait(barrier, 5)

    def relay(back, band):
        low, high = ((0, rows // 3), (rows // 3, 2 * rows // 3), (2 * rows // 3, rows))[band]
        if not back:
            low, high = ((0, lat), (lat, lat + GROUP), (lat + GROUP, rows))[band]
        return pltpu.make_async_remote_copy(
            src_ref=yb.at[low:high],
            dst_ref=(dy if back else xb).at[low:high],
            send_sem=relay_send.at[3 * back + band],
            recv_sem=relay_recv.at[3 * back + band],
            device_id=partner,
            device_id_type=MESH,
        )

    def kv_copy(shift, incoming):
        slot = lax.rem(me + n - shift, n) if incoming else me
        return pltpu.make_async_remote_copy(
            src_ref=kv_all.at[me], dst_ref=kv_all.at[slot],
            send_sem=kv_sem_s.at[shift - 1], recv_sem=kv_sem_r.at[shift - 1],
            device_id=(lax.rem(me + shift, n), section), device_id_type=MESH,
        )

    def kvg_copy(shift):
        there = lax.rem(me + shift, n)
        return pltpu.make_async_remote_copy(
            src_ref=kvg_send.at[there], dst_ref=kvg_recv.at[shift - 1],
            send_sem=kvg_sem_s.at[shift - 1], recv_sem=kvg_sem_r.at[shift - 1],
            device_id=(there, section), device_id_type=MESH,
        )

    chunks = [slice(c, c + 64) for c in range(0, GROUP, 64)]
    lane = lax.broadcasted_iota(jnp.int32, (1, 128), 1)
    halves = [(lane < 64).astype(F32).astype(LOW), (lane >= 64).astype(F32).astype(LOW)]
    eighths = [(h.astype(F32) * 0.125).astype(LOW) for h in halves]
    heads = (
        lax.broadcasted_iota(jnp.int32, (HEAD_PAD, width), 1) // 64
        == lax.broadcasted_iota(jnp.int32, (HEAD_PAD, width), 0)
    ).astype(F32)

    def block_diagonal(dst, base, src, row, column, scale):
        for i in range(LAT):
            line = src[row + i : row + i + 1, column : column + width] * scale
            dst[base + i * HEAD_PAD : base + (i + 1) * HEAD_PAD, :] = (line * heads).astype(LOW)

    def head_sum(dst, row, column, value, scale, add):
        for i in range(LAT):
            line = jnp.sum(
                value[i * HEAD_PAD : (i + 1) * HEAD_PAD] * heads, axis=0, keepdims=True
            )
            line = line * scale
            if add:
                line = line + dst[row + i : row + i + 1, column : column + width]
            dst[row + i : row + i + 1, column : column + width] = line

    def bands(body, lo, hi, size):
        def one(i, carry):
            body(pl.ds(pl.multiple_of(lo + i * size, 16), size))
            return carry

        lax.fori_loop(0, (hi - lo) // size, one, 0)

    third = rows // 3

    def grouped(body, lo, hi, count):
        def one(i, carry):
            base = lo + i * 16 * count
            body([pl.ds(pl.multiple_of(base + 16 * g, 16), 16) for g in range(count)])
            return carry

        lax.fori_loop(0, (hi - lo) // (16 * count), one, 0)

    def norm(load, gain, dst, lo, hi, count):
        def body(spans):
            means, scales = row_stats(load, spans)
            for r, mean, scale in zip(spans, means, scales):
                dst[r, :] = ((load(r) - mean) * scale * gain[...]).astype(LOW)

        grouped(body, lo, hi, count)

    def norm_back(load, grad, gain, gain_rows, store, lo, hi, count):
        def body(spans):
            means, scales = row_stats(load, spans)
            firsts, seconds = [], []
            kept = gains[0, gain_rows, :]
            for r, mean, scale in zip(spans, means, scales):
                along = grad[r, :] * ((load(r) - mean) * scale)
                kept = kept + along[0:8] + along[8:16]
                firsts.append(row_mean(grad[r, :] * gain[...]))
                seconds.append(row_mean(along * gain[...]))
            gains[0, gain_rows, :] = kept
            for r, mean, scale, one, two in zip(spans, means, scales, firsts, seconds):
                hat = (load(r) - mean) * scale
                store(r, ef[r, :] + scale * (grad[r, :] * gain[...] - one - hat * two))

        grouped(body, lo, hi, count)

    def tiles(count, body, size=TILE):
        def one(i, carry):
            body(at(i * size, size))
            return carry

        lax.fori_loop(0, count, one, 0)

    @pl.when(first)
    def _():
        for copy in x_loads:
            copy.wait()

    @pl.when(second)
    def _():
        spots = lax.broadcasted_iota(jnp.int32, (n, n * lat), 1) // lat
        spread_out = (spots == lax.broadcasted_iota(jnp.int32, (n, n * lat), 0)).astype(F32)
        groups = nn(slots[...].astype(F32).astype(LOW), spread_out.astype(LOW))
        of_micro = lax.rem(lax.broadcasted_iota(jnp.int32, (1, n * lat), 1), lat) // LAT
        for m in range(half):
            images = jnp.zeros((1, n * lat), F32)
            own_image = jnp.float32(0)
            end = jnp.int32(0)
            for i in range(image_at.shape[1]):
                end = end + image_at[m, i]
                images += jnp.where(end.astype(F32) <= groups[m : m + 1], 1.0, 0.0)
                own_image += jnp.where(end <= slot_at[m, me], 1.0, 0.0)
            seen = (images == own_image) & (of_micro == m)
            key_mask[m : m + 1, :] = jnp.where(seen, 0.0, masked_score)

    def load_in(r):
        return xb[r, :].astype(F32)

    def load_mid(r):
        return mid[r, :]

    def lat_bias(m, shape, axis):
        return jnp.where(
            lax.broadcasted_iota(jnp.int32, shape, axis) // LAT == m, 0.0, masked_score
        ).astype(F32)

    @pl.when(first)
    def _():
        norm(load_in, gain_attn, n1, 0, rows, 11)
        loads[0].wait()

        def project(c):
            proj[:, c] = nn(n1[...], wq[:, c]).astype(LOW)

        tiles(3 * width // TILE, project)
        latf[...] = proj[0:lat, :].astype(F32)

        def one_pair(it, side):
            m, p = it // pairs, lax.rem(it, pairs)
            r = pl.ds(pl.multiple_of(lat + m * GROUP, 16), GROUP)
            q = proj[r, at(p * 128, 128)]
            k = proj[r, at(width + p * 128, 128)]
            v = proj[r, at(2 * width + p * 128, 128)]
            kl = proj[0:lat, at(width + p * 128, 128)]
            vl = proj[0:lat, at(2 * width + p * 128, 128)]
            bias = lat_bias(m, (lat, GROUP), 0)
            total = jnp.zeros((GROUP, 128), F32)
            for e in (0, 1):
                qe = q * eighths[e]
                s = scores.at[2 * side + e]
                s[...] = nt(k, qe)
                sl = nt(kl, qe) + bias
                top = jnp.max(sl, axis=0, keepdims=True)
                for c in chunks:
                    top = jnp.maximum(top, jnp.max(s[c, :], axis=0, keepdims=True))
                el = jnp.exp(sl - top)
                whole_sum = jnp.sum(el, axis=0, keepdims=True)
                for c in chunks:
                    et = jnp.exp(s[c, :] - top)
                    s[c, :] = et
                    whole_sum += jnp.sum(et, axis=0, keepdims=True)
                scale = 1.0 / whole_sum
                for c in chunks:
                    probs[2 * it + e, c, :] = (s[c, :] * scale).astype(LOW)
                pe = (el * scale).astype(LOW)
                probs[2 * it + e, GROUP : GROUP + lat, :] = pe
                total += tn(probs[2 * it + e, 0:GROUP, :], v * halves[e])
                total += tn(pe, vl * halves[e])
            mixed[r, at(p * 128, 128)] = total.astype(LOW)

        def pair(i, carry):
            one_pair(2 * i, 0)
            one_pair(2 * i + 1, 1)
            return carry

        lax.fori_loop(0, half * pairs // 2, pair, 0)
        for m in range(half):
            r = slice(lat + m * GROUP, lat + (m + 1) * GROUP)
            b = slice(m * 128, (m + 1) * 128)
            block_diagonal(qbd, m * 128, latf, m * LAT, 0, 0.125)
            s = nt(qbd[b, :], proj[r, width : 2 * width])
            sl = nt(qbd[b, :], proj[0:lat, width : 2 * width]) + lat_bias(m, (128, lat), 1)
            top = jnp.maximum(
                jnp.max(s, axis=1, keepdims=True), jnp.max(sl, axis=1, keepdims=True)
            )
            et = jnp.exp(s - top)
            el = jnp.exp(sl - top)
            scale = 1.0 / (
                jnp.sum(et, axis=1, keepdims=True) + jnp.sum(el, axis=1, keepdims=True)
            )
            pt = (et * scale).astype(LOW)
            pe = (el * scale).astype(LOW)
            probs_lat[b, 0:GROUP] = pt
            probs_lat[b, GROUP : GROUP + lat] = pe
            o = nn(pt, proj[r, 2 * width :]) + nn(pe, proj[0:lat, 2 * width :])
            head_sum(mixf, m * LAT, 0, o, 1.0, False)
        mixed[0:lat, :] = mixf[...].astype(LOW)

    keys = n * lat

    root = 0.7978845608028654

    def mlp_in(lo, hi, count):
        r0 = slice(lo, hi)
        mid[r0, :] = xb[r0, :].astype(F32) + nn(mixed[r0, :], wo[...])

        norm(load_mid, gain_mlp, n2, lo, hi, count)

        def up_tile(dst, i):
            dst[r0, 0:512] = nn(n2[r0, :], wu[:, at(i * 512, 512)])

        def gelu(src, i):
            c = at(i * 512, 512)
            for g in range(lo, hi, 16):
                r = slice(g, g + 16)
                up = src[r, 0:512]
                square = up * up
                t = jnp.tanh(up * (root + (root * 0.044715) * square))
                gate = 0.5 + 0.5 * t
                value = up * gate
                slope = gate + (value + value) * (1.0 - gate) * (
                    root + (3.0 * root * 0.044715) * square
                )
                act[r, c] = value.astype(LOW)
                dup[r, c] = slope.astype(LOW)

        last = ff // 512 - 1

        def widen(i, carry):
            up_tile(out, 2 * i + 1)
            gelu(tmp, 2 * i)
            up_tile(tmp, jnp.minimum(2 * i + 2, last))
            gelu(out, 2 * i + 1)
            return carry

        up_tile(tmp, 0)
        lax.fori_loop(0, ff // 1024, widen, 0)

    out_copies = [
        pltpu.make_async_copy(out.at[lat:rows], out_tok, load_sem.at[8]),
        pltpu.make_async_copy(out.at[0:lat], out_lat, load_sem.at[9]),
    ]
    grad_copies = [
        pltpu.make_async_copy(out.at[lat:rows], grad_tok, load_sem.at[8]),
        pltpu.make_async_copy(out.at[0:lat], grad_lat, load_sem.at[9]),
    ]

    def layer_output(low, high, passed_on):
        r = slice(low, high)
        y = mid[r, :] + nn(act[r, :], wd[...])
        if passed_on:
            narrow_y = y.astype(LOW)
            yb[r, :] = narrow_y
            y = narrow_y.astype(F32)
        out[r, :] = y

    @pl.when(first)
    def _():
        for copy in loads[1:]:
            copy.wait()
        mlp_in(0, lat + GROUP, 17)
        layer_output(0, lat + GROUP, True)
        relay(0, 0).start()
        relay(0, 1).start()
        mlp_in(lat + GROUP, rows, 16)
        layer_output(lat + GROUP, rows, True)
        relay(0, 2).start()
        for copy in out_copies:
            copy.start()

    @pl.when(second)
    def _():
        for copy in loads:
            copy.wait()
        relay(0, 0).wait_recv()
        norm(load_in, gain_attn, n1, 0, lat, 1)
        lat_proj = nn(n1[0:lat, :], wq[...]).astype(LOW)
        kv_all[me] = lat_proj[:, width:]
        latf[...] = lat_proj.astype(F32)
        for shift in range(1, n):
            kv_copy(shift, False).start()
        for m in range(half):
            relay(0, 1 + m).wait_recv()
            low, high = lat + m * GROUP, lat + (m + 1) * GROUP
            r = slice(low, high)
            b = slice(m * 128, (m + 1) * 128)
            norm(load_in, gain_attn, n1, low, high, 16)
            proj[r, :width] = nn(n1[r, :], wq[:, :width]).astype(LOW)
            block_diagonal(qbd, m * 128, latf, m * LAT, 0, 0.125)
            block_diagonal(kbd, m * 128, latf, m * LAT, width, 1.0)
            block_diagonal(vbd, m * 128, latf, m * LAT, 2 * width, 1.0)
            s = nt(proj[r, :width] * jnp.asarray(0.125, LOW), kbd[b, :])
            et = jnp.exp(s - class_max(s))
            pt = (et / class_sum(et)).astype(LOW)
            probs[m, 0:GROUP, 0:128] = pt
            mixed[r, :] = nn(pt, vbd[b, :]).astype(LOW)
            mlp_in(low, high, 16)
        for shift in range(1, n):
            kv_copy(shift, True).wait_recv()
        k = kv_all[:, :, :width].reshape(keys, width)
        v = kv_all[:, :, width:].reshape(keys, width)
        for m in range(half):
            b = slice(m * 128, (m + 1) * 128)
            s = nt(qbd[b, :], k) + key_mask[m : m + 1, :]
            et = jnp.exp(s - jnp.max(s, axis=1, keepdims=True))
            pt = (et / jnp.sum(et, axis=1, keepdims=True)).astype(LOW)
            probs_lat[b, 0:keys] = pt
            head_sum(mixf, m * LAT, 0, nn(pt, v), 1.0, False)
        mixed[0:lat, :] = mixf[...].astype(LOW)
        mlp_in(0, lat, 1)

    @pl.when(first)
    def _():
        for band in range(3):
            relay(1, band).wait_recv()

        def widen_e(r):
            ef[r, :] = dy[r, :].astype(F32)

        bands(widen_e, 0, rows, third)

    @pl.when(second)
    def _():
        for copy in e_loads:
            copy.wait()

        def narrow_e(r):
            dy[r, :] = ef[r, :].astype(LOW)

        bands(narrow_e, 0, rows, third)

    part = 384
    unit = width // n
    many = part // unit

    def staged(slot, piece, chunk, share):
        return pltpu.make_async_copy(
            stage.at[slot, piece],
            grads.at[
                chunk,
                share // 8,
                lax.rem(share // 4, 2),
                lax.rem(share // 2, 2),
                lax.rem(share, 2),
            ],
            stage_sem.at[slot, piece],
        )

    def drain(slot):
        def one(piece, carry):
            staged(slot, piece, 0, 0).wait()
            return carry

        lax.fori_loop(0, many, one, 0)

    def weight_grad(place, start, count, left, *rights):
        def one(i, carry):
            turned = left(i).T
            for at_right, right in enumerate(rights):
                tile = i * len(rights) + at_right
                slot = lax.rem(tile, 2)
                value = nn(turned, right(i)).astype(LOW)

                @pl.when(tile >= start * len(rights) + 2)
                def _():
                    drain(slot)

                for piece in range(many):
                    stage[slot, piece] = value[piece * unit : (piece + 1) * unit]
                    staged(slot, piece, *place(i, at_right, piece)).start()
            return carry

        lax.fori_loop(start, start + count, one, 0)
        for slot in (0, 1):
            drain(slot)

    orders = ((0, 2, 1, 3), (1, 2, 0, 3), (2, 1, 0, 3))
    own_buf = (own_a, own_b, own_a)
    per_part = width // part
    wide = ff // width
    land = (
        (land1_a, land1_b, land1_c),
        (land2_a, land2_b, land2_c),
        (land3_a, land3_b, land3_c),
        (land4_a, land4_b, land4_c),
    )

    def chunk_of(kind, k):
        if kind == 2:
            return 2 * wide + 3 * k
        return 2 * k + kind + k // wide

    def source(kind, phase, k, theirs):
        pick = [(1 - here[bit]) if theirs else here[bit] for bit in orders[kind]]
        own_bit = [here[bit] for bit in orders[kind]]
        base = land[0][kind]
        if phase == 0:
            chunk = grads.at[chunk_of(kind, k)]
            return (chunk.at[:, :, :, pick[0]], chunk.at[:, :, pick[0]], chunk.at[:, pick[0]])[kind]
        if phase == 1:
            return base.at[k, :, pick[1]]
        if phase == 2:
            return base.at[k, :, own_bit[1], pick[2]]
        return base.at[k, pick[3], own_bit[1], own_bit[2]]

    def copy_of(kind, phase, k):
        return pltpu.make_async_remote_copy(
            src_ref=source(kind, phase, k, True),
            dst_ref=land[phase][kind].at[k],
            send_sem=send_sem.at[kind, phase, k],
            recv_sem=recv_sem.at[kind, phase, k],
            device_id=across(orders[kind][phase]),
            device_id_type=MESH,
        )

    def own(kind, k):
        return pltpu.make_async_copy(
            source(kind, 0, k, False), own_buf[kind], own_sem.at[kind]
        )

    def leave(kind, k):
        slot = lax.rem(k, 2)
        return pltpu.make_async_copy(
            leaving.at[slot, kind], summed.at[chunk_of(kind, k)], leave_sem.at[slot, kind]
        )

    def launch(phase, k, kinds=(0, 1)):
        for kind in kinds:
            copy_of(kind, phase, k).start()

    def onward(phase, k, kinds):
        for kind in kinds:
            if phase == 0:
                own(kind, k).wait()
            copy_of(kind, phase, k).wait_recv()
            base, into = land[0][kind], land[phase][kind]
            mine = [here[bit] for bit in orders[kind]]
            if phase == 0:

                def add(i, carry):
                    for j in (0, 1):
                        for h in (0, 1):
                            total = own_buf[kind][i, j, h].astype(F32)
                            total += base[k, i, j, h].astype(F32)
                            base[k, i, j, h] = total.astype(LOW)
                    return carry

                lax.fori_loop(0, 2, add, 0)
            elif phase == 1:
                for i in (0, 1):
                    for h in (0, 1):
                        total = base[k, i, mine[1], h].astype(F32)
                        total += into[k, i, h].astype(F32)
                        base[k, i, mine[1], h] = total.astype(LOW)
            elif phase == 2:
                for i in (0, 1):
                    total = base[k, i, mine[1], mine[2]].astype(F32)
                    total += into[k, i].astype(F32)
                    base[k, i, mine[1], mine[2]] = total.astype(LOW)
            else:
                total = base[k, mine[3], mine[1], mine[2]].astype(F32)
                total += into[k].astype(F32)
                slot = lax.rem(k, 2)

                @pl.when(k >= 2)
                def _():
                    leave(kind, k - 2).wait()

                leaving[slot, kind] = total
                leave(kind, k).start()
            if phase < 3:
                copy_of(kind, phase + 1, k).start()

    def run(phase, lo, hi, *kinds):
        def one(k, carry):
            if phase == 0:
                for kind in kinds:
                    own(kind, k).start()
            onward(phase, k, kinds)
            return carry

        lax.fori_loop(lo, hi, one, 0)

    def up_grad():
        weight_grad(
            lambda i, right, piece: (
                wide + lax.rem(i * many + piece, wide),
                (i * many + piece) // wide,
            ),
            0,
            ff // part,
            lambda i: dup[:, at(i * part, part)],
            lambda i: n2[...],
        )
        launch(0, 2)
        launch(0, 3)

    def down_grad(pair):
        weight_grad(
            lambda i, right, piece: (2 * pair + right, i * many + piece),
            0,
            per_part,
            lambda i: dy[:, at(i * part, part)],
            lambda i: act[:, 2 * pair * width : (2 * pair + 1) * width],
            lambda i: act[:, (2 * pair + 1) * width : (2 * pair + 2) * width],
        )

    down_grad(0)
    launch(0, 0)
    down_grad(1)
    launch(0, 1)

    def unwiden(c):
        dup[:, c] = (nt(dy[...], wd[c, :]) * dup[:, c].astype(F32)).astype(LOW)

    tiles(ff // TILE, unwiden)
    up_grad()

    def to_mid(c):
        tmp[:, c] = nt(dup[...], wu[c, :])

    tiles(width // 256, to_mid, 256)
    gains[0] = jnp.zeros_like(gains[0])

    def store_mid(r, total):
        ef[r, :] = total
        dy[r, :] = total.astype(LOW)

    norm_back(load_mid, tmp, gain_mlp, slice(8, 16), store_mid, 0, rows, 11)

    @pl.when(first)
    def _():
        for band in range(3):
            relay(0, band).wait_send()

    def to_mix(c):
        yb[:, c] = nt(dy[...], wo[c, :]).astype(LOW)

    tiles(width // TILE, to_mix)
    mixf[...] = yb[0:lat, :].astype(F32)

    @pl.when(second)
    def _():
        k = kv_all[:, :, :width].reshape(keys, width)
        v = kv_all[:, :, width:].reshape(keys, width)
        for m in range(half):
            b = slice(m * 128, (m + 1) * 128)
            block_diagonal(vbd.at[pl.ds(256, 256)], m * 128, mixf, m * LAT, 0, 1.0)
        both = slice(0, half * 128)
        do = vbd[256 : 256 + half * 128, :]
        pt = probs_lat[both, 0:keys]
        pf = pt.astype(F32)
        dp = nt(do, v)
        along = jnp.sum(pf * dp, axis=1, keepdims=True)
        ds = (pf * (dp - along)).astype(LOW)
        kvg_send[:, :, :width] = tn(ds, qbd[both, :]).astype(LOW).reshape(n, lat, width)
        kvg_send[:, :, width:] = tn(pt, do).astype(LOW).reshape(n, lat, width)
        for shift in range(1, n):
            kvg_copy(shift).start()
        dq = nn(ds, k)
        for m in range(half):
            head_sum(latf, m * LAT, 0, dq[m * 128 : (m + 1) * 128], 0.125, False)
        proj[0:lat, :width] = latf[:, :width].astype(LOW)
        layer_output(0, lat + GROUP, False)
        layer_output(lat + GROUP, rows, False)
        for copy in out_copies:
            copy.start()

    weight_grad(
        lambda i, right, piece: (2 * wide, i * many + piece),
        0,
        width // part,
        lambda i: dy[:, at(i * part, part)],
        lambda i: mixed[...],
    )
    launch(0, 0, (2,))
    for copy in out_copies:
        copy.wait()

    @pl.when(first)
    def _():
        for m in range(half):
            r = slice(lat + m * GROUP, lat + (m + 1) * GROUP)
            b = slice(m * 128, (m + 1) * 128)
            block_diagonal(vbd, m * 128, mixf, m * LAT, 0, 1.0)
            do = vbd[b, :]
            dp = nt(do, proj[r, 2 * width :])
            dl = nt(do, proj[0:lat, 2 * width :])
            pt = probs_lat[b, 0:GROUP]
            pe = probs_lat[b, GROUP : GROUP + lat]
            pf = pt.astype(F32)
            pg = pe.astype(F32)
            along = jnp.sum(pf * dp, axis=1, keepdims=True) + jnp.sum(
                pg * dl, axis=1, keepdims=True
            )
            ds = (pf * (dp - along)).astype(LOW)
            dsl = (pg * (dl - along)).astype(LOW)
            dq = nn(ds, proj[r, width : 2 * width]) + nn(dsl, proj[0:lat, width : 2 * width])
            head_sum(latf, m * LAT, 0, dq, 0.125, False)
            tmp[r, :] = tn(ds, qbd[b, :])
            out[r, :] = tn(pt, do)
            if m == 0:
                tmp[0:lat, :] = tn(dsl, qbd[b, :])
                out[0:lat, :] = tn(pe, do)
            else:
                tmp[0:lat, :] += tn(dsl, qbd[b, :])
                out[0:lat, :] += tn(pe, do)
        proj[0:lat, :width] = latf[:, :width].astype(LOW)

        def one_pair(it, side):
            m, p = it // pairs, lax.rem(it, pairs)
            r = pl.ds(pl.multiple_of(lat + m * GROUP, 16), GROUP)
            qc = at(p * 128, 128)
            q = proj[r, qc]
            k = proj[r, at(width + p * 128, 128)]
            v = proj[r, at(2 * width + p * 128, 128)]
            kl = proj[0:lat, at(width + p * 128, 128)]
            vl = proj[0:lat, at(2 * width + p * 128, 128)]
            dx = yb[r, qc]
            dq = jnp.zeros((GROUP, 128), F32)
            dk = tmp[r, qc]
            dv = out[r, qc]
            dkl = tmp[0:lat, qc]
            dvl = out[0:lat, qc]
            for e in (0, 1):
                qe = q * eighths[e]
                de = dx * halves[e]
                s = scores.at[2 * side + e]
                s[...] = nt(v, de)
                dl = nt(vl, de)
                pt = probs[2 * it + e, 0:GROUP, :]
                pe = probs[2 * it + e, GROUP : GROUP + lat, :]
                pg = pe.astype(F32)
                along = jnp.sum(pg * dl, axis=0, keepdims=True)
                for c in chunks:
                    pf = probs[2 * it + e, c, :].astype(F32)
                    along += jnp.sum(pf * s[c, :], axis=0, keepdims=True)
                for c in chunks:
                    pf = probs[2 * it + e, c, :].astype(F32)
                    slopes[2 * side + e, c, :] = (pf * (s[c, :] - along)).astype(LOW)
                ds = slopes[2 * side + e]
                dsl = (pg * (dl - along)).astype(LOW)
                dq += tn(ds, k * halves[e]) + tn(dsl, kl * halves[e])
                dk += nn(ds, qe)
                dkl += nn(dsl, qe)
                dv += nn(pt, de)
                dvl += nn(pe, de)
            proj[r, qc] = (dq * 0.125).astype(LOW)
            proj[r, at(width + p * 128, 128)] = dk.astype(LOW)
            proj[r, at(2 * width + p * 128, 128)] = dv.astype(LOW)
            tmp[0:lat, qc] = dkl
            out[0:lat, qc] = dvl

        def pair(i, carry):
            one_pair(2 * i, 0)
            one_pair(2 * i + 1, 1)
            return carry

        lax.fori_loop(0, half * pairs // 2, pair, 0)
        proj[0:lat, width : 2 * width] = tmp[0:lat, :].astype(LOW)
        proj[0:lat, 2 * width :] = out[0:lat, :].astype(LOW)

    @pl.when(second)
    def _():
        for m in range(half):
            r = slice(lat + m * GROUP, lat + (m + 1) * GROUP)
            b = slice(m * 128, (m + 1) * 128)
            pt = probs[m, 0:GROUP, 0:128]
            pf = pt.astype(F32)
            dx = yb[r, :]
            dp = nt(dx, vbd[b, :])
            ds = (pf * (dp - class_sum(pf * dp))).astype(LOW)
            dk = tn(ds, proj[r, :width])
            dv = tn(pt, dx)
            proj[r, :width] = (nn(ds, kbd[b, :]) * 0.125).astype(LOW)
            head_sum(latf, m * LAT, width, dk, 0.125, False)
            head_sum(latf, m * LAT, 2 * width, dv, 1.0, False)
        total = latf[:, width:] + kvg_send[me].astype(F32)
        for shift in range(1, n):
            kvg_copy(shift).wait_recv()
            total += kvg_recv[shift - 1].astype(F32)
        proj[0:lat, width:] = total.astype(LOW)

    def qkv_grad(start, count, r):
        weight_grad(
            lambda i, right, piece: (
                2 * wide + 1 + lax.rem(i * many + piece, 3),
                (i * many + piece) // 3,
            ),
            start,
            count,
            lambda i: proj[r, at(i * part, part)],
            lambda i: n1[r, :],
        )

    run(0, 0, wide, 0, 1)

    @pl.when(first)
    def _():
        qkv_grad(0, 3 * per_part, slice(0, rows))
        launch(0, wide)
        launch(0, 1, (2,))

    @pl.when(first)
    def _():
        def to_in(c):
            tmp[:, c] = nt(proj[...], wq[c, :])

        tiles(width // 256, to_in, 256)

    @pl.when(second)
    def _():
        tmp[...] = nt(proj[:, :width], wq[:, :width])
        tmp[0:lat, :] += nt(proj[0:lat, width:], wq[:, width:])

    def store_in(r, total):
        low = total.astype(LOW)
        yb[r, :] = low
        out[r, :] = jnp.where(first, total, low.astype(F32))

    for band in range(3):
        norm_back(
            load_in, tmp, gain_attn, slice(0, 8), store_in, band * third, (band + 1) * third, 11
        )

        @pl.when(second)
        def _():
            relay(1, band).start()

    for copy in grad_copies:
        copy.start()

    @pl.when(second)
    def _():
        qkv_grad(0, per_part, slice(0, rows))
        qkv_grad(per_part, 2 * per_part, slice(0, lat))
        launch(0, wide)
        launch(0, 1, (2,))

    def gain_copy(bit):
        return pltpu.make_async_remote_copy(
            src_ref=gains.at[bit],
            dst_ref=land_g.at[bit],
            send_sem=gain_s.at[bit],
            recv_sem=gain_r.at[bit],
            device_id=across(bit),
            device_id_type=MESH,
        )

    def gain_step(bit):
        gain_copy(bit).wait_recv()
        gains[bit + 1] = gains[bit] + land_g[bit]

    gain_copy(0).start()
    run(0, 0, 1, 2)
    run(1, 0, wide, 0, 1)
    gain_step(0)
    gain_copy(1).start()
    run(0, wide, wide + 1, 0, 1)
    run(0, 1, 2, 2)
    gain_step(1)
    gain_copy(2).start()
    run(1, 0, 1, 2)
    run(2, 0, wide, 0, 1)
    gain_step(2)
    gain_copy(3).start()
    run(1, wide, wide + 1, 0, 1)
    run(1, 1, 2, 2)
    run(2, 0, 1, 2)
    run(3, 0, wide, 0, 1)
    run(2, wide, wide + 1, 0, 1)
    run(2, 1, 2, 2)
    gain_step(3)
    run(3, 0, 1, 2)
    run(3, wide, wide + 1, 0, 1)
    run(3, 1, 2, 2)
    final = gains[4]
    for i in (0, 1):
        whole_gain = jnp.sum(final[8 * i : 8 * i + 8], axis=0, keepdims=True)
        whole_gain = jnp.broadcast_to(whole_gain, (8, width))
        rolled = pltpu.roll(whole_gain, lax.rem(width - me * unit, width), 1)
        gain_sums[8 * i : 8 * i + 8, :] = rolled[:, 0:128]

    def finish(kind):
        def one(k, carry):
            for phase in range(4):
                copy_of(kind, phase, k).wait_send()
            return carry

        lax.fori_loop(0, land[0][kind].shape[0], one, 0)

    for kind in range(3):
        finish(kind)
    for bit in range(4):
        gain_copy(bit).wait_send()
    for copy in grad_copies:
        copy.wait()
    for kind in range(3):
        count = land[0][kind].shape[0]
        for k in (count - 2, count - 1):
            leave(kind, k).wait()

    @pl.when(second)
    def _():
        for band in range(3):
            relay(1, band).wait_send()
        for shift in range(1, n):
            kv_copy(shift, False).wait_send()
            kvg_copy(shift).wait_send()


def both_layers(n, tokens, latents, slots, images, gains, weights, d_tokens, d_latents):
    tok, width = tokens.shape
    lat = latents.shape[0]
    rows = tok + lat
    w_qkv, w_out, w_up, w_down = weights
    ff = w_up.shape[1]
    keys = n * lat
    half = lat // LAT
    size = sum(w.size for w in weights)
    chunks = size // (width * width)
    most = chunks // 2 - 1
    unit = width // n
    vm, hbm = pl.BlockSpec(memory_space=pltpu.VMEM), pl.BlockSpec(memory_space=pl.ANY)
    sm = pl.BlockSpec(memory_space=pltpu.SMEM)
    scratch = [
        pltpu.VMEM(w.shape, LOW) for w in (w_qkv, w_out, w_up, w_down)
    ] + [
        pltpu.VMEM(shape, dtype)
        for shape, dtype in (
            ((rows, width), LOW),
            ((rows, width), LOW),
            ((rows, 3 * width), LOW),
            ((rows, width), LOW),
            ((rows, width), F32),
            ((rows, width), LOW),
            ((rows, ff), LOW),
            ((rows, ff), LOW),
            ((rows, width), LOW),
            ((rows, width), LOW),
            ((rows, width), F32),
            ((rows, width), F32),
            ((rows, width), F32),
            ((half * width // 64, GROUP + lat, GROUP), LOW),
            ((half * 128, max(keys, GROUP + 128)), LOW),
            ((4, GROUP, GROUP), F32),
            ((4, GROUP, GROUP), LOW),
            ((lat, 3 * width), F32),
            ((lat, width), F32),
            ((8, keys), F32),
            ((half * 128, width), LOW),
            ((half * 128, width), LOW),
            ((half * 256, width), LOW),
            ((n, lat, 2 * width), LOW),
            ((n, lat, 2 * width), LOW),
            ((n - 1, lat, 2 * width), LOW),
            ((2, 384 // unit, unit, width), LOW),
            ((5, 16, width), F32),
            ((2, 3, unit, width), F32),
            ((2, 2, 2, unit, width), LOW),
            ((2, 2, 2, unit, width), LOW),
            *(
                ((count, *shape, unit, width), LOW)
                for shape in ((2, 2, 2), (2, 2), (2,), ())
                for count in (most,) * 2 + (2,)
            ),
            ((4, 16, width), F32),
        )
    ] + [
        pltpu.SemaphoreType.DMA((10,)),
        pltpu.SemaphoreType.DMA((2, 384 // unit)),
        pltpu.SemaphoreType.DMA((3,)),
        pltpu.SemaphoreType.DMA((2, 3)),
        pltpu.SemaphoreType.DMA((3, 4, most)),
        pltpu.SemaphoreType.DMA((3, 4, most)),
        pltpu.SemaphoreType.DMA((4,)),
        pltpu.SemaphoreType.DMA((4,)),
        pltpu.SemaphoreType.DMA((6,)),
        pltpu.SemaphoreType.DMA((6,)),
        pltpu.SemaphoreType.DMA((n - 1,)),
        pltpu.SemaphoreType.DMA((n - 1,)),
        pltpu.SemaphoreType.DMA((n - 1,)),
        pltpu.SemaphoreType.DMA((n - 1,)),
    ]
    return pl.pallas_call(
        functools.partial(layer_kernel, n),
        out_shape=(
            jax.ShapeDtypeStruct((tok, width), F32),
            jax.ShapeDtypeStruct((lat, width), F32),
            jax.ShapeDtypeStruct((tok, width), F32),
            jax.ShapeDtypeStruct((lat, width), F32),
            jax.ShapeDtypeStruct((chunks, 2, 2, 2, 2, unit, width), LOW),
            jax.ShapeDtypeStruct((chunks, unit, width), F32),
            jax.ShapeDtypeStruct((16, 128), F32),
        ),
        in_specs=[hbm, hbm, vm, sm, sm, vm, vm] + [hbm] * 6,
        out_specs=(hbm,) * 6 + (vm,),
        scratch_shapes=scratch,
        compiler_params=pltpu.CompilerParams(
            collective_id=1, has_side_effects=True, vmem_limit_bytes=63 * 1024 * 1024
        ),
        cost_estimate=pl.CostEstimate(
            flops=6 * rows * size, bytes_accessed=4 * size, transcendentals=0
        ),
    )(tokens, latents, slots, slots, images, *gains, *weights, d_tokens, d_latents)


def finish_kernel(width, *refs):
    rows_in, (summed, gains), rows_out = refs[0:4], refs[4:6], refs[6:10]
    gain_attn, g_qkv, g_out, gain_mlp, g_up, g_down = refs[10:16]
    held, (sem_in, sem_out) = refs[16:21], refs[21:23]
    wide = g_down.shape[1] // width
    unit = g_out.shape[1]
    loads = [
        pltpu.make_async_copy(src, dst, sem_in.at[i])
        for i, (src, dst) in enumerate(zip((*rows_in, summed), held))
    ]
    for load in loads:
        load.start()
    all_rows, sums = held[0:4], held[4]
    moves = [[pair] for pair in zip(all_rows, rows_out)] + [
        [(sums.at[c], g_down.at[:, c * width : (c + 1) * width]) for c in range(wide)]
        + [
            (sums.at[wide : 2 * wide], g_up),
            (sums.at[2 * wide : 2 * wide + 1], g_out),
            (sums.at[2 * wide + 1 :], g_qkv),
        ]
    ]
    gain_attn[...] = gains[0:1, 0:unit]
    gain_mlp[...] = gains[8:9, 0:unit]
    started = []
    for load, group in zip(loads, moves):
        load.wait()
        for src, dst in group:
            started.append(pltpu.make_async_copy(src, dst, sem_out.at[len(started)]))
            started[-1].start()
    for move in started:
        move.wait()


def finished(rows, summed, gains, wide):
    chunks, unit, width = summed.shape
    hbm, vm = pl.BlockSpec(memory_space=pl.ANY), pl.BlockSpec(memory_space=pltpu.VMEM)
    shapes = [r.shape for r in rows] + [
        (1, unit),
        (3, unit, width),
        (1, unit, width),
        (1, unit),
        (wide, unit, width),
        (unit, wide * width),
    ]
    return pl.pallas_call(
        functools.partial(finish_kernel, width),
        out_shape=tuple(jax.ShapeDtypeStruct(s, F32) for s in shapes),
        in_specs=[hbm] * 5 + [vm],
        out_specs=(hbm,) * 4 + (vm, hbm, hbm, vm, hbm, hbm),
        scratch_shapes=[pltpu.VMEM(x.shape, F32) for x in (*rows, summed)]
        + [pltpu.SemaphoreType.DMA((5,)), pltpu.SemaphoreType.DMA((7 + wide,))],
        compiler_params=pltpu.CompilerParams(vmem_limit_bytes=62 * 1024 * 1024),
    )(*rows, summed, gains)
def fused_shards(
    unused_grid,
    tokens,
    latents,
    slot_group,
    image_groups,
    gain_attn,
    w_qkv,
    w_out,
    gain_mlp,
    w_up,
    w_down,
    d_tokens,
    d_latents,
):
    micro, tok, width = tokens.shape
    lat = latents.shape[1]
    out_tok, out_lat, grad_tok, grad_lat, unused_grads, summed, gains = both_layers(
        slot_group.shape[1],
        tokens.reshape(micro * tok, width),
        latents.reshape(micro * lat, width),
        slot_group,
        image_groups,
        (gain_attn, gain_mlp),
        (w_qkv[0], w_out[0], w_up[0], w_down[0]),
        d_tokens.reshape(micro * tok, width),
        d_latents.reshape(micro * lat, width),
    )
    wide = w_up.shape[2] // width
    rows = (out_tok, out_lat, grad_tok, grad_lat)
    *rows, first_gain, qkv, out, second_gain, up, down = finished(rows, summed, gains, wide)
    return (
        rows[0].reshape(1, micro, tok, width),
        rows[1].reshape(1, micro, lat, width),
        rows[2].reshape(1, micro, tok, width),
        rows[3].reshape(1, micro, lat, width),
        first_gain,
        qkv.reshape(-1, width).T[None],
        out.reshape(-1, width).T[None],
        second_gain,
        up.reshape(-1, width).T[None],
        down.T[None],
    )

def solution(mesh):
    in_specs = (
        P(None, "dp", None),
        P(None, "dp", None),
        P(),
        P(),
        P("section", None),
        P("section", None, None),
        P("section", None, None),
        P("section", None),
        P("section", None, None),
        P("section", None, None),
        P(None, "dp", None),
        P(None, "dp", None),
    )
    out_specs = (
        P("section", None, "dp", None),
        P("section", None, "dp", None),
        P("section", None, "dp", None),
        P("section", None, "dp", None),
        P("section", "dp"),
        P("section", None, "dp"),
        P("section", None, "dp"),
        P("section", "dp"),
        P("section", None, "dp"),
        P("section", None, "dp"),
    )
    grid = grid_of(mesh)

    def program(*args):
        n, width = mesh.shape["dp"], args[0].shape[2]
        one_group = args[0].shape[1] == n * GROUP
        body = fused_shards if one_group and n == 16 and width % (16 * n) == 0 else shards
        return jax.shard_map(
            functools.partial(body, grid), mesh=mesh, in_specs=in_specs, out_specs=out_specs, check_vma=False
        )(*args)

    return program
```

```python
import functools

import jax
import jax.numpy as jnp
from jax import lax
from jax.experimental import pallas as pl
from jax.experimental.pallas import tpu as pltpu
from jax.sharding import PartitionSpec as P

HEADS = 12
GROUP = 256
LAT = 8


epsilon = 1e-05
masked_score = -1e30


MESH = pl.DeviceIdType.MESH


def grid_of(mesh):
    n = mesh.shape["dp"]
    coords = [getattr(d, "coords", None) for d in mesh.devices.reshape(n, -1)[:, 0]]
    if any(c is None for c in coords):
        return (n // 4, 2, 2) if n % 4 == 0 else (n, 1, 1)
    sizes = {a: len({c[a] for c in coords}) for a in range(3)}
    strides = {
        a: min([i for i in range(n) if coords[i][a] != coords[0][a]], default=n) for a in range(3)
    }
    order = sorted(range(3), key=lambda a: -strides[a])
    return tuple(sizes[a] for a in order)


def spread_kernel(grid, pairs, g_ref, gain_ref, out_ref, gout_ref, *scratch):
    acc = scratch[0:3]
    land = [scratch[3 + 3 * i : 6 + 3 * i] for i in range(3)]
    send_sem, recv_sem, own_sem = scratch[12:15]
    me = lax.axis_index("dp")
    section = lax.axis_index("section")
    l0, l1, l2 = grid
    here = (me // (l1 * l2), lax.rem(me // l2, l1), lax.rem(me, l2))

    def device(axis, shift):
        there = list(here)
        there[axis] = lax.rem(here[axis] + shift, grid[axis])
        return there[axis], ((there[0] * l1 + there[1]) * l2 + there[2], section)

    barrier = pltpu.get_barrier_semaphore()
    for axis in range(3):
        for shift in range(1, grid[axis]):
            pl.semaphore_signal(
                barrier, inc=1, device_id=device(axis, shift)[1], device_id_type=MESH
            )
    pl.semaphore_wait(barrier, sum(grid) - 3)

    orders = ((2, 1, 0), (1, 2, 0), (2, 1, 0))

    def source(stream, phase, k, at):
        if phase == 0:
            if stream == 0:
                return g_ref.at[2 * k, :, :, at]
            if stream == 1:
                return g_ref.at[2 * k + 1, :, at]
            return gain_ref.at[:, :, at]
        if phase == 1:
            return acc[stream].at[k, :, at]
        return acc[stream].at[k, at, here[orders[stream][1]]]

    def copies(stream, phase, k):
        axis = orders[stream][phase]
        for shift in range(1, grid[axis]):
            at, target = device(axis, shift)
            yield pltpu.make_async_remote_copy(
                src_ref=source(stream, phase, k, at),
                dst_ref=land[phase][stream].at[k, shift - 1],
                send_sem=send_sem.at[stream, phase, k, shift - 1],
                recv_sem=recv_sem.at[stream, phase, k, shift - 1],
                device_id=target,
                device_id_type=MESH,
            )

    def own(stream, k):
        return pltpu.make_async_copy(
            source(stream, 0, k, here[orders[stream][0]]), acc[stream].at[k], own_sem.at[stream, k]
        )

    def launch(stream, phase, k):
        for copy in copies(stream, phase, k):
            copy.start()

    def absorb(stream, phase, k):
        axis = orders[stream][phase]
        if phase == 0:
            own(stream, k).wait()
        for copy in copies(stream, phase, k):
            copy.wait_recv()
        into = land[phase][stream]
        count = grid[axis] - 1
        if phase == 0:
            for a in range(acc[stream].shape[1]):
                for b in range(acc[stream].shape[2]):
                    total = acc[stream][k, a, b].astype(jnp.float32)
                    for s in range(count):
                        total += into[k, s, a, b].astype(jnp.float32)
                    acc[stream][k, a, b] = total.astype(acc[stream].dtype)
        elif phase == 1:
            mine = here[axis]
            for a in range(acc[stream].shape[1]):
                total = acc[stream][k, a, mine].astype(jnp.float32)
                for s in range(count):
                    total += into[k, s, a].astype(jnp.float32)
                acc[stream][k, a, mine] = total.astype(acc[stream].dtype)
        else:
            total = acc[stream][k, here[0], here[orders[stream][1]]].astype(jnp.float32)
            for s in range(count):
                total += into[k, s].astype(jnp.float32)
            if stream < 2:
                out_ref[2 * k + stream] = total
            else:
                gout_ref[...] = total

    own(2, 0).start()
    launch(2, 0, 0)

    def start_own(k, carry):
        for stream in (0, 1):
            own(stream, k).start()
        return carry

    for stream in (0, 1):
        launch(stream, 0, 0)
    lax.fori_loop(0, pairs, start_own, 0)

    def turn(t, carry):
        @pl.when(t + 1 < pairs)
        def _():
            for stream in (0, 1):
                launch(stream, 0, t + 1)

        @pl.when(t < pairs)
        def _():
            for stream in (0, 1):
                absorb(stream, 0, t)
                launch(stream, 1, t)

        @pl.when((t >= 1) & (t - 1 < pairs))
        def _():
            for stream in (0, 1):
                absorb(stream, 1, t - 1)
                launch(stream, 2, t - 1)

        @pl.when(t >= 2)
        def _():
            for stream in (0, 1):
                absorb(stream, 2, t - 2)

        return carry

    lax.fori_loop(0, pairs + 2, turn, 0)
    absorb(2, 0, 0)
    launch(2, 1, 0)
    absorb(2, 1, 0)
    launch(2, 2, 0)
    absorb(2, 2, 0)

    def finish(k, carry):
        for stream in (0, 1):
            for phase in range(3):
                for copy in copies(stream, phase, k):
                    copy.wait_send()
        return carry

    lax.fori_loop(0, pairs, finish, 0)
    for phase in range(3):
        for copy in copies(2, phase, 0):
            copy.wait_send()


def spread(grid, grads, gains):
    chunks, n, rows, width = grads.shape
    pairs = chunks // 2
    l0, l1, l2 = grid
    most = max(max(grid) - 1, 1)
    low = jnp.bfloat16
    shapes = ((pairs, rows, width, low), (pairs, rows, width, low), (1, 8, 128, jnp.float32))
    inner = ((l1, l2), (l2, l1), (l1, l2))
    acc, first, second, third = [], [], [], []
    for (count, r, w, dt), (kept, sent) in zip(shapes, inner):
        acc.append(pltpu.VMEM((count, l0, kept, r, w), dt))
        first.append(pltpu.VMEM((count, max(sent - 1, 1), l0, kept, r, w), dt))
        second.append(pltpu.VMEM((count, max(kept - 1, 1), l0, r, w), dt))
        third.append(pltpu.VMEM((count, max(l0 - 1, 1), r, w), dt))
    return pl.pallas_call(
        functools.partial(spread_kernel, grid, pairs),
        out_shape=(
            jax.ShapeDtypeStruct((chunks, rows, width), jnp.float32),
            jax.ShapeDtypeStruct((8, 128), jnp.float32),
        ),
        in_specs=[pl.BlockSpec(memory_space=pl.ANY)] * 2,
        out_specs=(pl.BlockSpec(memory_space=pltpu.VMEM),) * 2,
        scratch_shapes=acc
        + first
        + second
        + third
        + [
            pltpu.SemaphoreType.DMA((3, 3, pairs, most)),
            pltpu.SemaphoreType.DMA((3, 3, pairs, most)),
            pltpu.SemaphoreType.DMA((3, pairs)),
        ],
        compiler_params=pltpu.CompilerParams(
            collective_id=0, has_side_effects=True, vmem_limit_bytes=60 * 1024 * 1024
        ),
        cost_estimate=pl.CostEstimate(flops=0, bytes_accessed=grads.size * 4, transcendentals=0),
    )(grads.reshape(chunks, l0, l1, l2, rows, width), gains.reshape(l0, l1, l2, 8, 128))


def from_behind(x, axis, by):
    devices = lax.axis_size(axis)
    pairs = [(i, i + by) for i in range(devices) if 0 <= i + by < devices]
    return lax.ppermute(x, axis, pairs)


def layer_norm(values, gain):
    row_mean = jnp.mean(values, axis=-1, keepdims=True)
    centred = values - row_mean
    row_var = jnp.mean(centred * centred, axis=-1, keepdims=True)
    return centred * lax.rsqrt(row_var + epsilon) * gain


def front_half(all_rows, gain_attn, w_qkv):
    normed = layer_norm(all_rows, gain_attn).astype(jnp.bfloat16)
    projected = jnp.dot(normed, w_qkv, preferred_element_type=jnp.float32).astype(jnp.bfloat16)
    return (normed, projected)


def latent_operand(projected, tok_rows, model_width):
    return projected[tok_rows:, model_width:]


def back_half(all_rows, projected, remote_rows, allowed, weights):
    gain_attn, w_qkv, w_out, gain_mlp, w_up, w_down = weights
    row_count, model_width = all_rows.shape
    head_size = model_width // HEADS
    remote_pairs = remote_rows[:, remote_rows.shape[1] - 2 * model_width :]
    queries = projected[:, :model_width].reshape(row_count, HEADS, head_size)
    key_rows = jnp.concatenate(
        [projected[:, model_width : 2 * model_width], remote_pairs[:, :model_width]], axis=0
    )
    value_rows = jnp.concatenate(
        [projected[:, 2 * model_width :], remote_pairs[:, model_width:]], axis=0
    )
    key_rows = key_rows.reshape(-1, HEADS, head_size)
    value_rows = value_rows.reshape(-1, HEADS, head_size)
    scores = jnp.einsum(
        "qhd,khd->hqk", queries, key_rows, preferred_element_type=jnp.float32
    ) * head_size ** (-0.5)
    attn_weights = jax.nn.softmax(jnp.where(allowed[None], scores, masked_score), axis=-1)
    attn_low = attn_weights.astype(jnp.bfloat16)
    mixed_low = jnp.einsum("hqk,khd->qhd", attn_low, value_rows, preferred_element_type=jnp.float32)
    mixed_low = mixed_low.reshape(row_count, model_width).astype(jnp.bfloat16)
    mid_rows = all_rows + jnp.dot(mixed_low, w_out, preferred_element_type=jnp.float32)
    normed_mlp = layer_norm(mid_rows, gain_mlp).astype(jnp.bfloat16)
    up_proj = jnp.dot(normed_mlp, w_up, preferred_element_type=jnp.float32)
    activated = jax.nn.gelu(up_proj).astype(jnp.bfloat16)
    result = mid_rows + jnp.dot(activated, w_down, preferred_element_type=jnp.float32)
    return dict(
        queries=queries,
        key_rows=key_rows,
        value_rows=value_rows,
        attn_weights=attn_weights,
        attn_low=attn_low,
        mixed_low=mixed_low,
        mid_rows=mid_rows,
        normed_mlp=normed_mlp,
        up_proj=up_proj,
        activated=activated,
        result=result,
    )


def section_backward(saved, d_result, all_rows, normed, allowed, weights, latent_start):
    gain_attn, w_qkv, w_out, gain_mlp, w_up, w_down = weights
    row_count, model_width = all_rows.shape
    head_size = model_width // HEADS
    score_scale = head_size ** (-0.5)
    d_low = d_result.astype(jnp.bfloat16)
    grad_down = jnp.dot(d_low.T, saved["activated"], preferred_element_type=jnp.float32)
    d_activated = jnp.dot(d_low, w_down.T, preferred_element_type=jnp.float32)
    unused_up, gelu_back = jax.vjp(jax.nn.gelu, saved["up_proj"])
    d_up = gelu_back(d_activated)[0].astype(jnp.bfloat16)
    grad_up = jnp.dot(d_up.T, saved["normed_mlp"], preferred_element_type=jnp.float32)
    d_normed_mlp = jnp.dot(d_up, w_up.T, preferred_element_type=jnp.float32)
    unused_mid, second_back = jax.vjp(layer_norm, saved["mid_rows"], gain_mlp)
    d_mid_norm, grad_gain_mlp = second_back(d_normed_mlp)
    d_mid = d_result + d_mid_norm
    d_mid_low = d_mid.astype(jnp.bfloat16)
    grad_out = jnp.dot(d_mid_low.T, saved["mixed_low"], preferred_element_type=jnp.float32)
    d_mixed = jnp.dot(d_mid_low, w_out.T, preferred_element_type=jnp.float32).astype(jnp.bfloat16)
    d_mixed = d_mixed.reshape(row_count, HEADS, head_size)
    d_weights = jnp.einsum(
        "qhd,khd->hqk", d_mixed, saved["value_rows"], preferred_element_type=jnp.float32
    )
    d_values = jnp.einsum(
        "hqk,qhd->khd", saved["attn_low"], d_mixed, preferred_element_type=jnp.float32
    )
    attn_weights = saved["attn_weights"]
    d_scores = attn_weights * (
        d_weights - jnp.sum(attn_weights * d_weights, axis=-1, keepdims=True)
    )
    d_scores_low = jnp.where(allowed[None], d_scores, 0.0).astype(jnp.bfloat16)
    d_queries = (
        jnp.einsum(
            "hqk,khd->qhd", d_scores_low, saved["key_rows"], preferred_element_type=jnp.float32
        )
        * score_scale
    )
    d_keys = (
        jnp.einsum(
            "hqk,qhd->khd", d_scores_low, saved["queries"], preferred_element_type=jnp.float32
        )
        * score_scale
    )
    remote_part = jnp.concatenate(
        [
            d_keys[row_count:].reshape(-1, model_width),
            d_values[row_count:].reshape(-1, model_width),
        ],
        axis=1,
    )
    own_part = lax.psum_scatter(remote_part, "dp", scatter_dimension=0, tiled=True)
    local_pairs = jnp.concatenate(
        [
            d_keys[:row_count].reshape(row_count, model_width),
            d_values[:row_count].reshape(row_count, model_width),
        ],
        axis=1,
    )
    local_pairs = jnp.concatenate(
        [local_pairs[:latent_start], local_pairs[latent_start:] + own_part], axis=0
    )
    d_projected = jnp.concatenate(
        [d_queries.reshape(row_count, model_width), local_pairs], axis=1
    ).astype(jnp.bfloat16)
    grad_qkv = jnp.dot(d_projected.T, normed, preferred_element_type=jnp.float32)
    d_normed = jnp.dot(d_projected, w_qkv.T, preferred_element_type=jnp.float32)
    unused_rows, first_back = jax.vjp(layer_norm, all_rows, gain_attn)
    d_rows_norm, grad_gain_attn = first_back(d_normed)
    return (
        d_mid + d_rows_norm,
        (grad_gain_attn, grad_qkv, grad_out, grad_gain_mlp, grad_up, grad_down),
    )


def packed(grads, n):
    gain_first, qkv_grad, out_grad, gain_second, up_grad, down_grad = grads
    width = out_grad.shape[0]
    rows = width // n

    def by_rows(grad):
        return grad.reshape(n, -1, rows, width).transpose(1, 0, 2, 3).astype(jnp.bfloat16)

    down = down_grad.reshape(n, rows, -1, width).transpose(2, 0, 1, 3).astype(jnp.bfloat16)
    chunks = jnp.concatenate([down, by_rows(up_grad), by_rows(out_grad), by_rows(qkv_grad)], axis=0)
    gains = jnp.stack([gain_first.reshape(n, rows), gain_second.reshape(n, rows)], axis=1)
    return chunks, jnp.pad(gains, ((0, 0), (0, 6), (0, 128 - rows)))


def shards(
    grid,
    tokens,
    latents,
    slot_group,
    image_groups,
    gain_attn,
    w_qkv,
    w_out,
    gain_mlp,
    w_up,
    w_down,
    d_tokens,
    d_latents,
):
    micro = tokens.shape[0]
    tok_rows = tokens.shape[1]
    lat_rows = latents.shape[1]
    model_width = tokens.shape[2]
    local_groups = tok_rows // GROUP
    section_index = lax.axis_index("section")
    is_global = section_index == 1
    dp_index = lax.axis_index("dp")
    weights = (gain_attn[0], w_qkv[0], w_out[0], gain_mlp[0], w_up[0], w_down[0])
    image_ends = jnp.cumsum(image_groups, axis=1)
    slot_images = jnp.sum(
        (image_ends[:, None, :] <= slot_group[:, :, None]).astype(jnp.int32), axis=2
    )
    slot_total = slot_group.shape[1]
    row_group = jnp.concatenate([jnp.arange(tok_rows) // GROUP, jnp.arange(lat_rows) // LAT])
    row_latent = jnp.concatenate(
        [jnp.zeros((tok_rows,), jnp.bool_), jnp.ones((lat_rows,), jnp.bool_)]
    )
    same_group = row_group[:, None] == row_group[None, :]
    local_mask = jnp.where(
        is_global, (~row_latent)[:, None] & row_latent[None, :] & same_group, same_group
    )
    group_match = row_group[:, None] == jnp.arange(local_groups)[None, :]

    def key_images(batch):
        images_row = lax.dynamic_index_in_dim(slot_images, batch, 0, keepdims=False)
        return (images_row, jnp.broadcast_to(images_row[:, None], (slot_total, LAT)).reshape(-1))

    def allowed_for(batch):
        images_row, key_image = key_images(batch)
        own_images = lax.dynamic_slice_in_dim(images_row, dp_index * local_groups, local_groups)
        row_image = jnp.sum(jnp.where(group_match, own_images[None, :], 0), axis=1)
        remote_mask = is_global & row_latent[:, None] & (row_image[:, None] == key_image[None, :])
        return jnp.concatenate([local_mask, remote_mask], axis=1)

    def forward_turn(received, turn):
        recv_tokens, recv_latents = received
        batch = jnp.clip(turn - section_index, 0, micro - 1)
        own_tok = lax.dynamic_index_in_dim(tokens, batch, 0, keepdims=False)
        own_lat = lax.dynamic_index_in_dim(latents, batch, 0, keepdims=False)
        input_rows = jnp.concatenate(
            [
                jnp.where(is_global, recv_tokens, own_tok),
                jnp.where(is_global, recv_latents, own_lat),
            ],
            axis=0,
        )
        all_rows = input_rows.astype(jnp.float32)
        normed, projected = front_half(all_rows, weights[0], weights[1])
        remote_rows = lax.all_gather(
            latent_operand(projected, tok_rows, model_width), "dp", axis=0, tiled=True
        )
        saved = back_half(all_rows, projected, remote_rows, allowed_for(batch), weights)
        result = saved["result"]
        result_low = result.astype(jnp.bfloat16)
        stored = jnp.where(is_global, result, result_low.astype(jnp.float32))
        passed_on = from_behind((result_low[:tok_rows], result_low[tok_rows:]), "section", 1)
        return passed_on, (input_rows, stored[:tok_rows], stored[tok_rows:])

    nothing = (
        jnp.zeros((tok_rows, model_width), jnp.bfloat16),
        jnp.zeros((lat_rows, model_width), jnp.bfloat16),
    )
    turns = jnp.arange(micro + 1)
    unused_end, (kept_rows, tok_outputs, lat_outputs) = lax.scan(forward_turn, nothing, turns)

    def backward_turn(carry, turn):
        (recv_grad_tok, recv_grad_lat), totals = carry
        raw_batch = micro - turn - section_index
        valid = ((raw_batch >= 0) & (raw_batch < micro)).astype(jnp.float32)
        batch = jnp.clip(raw_batch, 0, micro - 1)
        all_rows = lax.dynamic_index_in_dim(
            kept_rows, batch + section_index, 0, keepdims=False
        ).astype(jnp.float32)
        normed, projected = front_half(all_rows, weights[0], weights[1])
        remote_rows = lax.all_gather(
            latent_operand(projected, tok_rows, model_width), "dp", axis=0, tiled=True
        )
        allowed = allowed_for(batch)
        saved = back_half(all_rows, projected, remote_rows, allowed, weights)
        given = (
            jnp.concatenate(
                [
                    lax.dynamic_index_in_dim(d_tokens, batch, 0, keepdims=False),
                    lax.dynamic_index_in_dim(d_latents, batch, 0, keepdims=False),
                ],
                axis=0,
            )
            * valid
        )
        passed = jnp.concatenate([recv_grad_tok, recv_grad_lat], axis=0).astype(jnp.float32)
        d_result = jnp.where(is_global, given, passed)
        d_rows, grads = section_backward(
            saved, d_result, all_rows, normed, allowed, weights, tok_rows
        )
        totals = tuple((accum + piece for accum, piece in zip(totals, grads)))
        d_rows_low = d_rows.astype(jnp.bfloat16)
        stored = jnp.where(is_global, d_rows_low.astype(jnp.float32), d_rows)
        sent = from_behind((d_rows_low[:tok_rows], d_rows_low[tok_rows:]), "section", -1)
        return (sent, totals), (stored[:tok_rows], stored[tok_rows:])

    totals = tuple(
        jnp.zeros(w.shape[::-1] if w.ndim == 2 else w.shape, jnp.float32) for w in weights
    )
    (unused_sent, totals), (tok_grads, lat_grads) = lax.scan(
        backward_turn, (nothing, totals), turns
    )
    chunks, gains = packed(totals, lax.axis_size("dp"))
    summed, gain_sums = spread(grid, chunks, gains)
    rows = summed.shape[1]
    layer_tokens = lax.dynamic_slice_in_dim(tok_outputs, section_index, micro, 0)[None]
    layer_latents = lax.dynamic_slice_in_dim(lat_outputs, section_index, micro, 0)[None]
    grad_tokens = lax.dynamic_slice_in_dim(tok_grads, 1 - section_index, micro, 0)[::-1][
        None
    ]
    grad_latents = lax.dynamic_slice_in_dim(lat_grads, 1 - section_index, micro, 0)[
        ::-1
    ][None]
    return (
        layer_tokens,
        layer_latents,
        grad_tokens,
        grad_latents,
        gain_sums[0:1, :rows],
        summed[9:].reshape(-1, model_width).T[None],
        summed[8].T[None],
        gain_sums[1:2, :rows],
        summed[4:8].reshape(-1, model_width).T[None],
        summed[0:4].transpose(0, 2, 1).reshape(-1, rows)[None],
    )


F32 = jnp.float32
LOW = jnp.bfloat16
HEAD_PAD = 16
TILE = 768


def nn(a, b):
    return jnp.dot(a, b, preferred_element_type=F32)


def nt(a, b):
    return lax.dot_general(a, b, (((1,), (1,)), ((), ())), preferred_element_type=F32)


def tn(a, b):
    return lax.dot_general(a, b, (((0,), (0,)), ((), ())), preferred_element_type=F32)


def row_mean(values):
    return jnp.mean(values, axis=-1, keepdims=True)


def row_stats(load, spans):
    means = [row_mean(load(r)) for r in spans]
    scales = []
    for r, mean in zip(spans, means):
        centred = load(r) - mean
        scales.append(lax.rsqrt(row_mean(centred * centred) + epsilon))
    return means, scales


def at(start, size):
    return pl.ds(pl.multiple_of(start, size), size)


def class_max(s):
    for by in (16, 32, 64):
        s = jnp.maximum(s, pltpu.roll(s, by, 1))
    return s


def class_sum(s):
    for by in (16, 32, 64):
        s = s + pltpu.roll(s, by, 1)
    return s


def layer_kernel(
    n,
    tokens,
    latents,
    slots,
    slot_at,
    image_at,
    gain_attn,
    gain_mlp,
    w_qkv,
    w_out,
    w_up,
    w_down,
    d_tokens,
    d_latents,
    out_tok,
    out_lat,
    grad_tok,
    grad_lat,
    grads,
    summed,
    gain_sums,
    wq,
    wo,
    wu,
    wd,
    xb,
    n1,
    proj,
    mixed,
    mid,
    n2,
    act,
    dup,
    yb,
    dy,
    ef,
    tmp,
    out,
    probs,
    probs_lat,
    scores,
    slopes,
    latf,
    mixf,
    key_mask,
    qbd,
    kbd,
    vbd,
    kv_all,
    kvg_send,
    kvg_recv,
    stage,
    gains,
    leaving,
    own_a,
    own_b,
    land1_a,
    land1_b,
    land1_c,
    land2_a,
    land2_b,
    land2_c,
    land3_a,
    land3_b,
    land3_c,
    land4_a,
    land4_b,
    land4_c,
    land_g,
    load_sem,
    stage_sem,
    own_sem,
    leave_sem,
    send_sem,
    recv_sem,
    gain_s,
    gain_r,
    relay_send,
    relay_recv,
    kv_sem_s,
    kv_sem_r,
    kvg_sem_s,
    kvg_sem_r,
):
    rows, width = xb.shape
    ff = act.shape[1]
    tok = tokens.shape[0]
    lat = latents.shape[0]
    half = lat // LAT
    pairs = width // 128
    me = lax.axis_index("dp")
    section = lax.axis_index("section")
    first = section == 0
    second = section == 1
    partner = (me, 1 - section)

    loads = [
        pltpu.make_async_copy(src, dst, load_sem.at[i])
        for i, (src, dst) in enumerate(((w_qkv, wq), (w_out, wo), (w_up, wu), (w_down, wd)))
    ]
    x_loads = [
        pltpu.make_async_copy(tokens, xb.at[lat:rows], load_sem.at[4]),
        pltpu.make_async_copy(latents, xb.at[0:lat], load_sem.at[5]),
    ]
    e_loads = [
        pltpu.make_async_copy(d_tokens, ef.at[lat:rows], load_sem.at[6]),
        pltpu.make_async_copy(d_latents, ef.at[0:lat], load_sem.at[7]),
    ]

    @pl.when(first)
    def _():
        for copy in x_loads:
            copy.start()

    for copy in loads:
        copy.start()

    @pl.when(second)
    def _():
        for copy in e_loads:
            copy.start()

    barrier = pltpu.get_barrier_semaphore()
    pl.semaphore_signal(barrier, inc=1, device_id=partner, device_id_type=MESH)

    here = [lax.rem(me // (1 << bit), 2) for bit in range(4)]

    def across(bit):
        return (me + (1 - 2 * here[bit]) * (1 << bit), section)

    @pl.when(second)
    def _():
        for shift in range(1, n):
            pl.semaphore_signal(
                barrier, inc=1, device_id=(lax.rem(me + shift, n), section), device_id_type=MESH
            )
        pl.semaphore_wait(barrier, n)

    @pl.when(first)
    def _():
        for bit in range(4):
            pl.semaphore_signal(barrier, inc=1, device_id=across(bit), device_id_type=MESH)
        pl.semaphore_wait(barrier, 5)

    def relay(back, band):
        low, high = ((0, rows // 3), (rows // 3, 2 * rows // 3), (2 * rows // 3, rows))[band]
        if not back:
            low, high = ((0, lat), (lat, lat + GROUP), (lat + GROUP, rows))[band]
        return pltpu.make_async_remote_copy(
            src_ref=yb.at[low:high],
            dst_ref=(dy if back else xb).at[low:high],
            send_sem=relay_send.at[3 * back + band],
            recv_sem=relay_recv.at[3 * back + band],
            device_id=partner,
            device_id_type=MESH,
        )

    def kv_copy(shift, incoming):
        slot = lax.rem(me + n - shift, n) if incoming else me
        return pltpu.make_async_remote_copy(
            src_ref=kv_all.at[me], dst_ref=kv_all.at[slot],
            send_sem=kv_sem_s.at[shift - 1], recv_sem=kv_sem_r.at[shift - 1],
            device_id=(lax.rem(me + shift, n), section), device_id_type=MESH,
        )

    def kvg_copy(shift):
        there = lax.rem(me + shift, n)
        return pltpu.make_async_remote_copy(
            src_ref=kvg_send.at[there], dst_ref=kvg_recv.at[shift - 1],
            send_sem=kvg_sem_s.at[shift - 1], recv_sem=kvg_sem_r.at[shift - 1],
            device_id=(there, section), device_id_type=MESH,
        )

    chunks = [slice(c, c + 64) for c in range(0, GROUP, 64)]
    lane = lax.broadcasted_iota(jnp.int32, (1, 128), 1)
    halves = [(lane < 64).astype(F32).astype(LOW), (lane >= 64).astype(F32).astype(LOW)]
    eighths = [(h.astype(F32) * 0.125).astype(LOW) for h in halves]
    heads = (
        lax.broadcasted_iota(jnp.int32, (HEAD_PAD, width), 1) // 64
        == lax.broadcasted_iota(jnp.int32, (HEAD_PAD, width), 0)
    ).astype(F32)

    def block_diagonal(dst, base, src, row, column, scale):
        for i in range(LAT):
            line = src[row + i : row + i + 1, column : column + width] * scale
            dst[base + i * HEAD_PAD : base + (i + 1) * HEAD_PAD, :] = (line * heads).astype(LOW)

    def head_sum(dst, row, column, value, scale, add):
        for i in range(LAT):
            line = jnp.sum(
                value[i * HEAD_PAD : (i + 1) * HEAD_PAD] * heads, axis=0, keepdims=True
            )
            line = line * scale
            if add:
                line = line + dst[row + i : row + i + 1, column : column + width]
            dst[row + i : row + i + 1, column : column + width] = line

    def bands(body, lo, hi, size):
        def one(i, carry):
            body(pl.ds(pl.multiple_of(lo + i * size, 16), size))
            return carry

        lax.fori_loop(0, (hi - lo) // size, one, 0)

    third = rows // 3

    def grouped(body, lo, hi, count):
        def one(i, carry):
            base = lo + i * 16 * count
            body([pl.ds(pl.multiple_of(base + 16 * g, 16), 16) for g in range(count)])
            return carry

        lax.fori_loop(0, (hi - lo) // (16 * count), one, 0)

    def norm(load, gain, dst, lo, hi, count):
        def body(spans):
            means, scales = row_stats(load, spans)
            for r, mean, scale in zip(spans, means, scales):
                dst[r, :] = ((load(r) - mean) * scale * gain[...]).astype(LOW)

        grouped(body, lo, hi, count)

    def norm_back(load, grad, gain, gain_rows, store, lo, hi, count):
        def body(spans):
            means, scales = row_stats(load, spans)
            firsts, seconds = [], []
            kept = gains[0, gain_rows, :]
            for r, mean, scale in zip(spans, means, scales):
                along = grad[r, :] * ((load(r) - mean) * scale)
                kept = kept + along[0:8] + along[8:16]
                firsts.append(row_mean(grad[r, :] * gain[...]))
                seconds.append(row_mean(along * gain[...]))
            gains[0, gain_rows, :] = kept
            for r, mean, scale, one, two in zip(spans, means, scales, firsts, seconds):
                hat = (load(r) - mean) * scale
                store(r, ef[r, :] + scale * (grad[r, :] * gain[...] - one - hat * two))

        grouped(body, lo, hi, count)

    def tiles(count, body, size=TILE):
        def one(i, carry):
            body(at(i * size, size))
            return carry

        lax.fori_loop(0, count, one, 0)

    @pl.when(first)
    def _():
        for copy in x_loads:
            copy.wait()

    @pl.when(second)
    def _():
        spots = lax.broadcasted_iota(jnp.int32, (n, n * lat), 1) // lat
        spread_out = (spots == lax.broadcasted_iota(jnp.int32, (n, n * lat), 0)).astype(F32)
        groups = nn(slots[...].astype(F32).astype(LOW), spread_out.astype(LOW))
        of_micro = lax.rem(lax.broadcasted_iota(jnp.int32, (1, n * lat), 1), lat) // LAT
        for m in range(half):
            images = jnp.zeros((1, n * lat), F32)
            own_image = jnp.float32(0)
            end = jnp.int32(0)
            for i in range(image_at.shape[1]):
                end = end + image_at[m, i]
                images += jnp.where(end.astype(F32) <= groups[m : m + 1], 1.0, 0.0)
                own_image += jnp.where(end <= slot_at[m, me], 1.0, 0.0)
            seen = (images == own_image) & (of_micro == m)
            key_mask[m : m + 1, :] = jnp.where(seen, 0.0, masked_score)

    def load_in(r):
        return xb[r, :].astype(F32)

    def load_mid(r):
        return mid[r, :]

    def lat_bias(m, shape, axis):
        return jnp.where(
            lax.broadcasted_iota(jnp.int32, shape, axis) // LAT == m, 0.0, masked_score
        ).astype(F32)

    @pl.when(first)
    def _():
        norm(load_in, gain_attn, n1, 0, rows, 11)
        loads[0].wait()

        def project(c):
            proj[:, c] = nn(n1[...], wq[:, c]).astype(LOW)

        tiles(3 * width // TILE, project)
        latf[...] = proj[0:lat, :].astype(F32)

        def one_pair(it, side):
            m, p = it // pairs, lax.rem(it, pairs)
            r = pl.ds(pl.multiple_of(lat + m * GROUP, 16), GROUP)
            q = proj[r, at(p * 128, 128)]
            k = proj[r, at(width + p * 128, 128)]
            v = proj[r, at(2 * width + p * 128, 128)]
            kl = proj[0:lat, at(width + p * 128, 128)]
            vl = proj[0:lat, at(2 * width + p * 128, 128)]
            bias = lat_bias(m, (lat, GROUP), 0)
            total = jnp.zeros((GROUP, 128), F32)
            for e in (0, 1):
                qe = q * eighths[e]
                s = scores.at[2 * side + e]
                s[...] = nt(k, qe)
                sl = nt(kl, qe) + bias
                top = jnp.max(sl, axis=0, keepdims=True)
                for c in chunks:
                    top = jnp.maximum(top, jnp.max(s[c, :], axis=0, keepdims=True))
                el = jnp.exp(sl - top)
                whole_sum = jnp.sum(el, axis=0, keepdims=True)
                for c in chunks:
                    et = jnp.exp(s[c, :] - top)
                    s[c, :] = et
                    whole_sum += jnp.sum(et, axis=0, keepdims=True)
                scale = 1.0 / whole_sum
                for c in chunks:
                    probs[2 * it + e, c, :] = (s[c, :] * scale).astype(LOW)
                pe = (el * scale).astype(LOW)
                probs[2 * it + e, GROUP : GROUP + lat, :] = pe
                total += tn(probs[2 * it + e, 0:GROUP, :], v * halves[e])
                total += tn(pe, vl * halves[e])
            mixed[r, at(p * 128, 128)] = total.astype(LOW)

        def pair(i, carry):
            one_pair(2 * i, 0)
            one_pair(2 * i + 1, 1)
            return carry

        lax.fori_loop(0, half * pairs // 2, pair, 0)
        for m in range(half):
            r = slice(lat + m * GROUP, lat + (m + 1) * GROUP)
            b = slice(m * 128, (m + 1) * 128)
            block_diagonal(qbd, m * 128, latf, m * LAT, 0, 0.125)
            s = nt(qbd[b, :], proj[r, width : 2 * width])
            sl = nt(qbd[b, :], proj[0:lat, width : 2 * width]) + lat_bias(m, (128, lat), 1)
            top = jnp.maximum(
                jnp.max(s, axis=1, keepdims=True), jnp.max(sl, axis=1, keepdims=True)
            )
            et = jnp.exp(s - top)
            el = jnp.exp(sl - top)
            scale = 1.0 / (
                jnp.sum(et, axis=1, keepdims=True) + jnp.sum(el, axis=1, keepdims=True)
            )
            pt = (et * scale).astype(LOW)
            pe = (el * scale).astype(LOW)
            probs_lat[b, 0:GROUP] = pt
            probs_lat[b, GROUP : GROUP + lat] = pe
            o = nn(pt, proj[r, 2 * width :]) + nn(pe, proj[0:lat, 2 * width :])
            head_sum(mixf, m * LAT, 0, o, 1.0, False)
        mixed[0:lat, :] = mixf[...].astype(LOW)

    keys = n * lat

    root = 0.7978845608028654

    def mlp_in(lo, hi, count, with_dact=False):
        r0 = slice(lo, hi)
        mid[r0, :] = xb[r0, :].astype(F32) + nn(mixed[r0, :], wo[...])

        norm(load_mid, gain_mlp, n2, lo, hi, count)

        def up_tile(dst, i):
            dst[r0, 0:512] = nn(n2[r0, :], wu[:, at(i * 512, 512)])

        def gelu(src, i):
            c = at(i * 512, 512)
            for g in range(lo, hi, 16):
                r = slice(g, g + 16)
                up = src[r, 0:512]
                square = up * up
                t = jnp.tanh(up * (root + (root * 0.044715) * square))
                gate = 0.5 + 0.5 * t
                value = up * gate
                slope = gate + (value + value) * (1.0 - gate) * (
                    root + (3.0 * root * 0.044715) * square
                )
                act[r, c] = value.astype(LOW)
                if with_dact:
                    slope = slope * dup[r, c].astype(F32)
                dup[r, c] = slope.astype(LOW)

        last = ff // 512 - 1

        def widen(i, carry):
            up_tile(out, 2 * i + 1)
            gelu(tmp, 2 * i)
            up_tile(tmp, jnp.minimum(2 * i + 2, last))
            gelu(out, 2 * i + 1)
            return carry

        up_tile(tmp, 0)
        lax.fori_loop(0, ff // 1024, widen, 0)

    out_copies = [
        pltpu.make_async_copy(out.at[lat:rows], out_tok, load_sem.at[8]),
        pltpu.make_async_copy(out.at[0:lat], out_lat, load_sem.at[9]),
    ]
    grad_copies = [
        pltpu.make_async_copy(out.at[lat:rows], grad_tok, load_sem.at[8]),
        pltpu.make_async_copy(out.at[0:lat], grad_lat, load_sem.at[9]),
    ]

    def layer_output(low, high, passed_on):
        r = slice(low, high)
        y = mid[r, :] + nn(act[r, :], wd[...])
        if passed_on:
            narrow_y = y.astype(LOW)
            yb[r, :] = narrow_y
            y = narrow_y.astype(F32)
        out[r, :] = y

    @pl.when(first)
    def _():
        for copy in loads[1:]:
            copy.wait()
        mlp_in(0, lat + GROUP, 17)
        layer_output(0, lat + GROUP, True)
        relay(0, 0).start()
        relay(0, 1).start()
        mlp_in(lat + GROUP, rows, 16)
        layer_output(lat + GROUP, rows, True)
        relay(0, 2).start()
        for copy in out_copies:
            copy.start()

    @pl.when(second)
    def _():
        for copy in e_loads:
            copy.wait()

        def narrow_e(r):
            dy[r, :] = ef[r, :].astype(LOW)

        bands(narrow_e, 0, rows, third)
        for copy in loads:
            copy.wait()

        def early(c):
            dup[:, c] = nt(dy[...], wd[c, :]).astype(LOW)

        tiles(ff // TILE, early)
        relay(0, 0).wait_recv()
        norm(load_in, gain_attn, n1, 0, lat, 1)
        lat_proj = nn(n1[0:lat, :], wq[...]).astype(LOW)
        kv_all[me] = lat_proj[:, width:]
        latf[...] = lat_proj.astype(F32)
        for shift in range(1, n):
            kv_copy(shift, False).start()
        for m in range(half):
            relay(0, 1 + m).wait_recv()
            low, high = lat + m * GROUP, lat + (m + 1) * GROUP
            r = slice(low, high)
            b = slice(m * 128, (m + 1) * 128)
            norm(load_in, gain_attn, n1, low, high, 16)
            proj[r, :width] = nn(n1[r, :], wq[:, :width]).astype(LOW)
            block_diagonal(qbd, m * 128, latf, m * LAT, 0, 0.125)
            block_diagonal(kbd, m * 128, latf, m * LAT, width, 1.0)
            block_diagonal(vbd, m * 128, latf, m * LAT, 2 * width, 1.0)
            s = nt(proj[r, :width] * jnp.asarray(0.125, LOW), kbd[b, :])
            et = jnp.exp(s - class_max(s))
            pt = (et / class_sum(et)).astype(LOW)
            probs[m, 0:GROUP, 0:128] = pt
            mixed[r, :] = nn(pt, vbd[b, :]).astype(LOW)
            mlp_in(low, high, 16, True)
        for shift in range(1, n):
            kv_copy(shift, True).wait_recv()
        k = kv_all[:, :, :width].reshape(keys, width)
        v = kv_all[:, :, width:].reshape(keys, width)
        for m in range(half):
            b = slice(m * 128, (m + 1) * 128)
            s = nt(qbd[b, :], k) + key_mask[m : m + 1, :]
            et = jnp.exp(s - jnp.max(s, axis=1, keepdims=True))
            pt = (et / jnp.sum(et, axis=1, keepdims=True)).astype(LOW)
            probs_lat[b, 0:keys] = pt
            head_sum(mixf, m * LAT, 0, nn(pt, v), 1.0, False)
        mixed[0:lat, :] = mixf[...].astype(LOW)
        mlp_in(0, lat, 1, True)

    @pl.when(first)
    def _():
        for band in range(3):
            relay(1, band).wait_recv()

        def widen_e(r):
            ef[r, :] = dy[r, :].astype(F32)

        bands(widen_e, 0, rows, third)

    part = 384
    unit = width // n
    many = part // unit

    def staged(slot, piece, chunk, share):
        return pltpu.make_async_copy(
            stage.at[slot, piece],
            grads.at[
                chunk,
                share // 8,
                lax.rem(share // 4, 2),
                lax.rem(share // 2, 2),
                lax.rem(share, 2),
            ],
            stage_sem.at[slot, piece],
        )

    def drain(slot):
        def one(piece, carry):
            staged(slot, piece, 0, 0).wait()
            return carry

        lax.fori_loop(0, many, one, 0)

    def weight_grad(place, start, count, left, *rights, settled=True):
        def one(i, carry):
            turned = left(i).T
            for at_right, right in enumerate(rights):
                tile = i * len(rights) + at_right
                slot = lax.rem(tile, 2)
                value = nn(turned, right(i)).astype(LOW)

                if settled:

                    @pl.when(tile >= start * len(rights) + 2)
                    def _():
                        drain(slot)

                else:
                    drain(slot)

                for piece in range(many):
                    stage[slot, piece] = value[piece * unit : (piece + 1) * unit]
                    staged(slot, piece, *place(i, at_right, piece)).start()
            return carry

        lax.fori_loop(start, start + count, one, 0)

    def settle():
        for slot in (0, 1):
            drain(slot)

    orders = ((0, 2, 1, 3), (1, 2, 0, 3), (2, 1, 0, 3))
    own_buf = (own_a, own_b, own_a)
    per_part = width // part
    wide = ff // width
    land = (
        (land1_a, land1_b, land1_c),
        (land2_a, land2_b, land2_c),
        (land3_a, land3_b, land3_c),
        (land4_a, land4_b, land4_c),
    )

    def chunk_of(kind, k):
        if kind == 2:
            return 2 * wide + 3 * k
        return 2 * k + kind + k // wide

    def source(kind, phase, k, theirs):
        pick = [(1 - here[bit]) if theirs else here[bit] for bit in orders[kind]]
        own_bit = [here[bit] for bit in orders[kind]]
        base = land[0][kind]
        if phase == 0:
            chunk = grads.at[chunk_of(kind, k)]
            return (chunk.at[:, :, :, pick[0]], chunk.at[:, :, pick[0]], chunk.at[:, pick[0]])[kind]
        if phase == 1:
            return base.at[k, :, pick[1]]
        if phase == 2:
            return base.at[k, :, own_bit[1], pick[2]]
        return base.at[k, pick[3], own_bit[1], own_bit[2]]

    def copy_of(kind, phase, k):
        return pltpu.make_async_remote_copy(
            src_ref=source(kind, phase, k, True),
            dst_ref=land[phase][kind].at[k],
            send_sem=send_sem.at[kind, phase, k],
            recv_sem=recv_sem.at[kind, phase, k],
            device_id=across(orders[kind][phase]),
            device_id_type=MESH,
        )

    def own(kind, k):
        return pltpu.make_async_copy(
            source(kind, 0, k, False), own_buf[kind], own_sem.at[kind]
        )

    def leave(kind, k):
        slot = lax.rem(k, 2)
        return pltpu.make_async_copy(
            leaving.at[slot, kind], summed.at[chunk_of(kind, k)], leave_sem.at[slot, kind]
        )

    def launch(phase, k, kinds=(0, 1)):
        for kind in kinds:
            copy_of(kind, phase, k).start()

    def onward(phase, k, kinds):
        for kind in kinds:
            if phase == 0:
                own(kind, k).wait()
            copy_of(kind, phase, k).wait_recv()
            base, into = land[0][kind], land[phase][kind]
            mine = [here[bit] for bit in orders[kind]]
            if phase == 0:

                def add(i, carry):
                    for j in (0, 1):
                        for h in (0, 1):
                            total = own_buf[kind][i, j, h].astype(F32)
                            total += base[k, i, j, h].astype(F32)
                            base[k, i, j, h] = total.astype(LOW)
                    return carry

                lax.fori_loop(0, 2, add, 0)
            elif phase == 1:
                for i in (0, 1):
                    for h in (0, 1):
                        total = base[k, i, mine[1], h].astype(F32)
                        total += into[k, i, h].astype(F32)
                        base[k, i, mine[1], h] = total.astype(LOW)
            elif phase == 2:
                for i in (0, 1):
                    total = base[k, i, mine[1], mine[2]].astype(F32)
                    total += into[k, i].astype(F32)
                    base[k, i, mine[1], mine[2]] = total.astype(LOW)
            else:
                total = base[k, mine[3], mine[1], mine[2]].astype(F32)
                total += into[k].astype(F32)
                slot = lax.rem(k, 2)

                @pl.when(k >= 2)
                def _():
                    leave(kind, k - 2).wait()

                leaving[slot, kind] = total
                leave(kind, k).start()
            if phase < 3:
                copy_of(kind, phase + 1, k).start()

    def run(phase, lo, hi, *kinds, fetched=False):
        if phase == 0 and not fetched:
            for kind in kinds:
                own(kind, lo).start()

        def one(k, carry):
            for kind in kinds:
                onward(phase, k, (kind,))
                if phase == 0:

                    @pl.when(k + 1 < hi)
                    def _():
                        own(kind, k + 1).start()

            return carry

        lax.fori_loop(lo, hi, one, 0)

    def up_grad():
        weight_grad(
            lambda i, right, piece: (
                wide + lax.rem(i * many + piece, wide),
                (i * many + piece) // wide,
            ),
            0,
            ff // part,
            lambda i: dup[:, at(i * part, part)],
            lambda i: n2[...],
        )
    def down_grad(pair, settled):
        weight_grad(
            lambda i, right, piece: (2 * pair + right, i * many + piece),
            0,
            per_part,
            lambda i: dy[:, at(i * part, part)],
            lambda i: act[:, 2 * pair * width : (2 * pair + 1) * width],
            lambda i: act[:, (2 * pair + 1) * width : (2 * pair + 2) * width],
            settled=settled,
        )

    down_grad(0, True)
    down_grad(1, False)
    launch(0, 0)

    @pl.when(first)
    def _():
        def unwiden(c):
            dup[:, c] = (nt(dy[...], wd[c, :]) * dup[:, c].astype(F32)).astype(LOW)

        tiles(ff // TILE, unwiden)

    settle()
    launch(0, 1)
    up_grad()

    def to_mid(c):
        tmp[:, c] = nt(dup[...], wu[c, :])

    tiles(width // 256, to_mid, 256)
    settle()
    launch(0, 2)
    launch(0, 3)
    gains[0] = jnp.zeros_like(gains[0])

    def store_mid(r, total):
        ef[r, :] = total
        dy[r, :] = total.astype(LOW)

    norm_back(load_mid, tmp, gain_mlp, slice(8, 16), store_mid, 0, rows, 11)

    @pl.when(first)
    def _():
        for band in range(3):
            relay(0, band).wait_send()

    def to_mix(c):
        yb[:, c] = nt(dy[...], wo[c, :]).astype(LOW)

    tiles(width // TILE, to_mix)
    mixf[...] = yb[0:lat, :].astype(F32)

    @pl.when(second)
    def _():
        k = kv_all[:, :, :width].reshape(keys, width)
        v = kv_all[:, :, width:].reshape(keys, width)
        for m in range(half):
            b = slice(m * 128, (m + 1) * 128)
            block_diagonal(vbd.at[pl.ds(256, 256)], m * 128, mixf, m * LAT, 0, 1.0)
        both = slice(0, half * 128)
        do = vbd[256 : 256 + half * 128, :]
        pt = probs_lat[both, 0:keys]
        pf = pt.astype(F32)
        dp = nt(do, v)
        along = jnp.sum(pf * dp, axis=1, keepdims=True)
        ds = (pf * (dp - along)).astype(LOW)
        kvg_send[:, :, :width] = tn(ds, qbd[both, :]).astype(LOW).reshape(n, lat, width)
        kvg_send[:, :, width:] = tn(pt, do).astype(LOW).reshape(n, lat, width)
        for shift in range(1, n):
            kvg_copy(shift).start()
        dq = nn(ds, k)
        for m in range(half):
            head_sum(latf, m * LAT, 0, dq[m * 128 : (m + 1) * 128], 0.125, False)
        proj[0:lat, :width] = latf[:, :width].astype(LOW)
        layer_output(0, lat + GROUP, False)
        layer_output(lat + GROUP, rows, False)
        for copy in out_copies:
            copy.start()

    weight_grad(
        lambda i, right, piece: (2 * wide, i * many + piece),
        0,
        width // part,
        lambda i: dy[:, at(i * part, part)],
        lambda i: mixed[...],
    )
    for copy in out_copies:
        copy.wait()
    for kind in (0, 1):
        own(kind, 0).start()

    @pl.when(first)
    def _():
        for m in range(half):
            r = slice(lat + m * GROUP, lat + (m + 1) * GROUP)
            b = slice(m * 128, (m + 1) * 128)
            block_diagonal(vbd, m * 128, mixf, m * LAT, 0, 1.0)
            do = vbd[b, :]
            dp = nt(do, proj[r, 2 * width :])
            dl = nt(do, proj[0:lat, 2 * width :])
            pt = probs_lat[b, 0:GROUP]
            pe = probs_lat[b, GROUP : GROUP + lat]
            pf = pt.astype(F32)
            pg = pe.astype(F32)
            along = jnp.sum(pf * dp, axis=1, keepdims=True) + jnp.sum(
                pg * dl, axis=1, keepdims=True
            )
            ds = (pf * (dp - along)).astype(LOW)
            dsl = (pg * (dl - along)).astype(LOW)
            dq = nn(ds, proj[r, width : 2 * width]) + nn(dsl, proj[0:lat, width : 2 * width])
            head_sum(latf, m * LAT, 0, dq, 0.125, False)
            tmp[r, :] = tn(ds, qbd[b, :])
            out[r, :] = tn(pt, do)
            if m == 0:
                tmp[0:lat, :] = tn(dsl, qbd[b, :])
                out[0:lat, :] = tn(pe, do)
            else:
                tmp[0:lat, :] += tn(dsl, qbd[b, :])
                out[0:lat, :] += tn(pe, do)
        proj[0:lat, :width] = latf[:, :width].astype(LOW)
        settle()
        launch(0, 0, (2,))

        def one_pair(it, side):
            m, p = it // pairs, lax.rem(it, pairs)
            r = pl.ds(pl.multiple_of(lat + m * GROUP, 16), GROUP)
            qc = at(p * 128, 128)
            q = proj[r, qc]
            k = proj[r, at(width + p * 128, 128)]
            v = proj[r, at(2 * width + p * 128, 128)]
            kl = proj[0:lat, at(width + p * 128, 128)]
            vl = proj[0:lat, at(2 * width + p * 128, 128)]
            dx = yb[r, qc]
            dq = jnp.zeros((GROUP, 128), F32)
            dk = tmp[r, qc]
            dv = out[r, qc]
            dkl = tmp[0:lat, qc]
            dvl = out[0:lat, qc]
            for e in (0, 1):
                qe = q * eighths[e]
                de = dx * halves[e]
                s = scores.at[2 * side + e]
                s[...] = nt(v, de)
                dl = nt(vl, de)
                pt = probs[2 * it + e, 0:GROUP, :]
                pe = probs[2 * it + e, GROUP : GROUP + lat, :]
                pg = pe.astype(F32)
                along = jnp.sum(pg * dl, axis=0, keepdims=True)
                for c in chunks:
                    pf = probs[2 * it + e, c, :].astype(F32)
                    along += jnp.sum(pf * s[c, :], axis=0, keepdims=True)
                for c in chunks:
                    pf = probs[2 * it + e, c, :].astype(F32)
                    slopes[2 * side + e, c, :] = (pf * (s[c, :] - along)).astype(LOW)
                ds = slopes[2 * side + e]
                dsl = (pg * (dl - along)).astype(LOW)
                dq += tn(ds, k * halves[e]) + tn(dsl, kl * halves[e])
                dk += nn(ds, qe)
                dkl += nn(dsl, qe)
                dv += nn(pt, de)
                dvl += nn(pe, de)
            proj[r, qc] = (dq * 0.125).astype(LOW)
            proj[r, at(width + p * 128, 128)] = dk.astype(LOW)
            proj[r, at(2 * width + p * 128, 128)] = dv.astype(LOW)
            tmp[0:lat, qc] = dkl
            out[0:lat, qc] = dvl

        def pair(i, carry):
            one_pair(2 * i, 0)
            one_pair(2 * i + 1, 1)
            return carry

        lax.fori_loop(0, half * pairs // 2, pair, 0)
        proj[0:lat, width : 2 * width] = tmp[0:lat, :].astype(LOW)
        proj[0:lat, 2 * width :] = out[0:lat, :].astype(LOW)

    @pl.when(second)
    def _():
        for m in range(half):
            r = slice(lat + m * GROUP, lat + (m + 1) * GROUP)
            b = slice(m * 128, (m + 1) * 128)
            pt = probs[m, 0:GROUP, 0:128]
            pf = pt.astype(F32)
            dx = yb[r, :]
            dp = nt(dx, vbd[b, :])
            ds = (pf * (dp - class_sum(pf * dp))).astype(LOW)
            dk = tn(ds, proj[r, :width])
            dv = tn(pt, dx)
            proj[r, :width] = (nn(ds, kbd[b, :]) * 0.125).astype(LOW)
            head_sum(latf, m * LAT, width, dk, 0.125, False)
            head_sum(latf, m * LAT, 2 * width, dv, 1.0, False)
        settle()
        launch(0, 0, (2,))
        total = latf[:, width:] + kvg_send[me].astype(F32)
        for shift in range(1, n):
            kvg_copy(shift).wait_recv()
            total += kvg_recv[shift - 1].astype(F32)
        proj[0:lat, width:] = total.astype(LOW)

    def qkv_grad(start, count, r):
        weight_grad(
            lambda i, right, piece: (
                2 * wide + 1 + lax.rem(i * many + piece, 3),
                (i * many + piece) // 3,
            ),
            start,
            count,
            lambda i: proj[r, at(i * part, part)],
            lambda i: n1[r, :],
        )

    @pl.when(first)
    def _():
        run(0, 0, wide, 0, 1, fetched=True)
        qkv_grad(0, 3 * per_part, slice(0, rows))
        settle()
        launch(0, wide)
        launch(0, 1, (2,))

    @pl.when(first)
    def _():
        def to_in(c):
            tmp[:, c] = nt(proj[...], wq[c, :])

        tiles(width // 256, to_in, 256)

    @pl.when(second)
    def _():
        tmp[...] = nt(proj[:, :width], wq[:, :width])
        tmp[0:lat, :] += nt(proj[0:lat, width:], wq[:, width:])

    def store_in(r, total):
        low = total.astype(LOW)
        yb[r, :] = low
        out[r, :] = jnp.where(first, total, low.astype(F32))

    for band in range(3):
        norm_back(
            load_in, tmp, gain_attn, slice(0, 8), store_in, band * third, (band + 1) * third, 11
        )

        @pl.when(second)
        def _():
            relay(1, band).start()

    for copy in grad_copies:
        copy.start()

    @pl.when(second)
    def _():
        qkv_grad(0, per_part, slice(0, rows))
        settle()
        qkv_grad(per_part, 2 * per_part, slice(0, lat))
        settle()
        launch(0, wide)
        launch(0, 1, (2,))
        run(0, 0, wide, 0, 1, fetched=True)

    def gain_copy(bit):
        return pltpu.make_async_remote_copy(
            src_ref=gains.at[bit],
            dst_ref=land_g.at[bit],
            send_sem=gain_s.at[bit],
            recv_sem=gain_r.at[bit],
            device_id=across(bit),
            device_id_type=MESH,
        )

    def gain_step(bit):
        gain_copy(bit).wait_recv()
        gains[bit + 1] = gains[bit] + land_g[bit]

    gain_copy(0).start()
    run(0, 0, 1, 2)
    run(1, 0, wide, 0, 1)
    gain_step(0)
    gain_copy(1).start()
    run(0, wide, wide + 1, 0, 1)
    run(0, 1, 2, 2)
    gain_step(1)
    gain_copy(2).start()
    run(1, 0, 1, 2)
    run(2, 0, wide, 0, 1)
    gain_step(2)
    gain_copy(3).start()
    run(1, wide, wide + 1, 0, 1)
    run(1, 1, 2, 2)
    run(2, 0, 1, 2)
    run(3, 0, wide, 0, 1)
    run(2, wide, wide + 1, 0, 1)
    run(2, 1, 2, 2)
    gain_step(3)
    run(3, 0, 1, 2)
    run(3, wide, wide + 1, 0, 1)
    run(3, 1, 2, 2)
    final = gains[4]
    for i in (0, 1):
        whole_gain = jnp.sum(final[8 * i : 8 * i + 8], axis=0, keepdims=True)
        whole_gain = jnp.broadcast_to(whole_gain, (8, width))
        rolled = pltpu.roll(whole_gain, lax.rem(width - me * unit, width), 1)
        gain_sums[8 * i : 8 * i + 8, :] = rolled[:, 0:128]

    def finish(kind):
        def one(k, carry):
            for phase in range(4):
                copy_of(kind, phase, k).wait_send()
            return carry

        lax.fori_loop(0, land[0][kind].shape[0], one, 0)

    for kind in range(3):
        finish(kind)
    for bit in range(4):
        gain_copy(bit).wait_send()
    for copy in grad_copies:
        copy.wait()
    for kind in range(3):
        count = land[0][kind].shape[0]
        for k in (count - 2, count - 1):
            leave(kind, k).wait()

    @pl.when(second)
    def _():
        for band in range(3):
            relay(1, band).wait_send()
        for shift in range(1, n):
            kv_copy(shift, False).wait_send()
            kvg_copy(shift).wait_send()


def both_layers(n, tokens, latents, slots, images, gains, weights, d_tokens, d_latents):
    tok, width = tokens.shape
    lat = latents.shape[0]
    rows = tok + lat
    w_qkv, w_out, w_up, w_down = weights
    ff = w_up.shape[1]
    keys = n * lat
    half = lat // LAT
    size = sum(w.size for w in weights)
    chunks = size // (width * width)
    most = chunks // 2 - 1
    unit = width // n
    vm, hbm = pl.BlockSpec(memory_space=pltpu.VMEM), pl.BlockSpec(memory_space=pl.ANY)
    sm = pl.BlockSpec(memory_space=pltpu.SMEM)
    scratch = [
        pltpu.VMEM(w.shape, LOW) for w in (w_qkv, w_out, w_up, w_down)
    ] + [
        pltpu.VMEM(shape, dtype)
        for shape, dtype in (
            ((rows, width), LOW),
            ((rows, width), LOW),
            ((rows, 3 * width), LOW),
            ((rows, width), LOW),
            ((rows, width), F32),
            ((rows, width), LOW),
            ((rows, ff), LOW),
            ((rows, ff), LOW),
            ((rows, width), LOW),
            ((rows, width), LOW),
            ((rows, width), F32),
            ((rows, width), F32),
            ((rows, width), F32),
            ((half * width // 64, GROUP + lat, GROUP), LOW),
            ((half * 128, max(keys, GROUP + 128)), LOW),
            ((4, GROUP, GROUP), F32),
            ((4, GROUP, GROUP), LOW),
            ((lat, 3 * width), F32),
            ((lat, width), F32),
            ((8, keys), F32),
            ((half * 128, width), LOW),
            ((half * 128, width), LOW),
            ((half * 256, width), LOW),
            ((n, lat, 2 * width), LOW),
            ((n, lat, 2 * width), LOW),
            ((n - 1, lat, 2 * width), LOW),
            ((2, 384 // unit, unit, width), LOW),
            ((5, 16, width), F32),
            ((2, 3, unit, width), F32),
            ((2, 2, 2, unit, width), LOW),
            ((2, 2, 2, unit, width), LOW),
            *(
                ((count, *shape, unit, width), LOW)
                for shape in ((2, 2, 2), (2, 2), (2,), ())
                for count in (most,) * 2 + (2,)
            ),
            ((4, 16, width), F32),
        )
    ] + [
        pltpu.SemaphoreType.DMA((10,)),
        pltpu.SemaphoreType.DMA((2, 384 // unit)),
        pltpu.SemaphoreType.DMA((3,)),
        pltpu.SemaphoreType.DMA((2, 3)),
        pltpu.SemaphoreType.DMA((3, 4, most)),
        pltpu.SemaphoreType.DMA((3, 4, most)),
        pltpu.SemaphoreType.DMA((4,)),
        pltpu.SemaphoreType.DMA((4,)),
        pltpu.SemaphoreType.DMA((6,)),
        pltpu.SemaphoreType.DMA((6,)),
        pltpu.SemaphoreType.DMA((n - 1,)),
        pltpu.SemaphoreType.DMA((n - 1,)),
        pltpu.SemaphoreType.DMA((n - 1,)),
        pltpu.SemaphoreType.DMA((n - 1,)),
    ]
    return pl.pallas_call(
        functools.partial(layer_kernel, n),
        out_shape=(
            jax.ShapeDtypeStruct((tok, width), F32),
            jax.ShapeDtypeStruct((lat, width), F32),
            jax.ShapeDtypeStruct((tok, width), F32),
            jax.ShapeDtypeStruct((lat, width), F32),
            jax.ShapeDtypeStruct((chunks, 2, 2, 2, 2, unit, width), LOW),
            jax.ShapeDtypeStruct((chunks, unit, width), F32),
            jax.ShapeDtypeStruct((16, 128), F32),
        ),
        in_specs=[hbm, hbm, vm, sm, sm, vm, vm] + [hbm] * 6,
        out_specs=(hbm,) * 6 + (vm,),
        scratch_shapes=scratch,
        compiler_params=pltpu.CompilerParams(
            collective_id=1, has_side_effects=True, vmem_limit_bytes=63 * 1024 * 1024
        ),
        cost_estimate=pl.CostEstimate(
            flops=6 * rows * size, bytes_accessed=4 * size, transcendentals=0
        ),
    )(tokens, latents, slots, slots, images, *gains, *weights, d_tokens, d_latents)


def finish_kernel(width, *refs):
    rows_in, (summed, gains), rows_out = refs[0:4], refs[4:6], refs[6:10]
    gain_attn, g_qkv, g_out, gain_mlp, g_up, g_down = refs[10:16]
    held, (sem_in, sem_out) = refs[16:21], refs[21:23]
    wide = g_down.shape[1] // width
    unit = g_out.shape[1]
    loads = [
        pltpu.make_async_copy(src, dst, sem_in.at[i])
        for i, (src, dst) in enumerate(zip((*rows_in, summed), held))
    ]
    for load in loads:
        load.start()
    all_rows, sums = held[0:4], held[4]
    moves = [[pair] for pair in zip(all_rows, rows_out)] + [
        [(sums.at[c], g_down.at[:, c * width : (c + 1) * width]) for c in range(wide)]
        + [
            (sums.at[wide : 2 * wide], g_up),
            (sums.at[2 * wide : 2 * wide + 1], g_out),
            (sums.at[2 * wide + 1 :], g_qkv),
        ]
    ]
    gain_attn[...] = gains[0:1, 0:unit]
    gain_mlp[...] = gains[8:9, 0:unit]
    started = []
    for load, group in zip(loads, moves):
        load.wait()
        for src, dst in group:
            started.append(pltpu.make_async_copy(src, dst, sem_out.at[len(started)]))
            started[-1].start()
    for move in started:
        move.wait()


def finished(rows, summed, gains, wide):
    chunks, unit, width = summed.shape
    hbm, vm = pl.BlockSpec(memory_space=pl.ANY), pl.BlockSpec(memory_space=pltpu.VMEM)
    shapes = [r.shape for r in rows] + [
        (1, unit),
        (3, unit, width),
        (1, unit, width),
        (1, unit),
        (wide, unit, width),
        (unit, wide * width),
    ]
    return pl.pallas_call(
        functools.partial(finish_kernel, width),
        out_shape=tuple(jax.ShapeDtypeStruct(s, F32) for s in shapes),
        in_specs=[hbm] * 5 + [vm],
        out_specs=(hbm,) * 4 + (vm, hbm, hbm, vm, hbm, hbm),
        scratch_shapes=[pltpu.VMEM(x.shape, F32) for x in (*rows, summed)]
        + [pltpu.SemaphoreType.DMA((5,)), pltpu.SemaphoreType.DMA((7 + wide,))],
        compiler_params=pltpu.CompilerParams(vmem_limit_bytes=62 * 1024 * 1024),
    )(*rows, summed, gains)
def fused_shards(
    unused_grid,
    tokens,
    latents,
    slot_group,
    image_groups,
    gain_attn,
    w_qkv,
    w_out,
    gain_mlp,
    w_up,
    w_down,
    d_tokens,
    d_latents,
):
    micro, tok, width = tokens.shape
    lat = latents.shape[1]
    out_tok, out_lat, grad_tok, grad_lat, unused_grads, summed, gains = both_layers(
        slot_group.shape[1],
        tokens.reshape(micro * tok, width),
        latents.reshape(micro * lat, width),
        slot_group,
        image_groups,
        (gain_attn, gain_mlp),
        (w_qkv[0], w_out[0], w_up[0], w_down[0]),
        d_tokens.reshape(micro * tok, width),
        d_latents.reshape(micro * lat, width),
    )
    wide = w_up.shape[2] // width
    rows = (out_tok, out_lat, grad_tok, grad_lat)
    *rows, first_gain, qkv, out, second_gain, up, down = finished(rows, summed, gains, wide)
    return (
        rows[0].reshape(1, micro, tok, width),
        rows[1].reshape(1, micro, lat, width),
        rows[2].reshape(1, micro, tok, width),
        rows[3].reshape(1, micro, lat, width),
        first_gain,
        qkv.reshape(-1, width).T[None],
        out.reshape(-1, width).T[None],
        second_gain,
        up.reshape(-1, width).T[None],
        down.T[None],
    )

def solution(mesh):
    in_specs = (
        P(None, "dp", None),
        P(None, "dp", None),
        P(),
        P(),
        P("section", None),
        P("section", None, None),
        P("section", None, None),
        P("section", None),
        P("section", None, None),
        P("section", None, None),
        P(None, "dp", None),
        P(None, "dp", None),
    )
    out_specs = (
        P("section", None, "dp", None),
        P("section", None, "dp", None),
        P("section", None, "dp", None),
        P("section", None, "dp", None),
        P("section", "dp"),
        P("section", None, "dp"),
        P("section", None, "dp"),
        P("section", "dp"),
        P("section", None, "dp"),
        P("section", None, "dp"),
    )
    grid = grid_of(mesh)

    def program(*args):
        n, width = mesh.shape["dp"], args[0].shape[2]
        one_group = args[0].shape[1] == n * GROUP
        body = fused_shards if one_group and n == 16 and width % (16 * n) == 0 else shards
        return jax.shard_map(
            functools.partial(body, grid), mesh=mesh, in_specs=in_specs, out_specs=out_specs, check_vma=False
        )(*args)

    return program
```

```python
import functools

import jax
import jax.numpy as jnp
from jax import lax
from jax.experimental import pallas as pl
from jax.experimental.pallas import tpu as pltpu
from jax.sharding import PartitionSpec as P

HEADS = 12
GROUP = 256
LAT = 8


epsilon = 1e-05
masked_score = -1e30


MESH = pl.DeviceIdType.MESH


def grid_of(mesh):
    n = mesh.shape["dp"]
    coords = [getattr(d, "coords", None) for d in mesh.devices.reshape(n, -1)[:, 0]]
    if any(c is None for c in coords):
        return (n // 4, 2, 2) if n % 4 == 0 else (n, 1, 1)
    sizes = {a: len({c[a] for c in coords}) for a in range(3)}
    strides = {
        a: min([i for i in range(n) if coords[i][a] != coords[0][a]], default=n) for a in range(3)
    }
    order = sorted(range(3), key=lambda a: -strides[a])
    return tuple(sizes[a] for a in order)


def spread_kernel(grid, pairs, g_ref, gain_ref, out_ref, gout_ref, *scratch):
    acc = scratch[0:3]
    land = [scratch[3 + 3 * i : 6 + 3 * i] for i in range(3)]
    send_sem, recv_sem, own_sem = scratch[12:15]
    me = lax.axis_index("dp")
    section = lax.axis_index("section")
    l0, l1, l2 = grid
    here = (me // (l1 * l2), lax.rem(me // l2, l1), lax.rem(me, l2))

    def device(axis, shift):
        there = list(here)
        there[axis] = lax.rem(here[axis] + shift, grid[axis])
        return there[axis], ((there[0] * l1 + there[1]) * l2 + there[2], section)

    barrier = pltpu.get_barrier_semaphore()
    for axis in range(3):
        for shift in range(1, grid[axis]):
            pl.semaphore_signal(
                barrier, inc=1, device_id=device(axis, shift)[1], device_id_type=MESH
            )
    pl.semaphore_wait(barrier, sum(grid) - 3)

    orders = ((2, 1, 0), (1, 2, 0), (2, 1, 0))

    def source(stream, phase, k, at):
        if phase == 0:
            if stream == 0:
                return g_ref.at[2 * k, :, :, at]
            if stream == 1:
                return g_ref.at[2 * k + 1, :, at]
            return gain_ref.at[:, :, at]
        if phase == 1:
            return acc[stream].at[k, :, at]
        return acc[stream].at[k, at, here[orders[stream][1]]]

    def copies(stream, phase, k):
        axis = orders[stream][phase]
        for shift in range(1, grid[axis]):
            at, target = device(axis, shift)
            yield pltpu.make_async_remote_copy(
                src_ref=source(stream, phase, k, at),
                dst_ref=land[phase][stream].at[k, shift - 1],
                send_sem=send_sem.at[stream, phase, k, shift - 1],
                recv_sem=recv_sem.at[stream, phase, k, shift - 1],
                device_id=target,
                device_id_type=MESH,
            )

    def own(stream, k):
        return pltpu.make_async_copy(
            source(stream, 0, k, here[orders[stream][0]]), acc[stream].at[k], own_sem.at[stream, k]
        )

    def launch(stream, phase, k):
        for copy in copies(stream, phase, k):
            copy.start()

    def absorb(stream, phase, k):
        axis = orders[stream][phase]
        if phase == 0:
            own(stream, k).wait()
        for copy in copies(stream, phase, k):
            copy.wait_recv()
        into = land[phase][stream]
        count = grid[axis] - 1
        if phase == 0:
            for a in range(acc[stream].shape[1]):
                for b in range(acc[stream].shape[2]):
                    total = acc[stream][k, a, b].astype(jnp.float32)
                    for s in range(count):
                        total += into[k, s, a, b].astype(jnp.float32)
                    acc[stream][k, a, b] = total.astype(acc[stream].dtype)
        elif phase == 1:
            mine = here[axis]
            for a in range(acc[stream].shape[1]):
                total = acc[stream][k, a, mine].astype(jnp.float32)
                for s in range(count):
                    total += into[k, s, a].astype(jnp.float32)
                acc[stream][k, a, mine] = total.astype(acc[stream].dtype)
        else:
            total = acc[stream][k, here[0], here[orders[stream][1]]].astype(jnp.float32)
            for s in range(count):
                total += into[k, s].astype(jnp.float32)
            if stream < 2:
                out_ref[2 * k + stream] = total
            else:
                gout_ref[...] = total

    own(2, 0).start()
    launch(2, 0, 0)

    def start_own(k, carry):
        for stream in (0, 1):
            own(stream, k).start()
        return carry

    for stream in (0, 1):
        launch(stream, 0, 0)
    lax.fori_loop(0, pairs, start_own, 0)

    def turn(t, carry):
        @pl.when(t + 1 < pairs)
        def _():
            for stream in (0, 1):
                launch(stream, 0, t + 1)

        @pl.when(t < pairs)
        def _():
            for stream in (0, 1):
                absorb(stream, 0, t)
                launch(stream, 1, t)

        @pl.when((t >= 1) & (t - 1 < pairs))
        def _():
            for stream in (0, 1):
                absorb(stream, 1, t - 1)
                launch(stream, 2, t - 1)

        @pl.when(t >= 2)
        def _():
            for stream in (0, 1):
                absorb(stream, 2, t - 2)

        return carry

    lax.fori_loop(0, pairs + 2, turn, 0)
    absorb(2, 0, 0)
    launch(2, 1, 0)
    absorb(2, 1, 0)
    launch(2, 2, 0)
    absorb(2, 2, 0)

    def finish(k, carry):
        for stream in (0, 1):
            for phase in range(3):
                for copy in copies(stream, phase, k):
                    copy.wait_send()
        return carry

    lax.fori_loop(0, pairs, finish, 0)
    for phase in range(3):
        for copy in copies(2, phase, 0):
            copy.wait_send()


def spread(grid, grads, gains):
    chunks, n, rows, width = grads.shape
    pairs = chunks // 2
    l0, l1, l2 = grid
    most = max(max(grid) - 1, 1)
    low = jnp.bfloat16
    shapes = ((pairs, rows, width, low), (pairs, rows, width, low), (1, 8, 128, jnp.float32))
    inner = ((l1, l2), (l2, l1), (l1, l2))
    acc, first, second, third = [], [], [], []
    for (count, r, w, dt), (kept, sent) in zip(shapes, inner):
        acc.append(pltpu.VMEM((count, l0, kept, r, w), dt))
        first.append(pltpu.VMEM((count, max(sent - 1, 1), l0, kept, r, w), dt))
        second.append(pltpu.VMEM((count, max(kept - 1, 1), l0, r, w), dt))
        third.append(pltpu.VMEM((count, max(l0 - 1, 1), r, w), dt))
    return pl.pallas_call(
        functools.partial(spread_kernel, grid, pairs),
        out_shape=(
            jax.ShapeDtypeStruct((chunks, rows, width), jnp.float32),
            jax.ShapeDtypeStruct((8, 128), jnp.float32),
        ),
        in_specs=[pl.BlockSpec(memory_space=pl.ANY)] * 2,
        out_specs=(pl.BlockSpec(memory_space=pltpu.VMEM),) * 2,
        scratch_shapes=acc
        + first
        + second
        + third
        + [
            pltpu.SemaphoreType.DMA((3, 3, pairs, most)),
            pltpu.SemaphoreType.DMA((3, 3, pairs, most)),
            pltpu.SemaphoreType.DMA((3, pairs)),
        ],
        compiler_params=pltpu.CompilerParams(
            collective_id=0, has_side_effects=True, vmem_limit_bytes=60 * 1024 * 1024
        ),
        cost_estimate=pl.CostEstimate(flops=0, bytes_accessed=grads.size * 4, transcendentals=0),
    )(grads.reshape(chunks, l0, l1, l2, rows, width), gains.reshape(l0, l1, l2, 8, 128))


def from_behind(x, axis, by):
    devices = lax.axis_size(axis)
    pairs = [(i, i + by) for i in range(devices) if 0 <= i + by < devices]
    return lax.ppermute(x, axis, pairs)


def layer_norm(values, gain):
    row_mean = jnp.mean(values, axis=-1, keepdims=True)
    centred = values - row_mean
    row_var = jnp.mean(centred * centred, axis=-1, keepdims=True)
    return centred * lax.rsqrt(row_var + epsilon) * gain


def front_half(all_rows, gain_attn, w_qkv):
    normed = layer_norm(all_rows, gain_attn).astype(jnp.bfloat16)
    projected = jnp.dot(normed, w_qkv, preferred_element_type=jnp.float32).astype(jnp.bfloat16)
    return (normed, projected)


def latent_operand(projected, tok_rows, model_width):
    return projected[tok_rows:, model_width:]


def back_half(all_rows, projected, remote_rows, allowed, weights):
    gain_attn, w_qkv, w_out, gain_mlp, w_up, w_down = weights
    row_count, model_width = all_rows.shape
    head_size = model_width // HEADS
    remote_pairs = remote_rows[:, remote_rows.shape[1] - 2 * model_width :]
    queries = projected[:, :model_width].reshape(row_count, HEADS, head_size)
    key_rows = jnp.concatenate(
        [projected[:, model_width : 2 * model_width], remote_pairs[:, :model_width]], axis=0
    )
    value_rows = jnp.concatenate(
        [projected[:, 2 * model_width :], remote_pairs[:, model_width:]], axis=0
    )
    key_rows = key_rows.reshape(-1, HEADS, head_size)
    value_rows = value_rows.reshape(-1, HEADS, head_size)
    scores = jnp.einsum(
        "qhd,khd->hqk", queries, key_rows, preferred_element_type=jnp.float32
    ) * head_size ** (-0.5)
    attn_weights = jax.nn.softmax(jnp.where(allowed[None], scores, masked_score), axis=-1)
    attn_low = attn_weights.astype(jnp.bfloat16)
    mixed_low = jnp.einsum("hqk,khd->qhd", attn_low, value_rows, preferred_element_type=jnp.float32)
    mixed_low = mixed_low.reshape(row_count, model_width).astype(jnp.bfloat16)
    mid_rows = all_rows + jnp.dot(mixed_low, w_out, preferred_element_type=jnp.float32)
    normed_mlp = layer_norm(mid_rows, gain_mlp).astype(jnp.bfloat16)
    up_proj = jnp.dot(normed_mlp, w_up, preferred_element_type=jnp.float32)
    activated = jax.nn.gelu(up_proj).astype(jnp.bfloat16)
    result = mid_rows + jnp.dot(activated, w_down, preferred_element_type=jnp.float32)
    return dict(
        queries=queries,
        key_rows=key_rows,
        value_rows=value_rows,
        attn_weights=attn_weights,
        attn_low=attn_low,
        mixed_low=mixed_low,
        mid_rows=mid_rows,
        normed_mlp=normed_mlp,
        up_proj=up_proj,
        activated=activated,
        result=result,
    )


def section_backward(saved, d_result, all_rows, normed, allowed, weights, latent_start):
    gain_attn, w_qkv, w_out, gain_mlp, w_up, w_down = weights
    row_count, model_width = all_rows.shape
    head_size = model_width // HEADS
    score_scale = head_size ** (-0.5)
    d_low = d_result.astype(jnp.bfloat16)
    grad_down = jnp.dot(d_low.T, saved["activated"], preferred_element_type=jnp.float32)
    d_activated = jnp.dot(d_low, w_down.T, preferred_element_type=jnp.float32)
    unused_up, gelu_back = jax.vjp(jax.nn.gelu, saved["up_proj"])
    d_up = gelu_back(d_activated)[0].astype(jnp.bfloat16)
    grad_up = jnp.dot(d_up.T, saved["normed_mlp"], preferred_element_type=jnp.float32)
    d_normed_mlp = jnp.dot(d_up, w_up.T, preferred_element_type=jnp.float32)
    unused_mid, second_back = jax.vjp(layer_norm, saved["mid_rows"], gain_mlp)
    d_mid_norm, grad_gain_mlp = second_back(d_normed_mlp)
    d_mid = d_result + d_mid_norm
    d_mid_low = d_mid.astype(jnp.bfloat16)
    grad_out = jnp.dot(d_mid_low.T, saved["mixed_low"], preferred_element_type=jnp.float32)
    d_mixed = jnp.dot(d_mid_low, w_out.T, preferred_element_type=jnp.float32).astype(jnp.bfloat16)
    d_mixed = d_mixed.reshape(row_count, HEADS, head_size)
    d_weights = jnp.einsum(
        "qhd,khd->hqk", d_mixed, saved["value_rows"], preferred_element_type=jnp.float32
    )
    d_values = jnp.einsum(
        "hqk,qhd->khd", saved["attn_low"], d_mixed, preferred_element_type=jnp.float32
    )
    attn_weights = saved["attn_weights"]
    d_scores = attn_weights * (
        d_weights - jnp.sum(attn_weights * d_weights, axis=-1, keepdims=True)
    )
    d_scores_low = jnp.where(allowed[None], d_scores, 0.0).astype(jnp.bfloat16)
    d_queries = (
        jnp.einsum(
            "hqk,khd->qhd", d_scores_low, saved["key_rows"], preferred_element_type=jnp.float32
        )
        * score_scale
    )
    d_keys = (
        jnp.einsum(
            "hqk,qhd->khd", d_scores_low, saved["queries"], preferred_element_type=jnp.float32
        )
        * score_scale
    )
    remote_part = jnp.concatenate(
        [
            d_keys[row_count:].reshape(-1, model_width),
            d_values[row_count:].reshape(-1, model_width),
        ],
        axis=1,
    )
    own_part = lax.psum_scatter(remote_part, "dp", scatter_dimension=0, tiled=True)
    local_pairs = jnp.concatenate(
        [
            d_keys[:row_count].reshape(row_count, model_width),
            d_values[:row_count].reshape(row_count, model_width),
        ],
        axis=1,
    )
    local_pairs = jnp.concatenate(
        [local_pairs[:latent_start], local_pairs[latent_start:] + own_part], axis=0
    )
    d_projected = jnp.concatenate(
        [d_queries.reshape(row_count, model_width), local_pairs], axis=1
    ).astype(jnp.bfloat16)
    grad_qkv = jnp.dot(d_projected.T, normed, preferred_element_type=jnp.float32)
    d_normed = jnp.dot(d_projected, w_qkv.T, preferred_element_type=jnp.float32)
    unused_rows, first_back = jax.vjp(layer_norm, all_rows, gain_attn)
    d_rows_norm, grad_gain_attn = first_back(d_normed)
    return (
        d_mid + d_rows_norm,
        (grad_gain_attn, grad_qkv, grad_out, grad_gain_mlp, grad_up, grad_down),
    )


def packed(grads, n):
    gain_first, qkv_grad, out_grad, gain_second, up_grad, down_grad = grads
    width = out_grad.shape[0]
    rows = width // n

    def by_rows(grad):
        return grad.reshape(n, -1, rows, width).transpose(1, 0, 2, 3).astype(jnp.bfloat16)

    down = down_grad.reshape(n, rows, -1, width).transpose(2, 0, 1, 3).astype(jnp.bfloat16)
    chunks = jnp.concatenate([down, by_rows(up_grad), by_rows(out_grad), by_rows(qkv_grad)], axis=0)
    gains = jnp.stack([gain_first.reshape(n, rows), gain_second.reshape(n, rows)], axis=1)
    return chunks, jnp.pad(gains, ((0, 0), (0, 6), (0, 128 - rows)))


def shards(
    grid,
    tokens,
    latents,
    slot_group,
    image_groups,
    gain_attn,
    w_qkv,
    w_out,
    gain_mlp,
    w_up,
    w_down,
    d_tokens,
    d_latents,
):
    micro = tokens.shape[0]
    tok_rows = tokens.shape[1]
    lat_rows = latents.shape[1]
    model_width = tokens.shape[2]
    local_groups = tok_rows // GROUP
    section_index = lax.axis_index("section")
    is_global = section_index == 1
    dp_index = lax.axis_index("dp")
    weights = (gain_attn[0], w_qkv[0], w_out[0], gain_mlp[0], w_up[0], w_down[0])
    image_ends = jnp.cumsum(image_groups, axis=1)
    slot_images = jnp.sum(
        (image_ends[:, None, :] <= slot_group[:, :, None]).astype(jnp.int32), axis=2
    )
    slot_total = slot_group.shape[1]
    row_group = jnp.concatenate([jnp.arange(tok_rows) // GROUP, jnp.arange(lat_rows) // LAT])
    row_latent = jnp.concatenate(
        [jnp.zeros((tok_rows,), jnp.bool_), jnp.ones((lat_rows,), jnp.bool_)]
    )
    same_group = row_group[:, None] == row_group[None, :]
    local_mask = jnp.where(
        is_global, (~row_latent)[:, None] & row_latent[None, :] & same_group, same_group
    )
    group_match = row_group[:, None] == jnp.arange(local_groups)[None, :]

    def key_images(batch):
        images_row = lax.dynamic_index_in_dim(slot_images, batch, 0, keepdims=False)
        return (images_row, jnp.broadcast_to(images_row[:, None], (slot_total, LAT)).reshape(-1))

    def allowed_for(batch):
        images_row, key_image = key_images(batch)
        own_images = lax.dynamic_slice_in_dim(images_row, dp_index * local_groups, local_groups)
        row_image = jnp.sum(jnp.where(group_match, own_images[None, :], 0), axis=1)
        remote_mask = is_global & row_latent[:, None] & (row_image[:, None] == key_image[None, :])
        return jnp.concatenate([local_mask, remote_mask], axis=1)

    def forward_turn(received, turn):
        recv_tokens, recv_latents = received
        batch = jnp.clip(turn - section_index, 0, micro - 1)
        own_tok = lax.dynamic_index_in_dim(tokens, batch, 0, keepdims=False)
        own_lat = lax.dynamic_index_in_dim(latents, batch, 0, keepdims=False)
        input_rows = jnp.concatenate(
            [
                jnp.where(is_global, recv_tokens, own_tok),
                jnp.where(is_global, recv_latents, own_lat),
            ],
            axis=0,
        )
        all_rows = input_rows.astype(jnp.float32)
        normed, projected = front_half(all_rows, weights[0], weights[1])
        remote_rows = lax.all_gather(
            latent_operand(projected, tok_rows, model_width), "dp", axis=0, tiled=True
        )
        saved = back_half(all_rows, projected, remote_rows, allowed_for(batch), weights)
        result = saved["result"]
        result_low = result.astype(jnp.bfloat16)
        stored = jnp.where(is_global, result, result_low.astype(jnp.float32))
        passed_on = from_behind((result_low[:tok_rows], result_low[tok_rows:]), "section", 1)
        return passed_on, (input_rows, stored[:tok_rows], stored[tok_rows:])

    nothing = (
        jnp.zeros((tok_rows, model_width), jnp.bfloat16),
        jnp.zeros((lat_rows, model_width), jnp.bfloat16),
    )
    turns = jnp.arange(micro + 1)
    unused_end, (kept_rows, tok_outputs, lat_outputs) = lax.scan(forward_turn, nothing, turns)

    def backward_turn(carry, turn):
        (recv_grad_tok, recv_grad_lat), totals = carry
        raw_batch = micro - turn - section_index
        valid = ((raw_batch >= 0) & (raw_batch < micro)).astype(jnp.float32)
        batch = jnp.clip(raw_batch, 0, micro - 1)
        all_rows = lax.dynamic_index_in_dim(
            kept_rows, batch + section_index, 0, keepdims=False
        ).astype(jnp.float32)
        normed, projected = front_half(all_rows, weights[0], weights[1])
        remote_rows = lax.all_gather(
            latent_operand(projected, tok_rows, model_width), "dp", axis=0, tiled=True
        )
        allowed = allowed_for(batch)
        saved = back_half(all_rows, projected, remote_rows, allowed, weights)
        given = (
            jnp.concatenate(
                [
                    lax.dynamic_index_in_dim(d_tokens, batch, 0, keepdims=False),
                    lax.dynamic_index_in_dim(d_latents, batch, 0, keepdims=False),
                ],
                axis=0,
            )
            * valid
        )
        passed = jnp.concatenate([recv_grad_tok, recv_grad_lat], axis=0).astype(jnp.float32)
        d_result = jnp.where(is_global, given, passed)
        d_rows, grads = section_backward(
            saved, d_result, all_rows, normed, allowed, weights, tok_rows
        )
        totals = tuple((accum + piece for accum, piece in zip(totals, grads)))
        d_rows_low = d_rows.astype(jnp.bfloat16)
        stored = jnp.where(is_global, d_rows_low.astype(jnp.float32), d_rows)
        sent = from_behind((d_rows_low[:tok_rows], d_rows_low[tok_rows:]), "section", -1)
        return (sent, totals), (stored[:tok_rows], stored[tok_rows:])

    totals = tuple(
        jnp.zeros(w.shape[::-1] if w.ndim == 2 else w.shape, jnp.float32) for w in weights
    )
    (unused_sent, totals), (tok_grads, lat_grads) = lax.scan(
        backward_turn, (nothing, totals), turns
    )
    chunks, gains = packed(totals, lax.axis_size("dp"))
    summed, gain_sums = spread(grid, chunks, gains)
    rows = summed.shape[1]
    layer_tokens = lax.dynamic_slice_in_dim(tok_outputs, section_index, micro, 0)[None]
    layer_latents = lax.dynamic_slice_in_dim(lat_outputs, section_index, micro, 0)[None]
    grad_tokens = lax.dynamic_slice_in_dim(tok_grads, 1 - section_index, micro, 0)[::-1][
        None
    ]
    grad_latents = lax.dynamic_slice_in_dim(lat_grads, 1 - section_index, micro, 0)[
        ::-1
    ][None]
    return (
        layer_tokens,
        layer_latents,
        grad_tokens,
        grad_latents,
        gain_sums[0:1, :rows],
        summed[9:].reshape(-1, model_width).T[None],
        summed[8].T[None],
        gain_sums[1:2, :rows],
        summed[4:8].reshape(-1, model_width).T[None],
        summed[0:4].transpose(0, 2, 1).reshape(-1, rows)[None],
    )


F32 = jnp.float32
LOW = jnp.bfloat16
HEAD_PAD = 16
TILE = 768


def nn(a, b):
    return jnp.dot(a, b, preferred_element_type=F32)


def nt(a, b):
    return lax.dot_general(a, b, (((1,), (1,)), ((), ())), preferred_element_type=F32)


def tn(a, b):
    return lax.dot_general(a, b, (((0,), (0,)), ((), ())), preferred_element_type=F32)


def row_mean(values):
    return jnp.mean(values, axis=-1, keepdims=True)


def row_stats(load, spans):
    means = [row_mean(load(r)) for r in spans]
    scales = []
    for r, mean in zip(spans, means):
        centred = load(r) - mean
        scales.append(lax.rsqrt(row_mean(centred * centred) + epsilon))
    return means, scales


def at(start, size):
    return pl.ds(pl.multiple_of(start, size), size)


def class_max(s):
    for by in (16, 32, 64):
        s = jnp.maximum(s, pltpu.roll(s, by, 1))
    return s


def class_sum(s):
    for by in (16, 32, 64):
        s = s + pltpu.roll(s, by, 1)
    return s


def layer_kernel(
    n,
    tokens,
    latents,
    slots,
    slot_at,
    image_at,
    gain_attn,
    gain_mlp,
    w_qkv,
    w_out,
    w_up,
    w_down,
    d_tokens,
    d_latents,
    out_tok,
    out_lat,
    grad_tok,
    grad_lat,
    grads,
    summed,
    gain_sums,
    wq,
    wo,
    wu,
    wd,
    xb,
    n1,
    proj,
    mixed,
    mid,
    n2,
    act,
    dup,
    yb,
    dy,
    ef,
    tmp,
    out,
    probs,
    probs_lat,
    scores,
    slopes,
    latf,
    mixf,
    key_mask,
    qbd,
    kbd,
    vbd,
    kv_all,
    kvg_send,
    kvg_recv,
    stage,
    gains,
    leaving,
    own_a,
    own_b,
    own_c,
    land1_a,
    land1_b,
    land1_c,
    land2_a,
    land2_b,
    land2_c,
    land3_a,
    land3_b,
    land3_c,
    land4_a,
    land4_b,
    land4_c,
    land_g,
    load_sem,
    stage_sem,
    own_sem,
    leave_sem,
    send_sem,
    recv_sem,
    gain_s,
    gain_r,
    relay_send,
    relay_recv,
    kv_sem_s,
    kv_sem_r,
    kvg_sem_s,
    kvg_sem_r,
):
    rows, width = xb.shape
    ff = act.shape[1]
    tok = tokens.shape[0]
    lat = latents.shape[0]
    half = lat // LAT
    pairs = width // 128
    me = lax.axis_index("dp")
    section = lax.axis_index("section")
    first = section == 0
    second = section == 1
    partner = (me, 1 - section)

    loads = [
        pltpu.make_async_copy(src, dst, load_sem.at[i])
        for i, (src, dst) in enumerate(((w_qkv, wq), (w_out, wo), (w_up, wu), (w_down, wd)))
    ]
    x_loads = [
        pltpu.make_async_copy(tokens, xb.at[lat:rows], load_sem.at[4]),
        pltpu.make_async_copy(latents, xb.at[0:lat], load_sem.at[5]),
    ]
    e_loads = [
        pltpu.make_async_copy(d_tokens, ef.at[lat:rows], load_sem.at[6]),
        pltpu.make_async_copy(d_latents, ef.at[0:lat], load_sem.at[7]),
    ]

    @pl.when(first)
    def _():
        for copy in x_loads:
            copy.start()

    for copy in loads:
        copy.start()

    @pl.when(second)
    def _():
        for copy in e_loads:
            copy.start()

    barrier = pltpu.get_barrier_semaphore()
    pl.semaphore_signal(barrier, inc=1, device_id=partner, device_id_type=MESH)

    here = [lax.rem(me // (1 << bit), 2) for bit in range(4)]

    def across(bit):
        return (me + (1 - 2 * here[bit]) * (1 << bit), section)

    @pl.when(second)
    def _():
        for shift in range(1, n):
            pl.semaphore_signal(
                barrier, inc=1, device_id=(lax.rem(me + shift, n), section), device_id_type=MESH
            )
        pl.semaphore_wait(barrier, n)

    @pl.when(first)
    def _():
        for bit in range(4):
            pl.semaphore_signal(barrier, inc=1, device_id=across(bit), device_id_type=MESH)
        pl.semaphore_wait(barrier, 5)

    def relay(back, band):
        low, high = ((0, rows // 3), (rows // 3, 2 * rows // 3), (2 * rows // 3, rows))[band]
        if not back:
            low, high = ((0, lat), (lat, lat + GROUP), (lat + GROUP, rows))[band]
        return pltpu.make_async_remote_copy(
            src_ref=yb.at[low:high],
            dst_ref=(dy if back else xb).at[low:high],
            send_sem=relay_send.at[3 * back + band],
            recv_sem=relay_recv.at[3 * back + band],
            device_id=partner,
            device_id_type=MESH,
        )

    def kv_copy(shift, incoming):
        slot = lax.rem(me + n - shift, n) if incoming else me
        return pltpu.make_async_remote_copy(
            src_ref=kv_all.at[me], dst_ref=kv_all.at[slot],
            send_sem=kv_sem_s.at[shift - 1], recv_sem=kv_sem_r.at[shift - 1],
            device_id=(lax.rem(me + shift, n), section), device_id_type=MESH,
        )

    def kvg_copy(shift):
        there = lax.rem(me + shift, n)
        return pltpu.make_async_remote_copy(
            src_ref=kvg_send.at[there], dst_ref=kvg_recv.at[shift - 1],
            send_sem=kvg_sem_s.at[shift - 1], recv_sem=kvg_sem_r.at[shift - 1],
            device_id=(there, section), device_id_type=MESH,
        )

    chunks = [slice(c, c + 64) for c in range(0, GROUP, 64)]
    lane = lax.broadcasted_iota(jnp.int32, (1, 128), 1)
    halves = [(lane < 64).astype(F32).astype(LOW), (lane >= 64).astype(F32).astype(LOW)]
    eighths = [(h.astype(F32) * 0.125).astype(LOW) for h in halves]
    heads = (
        lax.broadcasted_iota(jnp.int32, (HEAD_PAD, width), 1) // 64
        == lax.broadcasted_iota(jnp.int32, (HEAD_PAD, width), 0)
    ).astype(F32)

    def block_diagonal(dst, base, src, row, column, scale):
        for i in range(LAT):
            line = src[row + i : row + i + 1, column : column + width] * scale
            dst[base + i * HEAD_PAD : base + (i + 1) * HEAD_PAD, :] = (line * heads).astype(LOW)

    def head_sum(dst, row, column, value, scale, add):
        for i in range(LAT):
            line = jnp.sum(
                value[i * HEAD_PAD : (i + 1) * HEAD_PAD] * heads, axis=0, keepdims=True
            )
            line = line * scale
            if add:
                line = line + dst[row + i : row + i + 1, column : column + width]
            dst[row + i : row + i + 1, column : column + width] = line

    def bands(body, lo, hi, size):
        def one(i, carry):
            body(pl.ds(pl.multiple_of(lo + i * size, 16), size))
            return carry

        lax.fori_loop(0, (hi - lo) // size, one, 0)

    third = rows // 3

    def grouped(body, lo, hi, count):
        def one(i, carry):
            base = lo + i * 16 * count
            body([pl.ds(pl.multiple_of(base + 16 * g, 16), 16) for g in range(count)])
            return carry

        lax.fori_loop(0, (hi - lo) // (16 * count), one, 0)

    def norm(load, gain, dst, lo, hi, count):
        def body(spans):
            means, scales = row_stats(load, spans)
            for r, mean, scale in zip(spans, means, scales):
                dst[r, :] = ((load(r) - mean) * scale * gain[...]).astype(LOW)

        grouped(body, lo, hi, count)

    def norm_back(load, grad, gain, gain_rows, store, lo, hi, count):
        def body(spans):
            means, scales = row_stats(load, spans)
            firsts, seconds = [], []
            kept = gains[0, gain_rows, :]
            for r, mean, scale in zip(spans, means, scales):
                along = grad[r, :] * ((load(r) - mean) * scale)
                kept = kept + along[0:8] + along[8:16]
                firsts.append(row_mean(grad[r, :] * gain[...]))
                seconds.append(row_mean(along * gain[...]))
            gains[0, gain_rows, :] = kept
            for r, mean, scale, one, two in zip(spans, means, scales, firsts, seconds):
                hat = (load(r) - mean) * scale
                store(r, ef[r, :] + scale * (grad[r, :] * gain[...] - one - hat * two))

        grouped(body, lo, hi, count)

    def tiles(count, body, size=TILE):
        def one(i, carry):
            body(at(i * size, size))
            return carry

        lax.fori_loop(0, count, one, 0)

    @pl.when(first)
    def _():
        for copy in x_loads:
            copy.wait()

    @pl.when(second)
    def _():
        spots = lax.broadcasted_iota(jnp.int32, (n, n * lat), 1) // lat
        spread_out = (spots == lax.broadcasted_iota(jnp.int32, (n, n * lat), 0)).astype(F32)
        groups = nn(slots[...].astype(F32).astype(LOW), spread_out.astype(LOW))
        of_micro = lax.rem(lax.broadcasted_iota(jnp.int32, (1, n * lat), 1), lat) // LAT
        for m in range(half):
            images = jnp.zeros((1, n * lat), F32)
            own_image = jnp.float32(0)
            end = jnp.int32(0)
            for i in range(image_at.shape[1]):
                end = end + image_at[m, i]
                images += jnp.where(end.astype(F32) <= groups[m : m + 1], 1.0, 0.0)
                own_image += jnp.where(end <= slot_at[m, me], 1.0, 0.0)
            seen = (images == own_image) & (of_micro == m)
            key_mask[m : m + 1, :] = jnp.where(seen, 0.0, masked_score)

    def load_in(r):
        return xb[r, :].astype(F32)

    def load_mid(r):
        return mid[r, :]

    def lat_bias(m, shape, axis):
        return jnp.where(
            lax.broadcasted_iota(jnp.int32, shape, axis) // LAT == m, 0.0, masked_score
        ).astype(F32)

    @pl.when(first)
    def _():
        norm(load_in, gain_attn, n1, 0, rows, 11)
        loads[0].wait()

        def project(c):
            proj[:, c] = nn(n1[...], wq[:, c]).astype(LOW)

        tiles(3 * width // TILE, project)
        latf[...] = proj[0:lat, :].astype(F32)

        def one_pair(it, side):
            m, p = it // pairs, lax.rem(it, pairs)
            r = pl.ds(pl.multiple_of(lat + m * GROUP, 16), GROUP)
            q = proj[r, at(p * 128, 128)]
            k = proj[r, at(width + p * 128, 128)]
            v = proj[r, at(2 * width + p * 128, 128)]
            kl = proj[0:lat, at(width + p * 128, 128)]
            vl = proj[0:lat, at(2 * width + p * 128, 128)]
            bias = lat_bias(m, (lat, GROUP), 0)
            total = jnp.zeros((GROUP, 128), F32)
            for e in (0, 1):
                qe = q * eighths[e]
                s = scores.at[2 * side + e]
                s[...] = nt(k, qe)
                sl = nt(kl, qe) + bias
                top = jnp.max(sl, axis=0, keepdims=True)
                for c in chunks:
                    top = jnp.maximum(top, jnp.max(s[c, :], axis=0, keepdims=True))
                el = jnp.exp(sl - top)
                whole_sum = jnp.sum(el, axis=0, keepdims=True)
                for c in chunks:
                    et = jnp.exp(s[c, :] - top)
                    s[c, :] = et
                    whole_sum += jnp.sum(et, axis=0, keepdims=True)
                scale = 1.0 / whole_sum
                for c in chunks:
                    probs[2 * it + e, c, :] = (s[c, :] * scale).astype(LOW)
                pe = (el * scale).astype(LOW)
                probs[2 * it + e, GROUP : GROUP + lat, :] = pe
                total += tn(probs[2 * it + e, 0:GROUP, :], v * halves[e])
                total += tn(pe, vl * halves[e])
            mixed[r, at(p * 128, 128)] = total.astype(LOW)

        def pair(i, carry):
            one_pair(2 * i, 0)
            one_pair(2 * i + 1, 1)
            return carry

        lax.fori_loop(0, half * pairs // 2, pair, 0)
        for m in range(half):
            r = slice(lat + m * GROUP, lat + (m + 1) * GROUP)
            b = slice(m * 128, (m + 1) * 128)
            block_diagonal(qbd, m * 128, latf, m * LAT, 0, 0.125)
            s = nt(qbd[b, :], proj[r, width : 2 * width])
            sl = nt(qbd[b, :], proj[0:lat, width : 2 * width]) + lat_bias(m, (128, lat), 1)
            top = jnp.maximum(
                jnp.max(s, axis=1, keepdims=True), jnp.max(sl, axis=1, keepdims=True)
            )
            et = jnp.exp(s - top)
            el = jnp.exp(sl - top)
            scale = 1.0 / (
                jnp.sum(et, axis=1, keepdims=True) + jnp.sum(el, axis=1, keepdims=True)
            )
            pt = (et * scale).astype(LOW)
            pe = (el * scale).astype(LOW)
            probs_lat[b, 0:GROUP] = pt
            probs_lat[b, GROUP : GROUP + lat] = pe
            o = nn(pt, proj[r, 2 * width :]) + nn(pe, proj[0:lat, 2 * width :])
            head_sum(mixf, m * LAT, 0, o, 1.0, False)
        mixed[0:lat, :] = mixf[...].astype(LOW)

    keys = n * lat

    root = 0.7978845608028654

    def mlp_in(lo, hi, count, with_dact=False):
        r0 = slice(lo, hi)
        mid[r0, :] = xb[r0, :].astype(F32) + nn(mixed[r0, :], wo[...])

        norm(load_mid, gain_mlp, n2, lo, hi, count)

        def up_tile(dst, i):
            dst[r0, 0:512] = nn(n2[r0, :], wu[:, at(i * 512, 512)])

        def gelu(src, i):
            c = at(i * 512, 512)
            for g in range(lo, hi, 16):
                r = slice(g, g + 16)
                up = src[r, 0:512]
                square = up * up
                t = jnp.tanh(up * (root + (root * 0.044715) * square))
                gate = 0.5 + 0.5 * t
                value = up * gate
                slope = gate + (value + value) * (1.0 - gate) * (
                    root + (3.0 * root * 0.044715) * square
                )
                act[r, c] = value.astype(LOW)
                if with_dact:
                    slope = slope * dup[r, c].astype(F32)
                dup[r, c] = slope.astype(LOW)

        last = ff // 512 - 1

        def widen(i, carry):
            up_tile(out, 2 * i + 1)
            gelu(tmp, 2 * i)
            up_tile(tmp, jnp.minimum(2 * i + 2, last))
            gelu(out, 2 * i + 1)
            return carry

        up_tile(tmp, 0)
        lax.fori_loop(0, ff // 1024, widen, 0)

    out_copies = [
        pltpu.make_async_copy(out.at[lat:rows], out_tok, load_sem.at[8]),
        pltpu.make_async_copy(out.at[0:lat], out_lat, load_sem.at[9]),
    ]
    grad_copies = [
        pltpu.make_async_copy(out.at[lat:rows], grad_tok, load_sem.at[8]),
        pltpu.make_async_copy(out.at[0:lat], grad_lat, load_sem.at[9]),
    ]

    def layer_output(low, high, passed_on):
        r = slice(low, high)
        y = mid[r, :] + nn(act[r, :], wd[...])
        if passed_on:
            narrow_y = y.astype(LOW)
            yb[r, :] = narrow_y
            y = narrow_y.astype(F32)
        out[r, :] = y

    @pl.when(first)
    def _():
        for copy in loads[1:]:
            copy.wait()
        mlp_in(0, lat + GROUP, 17)
        layer_output(0, lat + GROUP, True)
        relay(0, 0).start()
        relay(0, 1).start()
        mlp_in(lat + GROUP, rows, 16)
        layer_output(lat + GROUP, rows, True)
        relay(0, 2).start()
        for copy in out_copies:
            copy.start()

    @pl.when(second)
    def _():
        for copy in e_loads:
            copy.wait()

        def narrow_e(r):
            dy[r, :] = ef[r, :].astype(LOW)

        bands(narrow_e, 0, rows, third)
        for copy in loads:
            copy.wait()

        def early(c):
            dup[:, c] = nt(dy[...], wd[c, :]).astype(LOW)

        tiles(ff // TILE, early)
        relay(0, 0).wait_recv()
        norm(load_in, gain_attn, n1, 0, lat, 1)
        lat_proj = nn(n1[0:lat, :], wq[...]).astype(LOW)
        kv_all[me] = lat_proj[:, width:]
        latf[...] = lat_proj.astype(F32)
        for shift in range(1, n):
            kv_copy(shift, False).start()
        for m in range(half):
            relay(0, 1 + m).wait_recv()
            low, high = lat + m * GROUP, lat + (m + 1) * GROUP
            r = slice(low, high)
            b = slice(m * 128, (m + 1) * 128)
            norm(load_in, gain_attn, n1, low, high, 16)
            proj[r, :width] = nn(n1[r, :], wq[:, :width]).astype(LOW)
            block_diagonal(qbd, m * 128, latf, m * LAT, 0, 0.125)
            block_diagonal(kbd, m * 128, latf, m * LAT, width, 1.0)
            block_diagonal(vbd, m * 128, latf, m * LAT, 2 * width, 1.0)
            s = nt(proj[r, :width] * jnp.asarray(0.125, LOW), kbd[b, :])
            et = jnp.exp(s - class_max(s))
            pt = (et / class_sum(et)).astype(LOW)
            probs[m, 0:GROUP, 0:128] = pt
            mixed[r, :] = nn(pt, vbd[b, :]).astype(LOW)
            mlp_in(low, high, 16, True)
        for shift in range(1, n):
            kv_copy(shift, True).wait_recv()
        k = kv_all[:, :, :width].reshape(keys, width)
        v = kv_all[:, :, width:].reshape(keys, width)
        for m in range(half):
            b = slice(m * 128, (m + 1) * 128)
            s = nt(qbd[b, :], k) + key_mask[m : m + 1, :]
            et = jnp.exp(s - jnp.max(s, axis=1, keepdims=True))
            pt = (et / jnp.sum(et, axis=1, keepdims=True)).astype(LOW)
            probs_lat[b, 0:keys] = pt
            head_sum(mixf, m * LAT, 0, nn(pt, v), 1.0, False)
        mixed[0:lat, :] = mixf[...].astype(LOW)
        mlp_in(0, lat, 1, True)

    @pl.when(first)
    def _():
        for band in range(3):
            relay(1, band).wait_recv()

        def widen_e(r):
            ef[r, :] = dy[r, :].astype(F32)

        bands(widen_e, 0, rows, third)

    part = 384
    unit = width // n
    many = part // unit

    def staged(slot, piece, chunk, share):
        return pltpu.make_async_copy(
            stage.at[slot, piece],
            grads.at[
                chunk,
                share // 8,
                lax.rem(share // 4, 2),
                lax.rem(share // 2, 2),
                lax.rem(share, 2),
            ],
            stage_sem.at[slot, piece],
        )

    def drain(slot):
        def one(piece, carry):
            staged(slot, piece, 0, 0).wait()
            return carry

        lax.fori_loop(0, many, one, 0)

    def weight_grad(place, start, count, left, *rights, settled=True):
        def one(i, carry):
            turned = left(i).T
            for at_right, right in enumerate(rights):
                tile = i * len(rights) + at_right
                slot = lax.rem(tile, 2)
                value = nn(turned, right(i)).astype(LOW)

                if settled:

                    @pl.when(tile >= start * len(rights) + 2)
                    def _():
                        drain(slot)

                else:
                    drain(slot)

                for piece in range(many):
                    stage[slot, piece] = value[piece * unit : (piece + 1) * unit]
                    staged(slot, piece, *place(i, at_right, piece)).start()
            return carry

        lax.fori_loop(start, start + count, one, 0)

    def settle():
        for slot in (0, 1):
            drain(slot)

    orders = ((0, 2, 1, 3), (1, 0, 2, 3), (2, 1, 0, 3))
    kinds = (0, 1, 2)
    own_buf = (own_a, own_b, own_c)
    per_part = width // part
    wide = ff // width
    groups = land1_a.shape[0]
    land = (
        (land1_a, land1_b, land1_c),
        (land2_a, land2_b, land2_c),
        (land3_a, land3_b, land3_c),
        (land4_a, land4_b, land4_c),
    )

    def spot(kind, second_bit, third_bit):
        return (third_bit, second_bit) if kind == 1 else (second_bit, third_bit)

    def source(kind, phase, k, theirs):
        mine = [here[bit] for bit in orders[kind]]
        pick = [1 - bit for bit in mine] if theirs else mine
        base = land[0][kind]
        every = slice(None)
        if phase == 0:
            chunk = grads.at[3 * k + kind]
            return (chunk.at[:, :, :, pick[0]], chunk.at[:, :, pick[0]], chunk.at[:, pick[0]])[kind]
        if phase == 1:
            return base.at[(k, every, *spot(kind, pick[1], every))]
        if phase == 2:
            return base.at[(k, every, *spot(kind, mine[1], pick[2]))]
        return base.at[(k, pick[3], *spot(kind, mine[1], mine[2]))]

    def copy_of(kind, phase, k):
        return pltpu.make_async_remote_copy(
            src_ref=source(kind, phase, k, True),
            dst_ref=land[phase][kind].at[k],
            send_sem=send_sem.at[kind, phase, k],
            recv_sem=recv_sem.at[kind, phase, k],
            device_id=across(orders[kind][phase]),
            device_id_type=MESH,
        )

    def own(kind, k):
        return pltpu.make_async_copy(
            source(kind, 0, k, False), own_buf[kind], own_sem.at[kind]
        )

    def leave(kind, k):
        slot = lax.rem(k, 2)
        return pltpu.make_async_copy(
            leaving.at[slot, kind], summed.at[3 * k + kind], leave_sem.at[slot, kind]
        )

    def launch(*chunks):
        for chunk in chunks:
            copy_of(chunk % 3, 0, chunk // 3).start()

    def onward(phase, k):
        for kind in kinds:
            if phase == 0:
                own(kind, k).wait()
            copy_of(kind, phase, k).wait_recv()
            base, into = land[0][kind], land[phase][kind]
            mine = [here[bit] for bit in orders[kind]]
            if phase == 0:

                def add(i, carry):
                    for j in (0, 1):
                        for h in (0, 1):
                            total = own_buf[kind][i, j, h].astype(F32)
                            total += base[k, i, j, h].astype(F32)
                            base[k, i, j, h] = total.astype(LOW)
                    return carry

                lax.fori_loop(0, 2, add, 0)
            elif phase == 1:
                for i in (0, 1):
                    for h in (0, 1):
                        at_share = (k, i, *spot(kind, mine[1], h))
                        total = base[at_share].astype(F32) + into[k, i, h].astype(F32)
                        base[at_share] = total.astype(LOW)
            elif phase == 2:
                for i in (0, 1):
                    at_share = (k, i, *spot(kind, mine[1], mine[2]))
                    total = base[at_share].astype(F32) + into[k, i].astype(F32)
                    base[at_share] = total.astype(LOW)
            else:
                total = base[(k, mine[3], *spot(kind, mine[1], mine[2]))].astype(F32)
                total += into[k].astype(F32)
                slot = lax.rem(k, 2)

                @pl.when(k >= 2)
                def _():
                    leave(kind, k - 2).wait()

                leaving[slot, kind] = total
                leave(kind, k).start()
            if phase < 3:
                copy_of(kind, phase + 1, k).start()

    def begin():
        for kind in kinds:
            own(kind, 0).start()
        turn(0, 0)

    def turn(t, carry):
        for phase in range(4):
            k = t - phase

            @pl.when((k >= 0) & (k < groups))
            def _():
                onward(phase, k)
                if phase == 0:

                    @pl.when(k + 1 < groups)
                    def _():
                        for kind in kinds:
                            own(kind, k + 1).start()

        return carry

    def up_grad():
        weight_grad(
            lambda i, right, piece: (
                wide + lax.rem(i * many + piece, wide),
                (i * many + piece) // wide,
            ),
            0,
            ff // part,
            lambda i: dup[:, at(i * part, part)],
            lambda i: n2[...],
        )
    def down_grad(pair, settled):
        weight_grad(
            lambda i, right, piece: (2 * pair + right, i * many + piece),
            0,
            per_part,
            lambda i: dy[:, at(i * part, part)],
            lambda i: act[:, 2 * pair * width : (2 * pair + 1) * width],
            lambda i: act[:, (2 * pair + 1) * width : (2 * pair + 2) * width],
            settled=settled,
        )

    down_grad(0, True)
    down_grad(1, False)
    launch(0, 1)

    @pl.when(first)
    def _():
        def unwiden(c):
            dup[:, c] = (nt(dy[...], wd[c, :]) * dup[:, c].astype(F32)).astype(LOW)

        tiles(ff // TILE, unwiden)

    settle()
    launch(2, 3)
    up_grad()

    def to_mid(c):
        tmp[:, c] = nt(dup[...], wu[c, :])

    tiles(width // 256, to_mid, 256)
    settle()
    launch(*range(wide, 2 * wide))
    gains[0] = jnp.zeros_like(gains[0])

    def store_mid(r, total):
        ef[r, :] = total
        dy[r, :] = total.astype(LOW)

    norm_back(load_mid, tmp, gain_mlp, slice(8, 16), store_mid, 0, rows, 11)

    @pl.when(first)
    def _():
        for band in range(3):
            relay(0, band).wait_send()

    def to_mix(c):
        yb[:, c] = nt(dy[...], wo[c, :]).astype(LOW)

    tiles(width // TILE, to_mix)
    mixf[...] = yb[0:lat, :].astype(F32)

    @pl.when(second)
    def _():
        k = kv_all[:, :, :width].reshape(keys, width)
        v = kv_all[:, :, width:].reshape(keys, width)
        for m in range(half):
            b = slice(m * 128, (m + 1) * 128)
            block_diagonal(vbd.at[pl.ds(256, 256)], m * 128, mixf, m * LAT, 0, 1.0)
        both = slice(0, half * 128)
        do = vbd[256 : 256 + half * 128, :]
        pt = probs_lat[both, 0:keys]
        pf = pt.astype(F32)
        dp = nt(do, v)
        along = jnp.sum(pf * dp, axis=1, keepdims=True)
        ds = (pf * (dp - along)).astype(LOW)
        kvg_send[:, :, :width] = tn(ds, qbd[both, :]).astype(LOW).reshape(n, lat, width)
        kvg_send[:, :, width:] = tn(pt, do).astype(LOW).reshape(n, lat, width)
        for shift in range(1, n):
            kvg_copy(shift).start()
        dq = nn(ds, k)
        for m in range(half):
            head_sum(latf, m * LAT, 0, dq[m * 128 : (m + 1) * 128], 0.125, False)
        proj[0:lat, :width] = latf[:, :width].astype(LOW)
        layer_output(0, lat + GROUP, False)
        layer_output(lat + GROUP, rows, False)
        for copy in out_copies:
            copy.start()

    weight_grad(
        lambda i, right, piece: (2 * wide, i * many + piece),
        0,
        width // part,
        lambda i: dy[:, at(i * part, part)],
        lambda i: mixed[...],
    )
    for copy in out_copies:
        copy.wait()

    @pl.when(first)
    def _():
        for m in range(half):
            r = slice(lat + m * GROUP, lat + (m + 1) * GROUP)
            b = slice(m * 128, (m + 1) * 128)
            block_diagonal(vbd, m * 128, mixf, m * LAT, 0, 1.0)
            do = vbd[b, :]
            dp = nt(do, proj[r, 2 * width :])
            dl = nt(do, proj[0:lat, 2 * width :])
            pt = probs_lat[b, 0:GROUP]
            pe = probs_lat[b, GROUP : GROUP + lat]
            pf = pt.astype(F32)
            pg = pe.astype(F32)
            along = jnp.sum(pf * dp, axis=1, keepdims=True) + jnp.sum(
                pg * dl, axis=1, keepdims=True
            )
            ds = (pf * (dp - along)).astype(LOW)
            dsl = (pg * (dl - along)).astype(LOW)
            dq = nn(ds, proj[r, width : 2 * width]) + nn(dsl, proj[0:lat, width : 2 * width])
            head_sum(latf, m * LAT, 0, dq, 0.125, False)
            tmp[r, :] = tn(ds, qbd[b, :])
            out[r, :] = tn(pt, do)
            if m == 0:
                tmp[0:lat, :] = tn(dsl, qbd[b, :])
                out[0:lat, :] = tn(pe, do)
            else:
                tmp[0:lat, :] += tn(dsl, qbd[b, :])
                out[0:lat, :] += tn(pe, do)
        proj[0:lat, :width] = latf[:, :width].astype(LOW)
        settle()
        launch(2 * wide)

        def one_pair(it, side):
            m, p = it // pairs, lax.rem(it, pairs)
            r = pl.ds(pl.multiple_of(lat + m * GROUP, 16), GROUP)
            qc = at(p * 128, 128)
            q = proj[r, qc]
            k = proj[r, at(width + p * 128, 128)]
            v = proj[r, at(2 * width + p * 128, 128)]
            kl = proj[0:lat, at(width + p * 128, 128)]
            vl = proj[0:lat, at(2 * width + p * 128, 128)]
            dx = yb[r, qc]
            dq = jnp.zeros((GROUP, 128), F32)
            dk = tmp[r, qc]
            dv = out[r, qc]
            dkl = tmp[0:lat, qc]
            dvl = out[0:lat, qc]
            for e in (0, 1):
                qe = q * eighths[e]
                de = dx * halves[e]
                s = scores.at[2 * side + e]
                s[...] = nt(v, de)
                dl = nt(vl, de)
                pt = probs[2 * it + e, 0:GROUP, :]
                pe = probs[2 * it + e, GROUP : GROUP + lat, :]
                pg = pe.astype(F32)
                along = jnp.sum(pg * dl, axis=0, keepdims=True)
                for c in chunks:
                    pf = probs[2 * it + e, c, :].astype(F32)
                    along += jnp.sum(pf * s[c, :], axis=0, keepdims=True)
                for c in chunks:
                    pf = probs[2 * it + e, c, :].astype(F32)
                    slopes[2 * side + e, c, :] = (pf * (s[c, :] - along)).astype(LOW)
                ds = slopes[2 * side + e]
                dsl = (pg * (dl - along)).astype(LOW)
                dq += tn(ds, k * halves[e]) + tn(dsl, kl * halves[e])
                dk += nn(ds, qe)
                dkl += nn(dsl, qe)
                dv += nn(pt, de)
                dvl += nn(pe, de)
            proj[r, qc] = (dq * 0.125).astype(LOW)
            proj[r, at(width + p * 128, 128)] = dk.astype(LOW)
            proj[r, at(2 * width + p * 128, 128)] = dv.astype(LOW)
            tmp[0:lat, qc] = dkl
            out[0:lat, qc] = dvl

        def pair(i, carry):
            one_pair(2 * i, 0)
            one_pair(2 * i + 1, 1)
            return carry

        lax.fori_loop(0, half * pairs // 2, pair, 0)
        proj[0:lat, width : 2 * width] = tmp[0:lat, :].astype(LOW)
        proj[0:lat, 2 * width :] = out[0:lat, :].astype(LOW)

    @pl.when(second)
    def _():
        for m in range(half):
            r = slice(lat + m * GROUP, lat + (m + 1) * GROUP)
            b = slice(m * 128, (m + 1) * 128)
            pt = probs[m, 0:GROUP, 0:128]
            pf = pt.astype(F32)
            dx = yb[r, :]
            dp = nt(dx, vbd[b, :])
            ds = (pf * (dp - class_sum(pf * dp))).astype(LOW)
            dk = tn(ds, proj[r, :width])
            dv = tn(pt, dx)
            proj[r, :width] = (nn(ds, kbd[b, :]) * 0.125).astype(LOW)
            head_sum(latf, m * LAT, width, dk, 0.125, False)
            head_sum(latf, m * LAT, 2 * width, dv, 1.0, False)
        settle()
        launch(2 * wide)
        total = latf[:, width:] + kvg_send[me].astype(F32)
        for shift in range(1, n):
            kvg_copy(shift).wait_recv()
            total += kvg_recv[shift - 1].astype(F32)
        proj[0:lat, width:] = total.astype(LOW)

    def qkv_grad(start, count, r):
        weight_grad(
            lambda i, right, piece: (
                2 * wide + 1 + lax.rem(i * many + piece, 3),
                (i * many + piece) // 3,
            ),
            start,
            count,
            lambda i: proj[r, at(i * part, part)],
            lambda i: n1[r, :],
        )

    @pl.when(first)
    def _():
        qkv_grad(0, 3 * per_part, slice(0, rows))
        settle()
        launch(*range(2 * wide + 1, 2 * wide + 4))
        begin()

    @pl.when(first)
    def _():
        def to_in(c):
            tmp[:, c] = nt(proj[...], wq[c, :])

        tiles(width // 256, to_in, 256)

    @pl.when(second)
    def _():
        tmp[...] = nt(proj[:, :width], wq[:, :width])
        tmp[0:lat, :] += nt(proj[0:lat, width:], wq[:, width:])

    def store_in(r, total):
        low = total.astype(LOW)
        yb[r, :] = low
        out[r, :] = jnp.where(first, total, low.astype(F32))

    for band in range(3):
        norm_back(
            load_in, tmp, gain_attn, slice(0, 8), store_in, band * third, (band + 1) * third, 11
        )

        @pl.when(second)
        def _():
            relay(1, band).start()

    for copy in grad_copies:
        copy.start()

    @pl.when(second)
    def _():
        qkv_grad(0, per_part, slice(0, rows))
        settle()
        qkv_grad(per_part, 2 * per_part, slice(0, lat))
        settle()
        launch(*range(2 * wide + 1, 2 * wide + 4))
        begin()

    def gain_copy(bit):
        return pltpu.make_async_remote_copy(
            src_ref=gains.at[bit],
            dst_ref=land_g.at[bit],
            send_sem=gain_s.at[bit],
            recv_sem=gain_r.at[bit],
            device_id=across(bit),
            device_id_type=MESH,
        )

    def gain_step(bit):
        gain_copy(bit).wait_recv()
        gains[bit + 1] = gains[bit] + land_g[bit]

    gain_copy(0).start()

    def turn_with_gains(t, carry):
        turn(t, 0)
        for bit in range(4):

            @pl.when(t == bit + 2)
            def _():
                gain_step(bit)
                if bit < 3:
                    gain_copy(bit + 1).start()

        return carry

    lax.fori_loop(1, groups + 3, turn_with_gains, 0)
    final = gains[4]
    for i in (0, 1):
        whole_gain = jnp.sum(final[8 * i : 8 * i + 8], axis=0, keepdims=True)
        whole_gain = jnp.broadcast_to(whole_gain, (8, width))
        rolled = pltpu.roll(whole_gain, lax.rem(width - me * unit, width), 1)
        gain_sums[8 * i : 8 * i + 8, :] = rolled[:, 0:128]

    def finish(kind):
        def one(k, carry):
            for phase in range(4):
                copy_of(kind, phase, k).wait_send()
            return carry

        lax.fori_loop(0, land[0][kind].shape[0], one, 0)

    for kind in range(3):
        finish(kind)
    for bit in range(4):
        gain_copy(bit).wait_send()
    for copy in grad_copies:
        copy.wait()
    for kind in range(3):
        count = land[0][kind].shape[0]
        for k in (count - 2, count - 1):
            leave(kind, k).wait()

    @pl.when(second)
    def _():
        for band in range(3):
            relay(1, band).wait_send()
        for shift in range(1, n):
            kv_copy(shift, False).wait_send()
            kvg_copy(shift).wait_send()


def both_layers(n, tokens, latents, slots, images, gains, weights, d_tokens, d_latents):
    tok, width = tokens.shape
    lat = latents.shape[0]
    rows = tok + lat
    w_qkv, w_out, w_up, w_down = weights
    ff = w_up.shape[1]
    keys = n * lat
    half = lat // LAT
    size = sum(w.size for w in weights)
    chunks = size // (width * width)
    most = chunks // 3
    unit = width // n
    vm, hbm = pl.BlockSpec(memory_space=pltpu.VMEM), pl.BlockSpec(memory_space=pl.ANY)
    sm = pl.BlockSpec(memory_space=pltpu.SMEM)
    scratch = [
        pltpu.VMEM(w.shape, LOW) for w in (w_qkv, w_out, w_up, w_down)
    ] + [
        pltpu.VMEM(shape, dtype)
        for shape, dtype in (
            ((rows, width), LOW),
            ((rows, width), LOW),
            ((rows, 3 * width), LOW),
            ((rows, width), LOW),
            ((rows, width), F32),
            ((rows, width), LOW),
            ((rows, ff), LOW),
            ((rows, ff), LOW),
            ((rows, width), LOW),
            ((rows, width), LOW),
            ((rows, width), F32),
            ((rows, width), F32),
            ((rows, width), F32),
            ((half * width // 64, GROUP + lat, GROUP), LOW),
            ((half * 128, max(keys, GROUP + 128)), LOW),
            ((4, GROUP, GROUP), F32),
            ((4, GROUP, GROUP), LOW),
            ((lat, 3 * width), F32),
            ((lat, width), F32),
            ((8, keys), F32),
            ((half * 128, width), LOW),
            ((half * 128, width), LOW),
            ((half * 256, width), LOW),
            ((n, lat, 2 * width), LOW),
            ((n, lat, 2 * width), LOW),
            ((n - 1, lat, 2 * width), LOW),
            ((2, 384 // unit, unit, width), LOW),
            ((5, 16, width), F32),
            ((2, 3, unit, width), F32),
            ((2, 2, 2, unit, width), LOW),
            ((2, 2, 2, unit, width), LOW),
            ((2, 2, 2, unit, width), LOW),
            *(
                ((chunks // 3, *shape, unit, width), LOW)
                for shape in ((2, 2, 2), (2, 2), (2,), ())
                for unused_kind in range(3)
            ),
            ((4, 16, width), F32),
        )
    ] + [
        pltpu.SemaphoreType.DMA((10,)),
        pltpu.SemaphoreType.DMA((2, 384 // unit)),
        pltpu.SemaphoreType.DMA((3,)),
        pltpu.SemaphoreType.DMA((2, 3)),
        pltpu.SemaphoreType.DMA((3, 4, most)),
        pltpu.SemaphoreType.DMA((3, 4, most)),
        pltpu.SemaphoreType.DMA((4,)),
        pltpu.SemaphoreType.DMA((4,)),
        pltpu.SemaphoreType.DMA((6,)),
        pltpu.SemaphoreType.DMA((6,)),
        pltpu.SemaphoreType.DMA((n - 1,)),
        pltpu.SemaphoreType.DMA((n - 1,)),
        pltpu.SemaphoreType.DMA((n - 1,)),
        pltpu.SemaphoreType.DMA((n - 1,)),
    ]
    return pl.pallas_call(
        functools.partial(layer_kernel, n),
        out_shape=(
            jax.ShapeDtypeStruct((tok, width), F32),
            jax.ShapeDtypeStruct((lat, width), F32),
            jax.ShapeDtypeStruct((tok, width), F32),
            jax.ShapeDtypeStruct((lat, width), F32),
            jax.ShapeDtypeStruct((chunks, 2, 2, 2, 2, unit, width), LOW),
            jax.ShapeDtypeStruct((chunks, unit, width), F32),
            jax.ShapeDtypeStruct((16, 128), F32),
        ),
        in_specs=[hbm, hbm, vm, sm, sm, vm, vm] + [hbm] * 6,
        out_specs=(hbm,) * 6 + (vm,),
        scratch_shapes=scratch,
        compiler_params=pltpu.CompilerParams(
            collective_id=1, has_side_effects=True, vmem_limit_bytes=63 * 1024 * 1024
        ),
        cost_estimate=pl.CostEstimate(
            flops=6 * rows * size, bytes_accessed=4 * size, transcendentals=0
        ),
    )(tokens, latents, slots, slots, images, *gains, *weights, d_tokens, d_latents)


def finish_kernel(width, *refs):
    rows_in, (summed, gains), rows_out = refs[0:4], refs[4:6], refs[6:10]
    gain_attn, g_qkv, g_out, gain_mlp, g_up, g_down = refs[10:16]
    held, (sem_in, sem_out) = refs[16:21], refs[21:23]
    wide = g_down.shape[1] // width
    unit = g_out.shape[1]
    loads = [
        pltpu.make_async_copy(src, dst, sem_in.at[i])
        for i, (src, dst) in enumerate(zip((*rows_in, summed), held))
    ]
    for load in loads:
        load.start()
    all_rows, sums = held[0:4], held[4]
    moves = [[pair] for pair in zip(all_rows, rows_out)] + [
        [(sums.at[c], g_down.at[:, c * width : (c + 1) * width]) for c in range(wide)]
        + [
            (sums.at[wide : 2 * wide], g_up),
            (sums.at[2 * wide : 2 * wide + 1], g_out),
            (sums.at[2 * wide + 1 :], g_qkv),
        ]
    ]
    gain_attn[...] = gains[0:1, 0:unit]
    gain_mlp[...] = gains[8:9, 0:unit]
    started = []
    for load, group in zip(loads, moves):
        load.wait()
        for src, dst in group:
            started.append(pltpu.make_async_copy(src, dst, sem_out.at[len(started)]))
            started[-1].start()
    for move in started:
        move.wait()


def finished(rows, summed, gains, wide):
    chunks, unit, width = summed.shape
    hbm, vm = pl.BlockSpec(memory_space=pl.ANY), pl.BlockSpec(memory_space=pltpu.VMEM)
    shapes = [r.shape for r in rows] + [
        (1, unit),
        (3, unit, width),
        (1, unit, width),
        (1, unit),
        (wide, unit, width),
        (unit, wide * width),
    ]
    return pl.pallas_call(
        functools.partial(finish_kernel, width),
        out_shape=tuple(jax.ShapeDtypeStruct(s, F32) for s in shapes),
        in_specs=[hbm] * 5 + [vm],
        out_specs=(hbm,) * 4 + (vm, hbm, hbm, vm, hbm, hbm),
        scratch_shapes=[pltpu.VMEM(x.shape, F32) for x in (*rows, summed)]
        + [pltpu.SemaphoreType.DMA((5,)), pltpu.SemaphoreType.DMA((7 + wide,))],
        compiler_params=pltpu.CompilerParams(vmem_limit_bytes=62 * 1024 * 1024),
    )(*rows, summed, gains)
def fused_shards(
    unused_grid,
    tokens,
    latents,
    slot_group,
    image_groups,
    gain_attn,
    w_qkv,
    w_out,
    gain_mlp,
    w_up,
    w_down,
    d_tokens,
    d_latents,
):
    micro, tok, width = tokens.shape
    lat = latents.shape[1]
    out_tok, out_lat, grad_tok, grad_lat, unused_grads, summed, gains = both_layers(
        slot_group.shape[1],
        tokens.reshape(micro * tok, width),
        latents.reshape(micro * lat, width),
        slot_group,
        image_groups,
        (gain_attn, gain_mlp),
        (w_qkv[0], w_out[0], w_up[0], w_down[0]),
        d_tokens.reshape(micro * tok, width),
        d_latents.reshape(micro * lat, width),
    )
    wide = w_up.shape[2] // width
    rows = (out_tok, out_lat, grad_tok, grad_lat)
    *rows, first_gain, qkv, out, second_gain, up, down = finished(rows, summed, gains, wide)
    return (
        rows[0].reshape(1, micro, tok, width),
        rows[1].reshape(1, micro, lat, width),
        rows[2].reshape(1, micro, tok, width),
        rows[3].reshape(1, micro, lat, width),
        first_gain,
        qkv.reshape(-1, width).T[None],
        out.reshape(-1, width).T[None],
        second_gain,
        up.reshape(-1, width).T[None],
        down.T[None],
    )

def solution(mesh):
    in_specs = (
        P(None, "dp", None),
        P(None, "dp", None),
        P(),
        P(),
        P("section", None),
        P("section", None, None),
        P("section", None, None),
        P("section", None),
        P("section", None, None),
        P("section", None, None),
        P(None, "dp", None),
        P(None, "dp", None),
    )
    out_specs = (
        P("section", None, "dp", None),
        P("section", None, "dp", None),
        P("section", None, "dp", None),
        P("section", None, "dp", None),
        P("section", "dp"),
        P("section", None, "dp"),
        P("section", None, "dp"),
        P("section", "dp"),
        P("section", None, "dp"),
        P("section", None, "dp"),
    )
    grid = grid_of(mesh)

    def program(*args):
        n, width = mesh.shape["dp"], args[0].shape[2]
        one_group = args[0].shape[1] == n * GROUP
        body = fused_shards if one_group and n == 16 and width % (16 * n) == 0 else shards
        return jax.shard_map(
            functools.partial(body, grid), mesh=mesh, in_specs=in_specs, out_specs=out_specs, check_vma=False
        )(*args)

    return program
```

```python
import functools

import jax
import jax.numpy as jnp
from jax import lax
from jax.experimental import pallas as pl
from jax.experimental.pallas import tpu as pltpu
from jax.sharding import PartitionSpec as P

HEADS = 12
GROUP = 256
LAT = 8


epsilon = 1e-05
masked_score = -1e30


MESH = pl.DeviceIdType.MESH


def grid_of(mesh):
    n = mesh.shape["dp"]
    coords = [getattr(d, "coords", None) for d in mesh.devices.reshape(n, -1)[:, 0]]
    if any(c is None for c in coords):
        return (n // 4, 2, 2) if n % 4 == 0 else (n, 1, 1)
    sizes = {a: len({c[a] for c in coords}) for a in range(3)}
    strides = {
        a: min([i for i in range(n) if coords[i][a] != coords[0][a]], default=n) for a in range(3)
    }
    order = sorted(range(3), key=lambda a: -strides[a])
    return tuple(sizes[a] for a in order)


def spread_kernel(grid, pairs, g_ref, gain_ref, out_ref, gout_ref, *scratch):
    acc = scratch[0:3]
    land = [scratch[3 + 3 * i : 6 + 3 * i] for i in range(3)]
    send_sem, recv_sem, own_sem = scratch[12:15]
    me = lax.axis_index("dp")
    section = lax.axis_index("section")
    l0, l1, l2 = grid
    here = (me // (l1 * l2), lax.rem(me // l2, l1), lax.rem(me, l2))

    def device(axis, shift):
        there = list(here)
        there[axis] = lax.rem(here[axis] + shift, grid[axis])
        return there[axis], ((there[0] * l1 + there[1]) * l2 + there[2], section)

    barrier = pltpu.get_barrier_semaphore()
    for axis in range(3):
        for shift in range(1, grid[axis]):
            pl.semaphore_signal(
                barrier, inc=1, device_id=device(axis, shift)[1], device_id_type=MESH
            )
    pl.semaphore_wait(barrier, sum(grid) - 3)

    orders = ((2, 1, 0), (1, 2, 0), (2, 1, 0))

    def source(stream, phase, k, at):
        if phase == 0:
            if stream == 0:
                return g_ref.at[2 * k, :, :, at]
            if stream == 1:
                return g_ref.at[2 * k + 1, :, at]
            return gain_ref.at[:, :, at]
        if phase == 1:
            return acc[stream].at[k, :, at]
        return acc[stream].at[k, at, here[orders[stream][1]]]

    def copies(stream, phase, k):
        axis = orders[stream][phase]
        for shift in range(1, grid[axis]):
            at, target = device(axis, shift)
            yield pltpu.make_async_remote_copy(
                src_ref=source(stream, phase, k, at),
                dst_ref=land[phase][stream].at[k, shift - 1],
                send_sem=send_sem.at[stream, phase, k, shift - 1],
                recv_sem=recv_sem.at[stream, phase, k, shift - 1],
                device_id=target,
                device_id_type=MESH,
            )

    def own(stream, k):
        return pltpu.make_async_copy(
            source(stream, 0, k, here[orders[stream][0]]), acc[stream].at[k], own_sem.at[stream, k]
        )

    def launch(stream, phase, k):
        for copy in copies(stream, phase, k):
            copy.start()

    def absorb(stream, phase, k):
        axis = orders[stream][phase]
        if phase == 0:
            own(stream, k).wait()
        for copy in copies(stream, phase, k):
            copy.wait_recv()
        into = land[phase][stream]
        count = grid[axis] - 1
        if phase == 0:
            for a in range(acc[stream].shape[1]):
                for b in range(acc[stream].shape[2]):
                    total = acc[stream][k, a, b].astype(jnp.float32)
                    for s in range(count):
                        total += into[k, s, a, b].astype(jnp.float32)
                    acc[stream][k, a, b] = total.astype(acc[stream].dtype)
        elif phase == 1:
            mine = here[axis]
            for a in range(acc[stream].shape[1]):
                total = acc[stream][k, a, mine].astype(jnp.float32)
                for s in range(count):
                    total += into[k, s, a].astype(jnp.float32)
                acc[stream][k, a, mine] = total.astype(acc[stream].dtype)
        else:
            total = acc[stream][k, here[0], here[orders[stream][1]]].astype(jnp.float32)
            for s in range(count):
                total += into[k, s].astype(jnp.float32)
            if stream < 2:
                out_ref[2 * k + stream] = total
            else:
                gout_ref[...] = total

    own(2, 0).start()
    launch(2, 0, 0)

    def start_own(k, carry):
        for stream in (0, 1):
            own(stream, k).start()
        return carry

    for stream in (0, 1):
        launch(stream, 0, 0)
    lax.fori_loop(0, pairs, start_own, 0)

    def turn(t, carry):
        @pl.when(t + 1 < pairs)
        def _():
            for stream in (0, 1):
                launch(stream, 0, t + 1)

        @pl.when(t < pairs)
        def _():
            for stream in (0, 1):
                absorb(stream, 0, t)
                launch(stream, 1, t)

        @pl.when((t >= 1) & (t - 1 < pairs))
        def _():
            for stream in (0, 1):
                absorb(stream, 1, t - 1)
                launch(stream, 2, t - 1)

        @pl.when(t >= 2)
        def _():
            for stream in (0, 1):
                absorb(stream, 2, t - 2)

        return carry

    lax.fori_loop(0, pairs + 2, turn, 0)
    absorb(2, 0, 0)
    launch(2, 1, 0)
    absorb(2, 1, 0)
    launch(2, 2, 0)
    absorb(2, 2, 0)

    def finish(k, carry):
        for stream in (0, 1):
            for phase in range(3):
                for copy in copies(stream, phase, k):
                    copy.wait_send()
        return carry

    lax.fori_loop(0, pairs, finish, 0)
    for phase in range(3):
        for copy in copies(2, phase, 0):
            copy.wait_send()


def spread(grid, grads, gains):
    chunks, n, rows, width = grads.shape
    pairs = chunks // 2
    l0, l1, l2 = grid
    most = max(max(grid) - 1, 1)
    low = jnp.bfloat16
    shapes = ((pairs, rows, width, low), (pairs, rows, width, low), (1, 8, 128, jnp.float32))
    inner = ((l1, l2), (l2, l1), (l1, l2))
    acc, first, second, third = [], [], [], []
    for (count, r, w, dt), (kept, sent) in zip(shapes, inner):
        acc.append(pltpu.VMEM((count, l0, kept, r, w), dt))
        first.append(pltpu.VMEM((count, max(sent - 1, 1), l0, kept, r, w), dt))
        second.append(pltpu.VMEM((count, max(kept - 1, 1), l0, r, w), dt))
        third.append(pltpu.VMEM((count, max(l0 - 1, 1), r, w), dt))
    return pl.pallas_call(
        functools.partial(spread_kernel, grid, pairs),
        out_shape=(
            jax.ShapeDtypeStruct((chunks, rows, width), jnp.float32),
            jax.ShapeDtypeStruct((8, 128), jnp.float32),
        ),
        in_specs=[pl.BlockSpec(memory_space=pl.ANY)] * 2,
        out_specs=(pl.BlockSpec(memory_space=pltpu.VMEM),) * 2,
        scratch_shapes=acc
        + first
        + second
        + third
        + [
            pltpu.SemaphoreType.DMA((3, 3, pairs, most)),
            pltpu.SemaphoreType.DMA((3, 3, pairs, most)),
            pltpu.SemaphoreType.DMA((3, pairs)),
        ],
        compiler_params=pltpu.CompilerParams(
            collective_id=0, has_side_effects=True, vmem_limit_bytes=60 * 1024 * 1024
        ),
        cost_estimate=pl.CostEstimate(flops=0, bytes_accessed=grads.size * 4, transcendentals=0),
    )(grads.reshape(chunks, l0, l1, l2, rows, width), gains.reshape(l0, l1, l2, 8, 128))


def from_behind(x, axis, by):
    devices = lax.axis_size(axis)
    pairs = [(i, i + by) for i in range(devices) if 0 <= i + by < devices]
    return lax.ppermute(x, axis, pairs)


def layer_norm(values, gain):
    row_mean = jnp.mean(values, axis=-1, keepdims=True)
    centred = values - row_mean
    row_var = jnp.mean(centred * centred, axis=-1, keepdims=True)
    return centred * lax.rsqrt(row_var + epsilon) * gain


def front_half(all_rows, gain_attn, w_qkv):
    normed = layer_norm(all_rows, gain_attn).astype(jnp.bfloat16)
    projected = jnp.dot(normed, w_qkv, preferred_element_type=jnp.float32).astype(jnp.bfloat16)
    return (normed, projected)


def latent_operand(projected, tok_rows, model_width):
    return projected[tok_rows:, model_width:]


def back_half(all_rows, projected, remote_rows, allowed, weights):
    gain_attn, w_qkv, w_out, gain_mlp, w_up, w_down = weights
    row_count, model_width = all_rows.shape
    head_size = model_width // HEADS
    remote_pairs = remote_rows[:, remote_rows.shape[1] - 2 * model_width :]
    queries = projected[:, :model_width].reshape(row_count, HEADS, head_size)
    key_rows = jnp.concatenate(
        [projected[:, model_width : 2 * model_width], remote_pairs[:, :model_width]], axis=0
    )
    value_rows = jnp.concatenate(
        [projected[:, 2 * model_width :], remote_pairs[:, model_width:]], axis=0
    )
    key_rows = key_rows.reshape(-1, HEADS, head_size)
    value_rows = value_rows.reshape(-1, HEADS, head_size)
    scores = jnp.einsum(
        "qhd,khd->hqk", queries, key_rows, preferred_element_type=jnp.float32
    ) * head_size ** (-0.5)
    attn_weights = jax.nn.softmax(jnp.where(allowed[None], scores, masked_score), axis=-1)
    attn_low = attn_weights.astype(jnp.bfloat16)
    mixed_low = jnp.einsum("hqk,khd->qhd", attn_low, value_rows, preferred_element_type=jnp.float32)
    mixed_low = mixed_low.reshape(row_count, model_width).astype(jnp.bfloat16)
    mid_rows = all_rows + jnp.dot(mixed_low, w_out, preferred_element_type=jnp.float32)
    normed_mlp = layer_norm(mid_rows, gain_mlp).astype(jnp.bfloat16)
    up_proj = jnp.dot(normed_mlp, w_up, preferred_element_type=jnp.float32)
    activated = jax.nn.gelu(up_proj).astype(jnp.bfloat16)
    result = mid_rows + jnp.dot(activated, w_down, preferred_element_type=jnp.float32)
    return dict(
        queries=queries,
        key_rows=key_rows,
        value_rows=value_rows,
        attn_weights=attn_weights,
        attn_low=attn_low,
        mixed_low=mixed_low,
        mid_rows=mid_rows,
        normed_mlp=normed_mlp,
        up_proj=up_proj,
        activated=activated,
        result=result,
    )


def section_backward(saved, d_result, all_rows, normed, allowed, weights, latent_start):
    gain_attn, w_qkv, w_out, gain_mlp, w_up, w_down = weights
    row_count, model_width = all_rows.shape
    head_size = model_width // HEADS
    score_scale = head_size ** (-0.5)
    d_low = d_result.astype(jnp.bfloat16)
    grad_down = jnp.dot(d_low.T, saved["activated"], preferred_element_type=jnp.float32)
    d_activated = jnp.dot(d_low, w_down.T, preferred_element_type=jnp.float32)
    unused_up, gelu_back = jax.vjp(jax.nn.gelu, saved["up_proj"])
    d_up = gelu_back(d_activated)[0].astype(jnp.bfloat16)
    grad_up = jnp.dot(d_up.T, saved["normed_mlp"], preferred_element_type=jnp.float32)
    d_normed_mlp = jnp.dot(d_up, w_up.T, preferred_element_type=jnp.float32)
    unused_mid, second_back = jax.vjp(layer_norm, saved["mid_rows"], gain_mlp)
    d_mid_norm, grad_gain_mlp = second_back(d_normed_mlp)
    d_mid = d_result + d_mid_norm
    d_mid_low = d_mid.astype(jnp.bfloat16)
    grad_out = jnp.dot(d_mid_low.T, saved["mixed_low"], preferred_element_type=jnp.float32)
    d_mixed = jnp.dot(d_mid_low, w_out.T, preferred_element_type=jnp.float32).astype(jnp.bfloat16)
    d_mixed = d_mixed.reshape(row_count, HEADS, head_size)
    d_weights = jnp.einsum(
        "qhd,khd->hqk", d_mixed, saved["value_rows"], preferred_element_type=jnp.float32
    )
    d_values = jnp.einsum(
        "hqk,qhd->khd", saved["attn_low"], d_mixed, preferred_element_type=jnp.float32
    )
    attn_weights = saved["attn_weights"]
    d_scores = attn_weights * (
        d_weights - jnp.sum(attn_weights * d_weights, axis=-1, keepdims=True)
    )
    d_scores_low = jnp.where(allowed[None], d_scores, 0.0).astype(jnp.bfloat16)
    d_queries = (
        jnp.einsum(
            "hqk,khd->qhd", d_scores_low, saved["key_rows"], preferred_element_type=jnp.float32
        )
        * score_scale
    )
    d_keys = (
        jnp.einsum(
            "hqk,qhd->khd", d_scores_low, saved["queries"], preferred_element_type=jnp.float32
        )
        * score_scale
    )
    remote_part = jnp.concatenate(
        [
            d_keys[row_count:].reshape(-1, model_width),
            d_values[row_count:].reshape(-1, model_width),
        ],
        axis=1,
    )
    own_part = lax.psum_scatter(remote_part, "dp", scatter_dimension=0, tiled=True)
    local_pairs = jnp.concatenate(
        [
            d_keys[:row_count].reshape(row_count, model_width),
            d_values[:row_count].reshape(row_count, model_width),
        ],
        axis=1,
    )
    local_pairs = jnp.concatenate(
        [local_pairs[:latent_start], local_pairs[latent_start:] + own_part], axis=0
    )
    d_projected = jnp.concatenate(
        [d_queries.reshape(row_count, model_width), local_pairs], axis=1
    ).astype(jnp.bfloat16)
    grad_qkv = jnp.dot(d_projected.T, normed, preferred_element_type=jnp.float32)
    d_normed = jnp.dot(d_projected, w_qkv.T, preferred_element_type=jnp.float32)
    unused_rows, first_back = jax.vjp(layer_norm, all_rows, gain_attn)
    d_rows_norm, grad_gain_attn = first_back(d_normed)
    return (
        d_mid + d_rows_norm,
        (grad_gain_attn, grad_qkv, grad_out, grad_gain_mlp, grad_up, grad_down),
    )


def packed(grads, n):
    gain_first, qkv_grad, out_grad, gain_second, up_grad, down_grad = grads
    width = out_grad.shape[0]
    rows = width // n

    def by_rows(grad):
        return grad.reshape(n, -1, rows, width).transpose(1, 0, 2, 3).astype(jnp.bfloat16)

    down = down_grad.reshape(n, rows, -1, width).transpose(2, 0, 1, 3).astype(jnp.bfloat16)
    chunks = jnp.concatenate([down, by_rows(up_grad), by_rows(out_grad), by_rows(qkv_grad)], axis=0)
    gains = jnp.stack([gain_first.reshape(n, rows), gain_second.reshape(n, rows)], axis=1)
    return chunks, jnp.pad(gains, ((0, 0), (0, 6), (0, 128 - rows)))


def shards(
    grid,
    tokens,
    latents,
    slot_group,
    image_groups,
    gain_attn,
    w_qkv,
    w_out,
    gain_mlp,
    w_up,
    w_down,
    d_tokens,
    d_latents,
):
    micro = tokens.shape[0]
    tok_rows = tokens.shape[1]
    lat_rows = latents.shape[1]
    model_width = tokens.shape[2]
    local_groups = tok_rows // GROUP
    section_index = lax.axis_index("section")
    is_global = section_index == 1
    dp_index = lax.axis_index("dp")
    weights = (gain_attn[0], w_qkv[0], w_out[0], gain_mlp[0], w_up[0], w_down[0])
    image_ends = jnp.cumsum(image_groups, axis=1)
    slot_images = jnp.sum(
        (image_ends[:, None, :] <= slot_group[:, :, None]).astype(jnp.int32), axis=2
    )
    slot_total = slot_group.shape[1]
    row_group = jnp.concatenate([jnp.arange(tok_rows) // GROUP, jnp.arange(lat_rows) // LAT])
    row_latent = jnp.concatenate(
        [jnp.zeros((tok_rows,), jnp.bool_), jnp.ones((lat_rows,), jnp.bool_)]
    )
    same_group = row_group[:, None] == row_group[None, :]
    local_mask = jnp.where(
        is_global, (~row_latent)[:, None] & row_latent[None, :] & same_group, same_group
    )
    group_match = row_group[:, None] == jnp.arange(local_groups)[None, :]

    def key_images(batch):
        images_row = lax.dynamic_index_in_dim(slot_images, batch, 0, keepdims=False)
        return (images_row, jnp.broadcast_to(images_row[:, None], (slot_total, LAT)).reshape(-1))

    def allowed_for(batch):
        images_row, key_image = key_images(batch)
        own_images = lax.dynamic_slice_in_dim(images_row, dp_index * local_groups, local_groups)
        row_image = jnp.sum(jnp.where(group_match, own_images[None, :], 0), axis=1)
        remote_mask = is_global & row_latent[:, None] & (row_image[:, None] == key_image[None, :])
        return jnp.concatenate([local_mask, remote_mask], axis=1)

    def forward_turn(received, turn):
        recv_tokens, recv_latents = received
        batch = jnp.clip(turn - section_index, 0, micro - 1)
        own_tok = lax.dynamic_index_in_dim(tokens, batch, 0, keepdims=False)
        own_lat = lax.dynamic_index_in_dim(latents, batch, 0, keepdims=False)
        input_rows = jnp.concatenate(
            [
                jnp.where(is_global, recv_tokens, own_tok),
                jnp.where(is_global, recv_latents, own_lat),
            ],
            axis=0,
        )
        all_rows = input_rows.astype(jnp.float32)
        normed, projected = front_half(all_rows, weights[0], weights[1])
        remote_rows = lax.all_gather(
            latent_operand(projected, tok_rows, model_width), "dp", axis=0, tiled=True
        )
        saved = back_half(all_rows, projected, remote_rows, allowed_for(batch), weights)
        result = saved["result"]
        result_low = result.astype(jnp.bfloat16)
        stored = jnp.where(is_global, result, result_low.astype(jnp.float32))
        passed_on = from_behind((result_low[:tok_rows], result_low[tok_rows:]), "section", 1)
        return passed_on, (input_rows, stored[:tok_rows], stored[tok_rows:])

    nothing = (
        jnp.zeros((tok_rows, model_width), jnp.bfloat16),
        jnp.zeros((lat_rows, model_width), jnp.bfloat16),
    )
    turns = jnp.arange(micro + 1)
    unused_end, (kept_rows, tok_outputs, lat_outputs) = lax.scan(forward_turn, nothing, turns)

    def backward_turn(carry, turn):
        (recv_grad_tok, recv_grad_lat), totals = carry
        raw_batch = micro - turn - section_index
        valid = ((raw_batch >= 0) & (raw_batch < micro)).astype(jnp.float32)
        batch = jnp.clip(raw_batch, 0, micro - 1)
        all_rows = lax.dynamic_index_in_dim(
            kept_rows, batch + section_index, 0, keepdims=False
        ).astype(jnp.float32)
        normed, projected = front_half(all_rows, weights[0], weights[1])
        remote_rows = lax.all_gather(
            latent_operand(projected, tok_rows, model_width), "dp", axis=0, tiled=True
        )
        allowed = allowed_for(batch)
        saved = back_half(all_rows, projected, remote_rows, allowed, weights)
        given = (
            jnp.concatenate(
                [
                    lax.dynamic_index_in_dim(d_tokens, batch, 0, keepdims=False),
                    lax.dynamic_index_in_dim(d_latents, batch, 0, keepdims=False),
                ],
                axis=0,
            )
            * valid
        )
        passed = jnp.concatenate([recv_grad_tok, recv_grad_lat], axis=0).astype(jnp.float32)
        d_result = jnp.where(is_global, given, passed)
        d_rows, grads = section_backward(
            saved, d_result, all_rows, normed, allowed, weights, tok_rows
        )
        totals = tuple((accum + piece for accum, piece in zip(totals, grads)))
        d_rows_low = d_rows.astype(jnp.bfloat16)
        stored = jnp.where(is_global, d_rows_low.astype(jnp.float32), d_rows)
        sent = from_behind((d_rows_low[:tok_rows], d_rows_low[tok_rows:]), "section", -1)
        return (sent, totals), (stored[:tok_rows], stored[tok_rows:])

    totals = tuple(
        jnp.zeros(w.shape[::-1] if w.ndim == 2 else w.shape, jnp.float32) for w in weights
    )
    (unused_sent, totals), (tok_grads, lat_grads) = lax.scan(
        backward_turn, (nothing, totals), turns
    )
    chunks, gains = packed(totals, lax.axis_size("dp"))
    summed, gain_sums = spread(grid, chunks, gains)
    rows = summed.shape[1]
    layer_tokens = lax.dynamic_slice_in_dim(tok_outputs, section_index, micro, 0)[None]
    layer_latents = lax.dynamic_slice_in_dim(lat_outputs, section_index, micro, 0)[None]
    grad_tokens = lax.dynamic_slice_in_dim(tok_grads, 1 - section_index, micro, 0)[::-1][
        None
    ]
    grad_latents = lax.dynamic_slice_in_dim(lat_grads, 1 - section_index, micro, 0)[
        ::-1
    ][None]
    return (
        layer_tokens,
        layer_latents,
        grad_tokens,
        grad_latents,
        gain_sums[0:1, :rows],
        summed[9:].reshape(-1, model_width).T[None],
        summed[8].T[None],
        gain_sums[1:2, :rows],
        summed[4:8].reshape(-1, model_width).T[None],
        summed[0:4].transpose(0, 2, 1).reshape(-1, rows)[None],
    )


F32 = jnp.float32
LOW = jnp.bfloat16
HEAD_PAD = 16
TILE = 768


def nn(a, b):
    return jnp.dot(a, b, preferred_element_type=F32)


def nt(a, b):
    return lax.dot_general(a, b, (((1,), (1,)), ((), ())), preferred_element_type=F32)


def tn(a, b):
    return lax.dot_general(a, b, (((0,), (0,)), ((), ())), preferred_element_type=F32)


def row_mean(values):
    return jnp.mean(values, axis=-1, keepdims=True)


def row_stats(load, spans):
    means = [row_mean(load(r)) for r in spans]
    scales = []
    for r, mean in zip(spans, means):
        centred = load(r) - mean
        scales.append(lax.rsqrt(row_mean(centred * centred) + epsilon))
    return means, scales


def at(start, size):
    return pl.ds(pl.multiple_of(start, size), size)


def class_max(s):
    for by in (16, 32, 64):
        s = jnp.maximum(s, pltpu.roll(s, by, 1))
    return s


def class_sum(s):
    for by in (16, 32, 64):
        s = s + pltpu.roll(s, by, 1)
    return s


ORDERS = ((2, 1, 0, 3), (1, 2, 0, 3), (0, 1, 2, 3), (1, 2, 0, 3), (2, 0, 1, 3), (2, 0, 1, 3), (1, 0, 2, 3), (0, 1, 2, 3), (0, 1, 2, 3), (0, 1, 2, 3), (1, 0, 2, 3), (2, 0, 1, 3))
SERVED = (
    (5, 3, 2, 4, 1, 7, 5, 3, 8, 6, 7, 4, 2, 3, 6, 5, 11, 9, 7, 2, 10, 1, 8, 6, 9, 11, 4, 0, 2, 1, 5, 11, 8, 10, 0, 1, 9, 0, 6, 10, 3, 4, 7, 9, 8, 0, 11, 10),
    (5, 3, 2, 4, 1, 7, 5, 3, 8, 6, 7, 4, 2, 3, 6, 5, 11, 9, 7, 2, 10, 1, 8, 6, 9, 11, 4, 0, 2, 1, 5, 11, 8, 10, 0, 1, 9, 0, 6, 10, 3, 4, 7, 9, 8, 0, 11, 10),
)


def layer_kernel(
    n,
    tokens,
    latents,
    slots,
    slot_at,
    image_at,
    gain_attn,
    gain_mlp,
    w_qkv,
    w_out,
    w_up,
    w_down,
    d_tokens,
    d_latents,
    out_tok,
    out_lat,
    grad_tok,
    grad_lat,
    grads,
    summed,
    gain_sums,
    wq,
    wo,
    wu,
    wd,
    xb,
    n1,
    proj,
    mixed,
    mid,
    n2,
    act,
    dup,
    yb,
    dy,
    ef,
    tmp,
    out,
    probs,
    probs_lat,
    scores,
    slopes,
    latf,
    mixf,
    key_mask,
    qbd,
    kbd,
    vbd,
    kv_all,
    kvg_send,
    kvg_recv,
    stage,
    gains,
    leaving,
    own_parts,
    land1,
    land2,
    land3,
    land4,
    land_g,
    load_sem,
    stage_sem,
    own_sem,
    leave_sem,
    send_sem,
    recv_sem,
    gain_s,
    gain_r,
    relay_send,
    relay_recv,
    kv_sem_s,
    kv_sem_r,
    kvg_sem_s,
    kvg_sem_r,
):
    rows, width = xb.shape
    ff = act.shape[1]
    tok = tokens.shape[0]
    lat = latents.shape[0]
    half = lat // LAT
    pairs = width // 128
    me = lax.axis_index("dp")
    section = lax.axis_index("section")
    first = section == 0
    second = section == 1
    partner = (me, 1 - section)

    loads = [
        pltpu.make_async_copy(src, dst, load_sem.at[i])
        for i, (src, dst) in enumerate(((w_qkv, wq), (w_out, wo), (w_up, wu), (w_down, wd)))
    ]
    x_loads = [
        pltpu.make_async_copy(tokens, xb.at[lat:rows], load_sem.at[4]),
        pltpu.make_async_copy(latents, xb.at[0:lat], load_sem.at[5]),
    ]
    e_loads = [
        pltpu.make_async_copy(d_tokens, ef.at[lat:rows], load_sem.at[6]),
        pltpu.make_async_copy(d_latents, ef.at[0:lat], load_sem.at[7]),
    ]

    @pl.when(first)
    def _():
        for copy in x_loads:
            copy.start()

    for copy in loads:
        copy.start()

    @pl.when(second)
    def _():
        for copy in e_loads:
            copy.start()

    barrier = pltpu.get_barrier_semaphore()
    pl.semaphore_signal(barrier, inc=1, device_id=partner, device_id_type=MESH)

    here = [lax.rem(me // (1 << bit), 2) for bit in range(4)]

    def across(bit):
        return (me + (1 - 2 * here[bit]) * (1 << bit), section)

    @pl.when(second)
    def _():
        for shift in range(1, n):
            pl.semaphore_signal(
                barrier, inc=1, device_id=(lax.rem(me + shift, n), section), device_id_type=MESH
            )
        pl.semaphore_wait(barrier, n)

    @pl.when(first)
    def _():
        for bit in range(4):
            pl.semaphore_signal(barrier, inc=1, device_id=across(bit), device_id_type=MESH)
        pl.semaphore_wait(barrier, 5)

    def relay(back, band):
        low, high = ((0, rows // 3), (rows // 3, 2 * rows // 3), (2 * rows // 3, rows))[band]
        if not back:
            low, high = ((0, lat), (lat, lat + GROUP), (lat + GROUP, rows))[band]
        return pltpu.make_async_remote_copy(
            src_ref=yb.at[low:high],
            dst_ref=(dy if back else xb).at[low:high],
            send_sem=relay_send.at[3 * back + band],
            recv_sem=relay_recv.at[3 * back + band],
            device_id=partner,
            device_id_type=MESH,
        )

    def kv_copy(shift, incoming):
        slot = lax.rem(me + n - shift, n) if incoming else me
        return pltpu.make_async_remote_copy(
            src_ref=kv_all.at[me], dst_ref=kv_all.at[slot],
            send_sem=kv_sem_s.at[shift - 1], recv_sem=kv_sem_r.at[shift - 1],
            device_id=(lax.rem(me + shift, n), section), device_id_type=MESH,
        )

    def kvg_copy(shift):
        there = lax.rem(me + shift, n)
        return pltpu.make_async_remote_copy(
            src_ref=kvg_send.at[there], dst_ref=kvg_recv.at[shift - 1],
            send_sem=kvg_sem_s.at[shift - 1], recv_sem=kvg_sem_r.at[shift - 1],
            device_id=(there, section), device_id_type=MESH,
        )

    chunks = [slice(c, c + 64) for c in range(0, GROUP, 64)]
    lane = lax.broadcasted_iota(jnp.int32, (1, 128), 1)
    halves = [(lane < 64).astype(F32).astype(LOW), (lane >= 64).astype(F32).astype(LOW)]
    eighths = [(h.astype(F32) * 0.125).astype(LOW) for h in halves]
    heads = (
        lax.broadcasted_iota(jnp.int32, (HEAD_PAD, width), 1) // 64
        == lax.broadcasted_iota(jnp.int32, (HEAD_PAD, width), 0)
    ).astype(F32)

    def block_diagonal(dst, base, src, row, column, scale):
        for i in range(LAT):
            line = src[row + i : row + i + 1, column : column + width] * scale
            dst[base + i * HEAD_PAD : base + (i + 1) * HEAD_PAD, :] = (line * heads).astype(LOW)

    def head_sum(dst, row, column, value, scale, add):
        for i in range(LAT):
            line = jnp.sum(
                value[i * HEAD_PAD : (i + 1) * HEAD_PAD] * heads, axis=0, keepdims=True
            )
            line = line * scale
            if add:
                line = line + dst[row + i : row + i + 1, column : column + width]
            dst[row + i : row + i + 1, column : column + width] = line

    def bands(body, lo, hi, size):
        def one(i, carry):
            body(pl.ds(pl.multiple_of(lo + i * size, 16), size))
            return carry

        lax.fori_loop(0, (hi - lo) // size, one, 0)

    third = rows // 3

    def grouped(body, lo, hi, count):
        def one(i, carry):
            base = lo + i * 16 * count
            body([pl.ds(pl.multiple_of(base + 16 * g, 16), 16) for g in range(count)])
            return carry

        lax.fori_loop(0, (hi - lo) // (16 * count), one, 0)

    def norm(load, gain, dst, lo, hi, count):
        def body(spans):
            means, scales = row_stats(load, spans)
            for r, mean, scale in zip(spans, means, scales):
                dst[r, :] = ((load(r) - mean) * scale * gain[...]).astype(LOW)

        grouped(body, lo, hi, count)

    def norm_back(load, grad, gain, gain_rows, store, lo, hi, count):
        def body(spans):
            means, scales = row_stats(load, spans)
            firsts, seconds = [], []
            kept = gains[0, gain_rows, :]
            for r, mean, scale in zip(spans, means, scales):
                along = grad[r, :] * ((load(r) - mean) * scale)
                kept = kept + along[0:8] + along[8:16]
                firsts.append(row_mean(grad[r, :] * gain[...]))
                seconds.append(row_mean(along * gain[...]))
            gains[0, gain_rows, :] = kept
            for r, mean, scale, one, two in zip(spans, means, scales, firsts, seconds):
                hat = (load(r) - mean) * scale
                store(r, ef[r, :] + scale * (grad[r, :] * gain[...] - one - hat * two))

        grouped(body, lo, hi, count)

    def tiles(count, body, size=TILE):
        def one(i, carry):
            body(at(i * size, size))
            return carry

        lax.fori_loop(0, count, one, 0)

    @pl.when(first)
    def _():
        for copy in x_loads:
            copy.wait()

    @pl.when(second)
    def _():
        spots = lax.broadcasted_iota(jnp.int32, (n, n * lat), 1) // lat
        spread_out = (spots == lax.broadcasted_iota(jnp.int32, (n, n * lat), 0)).astype(F32)
        groups = nn(slots[...].astype(F32).astype(LOW), spread_out.astype(LOW))
        of_micro = lax.rem(lax.broadcasted_iota(jnp.int32, (1, n * lat), 1), lat) // LAT
        for m in range(half):
            images = jnp.zeros((1, n * lat), F32)
            own_image = jnp.float32(0)
            end = jnp.int32(0)
            for i in range(image_at.shape[1]):
                end = end + image_at[m, i]
                images += jnp.where(end.astype(F32) <= groups[m : m + 1], 1.0, 0.0)
                own_image += jnp.where(end <= slot_at[m, me], 1.0, 0.0)
            seen = (images == own_image) & (of_micro == m)
            key_mask[m : m + 1, :] = jnp.where(seen, 0.0, masked_score)

    def load_in(r):
        return xb[r, :].astype(F32)

    def load_mid(r):
        return mid[r, :]

    def lat_bias(m, shape, axis):
        return jnp.where(
            lax.broadcasted_iota(jnp.int32, shape, axis) // LAT == m, 0.0, masked_score
        ).astype(F32)

    @pl.when(first)
    def _():
        norm(load_in, gain_attn, n1, 0, rows, 11)
        loads[0].wait()

        def project(c):
            proj[:, c] = nn(n1[...], wq[:, c]).astype(LOW)

        tiles(3 * width // TILE, project)
        latf[...] = proj[0:lat, :].astype(F32)

        def one_pair(it, side):
            m, p = it // pairs, lax.rem(it, pairs)
            r = pl.ds(pl.multiple_of(lat + m * GROUP, 16), GROUP)
            q = proj[r, at(p * 128, 128)]
            k = proj[r, at(width + p * 128, 128)]
            v = proj[r, at(2 * width + p * 128, 128)]
            kl = proj[0:lat, at(width + p * 128, 128)]
            vl = proj[0:lat, at(2 * width + p * 128, 128)]
            bias = lat_bias(m, (lat, GROUP), 0)
            total = jnp.zeros((GROUP, 128), F32)
            for e in (0, 1):
                qe = q * eighths[e]
                s = scores.at[2 * side + e]
                s[...] = nt(k, qe)
                sl = nt(kl, qe) + bias
                top = jnp.max(sl, axis=0, keepdims=True)
                for c in chunks:
                    top = jnp.maximum(top, jnp.max(s[c, :], axis=0, keepdims=True))
                el = jnp.exp(sl - top)
                whole_sum = jnp.sum(el, axis=0, keepdims=True)
                for c in chunks:
                    et = jnp.exp(s[c, :] - top)
                    s[c, :] = et
                    whole_sum += jnp.sum(et, axis=0, keepdims=True)
                scale = 1.0 / whole_sum
                for c in chunks:
                    probs[2 * it + e, c, :] = (s[c, :] * scale).astype(LOW)
                pe = (el * scale).astype(LOW)
                probs[2 * it + e, GROUP : GROUP + lat, :] = pe
                total += tn(probs[2 * it + e, 0:GROUP, :], v * halves[e])
                total += tn(pe, vl * halves[e])
            mixed[r, at(p * 128, 128)] = total.astype(LOW)

        def pair(i, carry):
            one_pair(2 * i, 0)
            one_pair(2 * i + 1, 1)
            return carry

        lax.fori_loop(0, half * pairs // 2, pair, 0)
        for m in range(half):
            r = slice(lat + m * GROUP, lat + (m + 1) * GROUP)
            b = slice(m * 128, (m + 1) * 128)
            block_diagonal(qbd, m * 128, latf, m * LAT, 0, 0.125)
            s = nt(qbd[b, :], proj[r, width : 2 * width])
            sl = nt(qbd[b, :], proj[0:lat, width : 2 * width]) + lat_bias(m, (128, lat), 1)
            top = jnp.maximum(
                jnp.max(s, axis=1, keepdims=True), jnp.max(sl, axis=1, keepdims=True)
            )
            et = jnp.exp(s - top)
            el = jnp.exp(sl - top)
            scale = 1.0 / (
                jnp.sum(et, axis=1, keepdims=True) + jnp.sum(el, axis=1, keepdims=True)
            )
            pt = (et * scale).astype(LOW)
            pe = (el * scale).astype(LOW)
            probs_lat[b, 0:GROUP] = pt
            probs_lat[b, GROUP : GROUP + lat] = pe
            o = nn(pt, proj[r, 2 * width :]) + nn(pe, proj[0:lat, 2 * width :])
            head_sum(mixf, m * LAT, 0, o, 1.0, False)
        mixed[0:lat, :] = mixf[...].astype(LOW)

    keys = n * lat

    root = 0.7978845608028654

    def mlp_in(lo, hi, count, with_dact=False):
        r0 = slice(lo, hi)
        mid[r0, :] = xb[r0, :].astype(F32) + nn(mixed[r0, :], wo[...])

        norm(load_mid, gain_mlp, n2, lo, hi, count)

        def up_tile(dst, i):
            dst[r0, 0:512] = nn(n2[r0, :], wu[:, at(i * 512, 512)])

        def gelu(src, i):
            c = at(i * 512, 512)
            for g in range(lo, hi, 16):
                r = slice(g, g + 16)
                up = src[r, 0:512]
                square = up * up
                t = jnp.tanh(up * (root + (root * 0.044715) * square))
                gate = 0.5 + 0.5 * t
                value = up * gate
                slope = gate + (value + value) * (1.0 - gate) * (
                    root + (3.0 * root * 0.044715) * square
                )
                act[r, c] = value.astype(LOW)
                if with_dact:
                    slope = slope * dup[r, c].astype(F32)
                dup[r, c] = slope.astype(LOW)

        last = ff // 512 - 1

        def widen(i, carry):
            up_tile(out, 2 * i + 1)
            gelu(tmp, 2 * i)
            up_tile(tmp, jnp.minimum(2 * i + 2, last))
            gelu(out, 2 * i + 1)
            return carry

        up_tile(tmp, 0)
        lax.fori_loop(0, ff // 1024, widen, 0)

    out_copies = [
        pltpu.make_async_copy(out.at[lat:rows], out_tok, load_sem.at[8]),
        pltpu.make_async_copy(out.at[0:lat], out_lat, load_sem.at[9]),
    ]
    grad_copies = [
        pltpu.make_async_copy(out.at[lat:rows], grad_tok, load_sem.at[8]),
        pltpu.make_async_copy(out.at[0:lat], grad_lat, load_sem.at[9]),
    ]

    def layer_output(low, high, passed_on):
        r = slice(low, high)
        y = mid[r, :] + nn(act[r, :], wd[...])
        if passed_on:
            narrow_y = y.astype(LOW)
            yb[r, :] = narrow_y
            y = narrow_y.astype(F32)
        out[r, :] = y

    @pl.when(first)
    def _():
        for copy in loads[1:]:
            copy.wait()
        mlp_in(0, lat + GROUP, 17)
        layer_output(0, lat + GROUP, True)
        relay(0, 0).start()
        relay(0, 1).start()
        mlp_in(lat + GROUP, rows, 16)
        layer_output(lat + GROUP, rows, True)
        relay(0, 2).start()
        for copy in out_copies:
            copy.start()

    @pl.when(second)
    def _():
        for copy in e_loads:
            copy.wait()

        def narrow_e(r):
            dy[r, :] = ef[r, :].astype(LOW)

        bands(narrow_e, 0, rows, third)
        for copy in loads:
            copy.wait()

        def early(c):
            dup[:, c] = nt(dy[...], wd[c, :]).astype(LOW)

        tiles(ff // TILE, early)
        relay(0, 0).wait_recv()
        norm(load_in, gain_attn, n1, 0, lat, 1)
        lat_proj = nn(n1[0:lat, :], wq[...]).astype(LOW)
        kv_all[me] = lat_proj[:, width:]
        latf[...] = lat_proj.astype(F32)
        for shift in range(1, n):
            kv_copy(shift, False).start()
        for m in range(half):
            relay(0, 1 + m).wait_recv()
            low, high = lat + m * GROUP, lat + (m + 1) * GROUP
            r = slice(low, high)
            b = slice(m * 128, (m + 1) * 128)
            norm(load_in, gain_attn, n1, low, high, 16)
            proj[r, :width] = nn(n1[r, :], wq[:, :width]).astype(LOW)
            block_diagonal(qbd, m * 128, latf, m * LAT, 0, 0.125)
            block_diagonal(kbd, m * 128, latf, m * LAT, width, 1.0)
            block_diagonal(vbd, m * 128, latf, m * LAT, 2 * width, 1.0)
            s = nt(proj[r, :width] * jnp.asarray(0.125, LOW), kbd[b, :])
            et = jnp.exp(s - class_max(s))
            pt = (et / class_sum(et)).astype(LOW)
            probs[m, 0:GROUP, 0:128] = pt
            mixed[r, :] = nn(pt, vbd[b, :]).astype(LOW)
            mlp_in(low, high, 16, True)
        for shift in range(1, n):
            kv_copy(shift, True).wait_recv()
        k = kv_all[:, :, :width].reshape(keys, width)
        v = kv_all[:, :, width:].reshape(keys, width)
        for m in range(half):
            b = slice(m * 128, (m + 1) * 128)
            s = nt(qbd[b, :], k) + key_mask[m : m + 1, :]
            et = jnp.exp(s - jnp.max(s, axis=1, keepdims=True))
            pt = (et / jnp.sum(et, axis=1, keepdims=True)).astype(LOW)
            probs_lat[b, 0:keys] = pt
            head_sum(mixf, m * LAT, 0, nn(pt, v), 1.0, False)
        mixed[0:lat, :] = mixf[...].astype(LOW)
        mlp_in(0, lat, 1, True)

    @pl.when(first)
    def _():
        for band in range(3):
            relay(1, band).wait_recv()

        def widen_e(r):
            ef[r, :] = dy[r, :].astype(F32)

        bands(widen_e, 0, rows, third)

    part = 384
    unit = width // n
    many = part // unit

    def staged(slot, piece, chunk, share):
        return pltpu.make_async_copy(
            stage.at[slot, piece],
            grads.at[
                chunk,
                share // 8,
                lax.rem(share // 4, 2),
                lax.rem(share // 2, 2),
                lax.rem(share, 2),
            ],
            stage_sem.at[slot, piece],
        )

    def drain(slot):
        def one(piece, carry):
            staged(slot, piece, 0, 0).wait()
            return carry

        lax.fori_loop(0, many, one, 0)

    def weight_grad(place, start, count, left, *rights, settled=True):
        def one(i, carry):
            turned = left(i).T
            for at_right, right in enumerate(rights):
                tile = i * len(rights) + at_right
                slot = lax.rem(tile, 2)
                value = nn(turned, right(i)).astype(LOW)

                if settled:

                    @pl.when(tile >= start * len(rights) + 2)
                    def _():
                        drain(slot)

                else:
                    drain(slot)

                for piece in range(many):
                    stage[slot, piece] = value[piece * unit : (piece + 1) * unit]
                    staged(slot, piece, *place(i, at_right, piece)).start()
            return carry

        lax.fori_loop(start, start + count, one, 0)

    def settle():
        for slot in (0, 1):
            drain(slot)

    per_part = width // part
    wide = ff // width
    lands = (land1, land2, land3, land4)
    mine = here

    def kept(order, parts):
        left = [bit for bit in (3, 2, 1, 0) if bit != order[0]]
        return tuple(parts.get(bit, slice(None)) for bit in left)

    def source(chunk, phase, theirs):
        order = ORDERS[chunk]
        parts = {bit: mine[bit] for bit in order[:phase]}
        bit = order[phase]
        parts[bit] = (1 - mine[bit]) if theirs else mine[bit]
        if phase == 0:
            return grads.at[(chunk, *(parts.get(b, slice(None)) for b in (3, 2, 1, 0)))]
        return land1.at[(chunk, *kept(order, parts))]

    def copy_of(chunk, phase):
        return pltpu.make_async_remote_copy(
            src_ref=source(chunk, phase, True),
            dst_ref=lands[phase].at[chunk],
            send_sem=send_sem.at[phase, chunk],
            recv_sem=recv_sem.at[phase, chunk],
            device_id=across(ORDERS[chunk][phase]),
            device_id_type=MESH,
        )

    def own(chunk, slot):
        return pltpu.make_async_copy(
            source(chunk, 0, False), own_parts.at[slot], own_sem.at[slot]
        )

    def leave(chunk, slot):
        return pltpu.make_async_copy(
            leaving.at[slot], summed.at[chunk], leave_sem.at[slot]
        )

    def launch(*chunks):
        for chunk in chunks:
            copy_of(chunk, 0).start()

    def serve(sequence):
        reached, fetched, left = {}, [], []
        steps = []
        for chunk in sequence:
            steps.append((chunk, reached.get(chunk, 0)))
            reached[chunk] = steps[-1][1] + 1
        starts = [chunk for chunk, phase in steps if phase == 0]
        for slot, chunk in enumerate(starts[:3]):
            own(chunk, slot).start()
        for chunk, phase in steps:
            order = ORDERS[chunk]
            into = lands[phase]
            if phase == 0:
                slot = len(fetched) % 3
                own(chunk, slot).wait()
            copy_of(chunk, phase).wait_recv()
            parts = {bit: mine[bit] for bit in order[: phase + 1]}
            rest = [bit for bit in (3, 2, 1, 0) if bit not in parts]

            def add(i, carry):
                spread_bits = {
                    bit: lax.rem(i // (1 << at_bit), 2) for at_bit, bit in enumerate(rest[::-1])
                }
                spot = (chunk, *kept(order, {**parts, **spread_bits}))
                here_in = (chunk, *(spread_bits[bit] for bit in rest))
                if phase == 0:
                    value = own_parts[(slot, *here_in[1:])].astype(F32) + land1[spot].astype(F32)
                else:
                    value = land1[spot].astype(F32) + into[here_in].astype(F32)
                land1[spot] = value.astype(LOW)
                return carry

            if phase < 3:
                lax.fori_loop(0, 1 << len(rest), add, 0)
                copy_of(chunk, phase + 1).start()
            else:
                total = land1[(chunk, *kept(order, parts))].astype(F32)
                total += land4[chunk].astype(F32)
                out_slot = len(left) % 4
                if len(left) >= 4:
                    leave(left[-4], out_slot).wait()
                leaving[out_slot] = total
                leave(chunk, out_slot).start()
                left.append(chunk)
            if phase == 0:
                fetched.append(chunk)
                if len(fetched) + 2 < len(starts):
                    own(starts[len(fetched) + 2], slot).start()
            yield chunk, phase
        for i, chunk in enumerate(left[-4:]):
            leave(chunk, (len(left) - len(left[-4:]) + i) % 4).wait()

    steps_of = [serve(SERVED[core]) for core in (0, 1)]

    def up_grad():
        weight_grad(
            lambda i, right, piece: (
                wide + lax.rem(i * many + piece, wide),
                (i * many + piece) // wide,
            ),
            0,
            ff // part,
            lambda i: dup[:, at(i * part, part)],
            lambda i: n2[...],
        )
    def down_grad(pair, settled):
        weight_grad(
            lambda i, right, piece: (2 * pair + right, i * many + piece),
            0,
            per_part,
            lambda i: dy[:, at(i * part, part)],
            lambda i: act[:, 2 * pair * width : (2 * pair + 1) * width],
            lambda i: act[:, (2 * pair + 1) * width : (2 * pair + 2) * width],
            settled=settled,
        )

    down_grad(0, True)
    down_grad(1, False)
    launch(0, 1)

    @pl.when(first)
    def _():
        def unwiden(c):
            dup[:, c] = (nt(dy[...], wd[c, :]) * dup[:, c].astype(F32)).astype(LOW)

        tiles(ff // TILE, unwiden)

    settle()
    launch(2, 3)
    up_grad()

    def to_mid(c):
        tmp[:, c] = nt(dup[...], wu[c, :])

    tiles(width // 256, to_mid, 256)
    settle()
    launch(*range(wide, 2 * wide))
    gains[0] = jnp.zeros_like(gains[0])

    def store_mid(r, total):
        ef[r, :] = total
        dy[r, :] = total.astype(LOW)

    norm_back(load_mid, tmp, gain_mlp, slice(8, 16), store_mid, 0, rows, 11)

    @pl.when(first)
    def _():
        for band in range(3):
            relay(0, band).wait_send()

    def to_mix(c):
        yb[:, c] = nt(dy[...], wo[c, :]).astype(LOW)

    tiles(width // TILE, to_mix)
    mixf[...] = yb[0:lat, :].astype(F32)

    @pl.when(second)
    def _():
        k = kv_all[:, :, :width].reshape(keys, width)
        v = kv_all[:, :, width:].reshape(keys, width)
        for m in range(half):
            b = slice(m * 128, (m + 1) * 128)
            block_diagonal(vbd.at[pl.ds(256, 256)], m * 128, mixf, m * LAT, 0, 1.0)
        both = slice(0, half * 128)
        do = vbd[256 : 256 + half * 128, :]
        pt = probs_lat[both, 0:keys]
        pf = pt.astype(F32)
        dp = nt(do, v)
        along = jnp.sum(pf * dp, axis=1, keepdims=True)
        ds = (pf * (dp - along)).astype(LOW)
        kvg_send[:, :, :width] = tn(ds, qbd[both, :]).astype(LOW).reshape(n, lat, width)
        kvg_send[:, :, width:] = tn(pt, do).astype(LOW).reshape(n, lat, width)
        for shift in range(1, n):
            kvg_copy(shift).start()
        dq = nn(ds, k)
        for m in range(half):
            head_sum(latf, m * LAT, 0, dq[m * 128 : (m + 1) * 128], 0.125, False)
        proj[0:lat, :width] = latf[:, :width].astype(LOW)
        layer_output(0, lat + GROUP, False)
        layer_output(lat + GROUP, rows, False)
        for copy in out_copies:
            copy.start()

    weight_grad(
        lambda i, right, piece: (2 * wide, i * many + piece),
        0,
        width // part,
        lambda i: dy[:, at(i * part, part)],
        lambda i: mixed[...],
    )
    for copy in out_copies:
        copy.wait()

    @pl.when(first)
    def _():
        for m in range(half):
            r = slice(lat + m * GROUP, lat + (m + 1) * GROUP)
            b = slice(m * 128, (m + 1) * 128)
            block_diagonal(vbd, m * 128, mixf, m * LAT, 0, 1.0)
            do = vbd[b, :]
            dp = nt(do, proj[r, 2 * width :])
            dl = nt(do, proj[0:lat, 2 * width :])
            pt = probs_lat[b, 0:GROUP]
            pe = probs_lat[b, GROUP : GROUP + lat]
            pf = pt.astype(F32)
            pg = pe.astype(F32)
            along = jnp.sum(pf * dp, axis=1, keepdims=True) + jnp.sum(
                pg * dl, axis=1, keepdims=True
            )
            ds = (pf * (dp - along)).astype(LOW)
            dsl = (pg * (dl - along)).astype(LOW)
            dq = nn(ds, proj[r, width : 2 * width]) + nn(dsl, proj[0:lat, width : 2 * width])
            head_sum(latf, m * LAT, 0, dq, 0.125, False)
            tmp[r, :] = tn(ds, qbd[b, :])
            out[r, :] = tn(pt, do)
            if m == 0:
                tmp[0:lat, :] = tn(dsl, qbd[b, :])
                out[0:lat, :] = tn(pe, do)
            else:
                tmp[0:lat, :] += tn(dsl, qbd[b, :])
                out[0:lat, :] += tn(pe, do)
        proj[0:lat, :width] = latf[:, :width].astype(LOW)
        settle()
        launch(2 * wide)

        def one_pair(it, side):
            m, p = it // pairs, lax.rem(it, pairs)
            r = pl.ds(pl.multiple_of(lat + m * GROUP, 16), GROUP)
            qc = at(p * 128, 128)
            q = proj[r, qc]
            k = proj[r, at(width + p * 128, 128)]
            v = proj[r, at(2 * width + p * 128, 128)]
            kl = proj[0:lat, at(width + p * 128, 128)]
            vl = proj[0:lat, at(2 * width + p * 128, 128)]
            dx = yb[r, qc]
            dq = jnp.zeros((GROUP, 128), F32)
            dk = tmp[r, qc]
            dv = out[r, qc]
            dkl = tmp[0:lat, qc]
            dvl = out[0:lat, qc]
            for e in (0, 1):
                qe = q * eighths[e]
                de = dx * halves[e]
                s = scores.at[2 * side + e]
                s[...] = nt(v, de)
                dl = nt(vl, de)
                pt = probs[2 * it + e, 0:GROUP, :]
                pe = probs[2 * it + e, GROUP : GROUP + lat, :]
                pg = pe.astype(F32)
                along = jnp.sum(pg * dl, axis=0, keepdims=True)
                for c in chunks:
                    pf = probs[2 * it + e, c, :].astype(F32)
                    along += jnp.sum(pf * s[c, :], axis=0, keepdims=True)
                for c in chunks:
                    pf = probs[2 * it + e, c, :].astype(F32)
                    slopes[2 * side + e, c, :] = (pf * (s[c, :] - along)).astype(LOW)
                ds = slopes[2 * side + e]
                dsl = (pg * (dl - along)).astype(LOW)
                dq += tn(ds, k * halves[e]) + tn(dsl, kl * halves[e])
                dk += nn(ds, qe)
                dkl += nn(dsl, qe)
                dv += nn(pt, de)
                dvl += nn(pe, de)
            proj[r, qc] = (dq * 0.125).astype(LOW)
            proj[r, at(width + p * 128, 128)] = dk.astype(LOW)
            proj[r, at(2 * width + p * 128, 128)] = dv.astype(LOW)
            tmp[0:lat, qc] = dkl
            out[0:lat, qc] = dvl

        def pair(i, carry):
            one_pair(2 * i, 0)
            one_pair(2 * i + 1, 1)
            return carry

        lax.fori_loop(0, half * pairs // 2, pair, 0)
        proj[0:lat, width : 2 * width] = tmp[0:lat, :].astype(LOW)
        proj[0:lat, 2 * width :] = out[0:lat, :].astype(LOW)

    @pl.when(second)
    def _():
        for m in range(half):
            r = slice(lat + m * GROUP, lat + (m + 1) * GROUP)
            b = slice(m * 128, (m + 1) * 128)
            pt = probs[m, 0:GROUP, 0:128]
            pf = pt.astype(F32)
            dx = yb[r, :]
            dp = nt(dx, vbd[b, :])
            ds = (pf * (dp - class_sum(pf * dp))).astype(LOW)
            dk = tn(ds, proj[r, :width])
            dv = tn(pt, dx)
            proj[r, :width] = (nn(ds, kbd[b, :]) * 0.125).astype(LOW)
            head_sum(latf, m * LAT, width, dk, 0.125, False)
            head_sum(latf, m * LAT, 2 * width, dv, 1.0, False)
        settle()
        launch(2 * wide)
        total = latf[:, width:] + kvg_send[me].astype(F32)
        for shift in range(1, n):
            kvg_copy(shift).wait_recv()
            total += kvg_recv[shift - 1].astype(F32)
        proj[0:lat, width:] = total.astype(LOW)

    def qkv_grad(start, count, r):
        weight_grad(
            lambda i, right, piece: (
                2 * wide + 1 + lax.rem(i * many + piece, 3),
                (i * many + piece) // 3,
            ),
            start,
            count,
            lambda i: proj[r, at(i * part, part)],
            lambda i: n1[r, :],
        )

    @pl.when(first)
    def _():
        qkv_grad(0, 3 * per_part, slice(0, rows))
        settle()
        launch(*range(2 * wide + 1, 2 * wide + 4))
        for unused_step in range(3):
            next(steps_of[0])

    @pl.when(first)
    def _():
        def to_in(c):
            tmp[:, c] = nt(proj[...], wq[c, :])

        tiles(width // 256, to_in, 256)

    @pl.when(second)
    def _():
        tmp[...] = nt(proj[:, :width], wq[:, :width])
        tmp[0:lat, :] += nt(proj[0:lat, width:], wq[:, width:])

    def store_in(r, total):
        low = total.astype(LOW)
        yb[r, :] = low
        out[r, :] = jnp.where(first, total, low.astype(F32))

    for band in range(3):
        norm_back(
            load_in, tmp, gain_attn, slice(0, 8), store_in, band * third, (band + 1) * third, 11
        )

        @pl.when(second)
        def _():
            relay(1, band).start()

    for copy in grad_copies:
        copy.start()

    @pl.when(second)
    def _():
        qkv_grad(0, per_part, slice(0, rows))
        settle()
        qkv_grad(per_part, 2 * per_part, slice(0, lat))
        settle()
        launch(*range(2 * wide + 1, 2 * wide + 4))

    def gain_copy(bit):
        return pltpu.make_async_remote_copy(
            src_ref=gains.at[bit],
            dst_ref=land_g.at[bit],
            send_sem=gain_s.at[bit],
            recv_sem=gain_r.at[bit],
            device_id=across(bit),
            device_id_type=MESH,
        )

    def gain_step(bit):
        gain_copy(bit).wait_recv()
        gains[bit + 1] = gains[bit] + land_g[bit]

    gain_copy(0).start()

    def serve_all(core):
        for i, unused_step in enumerate(steps_of[core]):
            if i in (10, 20, 30, 40):
                gain_step(i // 10 - 1)
                if i < 40:
                    gain_copy(i // 10).start()

    @pl.when(first)
    def _():
        serve_all(0)

    @pl.when(second)
    def _():
        serve_all(1)

    final = gains[4]
    for i in (0, 1):
        whole_gain = jnp.sum(final[8 * i : 8 * i + 8], axis=0, keepdims=True)
        whole_gain = jnp.broadcast_to(whole_gain, (8, width))
        rolled = pltpu.roll(whole_gain, lax.rem(width - me * unit, width), 1)
        gain_sums[8 * i : 8 * i + 8, :] = rolled[:, 0:128]

    for chunk in range(len(ORDERS)):
        for phase in range(4):
            copy_of(chunk, phase).wait_send()
    for bit in range(4):
        gain_copy(bit).wait_send()
    for copy in grad_copies:
        copy.wait()
    @pl.when(second)
    def _():
        for band in range(3):
            relay(1, band).wait_send()
        for shift in range(1, n):
            kv_copy(shift, False).wait_send()
            kvg_copy(shift).wait_send()


def both_layers(n, tokens, latents, slots, images, gains, weights, d_tokens, d_latents):
    tok, width = tokens.shape
    lat = latents.shape[0]
    rows = tok + lat
    w_qkv, w_out, w_up, w_down = weights
    ff = w_up.shape[1]
    keys = n * lat
    half = lat // LAT
    size = sum(w.size for w in weights)
    chunks = size // (width * width)
    unit = width // n
    vm, hbm = pl.BlockSpec(memory_space=pltpu.VMEM), pl.BlockSpec(memory_space=pl.ANY)
    sm = pl.BlockSpec(memory_space=pltpu.SMEM)
    scratch = [
        pltpu.VMEM(w.shape, LOW) for w in (w_qkv, w_out, w_up, w_down)
    ] + [
        pltpu.VMEM(shape, dtype)
        for shape, dtype in (
            ((rows, width), LOW),
            ((rows, width), LOW),
            ((rows, 3 * width), LOW),
            ((rows, width), LOW),
            ((rows, width), F32),
            ((rows, width), LOW),
            ((rows, ff), LOW),
            ((rows, ff), LOW),
            ((rows, width), LOW),
            ((rows, width), LOW),
            ((rows, width), F32),
            ((rows, width), F32),
            ((rows, width), F32),
            ((half * width // 64, GROUP + lat, GROUP), LOW),
            ((half * 128, max(keys, GROUP + 128)), LOW),
            ((4, GROUP, GROUP), F32),
            ((4, GROUP, GROUP), LOW),
            ((lat, 3 * width), F32),
            ((lat, width), F32),
            ((8, keys), F32),
            ((half * 128, width), LOW),
            ((half * 128, width), LOW),
            ((half * 256, width), LOW),
            ((n, lat, 2 * width), LOW),
            ((n, lat, 2 * width), LOW),
            ((n - 1, lat, 2 * width), LOW),
            ((2, 384 // unit, unit, width), LOW),
            ((5, 16, width), F32),
            ((4, unit, width), F32),
            ((3, 2, 2, 2, unit, width), LOW),
            *(
                ((chunks, *shape, unit, width), LOW)
                for shape in ((2, 2, 2), (2, 2), (2,), ())
            ),
            ((4, 16, width), F32),
        )
    ] + [
        pltpu.SemaphoreType.DMA((10,)),
        pltpu.SemaphoreType.DMA((2, 384 // unit)),
        pltpu.SemaphoreType.DMA((3,)),
        pltpu.SemaphoreType.DMA((4,)),
        pltpu.SemaphoreType.DMA((4, chunks)),
        pltpu.SemaphoreType.DMA((4, chunks)),
        pltpu.SemaphoreType.DMA((4,)),
        pltpu.SemaphoreType.DMA((4,)),
        pltpu.SemaphoreType.DMA((6,)),
        pltpu.SemaphoreType.DMA((6,)),
        pltpu.SemaphoreType.DMA((n - 1,)),
        pltpu.SemaphoreType.DMA((n - 1,)),
        pltpu.SemaphoreType.DMA((n - 1,)),
        pltpu.SemaphoreType.DMA((n - 1,)),
    ]
    return pl.pallas_call(
        functools.partial(layer_kernel, n),
        out_shape=(
            jax.ShapeDtypeStruct((tok, width), F32),
            jax.ShapeDtypeStruct((lat, width), F32),
            jax.ShapeDtypeStruct((tok, width), F32),
            jax.ShapeDtypeStruct((lat, width), F32),
            jax.ShapeDtypeStruct((chunks, 2, 2, 2, 2, unit, width), LOW),
            jax.ShapeDtypeStruct((chunks, unit, width), F32),
            jax.ShapeDtypeStruct((16, 128), F32),
        ),
        in_specs=[hbm, hbm, vm, sm, sm, vm, vm] + [hbm] * 6,
        out_specs=(hbm,) * 6 + (vm,),
        scratch_shapes=scratch,
        compiler_params=pltpu.CompilerParams(
            collective_id=1, has_side_effects=True, vmem_limit_bytes=63 * 1024 * 1024
        ),
        cost_estimate=pl.CostEstimate(
            flops=6 * rows * size, bytes_accessed=4 * size, transcendentals=0
        ),
    )(tokens, latents, slots, slots, images, *gains, *weights, d_tokens, d_latents)


def finish_kernel(width, *refs):
    rows_in, (summed, gains), rows_out = refs[0:4], refs[4:6], refs[6:10]
    gain_attn, g_qkv, g_out, gain_mlp, g_up, g_down = refs[10:16]
    held, (sem_in, sem_out) = refs[16:21], refs[21:23]
    wide = g_down.shape[1] // width
    unit = g_out.shape[1]
    loads = [
        pltpu.make_async_copy(src, dst, sem_in.at[i])
        for i, (src, dst) in enumerate(zip((*rows_in, summed), held))
    ]
    for load in loads:
        load.start()
    all_rows, sums = held[0:4], held[4]
    moves = [[pair] for pair in zip(all_rows, rows_out)] + [
        [(sums.at[c], g_down.at[:, c * width : (c + 1) * width]) for c in range(wide)]
        + [
            (sums.at[wide : 2 * wide], g_up),
            (sums.at[2 * wide : 2 * wide + 1], g_out),
            (sums.at[2 * wide + 1 :], g_qkv),
        ]
    ]
    gain_attn[...] = gains[0:1, 0:unit]
    gain_mlp[...] = gains[8:9, 0:unit]
    started = []
    for load, group in zip(loads, moves):
        load.wait()
        for src, dst in group:
            started.append(pltpu.make_async_copy(src, dst, sem_out.at[len(started)]))
            started[-1].start()
    for move in started:
        move.wait()


def finished(rows, summed, gains, wide):
    chunks, unit, width = summed.shape
    hbm, vm = pl.BlockSpec(memory_space=pl.ANY), pl.BlockSpec(memory_space=pltpu.VMEM)
    shapes = [r.shape for r in rows] + [
        (1, unit),
        (3, unit, width),
        (1, unit, width),
        (1, unit),
        (wide, unit, width),
        (unit, wide * width),
    ]
    return pl.pallas_call(
        functools.partial(finish_kernel, width),
        out_shape=tuple(jax.ShapeDtypeStruct(s, F32) for s in shapes),
        in_specs=[hbm] * 5 + [vm],
        out_specs=(hbm,) * 4 + (vm, hbm, hbm, vm, hbm, hbm),
        scratch_shapes=[pltpu.VMEM(x.shape, F32) for x in (*rows, summed)]
        + [pltpu.SemaphoreType.DMA((5,)), pltpu.SemaphoreType.DMA((7 + wide,))],
        compiler_params=pltpu.CompilerParams(vmem_limit_bytes=62 * 1024 * 1024),
    )(*rows, summed, gains)
def fused_shards(
    unused_grid,
    tokens,
    latents,
    slot_group,
    image_groups,
    gain_attn,
    w_qkv,
    w_out,
    gain_mlp,
    w_up,
    w_down,
    d_tokens,
    d_latents,
):
    micro, tok, width = tokens.shape
    lat = latents.shape[1]
    out_tok, out_lat, grad_tok, grad_lat, unused_grads, summed, gains = both_layers(
        slot_group.shape[1],
        tokens.reshape(micro * tok, width),
        latents.reshape(micro * lat, width),
        slot_group,
        image_groups,
        (gain_attn, gain_mlp),
        (w_qkv[0], w_out[0], w_up[0], w_down[0]),
        d_tokens.reshape(micro * tok, width),
        d_latents.reshape(micro * lat, width),
    )
    wide = w_up.shape[2] // width
    rows = (out_tok, out_lat, grad_tok, grad_lat)
    *rows, first_gain, qkv, out, second_gain, up, down = finished(rows, summed, gains, wide)
    return (
        rows[0].reshape(1, micro, tok, width),
        rows[1].reshape(1, micro, lat, width),
        rows[2].reshape(1, micro, tok, width),
        rows[3].reshape(1, micro, lat, width),
        first_gain,
        qkv.reshape(-1, width).T[None],
        out.reshape(-1, width).T[None],
        second_gain,
        up.reshape(-1, width).T[None],
        down.T[None],
    )

def solution(mesh):
    in_specs = (
        P(None, "dp", None),
        P(None, "dp", None),
        P(),
        P(),
        P("section", None),
        P("section", None, None),
        P("section", None, None),
        P("section", None),
        P("section", None, None),
        P("section", None, None),
        P(None, "dp", None),
        P(None, "dp", None),
    )
    out_specs = (
        P("section", None, "dp", None),
        P("section", None, "dp", None),
        P("section", None, "dp", None),
        P("section", None, "dp", None),
        P("section", "dp"),
        P("section", None, "dp"),
        P("section", None, "dp"),
        P("section", "dp"),
        P("section", None, "dp"),
        P("section", None, "dp"),
    )
    grid = grid_of(mesh)

    def program(*args):
        n, width = mesh.shape["dp"], args[0].shape[2]
        one_group = args[0].shape[1] == n * GROUP
        body = fused_shards if one_group and n == 16 and width % (16 * n) == 0 else shards
        return jax.shard_map(
            functools.partial(body, grid), mesh=mesh, in_specs=in_specs, out_specs=out_specs, check_vma=False
        )(*args)

    return program
```

```python
import functools

import jax
import jax.numpy as jnp
from jax import lax
from jax.experimental import pallas as pl
from jax.experimental.pallas import tpu as pltpu
from jax.sharding import PartitionSpec as P

HEADS = 12
GROUP = 256
LAT = 8


epsilon = 1e-05
masked_score = -1e30


MESH = pl.DeviceIdType.MESH


def grid_of(mesh):
    n = mesh.shape["dp"]
    coords = [getattr(d, "coords", None) for d in mesh.devices.reshape(n, -1)[:, 0]]
    if any(c is None for c in coords):
        return (n // 4, 2, 2) if n % 4 == 0 else (n, 1, 1)
    sizes = {a: len({c[a] for c in coords}) for a in range(3)}
    strides = {
        a: min([i for i in range(n) if coords[i][a] != coords[0][a]], default=n) for a in range(3)
    }
    order = sorted(range(3), key=lambda a: -strides[a])
    return tuple(sizes[a] for a in order)


def spread_kernel(grid, pairs, g_ref, gain_ref, out_ref, gout_ref, *scratch):
    acc = scratch[0:3]
    land = [scratch[3 + 3 * i : 6 + 3 * i] for i in range(3)]
    send_sem, recv_sem, own_sem = scratch[12:15]
    me = lax.axis_index("dp")
    section = lax.axis_index("section")
    l0, l1, l2 = grid
    here = (me // (l1 * l2), lax.rem(me // l2, l1), lax.rem(me, l2))

    def device(axis, shift):
        there = list(here)
        there[axis] = lax.rem(here[axis] + shift, grid[axis])
        return there[axis], ((there[0] * l1 + there[1]) * l2 + there[2], section)

    barrier = pltpu.get_barrier_semaphore()
    for axis in range(3):
        for shift in range(1, grid[axis]):
            pl.semaphore_signal(
                barrier, inc=1, device_id=device(axis, shift)[1], device_id_type=MESH
            )
    pl.semaphore_wait(barrier, sum(grid) - 3)

    orders = ((2, 1, 0), (1, 2, 0), (2, 1, 0))

    def source(stream, phase, k, at):
        if phase == 0:
            if stream == 0:
                return g_ref.at[2 * k, :, :, at]
            if stream == 1:
                return g_ref.at[2 * k + 1, :, at]
            return gain_ref.at[:, :, at]
        if phase == 1:
            return acc[stream].at[k, :, at]
        return acc[stream].at[k, at, here[orders[stream][1]]]

    def copies(stream, phase, k):
        axis = orders[stream][phase]
        for shift in range(1, grid[axis]):
            at, target = device(axis, shift)
            yield pltpu.make_async_remote_copy(
                src_ref=source(stream, phase, k, at),
                dst_ref=land[phase][stream].at[k, shift - 1],
                send_sem=send_sem.at[stream, phase, k, shift - 1],
                recv_sem=recv_sem.at[stream, phase, k, shift - 1],
                device_id=target,
                device_id_type=MESH,
            )

    def own(stream, k):
        return pltpu.make_async_copy(
            source(stream, 0, k, here[orders[stream][0]]), acc[stream].at[k], own_sem.at[stream, k]
        )

    def launch(stream, phase, k):
        for copy in copies(stream, phase, k):
            copy.start()

    def absorb(stream, phase, k):
        axis = orders[stream][phase]
        if phase == 0:
            own(stream, k).wait()
        for copy in copies(stream, phase, k):
            copy.wait_recv()
        into = land[phase][stream]
        count = grid[axis] - 1
        if phase == 0:
            for a in range(acc[stream].shape[1]):
                for b in range(acc[stream].shape[2]):
                    total = acc[stream][k, a, b].astype(jnp.float32)
                    for s in range(count):
                        total += into[k, s, a, b].astype(jnp.float32)
                    acc[stream][k, a, b] = total.astype(acc[stream].dtype)
        elif phase == 1:
            mine = here[axis]
            for a in range(acc[stream].shape[1]):
                total = acc[stream][k, a, mine].astype(jnp.float32)
                for s in range(count):
                    total += into[k, s, a].astype(jnp.float32)
                acc[stream][k, a, mine] = total.astype(acc[stream].dtype)
        else:
            total = acc[stream][k, here[0], here[orders[stream][1]]].astype(jnp.float32)
            for s in range(count):
                total += into[k, s].astype(jnp.float32)
            if stream < 2:
                out_ref[2 * k + stream] = total
            else:
                gout_ref[...] = total

    own(2, 0).start()
    launch(2, 0, 0)

    def start_own(k, carry):
        for stream in (0, 1):
            own(stream, k).start()
        return carry

    for stream in (0, 1):
        launch(stream, 0, 0)
    lax.fori_loop(0, pairs, start_own, 0)

    def turn(t, carry):
        @pl.when(t + 1 < pairs)
        def _():
            for stream in (0, 1):
                launch(stream, 0, t + 1)

        @pl.when(t < pairs)
        def _():
            for stream in (0, 1):
                absorb(stream, 0, t)
                launch(stream, 1, t)

        @pl.when((t >= 1) & (t - 1 < pairs))
        def _():
            for stream in (0, 1):
                absorb(stream, 1, t - 1)
                launch(stream, 2, t - 1)

        @pl.when(t >= 2)
        def _():
            for stream in (0, 1):
                absorb(stream, 2, t - 2)

        return carry

    lax.fori_loop(0, pairs + 2, turn, 0)
    absorb(2, 0, 0)
    launch(2, 1, 0)
    absorb(2, 1, 0)
    launch(2, 2, 0)
    absorb(2, 2, 0)

    def finish(k, carry):
        for stream in (0, 1):
            for phase in range(3):
                for copy in copies(stream, phase, k):
                    copy.wait_send()
        return carry

    lax.fori_loop(0, pairs, finish, 0)
    for phase in range(3):
        for copy in copies(2, phase, 0):
            copy.wait_send()


def spread(grid, grads, gains):
    chunks, n, rows, width = grads.shape
    pairs = chunks // 2
    l0, l1, l2 = grid
    most = max(max(grid) - 1, 1)
    low = jnp.bfloat16
    shapes = ((pairs, rows, width, low), (pairs, rows, width, low), (1, 8, 128, jnp.float32))
    inner = ((l1, l2), (l2, l1), (l1, l2))
    acc, first, second, third = [], [], [], []
    for (count, r, w, dt), (kept, sent) in zip(shapes, inner):
        acc.append(pltpu.VMEM((count, l0, kept, r, w), dt))
        first.append(pltpu.VMEM((count, max(sent - 1, 1), l0, kept, r, w), dt))
        second.append(pltpu.VMEM((count, max(kept - 1, 1), l0, r, w), dt))
        third.append(pltpu.VMEM((count, max(l0 - 1, 1), r, w), dt))
    return pl.pallas_call(
        functools.partial(spread_kernel, grid, pairs),
        out_shape=(
            jax.ShapeDtypeStruct((chunks, rows, width), jnp.float32),
            jax.ShapeDtypeStruct((8, 128), jnp.float32),
        ),
        in_specs=[pl.BlockSpec(memory_space=pl.ANY)] * 2,
        out_specs=(pl.BlockSpec(memory_space=pltpu.VMEM),) * 2,
        scratch_shapes=acc
        + first
        + second
        + third
        + [
            pltpu.SemaphoreType.DMA((3, 3, pairs, most)),
            pltpu.SemaphoreType.DMA((3, 3, pairs, most)),
            pltpu.SemaphoreType.DMA((3, pairs)),
        ],
        compiler_params=pltpu.CompilerParams(
            collective_id=0, has_side_effects=True, vmem_limit_bytes=60 * 1024 * 1024
        ),
        cost_estimate=pl.CostEstimate(flops=0, bytes_accessed=grads.size * 4, transcendentals=0),
    )(grads.reshape(chunks, l0, l1, l2, rows, width), gains.reshape(l0, l1, l2, 8, 128))


def from_behind(x, axis, by):
    devices = lax.axis_size(axis)
    pairs = [(i, i + by) for i in range(devices) if 0 <= i + by < devices]
    return lax.ppermute(x, axis, pairs)


def layer_norm(values, gain):
    row_mean = jnp.mean(values, axis=-1, keepdims=True)
    centred = values - row_mean
    row_var = jnp.mean(centred * centred, axis=-1, keepdims=True)
    return centred * lax.rsqrt(row_var + epsilon) * gain


def front_half(all_rows, gain_attn, w_qkv):
    normed = layer_norm(all_rows, gain_attn).astype(jnp.bfloat16)
    projected = jnp.dot(normed, w_qkv, preferred_element_type=jnp.float32).astype(jnp.bfloat16)
    return (normed, projected)


def latent_operand(projected, tok_rows, model_width):
    return projected[tok_rows:, model_width:]


def back_half(all_rows, projected, remote_rows, allowed, weights):
    gain_attn, w_qkv, w_out, gain_mlp, w_up, w_down = weights
    row_count, model_width = all_rows.shape
    head_size = model_width // HEADS
    remote_pairs = remote_rows[:, remote_rows.shape[1] - 2 * model_width :]
    queries = projected[:, :model_width].reshape(row_count, HEADS, head_size)
    key_rows = jnp.concatenate(
        [projected[:, model_width : 2 * model_width], remote_pairs[:, :model_width]], axis=0
    )
    value_rows = jnp.concatenate(
        [projected[:, 2 * model_width :], remote_pairs[:, model_width:]], axis=0
    )
    key_rows = key_rows.reshape(-1, HEADS, head_size)
    value_rows = value_rows.reshape(-1, HEADS, head_size)
    scores = jnp.einsum(
        "qhd,khd->hqk", queries, key_rows, preferred_element_type=jnp.float32
    ) * head_size ** (-0.5)
    attn_weights = jax.nn.softmax(jnp.where(allowed[None], scores, masked_score), axis=-1)
    attn_low = attn_weights.astype(jnp.bfloat16)
    mixed_low = jnp.einsum("hqk,khd->qhd", attn_low, value_rows, preferred_element_type=jnp.float32)
    mixed_low = mixed_low.reshape(row_count, model_width).astype(jnp.bfloat16)
    mid_rows = all_rows + jnp.dot(mixed_low, w_out, preferred_element_type=jnp.float32)
    normed_mlp = layer_norm(mid_rows, gain_mlp).astype(jnp.bfloat16)
    up_proj = jnp.dot(normed_mlp, w_up, preferred_element_type=jnp.float32)
    activated = jax.nn.gelu(up_proj).astype(jnp.bfloat16)
    result = mid_rows + jnp.dot(activated, w_down, preferred_element_type=jnp.float32)
    return dict(
        queries=queries,
        key_rows=key_rows,
        value_rows=value_rows,
        attn_weights=attn_weights,
        attn_low=attn_low,
        mixed_low=mixed_low,
        mid_rows=mid_rows,
        normed_mlp=normed_mlp,
        up_proj=up_proj,
        activated=activated,
        result=result,
    )


def section_backward(saved, d_result, all_rows, normed, allowed, weights, latent_start):
    gain_attn, w_qkv, w_out, gain_mlp, w_up, w_down = weights
    row_count, model_width = all_rows.shape
    head_size = model_width // HEADS
    score_scale = head_size ** (-0.5)
    d_low = d_result.astype(jnp.bfloat16)
    grad_down = jnp.dot(d_low.T, saved["activated"], preferred_element_type=jnp.float32)
    d_activated = jnp.dot(d_low, w_down.T, preferred_element_type=jnp.float32)
    unused_up, gelu_back = jax.vjp(jax.nn.gelu, saved["up_proj"])
    d_up = gelu_back(d_activated)[0].astype(jnp.bfloat16)
    grad_up = jnp.dot(d_up.T, saved["normed_mlp"], preferred_element_type=jnp.float32)
    d_normed_mlp = jnp.dot(d_up, w_up.T, preferred_element_type=jnp.float32)
    unused_mid, second_back = jax.vjp(layer_norm, saved["mid_rows"], gain_mlp)
    d_mid_norm, grad_gain_mlp = second_back(d_normed_mlp)
    d_mid = d_result + d_mid_norm
    d_mid_low = d_mid.astype(jnp.bfloat16)
    grad_out = jnp.dot(d_mid_low.T, saved["mixed_low"], preferred_element_type=jnp.float32)
    d_mixed = jnp.dot(d_mid_low, w_out.T, preferred_element_type=jnp.float32).astype(jnp.bfloat16)
    d_mixed = d_mixed.reshape(row_count, HEADS, head_size)
    d_weights = jnp.einsum(
        "qhd,khd->hqk", d_mixed, saved["value_rows"], preferred_element_type=jnp.float32
    )
    d_values = jnp.einsum(
        "hqk,qhd->khd", saved["attn_low"], d_mixed, preferred_element_type=jnp.float32
    )
    attn_weights = saved["attn_weights"]
    d_scores = attn_weights * (
        d_weights - jnp.sum(attn_weights * d_weights, axis=-1, keepdims=True)
    )
    d_scores_low = jnp.where(allowed[None], d_scores, 0.0).astype(jnp.bfloat16)
    d_queries = (
        jnp.einsum(
            "hqk,khd->qhd", d_scores_low, saved["key_rows"], preferred_element_type=jnp.float32
        )
        * score_scale
    )
    d_keys = (
        jnp.einsum(
            "hqk,qhd->khd", d_scores_low, saved["queries"], preferred_element_type=jnp.float32
        )
        * score_scale
    )
    remote_part = jnp.concatenate(
        [
            d_keys[row_count:].reshape(-1, model_width),
            d_values[row_count:].reshape(-1, model_width),
        ],
        axis=1,
    )
    own_part = lax.psum_scatter(remote_part, "dp", scatter_dimension=0, tiled=True)
    local_pairs = jnp.concatenate(
        [
            d_keys[:row_count].reshape(row_count, model_width),
            d_values[:row_count].reshape(row_count, model_width),
        ],
        axis=1,
    )
    local_pairs = jnp.concatenate(
        [local_pairs[:latent_start], local_pairs[latent_start:] + own_part], axis=0
    )
    d_projected = jnp.concatenate(
        [d_queries.reshape(row_count, model_width), local_pairs], axis=1
    ).astype(jnp.bfloat16)
    grad_qkv = jnp.dot(d_projected.T, normed, preferred_element_type=jnp.float32)
    d_normed = jnp.dot(d_projected, w_qkv.T, preferred_element_type=jnp.float32)
    unused_rows, first_back = jax.vjp(layer_norm, all_rows, gain_attn)
    d_rows_norm, grad_gain_attn = first_back(d_normed)
    return (
        d_mid + d_rows_norm,
        (grad_gain_attn, grad_qkv, grad_out, grad_gain_mlp, grad_up, grad_down),
    )


def packed(grads, n):
    gain_first, qkv_grad, out_grad, gain_second, up_grad, down_grad = grads
    width = out_grad.shape[0]
    rows = width // n

    def by_rows(grad):
        return grad.reshape(n, -1, rows, width).transpose(1, 0, 2, 3).astype(jnp.bfloat16)

    down = down_grad.reshape(n, rows, -1, width).transpose(2, 0, 1, 3).astype(jnp.bfloat16)
    chunks = jnp.concatenate([down, by_rows(up_grad), by_rows(out_grad), by_rows(qkv_grad)], axis=0)
    gains = jnp.stack([gain_first.reshape(n, rows), gain_second.reshape(n, rows)], axis=1)
    return chunks, jnp.pad(gains, ((0, 0), (0, 6), (0, 128 - rows)))


def shards(
    grid,
    tokens,
    latents,
    slot_group,
    image_groups,
    gain_attn,
    w_qkv,
    w_out,
    gain_mlp,
    w_up,
    w_down,
    d_tokens,
    d_latents,
):
    micro = tokens.shape[0]
    tok_rows = tokens.shape[1]
    lat_rows = latents.shape[1]
    model_width = tokens.shape[2]
    local_groups = tok_rows // GROUP
    section_index = lax.axis_index("section")
    is_global = section_index == 1
    dp_index = lax.axis_index("dp")
    weights = (gain_attn[0], w_qkv[0], w_out[0], gain_mlp[0], w_up[0], w_down[0])
    image_ends = jnp.cumsum(image_groups, axis=1)
    slot_images = jnp.sum(
        (image_ends[:, None, :] <= slot_group[:, :, None]).astype(jnp.int32), axis=2
    )
    slot_total = slot_group.shape[1]
    row_group = jnp.concatenate([jnp.arange(tok_rows) // GROUP, jnp.arange(lat_rows) // LAT])
    row_latent = jnp.concatenate(
        [jnp.zeros((tok_rows,), jnp.bool_), jnp.ones((lat_rows,), jnp.bool_)]
    )
    same_group = row_group[:, None] == row_group[None, :]
    local_mask = jnp.where(
        is_global, (~row_latent)[:, None] & row_latent[None, :] & same_group, same_group
    )
    group_match = row_group[:, None] == jnp.arange(local_groups)[None, :]

    def key_images(batch):
        images_row = lax.dynamic_index_in_dim(slot_images, batch, 0, keepdims=False)
        return (images_row, jnp.broadcast_to(images_row[:, None], (slot_total, LAT)).reshape(-1))

    def allowed_for(batch):
        images_row, key_image = key_images(batch)
        own_images = lax.dynamic_slice_in_dim(images_row, dp_index * local_groups, local_groups)
        row_image = jnp.sum(jnp.where(group_match, own_images[None, :], 0), axis=1)
        remote_mask = is_global & row_latent[:, None] & (row_image[:, None] == key_image[None, :])
        return jnp.concatenate([local_mask, remote_mask], axis=1)

    def forward_turn(received, turn):
        recv_tokens, recv_latents = received
        batch = jnp.clip(turn - section_index, 0, micro - 1)
        own_tok = lax.dynamic_index_in_dim(tokens, batch, 0, keepdims=False)
        own_lat = lax.dynamic_index_in_dim(latents, batch, 0, keepdims=False)
        input_rows = jnp.concatenate(
            [
                jnp.where(is_global, recv_tokens, own_tok),
                jnp.where(is_global, recv_latents, own_lat),
            ],
            axis=0,
        )
        all_rows = input_rows.astype(jnp.float32)
        normed, projected = front_half(all_rows, weights[0], weights[1])
        remote_rows = lax.all_gather(
            latent_operand(projected, tok_rows, model_width), "dp", axis=0, tiled=True
        )
        saved = back_half(all_rows, projected, remote_rows, allowed_for(batch), weights)
        result = saved["result"]
        result_low = result.astype(jnp.bfloat16)
        stored = jnp.where(is_global, result, result_low.astype(jnp.float32))
        passed_on = from_behind((result_low[:tok_rows], result_low[tok_rows:]), "section", 1)
        return passed_on, (input_rows, stored[:tok_rows], stored[tok_rows:])

    nothing = (
        jnp.zeros((tok_rows, model_width), jnp.bfloat16),
        jnp.zeros((lat_rows, model_width), jnp.bfloat16),
    )
    turns = jnp.arange(micro + 1)
    unused_end, (kept_rows, tok_outputs, lat_outputs) = lax.scan(forward_turn, nothing, turns)

    def backward_turn(carry, turn):
        (recv_grad_tok, recv_grad_lat), totals = carry
        raw_batch = micro - turn - section_index
        valid = ((raw_batch >= 0) & (raw_batch < micro)).astype(jnp.float32)
        batch = jnp.clip(raw_batch, 0, micro - 1)
        all_rows = lax.dynamic_index_in_dim(
            kept_rows, batch + section_index, 0, keepdims=False
        ).astype(jnp.float32)
        normed, projected = front_half(all_rows, weights[0], weights[1])
        remote_rows = lax.all_gather(
            latent_operand(projected, tok_rows, model_width), "dp", axis=0, tiled=True
        )
        allowed = allowed_for(batch)
        saved = back_half(all_rows, projected, remote_rows, allowed, weights)
        given = (
            jnp.concatenate(
                [
                    lax.dynamic_index_in_dim(d_tokens, batch, 0, keepdims=False),
                    lax.dynamic_index_in_dim(d_latents, batch, 0, keepdims=False),
                ],
                axis=0,
            )
            * valid
        )
        passed = jnp.concatenate([recv_grad_tok, recv_grad_lat], axis=0).astype(jnp.float32)
        d_result = jnp.where(is_global, given, passed)
        d_rows, grads = section_backward(
            saved, d_result, all_rows, normed, allowed, weights, tok_rows
        )
        totals = tuple((accum + piece for accum, piece in zip(totals, grads)))
        d_rows_low = d_rows.astype(jnp.bfloat16)
        stored = jnp.where(is_global, d_rows_low.astype(jnp.float32), d_rows)
        sent = from_behind((d_rows_low[:tok_rows], d_rows_low[tok_rows:]), "section", -1)
        return (sent, totals), (stored[:tok_rows], stored[tok_rows:])

    totals = tuple(
        jnp.zeros(w.shape[::-1] if w.ndim == 2 else w.shape, jnp.float32) for w in weights
    )
    (unused_sent, totals), (tok_grads, lat_grads) = lax.scan(
        backward_turn, (nothing, totals), turns
    )
    chunks, gains = packed(totals, lax.axis_size("dp"))
    summed, gain_sums = spread(grid, chunks, gains)
    rows = summed.shape[1]
    layer_tokens = lax.dynamic_slice_in_dim(tok_outputs, section_index, micro, 0)[None]
    layer_latents = lax.dynamic_slice_in_dim(lat_outputs, section_index, micro, 0)[None]
    grad_tokens = lax.dynamic_slice_in_dim(tok_grads, 1 - section_index, micro, 0)[::-1][
        None
    ]
    grad_latents = lax.dynamic_slice_in_dim(lat_grads, 1 - section_index, micro, 0)[
        ::-1
    ][None]
    return (
        layer_tokens,
        layer_latents,
        grad_tokens,
        grad_latents,
        gain_sums[0:1, :rows],
        summed[9:].reshape(-1, model_width).T[None],
        summed[8].T[None],
        gain_sums[1:2, :rows],
        summed[4:8].reshape(-1, model_width).T[None],
        summed[0:4].transpose(0, 2, 1).reshape(-1, rows)[None],
    )


F32 = jnp.float32
LOW = jnp.bfloat16
HEAD_PAD = 16
TILE = 768


def nn(a, b):
    return jnp.dot(a, b, preferred_element_type=F32)


def nt(a, b):
    return lax.dot_general(a, b, (((1,), (1,)), ((), ())), preferred_element_type=F32)


def tn(a, b):
    return lax.dot_general(a, b, (((0,), (0,)), ((), ())), preferred_element_type=F32)


def row_mean(values):
    return jnp.mean(values, axis=-1, keepdims=True)


def row_stats(load, spans):
    means = [row_mean(load(r)) for r in spans]
    scales = []
    for r, mean in zip(spans, means):
        centred = load(r) - mean
        scales.append(lax.rsqrt(row_mean(centred * centred) + epsilon))
    return means, scales


def at(start, size):
    return pl.ds(pl.multiple_of(start, size), size)


def class_max(s):
    for by in (16, 32, 64):
        s = jnp.maximum(s, pltpu.roll(s, by, 1))
    return s


def class_sum(s):
    for by in (16, 32, 64):
        s = s + pltpu.roll(s, by, 1)
    return s


def layer_kernel(
    n,
    tokens,
    latents,
    slots,
    slot_at,
    image_at,
    gain_attn,
    gain_mlp,
    w_qkv,
    w_out,
    w_up,
    w_down,
    d_tokens,
    d_latents,
    out_tok,
    out_lat,
    grad_tok,
    grad_lat,
    grads,
    summed,
    gain_sums,
    wq,
    wo,
    wu,
    wd,
    xb,
    n1,
    proj,
    mixed,
    mid,
    n2,
    act,
    dup,
    yb,
    dy,
    ef,
    tmp,
    out,
    probs,
    probs_lat,
    scores,
    slopes,
    latf,
    mixf,
    key_mask,
    qbd,
    kbd,
    vbd,
    kv_all,
    kvg_send,
    kvg_recv,
    stage,
    gains,
    leaving,
    own_a,
    own_b,
    own_c,
    land1_a,
    land1_b,
    land1_c,
    land2_a,
    land2_b,
    land2_c,
    land3_a,
    land3_b,
    land3_c,
    land4_a,
    land4_b,
    land4_c,
    land_g,
    load_sem,
    stage_sem,
    own_sem,
    leave_sem,
    send_sem,
    recv_sem,
    gain_s,
    gain_r,
    relay_send,
    relay_recv,
    kv_sem_s,
    kv_sem_r,
    kvg_sem_s,
    kvg_sem_r,
):
    rows, width = xb.shape
    ff = act.shape[1]
    tok = tokens.shape[0]
    lat = latents.shape[0]
    half = lat // LAT
    pairs = width // 128
    me = lax.axis_index("dp")
    section = lax.axis_index("section")
    first = section == 0
    second = section == 1
    partner = (me, 1 - section)

    loads = [
        pltpu.make_async_copy(src, dst, load_sem.at[i])
        for i, (src, dst) in enumerate(((w_qkv, wq), (w_out, wo), (w_up, wu), (w_down, wd)))
    ]
    x_loads = [
        pltpu.make_async_copy(tokens, xb.at[lat:rows], load_sem.at[4]),
        pltpu.make_async_copy(latents, xb.at[0:lat], load_sem.at[5]),
    ]
    e_loads = [
        pltpu.make_async_copy(d_tokens, ef.at[lat:rows], load_sem.at[6]),
        pltpu.make_async_copy(d_latents, ef.at[0:lat], load_sem.at[7]),
    ]

    @pl.when(first)
    def _():
        for copy in x_loads:
            copy.start()

    for copy in loads:
        copy.start()

    @pl.when(second)
    def _():
        for copy in e_loads:
            copy.start()

    barrier = pltpu.get_barrier_semaphore()
    pl.semaphore_signal(barrier, inc=1, device_id=partner, device_id_type=MESH)

    here = [lax.rem(me // (1 << bit), 2) for bit in range(4)]

    def across(bit):
        return (me + (1 - 2 * here[bit]) * (1 << bit), section)

    @pl.when(second)
    def _():
        for shift in range(1, n):
            pl.semaphore_signal(
                barrier, inc=1, device_id=(lax.rem(me + shift, n), section), device_id_type=MESH
            )
        pl.semaphore_wait(barrier, n)

    @pl.when(first)
    def _():
        for bit in range(4):
            pl.semaphore_signal(barrier, inc=1, device_id=across(bit), device_id_type=MESH)

    def relay(back, band):
        low, high = ((0, rows // 3), (rows // 3, 2 * rows // 3), (2 * rows // 3, rows))[band]
        if not back:
            low, high = ((0, lat), (lat, lat + GROUP), (lat + GROUP, rows))[band]
        return pltpu.make_async_remote_copy(
            src_ref=yb.at[low:high],
            dst_ref=(dy if back else xb).at[low:high],
            send_sem=relay_send.at[3 * back + band],
            recv_sem=relay_recv.at[3 * back + band],
            device_id=partner,
            device_id_type=MESH,
        )

    def kv_copy(shift, incoming):
        slot = lax.rem(me + n - shift, n) if incoming else me
        return pltpu.make_async_remote_copy(
            src_ref=kv_all.at[me], dst_ref=kv_all.at[slot],
            send_sem=kv_sem_s.at[shift - 1], recv_sem=kv_sem_r.at[shift - 1],
            device_id=(lax.rem(me + shift, n), section), device_id_type=MESH,
        )

    def kvg_copy(shift):
        there = lax.rem(me + shift, n)
        return pltpu.make_async_remote_copy(
            src_ref=kvg_send.at[there], dst_ref=kvg_recv.at[shift - 1],
            send_sem=kvg_sem_s.at[shift - 1], recv_sem=kvg_sem_r.at[shift - 1],
            device_id=(there, section), device_id_type=MESH,
        )

    chunks = [slice(c, c + 64) for c in range(0, GROUP, 64)]
    lane = lax.broadcasted_iota(jnp.int32, (1, 128), 1)
    halves = [(lane < 64).astype(F32).astype(LOW), (lane >= 64).astype(F32).astype(LOW)]
    eighths = [(h.astype(F32) * 0.125).astype(LOW) for h in halves]
    heads = (
        lax.broadcasted_iota(jnp.int32, (HEAD_PAD, width), 1) // 64
        == lax.broadcasted_iota(jnp.int32, (HEAD_PAD, width), 0)
    ).astype(F32)

    def block_diagonal(dst, base, src, row, column, scale):
        for i in range(LAT):
            line = src[row + i : row + i + 1, column : column + width] * scale
            dst[base + i * HEAD_PAD : base + (i + 1) * HEAD_PAD, :] = (line * heads).astype(LOW)

    def head_sum(dst, row, column, value, scale, add):
        for i in range(LAT):
            line = jnp.sum(
                value[i * HEAD_PAD : (i + 1) * HEAD_PAD] * heads, axis=0, keepdims=True
            )
            line = line * scale
            if add:
                line = line + dst[row + i : row + i + 1, column : column + width]
            dst[row + i : row + i + 1, column : column + width] = line

    def bands(body, lo, hi, size):
        def one(i, carry):
            body(pl.ds(pl.multiple_of(lo + i * size, 16), size))
            return carry

        lax.fori_loop(0, (hi - lo) // size, one, 0)

    third = rows // 3

    def grouped(body, lo, hi, count):
        def one(i, carry):
            base = lo + i * 16 * count
            body([pl.ds(pl.multiple_of(base + 16 * g, 16), 16) for g in range(count)])
            return carry

        lax.fori_loop(0, (hi - lo) // (16 * count), one, 0)

    def norm(load, gain, dst, lo, hi, count):
        def body(spans):
            means, scales = row_stats(load, spans)
            for r, mean, scale in zip(spans, means, scales):
                dst[r, :] = ((load(r) - mean) * scale * gain[...]).astype(LOW)

        grouped(body, lo, hi, count)

    def norm_back(load, grad, gain, gain_rows, store, lo, hi, count):
        def body(spans):
            means, scales = row_stats(load, spans)
            firsts, seconds = [], []
            kept = gains[0, gain_rows, :]
            for r, mean, scale in zip(spans, means, scales):
                along = grad[r, :] * ((load(r) - mean) * scale)
                kept = kept + along[0:8] + along[8:16]
                firsts.append(row_mean(grad[r, :] * gain[...]))
                seconds.append(row_mean(along * gain[...]))
            gains[0, gain_rows, :] = kept
            for r, mean, scale, one, two in zip(spans, means, scales, firsts, seconds):
                hat = (load(r) - mean) * scale
                store(r, ef[r, :] + scale * (grad[r, :] * gain[...] - one - hat * two))

        grouped(body, lo, hi, count)

    def tiles(count, body, size=TILE):
        def one(i, carry):
            body(at(i * size, size))
            return carry

        lax.fori_loop(0, count, one, 0)

    @pl.when(first)
    def _():
        for copy in x_loads:
            copy.wait()

    @pl.when(second)
    def _():
        spots = lax.broadcasted_iota(jnp.int32, (n, n * lat), 1) // lat
        spread_out = (spots == lax.broadcasted_iota(jnp.int32, (n, n * lat), 0)).astype(F32)
        groups = nn(slots[...].astype(F32).astype(LOW), spread_out.astype(LOW))
        of_micro = lax.rem(lax.broadcasted_iota(jnp.int32, (1, n * lat), 1), lat) // LAT
        for m in range(half):
            images = jnp.zeros((1, n * lat), F32)
            own_image = jnp.float32(0)
            end = jnp.int32(0)
            for i in range(image_at.shape[1]):
                end = end + image_at[m, i]
                images += jnp.where(end.astype(F32) <= groups[m : m + 1], 1.0, 0.0)
                own_image += jnp.where(end <= slot_at[m, me], 1.0, 0.0)
            seen = (images == own_image) & (of_micro == m)
            key_mask[m : m + 1, :] = jnp.where(seen, 0.0, masked_score)

    def load_in(r):
        return xb[r, :].astype(F32)

    def load_mid(r):
        return mid[r, :]

    def lat_bias(m, shape, axis):
        return jnp.where(
            lax.broadcasted_iota(jnp.int32, shape, axis) // LAT == m, 0.0, masked_score
        ).astype(F32)

    @pl.when(first)
    def _():
        norm(load_in, gain_attn, n1, 0, rows, 11)
        loads[0].wait()

        def project(c):
            proj[:, c] = nn(n1[...], wq[:, c]).astype(LOW)

        tiles(3 * width // TILE, project)
        latf[...] = proj[0:lat, :].astype(F32)

        def one_pair(it, side):
            m, p = it // pairs, lax.rem(it, pairs)
            r = pl.ds(pl.multiple_of(lat + m * GROUP, 16), GROUP)
            q = proj[r, at(p * 128, 128)]
            k = proj[r, at(width + p * 128, 128)]
            v = proj[r, at(2 * width + p * 128, 128)]
            kl = proj[0:lat, at(width + p * 128, 128)]
            vl = proj[0:lat, at(2 * width + p * 128, 128)]
            bias = lat_bias(m, (lat, GROUP), 0)
            total = jnp.zeros((GROUP, 128), F32)
            for e in (0, 1):
                qe = q * eighths[e]
                s = scores.at[2 * side + e]
                s[...] = nt(k, qe)
                sl = nt(kl, qe) + bias
                top = jnp.max(sl, axis=0, keepdims=True)
                for c in chunks:
                    top = jnp.maximum(top, jnp.max(s[c, :], axis=0, keepdims=True))
                el = jnp.exp(sl - top)
                whole_sum = jnp.sum(el, axis=0, keepdims=True)
                for c in chunks:
                    et = jnp.exp(s[c, :] - top)
                    s[c, :] = et
                    whole_sum += jnp.sum(et, axis=0, keepdims=True)
                scale = 1.0 / whole_sum
                for c in chunks:
                    probs[2 * it + e, c, :] = (s[c, :] * scale).astype(LOW)
                pe = (el * scale).astype(LOW)
                probs[2 * it + e, GROUP : GROUP + lat, :] = pe
                total += tn(probs[2 * it + e, 0:GROUP, :], v * halves[e])
                total += tn(pe, vl * halves[e])
            mixed[r, at(p * 128, 128)] = total.astype(LOW)

        def pair(i, carry):
            one_pair(2 * i, 0)
            one_pair(2 * i + 1, 1)
            return carry

        lax.fori_loop(0, half * pairs // 2, pair, 0)
        for m in range(half):
            r = slice(lat + m * GROUP, lat + (m + 1) * GROUP)
            b = slice(m * 128, (m + 1) * 128)
            block_diagonal(qbd, m * 128, latf, m * LAT, 0, 0.125)
            s = nt(qbd[b, :], proj[r, width : 2 * width])
            sl = nt(qbd[b, :], proj[0:lat, width : 2 * width]) + lat_bias(m, (128, lat), 1)
            top = jnp.maximum(
                jnp.max(s, axis=1, keepdims=True), jnp.max(sl, axis=1, keepdims=True)
            )
            et = jnp.exp(s - top)
            el = jnp.exp(sl - top)
            scale = 1.0 / (
                jnp.sum(et, axis=1, keepdims=True) + jnp.sum(el, axis=1, keepdims=True)
            )
            pt = (et * scale).astype(LOW)
            pe = (el * scale).astype(LOW)
            probs_lat[b, 0:GROUP] = pt
            probs_lat[b, GROUP : GROUP + lat] = pe
            o = nn(pt, proj[r, 2 * width :]) + nn(pe, proj[0:lat, 2 * width :])
            head_sum(mixf, m * LAT, 0, o, 1.0, False)
        mixed[0:lat, :] = mixf[...].astype(LOW)

    keys = n * lat

    root = 0.7978845608028654

    def mlp_in(lo, hi, count, with_dact=False):
        r0 = slice(lo, hi)
        mid[r0, :] = xb[r0, :].astype(F32) + nn(mixed[r0, :], wo[...])

        norm(load_mid, gain_mlp, n2, lo, hi, count)

        def up_tile(dst, i):
            dst[r0, 0:512] = nn(n2[r0, :], wu[:, at(i * 512, 512)])

        def gelu(src, i):
            c = at(i * 512, 512)
            for g in range(lo, hi, 16):
                r = slice(g, g + 16)
                up = src[r, 0:512]
                square = up * up
                t = jnp.tanh(up * (root + (root * 0.044715) * square))
                gate = 0.5 + 0.5 * t
                value = up * gate
                slope = gate + (value + value) * (1.0 - gate) * (
                    root + (3.0 * root * 0.044715) * square
                )
                act[r, c] = value.astype(LOW)
                if with_dact:
                    slope = slope * dup[r, c].astype(F32)
                dup[r, c] = slope.astype(LOW)

        last = ff // 512 - 1

        def widen(i, carry):
            up_tile(out, 2 * i + 1)
            gelu(tmp, 2 * i)
            up_tile(tmp, jnp.minimum(2 * i + 2, last))
            gelu(out, 2 * i + 1)
            return carry

        up_tile(tmp, 0)
        lax.fori_loop(0, ff // 1024, widen, 0)

    out_copies = [
        pltpu.make_async_copy(out.at[lat:rows], out_tok, load_sem.at[8]),
        pltpu.make_async_copy(out.at[0:lat], out_lat, load_sem.at[9]),
    ]
    grad_copies = [
        pltpu.make_async_copy(out.at[lat:rows], grad_tok, load_sem.at[8]),
        pltpu.make_async_copy(out.at[0:lat], grad_lat, load_sem.at[9]),
    ]

    def layer_output(low, high, passed_on):
        r = slice(low, high)
        y = mid[r, :] + nn(act[r, :], wd[...])
        if passed_on:
            narrow_y = y.astype(LOW)
            yb[r, :] = narrow_y
            y = narrow_y.astype(F32)
        out[r, :] = y

    @pl.when(first)
    def _():
        for copy in loads[1:]:
            copy.wait()
        mlp_in(0, lat + GROUP, 17)
        layer_output(0, lat + GROUP, True)
        pl.semaphore_wait(barrier, 5)
        relay(0, 0).start()
        relay(0, 1).start()
        mlp_in(lat + GROUP, rows, 16)
        layer_output(lat + GROUP, rows, True)
        relay(0, 2).start()
        for copy in out_copies:
            copy.start()

    @pl.when(second)
    def _():
        for copy in e_loads:
            copy.wait()

        def narrow_e(r):
            dy[r, :] = ef[r, :].astype(LOW)

        bands(narrow_e, 0, rows, third)
        for copy in loads:
            copy.wait()

        def early(c):
            dup[:, c] = nt(dy[...], wd[c, :]).astype(LOW)

        tiles(ff // TILE, early)
        relay(0, 0).wait_recv()
        norm(load_in, gain_attn, n1, 0, lat, 1)
        lat_proj = nn(n1[0:lat, :], wq[...]).astype(LOW)
        kv_all[me] = lat_proj[:, width:]
        latf[...] = lat_proj.astype(F32)
        for shift in range(1, n):
            kv_copy(shift, False).start()
        for m in range(half):
            relay(0, 1 + m).wait_recv()
            low, high = lat + m * GROUP, lat + (m + 1) * GROUP
            r = slice(low, high)
            b = slice(m * 128, (m + 1) * 128)
            norm(load_in, gain_attn, n1, low, high, 16)
            proj[r, :width] = nn(n1[r, :], wq[:, :width]).astype(LOW)
            block_diagonal(qbd, m * 128, latf, m * LAT, 0, 0.125)
            block_diagonal(kbd, m * 128, latf, m * LAT, width, 1.0)
            block_diagonal(vbd, m * 128, latf, m * LAT, 2 * width, 1.0)
            s = nt(proj[r, :width] * jnp.asarray(0.125, LOW), kbd[b, :])
            et = jnp.exp(s - class_max(s))
            pt = (et / class_sum(et)).astype(LOW)
            probs[m, 0:GROUP, 0:128] = pt
            mixed[r, :] = nn(pt, vbd[b, :]).astype(LOW)
            mlp_in(low, high, 16, True)
        for shift in range(1, n):
            kv_copy(shift, True).wait_recv()
        k = kv_all[:, :, :width].reshape(keys, width)
        v = kv_all[:, :, width:].reshape(keys, width)
        for m in range(half):
            b = slice(m * 128, (m + 1) * 128)
            s = nt(qbd[b, :], k) + key_mask[m : m + 1, :]
            et = jnp.exp(s - jnp.max(s, axis=1, keepdims=True))
            pt = (et / jnp.sum(et, axis=1, keepdims=True)).astype(LOW)
            probs_lat[b, 0:keys] = pt
            head_sum(mixf, m * LAT, 0, nn(pt, v), 1.0, False)
        mixed[0:lat, :] = mixf[...].astype(LOW)
        mlp_in(0, lat, 1, True)

    @pl.when(first)
    def _():
        for band in range(3):
            relay(1, band).wait_recv()

        def widen_e(r):
            ef[r, :] = dy[r, :].astype(F32)

        bands(widen_e, 0, rows, third)

    part = 384
    unit = width // n
    many = part // unit

    def staged(slot, piece, chunk, share):
        return pltpu.make_async_copy(
            stage.at[slot, piece],
            grads.at[
                chunk,
                share // 8,
                lax.rem(share // 4, 2),
                lax.rem(share // 2, 2),
                lax.rem(share, 2),
            ],
            stage_sem.at[slot, piece],
        )

    def drain(slot):
        def one(piece, carry):
            staged(slot, piece, 0, 0).wait()
            return carry

        lax.fori_loop(0, many, one, 0)

    def weight_grad(place, start, count, left, *rights, settled=True):
        def one(i, carry):
            turned = left(i).T
            for at_right, right in enumerate(rights):
                tile = i * len(rights) + at_right
                slot = lax.rem(tile, 2)
                value = nn(turned, right(i)).astype(LOW)

                if settled:

                    @pl.when(tile >= start * len(rights) + 2)
                    def _():
                        drain(slot)

                else:
                    drain(slot)

                for piece in range(many):
                    stage[slot, piece] = value[piece * unit : (piece + 1) * unit]
                    staged(slot, piece, *place(i, at_right, piece)).start()
            return carry

        lax.fori_loop(start, start + count, one, 0)

    def settle():
        for slot in (0, 1):
            drain(slot)

    orders = ((0, 2, 1, 3), (1, 0, 2, 3), (2, 1, 0, 3))
    kinds = (0, 1, 2)
    own_buf = (own_a, own_b, own_c)
    per_part = width // part
    wide = ff // width
    groups = land1_a.shape[0]
    land = (
        (land1_a, land1_b, land1_c),
        (land2_a, land2_b, land2_c),
        (land3_a, land3_b, land3_c),
        (land4_a, land4_b, land4_c),
    )

    def spot(kind, second_bit, third_bit):
        return (third_bit, second_bit) if kind == 1 else (second_bit, third_bit)

    def source(kind, phase, k, theirs):
        mine = [here[bit] for bit in orders[kind]]
        pick = [1 - bit for bit in mine] if theirs else mine
        base = land[0][kind]
        every = slice(None)
        if phase == 0:
            chunk = grads.at[3 * k + kind]
            return (chunk.at[:, :, :, pick[0]], chunk.at[:, :, pick[0]], chunk.at[:, pick[0]])[kind]
        if phase == 1:
            return base.at[(k, every, *spot(kind, pick[1], every))]
        if phase == 2:
            return base.at[(k, every, *spot(kind, mine[1], pick[2]))]
        return base.at[(k, pick[3], *spot(kind, mine[1], mine[2]))]

    def copy_of(kind, phase, k):
        return pltpu.make_async_remote_copy(
            src_ref=source(kind, phase, k, True),
            dst_ref=land[phase][kind].at[k],
            send_sem=send_sem.at[kind, phase, k],
            recv_sem=recv_sem.at[kind, phase, k],
            device_id=across(orders[kind][phase]),
            device_id_type=MESH,
        )

    def own(kind, k):
        return pltpu.make_async_copy(
            source(kind, 0, k, False), own_buf[kind], own_sem.at[kind]
        )

    def leave(kind, k):
        slot = lax.rem(k, 2)
        return pltpu.make_async_copy(
            leaving.at[slot, kind], summed.at[3 * k + kind], leave_sem.at[slot, kind]
        )

    def launch(*chunks):
        for chunk in chunks:
            copy_of(chunk % 3, 0, chunk // 3).start()

    def onward(phase, k):
        for kind in kinds:
            if phase == 0:
                own(kind, k).wait()
            copy_of(kind, phase, k).wait_recv()
            base, into = land[0][kind], land[phase][kind]
            mine = [here[bit] for bit in orders[kind]]
            if phase == 0:

                def add(i, carry):
                    for j in (0, 1):
                        for h in (0, 1):
                            total = own_buf[kind][i, j, h].astype(F32)
                            total += base[k, i, j, h].astype(F32)
                            base[k, i, j, h] = total.astype(LOW)
                    return carry

                lax.fori_loop(0, 2, add, 0)
            elif phase == 1:
                for i in (0, 1):
                    for h in (0, 1):
                        at_share = (k, i, *spot(kind, mine[1], h))
                        total = base[at_share].astype(F32) + into[k, i, h].astype(F32)
                        base[at_share] = total.astype(LOW)
            elif phase == 2:
                for i in (0, 1):
                    at_share = (k, i, *spot(kind, mine[1], mine[2]))
                    total = base[at_share].astype(F32) + into[k, i].astype(F32)
                    base[at_share] = total.astype(LOW)
            else:
                total = base[(k, mine[3], *spot(kind, mine[1], mine[2]))].astype(F32)
                total += into[k].astype(F32)
                slot = lax.rem(k, 2)

                @pl.when(k >= 2)
                def _():
                    leave(kind, k - 2).wait()

                leaving[slot, kind] = total
                leave(kind, k).start()
            if phase < 3:
                copy_of(kind, phase + 1, k).start()

    def begin():
        for kind in kinds:
            own(kind, 0).start()
        turn(0, 0)

    def turn(t, carry):
        for phase in range(4):
            k = t - phase

            @pl.when((k >= 0) & (k < groups))
            def _():
                onward(phase, k)
                if phase == 0:

                    @pl.when(k + 1 < groups)
                    def _():
                        for kind in kinds:
                            own(kind, k + 1).start()

        return carry

    def up_grad():
        weight_grad(
            lambda i, right, piece: (
                wide + lax.rem(i * many + piece, wide),
                (i * many + piece) // wide,
            ),
            0,
            ff // part,
            lambda i: dup[:, at(i * part, part)],
            lambda i: n2[...],
        )
    def down_grad(pair, settled):
        weight_grad(
            lambda i, right, piece: (2 * pair + right, i * many + piece),
            0,
            per_part,
            lambda i: dy[:, at(i * part, part)],
            lambda i: act[:, 2 * pair * width : (2 * pair + 1) * width],
            lambda i: act[:, (2 * pair + 1) * width : (2 * pair + 2) * width],
            settled=settled,
        )

    down_grad(0, True)
    down_grad(1, False)
    launch(0, 1)

    @pl.when(first)
    def _():
        def unwiden(c):
            dup[:, c] = (nt(dy[...], wd[c, :]) * dup[:, c].astype(F32)).astype(LOW)

        tiles(ff // TILE, unwiden)

    settle()
    launch(2, 3)
    up_grad()

    def to_mid(c):
        tmp[:, c] = nt(dup[...], wu[c, :])

    tiles(width // 256, to_mid, 256)
    settle()
    launch(*range(wide, 2 * wide))
    gains[0] = jnp.zeros_like(gains[0])

    def store_mid(r, total):
        ef[r, :] = total
        dy[r, :] = total.astype(LOW)

    norm_back(load_mid, tmp, gain_mlp, slice(8, 16), store_mid, 0, rows, 11)

    @pl.when(first)
    def _():
        for band in range(3):
            relay(0, band).wait_send()

    def to_mix(c):
        yb[:, c] = nt(dy[...], wo[c, :]).astype(LOW)

    tiles(width // TILE, to_mix)
    mixf[...] = yb[0:lat, :].astype(F32)

    @pl.when(second)
    def _():
        k = kv_all[:, :, :width].reshape(keys, width)
        v = kv_all[:, :, width:].reshape(keys, width)
        for m in range(half):
            b = slice(m * 128, (m + 1) * 128)
            block_diagonal(vbd.at[pl.ds(256, 256)], m * 128, mixf, m * LAT, 0, 1.0)
        both = slice(0, half * 128)
        do = vbd[256 : 256 + half * 128, :]
        pt = probs_lat[both, 0:keys]
        pf = pt.astype(F32)
        dp = nt(do, v)
        along = jnp.sum(pf * dp, axis=1, keepdims=True)
        ds = (pf * (dp - along)).astype(LOW)
        kvg_send[:, :, :width] = tn(ds, qbd[both, :]).astype(LOW).reshape(n, lat, width)
        kvg_send[:, :, width:] = tn(pt, do).astype(LOW).reshape(n, lat, width)
        for shift in range(1, n):
            kvg_copy(shift).start()
        dq = nn(ds, k)
        for m in range(half):
            head_sum(latf, m * LAT, 0, dq[m * 128 : (m + 1) * 128], 0.125, False)
        proj[0:lat, :width] = latf[:, :width].astype(LOW)
        layer_output(0, lat + GROUP, False)
        layer_output(lat + GROUP, rows, False)
        for copy in out_copies:
            copy.start()

    weight_grad(
        lambda i, right, piece: (2 * wide, i * many + piece),
        0,
        width // part,
        lambda i: dy[:, at(i * part, part)],
        lambda i: mixed[...],
    )
    for copy in out_copies:
        copy.wait()

    @pl.when(first)
    def _():
        for m in range(half):
            r = slice(lat + m * GROUP, lat + (m + 1) * GROUP)
            b = slice(m * 128, (m + 1) * 128)
            block_diagonal(vbd, m * 128, mixf, m * LAT, 0, 1.0)
            do = vbd[b, :]
            dp = nt(do, proj[r, 2 * width :])
            dl = nt(do, proj[0:lat, 2 * width :])
            pt = probs_lat[b, 0:GROUP]
            pe = probs_lat[b, GROUP : GROUP + lat]
            pf = pt.astype(F32)
            pg = pe.astype(F32)
            along = jnp.sum(pf * dp, axis=1, keepdims=True) + jnp.sum(
                pg * dl, axis=1, keepdims=True
            )
            ds = (pf * (dp - along)).astype(LOW)
            dsl = (pg * (dl - along)).astype(LOW)
            dq = nn(ds, proj[r, width : 2 * width]) + nn(dsl, proj[0:lat, width : 2 * width])
            head_sum(latf, m * LAT, 0, dq, 0.125, False)
            tmp[r, :] = tn(ds, qbd[b, :])
            out[r, :] = tn(pt, do)
            if m == 0:
                tmp[0:lat, :] = tn(dsl, qbd[b, :])
                out[0:lat, :] = tn(pe, do)
            else:
                tmp[0:lat, :] += tn(dsl, qbd[b, :])
                out[0:lat, :] += tn(pe, do)
        proj[0:lat, :width] = latf[:, :width].astype(LOW)
        settle()
        launch(2 * wide)

        def one_pair(it, side):
            m, p = it // pairs, lax.rem(it, pairs)
            r = pl.ds(pl.multiple_of(lat + m * GROUP, 16), GROUP)
            qc = at(p * 128, 128)
            q = proj[r, qc]
            k = proj[r, at(width + p * 128, 128)]
            v = proj[r, at(2 * width + p * 128, 128)]
            kl = proj[0:lat, at(width + p * 128, 128)]
            vl = proj[0:lat, at(2 * width + p * 128, 128)]
            dx = yb[r, qc]
            dq = jnp.zeros((GROUP, 128), F32)
            dk = tmp[r, qc]
            dv = out[r, qc]
            dkl = tmp[0:lat, qc]
            dvl = out[0:lat, qc]
            for e in (0, 1):
                qe = q * eighths[e]
                de = dx * halves[e]
                s = scores.at[2 * side + e]
                s[...] = nt(v, de)
                dl = nt(vl, de)
                pt = probs[2 * it + e, 0:GROUP, :]
                pe = probs[2 * it + e, GROUP : GROUP + lat, :]
                pg = pe.astype(F32)
                along = jnp.sum(pg * dl, axis=0, keepdims=True)
                for c in chunks:
                    pf = probs[2 * it + e, c, :].astype(F32)
                    along += jnp.sum(pf * s[c, :], axis=0, keepdims=True)
                for c in chunks:
                    pf = probs[2 * it + e, c, :].astype(F32)
                    slopes[2 * side + e, c, :] = (pf * (s[c, :] - along)).astype(LOW)
                ds = slopes[2 * side + e]
                dsl = (pg * (dl - along)).astype(LOW)
                dq += tn(ds, k * halves[e]) + tn(dsl, kl * halves[e])
                dk += nn(ds, qe)
                dkl += nn(dsl, qe)
                dv += nn(pt, de)
                dvl += nn(pe, de)
            proj[r, qc] = (dq * 0.125).astype(LOW)
            proj[r, at(width + p * 128, 128)] = dk.astype(LOW)
            proj[r, at(2 * width + p * 128, 128)] = dv.astype(LOW)
            tmp[0:lat, qc] = dkl
            out[0:lat, qc] = dvl

        def pair(i, carry):
            one_pair(2 * i, 0)
            one_pair(2 * i + 1, 1)
            return carry

        lax.fori_loop(0, half * pairs // 2, pair, 0)
        proj[0:lat, width : 2 * width] = tmp[0:lat, :].astype(LOW)
        proj[0:lat, 2 * width :] = out[0:lat, :].astype(LOW)

    @pl.when(second)
    def _():
        for m in range(half):
            r = slice(lat + m * GROUP, lat + (m + 1) * GROUP)
            b = slice(m * 128, (m + 1) * 128)
            pt = probs[m, 0:GROUP, 0:128]
            pf = pt.astype(F32)
            dx = yb[r, :]
            dp = nt(dx, vbd[b, :])
            ds = (pf * (dp - class_sum(pf * dp))).astype(LOW)
            dk = tn(ds, proj[r, :width])
            dv = tn(pt, dx)
            proj[r, :width] = (nn(ds, kbd[b, :]) * 0.125).astype(LOW)
            head_sum(latf, m * LAT, width, dk, 0.125, False)
            head_sum(latf, m * LAT, 2 * width, dv, 1.0, False)
        settle()
        launch(2 * wide)
        total = latf[:, width:] + kvg_send[me].astype(F32)
        for shift in range(1, n):
            kvg_copy(shift).wait_recv()
            total += kvg_recv[shift - 1].astype(F32)
        proj[0:lat, width:] = total.astype(LOW)

    def qkv_grad(start, count, r):
        weight_grad(
            lambda i, right, piece: (
                2 * wide + 1 + lax.rem(i * many + piece, 3),
                (i * many + piece) // 3,
            ),
            start,
            count,
            lambda i: proj[r, at(i * part, part)],
            lambda i: n1[r, :],
        )

    @pl.when(first)
    def _():
        qkv_grad(0, 3 * per_part, slice(0, rows))
        settle()
        launch(*range(2 * wide + 1, 2 * wide + 4))
        begin()

    @pl.when(first)
    def _():
        def to_in(c):
            tmp[:, c] = nt(proj[...], wq[c, :])

        tiles(width // 256, to_in, 256)

    @pl.when(second)
    def _():
        tmp[...] = nt(proj[:, :width], wq[:, :width])
        tmp[0:lat, :] += nt(proj[0:lat, width:], wq[:, width:])

    def store_in(r, total):
        low = total.astype(LOW)
        yb[r, :] = low
        out[r, :] = jnp.where(first, total, low.astype(F32))

    for band in range(3):
        norm_back(
            load_in, tmp, gain_attn, slice(0, 8), store_in, band * third, (band + 1) * third, 11
        )

        @pl.when(second)
        def _():
            relay(1, band).start()

    for copy in grad_copies:
        copy.start()

    @pl.when(second)
    def _():
        qkv_grad(0, per_part, slice(0, rows))
        settle()
        qkv_grad(per_part, 2 * per_part, slice(0, lat))
        settle()
        launch(*range(2 * wide + 1, 2 * wide + 4))
        begin()

    def gain_copy(bit):
        return pltpu.make_async_remote_copy(
            src_ref=gains.at[bit],
            dst_ref=land_g.at[bit],
            send_sem=gain_s.at[bit],
            recv_sem=gain_r.at[bit],
            device_id=across(bit),
            device_id_type=MESH,
        )

    def gain_step(bit):
        gain_copy(bit).wait_recv()
        gains[bit + 1] = gains[bit] + land_g[bit]

    gain_copy(0).start()

    def turn_with_gains(t, carry):
        turn(t, 0)
        for bit in range(4):

            @pl.when(t == bit + 2)
            def _():
                gain_step(bit)
                if bit < 3:
                    gain_copy(bit + 1).start()

        return carry

    lax.fori_loop(1, groups + 3, turn_with_gains, 0)
    final = gains[4]
    for i in (0, 1):
        whole_gain = jnp.sum(final[8 * i : 8 * i + 8], axis=0, keepdims=True)
        whole_gain = jnp.broadcast_to(whole_gain, (8, width))
        rolled = pltpu.roll(whole_gain, lax.rem(width - me * unit, width), 1)
        gain_sums[8 * i : 8 * i + 8, :] = rolled[:, 0:128]

    def finish(kind):
        def one(k, carry):
            for phase in range(4):
                copy_of(kind, phase, k).wait_send()
            return carry

        lax.fori_loop(0, land[0][kind].shape[0], one, 0)

    for kind in range(3):
        finish(kind)
    for bit in range(4):
        gain_copy(bit).wait_send()
    for copy in grad_copies:
        copy.wait()
    for kind in range(3):
        count = land[0][kind].shape[0]
        for k in (count - 2, count - 1):
            leave(kind, k).wait()

    @pl.when(second)
    def _():
        for band in range(3):
            relay(1, band).wait_send()
        for shift in range(1, n):
            kv_copy(shift, False).wait_send()
            kvg_copy(shift).wait_send()


def both_layers(n, tokens, latents, slots, images, gains, weights, d_tokens, d_latents):
    tok, width = tokens.shape
    lat = latents.shape[0]
    rows = tok + lat
    w_qkv, w_out, w_up, w_down = weights
    ff = w_up.shape[1]
    keys = n * lat
    half = lat // LAT
    size = sum(w.size for w in weights)
    chunks = size // (width * width)
    most = chunks // 3
    unit = width // n
    vm, hbm = pl.BlockSpec(memory_space=pltpu.VMEM), pl.BlockSpec(memory_space=pl.ANY)
    sm = pl.BlockSpec(memory_space=pltpu.SMEM)
    scratch = [
        pltpu.VMEM(w.shape, LOW) for w in (w_qkv, w_out, w_up, w_down)
    ] + [
        pltpu.VMEM(shape, dtype)
        for shape, dtype in (
            ((rows, width), LOW),
            ((rows, width), LOW),
            ((rows, 3 * width), LOW),
            ((rows, width), LOW),
            ((rows, width), F32),
            ((rows, width), LOW),
            ((rows, ff), LOW),
            ((rows, ff), LOW),
            ((rows, width), LOW),
            ((rows, width), LOW),
            ((rows, width), F32),
            ((rows, width), F32),
            ((rows, width), F32),
            ((half * width // 64, GROUP + lat, GROUP), LOW),
            ((half * 128, max(keys, GROUP + 128)), LOW),
            ((4, GROUP, GROUP), F32),
            ((4, GROUP, GROUP), LOW),
            ((lat, 3 * width), F32),
            ((lat, width), F32),
            ((8, keys), F32),
            ((half * 128, width), LOW),
            ((half * 128, width), LOW),
            ((half * 256, width), LOW),
            ((n, lat, 2 * width), LOW),
            ((n, lat, 2 * width), LOW),
            ((n - 1, lat, 2 * width), LOW),
            ((2, 384 // unit, unit, width), LOW),
            ((5, 16, width), F32),
            ((2, 3, unit, width), F32),
            ((2, 2, 2, unit, width), LOW),
            ((2, 2, 2, unit, width), LOW),
            ((2, 2, 2, unit, width), LOW),
            *(
                ((chunks // 3, *shape, unit, width), LOW)
                for shape in ((2, 2, 2), (2, 2), (2,), ())
                for unused_kind in range(3)
            ),
            ((4, 16, width), F32),
        )
    ] + [
        pltpu.SemaphoreType.DMA((10,)),
        pltpu.SemaphoreType.DMA((2, 384 // unit)),
        pltpu.SemaphoreType.DMA((3,)),
        pltpu.SemaphoreType.DMA((2, 3)),
        pltpu.SemaphoreType.DMA((3, 4, most)),
        pltpu.SemaphoreType.DMA((3, 4, most)),
        pltpu.SemaphoreType.DMA((4,)),
        pltpu.SemaphoreType.DMA((4,)),
        pltpu.SemaphoreType.DMA((6,)),
        pltpu.SemaphoreType.DMA((6,)),
        pltpu.SemaphoreType.DMA((n - 1,)),
        pltpu.SemaphoreType.DMA((n - 1,)),
        pltpu.SemaphoreType.DMA((n - 1,)),
        pltpu.SemaphoreType.DMA((n - 1,)),
    ]
    return pl.pallas_call(
        functools.partial(layer_kernel, n),
        out_shape=(
            jax.ShapeDtypeStruct((tok, width), F32),
            jax.ShapeDtypeStruct((lat, width), F32),
            jax.ShapeDtypeStruct((tok, width), F32),
            jax.ShapeDtypeStruct((lat, width), F32),
            jax.ShapeDtypeStruct((chunks, 2, 2, 2, 2, unit, width), LOW),
            jax.ShapeDtypeStruct((chunks, unit, width), F32),
            jax.ShapeDtypeStruct((16, 128), F32),
        ),
        in_specs=[hbm, hbm, vm, sm, sm, vm, vm] + [hbm] * 6,
        out_specs=(hbm,) * 6 + (vm,),
        scratch_shapes=scratch,
        compiler_params=pltpu.CompilerParams(
            collective_id=1, has_side_effects=True, vmem_limit_bytes=63 * 1024 * 1024
        ),
        cost_estimate=pl.CostEstimate(
            flops=6 * rows * size, bytes_accessed=4 * size, transcendentals=0
        ),
    )(tokens, latents, slots, slots, images, *gains, *weights, d_tokens, d_latents)


def finish_kernel(width, *refs):
    rows_in, (summed, gains), rows_out = refs[0:4], refs[4:6], refs[6:10]
    gain_attn, g_qkv, g_out, gain_mlp, g_up, g_down = refs[10:16]
    held, (sem_in, sem_out) = refs[16:21], refs[21:23]
    wide = g_down.shape[1] // width
    unit = g_out.shape[1]
    groups = []
    for src, dst, mid in zip(rows_in, rows_out, held):
        count = src.shape[0] // 128 or 1
        size = src.shape[0] // count
        for i in range(count):
            r = pl.ds(i * size, size)
            groups.append((src.at[r], mid.at[r], [(mid.at[r], dst.at[r])]))
    sums = held[4]
    for c in range(wide):
        target = g_down.at[:, c * width : (c + 1) * width]
        groups.append((summed.at[c], sums.at[c], [(sums.at[c], target)]))
    for low, high, dst in (
        (wide, 2 * wide, g_up),
        (2 * wide, 2 * wide + 1, g_out),
        (2 * wide + 1, 2 * wide + 4, g_qkv),
    ):
        r = pl.ds(low, high - low)
        groups.append((summed.at[r], sums.at[r], [(sums.at[r], dst)]))
    loads = [
        pltpu.make_async_copy(src, dst, sem_in.at[i]) for i, (src, dst, unused) in enumerate(groups)
    ]
    for load in loads:
        load.start()
    gain_attn[...] = gains[0:1, 0:unit]
    gain_mlp[...] = gains[8:9, 0:unit]
    started = []
    for load, (unused_src, unused_dst, moves) in zip(loads, groups):
        load.wait()
        for src, dst in moves:
            started.append(pltpu.make_async_copy(src, dst, sem_out.at[len(started)]))
            started[-1].start()
    for move in started:
        move.wait()


def finished(rows, summed, gains, wide):
    chunks, unit, width = summed.shape
    hbm, vm = pl.BlockSpec(memory_space=pl.ANY), pl.BlockSpec(memory_space=pltpu.VMEM)
    shapes = [r.shape for r in rows] + [
        (1, unit),
        (3, unit, width),
        (1, unit, width),
        (1, unit),
        (wide, unit, width),
        (unit, wide * width),
    ]
    return pl.pallas_call(
        functools.partial(finish_kernel, width),
        out_shape=tuple(jax.ShapeDtypeStruct(s, F32) for s in shapes),
        in_specs=[hbm] * 5 + [vm],
        out_specs=(hbm,) * 4 + (vm, hbm, hbm, vm, hbm, hbm),
        scratch_shapes=[pltpu.VMEM(x.shape, F32) for x in (*rows, summed)]
        + [pltpu.SemaphoreType.DMA((sum(r.shape[0] // 128 or 1 for r in rows) + 3 + wide,))] * 2,
        compiler_params=pltpu.CompilerParams(vmem_limit_bytes=62 * 1024 * 1024),
    )(*rows, summed, gains)
def fused_shards(
    unused_grid,
    tokens,
    latents,
    slot_group,
    image_groups,
    gain_attn,
    w_qkv,
    w_out,
    gain_mlp,
    w_up,
    w_down,
    d_tokens,
    d_latents,
):
    micro, tok, width = tokens.shape
    lat = latents.shape[1]
    out_tok, out_lat, grad_tok, grad_lat, unused_grads, summed, gains = both_layers(
        slot_group.shape[1],
        tokens.reshape(micro * tok, width),
        latents.reshape(micro * lat, width),
        slot_group,
        image_groups,
        (gain_attn, gain_mlp),
        (w_qkv[0], w_out[0], w_up[0], w_down[0]),
        d_tokens.reshape(micro * tok, width),
        d_latents.reshape(micro * lat, width),
    )
    wide = w_up.shape[2] // width
    rows = (out_tok, out_lat, grad_tok, grad_lat)
    *rows, first_gain, qkv, out, second_gain, up, down = finished(rows, summed, gains, wide)
    return (
        rows[0].reshape(1, micro, tok, width),
        rows[1].reshape(1, micro, lat, width),
        rows[2].reshape(1, micro, tok, width),
        rows[3].reshape(1, micro, lat, width),
        first_gain,
        qkv.reshape(-1, width).T[None],
        out.reshape(-1, width).T[None],
        second_gain,
        up.reshape(-1, width).T[None],
        down.T[None],
    )

def solution(mesh):
    in_specs = (
        P(None, "dp", None),
        P(None, "dp", None),
        P(),
        P(),
        P("section", None),
        P("section", None, None),
        P("section", None, None),
        P("section", None),
        P("section", None, None),
        P("section", None, None),
        P(None, "dp", None),
        P(None, "dp", None),
    )
    out_specs = (
        P("section", None, "dp", None),
        P("section", None, "dp", None),
        P("section", None, "dp", None),
        P("section", None, "dp", None),
        P("section", "dp"),
        P("section", None, "dp"),
        P("section", None, "dp"),
        P("section", "dp"),
        P("section", None, "dp"),
        P("section", None, "dp"),
    )
    grid = grid_of(mesh)

    def program(*args):
        n, width = mesh.shape["dp"], args[0].shape[2]
        one_group = args[0].shape[1] == n * GROUP
        body = fused_shards if one_group and n == 16 and width % (16 * n) == 0 else shards
        return jax.shard_map(
            functools.partial(body, grid), mesh=mesh, in_specs=in_specs, out_specs=out_specs, check_vma=False
        )(*args)

    return program
```
